32 devices in a mesh: rows: 8 (over y, x, core), cols: 4 (over z).
Axes of the slice: x: 2, y: 2, z: 4, core: 2. Of those that a mesh axis runs over, the one named last changes fastest.
Arguments:
- tokens: bfloat16 [16384, 1536], P(('rows', 'cols')), may hold values from -6 to 6
- query_weight: bfloat16 [1536, 1536], P('rows', 'cols'), may hold values from -0.15625 to 0.15625
- key_weight: bfloat16 [1536, 256], P('rows', 'cols'), may hold values from -0.15625 to 0.15625
- value_weight: bfloat16 [1536, 256], P('rows', 'cols'), may hold values from -0.15625 to 0.15625
- out_weight: bfloat16 [1536, 1536], P('rows', 'cols'), may hold values from -1.25 to 1.25
- router_weight: bfloat16 [1536, 16], P('rows', 'cols'), may hold values from -0.078125 to 0.078125
- attention_gain: bfloat16 [1536], P(('rows', 'cols')), may hold values from 0.5 to 1.5
- experts_gain: bfloat16 [1536], P(('rows', 'cols')), may hold values from 0.5 to 1.5
- gate_weight: bfloat16 [16, 1536, 768], P('rows', None, 'cols'), may hold values from -0.15625 to 0.15625
- upward_weight: bfloat16 [16, 1536, 768], P('rows', None, 'cols'), may hold values from -0.15625 to 0.15625
- down_weight: bfloat16 [16, 768, 1536], P('rows', 'cols'), may hold values from -0.4375 to 0.4375
- routes: int32 [16384, 4], P(('rows', 'cols')), may hold values from 0 to 15, all different within a row; in each aligned block of 512 rows (0 to 511, 512 to 1023, ...) at most 160 rows name the same one
- leaf_parent: int32 [16, 8], replicated, may hold values from 0 to 3
- cotangent: bfloat16 [16384, 1536], P(('rows', 'cols')), may hold values from -6 to 6
Outputs:
- layer_output: bfloat16 [16384, 1536], P(('rows', 'cols'))
- tokens_grad: bfloat16 [16384, 1536], P(('rows', 'cols'))
- query_grad: float32 [1536, 1536], P('rows', 'cols')
- key_grad: float32 [1536, 256], P('rows', 'cols')
- value_grad: float32 [1536, 256], P('rows', 'cols')
- out_grad: float32 [1536, 1536], P('rows', 'cols')
- router_grad: float32 [1536, 16], P('rows', 'cols')
- attention_gain_grad: float32 [1536], P(('rows', 'cols'))
- experts_gain_grad: float32 [1536], P(('rows', 'cols'))
- gate_grad: float32 [16, 1536, 768], P('rows', None, 'cols')
- upward_grad: float32 [16, 1536, 768], P('rows', None, 'cols')
- down_grad: float32 [16, 768, 1536], P('rows', 'cols')
The draws below stay inside these ranges and needn't reach their ends.
Inputs may be any that keep to these rules, and one draw needn't show every extreme that they name: `routes`: each row names 4 different experts. Within the 512 rows of one device no expert is named more than 160 times; on some device some expert is named exactly 160 times. `leaf_parent`: entry [j, l] is the branch (counted from 0) under which leaf l of tree j hangs.
All inputs are finite; a program needn't handle non-finite values.
Results may differ from the reference program's by a relative error of at most 0.022.
Values may be sent and summed in bfloat16 or wider, within the bound.
No kernel may reach another device: no remote copies, remote signals or barrier semaphores. Data moves between devices by JAX's collectives and lax.ppermute only.
A program may use at most 256 MiB of HBM per device.

```python
import math
import jax
import jax.numpy as jnp
import numpy as np
from jax import lax

D = 1536
HEADS = 12
KV_HEADS = 2
HEAD_DIM = 128
FF = 768
TOP = 4
TOK_DEV = 512
BRANCHES = 4
LEAVES = 8
TRUNK = 256
BRANCH = 64
TREES = 16
TOKENS = 16384
EXPERTS = 16
CAP = 160
DEVICES = 32


def set_ends(values, stream_key, low, largest):
    longest = values.shape.index(max(values.shape))
    spots = []
    for shift in (0, 1):
        where = [jax.random.randint(jax.random.fold_in(stream_key, axis), (), 0, length) for axis, length in enumerate(values.shape)]
        where[longest] = (where[longest] + shift) % values.shape[longest]
        spots.append(tuple(where))
    return values.at[spots[0]].set(low).at[spots[1]].set(largest)


def levels(own_key, shape, pieces, smallest, largest):
    level = 1.0
    for axis_at, parts in pieces:
        draws = jax.random.uniform(jax.random.fold_in(jax.random.fold_in(own_key, 6), axis_at), (parts,), jnp.float32, smallest / len(pieces), largest / len(pieces))
        level = level * jnp.repeat(jnp.exp(draws), shape[axis_at] // parts).reshape((-1,) + (1,) * (len(shape) - 1 - axis_at))
    return level


def routed_block(stream_key, own, number, rows, number_of, top, most, skew):
    sequence = jax.random.permutation(stream_key, number_of)
    crowded, usual = portions_of(number_of, rows * top, most, skew, True), portions_of(number_of, rows * top, most, skew, False)
    places = jnp.arange(number_of)

    def named(sizes, turn):
        used = int((sizes > 0).sum())
        fixed = max(1, used // 4)
        moved = fixed + (places - fixed + turn * (used - fixed)) % max(1, number_of - fixed)
        return jnp.zeros((number_of,), jnp.int32).at[sequence[jnp.where(places < fixed, places, moved)]].set(jnp.asarray(sizes, jnp.int32))

    sizes = jnp.where(number % 4 == 0, named(crowded, number // 4), named(usual, number - number // 4 - 1))
    mixed = jax.random.permutation(jax.random.fold_in(own, 3), number_of)
    source_of, receiver = mixed[0:number_of // 2 * 2:2], mixed[1:number_of // 2 * 2:2]
    room = jnp.minimum(sizes[source_of] - 1, most - sizes[receiver]) // 2
    room = jnp.where((source_of == sequence[0]) | (receiver == sequence[0]) | (sizes[receiver] == 0), 0, jnp.maximum(room, 0))
    moved = jax.random.randint(jax.random.fold_in(own, 4), (number_of // 2,), 0, 1 << 20) % (room + 1)
    sizes = sizes.at[source_of].add(-moved).at[receiver].add(moved)
    members = jnp.searchsorted(jnp.cumsum(sizes), jnp.arange(rows * top), side="right").astype(jnp.int32)
    listing = members.reshape(top, rows).T
    listing = listing[jax.random.permutation(jax.random.fold_in(own, 1), rows)]
    turn = jax.random.randint(jax.random.fold_in(own, 2), (rows, 1), 0, top)
    return jnp.take_along_axis(listing, (jnp.arange(top)[None, :] + turn) % top, axis=1)


def portions_of(number_of, total, limit, lean, full):
    portions = [(1 << 20) // math.isqrt(grade ** lean) + 1 for grade in range(1, number_of + 1)]
    largest = limit if full else min(limit, max(-(-total // number_of), total * portions[0] // sum(portions)))
    least = 1 if total - largest >= number_of - 1 else 0
    counts, surplus = [largest] + [least] * (number_of - 1), total - largest - least * (number_of - 1)
    while surplus > 0:
        free = [i for i in range(1, number_of) if counts[i] < largest] or [i for i in range(1, number_of) if counts[i] < limit]
        whole, remaining = sum([portions[i] for i in free]), surplus
        for i in free:
            extra = min(limit - counts[i], max(1, remaining * portions[i] // whole), surplus)
            counts[i] = counts[i] + extra
            surplus = surplus - extra
    return np.array(counts)


def normal_values(key, shape, spread, reach, pieces=(), held_as=jnp.bfloat16):
    level = levels(key, shape, pieces, -0.22, 0.18) if pieces else 1.0
    values = jax.random.normal(key, shape, jnp.float32) * spread * level
    return jnp.minimum(jnp.maximum(values, -reach), reach).astype(held_as)


def setup_inputs(seed: int = 0) -> dict:
    splits = jax.random.split(jax.random.key(seed), 15)
    tokens = normal_values(splits[0], (TOKENS, D), 1.0, 6.0, ((0, 32),))
    query_weight = normal_values(splits[1], (D, HEADS * HEAD_DIM), D ** -0.5, 0.15625, ((0, 8), (1, 4)))
    key_weight = normal_values(splits[2], (D, KV_HEADS * HEAD_DIM), D ** -0.5, 0.15625, ((0, 8), (1, 4)))
    value_weight = normal_values(splits[3], (D, KV_HEADS * HEAD_DIM), D ** -0.5, 0.15625, ((0, 8), (1, 4)))
    out_weight = normal_values(splits[4], (HEADS * HEAD_DIM, D), (HEADS * HEAD_DIM * 8 // TOK_DEV) ** -0.5, 1.25, ((0, 8), (1, 4)))
    router_weight = normal_values(splits[5], (D, EXPERTS), (4 * D) ** -0.5, 0.078125, ((0, 8), (1, 4)))
    attention_gain = jnp.clip(1.0 + 0.1 * jax.random.normal(splits[6], (D,), jnp.float32), 0.5, 1.5).astype(jnp.bfloat16)
    experts_gain = jnp.clip(1.0 + 0.1 * jax.random.normal(splits[7], (D,), jnp.float32), 0.5, 1.5).astype(jnp.bfloat16)
    gate_weight = normal_values(splits[8], (EXPERTS, D, FF), D ** -0.5, 0.15625, ((0, 8), (2, 4)))
    upward_weight = normal_values(splits[9], (EXPERTS, D, FF), D ** -0.5, 0.15625, ((0, 8), (2, 4)))
    down_weight = normal_values(splits[10], (EXPERTS, FF, D), (FF // 4) ** -0.5, 0.4375, ((0, 8), (1, 4)))
    routes_keys = jax.random.split(jax.random.fold_in(splits[11], 1), TOKENS // TOK_DEV)
    routes_turns = jax.random.permutation(jax.random.fold_in(splits[11], 3), TOKENS // TOK_DEV)
    routes = jax.vmap(lambda own, number: routed_block(jax.random.fold_in(splits[11], 2), own, number, TOK_DEV, EXPERTS, TOP, CAP, 0))(routes_keys, routes_turns).reshape((TOKENS, TOP))
    leaf_parent = set_ends(jax.random.randint(splits[12], (TREES, LEAVES), 0, BRANCHES), jax.random.fold_in(splits[12], 1), 0, BRANCHES - 1).astype(jnp.int32)
    cotangent = normal_values(splits[13], (TOKENS, D), 1.0, 6.0, ((0, 32),))
    return dict(tokens=tokens, query_weight=query_weight, key_weight=key_weight, value_weight=value_weight, out_weight=out_weight, router_weight=router_weight, attention_gain=attention_gain, experts_gain=experts_gain, gate_weight=gate_weight, upward_weight=upward_weight, down_weight=down_weight, routes=routes, leaf_parent=leaf_parent, cotangent=cotangent)


EPSILON = 1e-06
ROPE_BASE = 10000.0
MASKED = -1e+30
HIGHEST = lax.Precision.HIGHEST

@jax.custom_vjp
def low(v):
    return lax.optimization_barrier(v.astype(jnp.bfloat16)).astype(jnp.float32)

@jax.custom_vjp
def low_back(v):
    return v

def low_keep(v):
    return (low(v), None)

def low_pass(kept, grad):
    return (grad,)

def back_keep(v):
    return (v, None)

def back_low(kept, grad):
    return (low(grad),)
low.defvjp(low_keep, low_pass)
low_back.defvjp(back_keep, back_low)

def rms_norm(values, norm_gain):
    factor = lax.rsqrt(lax.optimization_barrier(jnp.mean(values * values, axis=-1, keepdims=True)) + EPSILON)
    return values * factor * norm_gain

def segment_of(token_index):
    branch_part = 1 + (token_index - TRUNK) // BRANCH
    leaf_part = 1 + BRANCHES + (token_index - TOK_DEV) // BRANCH
    return jnp.where(token_index < TRUNK, 0, jnp.where(token_index < TOK_DEV, branch_part, leaf_part)).astype(jnp.int32)

def position_of(token_index):
    branch_place = TRUNK + (token_index - TRUNK) % BRANCH
    leaf_place = TRUNK + BRANCH + (token_index - TOK_DEV) % BRANCH
    return jnp.where(token_index < TRUNK, token_index, jnp.where(token_index < TOK_DEV, branch_place, leaf_place)).astype(jnp.int32)

def tree_order():
    return ((jnp.arange(2 * TOK_DEV, dtype=jnp.int32) + TOK_DEV) % (2 * TOK_DEV)).astype(jnp.int32)

def path_mask(query_index, key_index, parent_row):
    query_part = segment_of(query_index)
    key_part = segment_of(key_index)
    leaf_slot = query_part - 1 - BRANCHES
    leaf_match = leaf_slot[:, None] == jnp.arange(LEAVES, dtype=jnp.int32)[None, :]
    ancestor = jnp.where(query_part > BRANCHES, 1 + lax.optimization_barrier(jnp.sum(jnp.where(leaf_match, parent_row[None, :], 0), axis=1)), 0)
    reachable = (key_part[None, :] == query_part[:, None]) | (key_part[None, :] == 0) | (key_part[None, :] == ancestor[:, None])
    return reachable & (key_index[None, :] <= query_index[:, None])

def rotary_tables(positions):
    half_dim = HEAD_DIM // 2
    frequency = ROPE_BASE ** (-jnp.arange(half_dim, dtype=jnp.float32) / half_dim)
    angles = positions.astype(jnp.float32)[:, None] * frequency[None, :]
    return (jnp.cos(angles)[:, None, :], jnp.sin(angles)[:, None, :])

def rotate(values, cosine, sine_table):
    half_dim = HEAD_DIM // 2
    first_half = values[..., :half_dim]
    second_half = values[..., half_dim:]
    return jnp.concatenate([first_half * cosine - second_half * sine_table, second_half * cosine + first_half * sine_table], axis=-1)

def tree_attention(inputs):
    queries, key_rows, value_rows, parent_row = inputs
    length = 2 * TOK_DEV
    token_index = tree_order()
    allowed = path_mask(token_index, token_index, parent_row)
    grouped = queries.reshape(length, KV_HEADS, HEADS // KV_HEADS, HEAD_DIM)
    scores = jnp.einsum('qkgd,skd->kgqs', grouped, key_rows, precision=HIGHEST)
    scores = low_back(scores * HEAD_DIM ** (-0.5))
    scores = jnp.where(allowed[None, None], scores, MASKED)
    attention = low(jax.nn.softmax(scores, axis=-1))
    mixed_heads = jnp.einsum('kgqs,skd->qkgd', attention, value_rows, precision=HIGHEST)
    return mixed_heads.reshape(length, HEADS * HEAD_DIM)

def expert_rows(inputs):
    row_block, gate_matrix, upward_matrix, down_matrix = inputs
    gate_act = low_back(jnp.dot(row_block, gate_matrix, precision=HIGHEST))
    upward = low_back(jnp.dot(row_block, upward_matrix, precision=HIGHEST))
    hidden = low(jax.nn.silu(gate_act) * upward)
    return low(low_back(jnp.dot(hidden, down_matrix, precision=HIGHEST)))

def dispatch_tables(routes):
    route_rows = routes.reshape(DEVICES, TOK_DEV * TOP)
    expert_ids = jnp.arange(EXPERTS, dtype=jnp.int32)
    onehot = (route_rows[:, :, None] == expert_ids[None, None, :]).astype(jnp.int32)
    earlier = jnp.cumsum(onehot, axis=1) - onehot
    slot_rank = lax.optimization_barrier(jnp.sum(earlier * onehot, axis=2))
    device = jnp.arange(DEVICES, dtype=jnp.int32)[:, None]
    slot_index = (route_rows * DEVICES + device) * CAP + slot_rank
    route_ids = device * (TOK_DEV * TOP) + jnp.arange(TOK_DEV * TOP, dtype=jnp.int32)[None, :]
    source = jnp.zeros((EXPERTS * DEVICES * CAP,), jnp.int32).at[slot_index.reshape(-1)].set(route_ids.reshape(-1) + 1)
    return (slot_index.reshape(TOKENS, TOP), source)

def forward(tokens, query_weight, key_weight, value_weight, out_weight, router_weight, attention_gain, experts_gain, gate_weight, upward_weight, down_weight, routes, leaf_parent):
    normed = low(rms_norm(tokens, attention_gain))
    query_lin = low_back(jnp.dot(normed, query_weight, precision=HIGHEST))
    key_lin = low_back(jnp.dot(normed, key_weight, precision=HIGHEST))
    value_all = low(low_back(jnp.dot(normed, value_weight, precision=HIGHEST)))
    positions = jnp.tile(position_of(tree_order()), TREES)
    cosine, sine_table = rotary_tables(positions)
    query_all = low(rotate(query_lin.reshape(TOKENS, HEADS, HEAD_DIM), cosine, sine_table))
    key_all = low(rotate(key_lin.reshape(TOKENS, KV_HEADS, HEAD_DIM), cosine, sine_table))
    mixed_heads = lax.map(jax.checkpoint(tree_attention), (query_all.reshape(TREES, 2 * TOK_DEV, HEADS * HEAD_DIM), key_all.reshape(TREES, 2 * TOK_DEV, KV_HEADS, HEAD_DIM), value_all.reshape(TREES, 2 * TOK_DEV, KV_HEADS, HEAD_DIM), leaf_parent))
    heads_out = low(low_back(mixed_heads.reshape(TOKENS, HEADS * HEAD_DIM)))
    residual = tokens + low_back(jnp.dot(heads_out, out_weight, precision=HIGHEST))
    normed_two = low(rms_norm(residual, experts_gain))
    logits = jnp.dot(normed_two, router_weight, precision=HIGHEST)
    softmax_out = jax.nn.softmax(logits, axis=-1)
    chosen = jnp.take_along_axis(softmax_out, routes, axis=1)
    gate_share = chosen / lax.optimization_barrier(jnp.sum(chosen, axis=1, keepdims=True))
    slot_index, source = dispatch_tables(routes)
    filled = source > 0
    token_of = jnp.maximum(source - 1, 0) // TOP
    row_block = jnp.where(filled[:, None], normed_two[token_of], 0.0)
    row_block = low_back(row_block).reshape(EXPERTS, DEVICES * CAP, D)
    results = lax.map(jax.checkpoint(expert_rows), (row_block, gate_weight, upward_weight, down_weight))
    picked = results.reshape(EXPERTS * DEVICES * CAP, D)[slot_index.reshape(-1)].reshape(TOKENS, TOP, D)
    mixture = lax.optimization_barrier(jnp.sum(gate_share[:, :, None] * picked, axis=1))
    return residual + mixture

def reference(tokens, query_weight, key_weight, value_weight, out_weight, router_weight, attention_gain, experts_gain, gate_weight, upward_weight, down_weight, routes, leaf_parent, cotangent):
    floats = tuple((array.astype(jnp.float32) for array in (tokens, query_weight, key_weight, value_weight, out_weight, router_weight, attention_gain, experts_gain, gate_weight, upward_weight, down_weight)))

    def objective(*weights_in):
        return forward(*weights_in, routes, leaf_parent)
    layer_out, pullback = jax.vjp(objective, *floats)
    gradients = pullback(cotangent.astype(jnp.float32))
    return (layer_out.astype(jnp.bfloat16), gradients[0].astype(jnp.bfloat16), gradients[1], gradients[2], gradients[3], gradients[4], gradients[5], gradients[6], gradients[7], gradients[8], gradients[9], gradients[10])
```

```python
import jax
import jax.numpy as jnp
from jax import lax
from jax.sharding import PartitionSpec as P

D = 1536
HEADS = 12
KV_HEADS = 2
HEAD_DIM = 128
TOP = 4
TOK_DEV = 512
BRANCHES = 4
LEAVES = 8
TRUNK = 256
BRANCH = 64


EPSILON = 1e-06
ROPE_BASE = 10000.0
MASKED = -1e30
HIGHEST = lax.Precision.HIGHEST


def rms_norm(values, norm_gain):
    factor = lax.rsqrt(jnp.mean(values * values, axis=-1, keepdims=True) + EPSILON)
    return values * factor * norm_gain


def segment_of(token_index):
    branch_part = 1 + (token_index - TRUNK) // BRANCH
    leaf_part = 1 + BRANCHES + (token_index - TOK_DEV) // BRANCH
    return jnp.where(
        token_index < TRUNK, 0, jnp.where(token_index < TOK_DEV, branch_part, leaf_part)
    )


def position_of(token_index):
    branch_place = TRUNK + (token_index - TRUNK) % BRANCH
    leaf_place = TRUNK + BRANCH + (token_index - TOK_DEV) % BRANCH
    return jnp.where(
        token_index < TRUNK, token_index, jnp.where(token_index < TOK_DEV, branch_place, leaf_place)
    )


def path_mask(query_index, key_index, parent_row):
    query_part = segment_of(query_index)
    key_part = segment_of(key_index)
    leaf_slot = query_part - 1 - BRANCHES
    leaf_match = leaf_slot[:, None] == jnp.arange(LEAVES, dtype=jnp.int32)[None, :]
    ancestor = jnp.where(
        query_part > BRANCHES, 1 + jnp.sum(jnp.where(leaf_match, parent_row[None, :], 0), axis=1), 0
    )
    reachable = (
        (key_part[None, :] == query_part[:, None])
        | (key_part[None, :] == 0)
        | (key_part[None, :] == ancestor[:, None])
    )
    return reachable & (key_index[None, :] <= query_index[:, None])


def rotary_tables(positions):
    half_dim = HEAD_DIM // 2
    frequency = ROPE_BASE ** (-jnp.arange(half_dim, dtype=jnp.float32) / half_dim)
    angles = positions.astype(jnp.float32)[:, None] * frequency[None, :]
    return (jnp.cos(angles)[:, None, :], jnp.sin(angles)[:, None, :])


def rotate(values, cosine, sine_table):
    half_dim = HEAD_DIM // 2
    first_half = values[..., :half_dim]
    second_half = values[..., half_dim:]
    return jnp.concatenate(
        [
            first_half * cosine - second_half * sine_table,
            second_half * cosine + first_half * sine_table,
        ],
        axis=-1,
    )


def take(block, index):
    return lax.dynamic_index_in_dim(block, index, 0, keepdims=False)


def pick(table, place):
    return jnp.asarray(table, jnp.int32)[place]


SLOT_SHARD = ((0, 2, 1, 3), (1, 3, 0, 2), (2, 0, 1, 3), (3, 1, 2, 0))


def slot_shards():
    count = lax.axis_size("cols")
    if count == 4:
        return pick(SLOT_SHARD, lax.axis_index("cols"))
    return jnp.arange(count, dtype=jnp.int32)


def gather_slots(block):
    count = lax.axis_size("cols")
    if count != 4:
        whole = lax.all_gather(block, "cols", axis=0)
        return [whole[i] for i in range(count)]
    place = lax.axis_index("cols")
    above = lax.ppermute(block, "cols", [(1, 0), (2, 1), (3, 2)])
    below = lax.ppermute(block, "cols", [(0, 1), (1, 2), (2, 3)])
    far = lax.ppermute(block, "cols", [(0, 3), (3, 0)])
    payload = jnp.where(place == 1, above, jnp.where(place == 2, below, block))
    second = lax.ppermute(payload, "cols", [(3, 1), (1, 0), (0, 2), (2, 3)])
    end = (place == 0) | (place == 3)
    return [
        block,
        second,
        jnp.where(place == 0, above, below),
        jnp.where(end, far, above),
    ]


def reduce_slots(slots):
    count = lax.axis_size("cols")
    if count != 4:
        whole = jnp.stack(slots).astype(jnp.bfloat16)
        return lax.psum_scatter(whole, "cols", scatter_dimension=0).astype(jnp.float32)
    place = lax.axis_index("cols")
    own, second, third, fourth = slots
    end = (place == 0) | (place == 3)
    relay = lax.ppermute(second, "cols", [(1, 3), (0, 1), (2, 0), (3, 2)])
    far = lax.ppermute(fourth, "cols", [(0, 3), (3, 0)])
    relayed = relay.astype(jnp.float32)
    upward_load = (
        jnp.where(place == 0, third, fourth).astype(jnp.float32)
        + jnp.where(place == 1, relayed, 0.0)
    ).astype(jnp.bfloat16)
    downward_load = (third.astype(jnp.float32) + jnp.where(place == 2, relayed, 0.0)).astype(
        jnp.bfloat16
    )
    below = lax.ppermute(upward_load, "cols", [(0, 1), (1, 2), (2, 3)])
    above = lax.ppermute(downward_load, "cols", [(1, 0), (2, 1), (3, 2)])
    return (
        own.astype(jnp.float32)
        + below.astype(jnp.float32)
        + above.astype(jnp.float32)
        + jnp.where(end, relayed + far.astype(jnp.float32), 0.0)
    )


def flip(block, bit):
    count = lax.axis_size("rows")
    return lax.ppermute(block, "rows", [(i, i ^ bit) for i in range(count)])


def gather_rows(block):
    count = lax.axis_size("rows")
    if count != 8:
        return lax.all_gather(block, "rows", axis=0)
    place = lax.axis_index("rows")
    core, side, level = place % 2, place // 2 % 2, place // 4
    half = block.shape[0] // 2
    beside = flip(block, 2)
    across = flip(block, 4)
    corner = jnp.concatenate([flip(beside[:half], 4), flip(across[half:], 2)], axis=0)
    near = [jnp.where(side == 0, block, beside), jnp.where(side == 0, beside, block)]
    away = [jnp.where(side == 0, across, corner), jnp.where(side == 0, corner, across)]
    same = jnp.stack(
        [jnp.where(level == 0, near[i], away[i]) for i in range(2)]
        + [jnp.where(level == 0, away[i], near[i]) for i in range(2)]
    )
    other = flip(same, 1)
    both = jnp.stack([jnp.where(core == 0, same, other), jnp.where(core == 0, other, same)], axis=1)
    return both.reshape((count,) + block.shape)


def reduce_rows(blocks):
    count = lax.axis_size("rows")
    if count != 8:
        return lax.psum_scatter(blocks, "rows", scatter_dimension=0).astype(jnp.float32)
    place = lax.axis_index("rows")
    core, side, level = place % 2, place // 2 % 2, place // 4
    half = blocks.shape[1] // 2
    rest = blocks.shape[1:]

    def own_of(array, axis, index):
        return lax.dynamic_index_in_dim(array, index, axis, keepdims=False)

    def add(array, axis, index, bit):
        arrived = flip(own_of(array, axis, 1 - index), bit)
        return own_of(array, axis, index).astype(jnp.float32) + arrived.astype(jnp.float32)

    chips = add(blocks.reshape((2, 2, 2) + rest), 2, core, 1).astype(jnp.bfloat16)
    first = add(chips[:, :, :half], 1, side, 2).astype(jnp.bfloat16)
    second = add(chips[:, :, half:], 0, level, 4).astype(jnp.bfloat16)
    return jnp.concatenate([add(first, 0, level, 4), add(second, 0, side, 2)], axis=0)


def on_device(
    tokens,
    query_weight,
    key_weight,
    value_weight,
    out_weight,
    router_weight,
    attention_gain,
    experts_gain,
    gate_weight,
    upward_weight,
    down_weight,
    routes,
    leaf_parent,
    cotangent,
):
    row_count = lax.axis_size("rows")
    col_count = lax.axis_size("cols")
    row_place = lax.axis_index("rows")
    col_place = lax.axis_index("cols")
    parity = col_place % 2
    tree_id = (row_place * col_count + col_place) // 2
    parent_row = lax.dynamic_slice_in_dim(leaf_parent, tree_id, 1, 0)[0]
    key_width = KV_HEADS * HEAD_DIM
    query_width = HEADS * HEAD_DIM
    group_size = HEADS // KV_HEADS
    depth, query_part = query_weight.shape
    key_part = key_weight.shape[1]
    router_part = router_weight.shape[1]
    gain_part = attention_gain.shape[0]
    expert_total = router_part * col_count
    local_experts = gate_weight.shape[0]
    capacity = TOK_DEV * TOP // expert_total * 5 // 4
    spare = 128

    extras = jnp.concatenate(
        [
            router_weight,
            jnp.pad(attention_gain, (0, depth - gain_part))[:, None],
            jnp.pad(experts_gain, (0, depth - gain_part))[:, None],
            jnp.zeros((depth, spare - router_part - 2), jnp.bfloat16),
        ],
        axis=1,
    )
    packed = jnp.concatenate([query_weight, key_weight, value_weight, out_weight, extras], axis=1)
    packed_width = packed.shape[1]
    packed_slots = jnp.stack(gather_slots(packed))
    shards = slot_shards()
    slot_of_shard = jnp.argsort(shards)
    packed_cols = jnp.take(packed_slots, slot_of_shard, axis=0)
    packed_all = gather_rows(packed_cols.reshape(col_count * depth, packed_width)).reshape(
        row_count, col_count, depth, packed_width
    )

    def unpack(start, width):
        part = packed_all[..., start : start + width]
        return jnp.swapaxes(part, 1, 2).reshape(row_count * depth, col_count * width)

    key_at = query_part
    value_at = key_at + key_part
    out_at = value_at + key_part
    extra_at = out_at + query_part
    query_full = unpack(0, query_part)
    key_full = unpack(key_at, key_part)
    value_full = unpack(value_at, key_part)
    out_full = unpack(out_at, query_part)
    router_full = unpack(extra_at, router_part)
    gain_at = extra_at + router_part
    attention_full = packed_all[:, :, :gain_part, gain_at].reshape(-1)
    experts_full = packed_all[:, :, :gain_part, gain_at + 1].reshape(-1)

    expert_weights = []
    ahead = packed_slots
    for expert in range(local_experts):
        block = jnp.stack(
            [gate_weight[expert].T, upward_weight[expert].T, down_weight[expert]], axis=0
        )
        block, ahead = lax.optimization_barrier((block, ahead))
        slots = gather_slots(block)
        ahead = slots[1]
        expert_weights.append(jnp.stack(slots, axis=1))

    routes_all = lax.all_gather(routes, "rows", axis=0)
    grad_all = lax.all_gather(cotangent, "rows", axis=0)

    token_float = tokens.astype(jnp.float32)
    attention_scale = attention_full.astype(jnp.float32)
    normed = rms_norm(token_float, attention_scale)
    normed_low = normed.astype(jnp.bfloat16)
    query_lin = jnp.dot(normed_low, query_full, preferred_element_type=jnp.float32)
    key_lin = jnp.dot(normed_low, key_full, preferred_element_type=jnp.float32)
    value_low = jnp.dot(normed_low, value_full, preferred_element_type=jnp.float32).astype(
        jnp.bfloat16
    )
    holds_leaves = parity == 0
    local_index = (1 - parity) * TOK_DEV + jnp.arange(TOK_DEV, dtype=jnp.int32)
    cosine, sine_table = rotary_tables(position_of(local_index))
    query_low = rotate(query_lin.reshape(TOK_DEV, HEADS, HEAD_DIM), cosine, sine_table).astype(
        jnp.bfloat16
    )
    key_low = (
        rotate(key_lin.reshape(TOK_DEV, KV_HEADS, HEAD_DIM), cosine, sine_table)
        .astype(jnp.bfloat16)
        .reshape(TOK_DEV, key_width)
    )
    pairs = [(i + 1, i) for i in range(0, col_count, 2)]
    own_pair = jnp.concatenate([key_low, value_low], axis=1)
    partner = lax.ppermute(own_pair, "cols", pairs)
    tree_rows = jnp.concatenate(
        [
            jnp.where(holds_leaves, partner, own_pair),
            jnp.where(holds_leaves, own_pair, jnp.zeros_like(own_pair)),
        ],
        axis=0,
    )
    key_tree = tree_rows[:, :key_width].reshape(2 * TOK_DEV, KV_HEADS, HEAD_DIM)
    value_tree = tree_rows[:, key_width:].reshape(2 * TOK_DEV, KV_HEADS, HEAD_DIM)
    key_index = jnp.arange(2 * TOK_DEV, dtype=jnp.int32)
    factor = HEAD_DIM ** (-0.5)
    query_group = query_low.reshape(TOK_DEV, KV_HEADS, group_size, HEAD_DIM)
    allowed = path_mask(local_index, key_index, parent_row)

    def block_scores():
        scores = (
            jnp.einsum("qkgd,skd->kgqs", query_group, key_tree, preferred_element_type=jnp.float32)
            * factor
        )
        return jnp.where(allowed[None, None], scores, MASKED)

    scores = block_scores()
    highest = jnp.max(scores, axis=-1, keepdims=True)
    weights = jnp.exp(scores - highest)
    totals = jnp.sum(weights, axis=-1, keepdims=True)
    attention = (weights / totals).astype(jnp.bfloat16)
    mixed_heads = jnp.einsum(
        "kgqs,skd->qkgd", attention, value_tree, preferred_element_type=jnp.float32
    )
    log_total = highest + jnp.log(totals)
    heads_low = mixed_heads.reshape(TOK_DEV, query_width).astype(jnp.bfloat16)
    residual = token_float + jnp.dot(heads_low, out_full, preferred_element_type=jnp.float32)
    experts_scale = experts_full.astype(jnp.float32)
    normed_two = rms_norm(residual, experts_scale)
    normed_two_low = normed_two.astype(jnp.bfloat16)
    normed_all = lax.all_gather(normed_two_low, "rows", axis=0)

    expert_ids = jnp.arange(expert_total, dtype=jnp.int32)

    def shares(chosen_of, logit_cols):
        softmax_out = jax.nn.softmax(logit_cols, axis=-2)
        return softmax_out / jnp.sum(
            jnp.where(chosen_of, softmax_out, 0.0), axis=-2, keepdims=True
        )

    own_ids = row_place * local_experts + jnp.arange(local_experts, dtype=jnp.int32)
    named = routes_all[:, :, :, None] == expert_ids[None, None, None, :]
    named = jnp.swapaxes(jnp.any(named, axis=2), 1, 2)
    logits_all = jnp.einsum(
        "de,rtd->ret", router_full, normed_all, preferred_element_type=jnp.float32
    )
    share_all = shares(named, logits_all)
    own_at = row_place * local_experts
    hit = lax.dynamic_slice_in_dim(named, own_at, local_experts, 1)
    share = lax.dynamic_slice_in_dim(share_all, own_at, local_experts, 1)
    earlier = jnp.arange(TOK_DEV)[:, None] < jnp.arange(TOK_DEV)[None, :]
    rank = jnp.einsum(
        "rlt,tu->rlu",
        hit.astype(jnp.bfloat16),
        earlier.astype(jnp.bfloat16),
        preferred_element_type=jnp.float32,
    ).astype(jnp.int32)
    place_ids = jnp.arange(capacity, dtype=jnp.int32)
    onehot = (hit[:, :, None, :] & (rank[:, :, None, :] == place_ids[None, None, :, None])).astype(
        jnp.bfloat16
    )
    share_rows = jnp.sum(
        onehot.astype(jnp.float32) * jnp.where(hit, share, 0.0)[:, :, None, :], axis=-1
    )
    token_rows = jnp.einsum("rlct,rtd->lrcd", onehot, normed_all).reshape(
        local_experts, row_count * capacity, D
    )
    grad_rows = jnp.einsum("rlct,rtd->lrcd", onehot, grad_all).reshape(
        local_experts, row_count * capacity, D
    )
    share_rows = jnp.swapaxes(share_rows, 0, 1).reshape(local_experts, row_count * capacity, 1)

    out_rows, back_rows, gate_dots, reduced = ([], [], [], [])
    for expert in range(local_experts):
        gate_full, upward_full, down_full = expert_weights[expert].reshape(3, -1, D)
        row_block = token_rows[expert]
        grad_block = grad_rows[expert].astype(jnp.float32)
        grad_expert = (share_rows[expert] * grad_block).astype(jnp.bfloat16)

        def dot(one, two, dims):
            return lax.dot_general(
                one, two, (dims, ((), ())), preferred_element_type=jnp.float32
            )

        gate_act = dot(row_block, gate_full, ((1,), (1,)))
        upward = dot(row_block, upward_full, ((1,), (1,)))
        silu_gate = jax.nn.silu(gate_act)
        hidden_low = (silu_gate * upward).astype(jnp.bfloat16)
        expert_out = dot(hidden_low, down_full, ((1,), (0,))).astype(jnp.bfloat16)
        grad_hidden = dot(grad_expert, down_full, ((1,), (1,)))
        sigmoid_gate = jax.nn.sigmoid(gate_act)
        grad_gate_act = (
            grad_hidden * upward * sigmoid_gate * (1.0 + gate_act * (1.0 - sigmoid_gate))
        ).astype(jnp.bfloat16)
        grad_upward = (grad_hidden * silu_gate).astype(jnp.bfloat16)
        down_grad = dot(hidden_low, grad_expert, ((0,), (0,)))
        gate_grad = dot(grad_gate_act, row_block, ((0,), (0,)))
        upward_grad = dot(grad_upward, row_block, ((0,), (0,)))
        slots = [
            jnp.stack(
                [
                    grad.astype(jnp.bfloat16).reshape(col_count, -1, D)[i]
                    for grad in (gate_grad, upward_grad, down_grad)
                ]
            )
            for i in range(col_count)
        ]
        reduced.append(reduce_slots(slots))
        grad_route_in = (
            dot(grad_gate_act, gate_full, ((1,), (0,)))
            + dot(grad_upward, upward_full, ((1,), (0,)))
        ).astype(jnp.bfloat16)
        out_float = expert_out.astype(jnp.float32)
        out_rows.append((share_rows[expert] * out_float).astype(jnp.bfloat16))
        back_rows.append(grad_route_in)
        gate_dots.append(jnp.sum(grad_block * out_float, axis=-1))

    out_rows = jnp.stack(out_rows).reshape(local_experts, row_count, capacity, D)
    back_rows = jnp.stack(back_rows).reshape(local_experts, row_count, capacity, D)
    gate_dots = jnp.stack(gate_dots).reshape(local_experts, row_count, capacity)
    grad_share = jnp.einsum(
        "rlct,lrc->rlt", onehot.astype(jnp.float32), gate_dots, precision=HIGHEST
    )
    back_part = jnp.einsum(
        "rlct,lrcd->rtd", onehot, back_rows, preferred_element_type=jnp.float32
    ).astype(jnp.bfloat16)
    out_part = jnp.einsum(
        "rlct,lrcd->rtd", onehot, out_rows, preferred_element_type=jnp.float32
    ).astype(jnp.bfloat16)
    grad_share_all = lax.all_gather(grad_share, "rows", axis=1, tiled=True)
    grad_shares = take(grad_share_all, row_place)
    back_sum = reduce_rows(back_part)
    mixture = reduce_rows(out_part)
    layer_output = (residual + mixture).astype(jnp.bfloat16)
    grad_out = cotangent.astype(jnp.float32)

    chosen_of = take(named, row_place)
    logits = take(logits_all, row_place)

    def shares_out(logit_cols):
        return jnp.where(chosen_of, shares(chosen_of, logit_cols), 0.0)

    _, router_pullback = jax.vjp(shares_out, logits)
    (grad_logits,) = router_pullback(grad_shares)
    router_float = router_full.astype(jnp.float32)
    grad_normed_two = back_sum + jnp.einsum(
        "et,de->td", grad_logits, router_float, precision=HIGHEST
    )
    router_grad = jnp.einsum(
        "td,et->de", normed_two_low.astype(jnp.float32), grad_logits, precision=HIGHEST
    )
    second_norm, second_pullback = jax.vjp(rms_norm, residual, experts_scale)
    grad_residual_norm, experts_gain_grad = second_pullback(grad_normed_two)
    grad_residual = grad_out + grad_residual_norm
    grad_branch_low = grad_residual.astype(jnp.bfloat16)
    out_grad = jnp.einsum(
        "tq,td->qd", heads_low, grad_branch_low, preferred_element_type=jnp.float32
    )
    grad_heads_low = jnp.einsum(
        "td,qd->tq", grad_branch_low, out_full, preferred_element_type=jnp.float32
    ).astype(jnp.bfloat16)
    grad_block = grad_heads_low.reshape(TOK_DEV, KV_HEADS, group_size, HEAD_DIM)

    attention = jnp.exp(block_scores() - log_total)
    attention_low = attention.astype(jnp.bfloat16)
    grad_attention = jnp.einsum(
        "qkgd,skd->kgqs", grad_block, value_tree, preferred_element_type=jnp.float32
    )
    grad_scores = (
        attention
        * (grad_attention - jnp.sum(attention * grad_attention, axis=-1, keepdims=True))
    ).astype(jnp.bfloat16)
    grad_query = (
        jnp.einsum("kgqs,skd->qkgd", grad_scores, key_tree, preferred_element_type=jnp.float32)
        * factor
    )
    key_tree_grad = (
        jnp.einsum("kgqs,qkgd->skd", grad_scores, query_group, preferred_element_type=jnp.float32)
        * factor
    ).reshape(2 * TOK_DEV, key_width)
    value_tree_grad = jnp.einsum(
        "kgqs,qkgd->skd", attention_low, grad_block, preferred_element_type=jnp.float32
    ).reshape(2 * TOK_DEV, key_width)
    tree_grads = jnp.concatenate([key_tree_grad, value_tree_grad], axis=1)
    arrived = lax.ppermute(
        tree_grads[:TOK_DEV].astype(jnp.bfloat16), "cols", [(j, i) for i, j in pairs]
    ).astype(jnp.float32)
    own_grads = jnp.where(holds_leaves, tree_grads[TOK_DEV:], tree_grads[:TOK_DEV] + arrived)
    grad_key_rot = own_grads[:, :key_width].reshape(TOK_DEV, KV_HEADS, HEAD_DIM)
    grad_key_low = (
        rotate(grad_key_rot, cosine, -sine_table).reshape(TOK_DEV, key_width).astype(jnp.bfloat16)
    )
    grad_value_low = own_grads[:, key_width:].astype(jnp.bfloat16)
    grad_query_low = (
        rotate(grad_query.reshape(TOK_DEV, HEADS, HEAD_DIM), cosine, -sine_table)
        .reshape(TOK_DEV, query_width)
        .astype(jnp.bfloat16)
    )
    query_grad = jnp.einsum(
        "td,tq->dq", normed_low, grad_query_low, preferred_element_type=jnp.float32
    )
    key_grad = jnp.einsum("td,tq->dq", normed_low, grad_key_low, preferred_element_type=jnp.float32)
    value_grad = jnp.einsum(
        "td,tq->dq", normed_low, grad_value_low, preferred_element_type=jnp.float32
    )
    grad_normed = (
        jnp.einsum("tq,dq->td", grad_query_low, query_full, preferred_element_type=jnp.float32)
        + jnp.einsum("tq,dq->td", grad_key_low, key_full, preferred_element_type=jnp.float32)
        + jnp.einsum("tq,dq->td", grad_value_low, value_full, preferred_element_type=jnp.float32)
    )
    first_norm, first_pullback = jax.vjp(rms_norm, token_float, attention_scale)
    grad_tokens_norm, attention_gain_grad = first_pullback(grad_normed)
    tokens_grad = (grad_residual + grad_tokens_norm).astype(jnp.bfloat16)

    def by_shard(grad, width):
        parts = grad.astype(jnp.bfloat16).reshape(row_count, depth, col_count, width)
        return jnp.swapaxes(parts, 1, 2)

    def gain_shard(grad):
        parts = grad.astype(jnp.bfloat16).reshape(row_count, col_count, gain_part)
        return jnp.pad(parts, ((0, 0), (0, 0), (0, depth - gain_part)))[..., None]

    packed_grad = jnp.concatenate(
        [
            by_shard(query_grad, query_part),
            by_shard(key_grad, key_part),
            by_shard(value_grad, key_part),
            by_shard(out_grad, query_part),
            by_shard(router_grad, router_part),
            gain_shard(attention_gain_grad),
            gain_shard(experts_gain_grad),
            jnp.zeros((row_count, col_count, depth, spare - router_part - 2), jnp.bfloat16),
        ],
        axis=-1,
    )
    row_sums = reduce_rows(packed_grad.reshape(row_count, col_count * depth, packed_width))
    row_sums = row_sums.astype(jnp.bfloat16).reshape(col_count, depth, packed_width)
    row_slots = jnp.take(row_sums, shards, axis=0)
    sums = reduce_slots([row_slots[i] for i in range(col_count)])

    def final(which):
        return jnp.stack([reduced[expert][which] for expert in range(local_experts)])

    return (
        layer_output,
        tokens_grad,
        sums[:, :key_at],
        sums[:, key_at:value_at],
        sums[:, value_at:out_at],
        sums[:, out_at:extra_at],
        sums[:, extra_at:gain_at],
        sums[:gain_part, gain_at],
        sums[:gain_part, gain_at + 1],
        jnp.swapaxes(final(0), 1, 2),
        jnp.swapaxes(final(1), 1, 2),
        final(2),
    )


def solution(mesh):
    in_specs = (
        P(("rows", "cols"), None),
        P("rows", "cols"),
        P("rows", "cols"),
        P("rows", "cols"),
        P("rows", "cols"),
        P("rows", "cols"),
        P(("rows", "cols")),
        P(("rows", "cols")),
        P("rows", None, "cols"),
        P("rows", None, "cols"),
        P("rows", "cols", None),
        P(("rows", "cols"), None),
        P(),
        P(("rows", "cols"), None),
    )
    out_specs = (
        P(("rows", "cols"), None),
        P(("rows", "cols"), None),
        P("rows", "cols"),
        P("rows", "cols"),
        P("rows", "cols"),
        P("rows", "cols"),
        P("rows", "cols"),
        P(("rows", "cols")),
        P(("rows", "cols")),
        P("rows", None, "cols"),
        P("rows", None, "cols"),
        P("rows", "cols", None),
    )
    return jax.shard_map(
        on_device, mesh=mesh, in_specs=in_specs, out_specs=out_specs, check_vma=False
    )
```

```python
import jax
import jax.numpy as jnp
from jax import lax
from jax.sharding import PartitionSpec as P

D = 1536
HEADS = 12
KV_HEADS = 2
HEAD_DIM = 128
TOP = 4
TOK_DEV = 512
BRANCHES = 4
LEAVES = 8
TRUNK = 256
BRANCH = 64


EPSILON = 1e-06
ROPE_BASE = 10000.0
MASKED = -1e30
HIGHEST = lax.Precision.HIGHEST


def rms_norm(values, norm_gain):
    factor = lax.rsqrt(jnp.mean(values * values, axis=-1, keepdims=True) + EPSILON)
    return values * factor * norm_gain


def segment_of(token_index):
    branch_part = 1 + (token_index - TRUNK) // BRANCH
    leaf_part = 1 + BRANCHES + (token_index - TOK_DEV) // BRANCH
    return jnp.where(
        token_index < TRUNK, 0, jnp.where(token_index < TOK_DEV, branch_part, leaf_part)
    )


def position_of(token_index):
    branch_place = TRUNK + (token_index - TRUNK) % BRANCH
    leaf_place = TRUNK + BRANCH + (token_index - TOK_DEV) % BRANCH
    return jnp.where(
        token_index < TRUNK, token_index, jnp.where(token_index < TOK_DEV, branch_place, leaf_place)
    )


def path_mask(query_index, key_index, parent_row):
    query_part = segment_of(query_index)
    key_part = segment_of(key_index)
    leaf_slot = query_part - 1 - BRANCHES
    leaf_match = leaf_slot[:, None] == jnp.arange(LEAVES, dtype=jnp.int32)[None, :]
    ancestor = jnp.where(
        query_part > BRANCHES, 1 + jnp.sum(jnp.where(leaf_match, parent_row[None, :], 0), axis=1), 0
    )
    reachable = (
        (key_part[None, :] == query_part[:, None])
        | (key_part[None, :] == 0)
        | (key_part[None, :] == ancestor[:, None])
    )
    return reachable & (key_index[None, :] <= query_index[:, None])


def rotary_tables(positions):
    half_dim = HEAD_DIM // 2
    frequency = ROPE_BASE ** (-jnp.arange(half_dim, dtype=jnp.float32) / half_dim)
    angles = positions.astype(jnp.float32)[:, None] * frequency[None, :]
    return (jnp.cos(angles)[:, None, :], jnp.sin(angles)[:, None, :])


def rotate(values, cosine, sine_table):
    half_dim = HEAD_DIM // 2
    first_half = values[..., :half_dim]
    second_half = values[..., half_dim:]
    return jnp.concatenate(
        [
            first_half * cosine - second_half * sine_table,
            second_half * cosine + first_half * sine_table,
        ],
        axis=-1,
    )


def after(values, *earlier):
    return lax.optimization_barrier((values, earlier))[0]


def take(block, index):
    return lax.dynamic_index_in_dim(block, index, 0, keepdims=False)


def pick(table, place):
    return jnp.asarray(table, jnp.int32)[place]


SLOT_SHARD = ((0, 2, 1, 3), (1, 3, 0, 2), (2, 0, 1, 3), (3, 1, 2, 0))


def slot_shards():
    count = lax.axis_size("cols")
    if count == 4:
        return pick(SLOT_SHARD, lax.axis_index("cols"))
    return jnp.arange(count, dtype=jnp.int32)


def gather_start(block):
    if lax.axis_size("cols") != 4:
        return (block, block, block)
    above = lax.ppermute(block, "cols", [(1, 0), (2, 1), (3, 2)])
    below = lax.ppermute(block, "cols", [(0, 1), (1, 2), (2, 3)])
    far = lax.ppermute(block, "cols", [(0, 3), (3, 0)])
    return (above, below, far)


def gather_slots(block, first=None):
    count = lax.axis_size("cols")
    if count != 4:
        whole = lax.all_gather(block, "cols", axis=0)
        return [whole[i] for i in range(count)]
    place = lax.axis_index("cols")
    if first is None:
        first = gather_start(block)
    above, below, far = first
    payload = jnp.where(place == 1, above, jnp.where(place == 2, below, block))
    second = lax.ppermute(payload, "cols", [(3, 1), (1, 0), (0, 2), (2, 3)])
    end = (place == 0) | (place == 3)
    return [
        block,
        second,
        jnp.where(place == 0, above, below),
        jnp.where(end, far, above),
    ]


def reduce_slots(slots, marks=None):
    count = lax.axis_size("cols")
    if count != 4:
        whole = jnp.stack(slots).astype(jnp.bfloat16)
        if marks is not None:
            marks.append((slots[0],) * 4)
        return lax.psum_scatter(whole, "cols", scatter_dimension=0).astype(jnp.float32)
    place = lax.axis_index("cols")
    own, second, third, fourth = slots
    end = (place == 0) | (place == 3)
    relay = lax.ppermute(second, "cols", [(1, 3), (0, 1), (2, 0), (3, 2)])
    far = lax.ppermute(fourth, "cols", [(0, 3), (3, 0)])
    relayed = relay.astype(jnp.float32)
    upward_load = (
        jnp.where(place == 0, third, fourth).astype(jnp.float32)
        + jnp.where(place == 1, relayed, 0.0)
    ).astype(jnp.bfloat16)
    downward_load = (third.astype(jnp.float32) + jnp.where(place == 2, relayed, 0.0)).astype(
        jnp.bfloat16
    )
    below = lax.ppermute(upward_load, "cols", [(0, 1), (1, 2), (2, 3)])
    above = lax.ppermute(downward_load, "cols", [(1, 0), (2, 1), (3, 2)])
    if marks is not None:
        marks.append((relay, far, below, above))
    return (
        own.astype(jnp.float32)
        + below.astype(jnp.float32)
        + above.astype(jnp.float32)
        + jnp.where(end, relayed + far.astype(jnp.float32), 0.0)
    )


def flip(block, bit):
    count = lax.axis_size("rows")
    return lax.ppermute(block, "rows", [(i, i ^ bit) for i in range(count)])


def gather_rows(block):
    count = lax.axis_size("rows")
    if count != 8:
        return lax.all_gather(block, "rows", axis=0)
    place = lax.axis_index("rows")
    core, side, level = place % 2, place // 2 % 2, place // 4
    half = block.shape[0] // 2
    beside = flip(block, 2)
    across = flip(block, 4)
    corner = jnp.concatenate([flip(beside[:half], 4), flip(across[half:], 2)], axis=0)
    near = [jnp.where(side == 0, block, beside), jnp.where(side == 0, beside, block)]
    away = [jnp.where(side == 0, across, corner), jnp.where(side == 0, corner, across)]
    same = jnp.stack(
        [jnp.where(level == 0, near[i], away[i]) for i in range(2)]
        + [jnp.where(level == 0, away[i], near[i]) for i in range(2)]
    )
    other = flip(same, 1)
    both = jnp.stack([jnp.where(core == 0, same, other), jnp.where(core == 0, other, same)], axis=1)
    return both.reshape((count,) + block.shape)


def reduce_rows(blocks):
    count = lax.axis_size("rows")
    if count != 8:
        return lax.psum_scatter(blocks, "rows", scatter_dimension=0).astype(jnp.float32)
    place = lax.axis_index("rows")
    core, side, level = place % 2, place // 2 % 2, place // 4
    half = blocks.shape[1] // 2
    rest = blocks.shape[1:]

    def own_of(array, axis, index):
        return lax.dynamic_index_in_dim(array, index, axis, keepdims=False)

    def add(array, axis, index, bit):
        arrived = flip(own_of(array, axis, 1 - index), bit)
        return own_of(array, axis, index).astype(jnp.float32) + arrived.astype(jnp.float32)

    chips = add(blocks.reshape((2, 2, 2) + rest), 2, core, 1).astype(jnp.bfloat16)
    first = add(chips[:, :, :half], 1, side, 2).astype(jnp.bfloat16)
    second = add(chips[:, :, half:], 0, level, 4).astype(jnp.bfloat16)
    return jnp.concatenate([add(first, 0, level, 4), add(second, 0, side, 2)], axis=0)


def on_device(
    tokens,
    query_weight,
    key_weight,
    value_weight,
    out_weight,
    router_weight,
    attention_gain,
    experts_gain,
    gate_weight,
    upward_weight,
    down_weight,
    routes,
    leaf_parent,
    cotangent,
):
    row_count = lax.axis_size("rows")
    col_count = lax.axis_size("cols")
    row_place = lax.axis_index("rows")
    col_place = lax.axis_index("cols")
    parity = col_place % 2
    tree_id = (row_place * col_count + col_place) // 2
    parent_row = lax.dynamic_slice_in_dim(leaf_parent, tree_id, 1, 0)[0]
    key_width = KV_HEADS * HEAD_DIM
    query_width = HEADS * HEAD_DIM
    group_size = HEADS // KV_HEADS
    depth, query_part = query_weight.shape
    key_part = key_weight.shape[1]
    router_part = router_weight.shape[1]
    gain_part = attention_gain.shape[0]
    expert_total = router_part * col_count
    local_experts = gate_weight.shape[0]
    capacity = TOK_DEV * TOP // expert_total * 5 // 4
    spare = 128

    extras = jnp.concatenate(
        [
            router_weight,
            jnp.pad(attention_gain, (0, depth - gain_part))[:, None],
            jnp.pad(experts_gain, (0, depth - gain_part))[:, None],
            jnp.zeros((depth, spare - router_part - 2), jnp.bfloat16),
        ],
        axis=1,
    )
    packed = jnp.concatenate([query_weight, key_weight, value_weight, out_weight, extras], axis=1)
    packed_width = packed.shape[1]
    packed_first = gather_start(packed)
    packed_slots = jnp.stack(gather_slots(packed, packed_first))
    shards = slot_shards()
    slot_of_shard = jnp.argsort(shards)
    packed_cols = jnp.take(packed_slots, slot_of_shard, axis=0)
    packed_all = gather_rows(packed_cols.reshape(col_count * depth, packed_width)).reshape(
        row_count, col_count, depth, packed_width
    )

    def unpack(start, width):
        part = packed_all[..., start : start + width]
        return jnp.swapaxes(part, 1, 2).reshape(row_count * depth, col_count * width)

    key_at = query_part
    value_at = key_at + key_part
    out_at = value_at + key_part
    extra_at = out_at + query_part
    query_full = unpack(0, query_part)
    key_full = unpack(key_at, key_part)
    value_full = unpack(value_at, key_part)
    out_full = unpack(out_at, query_part)
    router_full = unpack(extra_at, router_part)
    gain_at = extra_at + router_part
    attention_full = packed_all[:, :, :gain_part, gain_at].reshape(-1)
    experts_full = packed_all[:, :, :gain_part, gain_at + 1].reshape(-1)

    shard_blocks = [
        jnp.stack([gate_weight[expert].T, upward_weight[expert].T, down_weight[expert]], axis=0)
        for expert in range(local_experts)
    ]
    arrivals, expert_slots = ([], [])
    ahead = packed_first
    for expert in range(local_experts):
        block = after(shard_blocks[expert], *ahead)
        first = gather_start(block)
        slots = gather_slots(block, first)
        arrivals.append((first, slots[1]))
        expert_slots.append(slots)
        ahead = first

    routes_all = lax.all_gather(routes, "rows", axis=0)
    grad_all = lax.all_gather(cotangent, "rows", axis=0)

    token_float = tokens.astype(jnp.float32)
    attention_scale = attention_full.astype(jnp.float32)
    normed = rms_norm(token_float, attention_scale)
    normed_low = normed.astype(jnp.bfloat16)
    normed_low = after(normed_low, *arrivals[0][0])
    query_lin = jnp.dot(normed_low, query_full, preferred_element_type=jnp.float32)
    key_lin = jnp.dot(normed_low, key_full, preferred_element_type=jnp.float32)
    value_low = jnp.dot(normed_low, value_full, preferred_element_type=jnp.float32).astype(
        jnp.bfloat16
    )
    holds_leaves = parity == 0
    local_index = (1 - parity) * TOK_DEV + jnp.arange(TOK_DEV, dtype=jnp.int32)
    cosine, sine_table = rotary_tables(position_of(local_index))
    query_low = rotate(query_lin.reshape(TOK_DEV, HEADS, HEAD_DIM), cosine, sine_table).astype(
        jnp.bfloat16
    )
    key_low = (
        rotate(key_lin.reshape(TOK_DEV, KV_HEADS, HEAD_DIM), cosine, sine_table)
        .astype(jnp.bfloat16)
        .reshape(TOK_DEV, key_width)
    )
    pairs = [(i + 1, i) for i in range(0, col_count, 2)]
    own_pair = jnp.concatenate([key_low, value_low], axis=1)
    partner = lax.ppermute(own_pair, "cols", pairs)
    tree_rows = jnp.concatenate(
        [
            jnp.where(holds_leaves, partner, own_pair),
            jnp.where(holds_leaves, own_pair, jnp.zeros_like(own_pair)),
        ],
        axis=0,
    )
    key_tree = tree_rows[:, :key_width].reshape(2 * TOK_DEV, KV_HEADS, HEAD_DIM)
    value_tree = tree_rows[:, key_width:].reshape(2 * TOK_DEV, KV_HEADS, HEAD_DIM)
    key_index = jnp.arange(2 * TOK_DEV, dtype=jnp.int32)
    factor = HEAD_DIM ** (-0.5)
    query_low = after(query_low, arrivals[0][1])
    query_group = query_low.reshape(TOK_DEV, KV_HEADS, group_size, HEAD_DIM)
    allowed = path_mask(local_index, key_index, parent_row)

    def block_scores():
        scores = (
            jnp.einsum("qkgd,skd->kgqs", query_group, key_tree, preferred_element_type=jnp.float32)
            * factor
        )
        return jnp.where(allowed[None, None], scores, MASKED)

    scores = block_scores()
    highest = jnp.max(scores, axis=-1, keepdims=True)
    weights = jnp.exp(scores - highest)
    totals = jnp.sum(weights, axis=-1, keepdims=True)
    attention = (weights / totals).astype(jnp.bfloat16)
    mixed_heads = jnp.einsum(
        "kgqs,skd->qkgd", attention, value_tree, preferred_element_type=jnp.float32
    )
    log_total = highest + jnp.log(totals)
    heads_low = mixed_heads.reshape(TOK_DEV, query_width).astype(jnp.bfloat16)
    heads_low = after(heads_low, arrivals[1][0][0], arrivals[1][0][1])
    residual = token_float + jnp.dot(heads_low, out_full, preferred_element_type=jnp.float32)
    experts_scale = experts_full.astype(jnp.float32)
    normed_two = rms_norm(residual, experts_scale)
    normed_two_low = normed_two.astype(jnp.bfloat16)
    normed_all = lax.all_gather(normed_two_low, "rows", axis=0)

    expert_ids = jnp.arange(expert_total, dtype=jnp.int32)

    def shares(chosen_of, logit_cols):
        softmax_out = jax.nn.softmax(logit_cols, axis=-2)
        return softmax_out / jnp.sum(
            jnp.where(chosen_of, softmax_out, 0.0), axis=-2, keepdims=True
        )

    own_ids = row_place * local_experts + jnp.arange(local_experts, dtype=jnp.int32)
    named = routes_all[:, :, :, None] == expert_ids[None, None, None, :]
    named = jnp.swapaxes(jnp.any(named, axis=2), 1, 2)
    logits_all = jnp.einsum(
        "de,rtd->ret", router_full, normed_all, preferred_element_type=jnp.float32
    )
    share_all = shares(named, logits_all)
    own_at = row_place * local_experts
    hit = lax.dynamic_slice_in_dim(named, own_at, local_experts, 1)
    share = lax.dynamic_slice_in_dim(share_all, own_at, local_experts, 1)
    earlier = jnp.arange(TOK_DEV)[:, None] < jnp.arange(TOK_DEV)[None, :]
    rank = jnp.einsum(
        "rlt,tu->rlu",
        hit.astype(jnp.bfloat16),
        earlier.astype(jnp.bfloat16),
        preferred_element_type=jnp.float32,
    ).astype(jnp.int32)
    place_ids = jnp.arange(capacity, dtype=jnp.int32)
    onehot = (hit[:, :, None, :] & (rank[:, :, None, :] == place_ids[None, None, :, None])).astype(
        jnp.bfloat16
    )
    share_rows = jnp.sum(
        onehot.astype(jnp.float32) * jnp.where(hit, share, 0.0)[:, :, None, :], axis=-1
    )
    token_rows = jnp.einsum("rlct,rtd->lrcd", onehot, normed_all).reshape(
        local_experts, row_count * capacity, D
    )
    grad_rows = jnp.einsum("rlct,rtd->lrcd", onehot, grad_all).reshape(
        local_experts, row_count * capacity, D
    )
    share_rows = jnp.swapaxes(share_rows, 0, 1).reshape(local_experts, row_count * capacity, 1)

    out_rows, back_rows, gate_dots, reduced, marks = ([], [], [], [], [])
    for expert in range(local_experts):
        weights_all = jnp.stack(expert_slots[expert], axis=1).reshape(3, -1, D)
        gate_full, upward_full, down_full = (weights_all[0], weights_all[1], weights_all[2])
        row_block = token_rows[expert]
        if marks:
            row_block = after(row_block, marks[0][0])
        grad_block = grad_rows[expert].astype(jnp.float32)
        grad_expert = (share_rows[expert] * grad_block).astype(jnp.bfloat16)

        def dot(one, two, dims):
            return lax.dot_general(
                one, two, (dims, ((), ())), preferred_element_type=jnp.float32
            )

        gate_act = dot(row_block, gate_full, ((1,), (1,)))
        upward = dot(row_block, upward_full, ((1,), (1,)))
        silu_gate = jax.nn.silu(gate_act)
        hidden_low = (silu_gate * upward).astype(jnp.bfloat16)
        expert_out = dot(hidden_low, down_full, ((1,), (0,))).astype(jnp.bfloat16)
        grad_hidden = dot(grad_expert, down_full, ((1,), (1,)))
        sigmoid_gate = jax.nn.sigmoid(gate_act)
        grad_gate_act = (
            grad_hidden * upward * sigmoid_gate * (1.0 + gate_act * (1.0 - sigmoid_gate))
        ).astype(jnp.bfloat16)
        grad_upward = (grad_hidden * silu_gate).astype(jnp.bfloat16)
        down_grad = dot(hidden_low, grad_expert, ((0,), (0,)))
        gate_grad = dot(grad_gate_act, row_block, ((0,), (0,)))
        upward_grad = dot(grad_upward, row_block, ((0,), (0,)))
        slots = [
            jnp.stack(
                [
                    grad.astype(jnp.bfloat16).reshape(col_count, -1, D)[i]
                    for grad in (gate_grad, upward_grad, down_grad)
                ]
            )
            for i in range(col_count)
        ]
        if marks:
            slots = [after(slot, marks[0][0], marks[0][1]) for slot in slots]
        reduced.append(reduce_slots(slots, marks))
        grad_route_in = (
            dot(grad_gate_act, gate_full, ((1,), (0,)))
            + dot(grad_upward, upward_full, ((1,), (0,)))
        ).astype(jnp.bfloat16)
        out_float = expert_out.astype(jnp.float32)
        out_rows.append((share_rows[expert] * out_float).astype(jnp.bfloat16))
        back_rows.append(grad_route_in)
        gate_dots.append(jnp.sum(grad_block * out_float, axis=-1))

    out_rows = jnp.stack(out_rows).reshape(local_experts, row_count, capacity, D)
    back_rows = jnp.stack(back_rows).reshape(local_experts, row_count, capacity, D)
    gate_dots = jnp.stack(gate_dots).reshape(local_experts, row_count, capacity)
    grad_share = jnp.einsum(
        "rlct,lrc->rlt", onehot.astype(jnp.float32), gate_dots, precision=HIGHEST
    )
    back_part = jnp.einsum(
        "rlct,lrcd->rtd", onehot, back_rows, preferred_element_type=jnp.float32
    ).astype(jnp.bfloat16)
    out_part = jnp.einsum(
        "rlct,lrcd->rtd", onehot, out_rows, preferred_element_type=jnp.float32
    ).astype(jnp.bfloat16)
    grad_share_all = lax.all_gather(grad_share, "rows", axis=1, tiled=True)
    grad_shares = take(grad_share_all, row_place)
    back_sum = reduce_rows(back_part)
    back_sum = after(back_sum, *marks[0][1:])
    grad_out = cotangent.astype(jnp.float32)

    chosen_of = take(named, row_place)
    logits = take(logits_all, row_place)

    def shares_out(logit_cols):
        return jnp.where(chosen_of, shares(chosen_of, logit_cols), 0.0)

    _, router_pullback = jax.vjp(shares_out, logits)
    (grad_logits,) = router_pullback(grad_shares)
    router_float = router_full.astype(jnp.float32)
    grad_normed_two = back_sum + jnp.einsum(
        "et,de->td", grad_logits, router_float, precision=HIGHEST
    )
    router_grad = jnp.einsum(
        "td,et->de", normed_two_low.astype(jnp.float32), grad_logits, precision=HIGHEST
    )
    second_norm, second_pullback = jax.vjp(rms_norm, residual, experts_scale)
    grad_residual_norm, experts_gain_grad = second_pullback(grad_normed_two)
    grad_residual = grad_out + grad_residual_norm
    grad_branch_low = grad_residual.astype(jnp.bfloat16)
    out_grad = jnp.einsum(
        "tq,td->qd", heads_low, grad_branch_low, preferred_element_type=jnp.float32
    )
    grad_heads_low = jnp.einsum(
        "td,qd->tq", grad_branch_low, out_full, preferred_element_type=jnp.float32
    ).astype(jnp.bfloat16)
    grad_block = grad_heads_low.reshape(TOK_DEV, KV_HEADS, group_size, HEAD_DIM)

    grad_block = after(grad_block, marks[1][0], marks[1][1])
    out_part = after(out_part, back_sum)
    mixture = reduce_rows(out_part)
    layer_output = (residual + mixture).astype(jnp.bfloat16)
    attention = jnp.exp(block_scores() - log_total)
    attention_low = attention.astype(jnp.bfloat16)
    grad_attention = jnp.einsum(
        "qkgd,skd->kgqs", grad_block, value_tree, preferred_element_type=jnp.float32
    )
    grad_scores = (
        attention
        * (grad_attention - jnp.sum(attention * grad_attention, axis=-1, keepdims=True))
    ).astype(jnp.bfloat16)
    grad_query = (
        jnp.einsum("kgqs,skd->qkgd", grad_scores, key_tree, preferred_element_type=jnp.float32)
        * factor
    )
    key_tree_grad = (
        jnp.einsum("kgqs,qkgd->skd", grad_scores, query_group, preferred_element_type=jnp.float32)
        * factor
    ).reshape(2 * TOK_DEV, key_width)
    value_tree_grad = jnp.einsum(
        "kgqs,qkgd->skd", attention_low, grad_block, preferred_element_type=jnp.float32
    ).reshape(2 * TOK_DEV, key_width)
    tree_grads = jnp.concatenate([key_tree_grad, value_tree_grad], axis=1)
    tree_grads = after(tree_grads, mixture)
    arrived = lax.ppermute(
        tree_grads[:TOK_DEV].astype(jnp.bfloat16), "cols", [(j, i) for i, j in pairs]
    ).astype(jnp.float32)
    own_grads = jnp.where(holds_leaves, tree_grads[TOK_DEV:], tree_grads[:TOK_DEV] + arrived)
    grad_key_rot = own_grads[:, :key_width].reshape(TOK_DEV, KV_HEADS, HEAD_DIM)
    grad_key_low = (
        rotate(grad_key_rot, cosine, -sine_table).reshape(TOK_DEV, key_width).astype(jnp.bfloat16)
    )
    grad_value_low = own_grads[:, key_width:].astype(jnp.bfloat16)
    grad_query_low = (
        rotate(grad_query.reshape(TOK_DEV, HEADS, HEAD_DIM), cosine, -sine_table)
        .reshape(TOK_DEV, query_width)
        .astype(jnp.bfloat16)
    )
    query_grad = jnp.einsum(
        "td,tq->dq", normed_low, grad_query_low, preferred_element_type=jnp.float32
    )
    key_grad = jnp.einsum("td,tq->dq", normed_low, grad_key_low, preferred_element_type=jnp.float32)
    value_grad = jnp.einsum(
        "td,tq->dq", normed_low, grad_value_low, preferred_element_type=jnp.float32
    )
    grad_normed = (
        jnp.einsum("tq,dq->td", grad_query_low, query_full, preferred_element_type=jnp.float32)
        + jnp.einsum("tq,dq->td", grad_key_low, key_full, preferred_element_type=jnp.float32)
        + jnp.einsum("tq,dq->td", grad_value_low, value_full, preferred_element_type=jnp.float32)
    )
    first_norm, first_pullback = jax.vjp(rms_norm, token_float, attention_scale)
    grad_tokens_norm, attention_gain_grad = first_pullback(grad_normed)
    tokens_grad = (grad_residual + grad_tokens_norm).astype(jnp.bfloat16)

    def by_shard(grad, width):
        parts = grad.astype(jnp.bfloat16).reshape(row_count, depth, col_count, width)
        return jnp.swapaxes(parts, 1, 2)

    def gain_shard(grad):
        parts = grad.astype(jnp.bfloat16).reshape(row_count, col_count, gain_part)
        return jnp.pad(parts, ((0, 0), (0, 0), (0, depth - gain_part)))[..., None]

    packed_grad = jnp.concatenate(
        [
            by_shard(query_grad, query_part),
            by_shard(key_grad, key_part),
            by_shard(value_grad, key_part),
            by_shard(out_grad, query_part),
            by_shard(router_grad, router_part),
            gain_shard(attention_gain_grad),
            gain_shard(experts_gain_grad),
            jnp.zeros((row_count, col_count, depth, spare - router_part - 2), jnp.bfloat16),
        ],
        axis=-1,
    )
    packed_grad = after(packed_grad, marks[1][2], marks[1][3])
    row_sums = reduce_rows(packed_grad.reshape(row_count, col_count * depth, packed_width))
    row_sums = row_sums.astype(jnp.bfloat16).reshape(col_count, depth, packed_width)
    row_slots = jnp.take(row_sums, shards, axis=0)
    sums = reduce_slots([row_slots[i] for i in range(col_count)])

    def final(which):
        return jnp.stack([reduced[expert][which] for expert in range(local_experts)])

    return (
        layer_output,
        tokens_grad,
        sums[:, :key_at],
        sums[:, key_at:value_at],
        sums[:, value_at:out_at],
        sums[:, out_at:extra_at],
        sums[:, extra_at:gain_at],
        sums[:gain_part, gain_at],
        sums[:gain_part, gain_at + 1],
        jnp.swapaxes(final(0), 1, 2),
        jnp.swapaxes(final(1), 1, 2),
        final(2),
    )


def solution(mesh):
    in_specs = (
        P(("rows", "cols"), None),
        P("rows", "cols"),
        P("rows", "cols"),
        P("rows", "cols"),
        P("rows", "cols"),
        P("rows", "cols"),
        P(("rows", "cols")),
        P(("rows", "cols")),
        P("rows", None, "cols"),
        P("rows", None, "cols"),
        P("rows", "cols", None),
        P(("rows", "cols"), None),
        P(),
        P(("rows", "cols"), None),
    )
    out_specs = (
        P(("rows", "cols"), None),
        P(("rows", "cols"), None),
        P("rows", "cols"),
        P("rows", "cols"),
        P("rows", "cols"),
        P("rows", "cols"),
        P("rows", "cols"),
        P(("rows", "cols")),
        P(("rows", "cols")),
        P("rows", None, "cols"),
        P("rows", None, "cols"),
        P("rows", "cols", None),
    )
    return jax.shard_map(
        on_device, mesh=mesh, in_specs=in_specs, out_specs=out_specs, check_vma=False
    )
```

```python
import functools

import jax
import jax.numpy as jnp
from jax import lax
from jax.experimental import pallas as pl
from jax.experimental.pallas import tpu as pltpu
from jax.sharding import PartitionSpec as P

D = 1536
HEADS = 12
KV_HEADS = 2
HEAD_DIM = 128
TOP = 4
TOK_DEV = 512
BRANCHES = 4
LEAVES = 8
TRUNK = 256
BRANCH = 64

EPSILON = 1e-06
ROPE_BASE = 10000.0
MASKED = -1e30
LOW = jnp.bfloat16
WIDE = jnp.float32
KEY_WIDTH = KV_HEADS * HEAD_DIM
GROUP = HEADS // KV_HEADS
QUARTERS = 4
VMEM_LIMIT = 56 * 1024 * 1024

ANY = pl.BlockSpec(memory_space=pl.ANY)
SMEM = pl.BlockSpec(memory_space=pltpu.SMEM)


def nn(one, two):
    return lax.dot_general(one, two, (((1,), (0,)), ((), ())), preferred_element_type=WIDE)


def nt(one, two):
    return lax.dot_general(one, two, (((1,), (1,)), ((), ())), preferred_element_type=WIDE)


def tn(one, two):
    return lax.dot_general(one, two, (((0,), (0,)), ((), ())), preferred_element_type=WIDE)


def whole(shape):
    return pl.BlockSpec(shape, lambda *_: (0,) * len(shape))


def params():
    return pltpu.CompilerParams(vmem_limit_bytes=VMEM_LIMIT)


def turn(values, cosine, sine):
    return values * cosine + pltpu.roll(values, HEAD_DIM // 2, 1) * sine


def turn_back(values, cosine, sine):
    return values * cosine - pltpu.roll(values, HEAD_DIM // 2, 1) * sine


PIECES = tuple(
    (flip_bits + core, first, count)
    for core in (0, 1)
    for flip_bits, first, count in ((0, 0, 4), (2, 0, 4), (4, 0, 4), (6, 0, 2), (6, 2, 2))
)


def weight_copies(info, refs, target, sem, start, width):
    if len(refs) == 1:
        return [pltpu.make_async_copy(refs[0], target, sem)]
    depth = refs[0].shape[1]
    copies = []
    for ref, (flip_bits, first, count) in zip(refs, PIECES):
        row = pl.multiple_of((info[0] ^ flip_bits) * depth, depth)
        for slot in range(count):
            col = pl.multiple_of(info[2 + first + slot] * width, 128)
            copies.append(
                pltpu.make_async_copy(
                    ref.at[slot, :, pl.ds(start, width)],
                    target.at[pl.ds(row, depth), pl.ds(col, width)],
                    sem,
                )
            )
    return copies


def run_all(copies):
    for copy in copies:
        copy.start()


def wait_all(copies):
    for copy in copies:
        copy.wait()


def key_value_kernel(info, tokens, gain, cosine, sine, *rest):
    count = len(rest) - 4
    refs, (normed, out, weight, sem) = rest[:count], rest[count:]
    copies = weight_copies(info, refs, weight, sem, D // QUARTERS, 128)
    run_all(copies)
    values = tokens[...].astype(WIDE)
    factor = lax.rsqrt(jnp.mean(values * values, axis=-1, keepdims=True) + EPSILON)
    low = (values * factor * gain[...]).astype(LOW)
    normed[...] = low
    wait_all(copies)
    both = nn(low, weight[...])
    half = HEAD_DIM // 2
    first = lax.broadcasted_iota(jnp.int32, (TOK_DEV, HEAD_DIM), 1) < half
    for g in range(KV_HEADS):
        one = both[:, 256 * g : 256 * g + 128]
        two = both[:, 256 * g + 128 : 256 * g + 256]
        key = jnp.where(first, one, pltpu.roll(two, half, 1))
        value = jnp.where(first, pltpu.roll(one, half, 1), two)
        out[:, 128 * g : 128 * g + 128] = turn(key, cosine[...], sine[...]).astype(LOW)
        out[:, KEY_WIDTH + 128 * g : KEY_WIDTH + 128 * g + 128] = value.astype(LOW)


def key_value(info, tokens, gain, cosine, sine, refs):
    return pl.pallas_call(
        key_value_kernel,
        out_shape=(
            jax.ShapeDtypeStruct((TOK_DEV, D), LOW),
            jax.ShapeDtypeStruct((TOK_DEV, 2 * KEY_WIDTH), LOW),
        ),
        in_specs=[SMEM] + [pl.BlockSpec(memory_space=pltpu.VMEM)] * 4 + [ANY] * len(refs),
        out_specs=(pl.BlockSpec(memory_space=pltpu.VMEM),) * 2,
        scratch_shapes=[pltpu.VMEM((D, 2 * KEY_WIDTH), LOW), pltpu.SemaphoreType.DMA],
        compiler_params=params(),
        name="norm_key_value",
    )(info, tokens, gain, cosine, sine, *refs)


def query_kernel(info, normed, cosine, sine, *rest):
    count = len(rest) - 3
    refs, (out, weight, sem) = rest[:count], rest[count:]

    @pl.when(pl.program_id(0) == 0)
    def _():
        copies = weight_copies(info, refs, weight, sem, 0, D // QUARTERS)
        run_all(copies)
        wait_all(copies)

    at = pl.multiple_of(pl.program_id(0) * 256, 256)
    lin = nn(normed[...], weight[:, pl.ds(at, 256)])
    for h in range(2):
        out[:, 128 * h : 128 * h + 128] = turn(
            lin[:, 128 * h : 128 * h + 128], cosine[...], sine[...]
        ).astype(LOW)


def query(info, normed, cosine, sine, refs):
    return pl.pallas_call(
        query_kernel,
        grid=(D // 256,),
        out_shape=jax.ShapeDtypeStruct((TOK_DEV, D), LOW),
        in_specs=[SMEM, whole((TOK_DEV, D)), whole((TOK_DEV, 128)), whole((TOK_DEV, 128))]
        + [ANY] * len(refs),
        out_specs=pl.BlockSpec((TOK_DEV, 256), lambda i: (0, i)),
        scratch_shapes=[pltpu.VMEM((D, D), LOW), pltpu.SemaphoreType.DMA],
        compiler_params=params(),
        name="query_projection",
    )(info, normed, cosine, sine, *refs)


KEYS = TRUNK + 2 * BRANCH
CHUNKS = TOK_DEV // BRANCH


def chunk_keys(info, source, own, column, chunk):
    at = pl.multiple_of(info[6 + chunk], BRANCH)
    rows = pl.multiple_of(chunk * BRANCH, BRANCH)
    columns = slice(column, column + HEAD_DIM)
    return jnp.concatenate(
        [
            source[0:TRUNK, columns],
            source[pl.ds(at, BRANCH), columns],
            own[pl.ds(rows, BRANCH), columns],
        ],
        axis=0,
    )


def chunk_allowed(info, chunk, query_axis, shape):
    query_row = lax.broadcasted_iota(jnp.int32, shape, query_axis) & (BRANCH - 1)
    key = lax.broadcasted_iota(jnp.int32, shape, 1 - query_axis)
    leaves = info[1] == 0
    trunk = jnp.logical_and(jnp.logical_not(leaves), chunk < TRUNK // BRANCH)
    limit = jnp.where(trunk, chunk * BRANCH + query_row, TRUNK - 1)
    branch_limit = jnp.where(leaves, TRUNK + BRANCH - 1, 0)
    own_limit = jnp.where(trunk, 0, query_row + TRUNK + BRANCH)
    top = jnp.where(key < TRUNK, limit, jnp.where(key < TRUNK + BRANCH, branch_limit, own_limit))
    return key <= top


def group_rows(ref, g):
    first = g * GROUP
    return jnp.concatenate(
        [ref[:, 128 * h : 128 * h + 128] for h in range(first, first + GROUP)], axis=0
    )


def keep_source(info, partner, own, source):
    @pl.when(pl.program_id(0) == 0)
    def _():
        @pl.when(info[1] == 0)
        def _():
            source[...] = partner[...]

        @pl.when(info[1] != 0)
        def _():
            source[...] = own[...]


def attention_kernel(info, queries, own, partner, out, source):
    keep_source(info, partner, own, source)
    chunk = pl.program_id(0)
    rows = GROUP * BRANCH
    allowed = chunk_allowed(info, chunk, 0, (rows, KEYS))
    for g in range(KV_HEADS):
        keys = chunk_keys(info, source, own, 128 * g, chunk)
        values = chunk_keys(info, source, own, KEY_WIDTH + 128 * g, chunk)
        scores = nt(group_rows(queries, g), keys) * HEAD_DIM**-0.5
        scores = jnp.where(allowed, scores, MASKED)
        weights = jnp.exp(scores - jnp.max(scores, axis=1, keepdims=True))
        total = jnp.sum(weights, axis=1, keepdims=True)
        mixed = nn((weights * (1.0 / total)).astype(LOW), values).astype(LOW)
        for h in range(GROUP):
            at = (g * GROUP + h) * 128
            out[:, at : at + 128] = mixed[h * BRANCH : (h + 1) * BRANCH]


def attention(info, queries, own, partner):
    return pl.pallas_call(
        attention_kernel,
        grid=(CHUNKS,),
        out_shape=jax.ShapeDtypeStruct((TOK_DEV, D), LOW),
        in_specs=[
            SMEM,
            pl.BlockSpec((BRANCH, D), lambda i: (i, 0)),
            whole((TOK_DEV, 2 * KEY_WIDTH)),
            whole((TOK_DEV, 2 * KEY_WIDTH)),
        ],
        out_specs=pl.BlockSpec((BRANCH, D), lambda i: (i, 0)),
        scratch_shapes=[pltpu.VMEM((TOK_DEV, 2 * KEY_WIDTH), LOW)],
        compiler_params=params(),
        name="tree_attention",
    )(info, queries, own, partner)


def attention_back_kernel(
    info, queries, own, partner, grads, cosine, sine, grad_query, own_grad, source_grad, source
):
    keep_source(info, partner, own, source)
    chunk = pl.program_id(0)

    @pl.when(chunk == 0)
    def _():
        source_grad[...] = jnp.zeros_like(source_grad)

    rows = GROUP * BRANCH
    scale = HEAD_DIM**-0.5
    allowed = chunk_allowed(info, chunk, 1, (KEYS, rows))
    at = pl.multiple_of(info[6 + chunk], BRANCH)
    for g in range(KV_HEADS):
        keys = chunk_keys(info, source, own, 128 * g, chunk)
        values = chunk_keys(info, source, own, KEY_WIDTH + 128 * g, chunk)
        query_rows = group_rows(queries, g)
        grad_rows = group_rows(grads, g)
        scores = jnp.where(allowed, nt(keys, query_rows) * scale, MASKED)
        weights = jnp.exp(scores - jnp.max(scores, axis=0, keepdims=True))
        probs = weights * (1.0 / jnp.sum(weights, axis=0, keepdims=True))
        grad_probs = nt(values, grad_rows)
        mean = jnp.sum(probs * grad_probs, axis=0, keepdims=True)
        grad_scores = (probs * (grad_probs - mean)).astype(LOW)
        grad_values = nn(probs.astype(LOW), grad_rows)
        grad_keys = nn(grad_scores, query_rows) * scale
        grad_queries = tn(grad_scores, keys) * scale
        for h in range(GROUP):
            to = (g * GROUP + h) * 128
            grad_query[:, to : to + 128] = turn_back(
                grad_queries[h * BRANCH : (h + 1) * BRANCH], cosine[...], sine[...]
            ).astype(LOW)
        for column, grad in ((128 * g, grad_keys), (KEY_WIDTH + 128 * g, grad_values)):
            columns = slice(column, column + 128)
            source_grad[0:TRUNK, columns] += grad[0:TRUNK]
            source_grad[pl.ds(at, BRANCH), columns] += grad[TRUNK : TRUNK + BRANCH]
            own_grad[:, columns] = grad[TRUNK + BRANCH :]


def attention_back(info, queries, own, partner, grads, cosine, sine):
    chunked = pl.BlockSpec((BRANCH, D), lambda i: (i, 0))
    pair = (TOK_DEV, 2 * KEY_WIDTH)
    return pl.pallas_call(
        attention_back_kernel,
        grid=(CHUNKS,),
        out_shape=(
            jax.ShapeDtypeStruct((TOK_DEV, D), LOW),
            jax.ShapeDtypeStruct(pair, WIDE),
            jax.ShapeDtypeStruct(pair, WIDE),
        ),
        in_specs=[
            SMEM,
            chunked,
            whole(pair),
            whole(pair),
            chunked,
            pl.BlockSpec((BRANCH, 128), lambda i: (i, 0)),
            pl.BlockSpec((BRANCH, 128), lambda i: (i, 0)),
        ],
        out_specs=(
            chunked,
            pl.BlockSpec((BRANCH, 2 * KEY_WIDTH), lambda i: (i, 0)),
            whole(pair),
        ),
        scratch_shapes=[pltpu.VMEM(pair, LOW)],
        compiler_params=params(),
        name="tree_attention_back",
    )(info, queries, own, partner, grads, cosine, sine)


def out_kernel(info, heads, tokens, gain, *rest):
    count = len(rest) - 4
    refs, (residual, normed, weight, sem) = rest[:count], rest[count:]

    @pl.when(pl.program_id(0) == 0)
    def _():
        copies = weight_copies(info, refs, weight, sem, D // QUARTERS + 128, D // QUARTERS)
        run_all(copies)
        wait_all(copies)

    at = pl.ds(pl.multiple_of(pl.program_id(0) * 256, 256), 256)
    residual[:, at] = tokens[:, at].astype(WIDE) + nn(heads[...], weight[:, at])

    @pl.when(pl.program_id(0) == pl.num_programs(0) - 1)
    def _():
        values = residual[...]
        factor = lax.rsqrt(jnp.mean(values * values, axis=-1, keepdims=True) + EPSILON)
        normed[...] = (values * factor * gain[...]).astype(LOW)


def out_projection(info, heads, tokens, gain, refs):
    full = (TOK_DEV, D)
    return pl.pallas_call(
        out_kernel,
        grid=(D // 256,),
        out_shape=(jax.ShapeDtypeStruct(full, WIDE), jax.ShapeDtypeStruct(full, LOW)),
        in_specs=[SMEM, whole(full), whole(full), whole((1, D))] + [ANY] * len(refs),
        out_specs=(whole(full), whole(full)),
        scratch_shapes=[pltpu.VMEM((D, D), LOW), pltpu.SemaphoreType.DMA],
        compiler_params=params(),
        name="out_projection",
    )(info, heads, tokens, gain, *refs)


def dispatch_kernel(capacity, local, info, rows, grads, routes, router, *rest):
    token_outs, grad_outs = rest[:local], rest[local : 2 * local]
    share_outs, logits_out, earlier = rest[2 * local : 3 * local], rest[3 * local], rest[-1]
    total = router.shape[0]

    @pl.when(pl.program_id(0) == 0)
    def _():
        one = lax.broadcasted_iota(jnp.int32, (TOK_DEV, TOK_DEV), 0)
        two = lax.broadcasted_iota(jnp.int32, (TOK_DEV, TOK_DEV), 1)
        earlier[...] = jnp.where(one < two, 1.0, 0.0).astype(LOW)

    block = rows[0]
    logits = nt(router[...], block)
    logits_out[0] = logits
    ids = lax.broadcasted_iota(jnp.int32, (total, TOK_DEV), 0)
    hit = ids == routes[0, 0:1]
    for k in range(1, TOP):
        hit = jnp.logical_or(hit, ids == routes[0, k : k + 1])
    weights = jnp.exp(logits - jnp.max(logits, axis=0, keepdims=True))
    probs = weights / jnp.sum(weights, axis=0, keepdims=True)
    share = probs / jnp.sum(jnp.where(hit, probs, 0.0), axis=0, keepdims=True)
    hits = jnp.where(hit, 1.0, 0.0)
    rank = nn(hits.astype(LOW), earlier[...])
    place = jnp.where(hit, rank, -1.0)
    spots = lax.broadcasted_iota(jnp.int32, (capacity, TOK_DEV), 0).astype(WIDE)
    for e in range(local):
        mine = ids == info[0] * local + e
        place_row = jnp.sum(jnp.where(mine, place, 0.0), axis=0, keepdims=True)
        share_row = jnp.sum(jnp.where(mine, share, 0.0), axis=0, keepdims=True)
        chosen = spots == place_row
        onehot = jnp.where(chosen, 1.0, 0.0).astype(LOW)
        token_outs[e][0] = nn(onehot, block).astype(LOW)
        grad_outs[e][0] = nn(onehot, grads[0]).astype(LOW)
        share_outs[e][0] = jnp.sum(jnp.where(chosen, share_row, 0.0), axis=1, keepdims=True)


def dispatch(info, rows, grads, routes, router, capacity, local):
    count = rows.shape[0]
    total = router.shape[0]
    block = pl.BlockSpec((1, TOK_DEV, D), lambda i: (i, 0, 0))
    picked = pl.BlockSpec((1, capacity, D), lambda i: (i, 0, 0))
    shares = pl.BlockSpec((1, capacity, 1), lambda i: (i, 0, 0))
    return pl.pallas_call(
        functools.partial(dispatch_kernel, capacity, local),
        grid=(count,),
        out_shape=[jax.ShapeDtypeStruct((count, capacity, D), LOW)] * (2 * local)
        + [jax.ShapeDtypeStruct((count, capacity, 1), WIDE)] * local
        + [jax.ShapeDtypeStruct((count, total, TOK_DEV), WIDE)],
        in_specs=[
            SMEM,
            block,
            block,
            pl.BlockSpec((1, TOP, TOK_DEV), lambda i: (i, 0, 0)),
            whole((total, D)),
        ],
        out_specs=[picked] * (2 * local)
        + [shares] * local
        + [pl.BlockSpec((1, total, TOK_DEV), lambda i: (i, 0, 0))],
        scratch_shapes=[pltpu.VMEM((TOK_DEV, TOK_DEV), LOW)],
        compiler_params=params(),
        name="dispatch",
    )(info, rows, grads, routes, router)


def expert_kernel(slots, info, rows, grads, shares, *rest):
    count = len(rest) - 7
    refs = rest[:count]
    out_rows, back_rows, grad_rows, acts, dots, weight, sem = rest[count:]
    part = weight.shape[1] // slots

    @pl.when(pl.program_id(0) == 0)
    def _():
        def copies(ref, slot):
            return [
                pltpu.make_async_copy(
                    ref.at[pl.ds(which * part, part)],
                    weight.at[which, pl.ds(slot * part, part)],
                    sem,
                )
                for which in range(3)
            ]

        if count == slots:
            for slot in range(slots):
                run_all(copies(refs[slot], slot))
        else:
            block, second, above, below, far = refs
            low_end = info[2] == 0
            end = jnp.logical_or(low_end, info[2] == 3)
            run_all(copies(block, 0))
            run_all(copies(second, 1))

            @pl.when(low_end)
            def _():
                run_all(copies(above, 2))

            @pl.when(jnp.logical_not(low_end))
            def _():
                run_all(copies(below, 2))

            @pl.when(end)
            def _():
                run_all(copies(far, 3))

            @pl.when(jnp.logical_not(end))
            def _():
                run_all(copies(above, 3))

        for slot in range(slots):
            wait_all(copies(refs[0], slot))

    row_block = rows[...]
    share = shares[...]
    grad_float = grads[...].astype(WIDE)
    grad_low = (share * grad_float).astype(LOW)
    grad_rows[...] = grad_low
    gate_act = nt(row_block, weight[0])
    upward = nt(row_block, weight[1])
    sigmoid = 1.0 / (1.0 + jnp.exp(-gate_act))
    silu = gate_act * sigmoid
    hidden = (silu * upward).astype(LOW)
    expert_out = nn(hidden, weight[2]).astype(LOW).astype(WIDE)
    out_rows[...] = (share * expert_out).astype(LOW)
    dots[...] = jnp.sum(grad_float * expert_out, axis=1, keepdims=True)
    grad_hidden = nt(grad_low, weight[2])
    grad_gate = (grad_hidden * upward * sigmoid * (1.0 + gate_act * (1.0 - sigmoid))).astype(LOW)
    grad_up = (grad_hidden * silu).astype(LOW)
    back_rows[...] = (nn(grad_gate, weight[0]) + nn(grad_up, weight[1])).astype(LOW)
    for which, act in enumerate((grad_gate, grad_up, hidden)):
        turned = act.T
        for slot in range(slots):
            acts[slot, which * part : (which + 1) * part] = turned[
                slot * part : (slot + 1) * part
            ]


EXPERT_ROWS = 256


def expert(info, rows, grads, shares, refs, slots):
    height = rows.shape[0]
    part = refs[0].shape[0] // 3
    wide_block = pl.BlockSpec((EXPERT_ROWS, D), lambda i: (i, 0))
    thin_block = pl.BlockSpec((EXPERT_ROWS, 1), lambda i: (i, 0))
    return pl.pallas_call(
        functools.partial(expert_kernel, slots),
        grid=(height // EXPERT_ROWS,),
        out_shape=[jax.ShapeDtypeStruct((height, D), LOW)] * 3
        + [
            jax.ShapeDtypeStruct((slots, 3 * part, height), LOW),
            jax.ShapeDtypeStruct((height, 1), WIDE),
        ],
        in_specs=[SMEM, wide_block, wide_block, thin_block] + [ANY] * len(refs),
        out_specs=[wide_block] * 3
        + [pl.BlockSpec((slots, 3 * part, EXPERT_ROWS), lambda i: (0, 0, i)), thin_block],
        scratch_shapes=[pltpu.VMEM((3, slots * part, D), LOW), pltpu.SemaphoreType.DMA],
        compiler_params=params(),
        name="expert",
    )(info, rows, grads, shares, *refs)


def expert_grads_kernel(slots, rows, grads, *rest):
    acts, outs = rest[: len(slots)], rest[len(slots) :]
    part = acts[0].shape[1] // 3
    at = pl.ds(pl.multiple_of(pl.program_id(0) * 256, 256), 256)
    for act, out in zip(acts, outs):
        out[: 2 * part, :] = nn(act[0, : 2 * part], rows[:, at]).astype(LOW)
        out[2 * part :, :] = nn(act[0, 2 * part :], grads[:, at]).astype(LOW)


def expert_grads(acts, rows, grads, slots):
    _, part, height = acts.shape
    return pl.pallas_call(
        functools.partial(expert_grads_kernel, slots),
        grid=(D // 256,),
        out_shape=[jax.ShapeDtypeStruct((part, D), LOW) for _ in slots],
        in_specs=[whole((height, D))] * 2
        + [pl.BlockSpec((1, part, height), lambda i, s=slot: (s, 0, 0)) for slot in slots],
        out_specs=[pl.BlockSpec((part, 256), lambda i: (0, i)) for _ in slots],
        compiler_params=params(),
        name="expert_gradients",
    )(rows, grads, *[acts] * len(slots))


def combine_kernel(capacity, local, total, order, info, routes, *rest):
    rows, out, earlier = rest[:local], rest[local], rest[local + 1]

    @pl.when(pl.program_id(0) == 0)
    def _():
        one = lax.broadcasted_iota(jnp.int32, (TOK_DEV, TOK_DEV), 0)
        two = lax.broadcasted_iota(jnp.int32, (TOK_DEV, TOK_DEV), 1)
        earlier[...] = jnp.where(two < one, 1.0, 0.0).astype(LOW)

    ids = lax.broadcasted_iota(jnp.int32, (TOK_DEV, total), 1)
    hit = ids == routes[0, :, 0:1]
    for k in range(1, TOP):
        hit = jnp.logical_or(hit, ids == routes[0, :, k : k + 1])
    hits = jnp.where(hit, 1.0, 0.0)
    place = jnp.where(hit, nn(earlier[...], hits.astype(LOW)), -1.0)
    spots = lax.broadcasted_iota(jnp.int32, (TOK_DEV, capacity), 1).astype(WIDE)
    summed = None
    for e in range(local):
        mine = ids == info[0] * local + e
        place_col = jnp.sum(jnp.where(mine, place, 0.0), axis=1, keepdims=True)
        onehot = jnp.where(spots == place_col, 1.0, 0.0).astype(LOW)
        term = nn(onehot, rows[e][0])
        summed = term if summed is None else summed + term
    out[0] = summed.astype(LOW)


def combine(order, info, routes, rows, total):
    count, capacity = rows[0].shape[0], rows[0].shape[1]
    named = pl.BlockSpec((1, capacity, D), lambda i, order, info: (order[i], 0, 0))
    return pl.pallas_call(
        functools.partial(combine_kernel, capacity, len(rows), total),
        grid_spec=pltpu.PrefetchScalarGridSpec(
            num_scalar_prefetch=2,
            grid=(order.shape[0],),
            in_specs=[pl.BlockSpec((1, TOK_DEV, TOP), lambda i, order, info: (order[i], 0, 0))]
            + [named] * len(rows),
            out_specs=pl.BlockSpec((1, TOK_DEV, D), lambda i, order, info: (i, 0, 0)),
            scratch_shapes=[pltpu.VMEM((TOK_DEV, TOK_DEV), LOW)],
        ),
        out_shape=jax.ShapeDtypeStruct((order.shape[0], TOK_DEV, D), LOW),
        compiler_params=params(),
        name="combine",
    )(order, info, routes, *rows)


def split(values):
    high = values.astype(LOW)
    return high, (values - high.astype(WIDE)).astype(LOW)


def norm_back(values, gain, grad):
    factor = lax.rsqrt(jnp.mean(values * values, axis=-1, keepdims=True) + EPSILON)
    scaled = gain * grad
    mean = jnp.mean(values * scaled, axis=-1, keepdims=True)
    grad_values = factor * scaled - values * (factor * factor * factor * mean)
    grad_gain = jnp.sum(grad * values * factor, axis=0, keepdims=True)
    return grad_values, grad_gain


def branch_back_kernel(
    info, residual, normed, sums, cotangent, grad_logits, router, gain, *rest
):
    count = len(rest) - 7
    refs = rest[:count]
    grad_residual, grad_branch, grad_heads, grad_gain, grad_router, weight, sem = rest[count:]
    copies = weight_copies(info, refs, weight, sem, D // QUARTERS + 128, D // QUARTERS)

    @pl.when(pl.program_id(0) == 0)
    def _():
        run_all(copies)
        high, low = split(grad_logits[...])
        grad_router[...] = nn(high, normed[...]) + nn(low, normed[...])
        grad_normed = sums[...] + tn(high, router[...]) + tn(low, router[...])
        grad_values, gain_grad = norm_back(residual[...], gain[...], grad_normed)
        grad_gain[...] = gain_grad
        total = cotangent[...].astype(WIDE) + grad_values
        grad_residual[...] = total
        grad_branch[...] = total.astype(LOW)
        wait_all(copies)

    at = pl.ds(pl.multiple_of(pl.program_id(0) * 256, 256), 256)
    grad_heads[...] = nt(grad_branch[...], weight[at, :]).astype(LOW)


def branch_back(info, residual, normed, sums, cotangent, grad_logits, router, gain, refs):
    full = (TOK_DEV, D)
    total = router.shape[0]
    return pl.pallas_call(
        branch_back_kernel,
        grid=(D // 256,),
        out_shape=(
            jax.ShapeDtypeStruct(full, WIDE),
            jax.ShapeDtypeStruct(full, LOW),
            jax.ShapeDtypeStruct(full, LOW),
            jax.ShapeDtypeStruct((1, D), WIDE),
            jax.ShapeDtypeStruct((total, D), WIDE),
        ),
        in_specs=[SMEM]
        + [whole(full)] * 4
        + [whole((total, TOK_DEV)), whole((total, D)), whole((1, D))]
        + [ANY] * len(refs),
        out_specs=(
            whole(full),
            whole(full),
            pl.BlockSpec((TOK_DEV, 256), lambda i: (0, i)),
            whole((1, D)),
            whole((total, D)),
        ),
        scratch_shapes=[pltpu.VMEM((D, D), LOW), pltpu.SemaphoreType.DMA],
        compiler_params=params(),
        name="experts_norm_back",
    )(info, residual, normed, sums, cotangent, grad_logits, router, gain, *refs)


def join_grads_kernel(info, own_grad, source_grad, arrived, cosine, sine, out):
    half = HEAD_DIM // 2
    first = lax.broadcasted_iota(jnp.int32, (TOK_DEV, HEAD_DIM), 1) < half
    leaves = info[1] == 0

    def total(column):
        columns = slice(column, column + 128)
        extra = source_grad[:, columns] + arrived[:, columns].astype(WIDE)
        return own_grad[:, columns] + jnp.where(leaves, 0.0, extra)

    for g in range(KV_HEADS):
        key = turn_back(total(128 * g), cosine[...], sine[...])
        value = total(KEY_WIDTH + 128 * g)
        out[:, 256 * g : 256 * g + 128] = jnp.where(
            first, key, pltpu.roll(value, half, 1)
        ).astype(LOW)
        out[:, 256 * g + 128 : 256 * g + 256] = jnp.where(
            first, pltpu.roll(key, half, 1), value
        ).astype(LOW)


def join_grads(info, own_grad, source_grad, arrived, cosine, sine):
    vmem = pl.BlockSpec(memory_space=pltpu.VMEM)
    return pl.pallas_call(
        join_grads_kernel,
        out_shape=jax.ShapeDtypeStruct((TOK_DEV, 2 * KEY_WIDTH), LOW),
        in_specs=[SMEM] + [vmem] * 5,
        out_specs=vmem,
        compiler_params=params(),
        name="join_key_value_gradients",
    )(info, own_grad, source_grad, arrived, cosine, sine)


def token_back_kernel(info, grad_query, grad_pair, tokens, grad_residual, gain, *rest):
    count = (len(rest) - 6) // 2
    query_refs, pair_refs = rest[:count], rest[count : 2 * count]
    out, grad_gain, query_weight, pair_weight, grad_normed, sem = rest[2 * count :]

    @pl.when(pl.program_id(0) == 0)
    def _():
        copies = weight_copies(info, query_refs, query_weight, sem, 0, D // QUARTERS)
        copies += weight_copies(info, pair_refs, pair_weight, sem, D // QUARTERS, 128)
        run_all(copies)
        wait_all(copies)

    at = pl.ds(pl.multiple_of(pl.program_id(0) * 256, 256), 256)
    grad_normed[:, at] = nt(grad_query[...], query_weight[at, :]) + nt(
        grad_pair[...], pair_weight[at, :]
    )

    @pl.when(pl.program_id(0) == pl.num_programs(0) - 1)
    def _():
        grad_values, gain_grad = norm_back(
            tokens[...].astype(WIDE), gain[...], grad_normed[...]
        )
        grad_gain[...] = gain_grad
        out[...] = (grad_residual[...] + grad_values).astype(LOW)


def token_back(info, grad_query, grad_pair, tokens, grad_residual, gain, query_refs, pair_refs):
    full = (TOK_DEV, D)
    return pl.pallas_call(
        token_back_kernel,
        grid=(D // 256,),
        out_shape=(jax.ShapeDtypeStruct(full, LOW), jax.ShapeDtypeStruct((1, D), WIDE)),
        in_specs=[
            SMEM,
            whole(full),
            whole((TOK_DEV, 2 * KEY_WIDTH)),
            whole(full),
            whole(full),
            whole((1, D)),
        ]
        + [ANY] * (len(query_refs) + len(pair_refs)),
        out_specs=(whole(full), whole((1, D))),
        scratch_shapes=[
            pltpu.VMEM((D, D), LOW),
            pltpu.VMEM((D, 2 * KEY_WIDTH), LOW),
            pltpu.VMEM(full, WIDE),
            pltpu.SemaphoreType.DMA,
        ],
        compiler_params=params(),
        name="token_gradient",
    )(info, grad_query, grad_pair, tokens, grad_residual, gain, *query_refs, *pair_refs)


def weight_grads_kernel(info, normed, heads, grad_query, grad_pair, grad_branch, keep, send):
    quarter = D // QUARTERS
    depth = keep.shape[2]
    core = info[0] & 1

    def store(grads, start, width):
        low = grads.astype(LOW)
        for slot in range(QUARTERS):
            shard = info[2 + slot]
            for j in range(QUARTERS):
                piece = low[:, j * width : (j + 1) * width]
                upper, lower = piece[:depth], piece[depth:]

                @pl.when(shard == j)
                def _():
                    columns = slice(start, start + width)
                    keep[0, slot, :, columns] = jnp.where(core == 0, upper, lower)
                    send[0, slot, :, columns] = jnp.where(core == 0, lower, upper)

    store(tn(normed[...], grad_query[...]), 0, quarter)
    store(tn(normed[...], grad_pair[...]), quarter, 128)
    store(tn(heads[...], grad_branch[...]), quarter + 128, quarter)


def weight_grads(info, normed, heads, grad_query, grad_pair, grad_branch):
    full = (TOK_DEV, D)
    quarter = D // QUARTERS
    width = 2 * quarter + 128
    strip = pl.BlockSpec((TOK_DEV, quarter), lambda i, info: (0, i ^ (info[0] >> 1)))
    shape = (4, QUARTERS, quarter // 2, width)
    out = pl.BlockSpec((1,) + shape[1:], lambda i, info: (i, 0, 0, 0))

    def fixed(block):
        return pl.BlockSpec(block, lambda i, info: (0, 0))

    return pl.pallas_call(
        weight_grads_kernel,
        grid_spec=pltpu.PrefetchScalarGridSpec(
            num_scalar_prefetch=1,
            grid=(4,),
            in_specs=[
                strip,
                strip,
                fixed(full),
                fixed((TOK_DEV, 2 * KEY_WIDTH)),
                fixed(full),
            ],
            out_specs=(out, out),
        ),
        out_shape=(jax.ShapeDtypeStruct(shape, LOW),) * 2,
        compiler_params=params(),
        name="weight_gradients",
    )(info, normed, heads, grad_query, grad_pair, grad_branch)


def position_of(token_index):
    branch_place = TRUNK + (token_index - TRUNK) % BRANCH
    leaf_place = TRUNK + BRANCH + (token_index - TOK_DEV) % BRANCH
    return jnp.where(
        token_index < TRUNK, token_index, jnp.where(token_index < TOK_DEV, branch_place, leaf_place)
    )


def rotary_tables(positions):
    half_dim = HEAD_DIM // 2
    frequency = ROPE_BASE ** (-jnp.arange(half_dim, dtype=jnp.float32) / half_dim)
    angles = positions.astype(jnp.float32)[:, None] * frequency[None, :]
    cosine, sine = (jnp.cos(angles), jnp.sin(angles))
    return (
        jnp.concatenate([cosine, cosine], axis=1),
        jnp.concatenate([-sine, sine], axis=1),
    )


def after(values, *earlier):
    return lax.optimization_barrier((values, earlier))[0]


def fast_mesh():
    return lax.axis_size("rows") == 8 and lax.axis_size("cols") == 4


SLOT_SHARD = ((0, 2, 1, 3), (1, 3, 0, 2), (2, 0, 1, 3), (3, 1, 2, 0))
UP = [(0, 1), (1, 2), (2, 3)]
DOWN = [(1, 0), (2, 1), (3, 2)]
FAR = [(0, 3), (3, 0)]


def send_first(block):
    return (
        lax.ppermute(block, "cols", DOWN),
        lax.ppermute(block, "cols", UP),
        lax.ppermute(block, "cols", FAR),
    )


def send_second(block, first):
    place = lax.axis_index("cols")
    above, below, _ = first
    payload = jnp.where(place == 1, above, jnp.where(place == 2, below, block))
    return lax.ppermute(payload, "cols", [(3, 1), (1, 0), (0, 2), (2, 3)])


def slot_list(block, first, second):
    place = lax.axis_index("cols")
    above, below, far = first
    end = (place == 0) | (place == 3)
    return [
        block,
        second,
        jnp.where(place == 0, above, below),
        jnp.where(end, far, above),
    ]


def reduce_first(second, fourth):
    return (
        lax.ppermute(second, "cols", [(1, 3), (0, 1), (2, 0), (3, 2)]),
        lax.ppermute(fourth, "cols", FAR),
    )


def reduce_second(third, fourth, relay):
    place = lax.axis_index("cols")
    relayed = relay.astype(WIDE)
    upward_load = (
        jnp.where(place == 0, third, fourth).astype(WIDE) + jnp.where(place == 1, relayed, 0.0)
    ).astype(LOW)
    downward_load = (third.astype(WIDE) + jnp.where(place == 2, relayed, 0.0)).astype(LOW)
    return (
        lax.ppermute(upward_load, "cols", UP),
        lax.ppermute(downward_load, "cols", DOWN),
    )


def reduce_last(own, first, second):
    place = lax.axis_index("cols")
    relay, far = first
    below, above = second
    end = (place == 0) | (place == 3)
    return (
        own.astype(WIDE)
        + below.astype(WIDE)
        + above.astype(WIDE)
        + jnp.where(end, relay.astype(WIDE) + far.astype(WIDE), 0.0)
    )


def flip(block, bit):
    count = lax.axis_size("rows")
    return lax.ppermute(block, "rows", [(i, i ^ bit) for i in range(count)])


def add_low(one, two):
    return (one.astype(WIDE) + two.astype(WIDE)).astype(LOW)


def reduce_chips(keep, got):
    half = keep.shape[1] // 2

    def sums(chips, part):
        return jnp.stack([add_low(keep[i][part], got[i][part]) for i in chips])

    one, two = slice(0, half), slice(half, None)
    got_x = flip(sums((1, 3), one), 2)
    got_y = flip(sums((2, 3), two), 4)
    near_x = sums((0, 2), one)
    near_y = sums((0, 1), two)
    got_xy = flip(add_low(near_x[1], got_x[1]), 4)
    got_yx = flip(add_low(near_y[1], got_y[1]), 2)
    wide = [a.astype(WIDE) for a in (near_x[0], got_x[0], got_xy, near_y[0], got_y[0], got_yx)]
    return wide[0] + wide[1] + wide[2], wide[3] + wide[4] + wide[5]


def on_device(
    tokens,
    query_weight,
    key_weight,
    value_weight,
    out_weight,
    router_weight,
    attention_gain,
    experts_gain,
    gate_weight,
    upward_weight,
    down_weight,
    routes,
    leaf_parent,
    cotangent,
):
    row_count = lax.axis_size("rows")
    col_count = lax.axis_size("cols")
    row_place = lax.axis_index("rows")
    col_place = lax.axis_index("cols")
    fast = fast_mesh()
    parity = lax.rem(col_place, 2)
    tree_id = lax.div(row_place * col_count + col_place, 2)
    parent_row = lax.dynamic_slice_in_dim(leaf_parent, tree_id, 1, 0)[0]
    depth, query_part = query_weight.shape
    key_part = key_weight.shape[1]
    router_part = router_weight.shape[1]
    gain_part = attention_gain.shape[0]
    expert_total = router_part * col_count
    local_experts = gate_weight.shape[0]
    capacity = TOK_DEV * TOP // expert_total * 5 // 4

    shards = (
        jnp.asarray(SLOT_SHARD, jnp.int32)[col_place]
        if fast
        else jnp.arange(4, dtype=jnp.int32)
    )
    branch_rows = jnp.where(parity == 0, TRUNK + BRANCH * parent_row, TRUNK)
    info = jnp.concatenate(
        [jnp.stack([row_place, parity]), shards, branch_rows, jnp.zeros((2,), jnp.int32)]
    ).astype(jnp.int32)

    small = jnp.concatenate([attention_gain, experts_gain, router_weight.reshape(-1)])
    small_all = lax.all_gather(small, ("rows", "cols"), axis=0)
    attention_scale = small_all[:, :gain_part].reshape(1, D).astype(WIDE)
    experts_scale = small_all[:, gain_part : 2 * gain_part].reshape(1, D).astype(WIDE)
    router_rows = jnp.transpose(
        small_all[:, 2 * gain_part :].reshape(row_count, col_count, depth, router_part),
        (1, 3, 0, 2),
    ).reshape(expert_total, D)

    packed = jnp.concatenate([query_weight, key_weight, value_weight, out_weight], axis=1)
    shard_blocks = [
        jnp.concatenate(
            [gate_weight[expert].T, upward_weight[expert].T, down_weight[expert]], axis=0
        )
        for expert in range(local_experts)
    ]
    firsts, seconds = ([], [])
    if fast:
        packed_first = send_first(packed)
        packed_second = send_second(packed, packed_first)
        own = jnp.stack(slot_list(packed, packed_first, packed_second))
        ahead = packed_second
        for expert_at in range(local_experts):
            block = after(shard_blocks[expert_at], ahead)
            shard_blocks[expert_at] = block
            first = send_first(block)
            firsts.append(first)
            seconds.append(send_second(block, first))
            ahead = first
        beside, across = flip(own, 2), flip(own, 4)
        corner = [flip(beside[:2], 4), flip(across[2:], 2)]
        same = [own, beside, across] + corner
        same = [after(piece, firsts[0][0], firsts[0][1]) for piece in same]
        pieces = same + [flip(piece, 1) for piece in same]
        query_refs = pair_refs = out_refs = pieces
        expert_refs = [
            [shard_blocks[i], seconds[i], *firsts[i]] for i in range(local_experts)
        ]
    else:
        packed_all = lax.all_gather(lax.all_gather(packed, "cols", axis=0), "rows", axis=0)

        def unpack(start, width):
            part = packed_all[..., start : start + width]
            return jnp.swapaxes(part, 1, 2).reshape(row_count * depth, col_count * width)

        key_at = query_part
        query_refs = [unpack(0, query_part)]
        pair_refs = [
            jnp.concatenate(
                [
                    unpack(key_at, key_part).reshape(D, QUARTERS, -1),
                    unpack(key_at + key_part, key_part).reshape(D, QUARTERS, -1),
                ],
                axis=2,
            ).reshape(D, -1)
        ]
        out_refs = [unpack(key_at + 2 * key_part, query_part)]
        expert_refs = [
            [lax.all_gather(block, "cols", axis=0)[i] for i in range(col_count)]
            for block in shard_blocks
        ]

    routes_all = lax.all_gather(routes.T, "rows", axis=0)
    grad_all = lax.all_gather(cotangent, "rows", axis=0)

    local_index = (1 - parity) * TOK_DEV + jnp.arange(TOK_DEV, dtype=jnp.int32)
    cosine, sine = rotary_tables(position_of(local_index))
    normed, own_pair = key_value(info, tokens, attention_scale, cosine, sine, pair_refs)
    pairs = [(i + 1, i) for i in range(0, col_count, 2)]
    partner = lax.ppermute(own_pair, "cols", pairs)
    if fast:
        normed_query = after(normed, firsts[0][2])
    else:
        normed_query = normed
    queries = query(info, normed_query, cosine, sine, query_refs)
    if fast:
        queries = after(queries, seconds[0])
    heads = attention(info, queries, own_pair, partner)
    if fast:
        heads = after(heads, firsts[1][0], firsts[1][1])
    residual, normed_two = out_projection(info, heads, tokens, experts_scale, out_refs)
    rows_all = lax.all_gather(normed_two, "rows", axis=0)
    if fast:
        rows_all = after(rows_all, firsts[1][2])

    picked = dispatch(
        info, rows_all, grad_all, routes_all, router_rows, capacity, local_experts
    )
    height = row_count * capacity
    token_rows = [a.reshape(height, D) for a in picked[:local_experts]]
    grad_rows = [a.reshape(height, D) for a in picked[local_experts : 2 * local_experts]]
    share_rows = [a.reshape(height, 1) for a in picked[2 * local_experts : 3 * local_experts]]
    logits = lax.dynamic_index_in_dim(picked[-1], row_place, 0, keepdims=False)

    out_rows, back_rows, gate_dots, reduced, marks = ([], [], [], [], [])
    for e in range(local_experts):
        rows_in = token_rows[e]
        if fast and e == 0:
            rows_in = after(rows_in, seconds[0])
        if fast and e == 1:
            rows_in = after(rows_in, seconds[1], *marks[0])
        out_row, back_row, grad_row, acts, dots = expert(
            info, rows_in, grad_rows[e], share_rows[e], expert_refs[e], col_count
        )
        out_rows.append(out_row.reshape(row_count, capacity, D))
        back_rows.append(back_row.reshape(row_count, capacity, D))
        gate_dots.append(dots.reshape(row_count, capacity))
        if fast:
            second, fourth = expert_grads(acts, token_rows[e], grad_row, (1, 3))
            sent_first = reduce_first(second, fourth)
            marks.append([sent_first[0]])
            own_slot, third = expert_grads(acts, token_rows[e], grad_row, (0, 2))
            sent_second = reduce_second(third, fourth, sent_first[0])
            reduced.append((own_slot, sent_first, sent_second))
        else:
            slots = expert_grads(acts, token_rows[e], grad_row, tuple(range(col_count)))
            reduced.append(
                lax.psum_scatter(jnp.stack(slots), "cols", scatter_dimension=0).astype(WIDE)
            )

    routes_cols = jnp.swapaxes(routes_all, 1, 2)
    if fast:
        chips = jnp.arange(4, dtype=jnp.int32) * 2
        keep_order, send_order = (chips ^ row_place, (chips + 1) ^ row_place)

        def both_ways(rows):
            got = flip(combine(send_order, info, routes_cols, rows, expert_total), 1)
            keep = combine(keep_order, info, routes_cols, rows, expert_total)
            return reduce_chips(keep, got)

        back_sum = jnp.concatenate(both_ways(back_rows), axis=0)
        out_rows = [after(a, back_sum) for a in out_rows]
        mixture = jnp.concatenate(both_ways(out_rows), axis=0)
    else:
        order = jnp.arange(row_count, dtype=jnp.int32)

        def summed(rows):
            part = combine(order, info, routes_cols, rows, expert_total)
            return lax.psum_scatter(part, "rows", scatter_dimension=0).astype(WIDE)

        back_sum = summed(back_rows)
        mixture = summed(out_rows)
    layer_output = (residual + mixture).astype(LOW)

    ids = jnp.arange(expert_total, dtype=jnp.int32)
    named = routes_all[:, :, None, :] == ids[None, None, :, None]
    hit = jnp.any(named, axis=1)
    rank = jnp.cumsum(hit.astype(jnp.int32), axis=2) - 1
    own_at = row_place * local_experts
    own_hit = lax.dynamic_slice_in_dim(hit, own_at, local_experts, 1)
    own_rank = lax.dynamic_slice_in_dim(rank, own_at, local_experts, 1)
    dots = jnp.stack(gate_dots, axis=1)
    grad_share = jnp.where(
        own_hit, jnp.take_along_axis(dots, jnp.clip(own_rank, 0, capacity - 1), axis=2), 0.0
    )
    grad_share_all = lax.all_gather(grad_share, "rows", axis=1, tiled=True)
    grad_shares = lax.dynamic_index_in_dim(grad_share_all, row_place, 0, keepdims=False)
    chosen_of = lax.dynamic_index_in_dim(hit, row_place, 0, keepdims=False)

    def shares_out(logit_cols):
        softmax_out = jax.nn.softmax(logit_cols, axis=0)
        chosen = jnp.where(chosen_of, softmax_out, 0.0)
        return chosen / jnp.sum(chosen, axis=0, keepdims=True)

    _, router_pullback = jax.vjp(shares_out, logits)
    (grad_logits,) = router_pullback(grad_shares)

    grad_residual, grad_branch, grad_heads, experts_gain_grad, router_grad = branch_back(
        info,
        residual,
        normed_two,
        back_sum,
        cotangent,
        grad_logits,
        router_rows,
        experts_scale,
        out_refs,
    )
    grad_query, own_grad, source_grad = attention_back(
        info, queries, own_pair, partner, grad_heads, cosine, sine
    )
    arrived = lax.ppermute(source_grad.astype(LOW), "cols", [(j, i) for i, j in pairs])
    grad_pair = join_grads(info, own_grad, source_grad, arrived, cosine, sine)
    tokens_grad, attention_gain_grad = token_back(
        info, grad_query, grad_pair, tokens, grad_residual, attention_scale, query_refs, pair_refs
    )

    if fast:
        keep, send = weight_grads(info, normed, heads, grad_query, grad_pair, grad_branch)
        first_half, second_half = reduce_chips(keep, flip(send, 1))
        slots = [a.astype(LOW) for a in (*first_half, *second_half)]
        sent_first = reduce_first(slots[1], slots[3])
        sent_second = reduce_second(slots[2], slots[3], sent_first[0])
        sums = reduce_last(slots[0], sent_first, sent_second)
        expert_sums = [reduce_last(*parts) for parts in reduced]
    else:
        full_grads = [
            tn(normed, grad_query),
            *jnp.moveaxis(tn(normed, grad_pair).reshape(D, QUARTERS, 2, -1), 2, 0),
            tn(heads, grad_branch),
        ]
        packed_grad = jnp.concatenate(
            [
                grad.astype(LOW).reshape(row_count, depth, col_count, -1)
                for grad in full_grads
            ],
            axis=3,
        )
        row_sums = lax.psum_scatter(packed_grad, "rows", scatter_dimension=0)
        sums = lax.psum_scatter(row_sums, "cols", scatter_dimension=1).astype(WIDE)
        expert_sums = reduced

    small_grads = jnp.concatenate(
        [
            attention_gain_grad.reshape(-1, gain_part),
            experts_gain_grad.reshape(-1, gain_part),
            jnp.transpose(
                router_grad.reshape(col_count, router_part, row_count, depth), (2, 0, 3, 1)
            ).reshape(row_count * col_count, depth * router_part),
        ],
        axis=1,
    )
    small_sums = lax.psum_scatter(small_grads, ("rows", "cols"), scatter_dimension=0)

    key_at = query_part
    value_at = key_at + key_part
    out_at = value_at + key_part
    part = down_weight.shape[1]
    gate_grad, upward_grad, down_grad = (
        jnp.stack([sums_of[which * part : (which + 1) * part] for sums_of in expert_sums])
        for which in range(3)
    )
    return (
        layer_output,
        tokens_grad,
        sums[:, :key_at],
        sums[:, key_at:value_at],
        sums[:, value_at:out_at],
        sums[:, out_at:],
        small_sums[2 * gain_part :].reshape(depth, router_part),
        small_sums[:gain_part],
        small_sums[gain_part : 2 * gain_part],
        jnp.swapaxes(gate_grad, 1, 2),
        jnp.swapaxes(upward_grad, 1, 2),
        down_grad,
    )


def solution(mesh):
    in_specs = (
        P(("rows", "cols"), None),
        P("rows", "cols"),
        P("rows", "cols"),
        P("rows", "cols"),
        P("rows", "cols"),
        P("rows", "cols"),
        P(("rows", "cols")),
        P(("rows", "cols")),
        P("rows", None, "cols"),
        P("rows", None, "cols"),
        P("rows", "cols", None),
        P(("rows", "cols"), None),
        P(),
        P(("rows", "cols"), None),
    )
    out_specs = (
        P(("rows", "cols"), None),
        P(("rows", "cols"), None),
        P("rows", "cols"),
        P("rows", "cols"),
        P("rows", "cols"),
        P("rows", "cols"),
        P("rows", "cols"),
        P(("rows", "cols")),
        P(("rows", "cols")),
        P("rows", None, "cols"),
        P("rows", None, "cols"),
        P("rows", "cols", None),
    )
    return jax.shard_map(
        on_device, mesh=mesh, in_specs=in_specs, out_specs=out_specs, check_vma=False
    )
```

```python
import functools

import jax
import jax.numpy as jnp
from jax import lax
from jax.experimental import pallas as pl
from jax.experimental.pallas import tpu as pltpu
from jax.sharding import PartitionSpec as P

D = 1536
HEADS = 12
KV_HEADS = 2
HEAD_DIM = 128
TOP = 4
TOK_DEV = 512
BRANCHES = 4
LEAVES = 8
TRUNK = 256
BRANCH = 64

EPSILON = 1e-06
ROPE_BASE = 10000.0
MASKED = -1e30
LOW = jnp.bfloat16
WIDE = jnp.float32
KEY_WIDTH = KV_HEADS * HEAD_DIM
GROUP = HEADS // KV_HEADS
QUARTERS = 4
VMEM_LIMIT = 56 * 1024 * 1024

ANY = pl.BlockSpec(memory_space=pl.ANY)
SMEM = pl.BlockSpec(memory_space=pltpu.SMEM)


def nn(one, two):
    return lax.dot_general(one, two, (((1,), (0,)), ((), ())), preferred_element_type=WIDE)


def nt(one, two):
    return lax.dot_general(one, two, (((1,), (1,)), ((), ())), preferred_element_type=WIDE)


def tn(one, two):
    return lax.dot_general(one, two, (((0,), (0,)), ((), ())), preferred_element_type=WIDE)


def whole(shape):
    return pl.BlockSpec(shape, lambda *_: (0,) * len(shape))


def params():
    return pltpu.CompilerParams(vmem_limit_bytes=VMEM_LIMIT)


def turn(values, cosine, sine):
    return values * cosine + pltpu.roll(values, HEAD_DIM // 2, 1) * sine


def turn_back(values, cosine, sine):
    return values * cosine - pltpu.roll(values, HEAD_DIM // 2, 1) * sine


PIECES = tuple(
    (flip_bits + core, first, count)
    for core in (0, 1)
    for flip_bits, first, count in ((0, 0, 4), (2, 0, 4), (4, 0, 4), (6, 0, 2), (6, 2, 2))
)


def weight_copies(info, refs, target, sem, start, width):
    if len(refs) == 1:
        return [pltpu.make_async_copy(refs[0], target, sem)]
    depth = refs[0].shape[1]
    copies = []
    for ref, (flip_bits, first, count) in zip(refs, PIECES):
        row = pl.multiple_of((info[0] ^ flip_bits) * depth, depth)
        for slot in range(count):
            col = pl.multiple_of(info[2 + first + slot] * width, 128)
            copies.append(
                pltpu.make_async_copy(
                    ref.at[slot, :, pl.ds(start, width)],
                    target.at[pl.ds(row, depth), pl.ds(col, width)],
                    sem,
                )
            )
    return copies


def run_all(copies):
    for copy in copies:
        copy.start()


def wait_all(copies):
    for copy in copies:
        copy.wait()


def key_value_kernel(info, tokens, gain, cosine, sine, *rest):
    count = len(rest) - 4
    refs, (normed, out, weight, sem) = rest[:count], rest[count:]
    copies = weight_copies(info, refs, weight, sem, D // QUARTERS, 128)
    run_all(copies)
    values = tokens[...].astype(WIDE)
    factor = lax.rsqrt(jnp.mean(values * values, axis=-1, keepdims=True) + EPSILON)
    low = (values * factor * gain[...]).astype(LOW)
    normed[...] = low
    wait_all(copies)
    both = nn(low, weight[...])
    half = HEAD_DIM // 2
    first = lax.broadcasted_iota(jnp.int32, (TOK_DEV, HEAD_DIM), 1) < half
    for g in range(KV_HEADS):
        one = both[:, 256 * g : 256 * g + 128]
        two = both[:, 256 * g + 128 : 256 * g + 256]
        key = jnp.where(first, one, pltpu.roll(two, half, 1))
        value = jnp.where(first, pltpu.roll(one, half, 1), two)
        out[:, 128 * g : 128 * g + 128] = turn(key, cosine[...], sine[...]).astype(LOW)
        out[:, KEY_WIDTH + 128 * g : KEY_WIDTH + 128 * g + 128] = value.astype(LOW)


def key_value(info, tokens, gain, cosine, sine, refs):
    return pl.pallas_call(
        key_value_kernel,
        out_shape=(
            jax.ShapeDtypeStruct((TOK_DEV, D), LOW),
            jax.ShapeDtypeStruct((TOK_DEV, 2 * KEY_WIDTH), LOW),
        ),
        in_specs=[SMEM] + [pl.BlockSpec(memory_space=pltpu.VMEM)] * 4 + [ANY] * len(refs),
        out_specs=(pl.BlockSpec(memory_space=pltpu.VMEM),) * 2,
        scratch_shapes=[pltpu.VMEM((D, 2 * KEY_WIDTH), LOW), pltpu.SemaphoreType.DMA],
        compiler_params=params(),
        name="norm_key_value",
    )(info, tokens, gain, cosine, sine, *refs)


def query_kernel(info, normed, cosine, sine, *rest):
    count = len(rest) - 3
    refs, (out, weight, sem) = rest[:count], rest[count:]

    @pl.when(pl.program_id(0) == 0)
    def _():
        copies = weight_copies(info, refs, weight, sem, 0, D // QUARTERS)
        run_all(copies)
        wait_all(copies)

    at = pl.multiple_of(pl.program_id(0) * 256, 256)
    lin = nn(normed[...], weight[:, pl.ds(at, 256)])
    for h in range(2):
        out[:, 128 * h : 128 * h + 128] = turn(
            lin[:, 128 * h : 128 * h + 128], cosine[...], sine[...]
        ).astype(LOW)


def query(info, normed, cosine, sine, refs):
    return pl.pallas_call(
        query_kernel,
        grid=(D // 256,),
        out_shape=jax.ShapeDtypeStruct((TOK_DEV, D), LOW),
        in_specs=[SMEM, whole((TOK_DEV, D)), whole((TOK_DEV, 128)), whole((TOK_DEV, 128))]
        + [ANY] * len(refs),
        out_specs=pl.BlockSpec((TOK_DEV, 256), lambda i: (0, i)),
        scratch_shapes=[pltpu.VMEM((D, D), LOW), pltpu.SemaphoreType.DMA],
        compiler_params=params(),
        name="query_projection",
    )(info, normed, cosine, sine, *refs)


KEYS = TRUNK + 2 * BRANCH
CHUNKS = TOK_DEV // BRANCH


def chunk_keys(info, source, own, column, chunk):
    at = pl.multiple_of(info[6 + chunk], BRANCH)
    rows = pl.multiple_of(chunk * BRANCH, BRANCH)
    columns = slice(column, column + HEAD_DIM)
    return jnp.concatenate(
        [
            source[0:TRUNK, columns],
            source[pl.ds(at, BRANCH), columns],
            own[pl.ds(rows, BRANCH), columns],
        ],
        axis=0,
    )


def chunk_allowed(info, chunk, query_axis, shape):
    query_row = lax.broadcasted_iota(jnp.int32, shape, query_axis) & (BRANCH - 1)
    key = lax.broadcasted_iota(jnp.int32, shape, 1 - query_axis)
    leaves = info[1] == 0
    trunk = jnp.logical_and(jnp.logical_not(leaves), chunk < TRUNK // BRANCH)
    limit = jnp.where(trunk, chunk * BRANCH + query_row, TRUNK - 1)
    branch_limit = jnp.where(leaves, TRUNK + BRANCH - 1, 0)
    own_limit = jnp.where(trunk, 0, query_row + TRUNK + BRANCH)
    top = jnp.where(key < TRUNK, limit, jnp.where(key < TRUNK + BRANCH, branch_limit, own_limit))
    return key <= top


def group_rows(ref, g):
    first = g * GROUP
    return jnp.concatenate(
        [ref[:, 128 * h : 128 * h + 128] for h in range(first, first + GROUP)], axis=0
    )


def keep_source(info, partner, own, source):
    @pl.when(pl.program_id(0) == 0)
    def _():
        @pl.when(info[1] == 0)
        def _():
            source[...] = partner[...]

        @pl.when(info[1] != 0)
        def _():
            source[...] = own[...]


def attention_kernel(info, queries, own, partner, out, source):
    keep_source(info, partner, own, source)
    chunk = pl.program_id(0)
    rows = GROUP * BRANCH
    allowed = chunk_allowed(info, chunk, 0, (rows, KEYS))
    for g in range(KV_HEADS):
        keys = chunk_keys(info, source, own, 128 * g, chunk)
        values = chunk_keys(info, source, own, KEY_WIDTH + 128 * g, chunk)
        scores = nt(group_rows(queries, g), keys) * HEAD_DIM**-0.5
        scores = jnp.where(allowed, scores, MASKED)
        weights = jnp.exp(scores - jnp.max(scores, axis=1, keepdims=True))
        total = jnp.sum(weights, axis=1, keepdims=True)
        mixed = nn((weights * (1.0 / total)).astype(LOW), values).astype(LOW)
        for h in range(GROUP):
            at = (g * GROUP + h) * 128
            out[:, at : at + 128] = mixed[h * BRANCH : (h + 1) * BRANCH]


def attention(info, queries, own, partner):
    return pl.pallas_call(
        attention_kernel,
        grid=(CHUNKS,),
        out_shape=jax.ShapeDtypeStruct((TOK_DEV, D), LOW),
        in_specs=[
            SMEM,
            pl.BlockSpec((BRANCH, D), lambda i: (i, 0)),
            whole((TOK_DEV, 2 * KEY_WIDTH)),
            whole((TOK_DEV, 2 * KEY_WIDTH)),
        ],
        out_specs=pl.BlockSpec((BRANCH, D), lambda i: (i, 0)),
        scratch_shapes=[pltpu.VMEM((TOK_DEV, 2 * KEY_WIDTH), LOW)],
        compiler_params=params(),
        name="tree_attention",
    )(info, queries, own, partner)


def attention_back_kernel(
    info, queries, own, partner, grads, cosine, sine, grad_query, own_grad, source_grad, source
):
    keep_source(info, partner, own, source)
    chunk = pl.program_id(0)

    @pl.when(chunk == 0)
    def _():
        source_grad[...] = jnp.zeros_like(source_grad)

    rows = GROUP * BRANCH
    scale = HEAD_DIM**-0.5
    allowed = chunk_allowed(info, chunk, 1, (KEYS, rows))
    at = pl.multiple_of(info[6 + chunk], BRANCH)
    for g in range(KV_HEADS):
        keys = chunk_keys(info, source, own, 128 * g, chunk)
        values = chunk_keys(info, source, own, KEY_WIDTH + 128 * g, chunk)
        query_rows = group_rows(queries, g)
        grad_rows = group_rows(grads, g)
        scores = jnp.where(allowed, nt(keys, query_rows) * scale, MASKED)
        weights = jnp.exp(scores - jnp.max(scores, axis=0, keepdims=True))
        probs = weights * (1.0 / jnp.sum(weights, axis=0, keepdims=True))
        grad_probs = nt(values, grad_rows)
        mean = jnp.sum(probs * grad_probs, axis=0, keepdims=True)
        grad_scores = (probs * (grad_probs - mean)).astype(LOW)
        grad_values = nn(probs.astype(LOW), grad_rows)
        grad_keys = nn(grad_scores, query_rows) * scale
        grad_queries = tn(grad_scores, keys) * scale
        for h in range(GROUP):
            to = (g * GROUP + h) * 128
            grad_query[:, to : to + 128] = turn_back(
                grad_queries[h * BRANCH : (h + 1) * BRANCH], cosine[...], sine[...]
            ).astype(LOW)
        for column, grad in ((128 * g, grad_keys), (KEY_WIDTH + 128 * g, grad_values)):
            columns = slice(column, column + 128)
            source_grad[0:TRUNK, columns] += grad[0:TRUNK]
            source_grad[pl.ds(at, BRANCH), columns] += grad[TRUNK : TRUNK + BRANCH]
            own_grad[:, columns] = grad[TRUNK + BRANCH :]


def attention_back(info, queries, own, partner, grads, cosine, sine):
    chunked = pl.BlockSpec((BRANCH, D), lambda i: (i, 0))
    pair = (TOK_DEV, 2 * KEY_WIDTH)
    return pl.pallas_call(
        attention_back_kernel,
        grid=(CHUNKS,),
        out_shape=(
            jax.ShapeDtypeStruct((TOK_DEV, D), LOW),
            jax.ShapeDtypeStruct(pair, WIDE),
            jax.ShapeDtypeStruct(pair, WIDE),
        ),
        in_specs=[
            SMEM,
            chunked,
            whole(pair),
            whole(pair),
            chunked,
            pl.BlockSpec((BRANCH, 128), lambda i: (i, 0)),
            pl.BlockSpec((BRANCH, 128), lambda i: (i, 0)),
        ],
        out_specs=(
            chunked,
            pl.BlockSpec((BRANCH, 2 * KEY_WIDTH), lambda i: (i, 0)),
            whole(pair),
        ),
        scratch_shapes=[pltpu.VMEM(pair, LOW)],
        compiler_params=params(),
        name="tree_attention_back",
    )(info, queries, own, partner, grads, cosine, sine)


def out_kernel(info, heads, tokens, gain, *rest):
    count = len(rest) - 4
    refs, (residual, normed, weight, sem) = rest[:count], rest[count:]

    @pl.when(pl.program_id(0) == 0)
    def _():
        copies = weight_copies(info, refs, weight, sem, D // QUARTERS + 128, D // QUARTERS)
        run_all(copies)
        wait_all(copies)

    at = pl.ds(pl.multiple_of(pl.program_id(0) * 256, 256), 256)
    residual[:, at] = tokens[:, at].astype(WIDE) + nn(heads[...], weight[:, at])

    @pl.when(pl.program_id(0) == pl.num_programs(0) - 1)
    def _():
        values = residual[...]
        factor = lax.rsqrt(jnp.mean(values * values, axis=-1, keepdims=True) + EPSILON)
        normed[...] = (values * factor * gain[...]).astype(LOW)


def out_projection(info, heads, tokens, gain, refs):
    full = (TOK_DEV, D)
    return pl.pallas_call(
        out_kernel,
        grid=(D // 256,),
        out_shape=(jax.ShapeDtypeStruct(full, WIDE), jax.ShapeDtypeStruct(full, LOW)),
        in_specs=[SMEM, whole(full), whole(full), whole((1, D))] + [ANY] * len(refs),
        out_specs=(whole(full), whole(full)),
        scratch_shapes=[pltpu.VMEM((D, D), LOW), pltpu.SemaphoreType.DMA],
        compiler_params=params(),
        name="out_projection",
    )(info, heads, tokens, gain, *refs)


def dispatch_kernel(capacity, local, wide, order, info, rows, grads, routes, router, *rest):
    outs = rest[len(rest) // 2 - 1 : -2]
    token_outs, grad_outs = outs[:local], outs[local : 2 * local]
    share_outs, chosen_out, place_out = outs[2 * local : 3 * local], outs[-2], outs[-1]
    onehot, logits = rest[-2:]
    total = router.shape[1]
    step = pl.program_id(0)
    ids = lax.broadcasted_iota(jnp.int32, (total, TOK_DEV), 0)

    def hits():
        hit = ids == routes[0, 0:1]
        for k in range(1, TOP):
            hit = jnp.logical_or(hit, ids == routes[0, k : k + 1])
        return hit

    @pl.when(step == 0)
    def _():
        one = lax.broadcasted_iota(jnp.int32, (TOK_DEV, TOK_DEV), 0)
        two = lax.broadcasted_iota(jnp.int32, (TOK_DEV, TOK_DEV), 1)
        earlier = jnp.where(one < two, 1.0, 0.0).astype(LOW)
        hit = hits()
        rank = nn(jnp.where(hit, 1.0, 0.0).astype(LOW), earlier)
        place = jnp.where(hit, rank, -1.0)
        spots = lax.broadcasted_iota(jnp.int32, (capacity, TOK_DEV), 0).astype(WIDE)
        place_out[0] = jnp.full(place_out.shape[1:], -1.0, WIDE)
        for e in range(local):
            mine = ids == info[0] * local + e
            place_row = jnp.sum(jnp.where(mine, place, 0.0), axis=0, keepdims=True)
            place_out[0, e : e + 1] = place_row
            onehot[e * capacity : (e + 1) * capacity] = jnp.where(
                spots == place_row, 1.0, 0.0
            ).astype(LOW)
        chosen_out[0] = onehot[...]
        logits[...] = jnp.zeros_like(logits)

    block = rows[...]
    logits[...] += nn(block, router[...])
    for outs_of, source in ((token_outs, block), (grad_outs, grads[0])):
        rows_of = nn(onehot[...], source).astype(LOW)
        for e in range(local):
            outs_of[e][0] = rows_of[e * capacity : (e + 1) * capacity]

    @pl.when(step == pl.num_programs(0) - 1)
    def _():
        values = logits[...].T
        weights = jnp.exp(values - jnp.max(values, axis=0, keepdims=True))
        share = weights / jnp.sum(jnp.where(hits(), weights, 0.0), axis=0, keepdims=True)
        for e in range(local):
            mine = ids == info[0] * local + e
            share_row = jnp.sum(jnp.where(mine, share, 0.0), axis=0, keepdims=True)
            chosen = onehot[e * capacity : (e + 1) * capacity].astype(WIDE)
            share_outs[e][0] = jnp.sum(chosen * share_row, axis=1, keepdims=True)


def dispatch(order, info, rows, grads, routes, router, capacity, local, earlier):
    count = grads.shape[0]
    total = router.shape[1]
    wide = 512
    picked = pl.BlockSpec((1, capacity, wide), lambda i, order, info: (order[0], 0, i))

    def fixed(shape):
        return pl.BlockSpec((1,) + shape, lambda i, order, info: (order[0], 0, 0))

    out_shape = (
        [jax.ShapeDtypeStruct((count, capacity, D), LOW)] * (2 * local)
        + [jax.ShapeDtypeStruct((count, capacity, 1), WIDE)] * local
        + [
            jax.ShapeDtypeStruct((count, local * capacity, TOK_DEV), LOW),
            jax.ShapeDtypeStruct((count, 8, TOK_DEV), WIDE),
        ]
    )
    if earlier is None:
        earlier = [jnp.zeros((8, 128), shape.dtype) for shape in out_shape]
        aliases = {}
    else:
        aliases = {6 + i: i for i in range(len(out_shape))}
    return pl.pallas_call(
        functools.partial(dispatch_kernel, capacity, local, wide),
        grid_spec=pltpu.PrefetchScalarGridSpec(
            num_scalar_prefetch=2,
            grid=(D // wide,),
            in_specs=[
                pl.BlockSpec((TOK_DEV, wide), lambda i, order, info: (0, i)),
                pl.BlockSpec((1, TOK_DEV, wide), lambda i, order, info: (order[1], 0, i)),
                pl.BlockSpec((1, TOP, TOK_DEV), lambda i, order, info: (order[1], 0, 0)),
                pl.BlockSpec((wide, total), lambda i, order, info: (i, 0)),
            ]
            + [ANY] * len(out_shape),
            out_specs=[picked] * (2 * local)
            + [fixed((capacity, 1))] * local
            + [fixed((local * capacity, TOK_DEV)), fixed((8, TOK_DEV))],
            scratch_shapes=[
                pltpu.VMEM((local * capacity, TOK_DEV), LOW),
                pltpu.VMEM((TOK_DEV, total), WIDE),
            ],
        ),
        out_shape=out_shape,
        input_output_aliases=aliases,
        compiler_params=params(),
        name="dispatch",
    )(order, info, rows, grads, routes, router, *earlier)


def spread_kernel(local, place, *rest):
    dots, out = rest[:local], rest[local]
    spots = lax.broadcasted_iota(jnp.int32, (dots[0].shape[1], TOK_DEV), 0).astype(WIDE)
    for e in range(local):
        chosen = spots == place[0, e : e + 1]
        out[0, e : e + 1] = jnp.sum(jnp.where(chosen, dots[e][0], 0.0), axis=0, keepdims=True)


def spread(place, dots):
    count, capacity, _ = dots[0].shape
    local = len(dots)
    return pl.pallas_call(
        functools.partial(spread_kernel, local),
        grid=(count,),
        out_shape=jax.ShapeDtypeStruct((count, local, TOK_DEV), WIDE),
        in_specs=[pl.BlockSpec((1, 8, TOK_DEV), lambda i: (i, 0, 0))]
        + [pl.BlockSpec((1, capacity, 1), lambda i: (i, 0, 0))] * local,
        out_specs=pl.BlockSpec((1, local, TOK_DEV), lambda i: (i, 0, 0)),
        compiler_params=params(),
        name="spread",
    )(place, *dots)


def expert_kernel(slots, info, rows, grads, shares, *rest):
    count = len(rest) - 7
    refs = rest[:count]
    out_rows, back_rows, grad_rows, acts, dots, weight, sem = rest[count:]
    part = weight.shape[1] // slots

    @pl.when(pl.program_id(0) == 0)
    def _():
        def copies(ref, slot):
            return [
                pltpu.make_async_copy(
                    ref.at[pl.ds(which * part, part)],
                    weight.at[which, pl.ds(slot * part, part)],
                    sem,
                )
                for which in range(3)
            ]

        if count == slots:
            for slot in range(slots):
                run_all(copies(refs[slot], slot))
        else:
            block, second, above, below, far = refs
            low_end = info[2] == 0
            end = jnp.logical_or(low_end, info[2] == 3)
            run_all(copies(block, 0))
            run_all(copies(second, 1))

            @pl.when(low_end)
            def _():
                run_all(copies(above, 2))

            @pl.when(jnp.logical_not(low_end))
            def _():
                run_all(copies(below, 2))

            @pl.when(end)
            def _():
                run_all(copies(far, 3))

            @pl.when(jnp.logical_not(end))
            def _():
                run_all(copies(above, 3))

        for slot in range(slots):
            wait_all(copies(refs[0], slot))

    row_block = rows[...]
    share = shares[...]
    grad_float = grads[...].astype(WIDE)
    grad_low = (share * grad_float).astype(LOW)
    grad_rows[...] = grad_low
    gate_act = nt(row_block, weight[0])
    upward = nt(row_block, weight[1])
    sigmoid = 1.0 / (1.0 + jnp.exp(-gate_act))
    silu = gate_act * sigmoid
    hidden = (silu * upward).astype(LOW)
    expert_out = nn(hidden, weight[2]).astype(LOW).astype(WIDE)
    out_rows[...] = (share * expert_out).astype(LOW)
    dots[...] = jnp.sum(grad_float * expert_out, axis=1, keepdims=True)
    grad_hidden = nt(grad_low, weight[2])
    grad_gate = (grad_hidden * upward * sigmoid * (1.0 + gate_act * (1.0 - sigmoid))).astype(LOW)
    grad_up = (grad_hidden * silu).astype(LOW)
    back_rows[...] = (nn(grad_gate, weight[0]) + nn(grad_up, weight[1])).astype(LOW)
    for which, act in enumerate((grad_gate, grad_up, hidden)):
        turned = act.T
        for slot in range(slots):
            acts[slot, which * part : (which + 1) * part] = turned[
                slot * part : (slot + 1) * part
            ]


EXPERT_ROWS = 256


def expert(info, rows, grads, shares, refs, slots):
    height = rows.shape[0]
    part = refs[0].shape[0] // 3
    wide_block = pl.BlockSpec((EXPERT_ROWS, D), lambda i: (i, 0))
    thin_block = pl.BlockSpec((EXPERT_ROWS, 1), lambda i: (i, 0))
    return pl.pallas_call(
        functools.partial(expert_kernel, slots),
        grid=(height // EXPERT_ROWS,),
        out_shape=[jax.ShapeDtypeStruct((height, D), LOW)] * 3
        + [
            jax.ShapeDtypeStruct((slots, 3 * part, height), LOW),
            jax.ShapeDtypeStruct((height, 1), WIDE),
        ],
        in_specs=[SMEM, wide_block, wide_block, thin_block] + [ANY] * len(refs),
        out_specs=[wide_block] * 3
        + [pl.BlockSpec((slots, 3 * part, EXPERT_ROWS), lambda i: (0, 0, i)), thin_block],
        scratch_shapes=[pltpu.VMEM((3, slots * part, D), LOW), pltpu.SemaphoreType.DMA],
        compiler_params=params(),
        name="expert",
    )(info, rows, grads, shares, *refs)


def expert_grads_kernel(slots, rows, grads, *rest):
    acts, outs = rest[: len(slots)], rest[len(slots) :]
    part = acts[0].shape[1] // 3
    at = pl.ds(pl.multiple_of(pl.program_id(0) * 256, 256), 256)
    for act, out in zip(acts, outs):
        out[: 2 * part, :] = nn(act[0, : 2 * part], rows[:, at]).astype(LOW)
        out[2 * part :, :] = nn(act[0, 2 * part :], grads[:, at]).astype(LOW)


def expert_grads(acts, rows, grads, slots):
    _, part, height = acts.shape
    return pl.pallas_call(
        functools.partial(expert_grads_kernel, slots),
        grid=(D // 256,),
        out_shape=[jax.ShapeDtypeStruct((part, D), LOW) for _ in slots],
        in_specs=[whole((height, D))] * 2
        + [pl.BlockSpec((1, part, height), lambda i, s=slot: (s, 0, 0)) for slot in slots],
        out_specs=[pl.BlockSpec((part, 256), lambda i: (0, i)) for _ in slots],
        compiler_params=params(),
        name="expert_gradients",
    )(rows, grads, *[acts] * len(slots))


def combine_kernel(local, chosen, *rest):
    rows, out = rest[:local], rest[local]
    both = jnp.concatenate([ref[0] for ref in rows], axis=0)
    out[0] = tn(chosen[0], both).astype(LOW)


def combine(chosen, rows, first, step):
    count, capacity, _ = rows[0].shape
    number = (count - first + step - 1) // step
    return pl.pallas_call(
        functools.partial(combine_kernel, len(rows)),
        grid=(number,),
        out_shape=jax.ShapeDtypeStruct((number, TOK_DEV, D), LOW),
        in_specs=[
            pl.BlockSpec((1,) + chosen.shape[1:], lambda i: (first + step * i, 0, 0))
        ]
        + [pl.BlockSpec((1, capacity, D), lambda i: (first + step * i, 0, 0))] * len(rows),
        out_specs=pl.BlockSpec((1, TOK_DEV, D), lambda i: (i, 0, 0)),
        compiler_params=params(),
        name="combine",
    )(chosen, *rows)


def split(values):
    high = values.astype(LOW)
    return high, (values - high.astype(WIDE)).astype(LOW)


def norm_back(values, gain, grad):
    factor = lax.rsqrt(jnp.mean(values * values, axis=-1, keepdims=True) + EPSILON)
    scaled = gain * grad
    mean = jnp.mean(values * scaled, axis=-1, keepdims=True)
    grad_values = factor * scaled - values * (factor * factor * factor * mean)
    grad_gain = jnp.sum(grad * values * factor, axis=0, keepdims=True)
    return grad_values, grad_gain


def router_back(logits, routes, grad_shares):
    ids = lax.broadcasted_iota(jnp.int32, logits.shape, 0)
    hit = ids == routes[0:1]
    for k in range(1, TOP):
        hit = jnp.logical_or(hit, ids == routes[k : k + 1])
    weights = jnp.exp(logits - jnp.max(logits, axis=0, keepdims=True))
    probs = weights / jnp.sum(weights, axis=0, keepdims=True)
    chosen = jnp.sum(jnp.where(hit, probs, 0.0), axis=0, keepdims=True)
    grads = jnp.where(hit, grad_shares, 0.0)
    mean = jnp.sum(probs * grads, axis=0, keepdims=True) / chosen
    grad_probs = jnp.where(hit, (grads - mean) / chosen, 0.0)
    return probs * (grad_probs - jnp.sum(probs * grad_probs, axis=0, keepdims=True))


def branch_back_kernel(
    parts, info, residual, normed, cotangent, routes, grad_shares, router, gain, *rest
):
    sums, rest = rest[:parts], rest[parts:]
    count = len(rest) - 7
    refs = rest[:count]
    grad_residual, grad_branch, grad_heads, grad_gain, grad_router, weight, sem = rest[count:]

    @pl.when(pl.program_id(0) == 0)
    def _():
        copies = weight_copies(info, refs, weight, sem, D // QUARTERS + 128, D // QUARTERS)
        run_all(copies)
        logits = nt(router[...], normed[...])
        high, low = split(router_back(logits, routes[...], grad_shares[...]))
        grad_router[...] = nn(high, normed[...]) + nn(low, normed[...])
        grad_normed = tn(high, router[...]) + tn(low, router[...])
        if parts == 1:
            grad_normed += sums[0][...]
        else:
            values = [ref[...].astype(WIDE) for ref in sums]
            grad_normed += jnp.concatenate(
                [values[0] + values[1] + values[2], values[3] + values[4] + values[5]], axis=0
            )
        grad_values, gain_grad = norm_back(residual[...], gain[...], grad_normed)
        grad_gain[...] = gain_grad
        total = cotangent[...].astype(WIDE) + grad_values
        grad_residual[...] = total
        grad_branch[...] = total.astype(LOW)
        wait_all(copies)

    at = pl.ds(pl.multiple_of(pl.program_id(0) * 256, 256), 256)
    grad_heads[...] = nt(grad_branch[...], weight[at, :]).astype(LOW)


def branch_back(info, residual, normed, sums, cotangent, routes, grad_shares, router, gain, refs):
    full = (TOK_DEV, D)
    total = router.shape[0]
    return pl.pallas_call(
        functools.partial(branch_back_kernel, len(sums)),
        grid=(D // 256,),
        out_shape=(
            jax.ShapeDtypeStruct(full, WIDE),
            jax.ShapeDtypeStruct(full, LOW),
            jax.ShapeDtypeStruct(full, LOW),
            jax.ShapeDtypeStruct((1, D), WIDE),
            jax.ShapeDtypeStruct((total, D), WIDE),
        ),
        in_specs=[SMEM]
        + [whole(full)] * 3
        + [whole((TOP, TOK_DEV)), whole((total, TOK_DEV)), whole((total, D)), whole((1, D))]
        + [whole(part.shape) for part in sums]
        + [ANY] * len(refs),
        out_specs=(
            whole(full),
            whole(full),
            pl.BlockSpec((TOK_DEV, 256), lambda i: (0, i)),
            whole((1, D)),
            whole((total, D)),
        ),
        scratch_shapes=[pltpu.VMEM((D, D), LOW), pltpu.SemaphoreType.DMA],
        compiler_params=params(),
        name="experts_norm_back",
    )(info, residual, normed, cotangent, routes, grad_shares, router, gain, *sums, *refs)


def join_grads_kernel(info, own_grad, source_grad, arrived, cosine, sine, out):
    half = HEAD_DIM // 2
    first = lax.broadcasted_iota(jnp.int32, (TOK_DEV, HEAD_DIM), 1) < half
    leaves = info[1] == 0

    def total(column):
        columns = slice(column, column + 128)
        extra = source_grad[:, columns] + arrived[:, columns].astype(WIDE)
        return own_grad[:, columns] + jnp.where(leaves, 0.0, extra)

    for g in range(KV_HEADS):
        key = turn_back(total(128 * g), cosine[...], sine[...])
        value = total(KEY_WIDTH + 128 * g)
        out[:, 256 * g : 256 * g + 128] = jnp.where(
            first, key, pltpu.roll(value, half, 1)
        ).astype(LOW)
        out[:, 256 * g + 128 : 256 * g + 256] = jnp.where(
            first, pltpu.roll(key, half, 1), value
        ).astype(LOW)


def join_grads(info, own_grad, source_grad, arrived, cosine, sine):
    vmem = pl.BlockSpec(memory_space=pltpu.VMEM)
    return pl.pallas_call(
        join_grads_kernel,
        out_shape=jax.ShapeDtypeStruct((TOK_DEV, 2 * KEY_WIDTH), LOW),
        in_specs=[SMEM] + [vmem] * 5,
        out_specs=vmem,
        compiler_params=params(),
        name="join_key_value_gradients",
    )(info, own_grad, source_grad, arrived, cosine, sine)


def token_back_kernel(info, grad_query, grad_pair, tokens, grad_residual, gain, *rest):
    count = (len(rest) - 6) // 2
    query_refs, pair_refs = rest[:count], rest[count : 2 * count]
    out, grad_gain, query_weight, pair_weight, grad_normed, sem = rest[2 * count :]

    @pl.when(pl.program_id(0) == 0)
    def _():
        copies = weight_copies(info, query_refs, query_weight, sem, 0, D // QUARTERS)
        copies += weight_copies(info, pair_refs, pair_weight, sem, D // QUARTERS, 128)
        run_all(copies)
        wait_all(copies)

    at = pl.ds(pl.multiple_of(pl.program_id(0) * 256, 256), 256)
    grad_normed[:, at] = nt(grad_query[...], query_weight[at, :]) + nt(
        grad_pair[...], pair_weight[at, :]
    )

    @pl.when(pl.program_id(0) == pl.num_programs(0) - 1)
    def _():
        grad_values, gain_grad = norm_back(
            tokens[...].astype(WIDE), gain[...], grad_normed[...]
        )
        grad_gain[...] = gain_grad
        out[...] = (grad_residual[...] + grad_values).astype(LOW)


def token_back(info, grad_query, grad_pair, tokens, grad_residual, gain, query_refs, pair_refs):
    full = (TOK_DEV, D)
    return pl.pallas_call(
        token_back_kernel,
        grid=(D // 256,),
        out_shape=(jax.ShapeDtypeStruct(full, LOW), jax.ShapeDtypeStruct((1, D), WIDE)),
        in_specs=[
            SMEM,
            whole(full),
            whole((TOK_DEV, 2 * KEY_WIDTH)),
            whole(full),
            whole(full),
            whole((1, D)),
        ]
        + [ANY] * (len(query_refs) + len(pair_refs)),
        out_specs=(whole(full), whole((1, D))),
        scratch_shapes=[
            pltpu.VMEM((D, D), LOW),
            pltpu.VMEM((D, 2 * KEY_WIDTH), LOW),
            pltpu.VMEM(full, WIDE),
            pltpu.SemaphoreType.DMA,
        ],
        compiler_params=params(),
        name="token_gradient",
    )(info, grad_query, grad_pair, tokens, grad_residual, gain, *query_refs, *pair_refs)


def weight_grads_kernel(info, normed, heads, grad_query, grad_pair, grad_branch, keep, send):
    quarter = D // QUARTERS
    depth = keep.shape[2]
    core = info[0] & 1

    def store(grads, start, width):
        low = grads.astype(LOW)
        for slot in range(QUARTERS):
            shard = info[2 + slot]
            for j in range(QUARTERS):
                piece = low[:, j * width : (j + 1) * width]
                upper, lower = piece[:depth], piece[depth:]

                @pl.when(shard == j)
                def _():
                    columns = slice(start, start + width)
                    keep[0, slot, :, columns] = jnp.where(core == 0, upper, lower)
                    send[0, slot, :, columns] = jnp.where(core == 0, lower, upper)

    store(tn(normed[...], grad_query[...]), 0, quarter)
    store(tn(normed[...], grad_pair[...]), quarter, 128)
    store(tn(heads[...], grad_branch[...]), quarter + 128, quarter)


def weight_grads(info, normed, heads, grad_query, grad_pair, grad_branch):
    full = (TOK_DEV, D)
    quarter = D // QUARTERS
    width = 2 * quarter + 128
    strip = pl.BlockSpec((TOK_DEV, quarter), lambda i, info: (0, i ^ (info[0] >> 1)))
    shape = (4, QUARTERS, quarter // 2, width)
    out = pl.BlockSpec((1,) + shape[1:], lambda i, info: (i, 0, 0, 0))

    def fixed(block):
        return pl.BlockSpec(block, lambda i, info: (0, 0))

    return pl.pallas_call(
        weight_grads_kernel,
        grid_spec=pltpu.PrefetchScalarGridSpec(
            num_scalar_prefetch=1,
            grid=(4,),
            in_specs=[
                strip,
                strip,
                fixed(full),
                fixed((TOK_DEV, 2 * KEY_WIDTH)),
                fixed(full),
            ],
            out_specs=(out, out),
        ),
        out_shape=(jax.ShapeDtypeStruct(shape, LOW),) * 2,
        compiler_params=params(),
        name="weight_gradients",
    )(info, normed, heads, grad_query, grad_pair, grad_branch)


def position_of(token_index):
    branch_place = TRUNK + (token_index - TRUNK) % BRANCH
    leaf_place = TRUNK + BRANCH + (token_index - TOK_DEV) % BRANCH
    return jnp.where(
        token_index < TRUNK, token_index, jnp.where(token_index < TOK_DEV, branch_place, leaf_place)
    )


def rotary_tables(positions):
    half_dim = HEAD_DIM // 2
    frequency = ROPE_BASE ** (-jnp.arange(half_dim, dtype=jnp.float32) / half_dim)
    angles = positions.astype(jnp.float32)[:, None] * frequency[None, :]
    cosine, sine = (jnp.cos(angles), jnp.sin(angles))
    return (
        jnp.concatenate([cosine, cosine], axis=1),
        jnp.concatenate([-sine, sine], axis=1),
    )


def after(values, *earlier):
    return lax.optimization_barrier((values, earlier))[0]


def fast_mesh():
    return lax.axis_size("rows") == 8 and lax.axis_size("cols") == 4


SLOT_SHARD = ((0, 2, 1, 3), (1, 3, 0, 2), (2, 0, 1, 3), (3, 1, 2, 0))
UP = [(0, 1), (1, 2), (2, 3)]
DOWN = [(1, 0), (2, 1), (3, 2)]
FAR = [(0, 3), (3, 0)]


def send_first(block):
    return (
        lax.ppermute(block, "cols", DOWN),
        lax.ppermute(block, "cols", UP),
        lax.ppermute(block, "cols", FAR),
    )


def send_second(block, first):
    place = lax.axis_index("cols")
    above, below, _ = first
    payload = jnp.where(place == 1, above, jnp.where(place == 2, below, block))
    return lax.ppermute(payload, "cols", [(3, 1), (1, 0), (0, 2), (2, 3)])


def slot_list(block, first, second):
    place = lax.axis_index("cols")
    above, below, far = first
    end = (place == 0) | (place == 3)
    return [
        block,
        second,
        jnp.where(place == 0, above, below),
        jnp.where(end, far, above),
    ]


def reduce_first(second, fourth):
    return (
        lax.ppermute(second, "cols", [(1, 3), (0, 1), (2, 0), (3, 2)]),
        lax.ppermute(fourth, "cols", FAR),
    )


def reduce_second(third, fourth, relay):
    place = lax.axis_index("cols")
    relayed = relay.astype(WIDE)
    upward_load = (
        jnp.where(place == 0, third, fourth).astype(WIDE) + jnp.where(place == 1, relayed, 0.0)
    ).astype(LOW)
    downward_load = (third.astype(WIDE) + jnp.where(place == 2, relayed, 0.0)).astype(LOW)
    return (
        lax.ppermute(upward_load, "cols", UP),
        lax.ppermute(downward_load, "cols", DOWN),
    )


def reduce_last(own, first, second):
    place = lax.axis_index("cols")
    relay, far = first
    below, above = second
    end = (place == 0) | (place == 3)
    return (
        own.astype(WIDE)
        + below.astype(WIDE)
        + above.astype(WIDE)
        + jnp.where(end, relay.astype(WIDE) + far.astype(WIDE), 0.0)
    )


def flip(block, bit):
    count = lax.axis_size("rows")
    return lax.ppermute(block, "rows", [(i, i ^ bit) for i in range(count)])


def add_low(one, two):
    return (one.astype(WIDE) + two.astype(WIDE)).astype(LOW)


def reduce_chips(keep, got):
    half = keep.shape[1] // 2

    def sums(chips, part):
        return jnp.stack([add_low(keep[i][part], got[i][part]) for i in chips])

    one, two = slice(0, half), slice(half, None)
    got_x = flip(sums((1, 3), one), 2)
    got_y = flip(sums((2, 3), two), 4)
    near_x = sums((0, 2), one)
    near_y = sums((0, 1), two)
    got_xy = flip(add_low(near_x[1], got_x[1]), 4)
    got_yx = flip(add_low(near_y[1], got_y[1]), 2)
    return (near_x[0], got_x[0], got_xy, near_y[0], got_y[0], got_yx)


def sum_parts(parts):
    wide = [a.astype(WIDE) for a in parts]
    if len(wide) == 1:
        return wide[0]
    return jnp.concatenate([wide[0] + wide[1] + wide[2], wide[3] + wide[4] + wide[5]], axis=0)


def on_device(
    tokens,
    query_weight,
    key_weight,
    value_weight,
    out_weight,
    router_weight,
    attention_gain,
    experts_gain,
    gate_weight,
    upward_weight,
    down_weight,
    routes,
    leaf_parent,
    cotangent,
):
    row_count = lax.axis_size("rows")
    col_count = lax.axis_size("cols")
    row_place = lax.axis_index("rows")
    col_place = lax.axis_index("cols")
    fast = fast_mesh()
    parity = lax.rem(col_place, 2)
    tree_id = lax.div(row_place * col_count + col_place, 2)
    parent_row = lax.dynamic_slice_in_dim(leaf_parent, tree_id, 1, 0)[0]
    depth, query_part = query_weight.shape
    key_part = key_weight.shape[1]
    router_part = router_weight.shape[1]
    gain_part = attention_gain.shape[0]
    expert_total = router_part * col_count
    local_experts = gate_weight.shape[0]
    capacity = TOK_DEV * TOP // expert_total * 5 // 4

    shards = (
        jnp.asarray(SLOT_SHARD, jnp.int32)[col_place]
        if fast
        else jnp.arange(4, dtype=jnp.int32)
    )
    branch_rows = jnp.where(parity == 0, TRUNK + BRANCH * parent_row, TRUNK)
    info = jnp.concatenate(
        [jnp.stack([row_place, parity]), shards, branch_rows, jnp.zeros((2,), jnp.int32)]
    ).astype(jnp.int32)

    small = jnp.concatenate([attention_gain, experts_gain, router_weight.reshape(-1)])
    small = jnp.pad(small, (0, 2048 - small.shape[0])).reshape(16, 128)
    small_all = lax.all_gather(lax.all_gather(small, "cols", axis=0), "rows", axis=0)
    small_all = small_all.reshape(row_count * col_count, -1)
    small_all = small_all[:, : 2 * gain_part + depth * router_part]
    attention_scale = small_all[:, :gain_part].reshape(1, D).astype(WIDE)
    experts_scale = small_all[:, gain_part : 2 * gain_part].reshape(1, D).astype(WIDE)
    router_rows = jnp.transpose(
        small_all[:, 2 * gain_part :].reshape(row_count, col_count, depth, router_part),
        (1, 3, 0, 2),
    ).reshape(expert_total, D)

    packed = jnp.concatenate([query_weight, key_weight, value_weight, out_weight], axis=1)
    shard_blocks = [
        jnp.concatenate(
            [gate_weight[expert].T, upward_weight[expert].T, down_weight[expert]], axis=0
        )
        for expert in range(local_experts)
    ]
    firsts, seconds = ([], [])
    if fast:
        packed_first = send_first(packed)
        packed_second = send_second(packed, packed_first)
        own = jnp.stack(slot_list(packed, packed_first, packed_second))
        ahead = packed_second
        for expert_at in range(local_experts):
            block = after(shard_blocks[expert_at], ahead)
            shard_blocks[expert_at] = block
            first = send_first(block)
            firsts.append(first)
            seconds.append(send_second(block, first))
            ahead = first
        beside, across = flip(own, 2), flip(own, 4)
        corner = [flip(beside[:2], 4), flip(across[2:], 2)]
        same = [own, beside, across] + corner
        pieces = same + [flip(piece, 1) for piece in same]
        query_refs = pair_refs = out_refs = pieces
        expert_refs = [
            [shard_blocks[i], seconds[i], *firsts[i]] for i in range(local_experts)
        ]
    else:
        packed_all = lax.all_gather(lax.all_gather(packed, "cols", axis=0), "rows", axis=0)

        def unpack(start, width):
            part = packed_all[..., start : start + width]
            return jnp.swapaxes(part, 1, 2).reshape(row_count * depth, col_count * width)

        key_at = query_part
        query_refs = [unpack(0, query_part)]
        pair_refs = [
            jnp.concatenate(
                [
                    unpack(key_at, key_part).reshape(D, QUARTERS, -1),
                    unpack(key_at + key_part, key_part).reshape(D, QUARTERS, -1),
                ],
                axis=2,
            ).reshape(D, -1)
        ]
        out_refs = [unpack(key_at + 2 * key_part, query_part)]
        expert_refs = [
            [lax.all_gather(block, "cols", axis=0)[i] for i in range(col_count)]
            for block in shard_blocks
        ]

    routes_all = lax.all_gather(routes.T, "rows", axis=0)
    grad_in = after(cotangent, *pieces) if fast else cotangent
    grad_all = lax.all_gather(grad_in, "rows", axis=0)

    local_index = (1 - parity) * TOK_DEV + jnp.arange(TOK_DEV, dtype=jnp.int32)
    cosine, sine = rotary_tables(position_of(local_index))
    normed, own_pair = key_value(info, tokens, attention_scale, cosine, sine, pair_refs)
    pairs = [(i + 1, i) for i in range(0, col_count, 2)]
    partner = lax.ppermute(own_pair, "cols", pairs)
    queries = query(info, normed, cosine, sine, query_refs)
    if fast:
        queries = after(queries, *firsts[0])
    heads = attention(info, queries, own_pair, partner)
    residual, normed_two = out_projection(info, heads, tokens, experts_scale, out_refs)

    if fast:
        grad_all = after(grad_all, normed_two)
        beside, across = flip(normed_two, 2), flip(normed_two, 4)
        half = TOK_DEV // 2
        corner = jnp.concatenate([flip(beside[:half], 4), flip(across[half:], 2)], axis=0)
        near = [normed_two, beside, across, corner]
        blocks = [block for one in near for block in (one, flip(one, 1))]
        turns = [0, 1, 2, 3, 4, 5, 6, 7]
        places = [row_place ^ q for q in range(row_count)]
    else:
        rows_all = lax.all_gather(normed_two, "rows", axis=0)
        blocks = [rows_all[q] for q in range(row_count)]
        turns = list(range(row_count))
        places = turns
    router_cols = router_rows.T
    picked = None
    for q in turns:
        order = jnp.stack([jnp.int32(q), jnp.asarray(places[q], jnp.int32)])
        block = blocks[q]
        if fast and q == 4:
            block = after(block, *firsts[1])
        picked = dispatch(
            order, info, block, grad_all, routes_all, router_cols, capacity, local_experts, picked
        )
    height = row_count * capacity
    token_rows = [a.reshape(height, D) for a in picked[:local_experts]]
    grad_rows = [a.reshape(height, D) for a in picked[local_experts : 2 * local_experts]]
    share_rows = [a.reshape(height, 1) for a in picked[2 * local_experts : 3 * local_experts]]
    chosen, place_rows = picked[-2:]

    out_rows, back_rows, gate_dots, reduced, marks = ([], [], [], [], [])
    for e in range(local_experts):
        rows_in = token_rows[e]
        if fast and e == 0:
            rows_in = after(rows_in, seconds[0])
        if fast and e == 1:
            rows_in = after(rows_in, seconds[1])
        out_row, back_row, grad_row, acts, dots = expert(
            info, rows_in, grad_rows[e], share_rows[e], expert_refs[e], col_count
        )
        out_rows.append(out_row.reshape(row_count, capacity, D))
        back_rows.append(back_row.reshape(row_count, capacity, D))
        gate_dots.append(dots.reshape(row_count, capacity, 1))
        if fast:
            if e == 1:
                acts = after(acts, *marks[0])
            second, fourth = expert_grads(acts, token_rows[e], grad_row, (1, 3))
            sent_first = reduce_first(second, fourth)
            marks.append([sent_first[0]])
            own_slot, third = expert_grads(acts, token_rows[e], grad_row, (0, 2))
            sent_second = reduce_second(third, fourth, sent_first[0])
            reduced.append((own_slot, sent_first, sent_second))
        else:
            slots = expert_grads(acts, token_rows[e], grad_row, tuple(range(col_count)))
            reduced.append(
                lax.psum_scatter(jnp.stack(slots), "cols", scatter_dimension=0).astype(WIDE)
            )

    spread_dots = spread(place_rows, gate_dots)
    if fast:
        spread_dots = jnp.take(
            spread_dots, row_place ^ jnp.arange(row_count, dtype=jnp.int32), axis=0
        )
    grad_shares = lax.all_to_all(spread_dots, "rows", split_axis=0, concat_axis=0, tiled=True)
    grad_shares = grad_shares.reshape(expert_total, TOK_DEV)
    if fast:
        back_rows = [after(a, *reduced[1][0:1]) for a in back_rows]

        def both_ways(rows):
            got = flip(combine(chosen, rows, 1, 2), 1)
            return reduce_chips(combine(chosen, rows, 0, 2), got)

        back_parts = both_ways(back_rows)
        out_rows = [after(a, *back_parts) for a in out_rows]
        mixture = both_ways(out_rows)
        grad_shares = after(grad_shares, reduced[0][1][1], *reduced[0][2])
    else:

        def summed(rows):
            part = combine(chosen, rows, 0, 1)
            return (lax.psum_scatter(part, "rows", scatter_dimension=0).astype(WIDE),)

        back_parts = summed(back_rows)
        mixture = summed(out_rows)

    grad_residual, grad_branch, grad_heads, experts_gain_grad, router_grad = branch_back(
        info,
        residual,
        normed_two,
        back_parts,
        cotangent,
        routes.T,
        grad_shares,
        router_rows,
        experts_scale,
        out_refs,
    )
    if fast:
        grad_heads = after(grad_heads, reduced[1][1][0])
    grad_query, own_grad, source_grad = attention_back(
        info, queries, own_pair, partner, grad_heads, cosine, sine
    )
    arrived = lax.ppermute(source_grad.astype(LOW), "cols", [(j, i) for i, j in pairs])
    grad_pair = join_grads(info, own_grad, source_grad, arrived, cosine, sine)
    tokens_grad, attention_gain_grad = token_back(
        info, grad_query, grad_pair, tokens, grad_residual, attention_scale, query_refs, pair_refs
    )

    layer_output = (residual + sum_parts(mixture)).astype(LOW)
    if fast:
        keep, send = weight_grads(info, normed, heads, grad_query, grad_pair, grad_branch)
        slots = sum_parts(reduce_chips(keep, flip(send, 1))).astype(LOW)
        sent_first = reduce_first(slots[1], slots[3])
        sent_second = reduce_second(slots[2], slots[3], sent_first[0])
        sums = reduce_last(slots[0], sent_first, sent_second)
        expert_sums = [reduce_last(*parts) for parts in reduced]
    else:
        full_grads = [
            tn(normed, grad_query),
            *jnp.moveaxis(tn(normed, grad_pair).reshape(D, QUARTERS, 2, -1), 2, 0),
            tn(heads, grad_branch),
        ]
        packed_grad = jnp.concatenate(
            [
                grad.astype(LOW).reshape(row_count, depth, col_count, -1)
                for grad in full_grads
            ],
            axis=3,
        )
        row_sums = lax.psum_scatter(packed_grad, "rows", scatter_dimension=0)
        sums = lax.psum_scatter(row_sums, "cols", scatter_dimension=1).astype(WIDE)
        expert_sums = reduced

    small_grads = jnp.concatenate(
        [
            attention_gain_grad.reshape(-1, gain_part),
            experts_gain_grad.reshape(-1, gain_part),
            jnp.transpose(
                router_grad.reshape(col_count, router_part, row_count, depth), (2, 0, 3, 1)
            ).reshape(row_count * col_count, depth * router_part),
        ],
        axis=1,
    )
    small_grads = small_grads.reshape(row_count, -1)
    small_grads = lax.all_to_all(small_grads, "rows", split_axis=0, concat_axis=0, tiled=True)
    small_grads = jnp.sum(small_grads, axis=0).reshape(col_count, -1)
    small_grads = lax.all_to_all(small_grads, "cols", split_axis=0, concat_axis=0, tiled=True)
    small_sums = jnp.sum(small_grads, axis=0)

    key_at = query_part
    value_at = key_at + key_part
    out_at = value_at + key_part
    part = down_weight.shape[1]
    gate_grad, upward_grad, down_grad = (
        jnp.stack([sums_of[which * part : (which + 1) * part] for sums_of in expert_sums])
        for which in range(3)
    )
    return (
        layer_output,
        tokens_grad,
        sums[:, :key_at],
        sums[:, key_at:value_at],
        sums[:, value_at:out_at],
        sums[:, out_at:],
        small_sums[2 * gain_part :].reshape(depth, router_part),
        small_sums[:gain_part],
        small_sums[gain_part : 2 * gain_part],
        jnp.swapaxes(gate_grad, 1, 2),
        jnp.swapaxes(upward_grad, 1, 2),
        down_grad,
    )


def solution(mesh):
    in_specs = (
        P(("rows", "cols"), None),
        P("rows", "cols"),
        P("rows", "cols"),
        P("rows", "cols"),
        P("rows", "cols"),
        P("rows", "cols"),
        P(("rows", "cols")),
        P(("rows", "cols")),
        P("rows", None, "cols"),
        P("rows", None, "cols"),
        P("rows", "cols", None),
        P(("rows", "cols"), None),
        P(),
        P(("rows", "cols"), None),
    )
    out_specs = (
        P(("rows", "cols"), None),
        P(("rows", "cols"), None),
        P("rows", "cols"),
        P("rows", "cols"),
        P("rows", "cols"),
        P("rows", "cols"),
        P("rows", "cols"),
        P(("rows", "cols")),
        P(("rows", "cols")),
        P("rows", None, "cols"),
        P("rows", None, "cols"),
        P("rows", "cols", None),
    )
    return jax.shard_map(
        on_device, mesh=mesh, in_specs=in_specs, out_specs=out_specs, check_vma=False
    )
```

```python
import functools

import jax
import jax.numpy as jnp
from jax import lax
from jax.experimental import pallas as pl
from jax.experimental.pallas import tpu as pltpu
from jax.sharding import PartitionSpec as P

D = 1536
HEADS = 12
KV_HEADS = 2
HEAD_DIM = 128
TOP = 4
TOK_DEV = 512
BRANCHES = 4
LEAVES = 8
TRUNK = 256
BRANCH = 64

EPSILON = 1e-06
ROPE_BASE = 10000.0
MASKED = -1e30
LOW = jnp.bfloat16
WIDE = jnp.float32
KEY_WIDTH = KV_HEADS * HEAD_DIM
GROUP = HEADS // KV_HEADS
QUARTERS = 4
VMEM_LIMIT = 56 * 1024 * 1024

ANY = pl.BlockSpec(memory_space=pl.ANY)
SMEM = pl.BlockSpec(memory_space=pltpu.SMEM)


def nn(one, two):
    return lax.dot_general(one, two, (((1,), (0,)), ((), ())), preferred_element_type=WIDE)


def nt(one, two):
    return lax.dot_general(one, two, (((1,), (1,)), ((), ())), preferred_element_type=WIDE)


def tn(one, two):
    return lax.dot_general(one, two, (((0,), (0,)), ((), ())), preferred_element_type=WIDE)


def whole(shape):
    return pl.BlockSpec(shape, lambda *_: (0,) * len(shape))


def params():
    return pltpu.CompilerParams(vmem_limit_bytes=VMEM_LIMIT)


def turn(values, cosine, sine):
    return values * cosine + pltpu.roll(values, HEAD_DIM // 2, 1) * sine


def turn_back(values, cosine, sine):
    return values * cosine - pltpu.roll(values, HEAD_DIM // 2, 1) * sine


PIECES = tuple(
    (flip_bits + core, slots)
    for wave in ((0, 2), (1, 3))
    for core in (0, 1)
    for flip_bits, slots in ((0, wave), (2, wave), (4, wave), (6, wave[:1]), (6, wave[1:]))
)
EXTRA = 16


def weight_copies(info, refs, target, sem, start, width):
    if len(refs) == 1:
        return [pltpu.make_async_copy(refs[0], target, sem)]
    depth = refs[0].shape[1] - EXTRA
    copies = []
    for ref, (flip_bits, slots) in zip(refs, PIECES):
        row = pl.multiple_of((info[0] ^ flip_bits) * depth, depth)
        for at, slot in enumerate(slots):
            col = pl.multiple_of(info[2 + slot] * width, 128)
            copies.append(
                pltpu.make_async_copy(
                    ref.at[at, pl.ds(0, depth), pl.ds(start, width)],
                    target.at[pl.ds(row, depth), pl.ds(col, width)],
                    sem,
                )
            )
    return copies


def extras_kernel(info, *rest):
    refs, (out, sem) = rest[:-2], rest[-2:]
    depth = refs[0].shape[1] - EXTRA
    copies = []
    for ref, (flip_bits, slots) in zip(refs, PIECES):
        for at, slot in enumerate(slots):
            to = (info[0] ^ flip_bits) * QUARTERS + info[2 + slot]
            copies.append(pltpu.make_async_copy(ref.at[at, pl.ds(depth, EXTRA)], out.at[to], sem))
    run_all(copies)
    wait_all(copies)


def extras(info, refs):
    return pl.pallas_call(
        extras_kernel,
        out_shape=jax.ShapeDtypeStruct((8 * QUARTERS, EXTRA, refs[0].shape[2]), LOW),
        in_specs=[SMEM] + [ANY] * len(refs),
        out_specs=pl.BlockSpec(memory_space=pltpu.VMEM),
        scratch_shapes=[pltpu.SemaphoreType.DMA],
        compiler_params=params(),
        name="extra_rows",
    )(info, *refs)


def run_all(copies):
    for copy in copies:
        copy.start()


def wait_all(copies):
    for copy in copies:
        copy.wait()


def key_value_kernel(info, tokens, gain, cosine, sine, *rest):
    count = len(rest) - 4
    refs, (normed, out, weight, sem) = rest[:count], rest[count:]
    copies = weight_copies(info, refs, weight, sem, D // QUARTERS, 128)
    run_all(copies)
    values = tokens[...].astype(WIDE)
    factor = lax.rsqrt(jnp.mean(values * values, axis=-1, keepdims=True) + EPSILON)
    low = (values * factor * gain[...]).astype(LOW)
    normed[...] = low
    wait_all(copies)
    both = nn(low, weight[...])
    half = HEAD_DIM // 2
    first = lax.broadcasted_iota(jnp.int32, (TOK_DEV, HEAD_DIM), 1) < half
    for g in range(KV_HEADS):
        one = both[:, 256 * g : 256 * g + 128]
        two = both[:, 256 * g + 128 : 256 * g + 256]
        key = jnp.where(first, one, pltpu.roll(two, half, 1))
        value = jnp.where(first, pltpu.roll(one, half, 1), two)
        out[:, 128 * g : 128 * g + 128] = turn(key, cosine[...], sine[...]).astype(LOW)
        out[:, KEY_WIDTH + 128 * g : KEY_WIDTH + 128 * g + 128] = value.astype(LOW)


def key_value(info, tokens, gain, cosine, sine, refs):
    return pl.pallas_call(
        key_value_kernel,
        out_shape=(
            jax.ShapeDtypeStruct((TOK_DEV, D), LOW),
            jax.ShapeDtypeStruct((TOK_DEV, 2 * KEY_WIDTH), LOW),
        ),
        in_specs=[SMEM] + [pl.BlockSpec(memory_space=pltpu.VMEM)] * 4 + [ANY] * len(refs),
        out_specs=(pl.BlockSpec(memory_space=pltpu.VMEM),) * 2,
        scratch_shapes=[pltpu.VMEM((D, 2 * KEY_WIDTH), LOW), pltpu.SemaphoreType.DMA],
        compiler_params=params(),
        name="norm_key_value",
    )(info, tokens, gain, cosine, sine, *refs)


def query_kernel(info, normed, cosine, sine, *rest):
    count = len(rest) - 3
    refs, (out, weight, sem) = rest[:count], rest[count:]

    @pl.when(pl.program_id(0) == 0)
    def _():
        copies = weight_copies(info, refs, weight, sem, 0, D // QUARTERS)
        run_all(copies)
        wait_all(copies)

    at = pl.multiple_of(pl.program_id(0) * 256, 256)
    lin = nn(normed[...], weight[:, pl.ds(at, 256)])
    for h in range(2):
        out[:, 128 * h : 128 * h + 128] = turn(
            lin[:, 128 * h : 128 * h + 128], cosine[...], sine[...]
        ).astype(LOW)


def query(info, normed, cosine, sine, refs):
    return pl.pallas_call(
        query_kernel,
        grid=(D // 256,),
        out_shape=jax.ShapeDtypeStruct((TOK_DEV, D), LOW),
        in_specs=[SMEM, whole((TOK_DEV, D)), whole((TOK_DEV, 128)), whole((TOK_DEV, 128))]
        + [ANY] * len(refs),
        out_specs=pl.BlockSpec((TOK_DEV, 256), lambda i: (0, i)),
        scratch_shapes=[pltpu.VMEM((D, D), LOW), pltpu.SemaphoreType.DMA],
        compiler_params=params(),
        name="query_projection",
    )(info, normed, cosine, sine, *refs)


KEYS = TRUNK + 2 * BRANCH
CHUNKS = TOK_DEV // BRANCH


def chunk_keys(info, source, own, column, chunk):
    at = pl.multiple_of(info[6 + chunk], BRANCH)
    rows = pl.multiple_of(chunk * BRANCH, BRANCH)
    columns = slice(column, column + HEAD_DIM)
    return jnp.concatenate(
        [
            source[0:TRUNK, columns],
            source[pl.ds(at, BRANCH), columns],
            own[pl.ds(rows, BRANCH), columns],
        ],
        axis=0,
    )


def chunk_allowed(info, chunk, query_axis, shape):
    query_row = lax.broadcasted_iota(jnp.int32, shape, query_axis) & (BRANCH - 1)
    key = lax.broadcasted_iota(jnp.int32, shape, 1 - query_axis)
    leaves = info[1] == 0
    trunk = jnp.logical_and(jnp.logical_not(leaves), chunk < TRUNK // BRANCH)
    limit = jnp.where(trunk, chunk * BRANCH + query_row, TRUNK - 1)
    branch_limit = jnp.where(leaves, TRUNK + BRANCH - 1, 0)
    own_limit = jnp.where(trunk, 0, query_row + TRUNK + BRANCH)
    top = jnp.where(key < TRUNK, limit, jnp.where(key < TRUNK + BRANCH, branch_limit, own_limit))
    return key <= top


def group_rows(ref, g):
    first = g * GROUP
    return jnp.concatenate(
        [ref[:, 128 * h : 128 * h + 128] for h in range(first, first + GROUP)], axis=0
    )


def keep_source(info, partner, own, source):
    @pl.when(pl.program_id(0) == 0)
    def _():
        @pl.when(info[1] == 0)
        def _():
            source[...] = partner[...]

        @pl.when(info[1] != 0)
        def _():
            source[...] = own[...]


def attention_kernel(info, queries, own, partner, out, source):
    keep_source(info, partner, own, source)
    chunk = pl.program_id(0)
    rows = GROUP * BRANCH
    allowed = chunk_allowed(info, chunk, 0, (rows, KEYS))
    for g in range(KV_HEADS):
        keys = chunk_keys(info, source, own, 128 * g, chunk)
        values = chunk_keys(info, source, own, KEY_WIDTH + 128 * g, chunk)
        scores = nt(group_rows(queries, g), keys) * HEAD_DIM**-0.5
        scores = jnp.where(allowed, scores, MASKED)
        weights = jnp.exp(scores - jnp.max(scores, axis=1, keepdims=True))
        total = jnp.sum(weights, axis=1, keepdims=True)
        mixed = nn((weights * (1.0 / total)).astype(LOW), values).astype(LOW)
        for h in range(GROUP):
            at = (g * GROUP + h) * 128
            out[:, at : at + 128] = mixed[h * BRANCH : (h + 1) * BRANCH]


def attention(info, queries, own, partner):
    return pl.pallas_call(
        attention_kernel,
        grid=(CHUNKS,),
        out_shape=jax.ShapeDtypeStruct((TOK_DEV, D), LOW),
        in_specs=[
            SMEM,
            pl.BlockSpec((BRANCH, D), lambda i: (i, 0)),
            whole((TOK_DEV, 2 * KEY_WIDTH)),
            whole((TOK_DEV, 2 * KEY_WIDTH)),
        ],
        out_specs=pl.BlockSpec((BRANCH, D), lambda i: (i, 0)),
        scratch_shapes=[pltpu.VMEM((TOK_DEV, 2 * KEY_WIDTH), LOW)],
        compiler_params=params(),
        name="tree_attention",
    )(info, queries, own, partner)


def attention_back_kernel(
    info, queries, own, partner, grads, cosine, sine, grad_query, own_grad, source_grad, source
):
    keep_source(info, partner, own, source)
    chunk = pl.program_id(0)

    @pl.when(chunk == 0)
    def _():
        source_grad[...] = jnp.zeros_like(source_grad)

    rows = GROUP * BRANCH
    scale = HEAD_DIM**-0.5
    allowed = chunk_allowed(info, chunk, 1, (KEYS, rows))
    at = pl.multiple_of(info[6 + chunk], BRANCH)
    for g in range(KV_HEADS):
        keys = chunk_keys(info, source, own, 128 * g, chunk)
        values = chunk_keys(info, source, own, KEY_WIDTH + 128 * g, chunk)
        query_rows = group_rows(queries, g)
        grad_rows = group_rows(grads, g)
        scores = jnp.where(allowed, nt(keys, query_rows) * scale, MASKED)
        weights = jnp.exp(scores - jnp.max(scores, axis=0, keepdims=True))
        probs = weights * (1.0 / jnp.sum(weights, axis=0, keepdims=True))
        grad_probs = nt(values, grad_rows)
        mean = jnp.sum(probs * grad_probs, axis=0, keepdims=True)
        grad_scores = (probs * (grad_probs - mean)).astype(LOW)
        grad_values = nn(probs.astype(LOW), grad_rows)
        grad_keys = nn(grad_scores, query_rows) * scale
        grad_queries = tn(grad_scores, keys) * scale
        for h in range(GROUP):
            to = (g * GROUP + h) * 128
            grad_query[:, to : to + 128] = turn_back(
                grad_queries[h * BRANCH : (h + 1) * BRANCH], cosine[...], sine[...]
            ).astype(LOW)
        for column, grad in ((128 * g, grad_keys), (KEY_WIDTH + 128 * g, grad_values)):
            columns = slice(column, column + 128)
            source_grad[0:TRUNK, columns] += grad[0:TRUNK]
            source_grad[pl.ds(at, BRANCH), columns] += grad[TRUNK : TRUNK + BRANCH]
            own_grad[:, columns] = grad[TRUNK + BRANCH :]


def attention_back(info, queries, own, partner, grads, cosine, sine):
    chunked = pl.BlockSpec((BRANCH, D), lambda i: (i, 0))
    pair = (TOK_DEV, 2 * KEY_WIDTH)
    return pl.pallas_call(
        attention_back_kernel,
        grid=(CHUNKS,),
        out_shape=(
            jax.ShapeDtypeStruct((TOK_DEV, D), LOW),
            jax.ShapeDtypeStruct(pair, WIDE),
            jax.ShapeDtypeStruct(pair, WIDE),
        ),
        in_specs=[
            SMEM,
            chunked,
            whole(pair),
            whole(pair),
            chunked,
            pl.BlockSpec((BRANCH, 128), lambda i: (i, 0)),
            pl.BlockSpec((BRANCH, 128), lambda i: (i, 0)),
        ],
        out_specs=(
            chunked,
            pl.BlockSpec((BRANCH, 2 * KEY_WIDTH), lambda i: (i, 0)),
            whole(pair),
        ),
        scratch_shapes=[pltpu.VMEM(pair, LOW)],
        compiler_params=params(),
        name="tree_attention_back",
    )(info, queries, own, partner, grads, cosine, sine)


def out_kernel(info, heads, tokens, gain, *rest):
    count = len(rest) - 4
    refs, (residual, normed, weight, sem) = rest[:count], rest[count:]

    @pl.when(pl.program_id(0) == 0)
    def _():
        copies = weight_copies(info, refs, weight, sem, D // QUARTERS + 128, D // QUARTERS)
        run_all(copies)
        wait_all(copies)

    at = pl.ds(pl.multiple_of(pl.program_id(0) * 256, 256), 256)
    residual[:, at] = tokens[:, at].astype(WIDE) + nn(heads[...], weight[:, at])

    @pl.when(pl.program_id(0) == pl.num_programs(0) - 1)
    def _():
        values = residual[...]
        factor = lax.rsqrt(jnp.mean(values * values, axis=-1, keepdims=True) + EPSILON)
        normed[...] = (values * factor * gain[...]).astype(LOW)


def out_projection(info, heads, tokens, gain, refs):
    full = (TOK_DEV, D)
    return pl.pallas_call(
        out_kernel,
        grid=(D // 256,),
        out_shape=(jax.ShapeDtypeStruct(full, WIDE), jax.ShapeDtypeStruct(full, LOW)),
        in_specs=[SMEM, whole(full), whole(full), whole((1, D))] + [ANY] * len(refs),
        out_specs=(whole(full), whole(full)),
        scratch_shapes=[pltpu.VMEM((D, D), LOW), pltpu.SemaphoreType.DMA],
        compiler_params=params(),
        name="out_projection",
    )(info, heads, tokens, gain, *refs)


def hits_of(routes, ids):
    hit = ids == routes[0, 0:1]
    for k in range(1, TOP):
        hit = jnp.logical_or(hit, ids == routes[0, k : k + 1])
    return hit


def tables_kernel(capacity, local, total, order, info, routes, chosen_out, place_out, earlier):
    @pl.when(pl.program_id(0) == 0)
    def _():
        one = lax.broadcasted_iota(jnp.int32, (TOK_DEV, TOK_DEV), 0)
        two = lax.broadcasted_iota(jnp.int32, (TOK_DEV, TOK_DEV), 1)
        earlier[...] = jnp.where(one < two, 1.0, 0.0).astype(LOW)

    ids = lax.broadcasted_iota(jnp.int32, (total, TOK_DEV), 0)
    hit = hits_of(routes, ids)
    rank = nn(jnp.where(hit, 1.0, 0.0).astype(LOW), earlier[...])
    place = jnp.where(hit, rank, -1.0)
    spots = lax.broadcasted_iota(jnp.int32, (capacity, TOK_DEV), 0).astype(WIDE)
    place_out[0] = jnp.full(place_out.shape[1:], -1.0, WIDE)
    for e in range(local):
        mine = ids == info[0] * local + e
        place_row = jnp.sum(jnp.where(mine, place, 0.0), axis=0, keepdims=True)
        place_out[0, e : e + 1] = place_row
        chosen_out[0, e * capacity : (e + 1) * capacity] = jnp.where(
            spots == place_row, 1.0, 0.0
        ).astype(LOW)


def tables(order, info, routes, capacity, local, total):
    count = routes.shape[0]
    return pl.pallas_call(
        functools.partial(tables_kernel, capacity, local, total),
        grid_spec=pltpu.PrefetchScalarGridSpec(
            num_scalar_prefetch=2,
            grid=(count,),
            in_specs=[pl.BlockSpec((1, TOP, TOK_DEV), lambda i, order, info: (order[i], 0, 0))],
            out_specs=[
                pl.BlockSpec((1, local * capacity, TOK_DEV), lambda i, order, info: (i, 0, 0)),
                pl.BlockSpec((1, 8, TOK_DEV), lambda i, order, info: (i, 0, 0)),
            ],
            scratch_shapes=[pltpu.VMEM((TOK_DEV, TOK_DEV), LOW)],
        ),
        out_shape=[
            jax.ShapeDtypeStruct((count, local * capacity, TOK_DEV), LOW),
            jax.ShapeDtypeStruct((count, 8, TOK_DEV), WIDE),
        ],
        compiler_params=params(),
        name="route_tables",
    )(order, info, routes)


def pick_kernel(local, order, chosen, blocks, *outs):
    rows_of = nn(chosen[0], blocks[0]).astype(LOW)
    capacity = outs[0].shape[1]
    for e in range(local):
        outs[e][0] = rows_of[e * capacity : (e + 1) * capacity]


def pick_rows(order, chosen, blocks, local):
    count, height, _ = chosen.shape
    capacity = height // local
    return pl.pallas_call(
        functools.partial(pick_kernel, local),
        grid_spec=pltpu.PrefetchScalarGridSpec(
            num_scalar_prefetch=1,
            grid=(count,),
            in_specs=[
                pl.BlockSpec((1, height, TOK_DEV), lambda i, order: (i, 0, 0)),
                pl.BlockSpec((1, TOK_DEV, D), lambda i, order: (order[i], 0, 0)),
            ],
            out_specs=[pl.BlockSpec((1, capacity, D), lambda i, order: (i, 0, 0))] * local,
        ),
        out_shape=[jax.ShapeDtypeStruct((count, capacity, D), LOW)] * local,
        compiler_params=params(),
        name="pick_rows",
    )(order, chosen, blocks)


def dispatch_kernel(local, order, info, rows, chosen, routes, router, *rest):
    outs, logits = rest[2 * local : 4 * local], rest[-1]
    total = router.shape[1]
    step = pl.program_id(0)
    block = rows[...]
    rows_of = nn(chosen[0], block).astype(LOW)
    capacity = outs[0].shape[1]
    for e in range(local):
        outs[e][0] = rows_of[e * capacity : (e + 1) * capacity]
    part = nn(block, router[...])

    @pl.when(step == 0)
    def _():
        logits[...] = part

    @pl.when(step > 0)
    def _():
        logits[...] += part

    @pl.when(step == pl.num_programs(0) - 1)
    def _():
        values = logits[...].T
        ids = lax.broadcasted_iota(jnp.int32, (total, TOK_DEV), 0)
        weights = jnp.exp(values - jnp.max(values, axis=0, keepdims=True))
        hit = hits_of(routes, ids)
        share = weights / jnp.sum(jnp.where(hit, weights, 0.0), axis=0, keepdims=True)
        for e in range(local):
            mine = ids == info[0] * local + e
            share_row = jnp.sum(jnp.where(mine, share, 0.0), axis=0, keepdims=True)
            picked = chosen[0, e * capacity : (e + 1) * capacity].astype(WIDE)
            outs[local + e][0] = jnp.sum(picked * share_row, axis=1, keepdims=True)


def dispatch(order, info, rows, chosen, routes, router, local, earlier):
    count, height, _ = chosen.shape
    capacity = height // local
    total = router.shape[1]
    wide = 512
    out_shape = [jax.ShapeDtypeStruct((count, capacity, D), LOW)] * local + [
        jax.ShapeDtypeStruct((count, capacity, 1), WIDE)
    ] * local
    if earlier is None:
        earlier = [jnp.zeros((8, 128), shape.dtype) for shape in out_shape]
        aliases = {}
    else:
        aliases = {6 + i: i for i in range(len(out_shape))}
    return pl.pallas_call(
        functools.partial(dispatch_kernel, local),
        grid_spec=pltpu.PrefetchScalarGridSpec(
            num_scalar_prefetch=2,
            grid=(D // wide,),
            in_specs=[
                pl.BlockSpec((TOK_DEV, wide), lambda i, order, info: (0, i)),
                pl.BlockSpec((1, height, TOK_DEV), lambda i, order, info: (order[0], 0, 0)),
                pl.BlockSpec((1, TOP, TOK_DEV), lambda i, order, info: (order[1], 0, 0)),
                pl.BlockSpec((wide, total), lambda i, order, info: (i, 0)),
            ]
            + [ANY] * len(out_shape),
            out_specs=[
                pl.BlockSpec((1, capacity, wide), lambda i, order, info: (order[0], 0, i))
            ]
            * local
            + [pl.BlockSpec((1, capacity, 1), lambda i, order, info: (order[0], 0, 0))] * local,
            scratch_shapes=[pltpu.VMEM((TOK_DEV, total), WIDE)],
        ),
        out_shape=out_shape,
        input_output_aliases=aliases,
        compiler_params=params(),
        name="dispatch",
    )(order, info, rows, chosen, routes, router, *earlier)


def spread_kernel(local, place, *rest):
    dots, out = rest[:local], rest[local]
    spots = lax.broadcasted_iota(jnp.int32, (dots[0].shape[1], TOK_DEV), 0).astype(WIDE)
    for e in range(local):
        chosen = spots == place[0, e : e + 1]
        out[0, e : e + 1] = jnp.sum(jnp.where(chosen, dots[e][0], 0.0), axis=0, keepdims=True)


def spread(place, dots):
    count, capacity, _ = dots[0].shape
    local = len(dots)
    return pl.pallas_call(
        functools.partial(spread_kernel, local),
        grid=(count,),
        out_shape=jax.ShapeDtypeStruct((count, local, TOK_DEV), WIDE),
        in_specs=[pl.BlockSpec((1, 8, TOK_DEV), lambda i: (i, 0, 0))]
        + [pl.BlockSpec((1, capacity, 1), lambda i: (i, 0, 0))] * local,
        out_specs=pl.BlockSpec((1, local, TOK_DEV), lambda i: (i, 0, 0)),
        compiler_params=params(),
        name="spread",
    )(place, *dots)


def expert_kernel(slots, info, rows, grads, shares, *rest):
    count = len(rest) - 7
    refs = rest[:count]
    out_rows, back_rows, grad_rows, acts, dots, weight, sem = rest[count:]
    part = weight.shape[1] // slots

    @pl.when(pl.program_id(0) == 0)
    def _():
        def copies(ref, slot):
            return [
                pltpu.make_async_copy(
                    ref.at[pl.ds(which * part, part)],
                    weight.at[which, pl.ds(slot * part, part)],
                    sem,
                )
                for which in range(3)
            ]

        if count == slots:
            for slot in range(slots):
                run_all(copies(refs[slot], slot))
        else:
            block, second, above, below, far = refs
            low_end = info[2] == 0
            end = jnp.logical_or(low_end, info[2] == 3)
            run_all(copies(block, 0))
            run_all(copies(second, 1))

            @pl.when(low_end)
            def _():
                run_all(copies(above, 2))

            @pl.when(jnp.logical_not(low_end))
            def _():
                run_all(copies(below, 2))

            @pl.when(end)
            def _():
                run_all(copies(far, 3))

            @pl.when(jnp.logical_not(end))
            def _():
                run_all(copies(above, 3))

        for slot in range(slots):
            wait_all(copies(refs[0], slot))

    row_block = rows[...]
    share = shares[...]
    grad_float = grads[...].astype(WIDE)
    grad_low = (share * grad_float).astype(LOW)
    grad_rows[...] = grad_low
    gate_act = nt(row_block, weight[0])
    upward = nt(row_block, weight[1])
    sigmoid = 1.0 / (1.0 + jnp.exp(-gate_act))
    silu = gate_act * sigmoid
    hidden = (silu * upward).astype(LOW)
    expert_out = nn(hidden, weight[2]).astype(LOW).astype(WIDE)
    out_rows[...] = (share * expert_out).astype(LOW)
    dots[...] = jnp.sum(grad_float * expert_out, axis=1, keepdims=True)
    grad_hidden = nt(grad_low, weight[2])
    grad_gate = (grad_hidden * upward * sigmoid * (1.0 + gate_act * (1.0 - sigmoid))).astype(LOW)
    grad_up = (grad_hidden * silu).astype(LOW)
    back_rows[...] = (nn(grad_gate, weight[0]) + nn(grad_up, weight[1])).astype(LOW)
    for which, act in enumerate((grad_gate, grad_up, hidden)):
        turned = act.T
        for slot in range(slots):
            acts[slot, which * part : (which + 1) * part] = turned[
                slot * part : (slot + 1) * part
            ]


EXPERT_ROWS = 256


def expert(info, rows, grads, shares, refs, slots):
    height = rows.shape[0]
    part = refs[0].shape[0] // 3
    wide_block = pl.BlockSpec((EXPERT_ROWS, D), lambda i: (i, 0))
    thin_block = pl.BlockSpec((EXPERT_ROWS, 1), lambda i: (i, 0))
    return pl.pallas_call(
        functools.partial(expert_kernel, slots),
        grid=(height // EXPERT_ROWS,),
        out_shape=[jax.ShapeDtypeStruct((height, D), LOW)] * 3
        + [
            jax.ShapeDtypeStruct((slots, 3 * part, height), LOW),
            jax.ShapeDtypeStruct((height, 1), WIDE),
        ],
        in_specs=[SMEM, wide_block, wide_block, thin_block] + [ANY] * len(refs),
        out_specs=[wide_block] * 3
        + [pl.BlockSpec((slots, 3 * part, EXPERT_ROWS), lambda i: (0, 0, i)), thin_block],
        scratch_shapes=[pltpu.VMEM((3, slots * part, D), LOW), pltpu.SemaphoreType.DMA],
        compiler_params=params(),
        name="expert",
    )(info, rows, grads, shares, *refs)


def expert_grads_kernel(slots, rows, grads, *rest):
    acts, outs = rest[: len(slots)], rest[len(slots) :]
    part = acts[0].shape[1] // 3
    for act, out in zip(acts, outs):
        out[: 2 * part, :] = nn(act[0, : 2 * part], rows[...]).astype(LOW)
        out[2 * part :, :] = nn(act[0, 2 * part :], grads[...]).astype(LOW)


def expert_grads(acts, rows, grads, slots):
    _, part, height = acts.shape
    return pl.pallas_call(
        functools.partial(expert_grads_kernel, slots),
        grid=(D // 256,),
        out_shape=[jax.ShapeDtypeStruct((part, D), LOW) for _ in slots],
        in_specs=[pl.BlockSpec((height, 256), lambda i: (0, i))] * 2
        + [pl.BlockSpec((1, part, height), lambda i, s=slot: (s, 0, 0)) for slot in slots],
        out_specs=[pl.BlockSpec((part, 256), lambda i: (0, i)) for _ in slots],
        compiler_params=params(),
        name="expert_gradients",
    )(rows, grads, *[acts] * len(slots))


def combine_kernel(local, chosen, *rest):
    rows, out = rest[:local], rest[local]
    both = jnp.concatenate([ref[0] for ref in rows], axis=0)
    out[0] = tn(chosen[0], both).astype(LOW)


def combine(chosen, rows, first, step):
    count, capacity, _ = rows[0].shape
    number = (count - first + step - 1) // step
    return pl.pallas_call(
        functools.partial(combine_kernel, len(rows)),
        grid=(number,),
        out_shape=jax.ShapeDtypeStruct((number, TOK_DEV, D), LOW),
        in_specs=[
            pl.BlockSpec((1,) + chosen.shape[1:], lambda i: (first + step * i, 0, 0))
        ]
        + [pl.BlockSpec((1, capacity, D), lambda i: (first + step * i, 0, 0))] * len(rows),
        out_specs=pl.BlockSpec((1, TOK_DEV, D), lambda i: (i, 0, 0)),
        compiler_params=params(),
        name="combine",
    )(chosen, *rows)


def split(values):
    high = values.astype(LOW)
    return high, (values - high.astype(WIDE)).astype(LOW)


def norm_back(values, gain, grad):
    factor = lax.rsqrt(jnp.mean(values * values, axis=-1, keepdims=True) + EPSILON)
    scaled = gain * grad
    mean = jnp.mean(values * scaled, axis=-1, keepdims=True)
    grad_values = factor * scaled - values * (factor * factor * factor * mean)
    grad_gain = jnp.sum(grad * values * factor, axis=0, keepdims=True)
    return grad_values, grad_gain


def router_back(logits, routes, grad_shares):
    ids = lax.broadcasted_iota(jnp.int32, logits.shape, 0)
    hit = ids == routes[0:1]
    for k in range(1, TOP):
        hit = jnp.logical_or(hit, ids == routes[k : k + 1])
    weights = jnp.exp(logits - jnp.max(logits, axis=0, keepdims=True))
    probs = weights / jnp.sum(weights, axis=0, keepdims=True)
    chosen = jnp.sum(jnp.where(hit, probs, 0.0), axis=0, keepdims=True)
    grads = jnp.where(hit, grad_shares, 0.0)
    mean = jnp.sum(probs * grads, axis=0, keepdims=True) / chosen
    grad_probs = jnp.where(hit, (grads - mean) / chosen, 0.0)
    return probs * (grad_probs - jnp.sum(probs * grad_probs, axis=0, keepdims=True))


def branch_back_kernel(
    parts, info, residual, normed, cotangent, routes, grad_shares, router, gain, *rest
):
    sums, rest = rest[:parts], rest[parts:]
    count = len(rest) - 7
    refs = rest[:count]
    grad_residual, grad_branch, grad_heads, grad_gain, grad_router, weight, sem = rest[count:]

    @pl.when(pl.program_id(0) == 0)
    def _():
        copies = weight_copies(info, refs, weight, sem, D // QUARTERS + 128, D // QUARTERS)
        run_all(copies)
        logits = nt(router[...], normed[...])
        high, low = split(router_back(logits, routes[...], grad_shares[...]))
        grad_router[...] = nn(high, normed[...]) + nn(low, normed[...])
        grad_normed = tn(high, router[...]) + tn(low, router[...])
        if parts == 1:
            grad_normed += sums[0][...]
        else:
            values = [ref[...].astype(WIDE) for ref in sums]
            grad_normed += jnp.concatenate(
                [values[0] + values[1] + values[2], values[3] + values[4] + values[5]], axis=0
            )
        grad_values, gain_grad = norm_back(residual[...], gain[...], grad_normed)
        grad_gain[...] = gain_grad
        total = cotangent[...].astype(WIDE) + grad_values
        grad_residual[...] = total
        grad_branch[...] = total.astype(LOW)
        wait_all(copies)

    at = pl.ds(pl.multiple_of(pl.program_id(0) * 256, 256), 256)
    grad_heads[...] = nt(grad_branch[...], weight[at, :]).astype(LOW)


def branch_back(info, residual, normed, sums, cotangent, routes, grad_shares, router, gain, refs):
    full = (TOK_DEV, D)
    total = router.shape[0]
    return pl.pallas_call(
        functools.partial(branch_back_kernel, len(sums)),
        grid=(D // 256,),
        out_shape=(
            jax.ShapeDtypeStruct(full, WIDE),
            jax.ShapeDtypeStruct(full, LOW),
            jax.ShapeDtypeStruct(full, LOW),
            jax.ShapeDtypeStruct((1, D), WIDE),
            jax.ShapeDtypeStruct((total, D), WIDE),
        ),
        in_specs=[SMEM]
        + [whole(full)] * 3
        + [whole((TOP, TOK_DEV)), whole((total, TOK_DEV)), whole((total, D)), whole((1, D))]
        + [whole(part.shape) for part in sums]
        + [ANY] * len(refs),
        out_specs=(
            whole(full),
            whole(full),
            pl.BlockSpec((TOK_DEV, 256), lambda i: (0, i)),
            whole((1, D)),
            whole((total, D)),
        ),
        scratch_shapes=[pltpu.VMEM((D, D), LOW), pltpu.SemaphoreType.DMA],
        compiler_params=params(),
        name="experts_norm_back",
    )(info, residual, normed, cotangent, routes, grad_shares, router, gain, *sums, *refs)


def join_grads_kernel(info, own_grad, source_grad, arrived, cosine, sine, out):
    half = HEAD_DIM // 2
    first = lax.broadcasted_iota(jnp.int32, (TOK_DEV, HEAD_DIM), 1) < half
    leaves = info[1] == 0

    def total(column):
        columns = slice(column, column + 128)
        extra = source_grad[:, columns] + arrived[:, columns].astype(WIDE)
        return own_grad[:, columns] + jnp.where(leaves, 0.0, extra)

    for g in range(KV_HEADS):
        key = turn_back(total(128 * g), cosine[...], sine[...])
        value = total(KEY_WIDTH + 128 * g)
        out[:, 256 * g : 256 * g + 128] = jnp.where(
            first, key, pltpu.roll(value, half, 1)
        ).astype(LOW)
        out[:, 256 * g + 128 : 256 * g + 256] = jnp.where(
            first, pltpu.roll(key, half, 1), value
        ).astype(LOW)


def join_grads(info, own_grad, source_grad, arrived, cosine, sine):
    vmem = pl.BlockSpec(memory_space=pltpu.VMEM)
    return pl.pallas_call(
        join_grads_kernel,
        out_shape=jax.ShapeDtypeStruct((TOK_DEV, 2 * KEY_WIDTH), LOW),
        in_specs=[SMEM] + [vmem] * 5,
        out_specs=vmem,
        compiler_params=params(),
        name="join_key_value_gradients",
    )(info, own_grad, source_grad, arrived, cosine, sine)


def token_back_kernel(info, grad_query, grad_pair, tokens, grad_residual, gain, *rest):
    count = (len(rest) - 6) // 2
    query_refs, pair_refs = rest[:count], rest[count : 2 * count]
    out, grad_gain, query_weight, pair_weight, grad_normed, sem = rest[2 * count :]

    @pl.when(pl.program_id(0) == 0)
    def _():
        copies = weight_copies(info, query_refs, query_weight, sem, 0, D // QUARTERS)
        copies += weight_copies(info, pair_refs, pair_weight, sem, D // QUARTERS, 128)
        run_all(copies)
        wait_all(copies)

    at = pl.ds(pl.multiple_of(pl.program_id(0) * 256, 256), 256)
    grad_normed[:, at] = nt(grad_query[...], query_weight[at, :]) + nt(
        grad_pair[...], pair_weight[at, :]
    )

    @pl.when(pl.program_id(0) == pl.num_programs(0) - 1)
    def _():
        grad_values, gain_grad = norm_back(
            tokens[...].astype(WIDE), gain[...], grad_normed[...]
        )
        grad_gain[...] = gain_grad
        out[...] = (grad_residual[...] + grad_values).astype(LOW)


def token_back(info, grad_query, grad_pair, tokens, grad_residual, gain, query_refs, pair_refs):
    full = (TOK_DEV, D)
    return pl.pallas_call(
        token_back_kernel,
        grid=(D // 256,),
        out_shape=(jax.ShapeDtypeStruct(full, LOW), jax.ShapeDtypeStruct((1, D), WIDE)),
        in_specs=[
            SMEM,
            whole(full),
            whole((TOK_DEV, 2 * KEY_WIDTH)),
            whole(full),
            whole(full),
            whole((1, D)),
        ]
        + [ANY] * (len(query_refs) + len(pair_refs)),
        out_specs=(whole(full), whole((1, D))),
        scratch_shapes=[
            pltpu.VMEM((D, D), LOW),
            pltpu.VMEM((D, 2 * KEY_WIDTH), LOW),
            pltpu.VMEM(full, WIDE),
            pltpu.SemaphoreType.DMA,
        ],
        compiler_params=params(),
        name="token_gradient",
    )(info, grad_query, grad_pair, tokens, grad_residual, gain, *query_refs, *pair_refs)


def weight_grads_kernel(parts, info, *rest):
    ins, (keep, send) = rest[:-2], rest[-2:]
    depth = D // 8
    core = info[0] & 1
    chip = pl.program_id(0) ^ (info[0] >> 1)
    start = 0
    for strip_at, grads_at, width in parts:
        low = tn(ins[strip_at][...], ins[grads_at][...]).astype(LOW)
        columns = slice(start, start + width)
        start += width
        for slot in range(QUARTERS):
            for j in range(QUARTERS):

                @pl.when(info[2 + slot] == j)
                def _():
                    piece = low[:, j * width : (j + 1) * width]
                    upper, lower = piece[:depth], piece[depth:]
                    keep[0, slot, :depth, columns] = jnp.where(core == 0, upper, lower)
                    send[0, slot, :depth, columns] = jnp.where(core == 0, lower, upper)

    if keep.shape[2] > depth:
        extra = ins[-1]
        for slot in range(QUARTERS):
            to = info[2 + slot]
            keep[0, slot, depth:] = extra[(chip * 2 + core) * QUARTERS + to]
            send[0, slot, depth:] = extra[(chip * 2 + 1 - core) * QUARTERS + to]


def weight_grads(info, strips, grads, parts, extra):
    depth = D // 8
    width = sum(part[2] for part in parts)
    strip = pl.BlockSpec((TOK_DEV, 2 * depth), lambda i, info: (0, i ^ (info[0] >> 1)))
    more = [] if extra is None else [extra]
    shape = (4, QUARTERS, depth + EXTRA * len(more), width)
    out = pl.BlockSpec((1,) + shape[1:], lambda i, info: (i, 0, 0, 0))
    return pl.pallas_call(
        functools.partial(weight_grads_kernel, parts),
        grid_spec=pltpu.PrefetchScalarGridSpec(
            num_scalar_prefetch=1,
            grid=(4,),
            in_specs=[strip] * len(strips)
            + [
                pl.BlockSpec(a.shape, lambda i, info, n=a.ndim: (0,) * n)
                for a in (*grads, *more)
            ],
            out_specs=(out, out),
        ),
        out_shape=(jax.ShapeDtypeStruct(shape, LOW),) * 2,
        compiler_params=params(),
        name="weight_gradients",
    )(info, *strips, *grads, *more)


def position_of(token_index):
    branch_place = TRUNK + (token_index - TRUNK) % BRANCH
    leaf_place = TRUNK + BRANCH + (token_index - TOK_DEV) % BRANCH
    return jnp.where(
        token_index < TRUNK, token_index, jnp.where(token_index < TOK_DEV, branch_place, leaf_place)
    )


def rotary_tables(positions):
    half_dim = HEAD_DIM // 2
    frequency = ROPE_BASE ** (-jnp.arange(half_dim, dtype=jnp.float32) / half_dim)
    angles = positions.astype(jnp.float32)[:, None] * frequency[None, :]
    cosine, sine = (jnp.cos(angles), jnp.sin(angles))
    return (
        jnp.concatenate([cosine, cosine], axis=1),
        jnp.concatenate([-sine, sine], axis=1),
    )


def after(values, *earlier):
    return lax.optimization_barrier((values, earlier))[0]


def fast_mesh():
    return lax.axis_size("rows") == 8 and lax.axis_size("cols") == 4


SLOT_SHARD = ((0, 2, 1, 3), (1, 3, 0, 2), (2, 0, 1, 3), (3, 1, 2, 0))
UP = [(0, 1), (1, 2), (2, 3)]
DOWN = [(1, 0), (2, 1), (3, 2)]
FAR = [(0, 3), (3, 0)]


def send_first(block):
    return (
        lax.ppermute(block, "cols", DOWN),
        lax.ppermute(block, "cols", UP),
        lax.ppermute(block, "cols", FAR),
    )


def send_second(block, first):
    place = lax.axis_index("cols")
    above, below, _ = first
    payload = jnp.where(place == 1, above, jnp.where(place == 2, below, block))
    return lax.ppermute(payload, "cols", [(3, 1), (1, 0), (0, 2), (2, 3)])


def slot_list(block, first, second):
    place = lax.axis_index("cols")
    above, below, far = first
    end = (place == 0) | (place == 3)
    return [
        block,
        second,
        jnp.where(place == 0, above, below),
        jnp.where(end, far, above),
    ]


def reduce_first(second, fourth):
    return (
        lax.ppermute(second, "cols", [(1, 3), (0, 1), (2, 0), (3, 2)]),
        lax.ppermute(fourth, "cols", FAR),
    )


def reduce_second(third, fourth, relay):
    place = lax.axis_index("cols")
    relayed = relay.astype(WIDE)
    upward_load = (
        jnp.where(place == 0, third, fourth).astype(WIDE) + jnp.where(place == 1, relayed, 0.0)
    ).astype(LOW)
    downward_load = (third.astype(WIDE) + jnp.where(place == 2, relayed, 0.0)).astype(LOW)
    return (
        lax.ppermute(upward_load, "cols", UP),
        lax.ppermute(downward_load, "cols", DOWN),
    )


def reduce_last(own, first, second):
    place = lax.axis_index("cols")
    relay, far = first
    below, above = second
    end = (place == 0) | (place == 3)
    return (
        own.astype(WIDE)
        + below.astype(WIDE)
        + above.astype(WIDE)
        + jnp.where(end, relay.astype(WIDE) + far.astype(WIDE), 0.0)
    )


def flip(block, bit):
    count = lax.axis_size("rows")
    return lax.ppermute(block, "rows", [(i, i ^ bit) for i in range(count)])


def add_low(one, two):
    return (one.astype(WIDE) + two.astype(WIDE)).astype(LOW)


def reduce_chips(keep, got):
    half = keep.shape[1] // 2

    def sums(chips, part):
        return jnp.stack([add_low(keep[i][part], got[i][part]) for i in chips])

    one, two = slice(0, half), slice(half, None)
    got_x = flip(sums((1, 3), one), 2)
    got_y = flip(sums((2, 3), two), 4)
    near_x = sums((0, 2), one)
    near_y = sums((0, 1), two)
    got_xy = flip(add_low(near_x[1], got_x[1]), 4)
    got_yx = flip(add_low(near_y[1], got_y[1]), 2)
    return (near_x[0], got_x[0], got_xy, near_y[0], got_y[0], got_yx)


def sum_parts(parts):
    wide = [a.astype(WIDE) for a in parts]
    if len(wide) == 1:
        return wide[0]
    return jnp.concatenate([wide[0] + wide[1] + wide[2], wide[3] + wide[4] + wide[5]], axis=0)


def on_device(
    tokens,
    query_weight,
    key_weight,
    value_weight,
    out_weight,
    router_weight,
    attention_gain,
    experts_gain,
    gate_weight,
    upward_weight,
    down_weight,
    routes,
    leaf_parent,
    cotangent,
):
    row_count = lax.axis_size("rows")
    col_count = lax.axis_size("cols")
    row_place = lax.axis_index("rows")
    col_place = lax.axis_index("cols")
    fast = fast_mesh()
    parity = lax.rem(col_place, 2)
    tree_id = lax.div(row_place * col_count + col_place, 2)
    parent_row = lax.dynamic_slice_in_dim(leaf_parent, tree_id, 1, 0)[0]
    depth, query_part = query_weight.shape
    key_part = key_weight.shape[1]
    router_part = router_weight.shape[1]
    gain_part = attention_gain.shape[0]
    expert_total = router_part * col_count
    local_experts = gate_weight.shape[0]
    capacity = TOK_DEV * TOP // expert_total * 5 // 4

    shards = (
        jnp.asarray(SLOT_SHARD, jnp.int32)[col_place]
        if fast
        else jnp.arange(4, dtype=jnp.int32)
    )
    branch_rows = jnp.where(parity == 0, TRUNK + BRANCH * parent_row, TRUNK)
    info = jnp.concatenate(
        [jnp.stack([row_place, parity]), shards, branch_rows, jnp.zeros((2,), jnp.int32)]
    ).astype(jnp.int32)

    packed = jnp.concatenate([query_weight, key_weight, value_weight, out_weight], axis=1)
    local_index = (1 - parity) * TOK_DEV + jnp.arange(TOK_DEV, dtype=jnp.int32)
    cosine, sine = rotary_tables(position_of(local_index))
    routes_all = lax.all_gather(routes.T, "rows", axis=0)
    shard_blocks = [
        jnp.concatenate(
            [gate_weight[expert].T, upward_weight[expert].T, down_weight[expert]], axis=0
        )
        for expert in range(local_experts)
    ]
    firsts, seconds = ([], [])
    if fast:
        wide = packed.shape[1]
        gains = jnp.concatenate([attention_gain, experts_gain])[None, :]
        packed = jnp.concatenate(
            [
                packed,
                jnp.pad(router_weight.T, ((0, 0), (0, wide - depth))),
                jnp.pad(gains, ((0, 0), (0, wide - 2 * gain_part))),
                jnp.zeros((EXTRA - router_part - 1, wide), LOW),
            ],
            axis=0,
        )
        packed_first = send_first(packed)
        packed_second = send_second(packed, packed_first)
        slots = slot_list(packed, packed_first, packed_second)
        ahead = packed_second
        for expert_at in range(local_experts):
            block = after(shard_blocks[expert_at], ahead)
            shard_blocks[expert_at] = block
            first = send_first(block)
            firsts.append(first)
            seconds.append(send_second(block, first))
            ahead = first
        pieces, owns = ([], [])
        for wave in ((0, 2), (1, 3)):
            own = jnp.stack([slots[i] for i in wave])
            if wave[0] == 0:
                own = after(own, routes_all, info, cosine, sine)
            beside, across = flip(own, 2), flip(own, 4)
            same = [own, beside, across, flip(beside[:1], 4), flip(across[1:], 2)]
            pieces += same + [flip(piece, 1) for piece in same]
            owns.append(own)
        query_refs = pair_refs = out_refs = pieces
        expert_refs = [
            [shard_blocks[i], seconds[i], *firsts[i]] for i in range(local_experts)
        ]
        extra_rows = extras(info, pieces)
        router_all = extra_rows[:, :router_part, :depth]
        attention_scale = extra_rows[:, router_part, :gain_part]
        experts_scale = extra_rows[:, router_part, gain_part : 2 * gain_part]
    else:
        packed_all = lax.all_gather(lax.all_gather(packed, "cols", axis=0), "rows", axis=0)

        def unpack(start, width):
            part = packed_all[..., start : start + width]
            return jnp.swapaxes(part, 1, 2).reshape(row_count * depth, col_count * width)

        key_at = query_part
        query_refs = [unpack(0, query_part)]
        pair_refs = [
            jnp.concatenate(
                [
                    unpack(key_at, key_part).reshape(D, QUARTERS, -1),
                    unpack(key_at + key_part, key_part).reshape(D, QUARTERS, -1),
                ],
                axis=2,
            ).reshape(D, -1)
        ]
        out_refs = [unpack(key_at + 2 * key_part, query_part)]
        axes = ("rows", "cols")
        router_all = jnp.swapaxes(lax.all_gather(router_weight, axes, axis=0), 1, 2)
        attention_scale = lax.all_gather(attention_gain, axes, axis=0)
        experts_scale = lax.all_gather(experts_gain, axes, axis=0)
        expert_refs = [
            [lax.all_gather(block, "cols", axis=0)[i] for i in range(col_count)]
            for block in shard_blocks
        ]

    attention_scale = attention_scale.reshape(1, D).astype(WIDE)
    experts_scale = experts_scale.reshape(1, D).astype(WIDE)
    router_rows = jnp.transpose(
        router_all.reshape(row_count, col_count, router_part, depth), (1, 2, 0, 3)
    ).reshape(expert_total, D)
    router_cols = router_rows.T
    if fast:
        near_rows = row_place ^ jnp.arange(row_count, dtype=jnp.int32)
    else:
        near_rows = jnp.arange(row_count, dtype=jnp.int32)
    chosen, place_rows = tables(
        near_rows, info, routes_all, capacity, local_experts, expert_total
    )
    grad_in = after(cotangent, *pieces) if fast else cotangent
    grad_all = lax.all_gather(grad_in, "rows", axis=0)

    normed, own_pair = key_value(info, tokens, attention_scale, cosine, sine, pair_refs)
    pairs = [(i + 1, i) for i in range(0, col_count, 2)]
    partner = lax.ppermute(own_pair, "cols", pairs)
    queries = query(info, normed, cosine, sine, query_refs)
    if fast:
        queries = after(queries, *firsts[0])
    heads = attention(info, queries, own_pair, partner)
    residual, normed_two = out_projection(info, heads, tokens, experts_scale, out_refs)

    if fast:
        beside, across = flip(normed_two, 2), flip(normed_two, 4)
        beside_in = flip(normed_two, 1)
        grad_all = after(grad_all, normed_two)
    else:
        rows_all = lax.all_gather(normed_two, "rows", axis=0)
    grad_rows = pick_rows(near_rows, chosen, grad_all, local_experts)

    def place_block(q, block, picked):
        order = jnp.stack([jnp.int32(q), near_rows[q]])
        return dispatch(
            order, info, block, chosen, routes_all, router_cols, local_experts, picked
        )

    if fast:
        half = TOK_DEV // 2
        picked = place_block(0, normed_two, None)
        picked = place_block(1, beside_in, picked)
        beside, across = after((beside, across), picked, grad_rows)
        corner = [flip(beside[:half], 4), flip(across[half:], 2)]
        picked = place_block(2, beside, picked)
        picked = place_block(4, across, picked)
        picked = place_block(3, flip(beside, 1), picked)
        picked = place_block(5, flip(across, 1), picked)
        corner = jnp.concatenate(after(corner, picked), axis=0)
        corner_in = flip(corner, 1)
        picked = place_block(6, corner, picked)
        corner_in = after(corner_in, picked, *firsts[1])
        picked = place_block(7, corner_in, picked)
    else:
        picked = None
        for q in range(row_count):
            picked = place_block(q, rows_all[q], picked)
    height = row_count * capacity
    token_rows = [a.reshape(height, D) for a in picked[:local_experts]]
    grad_rows = [a.reshape(height, D) for a in grad_rows]
    share_rows = [a.reshape(height, 1) for a in picked[local_experts:]]

    out_rows, back_rows, gate_dots, reduced, marks = ([], [], [], [], [])
    for e in range(local_experts):
        rows_in = token_rows[e]
        if fast and e == 0:
            rows_in = after(rows_in, seconds[0])
        if fast and e == 1:
            rows_in = after(rows_in, seconds[1], own_slot, third)
        out_row, back_row, grad_row, acts, dots = expert(
            info, rows_in, grad_rows[e], share_rows[e], expert_refs[e], col_count
        )
        out_rows.append(out_row.reshape(row_count, capacity, D))
        back_rows.append(back_row.reshape(row_count, capacity, D))
        gate_dots.append(dots.reshape(row_count, capacity, 1))
        if fast:
            if e == 1:
                got = flip(combine(chosen, back_rows, 1, 2), 1)
                acts = after(acts, got, marks[0][0])
            second, fourth = expert_grads(acts, token_rows[e], grad_row, (1, 3))
            sent_first = reduce_first(second, fourth)
            marks.append(sent_first)
            own_slot, third = expert_grads(acts, token_rows[e], grad_row, (0, 2))
            sent_second = reduce_second(third, fourth, sent_first[0])
            reduced.append((own_slot, sent_first, sent_second))
        else:
            slots = expert_grads(acts, token_rows[e], grad_row, tuple(range(col_count)))
            reduced.append(
                lax.psum_scatter(jnp.stack(slots), "cols", scatter_dimension=0).astype(WIDE)
            )

    spread_dots = spread(place_rows, gate_dots)
    if fast:
        spread_dots = jnp.take(spread_dots, near_rows, axis=0)
    grad_shares = lax.all_to_all(spread_dots, "rows", split_axis=0, concat_axis=0, tiled=True)
    grad_shares = grad_shares.reshape(expert_total, TOK_DEV)
    if fast:
        back_parts = reduce_chips(combine(chosen, back_rows, 0, 2), got)
        grad_shares = after(grad_shares, own_slot, third, *reduced[0][1], *reduced[0][2])
    else:

        def summed(rows):
            part = combine(chosen, rows, 0, 1)
            return (lax.psum_scatter(part, "rows", scatter_dimension=0).astype(WIDE),)

        back_parts = summed(back_rows)
        mixture = summed(out_rows)

    grad_residual, grad_branch, grad_heads, experts_gain_grad, router_grad = branch_back(
        info,
        residual,
        normed_two,
        back_parts,
        cotangent,
        routes.T,
        grad_shares,
        router_rows,
        experts_scale,
        out_refs,
    )
    if fast:
        out_rows = [after(a, grad_heads) for a in out_rows]
        out_got = flip(combine(chosen, out_rows, 1, 2), 1)
        router_parts = jnp.transpose(
            router_grad.astype(LOW).reshape(col_count, router_part, row_count, depth),
            (2, 0, 1, 3),
        ).reshape(row_count * col_count, router_part, depth)
        gain_rows = experts_gain_grad.astype(LOW).reshape(row_count * col_count, 1, gain_part)
        extra = jnp.concatenate(
            [
                jnp.pad(router_parts, ((0, 0), (0, 0), (0, query_part - depth))),
                jnp.pad(gain_rows, ((0, 0), (0, 0), (0, query_part - gain_part))),
                jnp.zeros(
                    (row_count * col_count, EXTRA - router_part - 1, query_part), LOW
                ),
            ],
            axis=1,
        )
        out_keep, out_send = weight_grads(
            info, [heads], [grad_branch], ((0, 1, query_part),), extra
        )
        out_sent = flip(out_send, 1)
    grad_query, own_grad, source_grad = attention_back(
        info, queries, own_pair, partner, grad_heads, cosine, sine
    )
    arrived = lax.ppermute(source_grad.astype(LOW), "cols", [(j, i) for i, j in pairs])
    grad_pair = join_grads(info, own_grad, source_grad, arrived, cosine, sine)
    if fast:
        keep, send = weight_grads(
            info,
            [normed],
            [grad_query, grad_pair],
            ((0, 1, query_part), (0, 2, 2 * key_part)),
            None,
        )
        sent = flip(send, 1)
        grad_pair = after(grad_pair, keep)
    tokens_grad, attention_gain_grad = token_back(
        info, grad_query, grad_pair, tokens, grad_residual, attention_scale, query_refs, pair_refs
    )

    if fast:
        out_slots = sum_parts(reduce_chips(out_keep, out_sent)).astype(LOW)
        mixture = reduce_chips(combine(chosen, out_rows, 0, 2), out_got)
        slots = sum_parts(reduce_chips(keep, sent))
        own_slots = [owns[0][0], owns[1][0], owns[0][1], owns[1][1]]
        width = query_part + 2 * key_part
        gain_sums = sum(
            jnp.sum(own_slots[i][:depth, :width].astype(WIDE) * slots[i], axis=1)
            for i in range(4)
        )
        own_gains = lax.dynamic_slice_in_dim(attention_scale[0], row_place * depth, depth, 0)
        gain_sums = (gain_sums / own_gains).reshape(col_count, 1, gain_part)
        gain_sums = jnp.pad(
            jnp.take(gain_sums, shards, axis=0),
            ((0, 0), (0, EXTRA - 1), (0, width - gain_part)),
        )
        slots = jnp.concatenate([slots, gain_sums], axis=1).astype(LOW)

        def cols_sum(slots):
            sent_first = reduce_first(slots[1], slots[3])
            sent_second = reduce_second(slots[2], slots[3], sent_first[0])
            return reduce_last(slots[0], sent_first, sent_second)

        out_sums = cols_sum(out_slots)
        sums = cols_sum(slots)
        expert_sums = [reduce_last(*parts) for parts in reduced]
        router_sum = out_sums[depth : depth + router_part, :depth].T
        experts_gain_sum = out_sums[depth + router_part, :gain_part]
        attention_gain_sum = sums[depth, :gain_part]
        out_sum = out_sums[:depth]
        sums = sums[:depth]
    else:
        full_grads = [
            tn(normed, grad_query),
            *jnp.moveaxis(tn(normed, grad_pair).reshape(D, QUARTERS, 2, -1), 2, 0),
            tn(heads, grad_branch),
        ]
        packed_grad = jnp.concatenate(
            [
                grad.astype(LOW).reshape(row_count, depth, col_count, -1)
                for grad in full_grads
            ],
            axis=3,
        )
        row_sums = lax.psum_scatter(packed_grad, "rows", scatter_dimension=0)
        sums = lax.psum_scatter(row_sums, "cols", scatter_dimension=1).astype(WIDE)
        expert_sums = reduced
        small_grads = jnp.concatenate(
            [
                attention_gain_grad.reshape(-1, gain_part),
                experts_gain_grad.reshape(-1, gain_part),
                jnp.transpose(
                    router_grad.reshape(col_count, router_part, row_count, depth), (2, 0, 3, 1)
                ).reshape(row_count * col_count, depth * router_part),
            ],
            axis=1,
        )
        small_grads = small_grads.reshape(row_count, -1)
        small_grads = lax.all_to_all(small_grads, "rows", split_axis=0, concat_axis=0, tiled=True)
        small_grads = jnp.sum(small_grads, axis=0).reshape(col_count, -1)
        small_grads = lax.all_to_all(small_grads, "cols", split_axis=0, concat_axis=0, tiled=True)
        small_sums = jnp.sum(small_grads, axis=0)
        attention_gain_sum = small_sums[:gain_part]
        experts_gain_sum = small_sums[gain_part : 2 * gain_part]
        router_sum = small_sums[2 * gain_part :].reshape(depth, router_part)
        out_sum = sums[:, query_part + 2 * key_part :]

    layer_output = (residual + sum_parts(mixture)).astype(LOW)
    key_at = query_part
    value_at = key_at + key_part
    out_at = value_at + key_part
    part = down_weight.shape[1]
    gate_grad, upward_grad, down_grad = (
        jnp.stack([sums_of[which * part : (which + 1) * part] for sums_of in expert_sums])
        for which in range(3)
    )
    return (
        layer_output,
        tokens_grad,
        sums[:, :key_at],
        sums[:, key_at:value_at],
        sums[:, value_at:out_at],
        out_sum,
        router_sum,
        attention_gain_sum,
        experts_gain_sum,
        jnp.swapaxes(gate_grad, 1, 2),
        jnp.swapaxes(upward_grad, 1, 2),
        down_grad,
    )


def solution(mesh):
    in_specs = (
        P(("rows", "cols"), None),
        P("rows", "cols"),
        P("rows", "cols"),
        P("rows", "cols"),
        P("rows", "cols"),
        P("rows", "cols"),
        P(("rows", "cols")),
        P(("rows", "cols")),
        P("rows", None, "cols"),
        P("rows", None, "cols"),
        P("rows", "cols", None),
        P(("rows", "cols"), None),
        P(),
        P(("rows", "cols"), None),
    )
    out_specs = (
        P(("rows", "cols"), None),
        P(("rows", "cols"), None),
        P("rows", "cols"),
        P("rows", "cols"),
        P("rows", "cols"),
        P("rows", "cols"),
        P("rows", "cols"),
        P(("rows", "cols")),
        P(("rows", "cols")),
        P("rows", None, "cols"),
        P("rows", None, "cols"),
        P("rows", "cols", None),
    )
    return jax.shard_map(
        on_device, mesh=mesh, in_specs=in_specs, out_specs=out_specs, check_vma=False
    )
```

```python
import functools

import jax
import jax.numpy as jnp
from jax import lax
from jax.experimental import pallas as pl
from jax.experimental.pallas import tpu as pltpu
from jax.sharding import PartitionSpec as P

D = 1536
HEADS = 12
KV_HEADS = 2
HEAD_DIM = 128
TOP = 4
TOK_DEV = 512
BRANCHES = 4
LEAVES = 8
TRUNK = 256
BRANCH = 64

EPSILON = 1e-06
ROPE_BASE = 10000.0
MASKED = -1e30
LOW = jnp.bfloat16
WIDE = jnp.float32
KEY_WIDTH = KV_HEADS * HEAD_DIM
GROUP = HEADS // KV_HEADS
QUARTERS = 4
VMEM_LIMIT = 56 * 1024 * 1024

ANY = pl.BlockSpec(memory_space=pl.ANY)
SMEM = pl.BlockSpec(memory_space=pltpu.SMEM)


def nn(one, two):
    return lax.dot_general(one, two, (((1,), (0,)), ((), ())), preferred_element_type=WIDE)


def nt(one, two):
    return lax.dot_general(one, two, (((1,), (1,)), ((), ())), preferred_element_type=WIDE)


def tn(one, two):
    return lax.dot_general(one, two, (((0,), (0,)), ((), ())), preferred_element_type=WIDE)


def whole(shape):
    return pl.BlockSpec(shape, lambda *_: (0,) * len(shape))


LITTLE = pl.CostEstimate(flops=1, bytes_accessed=1, transcendentals=0)


def params():
    return pltpu.CompilerParams(vmem_limit_bytes=VMEM_LIMIT)


def turn(values, cosine, sine):
    return values * cosine + pltpu.roll(values, HEAD_DIM // 2, 1) * sine


def turn_back(values, cosine, sine):
    return values * cosine - pltpu.roll(values, HEAD_DIM // 2, 1) * sine


PIECES = tuple(
    (flip_bits + core, slots)
    for core in (0, 1)
    for flip_bits, slots in (
        (0, (0, 1, 2, 3)),
        (2, (0, 1, 2, 3)),
        (4, (0, 1, 2, 3)),
        (6, (0, 1)),
        (6, (2, 3)),
    )
)
EXTRA = 16


def weight_copies(info, refs, target, sem, start, width):
    if len(refs) == 1:
        return [pltpu.make_async_copy(refs[0], target, sem)]
    depth = refs[0].shape[1] - EXTRA
    copies = []
    for ref, (flip_bits, slots) in zip(refs, PIECES):
        row = pl.multiple_of((info[0] ^ flip_bits) * depth, depth)
        for at, slot in enumerate(slots):
            col = pl.multiple_of(info[2 + slot] * width, 128)
            copies.append(
                pltpu.make_async_copy(
                    ref.at[at, pl.ds(0, depth), pl.ds(start, width)],
                    target.at[pl.ds(row, depth), pl.ds(col, width)],
                    sem,
                )
            )
    return copies


def extras_kernel(info, *rest):
    refs, (out, sem) = rest[:-2], rest[-2:]
    depth = refs[0].shape[1] - EXTRA
    copies = []
    for ref, (flip_bits, slots) in zip(refs, PIECES):
        for at, slot in enumerate(slots):
            to = (info[0] ^ flip_bits) * QUARTERS + info[2 + slot]
            copies.append(pltpu.make_async_copy(ref.at[at, pl.ds(depth, EXTRA)], out.at[to], sem))
    run_all(copies)
    wait_all(copies)


def extras(info, refs):
    return pl.pallas_call(
        extras_kernel,
        out_shape=jax.ShapeDtypeStruct((8 * QUARTERS, EXTRA, refs[0].shape[2]), LOW),
        in_specs=[SMEM] + [ANY] * len(refs),
        out_specs=pl.BlockSpec(memory_space=pltpu.VMEM),
        scratch_shapes=[pltpu.SemaphoreType.DMA],
        compiler_params=params(),
        cost_estimate=LITTLE,
        name="extra_rows",
    )(info, *refs)


def run_all(copies):
    for copy in copies:
        copy.start()


def wait_all(copies):
    for copy in copies:
        copy.wait()


def key_value_kernel(info, tokens, gain, cosine, sine, *rest):
    count = len(rest) - 4
    refs, (normed, out, weight, sem) = rest[:count], rest[count:]
    copies = weight_copies(info, refs, weight, sem, D // QUARTERS, 128)
    run_all(copies)
    values = tokens[...].astype(WIDE)
    factor = lax.rsqrt(jnp.mean(values * values, axis=-1, keepdims=True) + EPSILON)
    low = (values * factor * gain[...]).astype(LOW)
    normed[...] = low
    wait_all(copies)
    both = nn(low, weight[...])
    half = HEAD_DIM // 2
    first = lax.broadcasted_iota(jnp.int32, (TOK_DEV, HEAD_DIM), 1) < half
    for g in range(KV_HEADS):
        one = both[:, 256 * g : 256 * g + 128]
        two = both[:, 256 * g + 128 : 256 * g + 256]
        key = jnp.where(first, one, pltpu.roll(two, half, 1))
        value = jnp.where(first, pltpu.roll(one, half, 1), two)
        out[:, 128 * g : 128 * g + 128] = turn(key, cosine[...], sine[...]).astype(LOW)
        out[:, KEY_WIDTH + 128 * g : KEY_WIDTH + 128 * g + 128] = value.astype(LOW)


def key_value(info, tokens, gain, cosine, sine, refs):
    return pl.pallas_call(
        key_value_kernel,
        out_shape=(
            jax.ShapeDtypeStruct((TOK_DEV, D), LOW),
            jax.ShapeDtypeStruct((TOK_DEV, 2 * KEY_WIDTH), LOW),
        ),
        in_specs=[SMEM] + [pl.BlockSpec(memory_space=pltpu.VMEM)] * 4 + [ANY] * len(refs),
        out_specs=(pl.BlockSpec(memory_space=pltpu.VMEM),) * 2,
        scratch_shapes=[pltpu.VMEM((D, 2 * KEY_WIDTH), LOW), pltpu.SemaphoreType.DMA],
        compiler_params=params(),
        cost_estimate=LITTLE,
        name="norm_key_value",
    )(info, tokens, gain, cosine, sine, *refs)


def query_kernel(info, normed, cosine, sine, *rest):
    count = len(rest) - 3
    refs, (out, weight, sem) = rest[:count], rest[count:]

    @pl.when(pl.program_id(0) == 0)
    def _():
        copies = weight_copies(info, refs, weight, sem, 0, D // QUARTERS)
        run_all(copies)
        wait_all(copies)

    at = pl.multiple_of(pl.program_id(0) * 256, 256)
    lin = nn(normed[...], weight[:, pl.ds(at, 256)])
    for h in range(2):
        out[:, 128 * h : 128 * h + 128] = turn(
            lin[:, 128 * h : 128 * h + 128], cosine[...], sine[...]
        ).astype(LOW)


def query(info, normed, cosine, sine, refs):
    return pl.pallas_call(
        query_kernel,
        grid=(D // 256,),
        out_shape=jax.ShapeDtypeStruct((TOK_DEV, D), LOW),
        in_specs=[SMEM, whole((TOK_DEV, D)), whole((TOK_DEV, 128)), whole((TOK_DEV, 128))]
        + [ANY] * len(refs),
        out_specs=pl.BlockSpec((TOK_DEV, 256), lambda i: (0, i)),
        scratch_shapes=[pltpu.VMEM((D, D), LOW), pltpu.SemaphoreType.DMA],
        compiler_params=params(),
        cost_estimate=LITTLE,
        name="query_projection",
    )(info, normed, cosine, sine, *refs)


KEYS = TRUNK + 2 * BRANCH
CHUNKS = TOK_DEV // BRANCH


def chunk_keys(info, source, own, column, chunk):
    at = pl.multiple_of(info[6 + chunk], BRANCH)
    rows = pl.multiple_of(chunk * BRANCH, BRANCH)
    columns = slice(column, column + HEAD_DIM)
    return jnp.concatenate(
        [
            source[0:TRUNK, columns],
            source[pl.ds(at, BRANCH), columns],
            own[pl.ds(rows, BRANCH), columns],
        ],
        axis=0,
    )


def chunk_allowed(info, chunk, query_axis, shape):
    query_row = lax.broadcasted_iota(jnp.int32, shape, query_axis) & (BRANCH - 1)
    key = lax.broadcasted_iota(jnp.int32, shape, 1 - query_axis)
    leaves = info[1] == 0
    trunk = jnp.logical_and(jnp.logical_not(leaves), chunk < TRUNK // BRANCH)
    limit = jnp.where(trunk, chunk * BRANCH + query_row, TRUNK - 1)
    branch_limit = jnp.where(leaves, TRUNK + BRANCH - 1, 0)
    own_limit = jnp.where(trunk, 0, query_row + TRUNK + BRANCH)
    top = jnp.where(key < TRUNK, limit, jnp.where(key < TRUNK + BRANCH, branch_limit, own_limit))
    return key <= top


def group_rows(ref, g):
    first = g * GROUP
    return jnp.concatenate(
        [ref[:, 128 * h : 128 * h + 128] for h in range(first, first + GROUP)], axis=0
    )


def keep_source(info, partner, own, source):
    @pl.when(pl.program_id(0) == 0)
    def _():
        @pl.when(info[1] == 0)
        def _():
            source[...] = partner[...]

        @pl.when(info[1] != 0)
        def _():
            source[...] = own[...]


def attention_kernel(info, queries, own, partner, out, source):
    keep_source(info, partner, own, source)
    chunk = pl.program_id(0)
    rows = GROUP * BRANCH
    allowed = chunk_allowed(info, chunk, 0, (rows, KEYS))
    for g in range(KV_HEADS):
        keys = chunk_keys(info, source, own, 128 * g, chunk)
        values = chunk_keys(info, source, own, KEY_WIDTH + 128 * g, chunk)
        scores = nt(group_rows(queries, g), keys) * HEAD_DIM**-0.5
        scores = jnp.where(allowed, scores, MASKED)
        weights = jnp.exp(scores - jnp.max(scores, axis=1, keepdims=True))
        total = jnp.sum(weights, axis=1, keepdims=True)
        mixed = nn((weights * (1.0 / total)).astype(LOW), values).astype(LOW)
        for h in range(GROUP):
            at = (g * GROUP + h) * 128
            out[:, at : at + 128] = mixed[h * BRANCH : (h + 1) * BRANCH]


def attention(info, queries, own, partner):
    return pl.pallas_call(
        attention_kernel,
        grid=(CHUNKS,),
        out_shape=jax.ShapeDtypeStruct((TOK_DEV, D), LOW),
        in_specs=[
            SMEM,
            pl.BlockSpec((BRANCH, D), lambda i: (i, 0)),
            whole((TOK_DEV, 2 * KEY_WIDTH)),
            whole((TOK_DEV, 2 * KEY_WIDTH)),
        ],
        out_specs=pl.BlockSpec((BRANCH, D), lambda i: (i, 0)),
        scratch_shapes=[pltpu.VMEM((TOK_DEV, 2 * KEY_WIDTH), LOW)],
        compiler_params=params(),
        cost_estimate=LITTLE,
        name="tree_attention",
    )(info, queries, own, partner)


def attention_back_kernel(
    info, queries, own, partner, grads, cosine, sine, grad_query, own_grad, source_grad, source
):
    keep_source(info, partner, own, source)
    chunk = pl.program_id(0)

    @pl.when(chunk == 0)
    def _():
        source_grad[...] = jnp.zeros_like(source_grad)

    rows = GROUP * BRANCH
    scale = HEAD_DIM**-0.5
    allowed = chunk_allowed(info, chunk, 1, (KEYS, rows))
    at = pl.multiple_of(info[6 + chunk], BRANCH)
    for g in range(KV_HEADS):
        keys = chunk_keys(info, source, own, 128 * g, chunk)
        values = chunk_keys(info, source, own, KEY_WIDTH + 128 * g, chunk)
        query_rows = group_rows(queries, g)
        grad_rows = group_rows(grads, g)
        scores = jnp.where(allowed, nt(keys, query_rows) * scale, MASKED)
        weights = jnp.exp(scores - jnp.max(scores, axis=0, keepdims=True))
        probs = weights * (1.0 / jnp.sum(weights, axis=0, keepdims=True))
        grad_probs = nt(values, grad_rows)
        mean = jnp.sum(probs * grad_probs, axis=0, keepdims=True)
        grad_scores = (probs * (grad_probs - mean)).astype(LOW)
        grad_values = nn(probs.astype(LOW), grad_rows)
        grad_keys = nn(grad_scores, query_rows) * scale
        grad_queries = tn(grad_scores, keys) * scale
        for h in range(GROUP):
            to = (g * GROUP + h) * 128
            grad_query[:, to : to + 128] = turn_back(
                grad_queries[h * BRANCH : (h + 1) * BRANCH], cosine[...], sine[...]
            ).astype(LOW)
        for column, grad in ((128 * g, grad_keys), (KEY_WIDTH + 128 * g, grad_values)):
            columns = slice(column, column + 128)
            source_grad[0:TRUNK, columns] += grad[0:TRUNK]
            source_grad[pl.ds(at, BRANCH), columns] += grad[TRUNK : TRUNK + BRANCH]
            own_grad[:, columns] = grad[TRUNK + BRANCH :]


def attention_back(info, queries, own, partner, grads, cosine, sine):
    chunked = pl.BlockSpec((BRANCH, D), lambda i: (i, 0))
    pair = (TOK_DEV, 2 * KEY_WIDTH)
    return pl.pallas_call(
        attention_back_kernel,
        grid=(CHUNKS,),
        out_shape=(
            jax.ShapeDtypeStruct((TOK_DEV, D), LOW),
            jax.ShapeDtypeStruct(pair, WIDE),
            jax.ShapeDtypeStruct(pair, WIDE),
        ),
        in_specs=[
            SMEM,
            chunked,
            whole(pair),
            whole(pair),
            chunked,
            pl.BlockSpec((BRANCH, 128), lambda i: (i, 0)),
            pl.BlockSpec((BRANCH, 128), lambda i: (i, 0)),
        ],
        out_specs=(
            chunked,
            pl.BlockSpec((BRANCH, 2 * KEY_WIDTH), lambda i: (i, 0)),
            whole(pair),
        ),
        scratch_shapes=[pltpu.VMEM(pair, LOW)],
        compiler_params=params(),
        cost_estimate=LITTLE,
        name="tree_attention_back",
    )(info, queries, own, partner, grads, cosine, sine)


def out_kernel(info, heads, tokens, gain, *rest):
    count = len(rest) - 4
    refs, (residual, normed, weight, sem) = rest[:count], rest[count:]

    @pl.when(pl.program_id(0) == 0)
    def _():
        copies = weight_copies(info, refs, weight, sem, D // QUARTERS + 128, D // QUARTERS)
        run_all(copies)
        wait_all(copies)

    at = pl.ds(pl.multiple_of(pl.program_id(0) * 256, 256), 256)
    residual[:, at] = tokens[:, at].astype(WIDE) + nn(heads[...], weight[:, at])

    @pl.when(pl.program_id(0) == pl.num_programs(0) - 1)
    def _():
        values = residual[...]
        factor = lax.rsqrt(jnp.mean(values * values, axis=-1, keepdims=True) + EPSILON)
        normed[...] = (values * factor * gain[...]).astype(LOW)


def out_projection(info, heads, tokens, gain, refs):
    full = (TOK_DEV, D)
    return pl.pallas_call(
        out_kernel,
        grid=(D // 256,),
        out_shape=(jax.ShapeDtypeStruct(full, WIDE), jax.ShapeDtypeStruct(full, LOW)),
        in_specs=[SMEM, whole(full), whole(full), whole((1, D))] + [ANY] * len(refs),
        out_specs=(whole(full), whole(full)),
        scratch_shapes=[pltpu.VMEM((D, D), LOW), pltpu.SemaphoreType.DMA],
        compiler_params=params(),
        cost_estimate=LITTLE,
        name="out_projection",
    )(info, heads, tokens, gain, *refs)


def hits_of(routes, ids):
    hit = ids == routes[0, 0:1]
    for k in range(1, TOP):
        hit = jnp.logical_or(hit, ids == routes[0, k : k + 1])
    return hit


def tables_kernel(capacity, local, total, order, info, routes, chosen_out, place_out, earlier):
    @pl.when(pl.program_id(0) == 0)
    def _():
        one = lax.broadcasted_iota(jnp.int32, (TOK_DEV, TOK_DEV), 0)
        two = lax.broadcasted_iota(jnp.int32, (TOK_DEV, TOK_DEV), 1)
        earlier[...] = jnp.where(one < two, 1.0, 0.0).astype(LOW)

    ids = lax.broadcasted_iota(jnp.int32, (total, TOK_DEV), 0)
    hit = hits_of(routes, ids)
    rank = nn(jnp.where(hit, 1.0, 0.0).astype(LOW), earlier[...])
    place = jnp.where(hit, rank, -1.0)
    spots = lax.broadcasted_iota(jnp.int32, (capacity, TOK_DEV), 0).astype(WIDE)
    place_out[0] = jnp.full(place_out.shape[1:], -1.0, WIDE)
    for e in range(local):
        mine = ids == info[0] * local + e
        place_row = jnp.sum(jnp.where(mine, place, 0.0), axis=0, keepdims=True)
        place_out[0, e : e + 1] = place_row
        chosen_out[0, e * capacity : (e + 1) * capacity] = jnp.where(
            spots == place_row, 1.0, 0.0
        ).astype(LOW)


def tables(order, info, routes, capacity, local, total):
    count = routes.shape[0]
    return pl.pallas_call(
        functools.partial(tables_kernel, capacity, local, total),
        grid_spec=pltpu.PrefetchScalarGridSpec(
            num_scalar_prefetch=2,
            grid=(count,),
            in_specs=[pl.BlockSpec((1, TOP, TOK_DEV), lambda i, order, info: (order[i], 0, 0))],
            out_specs=[
                pl.BlockSpec((1, local * capacity, TOK_DEV), lambda i, order, info: (i, 0, 0)),
                pl.BlockSpec((1, 8, TOK_DEV), lambda i, order, info: (i, 0, 0)),
            ],
            scratch_shapes=[pltpu.VMEM((TOK_DEV, TOK_DEV), LOW)],
        ),
        out_shape=[
            jax.ShapeDtypeStruct((count, local * capacity, TOK_DEV), LOW),
            jax.ShapeDtypeStruct((count, 8, TOK_DEV), WIDE),
        ],
        compiler_params=params(),
        cost_estimate=LITTLE,
        name="route_tables",
    )(order, info, routes)


def pick_kernel(local, order, chosen, blocks, *outs):
    rows_of = nn(chosen[0], blocks[0]).astype(LOW)
    capacity = outs[0].shape[1]
    for e in range(local):
        outs[e][0] = rows_of[e * capacity : (e + 1) * capacity]


def pick_rows(order, chosen, blocks, local):
    count, height, _ = chosen.shape
    capacity = height // local
    return pl.pallas_call(
        functools.partial(pick_kernel, local),
        grid_spec=pltpu.PrefetchScalarGridSpec(
            num_scalar_prefetch=1,
            grid=(count,),
            in_specs=[
                pl.BlockSpec((1, height, TOK_DEV), lambda i, order: (i, 0, 0)),
                pl.BlockSpec((1, TOK_DEV, D), lambda i, order: (order[i], 0, 0)),
            ],
            out_specs=[pl.BlockSpec((1, capacity, D), lambda i, order: (i, 0, 0))] * local,
        ),
        out_shape=[jax.ShapeDtypeStruct((count, capacity, D), LOW)] * local,
        compiler_params=params(),
        cost_estimate=LITTLE,
        name="pick_rows",
    )(order, chosen, blocks)


def dispatch_kernel(local, near, info, rows, chosen, routes, router, *rest):
    outs, logits = rest[2 * local : 4 * local], rest[-1]
    total = router.shape[1]
    step = pl.program_id(0)
    block = rows[...]
    rows_of = nn(chosen[0], block).astype(LOW)
    capacity = outs[0].shape[1]
    for e in range(local):
        outs[e][0] = rows_of[e * capacity : (e + 1) * capacity]
    part = nn(block, router[...])

    @pl.when(step == 0)
    def _():
        logits[...] = part

    @pl.when(step > 0)
    def _():
        logits[...] += part

    @pl.when(step == pl.num_programs(0) - 1)
    def _():
        values = logits[...].T
        ids = lax.broadcasted_iota(jnp.int32, (total, TOK_DEV), 0)
        weights = jnp.exp(values - jnp.max(values, axis=0, keepdims=True))
        hit = hits_of(routes, ids)
        share = weights / jnp.sum(jnp.where(hit, weights, 0.0), axis=0, keepdims=True)
        for e in range(local):
            mine = ids == info[0] * local + e
            share_row = jnp.sum(jnp.where(mine, share, 0.0), axis=0, keepdims=True)
            picked = chosen[0, e * capacity : (e + 1) * capacity].astype(WIDE)
            outs[local + e][0] = jnp.sum(picked * share_row, axis=1, keepdims=True)


def dispatch(at, near, info, rows, chosen, routes, router, local, earlier):
    count, height, _ = chosen.shape
    capacity = height // local
    total = router.shape[1]
    wide = 512
    out_shape = [jax.ShapeDtypeStruct((count, capacity, D), LOW)] * local + [
        jax.ShapeDtypeStruct((count, capacity, 1), WIDE)
    ] * local
    if earlier is None:
        earlier = [jnp.zeros((8, 128), shape.dtype) for shape in out_shape]
        aliases = {}
    else:
        aliases = {6 + i: i for i in range(len(out_shape))}
    return pl.pallas_call(
        functools.partial(dispatch_kernel, local),
        grid_spec=pltpu.PrefetchScalarGridSpec(
            num_scalar_prefetch=2,
            grid=(D // wide,),
            in_specs=[
                pl.BlockSpec((TOK_DEV, wide), lambda i, near, info: (0, i)),
                pl.BlockSpec((1, height, TOK_DEV), lambda i, near, info: (at, 0, 0)),
                pl.BlockSpec((1, TOP, TOK_DEV), lambda i, near, info: (near[at], 0, 0)),
                pl.BlockSpec((wide, total), lambda i, near, info: (i, 0)),
            ]
            + [ANY] * len(out_shape),
            out_specs=[
                pl.BlockSpec((1, capacity, wide), lambda i, near, info: (at, 0, i))
            ]
            * local
            + [pl.BlockSpec((1, capacity, 1), lambda i, near, info: (at, 0, 0))] * local,
            scratch_shapes=[pltpu.VMEM((TOK_DEV, total), WIDE)],
        ),
        out_shape=out_shape,
        input_output_aliases=aliases,
        compiler_params=params(),
        cost_estimate=LITTLE,
        name="dispatch",
    )(near, info, rows, chosen, routes, router, *earlier)


def spread_kernel(local, place, *rest):
    dots, out = rest[:local], rest[local]
    spots = lax.broadcasted_iota(jnp.int32, (dots[0].shape[1], TOK_DEV), 0).astype(WIDE)
    for e in range(local):
        chosen = spots == place[0, e : e + 1]
        out[0, e : e + 1] = jnp.sum(jnp.where(chosen, dots[e][0], 0.0), axis=0, keepdims=True)


def spread(place, dots):
    count, capacity, _ = dots[0].shape
    local = len(dots)
    return pl.pallas_call(
        functools.partial(spread_kernel, local),
        grid=(count,),
        out_shape=jax.ShapeDtypeStruct((count, local, TOK_DEV), WIDE),
        in_specs=[pl.BlockSpec((1, 8, TOK_DEV), lambda i: (i, 0, 0))]
        + [pl.BlockSpec((1, capacity, 1), lambda i: (i, 0, 0))] * local,
        out_specs=pl.BlockSpec((1, local, TOK_DEV), lambda i: (i, 0, 0)),
        compiler_params=params(),
        cost_estimate=LITTLE,
        name="spread",
    )(place, *dots)


def expert_kernel(slots, info, rows, grads, shares, *rest):
    count = len(rest) - 7
    refs = rest[:count]
    out_rows, back_rows, grad_rows, acts, dots, weight, sem = rest[count:]
    part = weight.shape[1] // slots

    @pl.when(pl.program_id(0) == 0)
    def _():
        def copies(ref, slot):
            return [
                pltpu.make_async_copy(
                    ref.at[pl.ds(which * part, part)],
                    weight.at[which, pl.ds(slot * part, part)],
                    sem,
                )
                for which in range(3)
            ]

        if count == slots:
            for slot in range(slots):
                run_all(copies(refs[slot], slot))
        else:
            block, second, above, below, far = refs
            low_end = info[2] == 0
            end = jnp.logical_or(low_end, info[2] == 3)
            run_all(copies(block, 0))
            run_all(copies(second, 1))

            @pl.when(low_end)
            def _():
                run_all(copies(above, 2))

            @pl.when(jnp.logical_not(low_end))
            def _():
                run_all(copies(below, 2))

            @pl.when(end)
            def _():
                run_all(copies(far, 3))

            @pl.when(jnp.logical_not(end))
            def _():
                run_all(copies(above, 3))

        for slot in range(slots):
            wait_all(copies(refs[0], slot))

    row_block = rows[...]
    share = shares[...]
    grad_float = grads[...].astype(WIDE)
    grad_low = (share * grad_float).astype(LOW)
    grad_rows[...] = grad_low
    gate_act = nt(row_block, weight[0])
    upward = nt(row_block, weight[1])
    sigmoid = 1.0 / (1.0 + jnp.exp(-gate_act))
    silu = gate_act * sigmoid
    hidden = (silu * upward).astype(LOW)
    expert_out = nn(hidden, weight[2]).astype(LOW).astype(WIDE)
    out_rows[...] = (share * expert_out).astype(LOW)
    dots[...] = jnp.sum(grad_float * expert_out, axis=1, keepdims=True)
    grad_hidden = nt(grad_low, weight[2])
    grad_gate = (grad_hidden * upward * sigmoid * (1.0 + gate_act * (1.0 - sigmoid))).astype(LOW)
    grad_up = (grad_hidden * silu).astype(LOW)
    back_rows[...] = (nn(grad_gate, weight[0]) + nn(grad_up, weight[1])).astype(LOW)
    for which, act in enumerate((grad_gate, grad_up, hidden)):
        turned = act.T
        for slot in range(slots):
            acts[slot, which * part : (which + 1) * part] = turned[
                slot * part : (slot + 1) * part
            ]


EXPERT_ROWS = 256


def expert(info, rows, grads, shares, refs, slots):
    height = rows.shape[0]
    part = refs[0].shape[0] // 3
    wide_block = pl.BlockSpec((EXPERT_ROWS, D), lambda i: (i, 0))
    thin_block = pl.BlockSpec((EXPERT_ROWS, 1), lambda i: (i, 0))
    return pl.pallas_call(
        functools.partial(expert_kernel, slots),
        grid=(height // EXPERT_ROWS,),
        out_shape=[jax.ShapeDtypeStruct((height, D), LOW)] * 3
        + [
            jax.ShapeDtypeStruct((slots, 3 * part, height), LOW),
            jax.ShapeDtypeStruct((height, 1), WIDE),
        ],
        in_specs=[SMEM, wide_block, wide_block, thin_block] + [ANY] * len(refs),
        out_specs=[wide_block] * 3
        + [pl.BlockSpec((slots, 3 * part, EXPERT_ROWS), lambda i: (0, 0, i)), thin_block],
        scratch_shapes=[pltpu.VMEM((3, slots * part, D), LOW), pltpu.SemaphoreType.DMA],
        compiler_params=params(),
        cost_estimate=LITTLE,
        name="expert",
    )(info, rows, grads, shares, *refs)


def expert_grads_kernel(slots, rows, grads, *rest):
    acts, outs = rest[: len(slots)], rest[len(slots) :]
    part = acts[0].shape[1] // 3
    for act, out in zip(acts, outs):
        out[: 2 * part, :] = nn(act[0, : 2 * part], rows[...]).astype(LOW)
        out[2 * part :, :] = nn(act[0, 2 * part :], grads[...]).astype(LOW)


def expert_grads(acts, rows, grads, slots):
    _, part, height = acts.shape
    return pl.pallas_call(
        functools.partial(expert_grads_kernel, slots),
        grid=(D // 256,),
        out_shape=[jax.ShapeDtypeStruct((part, D), LOW) for _ in slots],
        in_specs=[pl.BlockSpec((height, 256), lambda i: (0, i))] * 2
        + [pl.BlockSpec((1, part, height), lambda i, s=slot: (s, 0, 0)) for slot in slots],
        out_specs=[pl.BlockSpec((part, 256), lambda i: (0, i)) for _ in slots],
        compiler_params=params(),
        cost_estimate=LITTLE,
        name="expert_gradients",
    )(rows, grads, *[acts] * len(slots))


def combine_kernel(local, chosen, *rest):
    rows, out = rest[:local], rest[local]
    both = jnp.concatenate([ref[0] for ref in rows], axis=0)
    out[0] = tn(chosen[0], both).astype(LOW)


def combine(chosen, rows, first, step):
    count, capacity, _ = rows[0].shape
    number = (count - first + step - 1) // step
    return pl.pallas_call(
        functools.partial(combine_kernel, len(rows)),
        grid=(number,),
        out_shape=jax.ShapeDtypeStruct((number, TOK_DEV, D), LOW),
        in_specs=[
            pl.BlockSpec((1,) + chosen.shape[1:], lambda i: (first + step * i, 0, 0))
        ]
        + [pl.BlockSpec((1, capacity, D), lambda i: (first + step * i, 0, 0))] * len(rows),
        out_specs=pl.BlockSpec((1, TOK_DEV, D), lambda i: (i, 0, 0)),
        compiler_params=params(),
        cost_estimate=LITTLE,
        name="combine",
    )(chosen, *rows)


def split(values):
    high = values.astype(LOW)
    return high, (values - high.astype(WIDE)).astype(LOW)


def norm_back(values, gain, grad):
    factor = lax.rsqrt(jnp.mean(values * values, axis=-1, keepdims=True) + EPSILON)
    scaled = gain * grad
    mean = jnp.mean(values * scaled, axis=-1, keepdims=True)
    grad_values = factor * scaled - values * (factor * factor * factor * mean)
    grad_gain = jnp.sum(grad * values * factor, axis=0, keepdims=True)
    return grad_values, grad_gain


def router_back(logits, routes, grad_shares):
    ids = lax.broadcasted_iota(jnp.int32, logits.shape, 0)
    hit = ids == routes[0:1]
    for k in range(1, TOP):
        hit = jnp.logical_or(hit, ids == routes[k : k + 1])
    weights = jnp.exp(logits - jnp.max(logits, axis=0, keepdims=True))
    probs = weights / jnp.sum(weights, axis=0, keepdims=True)
    chosen = jnp.sum(jnp.where(hit, probs, 0.0), axis=0, keepdims=True)
    grads = jnp.where(hit, grad_shares, 0.0)
    mean = jnp.sum(probs * grads, axis=0, keepdims=True) / chosen
    grad_probs = jnp.where(hit, (grads - mean) / chosen, 0.0)
    return probs * (grad_probs - jnp.sum(probs * grad_probs, axis=0, keepdims=True))


def branch_back_kernel(
    parts, info, residual, normed, cotangent, routes, grad_shares, router, gain, *rest
):
    sums, rest = rest[:parts], rest[parts:]
    count = len(rest) - 7
    refs = rest[:count]
    grad_residual, grad_branch, grad_heads, grad_gain, grad_router, weight, sem = rest[count:]

    @pl.when(pl.program_id(0) == 0)
    def _():
        copies = weight_copies(info, refs, weight, sem, D // QUARTERS + 128, D // QUARTERS)
        run_all(copies)
        logits = nt(router[...], normed[...])
        high, low = split(router_back(logits, routes[...], grad_shares[...]))
        grad_router[...] = nn(high, normed[...]) + nn(low, normed[...])
        grad_normed = tn(high, router[...]) + tn(low, router[...])
        if parts == 1:
            grad_normed += sums[0][...]
        else:
            values = [ref[...].astype(WIDE) for ref in sums]
            grad_normed += jnp.concatenate(
                [values[0] + values[1] + values[2], values[3] + values[4] + values[5]], axis=0
            )
        grad_values, gain_grad = norm_back(residual[...], gain[...], grad_normed)
        grad_gain[...] = gain_grad
        total = cotangent[...].astype(WIDE) + grad_values
        grad_residual[...] = total
        grad_branch[...] = total.astype(LOW)
        wait_all(copies)

    at = pl.ds(pl.multiple_of(pl.program_id(0) * 256, 256), 256)
    grad_heads[...] = nt(grad_branch[...], weight[at, :]).astype(LOW)


def branch_back(info, residual, normed, sums, cotangent, routes, grad_shares, router, gain, refs):
    full = (TOK_DEV, D)
    total = router.shape[0]
    return pl.pallas_call(
        functools.partial(branch_back_kernel, len(sums)),
        grid=(D // 256,),
        out_shape=(
            jax.ShapeDtypeStruct(full, WIDE),
            jax.ShapeDtypeStruct(full, LOW),
            jax.ShapeDtypeStruct(full, LOW),
            jax.ShapeDtypeStruct((1, D), WIDE),
            jax.ShapeDtypeStruct((total, D), WIDE),
        ),
        in_specs=[SMEM]
        + [whole(full)] * 3
        + [whole((TOP, TOK_DEV)), whole((total, TOK_DEV)), whole((total, D)), whole((1, D))]
        + [whole(part.shape) for part in sums]
        + [ANY] * len(refs),
        out_specs=(
            whole(full),
            whole(full),
            pl.BlockSpec((TOK_DEV, 256), lambda i: (0, i)),
            whole((1, D)),
            whole((total, D)),
        ),
        scratch_shapes=[pltpu.VMEM((D, D), LOW), pltpu.SemaphoreType.DMA],
        compiler_params=params(),
        cost_estimate=LITTLE,
        name="experts_norm_back",
    )(info, residual, normed, cotangent, routes, grad_shares, router, gain, *sums, *refs)


def join_grads_kernel(info, own_grad, source_grad, arrived, cosine, sine, out):
    half = HEAD_DIM // 2
    first = lax.broadcasted_iota(jnp.int32, (TOK_DEV, HEAD_DIM), 1) < half
    leaves = info[1] == 0

    def total(column):
        columns = slice(column, column + 128)
        extra = source_grad[:, columns] + arrived[:, columns].astype(WIDE)
        return own_grad[:, columns] + jnp.where(leaves, 0.0, extra)

    for g in range(KV_HEADS):
        key = turn_back(total(128 * g), cosine[...], sine[...])
        value = total(KEY_WIDTH + 128 * g)
        out[:, 256 * g : 256 * g + 128] = jnp.where(
            first, key, pltpu.roll(value, half, 1)
        ).astype(LOW)
        out[:, 256 * g + 128 : 256 * g + 256] = jnp.where(
            first, pltpu.roll(key, half, 1), value
        ).astype(LOW)


def join_grads(info, own_grad, source_grad, arrived, cosine, sine):
    vmem = pl.BlockSpec(memory_space=pltpu.VMEM)
    return pl.pallas_call(
        join_grads_kernel,
        out_shape=jax.ShapeDtypeStruct((TOK_DEV, 2 * KEY_WIDTH), LOW),
        in_specs=[SMEM] + [vmem] * 5,
        out_specs=vmem,
        compiler_params=params(),
        cost_estimate=LITTLE,
        name="join_key_value_gradients",
    )(info, own_grad, source_grad, arrived, cosine, sine)


def token_back_kernel(info, grad_query, grad_pair, tokens, grad_residual, gain, *rest):
    count = (len(rest) - 6) // 2
    query_refs, pair_refs = rest[:count], rest[count : 2 * count]
    out, grad_gain, query_weight, pair_weight, grad_normed, sem = rest[2 * count :]

    @pl.when(pl.program_id(0) == 0)
    def _():
        copies = weight_copies(info, query_refs, query_weight, sem, 0, D // QUARTERS)
        copies += weight_copies(info, pair_refs, pair_weight, sem, D // QUARTERS, 128)
        run_all(copies)
        wait_all(copies)

    at = pl.ds(pl.multiple_of(pl.program_id(0) * 256, 256), 256)
    grad_normed[:, at] = nt(grad_query[...], query_weight[at, :]) + nt(
        grad_pair[...], pair_weight[at, :]
    )

    @pl.when(pl.program_id(0) == pl.num_programs(0) - 1)
    def _():
        grad_values, gain_grad = norm_back(
            tokens[...].astype(WIDE), gain[...], grad_normed[...]
        )
        grad_gain[...] = gain_grad
        out[...] = (grad_residual[...] + grad_values).astype(LOW)


def token_back(info, grad_query, grad_pair, tokens, grad_residual, gain, query_refs, pair_refs):
    full = (TOK_DEV, D)
    return pl.pallas_call(
        token_back_kernel,
        grid=(D // 256,),
        out_shape=(jax.ShapeDtypeStruct(full, LOW), jax.ShapeDtypeStruct((1, D), WIDE)),
        in_specs=[
            SMEM,
            whole(full),
            whole((TOK_DEV, 2 * KEY_WIDTH)),
            whole(full),
            whole(full),
            whole((1, D)),
        ]
        + [ANY] * (len(query_refs) + len(pair_refs)),
        out_specs=(whole(full), whole((1, D))),
        scratch_shapes=[
            pltpu.VMEM((D, D), LOW),
            pltpu.VMEM((D, 2 * KEY_WIDTH), LOW),
            pltpu.VMEM(full, WIDE),
            pltpu.SemaphoreType.DMA,
        ],
        compiler_params=params(),
        cost_estimate=LITTLE,
        name="token_gradient",
    )(info, grad_query, grad_pair, tokens, grad_residual, gain, *query_refs, *pair_refs)


def weight_grads_kernel(parts, info, *rest):
    ins, (keep, send) = rest[:-2], rest[-2:]
    depth = D // 8
    core = info[0] & 1
    chip = pl.program_id(0) ^ (info[0] >> 1)
    start = 0
    for strip_at, grads_at, width in parts:
        low = tn(ins[strip_at][...], ins[grads_at][...]).astype(LOW)
        columns = slice(start, start + width)
        start += width
        for slot in range(QUARTERS):
            for j in range(QUARTERS):

                @pl.when(info[2 + slot] == j)
                def _():
                    piece = low[:, j * width : (j + 1) * width]
                    upper, lower = piece[:depth], piece[depth:]
                    keep[0, slot, :depth, columns] = jnp.where(core == 0, upper, lower)
                    send[0, slot, :depth, columns] = jnp.where(core == 0, lower, upper)

    if keep.shape[2] > depth:
        extra = ins[-1]
        for slot in range(QUARTERS):
            to = info[2 + slot]
            keep[0, slot, depth:] = extra[(chip * 2 + core) * QUARTERS + to]
            send[0, slot, depth:] = extra[(chip * 2 + 1 - core) * QUARTERS + to]


def weight_grads(info, strips, grads, parts, extra):
    depth = D // 8
    width = sum(part[2] for part in parts)
    strip = pl.BlockSpec((TOK_DEV, 2 * depth), lambda i, info: (0, i ^ (info[0] >> 1)))
    more = [] if extra is None else [extra]
    shape = (4, QUARTERS, depth + EXTRA * len(more), width)
    out = pl.BlockSpec((1,) + shape[1:], lambda i, info: (i, 0, 0, 0))
    return pl.pallas_call(
        functools.partial(weight_grads_kernel, parts),
        grid_spec=pltpu.PrefetchScalarGridSpec(
            num_scalar_prefetch=1,
            grid=(4,),
            in_specs=[strip] * len(strips)
            + [
                pl.BlockSpec(a.shape, lambda i, info, n=a.ndim: (0,) * n)
                for a in (*grads, *more)
            ],
            out_specs=(out, out),
        ),
        out_shape=(jax.ShapeDtypeStruct(shape, LOW),) * 2,
        compiler_params=params(),
        cost_estimate=LITTLE,
        name="weight_gradients",
    )(info, *strips, *grads, *more)


def position_of(token_index):
    branch_place = TRUNK + (token_index - TRUNK) % BRANCH
    leaf_place = TRUNK + BRANCH + (token_index - TOK_DEV) % BRANCH
    return jnp.where(
        token_index < TRUNK, token_index, jnp.where(token_index < TOK_DEV, branch_place, leaf_place)
    )


def rotary_tables(positions):
    half_dim = HEAD_DIM // 2
    frequency = ROPE_BASE ** (-jnp.arange(half_dim, dtype=jnp.float32) / half_dim)
    angles = positions.astype(jnp.float32)[:, None] * frequency[None, :]
    cosine, sine = (jnp.cos(angles), jnp.sin(angles))
    return (
        jnp.concatenate([cosine, cosine], axis=1),
        jnp.concatenate([-sine, sine], axis=1),
    )


def after(values, *earlier):
    return lax.optimization_barrier((values, earlier))[0]


def fast_mesh():
    return lax.axis_size("rows") == 8 and lax.axis_size("cols") == 4


SLOT_SHARD = ((0, 2, 1, 3), (1, 3, 0, 2), (2, 0, 1, 3), (3, 1, 2, 0))
UP = [(0, 1), (1, 2), (2, 3)]
DOWN = [(1, 0), (2, 1), (3, 2)]
FAR = [(0, 3), (3, 0)]


def send_first(block, chain=False):
    above = lax.ppermute(block, "cols", DOWN)
    below = lax.ppermute(block, "cols", UP)
    later = after(block, above, below) if chain else block
    return above, below, lax.ppermute(later, "cols", FAR)


def send_second(block, first):
    place = lax.axis_index("cols")
    above, below, _ = first
    payload = jnp.where(place == 1, above, jnp.where(place == 2, below, block))
    return lax.ppermute(payload, "cols", [(3, 1), (1, 0), (0, 2), (2, 3)])


def slot_list(block, first, second):
    place = lax.axis_index("cols")
    above, below, far = first
    end = (place == 0) | (place == 3)
    return [
        block,
        second,
        jnp.where(place == 0, above, below),
        jnp.where(end, far, above),
    ]


def reduce_first(second, fourth):
    return (
        lax.ppermute(second, "cols", [(1, 3), (0, 1), (2, 0), (3, 2)]),
        lax.ppermute(fourth, "cols", FAR),
    )


def reduce_second(third, fourth, relay):
    place = lax.axis_index("cols")
    relayed = relay.astype(WIDE)
    upward_load = (
        jnp.where(place == 0, third, fourth).astype(WIDE) + jnp.where(place == 1, relayed, 0.0)
    ).astype(LOW)
    downward_load = (third.astype(WIDE) + jnp.where(place == 2, relayed, 0.0)).astype(LOW)
    return (
        lax.ppermute(upward_load, "cols", UP),
        lax.ppermute(downward_load, "cols", DOWN),
    )


def reduce_last(own, first, second):
    place = lax.axis_index("cols")
    relay, far = first
    below, above = second
    end = (place == 0) | (place == 3)
    return (
        own.astype(WIDE)
        + below.astype(WIDE)
        + above.astype(WIDE)
        + jnp.where(end, relay.astype(WIDE) + far.astype(WIDE), 0.0)
    )


def flip(block, bit):
    count = lax.axis_size("rows")
    return lax.ppermute(block, "rows", [(i, i ^ bit) for i in range(count)])


def add_low(one, two):
    return (one.astype(WIDE) + two.astype(WIDE)).astype(LOW)


def reduce_chips(keep, got, hold=()):
    half = keep.shape[1] // 2

    def sums(chips, part):
        return jnp.stack([add_low(keep[i][part], got[i][part]) for i in chips])

    one, two = slice(0, half), slice(half, None)
    got_x = flip(sums((1, 3), one), 2)
    got_y = flip(sums((2, 3), two), 4)
    if hold:
        got_x, got_y = after((got_x, got_y), *hold)
    near_x = sums((0, 2), one)
    near_y = sums((0, 1), two)
    got_xy = flip(add_low(near_x[1], got_x[1]), 4)
    got_yx = flip(add_low(near_y[1], got_y[1]), 2)
    return (near_x[0], got_x[0], got_xy, near_y[0], got_y[0], got_yx)


def sum_parts(parts):
    wide = [a.astype(WIDE) for a in parts]
    if len(wide) == 1:
        return wide[0]
    return jnp.concatenate([wide[0] + wide[1] + wide[2], wide[3] + wide[4] + wide[5]], axis=0)


def on_device(
    tokens,
    query_weight,
    key_weight,
    value_weight,
    out_weight,
    router_weight,
    attention_gain,
    experts_gain,
    gate_weight,
    upward_weight,
    down_weight,
    routes,
    leaf_parent,
    cotangent,
):
    row_count = lax.axis_size("rows")
    col_count = lax.axis_size("cols")
    row_place = lax.axis_index("rows")
    col_place = lax.axis_index("cols")
    fast = fast_mesh()
    parity = lax.rem(col_place, 2)
    tree_id = lax.div(row_place * col_count + col_place, 2)
    parent_row = lax.dynamic_slice_in_dim(leaf_parent, tree_id, 1, 0)[0]
    depth, query_part = query_weight.shape
    key_part = key_weight.shape[1]
    router_part = router_weight.shape[1]
    gain_part = attention_gain.shape[0]
    expert_total = router_part * col_count
    local_experts = gate_weight.shape[0]
    capacity = TOK_DEV * TOP // expert_total * 5 // 4

    shards = (
        jnp.asarray(SLOT_SHARD, jnp.int32)[col_place]
        if fast
        else jnp.arange(4, dtype=jnp.int32)
    )
    branch_rows = jnp.where(parity == 0, TRUNK + BRANCH * parent_row, TRUNK)
    info = jnp.concatenate(
        [jnp.stack([row_place, parity]), shards, branch_rows, jnp.zeros((2,), jnp.int32)]
    ).astype(jnp.int32)

    packed = jnp.concatenate([query_weight, key_weight, value_weight, out_weight], axis=1)
    local_index = (1 - parity) * TOK_DEV + jnp.arange(TOK_DEV, dtype=jnp.int32)
    cosine, sine = rotary_tables(position_of(local_index))
    shard_blocks = [
        jnp.concatenate(
            [gate_weight[expert].T, upward_weight[expert].T, down_weight[expert]], axis=0
        )
        for expert in range(local_experts)
    ]
    firsts, seconds = ([], [])
    if fast:
        wide = packed.shape[1]
        gains = jnp.concatenate([attention_gain, experts_gain])[None, :]
        packed = jnp.concatenate(
            [
                packed,
                jnp.pad(router_weight.T, ((0, 0), (0, wide - depth))),
                jnp.pad(gains, ((0, 0), (0, wide - 2 * gain_part))),
                jnp.pad(routes.T.astype(LOW), ((0, 0), (0, wide - TOK_DEV))),
                jnp.zeros((EXTRA - router_part - 1 - TOP, wide), LOW),
            ],
            axis=0,
        )
        packed_first = send_first(packed)
        packed_second = send_second(packed, packed_first)
        own = jnp.stack(slot_list(packed, packed_first, packed_second))
        ahead = packed_first[:2]
        for expert_at in range(local_experts):
            block = after(shard_blocks[expert_at], *ahead)
            shard_blocks[expert_at] = block
            first = send_first(block, chain=True)
            firsts.append(first)
            seconds.append(send_second(block, first))
            ahead = (first[2], seconds[-1])
        own = after(own, info, cosine, sine)
        beside, across = flip(own, 2), flip(own, 4)
        beside, across = after((beside, across), *firsts[0][:2])
        same = [own, beside, across, flip(beside[:2], 4), flip(across[2:], 2)]
        pieces = same + [flip(piece, 1) for piece in same]
        query_refs = pair_refs = out_refs = pieces
        expert_refs = [
            [shard_blocks[i], seconds[i], *firsts[i]] for i in range(local_experts)
        ]
        extra_rows = extras(info, pieces)
        router_all = extra_rows[:, :router_part, :depth]
        attention_scale = extra_rows[:, router_part, :gain_part]
        experts_scale = extra_rows[:, router_part, gain_part : 2 * gain_part]
        routes_all = lax.dynamic_index_in_dim(
            extra_rows.reshape(row_count, col_count, EXTRA, -1), col_place, 1, keepdims=False
        )
        routes_all = routes_all[:, router_part + 1 : router_part + 1 + TOP, :TOK_DEV]
        routes_all = routes_all.astype(jnp.int32)
    else:
        packed_all = lax.all_gather(lax.all_gather(packed, "cols", axis=0), "rows", axis=0)

        def unpack(start, width):
            part = packed_all[..., start : start + width]
            return jnp.swapaxes(part, 1, 2).reshape(row_count * depth, col_count * width)

        key_at = query_part
        query_refs = [unpack(0, query_part)]
        pair_refs = [
            jnp.concatenate(
                [
                    unpack(key_at, key_part).reshape(D, QUARTERS, -1),
                    unpack(key_at + key_part, key_part).reshape(D, QUARTERS, -1),
                ],
                axis=2,
            ).reshape(D, -1)
        ]
        out_refs = [unpack(key_at + 2 * key_part, query_part)]
        routes_all = lax.all_gather(routes.T, "rows", axis=0)
        axes = ("rows", "cols")
        router_all = jnp.swapaxes(lax.all_gather(router_weight, axes, axis=0), 1, 2)
        attention_scale = lax.all_gather(attention_gain, axes, axis=0)
        experts_scale = lax.all_gather(experts_gain, axes, axis=0)
        expert_refs = [
            [lax.all_gather(block, "cols", axis=0)[i] for i in range(col_count)]
            for block in shard_blocks
        ]

    attention_scale = attention_scale.reshape(1, D).astype(WIDE)
    experts_scale = experts_scale.reshape(1, D).astype(WIDE)
    router_rows = jnp.transpose(
        router_all.reshape(row_count, col_count, router_part, depth), (1, 2, 0, 3)
    ).reshape(expert_total, D)
    router_cols = router_rows.T
    if fast:
        near_rows = row_place ^ jnp.arange(row_count, dtype=jnp.int32)
    else:
        near_rows = jnp.arange(row_count, dtype=jnp.int32)
    chosen, place_rows = tables(
        near_rows, info, routes_all, capacity, local_experts, expert_total
    )
    grad_in = after(cotangent, *pieces) if fast else cotangent
    grad_all = lax.all_gather(grad_in, "rows", axis=0)

    normed, own_pair = key_value(info, tokens, attention_scale, cosine, sine, pair_refs)
    pairs = [(i + 1, i) for i in range(0, col_count, 2)]
    partner = lax.ppermute(own_pair, "cols", pairs)
    queries = query(info, normed, cosine, sine, query_refs)
    heads = attention(info, queries, own_pair, partner)
    residual, normed_two = out_projection(info, heads, tokens, experts_scale, out_refs)

    if fast:
        beside, across = flip(normed_two, 2), flip(normed_two, 4)
        beside_in = flip(normed_two, 1)
        chosen = after(chosen, firsts[0][2], seconds[0])
        grad_all = after(grad_all, normed_two)
    else:
        rows_all = lax.all_gather(normed_two, "rows", axis=0)
    grad_rows = pick_rows(near_rows, chosen, grad_all, local_experts)

    def place_block(q, block, picked):
        return dispatch(
            q, near_rows, info, block, chosen, routes_all, router_cols, local_experts, picked
        )

    if fast:
        half = TOK_DEV // 2
        picked = place_block(0, normed_two, None)
        picked = place_block(1, beside_in, picked)
        beside, across = after((beside, across), picked, grad_rows, *firsts[1][:2])
        corner = [flip(beside[:half], 4), flip(across[half:], 2)]
        picked = place_block(2, beside, picked)
        picked = place_block(4, across, picked)
        picked = place_block(3, flip(beside, 1), picked)
        picked = place_block(5, flip(across, 1), picked)
        corner = jnp.concatenate(after(corner, picked), axis=0)
        corner_in = flip(corner, 1)
        picked = place_block(6, corner, picked)
        picked = place_block(7, corner_in, picked)
    else:
        picked = None
        for q in range(row_count):
            picked = place_block(q, rows_all[q], picked)
    height = row_count * capacity
    token_rows = [a.reshape(height, D) for a in picked[:local_experts]]
    grad_rows = [a.reshape(height, D) for a in grad_rows]
    share_rows = [a.reshape(height, 1) for a in picked[local_experts:]]

    out_rows, back_rows, gate_dots, reduced, marks = ([], [], [], [], [])
    for e in range(local_experts):
        rows_in = token_rows[e]
        if fast and e == 1:
            rows_in = after(rows_in, firsts[1][2], seconds[1], own_slot, third)
        out_row, back_row, grad_row, acts, dots = expert(
            info, rows_in, grad_rows[e], share_rows[e], expert_refs[e], col_count
        )
        out_rows.append(out_row.reshape(row_count, capacity, D))
        back_rows.append(back_row.reshape(row_count, capacity, D))
        gate_dots.append(dots.reshape(row_count, capacity, 1))
        if fast:
            if e == 1:
                got = flip(combine(chosen, back_rows, 1, 2), 1)
                acts = after(acts, got)
            second, fourth = expert_grads(acts, token_rows[e], grad_row, (1, 3))
            if e == 1:
                got = after(got, *marks[0], second)
                waits = reduced[0][2]
                second_out, fourth_out = after((second, fourth), *waits)
            else:
                second_out, fourth_out = second, fourth
            sent_first = reduce_first(second_out, fourth_out)
            marks.append(sent_first)
            own_slot, third = expert_grads(acts, token_rows[e], grad_row, (0, 2))
            sent_second = reduce_second(third, fourth, sent_first[0])
            reduced.append((own_slot, sent_first, sent_second))
        else:
            slots = expert_grads(acts, token_rows[e], grad_row, tuple(range(col_count)))
            reduced.append(
                lax.psum_scatter(jnp.stack(slots), "cols", scatter_dimension=0).astype(WIDE)
            )

    spread_dots = spread(place_rows, gate_dots)
    if fast:
        spread_dots = jnp.take(spread_dots, near_rows, axis=0)
    grad_shares = lax.all_to_all(spread_dots, "rows", split_axis=0, concat_axis=0, tiled=True)
    grad_shares = grad_shares.reshape(expert_total, TOK_DEV)
    if fast:
        back_parts = reduce_chips(combine(chosen, back_rows, 0, 2), got)
        out_got = flip(combine(chosen, out_rows, 1, 2), 1)
        out_keep = combine(chosen, out_rows, 0, 2)
        grad_shares = after(grad_shares, own_slot, third, out_keep, out_got, *reduced[0][2])
    else:

        def summed(rows):
            part = combine(chosen, rows, 0, 1)
            return (lax.psum_scatter(part, "rows", scatter_dimension=0).astype(WIDE),)

        back_parts = summed(back_rows)
        mixture = summed(out_rows)

    grad_residual, grad_branch, grad_heads, experts_gain_grad, router_grad = branch_back(
        info,
        residual,
        normed_two,
        back_parts,
        cotangent,
        routes.T,
        grad_shares,
        router_rows,
        experts_scale,
        out_refs,
    )
    if fast:
        router_parts = jnp.transpose(
            router_grad.astype(LOW).reshape(col_count, router_part, row_count, depth),
            (2, 0, 1, 3),
        ).reshape(row_count * col_count, router_part, depth)
        gain_rows = experts_gain_grad.astype(LOW).reshape(row_count * col_count, 1, gain_part)
        extra = jnp.concatenate(
            [
                jnp.pad(router_parts, ((0, 0), (0, 0), (0, wide - depth))),
                jnp.pad(gain_rows, ((0, 0), (0, 0), (0, wide - gain_part))),
                jnp.zeros((row_count * col_count, EXTRA - router_part - 1, wide), LOW),
            ],
            axis=1,
        )
    grad_query, own_grad, source_grad = attention_back(
        info, queries, own_pair, partner, grad_heads, cosine, sine
    )
    arrived = lax.ppermute(source_grad.astype(LOW), "cols", [(j, i) for i, j in pairs])
    grad_pair = join_grads(info, own_grad, source_grad, arrived, cosine, sine)
    if fast:
        keep, send = weight_grads(
            info,
            [normed, heads],
            [grad_query, grad_pair, grad_branch],
            ((0, 2, query_part), (0, 3, 2 * key_part), (1, 4, query_part)),
            extra,
        )
        sent = flip(send, 1)
        grad_pair = after(grad_pair, keep)
    tokens_grad, attention_gain_grad = token_back(
        info, grad_query, grad_pair, tokens, grad_residual, attention_scale, query_refs, pair_refs
    )

    if fast:
        mixture = reduce_chips(out_keep, out_got)
        slots = sum_parts(reduce_chips(keep, sent, marks[1]))
        width = query_part + 2 * key_part
        gain_sums = sum(
            jnp.sum(own[i, :depth, :width].astype(WIDE) * slots[i, :depth, :width], axis=1)
            for i in range(4)
        )
        own_gains = lax.dynamic_slice_in_dim(attention_scale[0], row_place * depth, depth, 0)
        gain_sums = (gain_sums / own_gains).reshape(col_count, 1, gain_part)
        gain_sums = jnp.pad(
            jnp.take(gain_sums, shards, axis=0),
            ((0, 0), (depth + router_part + 1, EXTRA - router_part - 2), (0, wide - gain_part)),
        )
        slots = (slots + gain_sums).astype(LOW)

        def cols_sum(slots):
            sent_first = reduce_first(slots[1], slots[3])
            sent_second = reduce_second(slots[2], slots[3], sent_first[0])
            return reduce_last(slots[0], sent_first, sent_second)

        sums = cols_sum(slots)
        expert_sums = [reduce_last(*parts) for parts in reduced]
        router_sum = sums[depth : depth + router_part, :depth].T
        experts_gain_sum = sums[depth + router_part, :gain_part]
        attention_gain_sum = sums[depth + router_part + 1, :gain_part]
        sums = sums[:depth]
    else:
        full_grads = [
            tn(normed, grad_query),
            *jnp.moveaxis(tn(normed, grad_pair).reshape(D, QUARTERS, 2, -1), 2, 0),
            tn(heads, grad_branch),
        ]
        packed_grad = jnp.concatenate(
            [
                grad.astype(LOW).reshape(row_count, depth, col_count, -1)
                for grad in full_grads
            ],
            axis=3,
        )
        row_sums = lax.psum_scatter(packed_grad, "rows", scatter_dimension=0)
        sums = lax.psum_scatter(row_sums, "cols", scatter_dimension=1).astype(WIDE)
        expert_sums = reduced
        small_grads = jnp.concatenate(
            [
                attention_gain_grad.reshape(-1, gain_part),
                experts_gain_grad.reshape(-1, gain_part),
                jnp.transpose(
                    router_grad.reshape(col_count, router_part, row_count, depth), (2, 0, 3, 1)
                ).reshape(row_count * col_count, depth * router_part),
            ],
            axis=1,
        )
        small_grads = small_grads.reshape(row_count, -1)
        small_grads = lax.all_to_all(small_grads, "rows", split_axis=0, concat_axis=0, tiled=True)
        small_grads = jnp.sum(small_grads, axis=0).reshape(col_count, -1)
        small_grads = lax.all_to_all(small_grads, "cols", split_axis=0, concat_axis=0, tiled=True)
        small_sums = jnp.sum(small_grads, axis=0)
        attention_gain_sum = small_sums[:gain_part]
        experts_gain_sum = small_sums[gain_part : 2 * gain_part]
        router_sum = small_sums[2 * gain_part :].reshape(depth, router_part)

    layer_output = (residual + sum_parts(mixture)).astype(LOW)
    key_at = query_part
    value_at = key_at + key_part
    out_at = value_at + key_part
    part = down_weight.shape[1]
    gate_grad, upward_grad, down_grad = (
        jnp.stack([sums_of[which * part : (which + 1) * part] for sums_of in expert_sums])
        for which in range(3)
    )
    return (
        layer_output,
        tokens_grad,
        sums[:, :key_at],
        sums[:, key_at:value_at],
        sums[:, value_at:out_at],
        sums[:, out_at:],
        router_sum,
        attention_gain_sum,
        experts_gain_sum,
        jnp.swapaxes(gate_grad, 1, 2),
        jnp.swapaxes(upward_grad, 1, 2),
        down_grad,
    )


def solution(mesh):
    in_specs = (
        P(("rows", "cols"), None),
        P("rows", "cols"),
        P("rows", "cols"),
        P("rows", "cols"),
        P("rows", "cols"),
        P("rows", "cols"),
        P(("rows", "cols")),
        P(("rows", "cols")),
        P("rows", None, "cols"),
        P("rows", None, "cols"),
        P("rows", "cols", None),
        P(("rows", "cols"), None),
        P(),
        P(("rows", "cols"), None),
    )
    out_specs = (
        P(("rows", "cols"), None),
        P(("rows", "cols"), None),
        P("rows", "cols"),
        P("rows", "cols"),
        P("rows", "cols"),
        P("rows", "cols"),
        P("rows", "cols"),
        P(("rows", "cols")),
        P(("rows", "cols")),
        P("rows", None, "cols"),
        P("rows", None, "cols"),
        P("rows", "cols", None),
    )
    return jax.shard_map(
        on_device, mesh=mesh, in_specs=in_specs, out_specs=out_specs, check_vma=False
    )
```

```python
import functools

import jax
import jax.numpy as jnp
from jax import lax
from jax.experimental import pallas as pl
from jax.experimental.pallas import tpu as pltpu
from jax.sharding import PartitionSpec as P

D = 1536
HEADS = 12
KV_HEADS = 2
HEAD_DIM = 128
TOP = 4
TOK_DEV = 512
BRANCHES = 4
LEAVES = 8
TRUNK = 256
BRANCH = 64

EPSILON = 1e-06
ROPE_BASE = 10000.0
MASKED = -1e30
LOW = jnp.bfloat16
WIDE = jnp.float32
KEY_WIDTH = KV_HEADS * HEAD_DIM
GROUP = HEADS // KV_HEADS
QUARTERS = 4
VMEM_LIMIT = 56 * 1024 * 1024

ANY = pl.BlockSpec(memory_space=pl.ANY)
SMEM = pl.BlockSpec(memory_space=pltpu.SMEM)


def nn(one, two):
    return lax.dot_general(one, two, (((1,), (0,)), ((), ())), preferred_element_type=WIDE)


def nt(one, two):
    return lax.dot_general(one, two, (((1,), (1,)), ((), ())), preferred_element_type=WIDE)


def tn(one, two):
    return lax.dot_general(one, two, (((0,), (0,)), ((), ())), preferred_element_type=WIDE)


def whole(shape):
    return pl.BlockSpec(shape, lambda *_: (0,) * len(shape))


LITTLE = pl.CostEstimate(flops=1, bytes_accessed=1, transcendentals=0)


def params():
    return pltpu.CompilerParams(vmem_limit_bytes=VMEM_LIMIT)


def turn(values, cosine, sine):
    return values * cosine + pltpu.roll(values, HEAD_DIM // 2, 1) * sine


def turn_back(values, cosine, sine):
    return values * cosine - pltpu.roll(values, HEAD_DIM // 2, 1) * sine


SLOTS = range(4)
PIECES = (
    tuple((0, slot) for slot in SLOTS),
    tuple((2, slot) for slot in SLOTS),
    tuple((4, slot) for slot in SLOTS),
    ((6, 0), (6, 1)),
    ((6, 2), (6, 3)),
    tuple((1, slot) for slot in SLOTS),
    tuple((flip_bits, slot) for flip_bits in (3, 5) for slot in SLOTS),
    ((7, 0), (7, 1)),
    ((7, 2), (7, 3)),
)
EXTRA = 16


def weight_copies(info, refs, target, sem, start, width):
    if len(refs) == 1:
        return [pltpu.make_async_copy(refs[0], target, sem)]
    depth = refs[0].shape[1] - EXTRA
    copies = []
    for ref, parts in zip(refs, PIECES):
        for at, (flip_bits, slot) in enumerate(parts):
            row = pl.multiple_of((info[0] ^ flip_bits) * depth, depth)
            col = pl.multiple_of(info[2 + slot] * width, 128)
            copies.append(
                pltpu.make_async_copy(
                    ref.at[at, pl.ds(0, depth), pl.ds(start, width)],
                    target.at[pl.ds(row, depth), pl.ds(col, width)],
                    sem,
                )
            )
    return copies


def extras_kernel(info, *rest):
    refs, (out, sem) = rest[:-2], rest[-2:]
    depth = refs[0].shape[1] - EXTRA
    copies = []
    for ref, parts in zip(refs, PIECES):
        for at, (flip_bits, slot) in enumerate(parts):
            to = (info[0] ^ flip_bits) * QUARTERS + info[2 + slot]
            copies.append(pltpu.make_async_copy(ref.at[at, pl.ds(depth, EXTRA)], out.at[to], sem))
    run_all(copies)
    wait_all(copies)


def extras(info, refs):
    return pl.pallas_call(
        extras_kernel,
        out_shape=jax.ShapeDtypeStruct((8 * QUARTERS, EXTRA, refs[0].shape[2]), LOW),
        in_specs=[SMEM] + [ANY] * len(refs),
        out_specs=pl.BlockSpec(memory_space=pltpu.VMEM),
        scratch_shapes=[pltpu.SemaphoreType.DMA],
        compiler_params=params(),
        cost_estimate=LITTLE,
        name="extra_rows",
    )(info, *refs)


def run_all(copies):
    for copy in copies:
        copy.start()


def wait_all(copies):
    for copy in copies:
        copy.wait()


def key_value_kernel(info, tokens, gain, cosine, sine, *rest):
    count = len(rest) - 4
    refs, (normed, out, weight, sem) = rest[:count], rest[count:]
    copies = weight_copies(info, refs, weight, sem, D // QUARTERS, 128)
    run_all(copies)
    values = tokens[...].astype(WIDE)
    factor = lax.rsqrt(jnp.mean(values * values, axis=-1, keepdims=True) + EPSILON)
    low = (values * factor * gain[...]).astype(LOW)
    normed[...] = low
    wait_all(copies)
    both = nn(low, weight[...])
    half = HEAD_DIM // 2
    first = lax.broadcasted_iota(jnp.int32, (TOK_DEV, HEAD_DIM), 1) < half
    for g in range(KV_HEADS):
        one = both[:, 256 * g : 256 * g + 128]
        two = both[:, 256 * g + 128 : 256 * g + 256]
        key = jnp.where(first, one, pltpu.roll(two, half, 1))
        value = jnp.where(first, pltpu.roll(one, half, 1), two)
        out[:, 128 * g : 128 * g + 128] = turn(key, cosine[...], sine[...]).astype(LOW)
        out[:, KEY_WIDTH + 128 * g : KEY_WIDTH + 128 * g + 128] = value.astype(LOW)


def key_value(info, tokens, gain, cosine, sine, refs):
    return pl.pallas_call(
        key_value_kernel,
        out_shape=(
            jax.ShapeDtypeStruct((TOK_DEV, D), LOW),
            jax.ShapeDtypeStruct((TOK_DEV, 2 * KEY_WIDTH), LOW),
        ),
        in_specs=[SMEM] + [pl.BlockSpec(memory_space=pltpu.VMEM)] * 4 + [ANY] * len(refs),
        out_specs=(pl.BlockSpec(memory_space=pltpu.VMEM),) * 2,
        scratch_shapes=[pltpu.VMEM((D, 2 * KEY_WIDTH), LOW), pltpu.SemaphoreType.DMA],
        compiler_params=params(),
        cost_estimate=LITTLE,
        name="norm_key_value",
    )(info, tokens, gain, cosine, sine, *refs)


def query_kernel(info, normed, cosine, sine, *rest):
    count = len(rest) - 3
    refs, (out, weight, sem) = rest[:count], rest[count:]

    @pl.when(pl.program_id(0) == 0)
    def _():
        copies = weight_copies(info, refs, weight, sem, 0, D // QUARTERS)
        run_all(copies)
        wait_all(copies)

    at = pl.multiple_of(pl.program_id(0) * 256, 256)
    lin = nn(normed[...], weight[:, pl.ds(at, 256)])
    for h in range(2):
        out[:, 128 * h : 128 * h + 128] = turn(
            lin[:, 128 * h : 128 * h + 128], cosine[...], sine[...]
        ).astype(LOW)


def query(info, normed, cosine, sine, refs):
    return pl.pallas_call(
        query_kernel,
        grid=(D // 256,),
        out_shape=jax.ShapeDtypeStruct((TOK_DEV, D), LOW),
        in_specs=[SMEM, whole((TOK_DEV, D)), whole((TOK_DEV, 128)), whole((TOK_DEV, 128))]
        + [ANY] * len(refs),
        out_specs=pl.BlockSpec((TOK_DEV, 256), lambda i: (0, i)),
        scratch_shapes=[pltpu.VMEM((D, D), LOW), pltpu.SemaphoreType.DMA],
        compiler_params=params(),
        cost_estimate=LITTLE,
        name="query_projection",
    )(info, normed, cosine, sine, *refs)


KEYS = TRUNK + 2 * BRANCH
CHUNKS = TOK_DEV // BRANCH


def chunk_keys(info, source, own, column, chunk):
    at = pl.multiple_of(info[6 + chunk], BRANCH)
    rows = pl.multiple_of(chunk * BRANCH, BRANCH)
    columns = slice(column, column + HEAD_DIM)
    return jnp.concatenate(
        [
            source[0:TRUNK, columns],
            source[pl.ds(at, BRANCH), columns],
            own[pl.ds(rows, BRANCH), columns],
        ],
        axis=0,
    )


def chunk_allowed(info, chunk, query_axis, shape):
    query_row = lax.broadcasted_iota(jnp.int32, shape, query_axis) & (BRANCH - 1)
    key = lax.broadcasted_iota(jnp.int32, shape, 1 - query_axis)
    leaves = info[1] == 0
    trunk = jnp.logical_and(jnp.logical_not(leaves), chunk < TRUNK // BRANCH)
    limit = jnp.where(trunk, chunk * BRANCH + query_row, TRUNK - 1)
    branch_limit = jnp.where(leaves, TRUNK + BRANCH - 1, 0)
    own_limit = jnp.where(trunk, 0, query_row + TRUNK + BRANCH)
    top = jnp.where(key < TRUNK, limit, jnp.where(key < TRUNK + BRANCH, branch_limit, own_limit))
    return key <= top


def group_rows(ref, g):
    first = g * GROUP
    return jnp.concatenate(
        [ref[:, 128 * h : 128 * h + 128] for h in range(first, first + GROUP)], axis=0
    )


def keep_source(info, partner, own, source):
    @pl.when(pl.program_id(0) == 0)
    def _():
        @pl.when(info[1] == 0)
        def _():
            source[...] = partner[...]

        @pl.when(info[1] != 0)
        def _():
            source[...] = own[...]


def attention_kernel(info, queries, own, partner, out, source):
    keep_source(info, partner, own, source)
    chunk = pl.program_id(0)
    rows = GROUP * BRANCH
    allowed = chunk_allowed(info, chunk, 0, (rows, KEYS))
    for g in range(KV_HEADS):
        keys = chunk_keys(info, source, own, 128 * g, chunk)
        values = chunk_keys(info, source, own, KEY_WIDTH + 128 * g, chunk)
        scores = nt(group_rows(queries, g), keys) * HEAD_DIM**-0.5
        scores = jnp.where(allowed, scores, MASKED)
        weights = jnp.exp(scores - jnp.max(scores, axis=1, keepdims=True))
        total = jnp.sum(weights, axis=1, keepdims=True)
        mixed = nn((weights * (1.0 / total)).astype(LOW), values).astype(LOW)
        for h in range(GROUP):
            at = (g * GROUP + h) * 128
            out[:, at : at + 128] = mixed[h * BRANCH : (h + 1) * BRANCH]


def attention(info, queries, own, partner):
    return pl.pallas_call(
        attention_kernel,
        grid=(CHUNKS,),
        out_shape=jax.ShapeDtypeStruct((TOK_DEV, D), LOW),
        in_specs=[
            SMEM,
            pl.BlockSpec((BRANCH, D), lambda i: (i, 0)),
            whole((TOK_DEV, 2 * KEY_WIDTH)),
            whole((TOK_DEV, 2 * KEY_WIDTH)),
        ],
        out_specs=pl.BlockSpec((BRANCH, D), lambda i: (i, 0)),
        scratch_shapes=[pltpu.VMEM((TOK_DEV, 2 * KEY_WIDTH), LOW)],
        compiler_params=params(),
        cost_estimate=LITTLE,
        name="tree_attention",
    )(info, queries, own, partner)


def attention_back_kernel(
    info, queries, own, partner, grads, cosine, sine, grad_query, own_grad, source_grad, source
):
    keep_source(info, partner, own, source)
    chunk = pl.program_id(0)

    @pl.when(chunk == 0)
    def _():
        source_grad[...] = jnp.zeros_like(source_grad)

    rows = GROUP * BRANCH
    scale = HEAD_DIM**-0.5
    allowed = chunk_allowed(info, chunk, 1, (KEYS, rows))
    at = pl.multiple_of(info[6 + chunk], BRANCH)
    for g in range(KV_HEADS):
        keys = chunk_keys(info, source, own, 128 * g, chunk)
        values = chunk_keys(info, source, own, KEY_WIDTH + 128 * g, chunk)
        query_rows = group_rows(queries, g)
        grad_rows = group_rows(grads, g)
        scores = jnp.where(allowed, nt(keys, query_rows) * scale, MASKED)
        weights = jnp.exp(scores - jnp.max(scores, axis=0, keepdims=True))
        probs = weights * (1.0 / jnp.sum(weights, axis=0, keepdims=True))
        grad_probs = nt(values, grad_rows)
        mean = jnp.sum(probs * grad_probs, axis=0, keepdims=True)
        grad_scores = (probs * (grad_probs - mean)).astype(LOW)
        grad_values = nn(probs.astype(LOW), grad_rows)
        grad_keys = nn(grad_scores, query_rows) * scale
        grad_queries = tn(grad_scores, keys) * scale
        for h in range(GROUP):
            to = (g * GROUP + h) * 128
            grad_query[:, to : to + 128] = turn_back(
                grad_queries[h * BRANCH : (h + 1) * BRANCH], cosine[...], sine[...]
            ).astype(LOW)
        for column, grad in ((128 * g, grad_keys), (KEY_WIDTH + 128 * g, grad_values)):
            columns = slice(column, column + 128)
            source_grad[0:TRUNK, columns] += grad[0:TRUNK]
            source_grad[pl.ds(at, BRANCH), columns] += grad[TRUNK : TRUNK + BRANCH]
            own_grad[:, columns] = grad[TRUNK + BRANCH :]


def attention_back(info, queries, own, partner, grads, cosine, sine):
    chunked = pl.BlockSpec((BRANCH, D), lambda i: (i, 0))
    pair = (TOK_DEV, 2 * KEY_WIDTH)
    return pl.pallas_call(
        attention_back_kernel,
        grid=(CHUNKS,),
        out_shape=(
            jax.ShapeDtypeStruct((TOK_DEV, D), LOW),
            jax.ShapeDtypeStruct(pair, WIDE),
            jax.ShapeDtypeStruct(pair, WIDE),
        ),
        in_specs=[
            SMEM,
            chunked,
            whole(pair),
            whole(pair),
            chunked,
            pl.BlockSpec((BRANCH, 128), lambda i: (i, 0)),
            pl.BlockSpec((BRANCH, 128), lambda i: (i, 0)),
        ],
        out_specs=(
            chunked,
            pl.BlockSpec((BRANCH, 2 * KEY_WIDTH), lambda i: (i, 0)),
            whole(pair),
        ),
        scratch_shapes=[pltpu.VMEM(pair, LOW)],
        compiler_params=params(),
        cost_estimate=LITTLE,
        name="tree_attention_back",
    )(info, queries, own, partner, grads, cosine, sine)


def out_kernel(info, heads, tokens, gain, *rest):
    count = len(rest) - 4
    refs, (residual, normed, weight, sem) = rest[:count], rest[count:]

    @pl.when(pl.program_id(0) == 0)
    def _():
        copies = weight_copies(info, refs, weight, sem, D // QUARTERS + 128, D // QUARTERS)
        run_all(copies)
        wait_all(copies)

    at = pl.ds(pl.multiple_of(pl.program_id(0) * 256, 256), 256)
    residual[:, at] = tokens[:, at].astype(WIDE) + nn(heads[...], weight[:, at])

    @pl.when(pl.program_id(0) == pl.num_programs(0) - 1)
    def _():
        values = residual[...]
        factor = lax.rsqrt(jnp.mean(values * values, axis=-1, keepdims=True) + EPSILON)
        normed[...] = (values * factor * gain[...]).astype(LOW)


def out_projection(info, heads, tokens, gain, refs):
    full = (TOK_DEV, D)
    return pl.pallas_call(
        out_kernel,
        grid=(D // 256,),
        out_shape=(jax.ShapeDtypeStruct(full, WIDE), jax.ShapeDtypeStruct(full, LOW)),
        in_specs=[SMEM, whole(full), whole(full), whole((1, D))] + [ANY] * len(refs),
        out_specs=(whole(full), whole(full)),
        scratch_shapes=[pltpu.VMEM((D, D), LOW), pltpu.SemaphoreType.DMA],
        compiler_params=params(),
        cost_estimate=LITTLE,
        name="out_projection",
    )(info, heads, tokens, gain, *refs)


def hits_of(routes, ids):
    hit = ids == routes[0, 0:1]
    for k in range(1, TOP):
        hit = jnp.logical_or(hit, ids == routes[0, k : k + 1])
    return hit


def tables_kernel(capacity, local, total, order, info, routes, chosen_out, place_out, earlier):
    @pl.when(pl.program_id(0) == 0)
    def _():
        one = lax.broadcasted_iota(jnp.int32, (TOK_DEV, TOK_DEV), 0)
        two = lax.broadcasted_iota(jnp.int32, (TOK_DEV, TOK_DEV), 1)
        earlier[...] = jnp.where(one < two, 1.0, 0.0).astype(LOW)

    ids = lax.broadcasted_iota(jnp.int32, (total, TOK_DEV), 0)
    hit = hits_of(routes, ids)
    rank = nn(jnp.where(hit, 1.0, 0.0).astype(LOW), earlier[...])
    place = jnp.where(hit, rank, -1.0)
    spots = lax.broadcasted_iota(jnp.int32, (capacity, TOK_DEV), 0).astype(WIDE)
    place_out[0] = jnp.full(place_out.shape[1:], -1.0, WIDE)
    for e in range(local):
        mine = ids == info[0] * local + e
        place_row = jnp.sum(jnp.where(mine, place, 0.0), axis=0, keepdims=True)
        place_out[0, e : e + 1] = place_row
        chosen_out[0, e * capacity : (e + 1) * capacity] = jnp.where(
            spots == place_row, 1.0, 0.0
        ).astype(LOW)


def tables(order, info, routes, capacity, local, total):
    count = routes.shape[0]
    return pl.pallas_call(
        functools.partial(tables_kernel, capacity, local, total),
        grid_spec=pltpu.PrefetchScalarGridSpec(
            num_scalar_prefetch=2,
            grid=(count,),
            in_specs=[pl.BlockSpec((1, TOP, TOK_DEV), lambda i, order, info: (order[i], 0, 0))],
            out_specs=[
                pl.BlockSpec((1, local * capacity, TOK_DEV), lambda i, order, info: (i, 0, 0)),
                pl.BlockSpec((1, 8, TOK_DEV), lambda i, order, info: (i, 0, 0)),
            ],
            scratch_shapes=[pltpu.VMEM((TOK_DEV, TOK_DEV), LOW)],
        ),
        out_shape=[
            jax.ShapeDtypeStruct((count, local * capacity, TOK_DEV), LOW),
            jax.ShapeDtypeStruct((count, 8, TOK_DEV), WIDE),
        ],
        compiler_params=params(),
        cost_estimate=LITTLE,
        name="route_tables",
    )(order, info, routes)


def pick_kernel(local, order, chosen, blocks, *outs):
    rows_of = nn(chosen[0], blocks[0]).astype(LOW)
    capacity = outs[0].shape[1]
    for e in range(local):
        outs[e][0] = rows_of[e * capacity : (e + 1) * capacity]


def pick_rows(order, chosen, blocks, local):
    count, height, _ = chosen.shape
    capacity = height // local
    return pl.pallas_call(
        functools.partial(pick_kernel, local),
        grid_spec=pltpu.PrefetchScalarGridSpec(
            num_scalar_prefetch=1,
            grid=(count,),
            in_specs=[
                pl.BlockSpec((1, height, TOK_DEV), lambda i, order: (i, 0, 0)),
                pl.BlockSpec((1, TOK_DEV, D), lambda i, order: (order[i], 0, 0)),
            ],
            out_specs=[pl.BlockSpec((1, capacity, D), lambda i, order: (i, 0, 0))] * local,
        ),
        out_shape=[jax.ShapeDtypeStruct((count, capacity, D), LOW)] * local,
        compiler_params=params(),
        cost_estimate=LITTLE,
        name="pick_rows",
    )(order, chosen, blocks)


def dispatch_kernel(local, near, info, rows, chosen, routes, router, *rest):
    outs, logits = rest[2 * local : 4 * local], rest[-1]
    total = router.shape[1]
    step = pl.program_id(0)
    block = rows[...]
    rows_of = nn(chosen[0], block).astype(LOW)
    capacity = outs[0].shape[1]
    for e in range(local):
        outs[e][0] = rows_of[e * capacity : (e + 1) * capacity]
    part = nn(block, router[...])

    @pl.when(step == 0)
    def _():
        logits[...] = part

    @pl.when(step > 0)
    def _():
        logits[...] += part

    @pl.when(step == pl.num_programs(0) - 1)
    def _():
        values = logits[...].T
        ids = lax.broadcasted_iota(jnp.int32, (total, TOK_DEV), 0)
        weights = jnp.exp(values - jnp.max(values, axis=0, keepdims=True))
        hit = hits_of(routes, ids)
        share = weights / jnp.sum(jnp.where(hit, weights, 0.0), axis=0, keepdims=True)
        for e in range(local):
            mine = ids == info[0] * local + e
            share_row = jnp.sum(jnp.where(mine, share, 0.0), axis=0, keepdims=True)
            picked = chosen[0, e * capacity : (e + 1) * capacity].astype(WIDE)
            outs[local + e][0] = jnp.sum(picked * share_row, axis=1, keepdims=True)


def dispatch(at, near, info, rows, chosen, routes, router, local, earlier):
    count, height, _ = chosen.shape
    capacity = height // local
    total = router.shape[1]
    wide = 512
    out_shape = [jax.ShapeDtypeStruct((count, capacity, D), LOW)] * local + [
        jax.ShapeDtypeStruct((count, capacity, 1), WIDE)
    ] * local
    if earlier is None:
        earlier = [jnp.zeros((8, 128), shape.dtype) for shape in out_shape]
        aliases = {}
    else:
        aliases = {6 + i: i for i in range(len(out_shape))}
    return pl.pallas_call(
        functools.partial(dispatch_kernel, local),
        grid_spec=pltpu.PrefetchScalarGridSpec(
            num_scalar_prefetch=2,
            grid=(D // wide,),
            in_specs=[
                pl.BlockSpec((TOK_DEV, wide), lambda i, near, info: (0, i)),
                pl.BlockSpec((1, height, TOK_DEV), lambda i, near, info: (at, 0, 0)),
                pl.BlockSpec((1, TOP, TOK_DEV), lambda i, near, info: (near[at], 0, 0)),
                pl.BlockSpec((wide, total), lambda i, near, info: (i, 0)),
            ]
            + [ANY] * len(out_shape),
            out_specs=[
                pl.BlockSpec((1, capacity, wide), lambda i, near, info: (at, 0, i))
            ]
            * local
            + [pl.BlockSpec((1, capacity, 1), lambda i, near, info: (at, 0, 0))] * local,
            scratch_shapes=[pltpu.VMEM((TOK_DEV, total), WIDE)],
        ),
        out_shape=out_shape,
        input_output_aliases=aliases,
        compiler_params=params(),
        cost_estimate=LITTLE,
        name="dispatch",
    )(near, info, rows, chosen, routes, router, *earlier)


def spread_kernel(local, place, *rest):
    dots, out = rest[:local], rest[local]
    spots = lax.broadcasted_iota(jnp.int32, (dots[0].shape[1], TOK_DEV), 0).astype(WIDE)
    for e in range(local):
        chosen = spots == place[0, e : e + 1]
        out[0, e : e + 1] = jnp.sum(jnp.where(chosen, dots[e][0], 0.0), axis=0, keepdims=True)


def spread(place, dots):
    count, capacity, _ = dots[0].shape
    local = len(dots)
    return pl.pallas_call(
        functools.partial(spread_kernel, local),
        grid=(count,),
        out_shape=jax.ShapeDtypeStruct((count, local, TOK_DEV), WIDE),
        in_specs=[pl.BlockSpec((1, 8, TOK_DEV), lambda i: (i, 0, 0))]
        + [pl.BlockSpec((1, capacity, 1), lambda i: (i, 0, 0))] * local,
        out_specs=pl.BlockSpec((1, local, TOK_DEV), lambda i: (i, 0, 0)),
        compiler_params=params(),
        cost_estimate=LITTLE,
        name="spread",
    )(place, *dots)


def expert_kernel(slots, info, rows, grads, shares, *rest):
    count = len(rest) - 7
    refs = rest[:count]
    out_rows, back_rows, grad_rows, acts, dots, weight, sem = rest[count:]
    part = weight.shape[1] // slots

    @pl.when(pl.program_id(0) == 0)
    def _():
        def copies(ref, slot):
            return [
                pltpu.make_async_copy(
                    ref.at[pl.ds(which * part, part)],
                    weight.at[which, pl.ds(slot * part, part)],
                    sem,
                )
                for which in range(3)
            ]

        if count == slots:
            for slot in range(slots):
                run_all(copies(refs[slot], slot))
        else:
            block, second, above, below, far = refs
            low_end = info[2] == 0
            end = jnp.logical_or(low_end, info[2] == 3)
            run_all(copies(block, 0))
            run_all(copies(second, 1))

            @pl.when(low_end)
            def _():
                run_all(copies(above, 2))

            @pl.when(jnp.logical_not(low_end))
            def _():
                run_all(copies(below, 2))

            @pl.when(end)
            def _():
                run_all(copies(far, 3))

            @pl.when(jnp.logical_not(end))
            def _():
                run_all(copies(above, 3))

        for slot in range(slots):
            wait_all(copies(refs[0], slot))

    row_block = rows[...]
    share = shares[...]
    grad_float = grads[...].astype(WIDE)
    grad_low = (share * grad_float).astype(LOW)
    grad_rows[...] = grad_low
    gate_act = nt(row_block, weight[0])
    upward = nt(row_block, weight[1])
    sigmoid = 1.0 / (1.0 + jnp.exp(-gate_act))
    silu = gate_act * sigmoid
    hidden = (silu * upward).astype(LOW)
    expert_out = nn(hidden, weight[2]).astype(LOW).astype(WIDE)
    out_rows[...] = (share * expert_out).astype(LOW)
    dots[...] = jnp.sum(grad_float * expert_out, axis=1, keepdims=True)
    grad_hidden = nt(grad_low, weight[2])
    grad_gate = (grad_hidden * upward * sigmoid * (1.0 + gate_act * (1.0 - sigmoid))).astype(LOW)
    grad_up = (grad_hidden * silu).astype(LOW)
    back_rows[...] = (nn(grad_gate, weight[0]) + nn(grad_up, weight[1])).astype(LOW)
    for which, act in enumerate((grad_gate, grad_up, hidden)):
        turned = act.T
        for slot in range(slots):
            acts[slot, which * part : (which + 1) * part] = turned[
                slot * part : (slot + 1) * part
            ]


EXPERT_ROWS = 256


def expert(info, rows, grads, shares, refs, slots):
    height = rows.shape[0]
    part = refs[0].shape[0] // 3
    wide_block = pl.BlockSpec((EXPERT_ROWS, D), lambda i: (i, 0))
    thin_block = pl.BlockSpec((EXPERT_ROWS, 1), lambda i: (i, 0))
    return pl.pallas_call(
        functools.partial(expert_kernel, slots),
        grid=(height // EXPERT_ROWS,),
        out_shape=[jax.ShapeDtypeStruct((height, D), LOW)] * 3
        + [
            jax.ShapeDtypeStruct((slots, 3 * part, height), LOW),
            jax.ShapeDtypeStruct((height, 1), WIDE),
        ],
        in_specs=[SMEM, wide_block, wide_block, thin_block] + [ANY] * len(refs),
        out_specs=[wide_block] * 3
        + [pl.BlockSpec((slots, 3 * part, EXPERT_ROWS), lambda i: (0, 0, i)), thin_block],
        scratch_shapes=[pltpu.VMEM((3, slots * part, D), LOW), pltpu.SemaphoreType.DMA],
        compiler_params=params(),
        cost_estimate=LITTLE,
        name="expert",
    )(info, rows, grads, shares, *refs)


def expert_grads_kernel(slots, rows, grads, *rest):
    acts, outs = rest[: len(slots)], rest[len(slots) :]
    part = acts[0].shape[1] // 3
    for act, out in zip(acts, outs):
        out[: 2 * part, :] = nn(act[0, : 2 * part], rows[...]).astype(LOW)
        out[2 * part :, :] = nn(act[0, 2 * part :], grads[...]).astype(LOW)


def expert_grads(acts, rows, grads, slots):
    _, part, height = acts.shape
    return pl.pallas_call(
        functools.partial(expert_grads_kernel, slots),
        grid=(D // 256,),
        out_shape=[jax.ShapeDtypeStruct((part, D), LOW) for _ in slots],
        in_specs=[pl.BlockSpec((height, 256), lambda i: (0, i))] * 2
        + [pl.BlockSpec((1, part, height), lambda i, s=slot: (s, 0, 0)) for slot in slots],
        out_specs=[pl.BlockSpec((part, 256), lambda i: (0, i)) for _ in slots],
        compiler_params=params(),
        cost_estimate=LITTLE,
        name="expert_gradients",
    )(rows, grads, *[acts] * len(slots))


def combine_kernel(local, chosen, *rest):
    rows, out = rest[:local], rest[local]
    both = jnp.concatenate([ref[0] for ref in rows], axis=0)
    out[0] = tn(chosen[0], both).astype(LOW)


def combine(chosen, rows, first, step):
    count, capacity, _ = rows[0].shape
    number = (count - first + step - 1) // step
    return pl.pallas_call(
        functools.partial(combine_kernel, len(rows)),
        grid=(number,),
        out_shape=jax.ShapeDtypeStruct((number, TOK_DEV, D), LOW),
        in_specs=[
            pl.BlockSpec((1,) + chosen.shape[1:], lambda i: (first + step * i, 0, 0))
        ]
        + [pl.BlockSpec((1, capacity, D), lambda i: (first + step * i, 0, 0))] * len(rows),
        out_specs=pl.BlockSpec((1, TOK_DEV, D), lambda i: (i, 0, 0)),
        compiler_params=params(),
        cost_estimate=LITTLE,
        name="combine",
    )(chosen, *rows)


def split(values):
    high = values.astype(LOW)
    return high, (values - high.astype(WIDE)).astype(LOW)


def norm_back(values, gain, grad):
    factor = lax.rsqrt(jnp.mean(values * values, axis=-1, keepdims=True) + EPSILON)
    scaled = gain * grad
    mean = jnp.mean(values * scaled, axis=-1, keepdims=True)
    grad_values = factor * scaled - values * (factor * factor * factor * mean)
    grad_gain = jnp.sum(grad * values * factor, axis=0, keepdims=True)
    return grad_values, grad_gain


def router_back(logits, routes, grad_shares):
    ids = lax.broadcasted_iota(jnp.int32, logits.shape, 0)
    hit = ids == routes[0:1]
    for k in range(1, TOP):
        hit = jnp.logical_or(hit, ids == routes[k : k + 1])
    weights = jnp.exp(logits - jnp.max(logits, axis=0, keepdims=True))
    probs = weights / jnp.sum(weights, axis=0, keepdims=True)
    chosen = jnp.sum(jnp.where(hit, probs, 0.0), axis=0, keepdims=True)
    grads = jnp.where(hit, grad_shares, 0.0)
    mean = jnp.sum(probs * grads, axis=0, keepdims=True) / chosen
    grad_probs = jnp.where(hit, (grads - mean) / chosen, 0.0)
    return probs * (grad_probs - jnp.sum(probs * grad_probs, axis=0, keepdims=True))


def branch_back_kernel(
    parts, info, residual, normed, cotangent, routes, grad_shares, router, gain, *rest
):
    sums, rest = rest[:parts], rest[parts:]
    count = len(rest) - 7
    refs = rest[:count]
    grad_residual, grad_branch, grad_heads, grad_gain, grad_router, weight, sem = rest[count:]

    @pl.when(pl.program_id(0) == 0)
    def _():
        copies = weight_copies(info, refs, weight, sem, D // QUARTERS + 128, D // QUARTERS)
        run_all(copies)
        logits = nt(router[...], normed[...])
        high, low = split(router_back(logits, routes[...], grad_shares[...]))
        grad_router[...] = nn(high, normed[...]) + nn(low, normed[...])
        grad_normed = tn(high, router[...]) + tn(low, router[...])
        if parts == 1:
            grad_normed += sums[0][...]
        else:
            values = [ref[...].astype(WIDE) for ref in sums]
            grad_normed += jnp.concatenate(
                [values[0] + values[1] + values[2], values[3] + values[4] + values[5]], axis=0
            )
        grad_values, gain_grad = norm_back(residual[...], gain[...], grad_normed)
        grad_gain[...] = gain_grad
        total = cotangent[...].astype(WIDE) + grad_values
        grad_residual[...] = total
        grad_branch[...] = total.astype(LOW)
        wait_all(copies)

    at = pl.ds(pl.multiple_of(pl.program_id(0) * 256, 256), 256)
    grad_heads[...] = nt(grad_branch[...], weight[at, :]).astype(LOW)


def branch_back(info, residual, normed, sums, cotangent, routes, grad_shares, router, gain, refs):
    full = (TOK_DEV, D)
    total = router.shape[0]
    return pl.pallas_call(
        functools.partial(branch_back_kernel, len(sums)),
        grid=(D // 256,),
        out_shape=(
            jax.ShapeDtypeStruct(full, WIDE),
            jax.ShapeDtypeStruct(full, LOW),
            jax.ShapeDtypeStruct(full, LOW),
            jax.ShapeDtypeStruct((1, D), WIDE),
            jax.ShapeDtypeStruct((total, D), WIDE),
        ),
        in_specs=[SMEM]
        + [whole(full)] * 3
        + [whole((TOP, TOK_DEV)), whole((total, TOK_DEV)), whole((total, D)), whole((1, D))]
        + [whole(part.shape) for part in sums]
        + [ANY] * len(refs),
        out_specs=(
            whole(full),
            whole(full),
            pl.BlockSpec((TOK_DEV, 256), lambda i: (0, i)),
            whole((1, D)),
            whole((total, D)),
        ),
        scratch_shapes=[pltpu.VMEM((D, D), LOW), pltpu.SemaphoreType.DMA],
        compiler_params=params(),
        cost_estimate=LITTLE,
        name="experts_norm_back",
    )(info, residual, normed, cotangent, routes, grad_shares, router, gain, *sums, *refs)


def join_grads_kernel(info, own_grad, source_grad, arrived, cosine, sine, out):
    half = HEAD_DIM // 2
    first = lax.broadcasted_iota(jnp.int32, (TOK_DEV, HEAD_DIM), 1) < half
    leaves = info[1] == 0

    def total(column):
        columns = slice(column, column + 128)
        extra = source_grad[:, columns] + arrived[:, columns].astype(WIDE)
        return own_grad[:, columns] + jnp.where(leaves, 0.0, extra)

    for g in range(KV_HEADS):
        key = turn_back(total(128 * g), cosine[...], sine[...])
        value = total(KEY_WIDTH + 128 * g)
        out[:, 256 * g : 256 * g + 128] = jnp.where(
            first, key, pltpu.roll(value, half, 1)
        ).astype(LOW)
        out[:, 256 * g + 128 : 256 * g + 256] = jnp.where(
            first, pltpu.roll(key, half, 1), value
        ).astype(LOW)


def join_grads(info, own_grad, source_grad, arrived, cosine, sine):
    vmem = pl.BlockSpec(memory_space=pltpu.VMEM)
    return pl.pallas_call(
        join_grads_kernel,
        out_shape=jax.ShapeDtypeStruct((TOK_DEV, 2 * KEY_WIDTH), LOW),
        in_specs=[SMEM] + [vmem] * 5,
        out_specs=vmem,
        compiler_params=params(),
        cost_estimate=LITTLE,
        name="join_key_value_gradients",
    )(info, own_grad, source_grad, arrived, cosine, sine)


def token_back_kernel(info, grad_query, grad_pair, tokens, grad_residual, gain, *rest):
    count = (len(rest) - 6) // 2
    query_refs, pair_refs = rest[:count], rest[count : 2 * count]
    out, grad_gain, query_weight, pair_weight, grad_normed, sem = rest[2 * count :]

    @pl.when(pl.program_id(0) == 0)
    def _():
        copies = weight_copies(info, query_refs, query_weight, sem, 0, D // QUARTERS)
        copies += weight_copies(info, pair_refs, pair_weight, sem, D // QUARTERS, 128)
        run_all(copies)
        wait_all(copies)

    at = pl.ds(pl.multiple_of(pl.program_id(0) * 256, 256), 256)
    grad_normed[:, at] = nt(grad_query[...], query_weight[at, :]) + nt(
        grad_pair[...], pair_weight[at, :]
    )

    @pl.when(pl.program_id(0) == pl.num_programs(0) - 1)
    def _():
        grad_values, gain_grad = norm_back(
            tokens[...].astype(WIDE), gain[...], grad_normed[...]
        )
        grad_gain[...] = gain_grad
        out[...] = (grad_residual[...] + grad_values).astype(LOW)


def token_back(info, grad_query, grad_pair, tokens, grad_residual, gain, query_refs, pair_refs):
    full = (TOK_DEV, D)
    return pl.pallas_call(
        token_back_kernel,
        grid=(D // 256,),
        out_shape=(jax.ShapeDtypeStruct(full, LOW), jax.ShapeDtypeStruct((1, D), WIDE)),
        in_specs=[
            SMEM,
            whole(full),
            whole((TOK_DEV, 2 * KEY_WIDTH)),
            whole(full),
            whole(full),
            whole((1, D)),
        ]
        + [ANY] * (len(query_refs) + len(pair_refs)),
        out_specs=(whole(full), whole((1, D))),
        scratch_shapes=[
            pltpu.VMEM((D, D), LOW),
            pltpu.VMEM((D, 2 * KEY_WIDTH), LOW),
            pltpu.VMEM(full, WIDE),
            pltpu.SemaphoreType.DMA,
        ],
        compiler_params=params(),
        cost_estimate=LITTLE,
        name="token_gradient",
    )(info, grad_query, grad_pair, tokens, grad_residual, gain, *query_refs, *pair_refs)


def weight_grads_kernel(parts, info, *rest):
    ins, (keep, send) = rest[:-2], rest[-2:]
    depth = D // 8
    core = info[0] & 1
    chip = pl.program_id(0) ^ (info[0] >> 1)
    start = 0
    for strip_at, grads_at, width in parts:
        low = tn(ins[strip_at][...], ins[grads_at][...]).astype(LOW)
        columns = slice(start, start + width)
        start += width
        for slot in range(QUARTERS):
            for j in range(QUARTERS):

                @pl.when(info[2 + slot] == j)
                def _():
                    piece = low[:, j * width : (j + 1) * width]
                    upper, lower = piece[:depth], piece[depth:]
                    keep[0, slot, :depth, columns] = jnp.where(core == 0, upper, lower)
                    send[0, slot, :depth, columns] = jnp.where(core == 0, lower, upper)

    if keep.shape[2] > depth:
        extra = ins[-1]
        for slot in range(QUARTERS):
            to = info[2 + slot]
            keep[0, slot, depth:] = extra[(chip * 2 + core) * QUARTERS + to]
            send[0, slot, depth:] = extra[(chip * 2 + 1 - core) * QUARTERS + to]


def weight_grads(info, strips, grads, parts, extra):
    depth = D // 8
    width = sum(part[2] for part in parts)
    strip = pl.BlockSpec((TOK_DEV, 2 * depth), lambda i, info: (0, i ^ (info[0] >> 1)))
    more = [] if extra is None else [extra]
    shape = (4, QUARTERS, depth + EXTRA * len(more), width)
    out = pl.BlockSpec((1,) + shape[1:], lambda i, info: (i, 0, 0, 0))
    return pl.pallas_call(
        functools.partial(weight_grads_kernel, parts),
        grid_spec=pltpu.PrefetchScalarGridSpec(
            num_scalar_prefetch=1,
            grid=(4,),
            in_specs=[strip] * len(strips)
            + [
                pl.BlockSpec(a.shape, lambda i, info, n=a.ndim: (0,) * n)
                for a in (*grads, *more)
            ],
            out_specs=(out, out),
        ),
        out_shape=(jax.ShapeDtypeStruct(shape, LOW),) * 2,
        compiler_params=params(),
        cost_estimate=LITTLE,
        name="weight_gradients",
    )(info, *strips, *grads, *more)


def position_of(token_index):
    branch_place = TRUNK + (token_index - TRUNK) % BRANCH
    leaf_place = TRUNK + BRANCH + (token_index - TOK_DEV) % BRANCH
    return jnp.where(
        token_index < TRUNK, token_index, jnp.where(token_index < TOK_DEV, branch_place, leaf_place)
    )


def rotary_tables(positions):
    half_dim = HEAD_DIM // 2
    frequency = ROPE_BASE ** (-jnp.arange(half_dim, dtype=jnp.float32) / half_dim)
    angles = positions.astype(jnp.float32)[:, None] * frequency[None, :]
    cosine, sine = (jnp.cos(angles), jnp.sin(angles))
    return (
        jnp.concatenate([cosine, cosine], axis=1),
        jnp.concatenate([-sine, sine], axis=1),
    )


def after(values, *earlier):
    return lax.optimization_barrier((values, earlier))[0]


def fast_mesh():
    return lax.axis_size("rows") == 8 and lax.axis_size("cols") == 4


SLOT_SHARD = ((0, 2, 1, 3), (1, 3, 0, 2), (2, 0, 1, 3), (3, 1, 2, 0))
UP = [(0, 1), (1, 2), (2, 3)]
DOWN = [(1, 0), (2, 1), (3, 2)]
FAR = [(0, 3), (3, 0)]


def send_near(block):
    return lax.ppermute(block, "cols", DOWN), lax.ppermute(block, "cols", UP)


def send_far(block):
    return lax.ppermute(block, "cols", FAR)


def send_second(block, near):
    place = lax.axis_index("cols")
    above, below = near
    payload = jnp.where(place == 1, above, jnp.where(place == 2, below, block))
    return lax.ppermute(payload, "cols", [(3, 1), (1, 0), (0, 2), (2, 3)])


def slot_list(block, near, second, far):
    place = lax.axis_index("cols")
    above, below = near
    end = (place == 0) | (place == 3)
    return [
        block,
        second,
        jnp.where(place == 0, above, below),
        jnp.where(end, far, above),
    ]


def reduce_first(second, fourth, chain=False):
    relay = lax.ppermute(second, "cols", [(1, 3), (0, 1), (2, 0), (3, 2)])
    return relay, lax.ppermute(after(fourth, relay) if chain else fourth, "cols", FAR)


def reduce_second(third, fourth, relay):
    place = lax.axis_index("cols")
    relayed = relay.astype(WIDE)
    upward_load = (
        jnp.where(place == 0, third, fourth).astype(WIDE) + jnp.where(place == 1, relayed, 0.0)
    ).astype(LOW)
    downward_load = (third.astype(WIDE) + jnp.where(place == 2, relayed, 0.0)).astype(LOW)
    return (
        lax.ppermute(upward_load, "cols", UP),
        lax.ppermute(downward_load, "cols", DOWN),
    )


def reduce_last(own, first, second):
    place = lax.axis_index("cols")
    relay, far = first
    below, above = second
    end = (place == 0) | (place == 3)
    return (
        own.astype(WIDE)
        + below.astype(WIDE)
        + above.astype(WIDE)
        + jnp.where(end, relay.astype(WIDE) + far.astype(WIDE), 0.0)
    )


def flip(block, bit):
    count = lax.axis_size("rows")
    return lax.ppermute(block, "rows", [(i, i ^ bit) for i in range(count)])


def add_low(one, two):
    return (one.astype(WIDE) + two.astype(WIDE)).astype(LOW)


def reduce_chips(keep, got):
    half = keep.shape[1] // 2

    def sums(chips, part):
        return jnp.stack([add_low(keep[i][part], got[i][part]) for i in chips])

    one, two = slice(0, half), slice(half, None)
    got_x = flip(sums((1, 3), one), 2)
    got_y = flip(sums((2, 3), two), 4)
    near_x = sums((0, 2), one)
    near_y = sums((0, 1), two)
    got_xy = flip(add_low(near_x[1], got_x[1]), 4)
    got_yx = flip(add_low(near_y[1], got_y[1]), 2)
    return (near_x[0], got_x[0], got_xy, near_y[0], got_y[0], got_yx)


def sum_parts(parts):
    wide = [a.astype(WIDE) for a in parts]
    if len(wide) == 1:
        return wide[0]
    return jnp.concatenate([wide[0] + wide[1] + wide[2], wide[3] + wide[4] + wide[5]], axis=0)


def on_device(
    tokens,
    query_weight,
    key_weight,
    value_weight,
    out_weight,
    router_weight,
    attention_gain,
    experts_gain,
    gate_weight,
    upward_weight,
    down_weight,
    routes,
    leaf_parent,
    cotangent,
):
    row_count = lax.axis_size("rows")
    col_count = lax.axis_size("cols")
    row_place = lax.axis_index("rows")
    col_place = lax.axis_index("cols")
    fast = fast_mesh()
    parity = lax.rem(col_place, 2)
    tree_id = lax.div(row_place * col_count + col_place, 2)
    parent_row = lax.dynamic_slice_in_dim(leaf_parent, tree_id, 1, 0)[0]
    depth, query_part = query_weight.shape
    key_part = key_weight.shape[1]
    router_part = router_weight.shape[1]
    gain_part = attention_gain.shape[0]
    expert_total = router_part * col_count
    local_experts = gate_weight.shape[0]
    capacity = TOK_DEV * TOP // expert_total * 5 // 4

    shards = (
        jnp.asarray(SLOT_SHARD, jnp.int32)[col_place]
        if fast
        else jnp.arange(4, dtype=jnp.int32)
    )
    branch_rows = jnp.where(parity == 0, TRUNK + BRANCH * parent_row, TRUNK)
    info = jnp.concatenate(
        [jnp.stack([row_place, parity]), shards, branch_rows, jnp.zeros((2,), jnp.int32)]
    ).astype(jnp.int32)

    packed = jnp.concatenate([query_weight, key_weight, value_weight, out_weight], axis=1)
    local_index = (1 - parity) * TOK_DEV + jnp.arange(TOK_DEV, dtype=jnp.int32)
    cosine, sine = rotary_tables(position_of(local_index))
    shard_blocks = [
        jnp.concatenate(
            [gate_weight[expert].T, upward_weight[expert].T, down_weight[expert]], axis=0
        )
        for expert in range(local_experts)
    ]
    nears, seconds, fars = ([], [], [])
    if fast:
        wide = packed.shape[1]
        gains = jnp.concatenate([attention_gain, experts_gain])[None, :]
        packed = jnp.concatenate(
            [
                packed,
                jnp.pad(router_weight.T, ((0, 0), (0, wide - depth))),
                jnp.pad(gains, ((0, 0), (0, wide - 2 * gain_part))),
                jnp.pad(routes.T.astype(LOW), ((0, 0), (0, wide - TOK_DEV))),
                jnp.zeros((EXTRA - router_part - 1 - TOP, wide), LOW),
            ],
            axis=0,
        )
        packed_near = send_near(packed)
        packed_far = send_far(packed)
        packed_second = send_second(packed, packed_near)
        own = jnp.stack(slot_list(packed, packed_near, packed_second, packed_far))

        def gather_expert(*earlier):
            expert_at = len(nears)
            block = after(shard_blocks[expert_at], *earlier)
            shard_blocks[expert_at] = block
            nears.append(send_near(block))
            seconds.append(send_second(block, nears[expert_at]))

        gather_expert(*packed_near)
        own = after(own, info, cosine, sine)
        beside, across = flip(own, 2), flip(own, 4)
        own_in = flip(own, 1)
        beside, across = after((beside, across), own_in, *nears[0])
        corner = [flip(beside[:2], 4), flip(across[2:], 2)]
        pair_in = flip(jnp.concatenate([beside, across], axis=0), 1)
        corner_in = [flip(piece, 1) for piece in corner]
        pieces = [own, beside, across, *corner, own_in, pair_in, *corner_in]
        query_refs = pair_refs = out_refs = pieces
        extra_rows = extras(info, pieces)
        router_all = extra_rows[:, :router_part, :depth]
        attention_scale = extra_rows[:, router_part, :gain_part]
        experts_scale = extra_rows[:, router_part, gain_part : 2 * gain_part]
        routes_all = lax.dynamic_index_in_dim(
            extra_rows.reshape(row_count, col_count, EXTRA, -1), col_place, 1, keepdims=False
        )
        routes_all = routes_all[:, router_part + 1 : router_part + 1 + TOP, :TOK_DEV]
        routes_all = routes_all.astype(jnp.int32)
    else:
        packed_all = lax.all_gather(lax.all_gather(packed, "cols", axis=0), "rows", axis=0)

        def unpack(start, width):
            part = packed_all[..., start : start + width]
            return jnp.swapaxes(part, 1, 2).reshape(row_count * depth, col_count * width)

        key_at = query_part
        query_refs = [unpack(0, query_part)]
        pair_refs = [
            jnp.concatenate(
                [
                    unpack(key_at, key_part).reshape(D, QUARTERS, -1),
                    unpack(key_at + key_part, key_part).reshape(D, QUARTERS, -1),
                ],
                axis=2,
            ).reshape(D, -1)
        ]
        out_refs = [unpack(key_at + 2 * key_part, query_part)]
        routes_all = lax.all_gather(routes.T, "rows", axis=0)
        axes = ("rows", "cols")
        router_all = jnp.swapaxes(lax.all_gather(router_weight, axes, axis=0), 1, 2)
        attention_scale = lax.all_gather(attention_gain, axes, axis=0)
        experts_scale = lax.all_gather(experts_gain, axes, axis=0)
        expert_refs = [
            [lax.all_gather(block, "cols", axis=0)[i] for i in range(col_count)]
            for block in shard_blocks
        ]

    attention_scale = attention_scale.reshape(1, D).astype(WIDE)
    experts_scale = experts_scale.reshape(1, D).astype(WIDE)
    router_rows = jnp.transpose(
        router_all.reshape(row_count, col_count, router_part, depth), (1, 2, 0, 3)
    ).reshape(expert_total, D)
    router_cols = router_rows.T
    if fast:
        near_rows = row_place ^ jnp.arange(row_count, dtype=jnp.int32)
    else:
        near_rows = jnp.arange(row_count, dtype=jnp.int32)
    chosen, place_rows = tables(
        near_rows, info, routes_all, capacity, local_experts, expert_total
    )
    grad_in = after(cotangent, *pieces) if fast else cotangent
    grad_all = lax.all_gather(grad_in, "rows", axis=0)

    normed, own_pair = key_value(info, tokens, attention_scale, cosine, sine, pair_refs)
    pairs = [(i + 1, i) for i in range(0, col_count, 2)]
    partner = lax.ppermute(own_pair, "cols", pairs)
    queries = query(info, normed, cosine, sine, query_refs)
    if fast:
        queries = after(queries, seconds[0])
        fars.append(send_far(after(shard_blocks[0], seconds[0], queries)))
    heads = attention(info, queries, own_pair, partner)
    residual, normed_two = out_projection(info, heads, tokens, experts_scale, out_refs)

    if fast:
        beside, across = flip(normed_two, 2), flip(normed_two, 4)
        beside_in = flip(normed_two, 1)
        gather_expert(fars[0], normed_two)
        grad_all = after(grad_all, normed_two)
    else:
        rows_all = lax.all_gather(normed_two, "rows", axis=0)
    grad_rows = pick_rows(near_rows, chosen, grad_all, local_experts)

    def place_block(q, block, picked):
        return dispatch(
            q, near_rows, info, block, chosen, routes_all, router_cols, local_experts, picked
        )

    if fast:
        half = TOK_DEV // 2
        picked = place_block(0, normed_two, None)
        picked = place_block(1, beside_in, picked)
        beside, across = after((beside, across), picked, grad_rows, *nears[1])
        corner = [flip(beside[:half], 4), flip(across[half:], 2)]
        picked = place_block(2, beside, picked)
        picked = place_block(4, across, picked)
        beside_in = flip(beside, 1)
        across_in = flip(after(across, beside_in), 1)
        picked = place_block(3, beside_in, picked)
        picked = place_block(5, across_in, picked)
        corner = jnp.concatenate(after(corner, picked), axis=0)
        corner_in = flip(corner, 1)
        picked = place_block(6, corner, picked)
        picked = place_block(7, corner_in, picked)
        fars.append(send_far(after(shard_blocks[1], seconds[1], picked)))
        expert_refs = [
            [shard_blocks[i], seconds[i], *nears[i], fars[i]] for i in range(local_experts)
        ]
    else:
        picked = None
        for q in range(row_count):
            picked = place_block(q, rows_all[q], picked)
    height = row_count * capacity
    token_rows = [a.reshape(height, D) for a in picked[:local_experts]]
    grad_rows = [a.reshape(height, D) for a in grad_rows]
    share_rows = [a.reshape(height, 1) for a in picked[local_experts:]]

    out_rows, back_rows, gate_dots, reduced, marks = ([], [], [], [], [])
    for e in range(local_experts):
        rows_in = token_rows[e]
        if fast and e == 0:
            rows_in = after(rows_in, seconds[1])
        if fast and e == 1:
            rows_in = after(rows_in, fars[1], second, fourth, own_slot, third)
        out_row, back_row, grad_row, acts, dots = expert(
            info, rows_in, grad_rows[e], share_rows[e], expert_refs[e], col_count
        )
        out_rows.append(out_row.reshape(row_count, capacity, D))
        back_rows.append(back_row.reshape(row_count, capacity, D))
        gate_dots.append(dots.reshape(row_count, capacity, 1))
        if fast:
            if e == 1:
                back_rows = after(back_rows, marks[0][0])
                got = flip(combine(chosen, back_rows, 1, 2), 1)
                acts = after(acts, got)
            second, fourth = expert_grads(acts, token_rows[e], grad_row, (1, 3))
            if e == 1:
                second_out, fourth_out = after(
                    (second, fourth), marks[0][1], *reduced[0][2]
                )
            else:
                second_out, fourth_out = second, fourth
            sent_first = reduce_first(second_out, fourth_out, chain=True)
            marks.append(sent_first)
            own_slot, third = expert_grads(acts, token_rows[e], grad_row, (0, 2))
            sent_second = reduce_second(third, fourth, sent_first[0])
            reduced.append((own_slot, sent_first, sent_second))
        else:
            slots = expert_grads(acts, token_rows[e], grad_row, tuple(range(col_count)))
            reduced.append(
                lax.psum_scatter(jnp.stack(slots), "cols", scatter_dimension=0).astype(WIDE)
            )

    spread_dots = spread(place_rows, gate_dots)
    if fast:
        spread_dots = jnp.take(spread_dots, near_rows, axis=0)
    grad_shares = lax.all_to_all(spread_dots, "rows", split_axis=0, concat_axis=0, tiled=True)
    grad_shares = grad_shares.reshape(expert_total, TOK_DEV)
    if fast:
        back_keep = combine(chosen, back_rows, 0, 2)
        back_parts = reduce_chips(back_keep, got)
        out_rows = [after(a, back_keep) for a in out_rows]
        out_got = flip(combine(chosen, out_rows, 1, 2), 1)
        out_keep = combine(chosen, out_rows, 0, 2)
        grad_shares = after(
            grad_shares, own_slot, third, out_keep, out_got, marks[0][1], *reduced[0][2]
        )
    else:

        def summed(rows):
            part = combine(chosen, rows, 0, 1)
            return (lax.psum_scatter(part, "rows", scatter_dimension=0).astype(WIDE),)

        back_parts = summed(back_rows)
        mixture = summed(out_rows)

    grad_residual, grad_branch, grad_heads, experts_gain_grad, router_grad = branch_back(
        info,
        residual,
        normed_two,
        back_parts,
        cotangent,
        routes.T,
        grad_shares,
        router_rows,
        experts_scale,
        out_refs,
    )
    if fast:
        router_parts = jnp.transpose(
            router_grad.astype(LOW).reshape(col_count, router_part, row_count, depth),
            (2, 0, 1, 3),
        ).reshape(row_count * col_count, router_part, depth)
        gain_rows = experts_gain_grad.astype(LOW).reshape(row_count * col_count, 1, gain_part)
        extra = jnp.concatenate(
            [
                jnp.pad(router_parts, ((0, 0), (0, 0), (0, wide - depth))),
                jnp.pad(gain_rows, ((0, 0), (0, 0), (0, wide - gain_part))),
                jnp.zeros((row_count * col_count, EXTRA - router_part - 1, wide), LOW),
            ],
            axis=1,
        )
    grad_query, own_grad, source_grad = attention_back(
        info, queries, own_pair, partner, grad_heads, cosine, sine
    )
    arrived = lax.ppermute(source_grad.astype(LOW), "cols", [(j, i) for i, j in pairs])
    grad_pair = join_grads(info, own_grad, source_grad, arrived, cosine, sine)
    if fast:
        grad_branch = after(grad_branch, marks[1][0])
        keep, send = weight_grads(
            info,
            [normed, heads],
            [grad_query, grad_pair, grad_branch],
            ((0, 2, query_part), (0, 3, 2 * key_part), (1, 4, query_part)),
            extra,
        )
        sent = flip(send, 1)
        grad_pair = after(grad_pair, keep)
    tokens_grad, attention_gain_grad = token_back(
        info, grad_query, grad_pair, tokens, grad_residual, attention_scale, query_refs, pair_refs
    )

    if fast:
        mixture = reduce_chips(out_keep, out_got)
        slots = sum_parts(reduce_chips(keep, sent))
        width = query_part + 2 * key_part
        gain_sums = sum(
            jnp.sum(own[i, :depth, :width].astype(WIDE) * slots[i, :depth, :width], axis=1)
            for i in range(4)
        )
        own_gains = lax.dynamic_slice_in_dim(attention_scale[0], row_place * depth, depth, 0)
        gain_sums = (gain_sums / own_gains).reshape(col_count, 1, gain_part)
        gain_sums = jnp.pad(
            jnp.take(gain_sums, shards, axis=0),
            ((0, 0), (depth + router_part + 1, EXTRA - router_part - 2), (0, wide - gain_part)),
        )
        slots = (slots + gain_sums).astype(LOW)

        def cols_sum(slots):
            sent_first = reduce_first(slots[1], slots[3])
            sent_second = reduce_second(slots[2], slots[3], sent_first[0])
            return reduce_last(slots[0], sent_first, sent_second)

        sums = cols_sum(slots)
        expert_sums = [reduce_last(*parts) for parts in reduced]
        router_sum = sums[depth : depth + router_part, :depth].T
        experts_gain_sum = sums[depth + router_part, :gain_part]
        attention_gain_sum = sums[depth + router_part + 1, :gain_part]
        sums = sums[:depth]
    else:
        full_grads = [
            tn(normed, grad_query),
            *jnp.moveaxis(tn(normed, grad_pair).reshape(D, QUARTERS, 2, -1), 2, 0),
            tn(heads, grad_branch),
        ]
        packed_grad = jnp.concatenate(
            [
                grad.astype(LOW).reshape(row_count, depth, col_count, -1)
                for grad in full_grads
            ],
            axis=3,
        )
        row_sums = lax.psum_scatter(packed_grad, "rows", scatter_dimension=0)
        sums = lax.psum_scatter(row_sums, "cols", scatter_dimension=1).astype(WIDE)
        expert_sums = reduced
        small_grads = jnp.concatenate(
            [
                attention_gain_grad.reshape(-1, gain_part),
                experts_gain_grad.reshape(-1, gain_part),
                jnp.transpose(
                    router_grad.reshape(col_count, router_part, row_count, depth), (2, 0, 3, 1)
                ).reshape(row_count * col_count, depth * router_part),
            ],
            axis=1,
        )
        small_grads = small_grads.reshape(row_count, -1)
        small_grads = lax.all_to_all(small_grads, "rows", split_axis=0, concat_axis=0, tiled=True)
        small_grads = jnp.sum(small_grads, axis=0).reshape(col_count, -1)
        small_grads = lax.all_to_all(small_grads, "cols", split_axis=0, concat_axis=0, tiled=True)
        small_sums = jnp.sum(small_grads, axis=0)
        attention_gain_sum = small_sums[:gain_part]
        experts_gain_sum = small_sums[gain_part : 2 * gain_part]
        router_sum = small_sums[2 * gain_part :].reshape(depth, router_part)

    layer_output = (residual + sum_parts(mixture)).astype(LOW)
    key_at = query_part
    value_at = key_at + key_part
    out_at = value_at + key_part
    part = down_weight.shape[1]
    gate_grad, upward_grad, down_grad = (
        jnp.stack([sums_of[which * part : (which + 1) * part] for sums_of in expert_sums])
        for which in range(3)
    )
    return (
        layer_output,
        tokens_grad,
        sums[:, :key_at],
        sums[:, key_at:value_at],
        sums[:, value_at:out_at],
        sums[:, out_at:],
        router_sum,
        attention_gain_sum,
        experts_gain_sum,
        jnp.swapaxes(gate_grad, 1, 2),
        jnp.swapaxes(upward_grad, 1, 2),
        down_grad,
    )


def solution(mesh):
    in_specs = (
        P(("rows", "cols"), None),
        P("rows", "cols"),
        P("rows", "cols"),
        P("rows", "cols"),
        P("rows", "cols"),
        P("rows", "cols"),
        P(("rows", "cols")),
        P(("rows", "cols")),
        P("rows", None, "cols"),
        P("rows", None, "cols"),
        P("rows", "cols", None),
        P(("rows", "cols"), None),
        P(),
        P(("rows", "cols"), None),
    )
    out_specs = (
        P(("rows", "cols"), None),
        P(("rows", "cols"), None),
        P("rows", "cols"),
        P("rows", "cols"),
        P("rows", "cols"),
        P("rows", "cols"),
        P("rows", "cols"),
        P(("rows", "cols")),
        P(("rows", "cols")),
        P("rows", None, "cols"),
        P("rows", None, "cols"),
        P("rows", "cols", None),
    )
    return jax.shard_map(
        on_device, mesh=mesh, in_specs=in_specs, out_specs=out_specs, check_vma=False
    )
```

```python
import functools

import jax
import jax.numpy as jnp
from jax import lax
from jax.experimental import pallas as pl
from jax.experimental.pallas import tpu as pltpu
from jax.sharding import PartitionSpec as P

D = 1536
HEADS = 12
KV_HEADS = 2
HEAD_DIM = 128
TOP = 4
TOK_DEV = 512
BRANCHES = 4
LEAVES = 8
TRUNK = 256
BRANCH = 64

EPSILON = 1e-06
ROPE_BASE = 10000.0
MASKED = -1e30
LOW = jnp.bfloat16
WIDE = jnp.float32
KEY_WIDTH = KV_HEADS * HEAD_DIM
GROUP = HEADS // KV_HEADS
QUARTERS = 4
VMEM_LIMIT = 56 * 1024 * 1024

ANY = pl.BlockSpec(memory_space=pl.ANY)
SMEM = pl.BlockSpec(memory_space=pltpu.SMEM)


def nn(one, two):
    return lax.dot_general(one, two, (((1,), (0,)), ((), ())), preferred_element_type=WIDE)


def nt(one, two):
    return lax.dot_general(one, two, (((1,), (1,)), ((), ())), preferred_element_type=WIDE)


def tn(one, two):
    return lax.dot_general(one, two, (((0,), (0,)), ((), ())), preferred_element_type=WIDE)


def whole(shape):
    return pl.BlockSpec(shape, lambda *_: (0,) * len(shape))


LITTLE = pl.CostEstimate(flops=1, bytes_accessed=1, transcendentals=0)


def params():
    return pltpu.CompilerParams(vmem_limit_bytes=VMEM_LIMIT)


def turn(values, cosine, sine):
    return values * cosine + pltpu.roll(values, HEAD_DIM // 2, 1) * sine


def turn_back(values, cosine, sine):
    return values * cosine - pltpu.roll(values, HEAD_DIM // 2, 1) * sine


SLOTS = range(4)
PIECES = (
    tuple((0, slot) for slot in SLOTS),
    tuple((2, slot) for slot in SLOTS),
    tuple((4, slot) for slot in SLOTS),
    ((6, 0), (6, 1)),
    ((6, 2), (6, 3)),
    tuple((1, slot) for slot in SLOTS),
    tuple((flip_bits, slot) for flip_bits in (3, 5) for slot in SLOTS),
    ((7, 0), (7, 1)),
    ((7, 2), (7, 3)),
)
EXTRA = 16


def weight_copies(info, refs, target, sem, start, width):
    if len(refs) == 1:
        return [pltpu.make_async_copy(refs[0], target, sem)]
    depth = refs[0].shape[1] - EXTRA
    copies = []
    for ref, parts in zip(refs, PIECES):
        for at, (flip_bits, slot) in enumerate(parts):
            row = pl.multiple_of((info[0] ^ flip_bits) * depth, depth)
            col = pl.multiple_of(info[2 + slot] * width, 128)
            copies.append(
                pltpu.make_async_copy(
                    ref.at[at, pl.ds(0, depth), pl.ds(start, width)],
                    target.at[pl.ds(row, depth), pl.ds(col, width)],
                    sem,
                )
            )
    return copies


def extras_kernel(info, *rest):
    refs, (out, sem) = rest[:-2], rest[-2:]
    depth = refs[0].shape[1] - EXTRA
    copies = []
    for ref, parts in zip(refs, PIECES):
        for at, (flip_bits, slot) in enumerate(parts):
            to = (info[0] ^ flip_bits) * QUARTERS + info[2 + slot]
            copies.append(pltpu.make_async_copy(ref.at[at, pl.ds(depth, EXTRA)], out.at[to], sem))
    run_all(copies)
    wait_all(copies)


def extras(info, refs):
    return pl.pallas_call(
        extras_kernel,
        out_shape=jax.ShapeDtypeStruct((8 * QUARTERS, EXTRA, refs[0].shape[2]), LOW),
        in_specs=[SMEM] + [ANY] * len(refs),
        out_specs=pl.BlockSpec(memory_space=pltpu.VMEM),
        scratch_shapes=[pltpu.SemaphoreType.DMA],
        compiler_params=params(),
        cost_estimate=LITTLE,
        name="extra_rows",
    )(info, *refs)


def run_all(copies):
    for copy in copies:
        copy.start()


def wait_all(copies):
    for copy in copies:
        copy.wait()


def key_value_kernel(info, tokens, gain, cosine, sine, *rest):
    count = len(rest) - 4
    refs, (normed, out, weight, sem) = rest[:count], rest[count:]
    copies = weight_copies(info, refs, weight, sem, D // QUARTERS, 128)
    run_all(copies)
    values = tokens[...].astype(WIDE)
    factor = lax.rsqrt(jnp.mean(values * values, axis=-1, keepdims=True) + EPSILON)
    low = (values * factor * gain[...]).astype(LOW)
    normed[...] = low
    wait_all(copies)
    both = nn(low, weight[...])
    half = HEAD_DIM // 2
    first = lax.broadcasted_iota(jnp.int32, (TOK_DEV, HEAD_DIM), 1) < half
    for g in range(KV_HEADS):
        one = both[:, 256 * g : 256 * g + 128]
        two = both[:, 256 * g + 128 : 256 * g + 256]
        key = jnp.where(first, one, pltpu.roll(two, half, 1))
        value = jnp.where(first, pltpu.roll(one, half, 1), two)
        out[:, 128 * g : 128 * g + 128] = turn(key, cosine[...], sine[...]).astype(LOW)
        out[:, KEY_WIDTH + 128 * g : KEY_WIDTH + 128 * g + 128] = value.astype(LOW)


def key_value(info, tokens, gain, cosine, sine, refs):
    return pl.pallas_call(
        key_value_kernel,
        out_shape=(
            jax.ShapeDtypeStruct((TOK_DEV, D), LOW),
            jax.ShapeDtypeStruct((TOK_DEV, 2 * KEY_WIDTH), LOW),
        ),
        in_specs=[SMEM] + [pl.BlockSpec(memory_space=pltpu.VMEM)] * 4 + [ANY] * len(refs),
        out_specs=(pl.BlockSpec(memory_space=pltpu.VMEM),) * 2,
        scratch_shapes=[pltpu.VMEM((D, 2 * KEY_WIDTH), LOW), pltpu.SemaphoreType.DMA],
        compiler_params=params(),
        cost_estimate=LITTLE,
        name="norm_key_value",
    )(info, tokens, gain, cosine, sine, *refs)


def query_kernel(info, normed, cosine, sine, *rest):
    count = len(rest) - 3
    refs, (out, weight, sem) = rest[:count], rest[count:]

    @pl.when(pl.program_id(0) == 0)
    def _():
        copies = weight_copies(info, refs, weight, sem, 0, D // QUARTERS)
        run_all(copies)
        wait_all(copies)

    at = pl.multiple_of(pl.program_id(0) * 256, 256)
    lin = nn(normed[...], weight[:, pl.ds(at, 256)])
    for h in range(2):
        out[:, 128 * h : 128 * h + 128] = turn(
            lin[:, 128 * h : 128 * h + 128], cosine[...], sine[...]
        ).astype(LOW)


def query(info, normed, cosine, sine, refs):
    return pl.pallas_call(
        query_kernel,
        grid=(D // 256,),
        out_shape=jax.ShapeDtypeStruct((TOK_DEV, D), LOW),
        in_specs=[SMEM, whole((TOK_DEV, D)), whole((TOK_DEV, 128)), whole((TOK_DEV, 128))]
        + [ANY] * len(refs),
        out_specs=pl.BlockSpec((TOK_DEV, 256), lambda i: (0, i)),
        scratch_shapes=[pltpu.VMEM((D, D), LOW), pltpu.SemaphoreType.DMA],
        compiler_params=params(),
        cost_estimate=LITTLE,
        name="query_projection",
    )(info, normed, cosine, sine, *refs)


KEYS = TRUNK + 2 * BRANCH
CHUNKS = TOK_DEV // BRANCH


def chunk_keys(info, source, own, column, chunk):
    at = pl.multiple_of(info[6 + chunk], BRANCH)
    rows = pl.multiple_of(chunk * BRANCH, BRANCH)
    columns = slice(column, column + HEAD_DIM)
    return jnp.concatenate(
        [
            source[0:TRUNK, columns],
            source[pl.ds(at, BRANCH), columns],
            own[pl.ds(rows, BRANCH), columns],
        ],
        axis=0,
    )


def chunk_allowed(info, chunk, query_axis, shape):
    query_row = lax.broadcasted_iota(jnp.int32, shape, query_axis) & (BRANCH - 1)
    key = lax.broadcasted_iota(jnp.int32, shape, 1 - query_axis)
    leaves = info[1] == 0
    trunk = jnp.logical_and(jnp.logical_not(leaves), chunk < TRUNK // BRANCH)
    limit = jnp.where(trunk, chunk * BRANCH + query_row, TRUNK - 1)
    branch_limit = jnp.where(leaves, TRUNK + BRANCH - 1, 0)
    own_limit = jnp.where(trunk, 0, query_row + TRUNK + BRANCH)
    top = jnp.where(key < TRUNK, limit, jnp.where(key < TRUNK + BRANCH, branch_limit, own_limit))
    return key <= top


def group_rows(ref, g):
    first = g * GROUP
    return jnp.concatenate(
        [ref[:, 128 * h : 128 * h + 128] for h in range(first, first + GROUP)], axis=0
    )


def keep_source(info, partner, own, source):
    @pl.when(pl.program_id(0) == 0)
    def _():
        @pl.when(info[1] == 0)
        def _():
            source[...] = partner[...]

        @pl.when(info[1] != 0)
        def _():
            source[...] = own[...]


def attention_kernel(info, queries, own, partner, out, source):
    keep_source(info, partner, own, source)
    chunk = pl.program_id(0)
    rows = GROUP * BRANCH
    allowed = chunk_allowed(info, chunk, 0, (rows, KEYS))
    for g in range(KV_HEADS):
        keys = chunk_keys(info, source, own, 128 * g, chunk)
        values = chunk_keys(info, source, own, KEY_WIDTH + 128 * g, chunk)
        scores = nt(group_rows(queries, g), keys) * HEAD_DIM**-0.5
        scores = jnp.where(allowed, scores, MASKED)
        weights = jnp.exp(scores - jnp.max(scores, axis=1, keepdims=True))
        total = jnp.sum(weights, axis=1, keepdims=True)
        mixed = nn((weights * (1.0 / total)).astype(LOW), values).astype(LOW)
        for h in range(GROUP):
            at = (g * GROUP + h) * 128
            out[:, at : at + 128] = mixed[h * BRANCH : (h + 1) * BRANCH]


def attention(info, queries, own, partner):
    return pl.pallas_call(
        attention_kernel,
        grid=(CHUNKS,),
        out_shape=jax.ShapeDtypeStruct((TOK_DEV, D), LOW),
        in_specs=[
            SMEM,
            pl.BlockSpec((BRANCH, D), lambda i: (i, 0)),
            whole((TOK_DEV, 2 * KEY_WIDTH)),
            whole((TOK_DEV, 2 * KEY_WIDTH)),
        ],
        out_specs=pl.BlockSpec((BRANCH, D), lambda i: (i, 0)),
        scratch_shapes=[pltpu.VMEM((TOK_DEV, 2 * KEY_WIDTH), LOW)],
        compiler_params=params(),
        cost_estimate=LITTLE,
        name="tree_attention",
    )(info, queries, own, partner)


def attention_back_kernel(
    info, queries, own, partner, grads, cosine, sine, grad_query, own_grad, source_grad, source
):
    keep_source(info, partner, own, source)
    chunk = pl.program_id(0)

    @pl.when(chunk == 0)
    def _():
        source_grad[...] = jnp.zeros_like(source_grad)

    rows = GROUP * BRANCH
    scale = HEAD_DIM**-0.5
    allowed = chunk_allowed(info, chunk, 1, (KEYS, rows))
    at = pl.multiple_of(info[6 + chunk], BRANCH)
    for g in range(KV_HEADS):
        keys = chunk_keys(info, source, own, 128 * g, chunk)
        values = chunk_keys(info, source, own, KEY_WIDTH + 128 * g, chunk)
        query_rows = group_rows(queries, g)
        grad_rows = group_rows(grads, g)
        scores = jnp.where(allowed, nt(keys, query_rows) * scale, MASKED)
        weights = jnp.exp(scores - jnp.max(scores, axis=0, keepdims=True))
        probs = weights * (1.0 / jnp.sum(weights, axis=0, keepdims=True))
        grad_probs = nt(values, grad_rows)
        mean = jnp.sum(probs * grad_probs, axis=0, keepdims=True)
        grad_scores = (probs * (grad_probs - mean)).astype(LOW)
        grad_values = nn(probs.astype(LOW), grad_rows)
        grad_keys = nn(grad_scores, query_rows) * scale
        grad_queries = tn(grad_scores, keys) * scale
        for h in range(GROUP):
            to = (g * GROUP + h) * 128
            grad_query[:, to : to + 128] = turn_back(
                grad_queries[h * BRANCH : (h + 1) * BRANCH], cosine[...], sine[...]
            ).astype(LOW)
        for column, grad in ((128 * g, grad_keys), (KEY_WIDTH + 128 * g, grad_values)):
            columns = slice(column, column + 128)
            source_grad[0:TRUNK, columns] += grad[0:TRUNK]
            source_grad[pl.ds(at, BRANCH), columns] += grad[TRUNK : TRUNK + BRANCH]
            own_grad[:, columns] = grad[TRUNK + BRANCH :]


def attention_back(info, queries, own, partner, grads, cosine, sine):
    chunked = pl.BlockSpec((BRANCH, D), lambda i: (i, 0))
    pair = (TOK_DEV, 2 * KEY_WIDTH)
    return pl.pallas_call(
        attention_back_kernel,
        grid=(CHUNKS,),
        out_shape=(
            jax.ShapeDtypeStruct((TOK_DEV, D), LOW),
            jax.ShapeDtypeStruct(pair, WIDE),
            jax.ShapeDtypeStruct(pair, WIDE),
        ),
        in_specs=[
            SMEM,
            chunked,
            whole(pair),
            whole(pair),
            chunked,
            pl.BlockSpec((BRANCH, 128), lambda i: (i, 0)),
            pl.BlockSpec((BRANCH, 128), lambda i: (i, 0)),
        ],
        out_specs=(
            chunked,
            pl.BlockSpec((BRANCH, 2 * KEY_WIDTH), lambda i: (i, 0)),
            whole(pair),
        ),
        scratch_shapes=[pltpu.VMEM(pair, LOW)],
        compiler_params=params(),
        cost_estimate=LITTLE,
        name="tree_attention_back",
    )(info, queries, own, partner, grads, cosine, sine)


def out_kernel(info, heads, tokens, gain, *rest):
    count = len(rest) - 4
    refs, (residual, normed, weight, sem) = rest[:count], rest[count:]

    @pl.when(pl.program_id(0) == 0)
    def _():
        copies = weight_copies(info, refs, weight, sem, D // QUARTERS + 128, D // QUARTERS)
        run_all(copies)
        wait_all(copies)

    at = pl.ds(pl.multiple_of(pl.program_id(0) * 256, 256), 256)
    residual[:, at] = tokens[:, at].astype(WIDE) + nn(heads[...], weight[:, at])

    @pl.when(pl.program_id(0) == pl.num_programs(0) - 1)
    def _():
        values = residual[...]
        factor = lax.rsqrt(jnp.mean(values * values, axis=-1, keepdims=True) + EPSILON)
        normed[...] = (values * factor * gain[...]).astype(LOW)


def out_projection(info, heads, tokens, gain, refs):
    full = (TOK_DEV, D)
    return pl.pallas_call(
        out_kernel,
        grid=(D // 256,),
        out_shape=(jax.ShapeDtypeStruct(full, WIDE), jax.ShapeDtypeStruct(full, LOW)),
        in_specs=[SMEM, whole(full), whole(full), whole((1, D))] + [ANY] * len(refs),
        out_specs=(whole(full), whole(full)),
        scratch_shapes=[pltpu.VMEM((D, D), LOW), pltpu.SemaphoreType.DMA],
        compiler_params=params(),
        cost_estimate=LITTLE,
        name="out_projection",
    )(info, heads, tokens, gain, *refs)


def hits_of(routes, ids):
    hit = ids == routes[0, 0:1]
    for k in range(1, TOP):
        hit = jnp.logical_or(hit, ids == routes[0, k : k + 1])
    return hit


def tables_kernel(capacity, local, total, order, info, routes, chosen_out, place_out, earlier):
    @pl.when(pl.program_id(0) == 0)
    def _():
        one = lax.broadcasted_iota(jnp.int32, (TOK_DEV, TOK_DEV), 0)
        two = lax.broadcasted_iota(jnp.int32, (TOK_DEV, TOK_DEV), 1)
        earlier[...] = jnp.where(one < two, 1.0, 0.0).astype(LOW)

    ids = lax.broadcasted_iota(jnp.int32, (total, TOK_DEV), 0)
    hit = hits_of(routes, ids)
    rank = nn(jnp.where(hit, 1.0, 0.0).astype(LOW), earlier[...])
    place = jnp.where(hit, rank, -1.0)
    spots = lax.broadcasted_iota(jnp.int32, (capacity, TOK_DEV), 0).astype(WIDE)
    place_out[0] = jnp.full(place_out.shape[1:], -1.0, WIDE)
    for e in range(local):
        mine = ids == info[0] * local + e
        place_row = jnp.sum(jnp.where(mine, place, 0.0), axis=0, keepdims=True)
        place_out[0, e : e + 1] = place_row
        chosen_out[0, e * capacity : (e + 1) * capacity] = jnp.where(
            spots == place_row, 1.0, 0.0
        ).astype(LOW)


def tables(order, info, routes, capacity, local, total):
    count = routes.shape[0]
    return pl.pallas_call(
        functools.partial(tables_kernel, capacity, local, total),
        grid_spec=pltpu.PrefetchScalarGridSpec(
            num_scalar_prefetch=2,
            grid=(count,),
            in_specs=[pl.BlockSpec((1, TOP, TOK_DEV), lambda i, order, info: (order[i], 0, 0))],
            out_specs=[
                pl.BlockSpec((1, local * capacity, TOK_DEV), lambda i, order, info: (i, 0, 0)),
                pl.BlockSpec((1, 8, TOK_DEV), lambda i, order, info: (i, 0, 0)),
            ],
            scratch_shapes=[pltpu.VMEM((TOK_DEV, TOK_DEV), LOW)],
        ),
        out_shape=[
            jax.ShapeDtypeStruct((count, local * capacity, TOK_DEV), LOW),
            jax.ShapeDtypeStruct((count, 8, TOK_DEV), WIDE),
        ],
        compiler_params=params(),
        cost_estimate=LITTLE,
        name="route_tables",
    )(order, info, routes)


def pick_kernel(local, order, chosen, blocks, *outs):
    rows_of = nn(chosen[0], blocks[0]).astype(LOW)
    capacity = outs[0].shape[1]
    for e in range(local):
        outs[e][0] = rows_of[e * capacity : (e + 1) * capacity]


def pick_rows(order, chosen, blocks, local):
    count, height, _ = chosen.shape
    capacity = height // local
    return pl.pallas_call(
        functools.partial(pick_kernel, local),
        grid_spec=pltpu.PrefetchScalarGridSpec(
            num_scalar_prefetch=1,
            grid=(count,),
            in_specs=[
                pl.BlockSpec((1, height, TOK_DEV), lambda i, order: (i, 0, 0)),
                pl.BlockSpec((1, TOK_DEV, D), lambda i, order: (order[i], 0, 0)),
            ],
            out_specs=[pl.BlockSpec((1, capacity, D), lambda i, order: (i, 0, 0))] * local,
        ),
        out_shape=[jax.ShapeDtypeStruct((count, capacity, D), LOW)] * local,
        compiler_params=params(),
        cost_estimate=LITTLE,
        name="pick_rows",
    )(order, chosen, blocks)


def dispatch_kernel(local, near, info, rows, chosen, routes, router, *rest):
    outs, logits = rest[2 * local : 4 * local], rest[-1]
    total = router.shape[1]
    step = pl.program_id(0)
    block = rows[...]
    rows_of = nn(chosen[0], block).astype(LOW)
    capacity = outs[0].shape[1]
    for e in range(local):
        outs[e][0] = rows_of[e * capacity : (e + 1) * capacity]
    part = nn(block, router[...])

    @pl.when(step == 0)
    def _():
        logits[...] = part

    @pl.when(step > 0)
    def _():
        logits[...] += part

    @pl.when(step == pl.num_programs(0) - 1)
    def _():
        values = logits[...].T
        ids = lax.broadcasted_iota(jnp.int32, (total, TOK_DEV), 0)
        weights = jnp.exp(values - jnp.max(values, axis=0, keepdims=True))
        hit = hits_of(routes, ids)
        share = weights / jnp.sum(jnp.where(hit, weights, 0.0), axis=0, keepdims=True)
        for e in range(local):
            mine = ids == info[0] * local + e
            share_row = jnp.sum(jnp.where(mine, share, 0.0), axis=0, keepdims=True)
            picked = chosen[0, e * capacity : (e + 1) * capacity].astype(WIDE)
            outs[local + e][0] = jnp.sum(picked * share_row, axis=1, keepdims=True)


def dispatch(at, near, info, rows, chosen, routes, router, local, earlier):
    count, height, _ = chosen.shape
    capacity = height // local
    total = router.shape[1]
    wide = 512
    out_shape = [jax.ShapeDtypeStruct((count, capacity, D), LOW)] * local + [
        jax.ShapeDtypeStruct((count, capacity, 1), WIDE)
    ] * local
    if earlier is None:
        earlier = [jnp.zeros((8, 128), shape.dtype) for shape in out_shape]
        aliases = {}
    else:
        aliases = {6 + i: i for i in range(len(out_shape))}
    return pl.pallas_call(
        functools.partial(dispatch_kernel, local),
        grid_spec=pltpu.PrefetchScalarGridSpec(
            num_scalar_prefetch=2,
            grid=(D // wide,),
            in_specs=[
                pl.BlockSpec((TOK_DEV, wide), lambda i, near, info: (0, i)),
                pl.BlockSpec((1, height, TOK_DEV), lambda i, near, info: (at, 0, 0)),
                pl.BlockSpec((1, TOP, TOK_DEV), lambda i, near, info: (near[at], 0, 0)),
                pl.BlockSpec((wide, total), lambda i, near, info: (i, 0)),
            ]
            + [ANY] * len(out_shape),
            out_specs=[
                pl.BlockSpec((1, capacity, wide), lambda i, near, info: (at, 0, i))
            ]
            * local
            + [pl.BlockSpec((1, capacity, 1), lambda i, near, info: (at, 0, 0))] * local,
            scratch_shapes=[pltpu.VMEM((TOK_DEV, total), WIDE)],
        ),
        out_shape=out_shape,
        input_output_aliases=aliases,
        compiler_params=params(),
        cost_estimate=LITTLE,
        name="dispatch",
    )(near, info, rows, chosen, routes, router, *earlier)


def spread_kernel(local, place, *rest):
    dots, out = rest[:local], rest[local]
    spots = lax.broadcasted_iota(jnp.int32, (dots[0].shape[1], TOK_DEV), 0).astype(WIDE)
    for e in range(local):
        chosen = spots == place[0, e : e + 1]
        out[0, e : e + 1] = jnp.sum(jnp.where(chosen, dots[e][0], 0.0), axis=0, keepdims=True)


def spread(place, dots):
    count, capacity, _ = dots[0].shape
    local = len(dots)
    return pl.pallas_call(
        functools.partial(spread_kernel, local),
        grid=(count,),
        out_shape=jax.ShapeDtypeStruct((count, local, TOK_DEV), WIDE),
        in_specs=[pl.BlockSpec((1, 8, TOK_DEV), lambda i: (i, 0, 0))]
        + [pl.BlockSpec((1, capacity, 1), lambda i: (i, 0, 0))] * local,
        out_specs=pl.BlockSpec((1, local, TOK_DEV), lambda i: (i, 0, 0)),
        compiler_params=params(),
        cost_estimate=LITTLE,
        name="spread",
    )(place, *dots)


def expert_kernel(slots, info, rows, grads, shares, *rest):
    count = len(rest) - 7
    refs = rest[:count]
    out_rows, back_rows, grad_rows, acts, dots, weight, sem = rest[count:]
    part = weight.shape[1] // slots

    @pl.when(pl.program_id(0) == 0)
    def _():
        def copies(ref, slot):
            return [
                pltpu.make_async_copy(
                    ref.at[pl.ds(which * part, part)],
                    weight.at[which, pl.ds(slot * part, part)],
                    sem,
                )
                for which in range(3)
            ]

        if count == slots:
            for slot in range(slots):
                run_all(copies(refs[slot], slot))
        else:
            block, second, above, below, far = refs
            low_end = info[2] == 0
            end = jnp.logical_or(low_end, info[2] == 3)
            run_all(copies(block, 0))
            run_all(copies(second, 1))

            @pl.when(low_end)
            def _():
                run_all(copies(above, 2))

            @pl.when(jnp.logical_not(low_end))
            def _():
                run_all(copies(below, 2))

            @pl.when(end)
            def _():
                run_all(copies(far, 3))

            @pl.when(jnp.logical_not(end))
            def _():
                run_all(copies(above, 3))

        for slot in range(slots):
            wait_all(copies(refs[0], slot))

    row_block = rows[...]
    share = shares[...]
    grad_float = grads[...].astype(WIDE)
    grad_low = (share * grad_float).astype(LOW)
    grad_rows[...] = grad_low
    gate_act = nt(row_block, weight[0])
    upward = nt(row_block, weight[1])
    sigmoid = 1.0 / (1.0 + jnp.exp(-gate_act))
    silu = gate_act * sigmoid
    hidden = (silu * upward).astype(LOW)
    expert_out = nn(hidden, weight[2]).astype(LOW).astype(WIDE)
    out_rows[...] = (share * expert_out).astype(LOW)
    dots[...] = jnp.sum(grad_float * expert_out, axis=1, keepdims=True)
    grad_hidden = nt(grad_low, weight[2])
    grad_gate = (grad_hidden * upward * sigmoid * (1.0 + gate_act * (1.0 - sigmoid))).astype(LOW)
    grad_up = (grad_hidden * silu).astype(LOW)
    back_rows[...] = (nn(grad_gate, weight[0]) + nn(grad_up, weight[1])).astype(LOW)
    for which, act in enumerate((grad_gate, grad_up, hidden)):
        turned = act.T
        for slot in range(slots):
            acts[slot, which * part : (which + 1) * part] = turned[
                slot * part : (slot + 1) * part
            ]


EXPERT_ROWS = 256


def expert(info, rows, grads, shares, refs, slots):
    height = rows.shape[0]
    part = refs[0].shape[0] // 3
    wide_block = pl.BlockSpec((EXPERT_ROWS, D), lambda i: (i, 0))
    thin_block = pl.BlockSpec((EXPERT_ROWS, 1), lambda i: (i, 0))
    return pl.pallas_call(
        functools.partial(expert_kernel, slots),
        grid=(height // EXPERT_ROWS,),
        out_shape=[jax.ShapeDtypeStruct((height, D), LOW)] * 3
        + [
            jax.ShapeDtypeStruct((slots, 3 * part, height), LOW),
            jax.ShapeDtypeStruct((height, 1), WIDE),
        ],
        in_specs=[SMEM, wide_block, wide_block, thin_block] + [ANY] * len(refs),
        out_specs=[wide_block] * 3
        + [pl.BlockSpec((slots, 3 * part, EXPERT_ROWS), lambda i: (0, 0, i)), thin_block],
        scratch_shapes=[pltpu.VMEM((3, slots * part, D), LOW), pltpu.SemaphoreType.DMA],
        compiler_params=params(),
        cost_estimate=LITTLE,
        name="expert",
    )(info, rows, grads, shares, *refs)


def expert_grads_kernel(slots, rows, grads, *rest):
    acts, outs = rest[: len(slots)], rest[len(slots) :]
    part = acts[0].shape[1] // 3
    for act, out in zip(acts, outs):
        out[: 2 * part, :] = nn(act[0, : 2 * part], rows[...]).astype(LOW)
        out[2 * part :, :] = nn(act[0, 2 * part :], grads[...]).astype(LOW)


def expert_grads(acts, rows, grads, slots):
    _, part, height = acts.shape
    return pl.pallas_call(
        functools.partial(expert_grads_kernel, slots),
        grid=(D // 256,),
        out_shape=[jax.ShapeDtypeStruct((part, D), LOW) for _ in slots],
        in_specs=[pl.BlockSpec((height, 256), lambda i: (0, i))] * 2
        + [pl.BlockSpec((1, part, height), lambda i, s=slot: (s, 0, 0)) for slot in slots],
        out_specs=[pl.BlockSpec((part, 256), lambda i: (0, i)) for _ in slots],
        compiler_params=params(),
        cost_estimate=LITTLE,
        name="expert_gradients",
    )(rows, grads, *[acts] * len(slots))


def combine_kernel(local, chosen, *rest):
    rows, out = rest[:local], rest[local]
    both = jnp.concatenate([ref[0] for ref in rows], axis=0)
    out[0] = tn(chosen[0], both).astype(LOW)


def combine(chosen, rows, first, step):
    count, capacity, _ = rows[0].shape
    number = (count - first + step - 1) // step
    return pl.pallas_call(
        functools.partial(combine_kernel, len(rows)),
        grid=(number,),
        out_shape=jax.ShapeDtypeStruct((number, TOK_DEV, D), LOW),
        in_specs=[
            pl.BlockSpec((1,) + chosen.shape[1:], lambda i: (first + step * i, 0, 0))
        ]
        + [pl.BlockSpec((1, capacity, D), lambda i: (first + step * i, 0, 0))] * len(rows),
        out_specs=pl.BlockSpec((1, TOK_DEV, D), lambda i: (i, 0, 0)),
        compiler_params=params(),
        cost_estimate=LITTLE,
        name="combine",
    )(chosen, *rows)


def split(values):
    high = values.astype(LOW)
    return high, (values - high.astype(WIDE)).astype(LOW)


def norm_back(values, gain, grad):
    factor = lax.rsqrt(jnp.mean(values * values, axis=-1, keepdims=True) + EPSILON)
    scaled = gain * grad
    mean = jnp.mean(values * scaled, axis=-1, keepdims=True)
    grad_values = factor * scaled - values * (factor * factor * factor * mean)
    grad_gain = jnp.sum(grad * values * factor, axis=0, keepdims=True)
    return grad_values, grad_gain


def router_back(logits, routes, grad_shares):
    ids = lax.broadcasted_iota(jnp.int32, logits.shape, 0)
    hit = ids == routes[0:1]
    for k in range(1, TOP):
        hit = jnp.logical_or(hit, ids == routes[k : k + 1])
    weights = jnp.exp(logits - jnp.max(logits, axis=0, keepdims=True))
    probs = weights / jnp.sum(weights, axis=0, keepdims=True)
    chosen = jnp.sum(jnp.where(hit, probs, 0.0), axis=0, keepdims=True)
    grads = jnp.where(hit, grad_shares, 0.0)
    mean = jnp.sum(probs * grads, axis=0, keepdims=True) / chosen
    grad_probs = jnp.where(hit, (grads - mean) / chosen, 0.0)
    return probs * (grad_probs - jnp.sum(probs * grad_probs, axis=0, keepdims=True))


def branch_back_kernel(
    parts, info, residual, normed, cotangent, routes, grad_shares, router, gain, *rest
):
    sums, rest = rest[:parts], rest[parts:]
    count = len(rest) - 7
    refs = rest[:count]
    grad_residual, grad_branch, grad_heads, grad_gain, grad_router, weight, sem = rest[count:]

    @pl.when(pl.program_id(0) == 0)
    def _():
        copies = weight_copies(info, refs, weight, sem, D // QUARTERS + 128, D // QUARTERS)
        run_all(copies)
        logits = nt(router[...], normed[...])
        high, low = split(router_back(logits, routes[...], grad_shares[...]))
        grad_router[...] = nn(high, normed[...]) + nn(low, normed[...])
        grad_normed = tn(high, router[...]) + tn(low, router[...])
        if parts == 1:
            grad_normed += sums[0][...]
        else:
            values = [ref[...].astype(WIDE) for ref in sums]
            grad_normed += jnp.concatenate(
                [values[0] + values[1] + values[2], values[3] + values[4] + values[5]], axis=0
            )
        grad_values, gain_grad = norm_back(residual[...], gain[...], grad_normed)
        grad_gain[...] = gain_grad
        total = cotangent[...].astype(WIDE) + grad_values
        grad_residual[...] = total
        grad_branch[...] = total.astype(LOW)
        wait_all(copies)

    at = pl.ds(pl.multiple_of(pl.program_id(0) * 256, 256), 256)
    grad_heads[...] = nt(grad_branch[...], weight[at, :]).astype(LOW)


def branch_back(info, residual, normed, sums, cotangent, routes, grad_shares, router, gain, refs):
    full = (TOK_DEV, D)
    total = router.shape[0]
    return pl.pallas_call(
        functools.partial(branch_back_kernel, len(sums)),
        grid=(D // 256,),
        out_shape=(
            jax.ShapeDtypeStruct(full, WIDE),
            jax.ShapeDtypeStruct(full, LOW),
            jax.ShapeDtypeStruct(full, LOW),
            jax.ShapeDtypeStruct((1, D), WIDE),
            jax.ShapeDtypeStruct((total, D), WIDE),
        ),
        in_specs=[SMEM]
        + [whole(full)] * 3
        + [whole((TOP, TOK_DEV)), whole((total, TOK_DEV)), whole((total, D)), whole((1, D))]
        + [whole(part.shape) for part in sums]
        + [ANY] * len(refs),
        out_specs=(
            whole(full),
            whole(full),
            pl.BlockSpec((TOK_DEV, 256), lambda i: (0, i)),
            whole((1, D)),
            whole((total, D)),
        ),
        scratch_shapes=[pltpu.VMEM((D, D), LOW), pltpu.SemaphoreType.DMA],
        compiler_params=params(),
        cost_estimate=LITTLE,
        name="experts_norm_back",
    )(info, residual, normed, cotangent, routes, grad_shares, router, gain, *sums, *refs)


def join_grads_kernel(info, own_grad, source_grad, arrived, cosine, sine, out):
    half = HEAD_DIM // 2
    first = lax.broadcasted_iota(jnp.int32, (TOK_DEV, HEAD_DIM), 1) < half
    leaves = info[1] == 0

    def total(column):
        columns = slice(column, column + 128)
        extra = source_grad[:, columns] + arrived[:, columns].astype(WIDE)
        return own_grad[:, columns] + jnp.where(leaves, 0.0, extra)

    for g in range(KV_HEADS):
        key = turn_back(total(128 * g), cosine[...], sine[...])
        value = total(KEY_WIDTH + 128 * g)
        out[:, 256 * g : 256 * g + 128] = jnp.where(
            first, key, pltpu.roll(value, half, 1)
        ).astype(LOW)
        out[:, 256 * g + 128 : 256 * g + 256] = jnp.where(
            first, pltpu.roll(key, half, 1), value
        ).astype(LOW)


def join_grads(info, own_grad, source_grad, arrived, cosine, sine):
    vmem = pl.BlockSpec(memory_space=pltpu.VMEM)
    return pl.pallas_call(
        join_grads_kernel,
        out_shape=jax.ShapeDtypeStruct((TOK_DEV, 2 * KEY_WIDTH), LOW),
        in_specs=[SMEM] + [vmem] * 5,
        out_specs=vmem,
        compiler_params=params(),
        cost_estimate=LITTLE,
        name="join_key_value_gradients",
    )(info, own_grad, source_grad, arrived, cosine, sine)


def token_back_kernel(info, grad_query, grad_pair, tokens, grad_residual, gain, *rest):
    count = (len(rest) - 6) // 2
    query_refs, pair_refs = rest[:count], rest[count : 2 * count]
    out, grad_gain, query_weight, pair_weight, grad_normed, sem = rest[2 * count :]

    @pl.when(pl.program_id(0) == 0)
    def _():
        copies = weight_copies(info, query_refs, query_weight, sem, 0, D // QUARTERS)
        copies += weight_copies(info, pair_refs, pair_weight, sem, D // QUARTERS, 128)
        run_all(copies)
        wait_all(copies)

    at = pl.ds(pl.multiple_of(pl.program_id(0) * 256, 256), 256)
    grad_normed[:, at] = nt(grad_query[...], query_weight[at, :]) + nt(
        grad_pair[...], pair_weight[at, :]
    )

    @pl.when(pl.program_id(0) == pl.num_programs(0) - 1)
    def _():
        grad_values, gain_grad = norm_back(
            tokens[...].astype(WIDE), gain[...], grad_normed[...]
        )
        grad_gain[...] = gain_grad
        out[...] = (grad_residual[...] + grad_values).astype(LOW)


def token_back(info, grad_query, grad_pair, tokens, grad_residual, gain, query_refs, pair_refs):
    full = (TOK_DEV, D)
    return pl.pallas_call(
        token_back_kernel,
        grid=(D // 256,),
        out_shape=(jax.ShapeDtypeStruct(full, LOW), jax.ShapeDtypeStruct((1, D), WIDE)),
        in_specs=[
            SMEM,
            whole(full),
            whole((TOK_DEV, 2 * KEY_WIDTH)),
            whole(full),
            whole(full),
            whole((1, D)),
        ]
        + [ANY] * (len(query_refs) + len(pair_refs)),
        out_specs=(whole(full), whole((1, D))),
        scratch_shapes=[
            pltpu.VMEM((D, D), LOW),
            pltpu.VMEM((D, 2 * KEY_WIDTH), LOW),
            pltpu.VMEM(full, WIDE),
            pltpu.SemaphoreType.DMA,
        ],
        compiler_params=params(),
        cost_estimate=LITTLE,
        name="token_gradient",
    )(info, grad_query, grad_pair, tokens, grad_residual, gain, *query_refs, *pair_refs)


def weight_grads_kernel(parts, info, *rest):
    ins, (keep, send) = rest[:-2], rest[-2:]
    depth = D // 8
    core = info[0] & 1
    chip = pl.program_id(0) ^ (info[0] >> 1)
    start = 0
    for strip_at, grads_at, width in parts:
        low = tn(ins[strip_at][...], ins[grads_at][...]).astype(LOW)
        columns = slice(start, start + width)
        start += width
        for slot in range(QUARTERS):
            for j in range(QUARTERS):

                @pl.when(info[2 + slot] == j)
                def _():
                    piece = low[:, j * width : (j + 1) * width]
                    upper, lower = piece[:depth], piece[depth:]
                    keep[0, slot, :depth, columns] = jnp.where(core == 0, upper, lower)
                    send[0, slot, :depth, columns] = jnp.where(core == 0, lower, upper)

    if keep.shape[2] > depth:
        extra = ins[-1]
        for slot in range(QUARTERS):
            to = info[2 + slot]
            keep[0, slot, depth:] = extra[(chip * 2 + core) * QUARTERS + to]
            send[0, slot, depth:] = extra[(chip * 2 + 1 - core) * QUARTERS + to]


def weight_grads(info, strips, grads, parts, extra):
    depth = D // 8
    width = sum(part[2] for part in parts)
    strip = pl.BlockSpec((TOK_DEV, 2 * depth), lambda i, info: (0, i ^ (info[0] >> 1)))
    more = [] if extra is None else [extra]
    shape = (4, QUARTERS, depth + EXTRA * len(more), width)
    out = pl.BlockSpec((1,) + shape[1:], lambda i, info: (i, 0, 0, 0))
    return pl.pallas_call(
        functools.partial(weight_grads_kernel, parts),
        grid_spec=pltpu.PrefetchScalarGridSpec(
            num_scalar_prefetch=1,
            grid=(4,),
            in_specs=[strip] * len(strips)
            + [
                pl.BlockSpec(a.shape, lambda i, info, n=a.ndim: (0,) * n)
                for a in (*grads, *more)
            ],
            out_specs=(out, out),
        ),
        out_shape=(jax.ShapeDtypeStruct(shape, LOW),) * 2,
        compiler_params=params(),
        cost_estimate=LITTLE,
        name="weight_gradients",
    )(info, *strips, *grads, *more)


def position_of(token_index):
    branch_place = TRUNK + (token_index - TRUNK) % BRANCH
    leaf_place = TRUNK + BRANCH + (token_index - TOK_DEV) % BRANCH
    return jnp.where(
        token_index < TRUNK, token_index, jnp.where(token_index < TOK_DEV, branch_place, leaf_place)
    )


def rotary_tables(positions):
    half_dim = HEAD_DIM // 2
    frequency = ROPE_BASE ** (-jnp.arange(half_dim, dtype=jnp.float32) / half_dim)
    angles = positions.astype(jnp.float32)[:, None] * frequency[None, :]
    cosine, sine = (jnp.cos(angles), jnp.sin(angles))
    return (
        jnp.concatenate([cosine, cosine], axis=1),
        jnp.concatenate([-sine, sine], axis=1),
    )


def after(values, *earlier):
    return lax.optimization_barrier((values, earlier))[0]


def fast_mesh():
    return lax.axis_size("rows") == 8 and lax.axis_size("cols") == 4


SLOT_SHARD = ((0, 2, 1, 3), (1, 3, 0, 2), (2, 0, 1, 3), (3, 1, 2, 0))
UP = [(0, 1), (1, 2), (2, 3)]
DOWN = [(1, 0), (2, 1), (3, 2)]
FAR = [(0, 3), (3, 0)]


def send_near(block):
    return lax.ppermute(block, "cols", DOWN), lax.ppermute(block, "cols", UP)


def send_far(block):
    return lax.ppermute(block, "cols", FAR)


def send_second(block, near):
    place = lax.axis_index("cols")
    above, below = near
    payload = jnp.where(place == 1, above, jnp.where(place == 2, below, block))
    return lax.ppermute(payload, "cols", [(3, 1), (1, 0), (0, 2), (2, 3)])


def slot_list(block, near, second, far):
    place = lax.axis_index("cols")
    above, below = near
    end = (place == 0) | (place == 3)
    return [
        block,
        second,
        jnp.where(place == 0, above, below),
        jnp.where(end, far, above),
    ]


def reduce_first(second, fourth, chain=False):
    relay = lax.ppermute(second, "cols", [(1, 3), (0, 1), (2, 0), (3, 2)])
    return relay, None if chain else lax.ppermute(fourth, "cols", FAR)


def reduce_second(third, fourth, relay):
    place = lax.axis_index("cols")
    relayed = relay.astype(WIDE)
    upward_load = (
        jnp.where(place == 0, third, fourth).astype(WIDE) + jnp.where(place == 1, relayed, 0.0)
    ).astype(LOW)
    downward_load = (third.astype(WIDE) + jnp.where(place == 2, relayed, 0.0)).astype(LOW)
    return (
        lax.ppermute(upward_load, "cols", UP),
        lax.ppermute(downward_load, "cols", DOWN),
    )


def reduce_last(own, first, second):
    place = lax.axis_index("cols")
    relay, far = first
    below, above = second
    end = (place == 0) | (place == 3)
    return (
        own.astype(WIDE)
        + below.astype(WIDE)
        + above.astype(WIDE)
        + jnp.where(end, relay.astype(WIDE) + far.astype(WIDE), 0.0)
    )


def flip(block, bit):
    count = lax.axis_size("rows")
    return lax.ppermute(block, "rows", [(i, i ^ bit) for i in range(count)])


def add_low(one, two):
    return (one.astype(WIDE) + two.astype(WIDE)).astype(LOW)


def chip_sums(keep, got, chips, part):
    return jnp.stack([add_low(keep[i][part], got[i][part]) for i in chips])


def halves(keep):
    half = keep.shape[1] // 2
    return slice(0, half), slice(half, None)


def chips_first(keep, got):
    one, two = halves(keep)
    return chip_sums(keep, got, (1, 3), one), chip_sums(keep, got, (2, 3), two)


def chips_second(keep, got, got_x, got_y):
    one, two = halves(keep)
    near_x = chip_sums(keep, got, (0, 2), one)
    near_y = chip_sums(keep, got, (0, 1), two)
    got_xy = flip(add_low(near_x[1], got_x[1]), 4)
    got_yx = flip(add_low(near_y[1], got_y[1]), 2)
    return (near_x[0], got_x[0], got_xy, near_y[0], got_y[0], got_yx)


def send_chips(sums):
    return flip(sums[0], 2), flip(sums[1], 4)


def sum_parts(parts):
    wide = [a.astype(WIDE) for a in parts]
    if len(wide) == 1:
        return wide[0]
    return jnp.concatenate([wide[0] + wide[1] + wide[2], wide[3] + wide[4] + wide[5]], axis=0)


def on_device(
    tokens,
    query_weight,
    key_weight,
    value_weight,
    out_weight,
    router_weight,
    attention_gain,
    experts_gain,
    gate_weight,
    upward_weight,
    down_weight,
    routes,
    leaf_parent,
    cotangent,
):
    row_count = lax.axis_size("rows")
    col_count = lax.axis_size("cols")
    row_place = lax.axis_index("rows")
    col_place = lax.axis_index("cols")
    fast = fast_mesh()
    parity = lax.rem(col_place, 2)
    tree_id = lax.div(row_place * col_count + col_place, 2)
    parent_row = lax.dynamic_slice_in_dim(leaf_parent, tree_id, 1, 0)[0]
    depth, query_part = query_weight.shape
    key_part = key_weight.shape[1]
    router_part = router_weight.shape[1]
    gain_part = attention_gain.shape[0]
    expert_total = router_part * col_count
    local_experts = gate_weight.shape[0]
    capacity = TOK_DEV * TOP // expert_total * 5 // 4

    shards = (
        jnp.asarray(SLOT_SHARD, jnp.int32)[col_place]
        if fast
        else jnp.arange(4, dtype=jnp.int32)
    )
    branch_rows = jnp.where(parity == 0, TRUNK + BRANCH * parent_row, TRUNK)
    info = jnp.concatenate(
        [jnp.stack([row_place, parity]), shards, branch_rows, jnp.zeros((2,), jnp.int32)]
    ).astype(jnp.int32)

    packed = jnp.concatenate([query_weight, key_weight, value_weight, out_weight], axis=1)
    local_index = (1 - parity) * TOK_DEV + jnp.arange(TOK_DEV, dtype=jnp.int32)
    cosine, sine = rotary_tables(position_of(local_index))
    shard_blocks = [
        jnp.concatenate(
            [gate_weight[expert].T, upward_weight[expert].T, down_weight[expert]], axis=0
        )
        for expert in range(local_experts)
    ]
    nears, seconds, fars = ([], [], [])
    if fast:
        wide = packed.shape[1]
        gains = jnp.concatenate([attention_gain, experts_gain])[None, :]
        packed = jnp.concatenate(
            [
                packed,
                jnp.pad(router_weight.T, ((0, 0), (0, wide - depth))),
                jnp.pad(gains, ((0, 0), (0, wide - 2 * gain_part))),
                jnp.pad(routes.T.astype(LOW), ((0, 0), (0, wide - TOK_DEV))),
                jnp.zeros((EXTRA - router_part - 1 - TOP, wide), LOW),
            ],
            axis=0,
        )
        packed_near = send_near(packed)
        packed_far = send_far(packed)
        packed_second = send_second(packed, packed_near)
        own = jnp.stack(slot_list(packed, packed_near, packed_second, packed_far))

        def gather_expert(*earlier):
            expert_at = len(nears)
            block = after(shard_blocks[expert_at], *earlier)
            shard_blocks[expert_at] = block
            nears.append(send_near(block))
            seconds.append(send_second(block, nears[expert_at]))

        gather_expert(*packed_near)
        own = after(own, info, cosine, sine)
        beside, across = flip(own, 2), flip(own, 4)
        own_in = flip(own, 1)
        beside, across = after((beside, across), own_in, *nears[0])
        corner = [flip(beside[:2], 4), flip(across[2:], 2)]
        pair_in = flip(jnp.concatenate([beside, across], axis=0), 1)
        corner_in = [flip(piece, 1) for piece in corner]
        pieces = [own, beside, across, *corner, own_in, pair_in, *corner_in]
        query_refs = pair_refs = out_refs = pieces
        extra_rows = extras(info, pieces)
        router_all = extra_rows[:, :router_part, :depth]
        attention_scale = extra_rows[:, router_part, :gain_part]
        experts_scale = extra_rows[:, router_part, gain_part : 2 * gain_part]
        routes_all = lax.dynamic_index_in_dim(
            extra_rows.reshape(row_count, col_count, EXTRA, -1), col_place, 1, keepdims=False
        )
        routes_all = routes_all[:, router_part + 1 : router_part + 1 + TOP, :TOK_DEV]
        routes_all = routes_all.astype(jnp.int32)
    else:
        packed_all = lax.all_gather(lax.all_gather(packed, "cols", axis=0), "rows", axis=0)

        def unpack(start, width):
            part = packed_all[..., start : start + width]
            return jnp.swapaxes(part, 1, 2).reshape(row_count * depth, col_count * width)

        key_at = query_part
        query_refs = [unpack(0, query_part)]
        pair_refs = [
            jnp.concatenate(
                [
                    unpack(key_at, key_part).reshape(D, QUARTERS, -1),
                    unpack(key_at + key_part, key_part).reshape(D, QUARTERS, -1),
                ],
                axis=2,
            ).reshape(D, -1)
        ]
        out_refs = [unpack(key_at + 2 * key_part, query_part)]
        routes_all = lax.all_gather(routes.T, "rows", axis=0)
        axes = ("rows", "cols")
        router_all = jnp.swapaxes(lax.all_gather(router_weight, axes, axis=0), 1, 2)
        attention_scale = lax.all_gather(attention_gain, axes, axis=0)
        experts_scale = lax.all_gather(experts_gain, axes, axis=0)
        expert_refs = [
            [lax.all_gather(block, "cols", axis=0)[i] for i in range(col_count)]
            for block in shard_blocks
        ]

    attention_scale = attention_scale.reshape(1, D).astype(WIDE)
    experts_scale = experts_scale.reshape(1, D).astype(WIDE)
    router_rows = jnp.transpose(
        router_all.reshape(row_count, col_count, router_part, depth), (1, 2, 0, 3)
    ).reshape(expert_total, D)
    router_cols = router_rows.T
    if fast:
        near_rows = row_place ^ jnp.arange(row_count, dtype=jnp.int32)
    else:
        near_rows = jnp.arange(row_count, dtype=jnp.int32)
    chosen, place_rows = tables(
        near_rows, info, routes_all, capacity, local_experts, expert_total
    )
    tokens_in = after(tokens, seconds[0]) if fast else tokens
    normed, own_pair = key_value(info, tokens_in, attention_scale, cosine, sine, pair_refs)
    grad_in = after(cotangent, normed) if fast else cotangent
    grad_all = lax.all_gather(grad_in, "rows", axis=0)
    pairs = [(i + 1, i) for i in range(0, col_count, 2)]
    partner = lax.ppermute(own_pair, "cols", pairs)
    queries = query(info, normed, cosine, sine, query_refs)
    if fast:
        fars.append(send_far(after(shard_blocks[0], seconds[0], partner, queries)))
    heads = attention(info, queries, own_pair, partner)
    residual, normed_two = out_projection(info, heads, tokens, experts_scale, out_refs)

    if fast:
        beside, across = flip(normed_two, 2), flip(normed_two, 4)
        beside_in = flip(normed_two, 1)
        gather_expert(fars[0], normed_two)
        grad_all = after(grad_all, normed_two)
    else:
        rows_all = lax.all_gather(normed_two, "rows", axis=0)
    grad_rows = pick_rows(near_rows, chosen, grad_all, local_experts)

    def place_block(q, block, picked):
        return dispatch(
            q, near_rows, info, block, chosen, routes_all, router_cols, local_experts, picked
        )

    if fast:
        half = TOK_DEV // 2
        picked = place_block(0, normed_two, None)
        picked = place_block(1, beside_in, picked)
        beside, across = after((beside, across), picked, grad_rows, *nears[1])
        corner = [flip(beside[:half], 4), flip(across[half:], 2)]
        picked = place_block(2, beside, picked)
        picked = place_block(4, across, picked)
        beside_in = flip(beside, 1)
        across_in = flip(after(across, beside_in), 1)
        picked = place_block(3, beside_in, picked)
        picked = place_block(5, across_in, picked)
        corner = jnp.concatenate(after(corner, picked), axis=0)
        corner_in = flip(corner, 1)
        picked = place_block(6, corner, picked)
        picked = place_block(7, corner_in, picked)
        fars.append(send_far(after(shard_blocks[1], seconds[1], picked)))
        expert_refs = [
            [shard_blocks[i], seconds[i], *nears[i], fars[i]] for i in range(local_experts)
        ]
    else:
        picked = None
        for q in range(row_count):
            picked = place_block(q, rows_all[q], picked)
    height = row_count * capacity
    token_rows = [a.reshape(height, D) for a in picked[:local_experts]]
    grad_rows = [a.reshape(height, D) for a in grad_rows]
    share_rows = [a.reshape(height, 1) for a in picked[local_experts:]]

    out_rows, back_rows, gate_dots, reduced, marks = ([], [], [], [], [])
    grad_slots = []
    for e in range(local_experts):
        rows_in = token_rows[e]
        if fast and e == 0:
            rows_in = after(rows_in, seconds[1])
        if fast and e == 1:
            rows_in = after(rows_in, fars[1], second, fourth, own_slot, third)
        out_row, back_row, grad_row, acts, dots = expert(
            info, rows_in, grad_rows[e], share_rows[e], expert_refs[e], col_count
        )
        out_rows.append(out_row.reshape(row_count, capacity, D))
        back_rows.append(back_row.reshape(row_count, capacity, D))
        gate_dots.append(dots.reshape(row_count, capacity, 1))
        if fast:
            if e == 1:
                back_rows = after(back_rows, marks[0][0])
                got = flip(combine(chosen, back_rows, 1, 2), 1)
                acts = after(acts, got)
            second, fourth = expert_grads(acts, token_rows[e], grad_row, (1, 3))
            if e == 0:
                relay, _ = reduce_first(second, fourth, chain=True)
                marks.append((relay,))
            own_slot, third = expert_grads(acts, token_rows[e], grad_row, (0, 2))
            grad_slots.append((own_slot, second, third, fourth))
        else:
            slots = expert_grads(acts, token_rows[e], grad_row, tuple(range(col_count)))
            reduced.append(
                lax.psum_scatter(jnp.stack(slots), "cols", scatter_dimension=0).astype(WIDE)
            )

    spread_dots = spread(place_rows, gate_dots)
    if fast:
        spread_dots = jnp.take(spread_dots, near_rows, axis=0)
    grad_shares = lax.all_to_all(spread_dots, "rows", split_axis=0, concat_axis=0, tiled=True)
    grad_shares = grad_shares.reshape(expert_total, TOK_DEV)
    if fast:
        back_keep = combine(chosen, back_rows, 0, 2)
        sent_second = reduce_second(grad_slots[0][2], grad_slots[0][3], marks[0][0])
        far_back = lax.ppermute(
            after(grad_slots[0][3], *sent_second, *grad_slots[1], spread_dots), "cols", FAR
        )
        reduced.append((grad_slots[0][0], (marks[0][0], far_back), sent_second))
        back_first = chips_first(back_keep, got)
        back_parts = chips_second(back_keep, got, *send_chips(back_first))
        out_rows = [after(a, *back_first) for a in out_rows]
        out_got = flip(combine(chosen, out_rows, 1, 2), 1)
        out_keep = combine(chosen, out_rows, 0, 2)
        relay, _ = reduce_first(
            after(grad_slots[1][1], far_back, back_parts[2], back_parts[5]), fourth, chain=True
        )
        marks.append((relay,))
        grad_shares = after(grad_shares, own_slot, third, out_keep, out_got, far_back)
    else:

        def summed(rows):
            part = combine(chosen, rows, 0, 1)
            return (lax.psum_scatter(part, "rows", scatter_dimension=0).astype(WIDE),)

        back_parts = summed(back_rows)
        mixture = summed(out_rows)

    grad_residual, grad_branch, grad_heads, experts_gain_grad, router_grad = branch_back(
        info,
        residual,
        normed_two,
        back_parts,
        cotangent,
        routes.T,
        grad_shares,
        router_rows,
        experts_scale,
        out_refs,
    )
    if fast:
        out_first = chips_first(out_keep, out_got)
        out_flips = send_chips(out_first)
        grad_heads = after(grad_heads, *out_first)
        router_parts = jnp.transpose(
            router_grad.astype(LOW).reshape(col_count, router_part, row_count, depth),
            (2, 0, 1, 3),
        ).reshape(row_count * col_count, router_part, depth)
        gain_rows = experts_gain_grad.astype(LOW).reshape(row_count * col_count, 1, gain_part)
        extra = jnp.concatenate(
            [
                jnp.pad(router_parts, ((0, 0), (0, 0), (0, wide - depth))),
                jnp.pad(gain_rows, ((0, 0), (0, 0), (0, wide - gain_part))),
                jnp.zeros((row_count * col_count, EXTRA - router_part - 1, wide), LOW),
            ],
            axis=1,
        )
    grad_query, own_grad, source_grad = attention_back(
        info, queries, own_pair, partner, grad_heads, cosine, sine
    )
    arrived = lax.ppermute(source_grad.astype(LOW), "cols", [(j, i) for i, j in pairs])
    grad_pair = join_grads(info, own_grad, source_grad, arrived, cosine, sine)
    if fast:
        grad_branch = after(grad_branch, marks[1][0], *out_flips)
        keep, send = weight_grads(
            info,
            [normed, heads],
            [grad_query, grad_pair, grad_branch],
            ((0, 2, query_part), (0, 3, 2 * key_part), (1, 4, query_part)),
            extra,
        )
        sent = flip(send, 1)
        sent_second = reduce_second(grad_slots[1][2], grad_slots[1][3], marks[1][0])
        grad_pair = after(grad_pair, keep)
    tokens_grad, attention_gain_grad = token_back(
        info, grad_query, grad_pair, tokens, grad_residual, attention_scale, query_refs, pair_refs
    )

    if fast:
        far_back = lax.ppermute(after(grad_slots[1][3], *sent_second, tokens_grad), "cols", FAR)
        reduced.append((grad_slots[1][0], (marks[1][0], far_back), sent_second))
        mixture = chips_second(out_keep, out_got, *out_flips)
        sent_chips = send_chips(chips_first(keep, sent))
        slots = sum_parts(chips_second(keep, sent, *sent_chips))
        width = query_part + 2 * key_part
        gain_sums = sum(
            jnp.sum(own[i, :depth, :width].astype(WIDE) * slots[i, :depth, :width], axis=1)
            for i in range(4)
        )
        own_gains = lax.dynamic_slice_in_dim(attention_scale[0], row_place * depth, depth, 0)
        gain_sums = (gain_sums / own_gains).reshape(col_count, 1, gain_part)
        gain_sums = jnp.pad(
            jnp.take(gain_sums, shards, axis=0),
            ((0, 0), (depth + router_part + 1, EXTRA - router_part - 2), (0, wide - gain_part)),
        )
        slots = (slots + gain_sums).astype(LOW)

        def cols_sum(slots):
            sent_first = reduce_first(slots[1], slots[3])
            sent_second = reduce_second(slots[2], slots[3], sent_first[0])
            return reduce_last(slots[0], sent_first, sent_second)

        sums = cols_sum(slots)
        expert_sums = [reduce_last(*parts) for parts in reduced]
        router_sum = sums[depth : depth + router_part, :depth].T
        experts_gain_sum = sums[depth + router_part, :gain_part]
        attention_gain_sum = sums[depth + router_part + 1, :gain_part]
        sums = sums[:depth]
    else:
        full_grads = [
            tn(normed, grad_query),
            *jnp.moveaxis(tn(normed, grad_pair).reshape(D, QUARTERS, 2, -1), 2, 0),
            tn(heads, grad_branch),
        ]
        packed_grad = jnp.concatenate(
            [
                grad.astype(LOW).reshape(row_count, depth, col_count, -1)
                for grad in full_grads
            ],
            axis=3,
        )
        row_sums = lax.psum_scatter(packed_grad, "rows", scatter_dimension=0)
        sums = lax.psum_scatter(row_sums, "cols", scatter_dimension=1).astype(WIDE)
        expert_sums = reduced
        small_grads = jnp.concatenate(
            [
                attention_gain_grad.reshape(-1, gain_part),
                experts_gain_grad.reshape(-1, gain_part),
                jnp.transpose(
                    router_grad.reshape(col_count, router_part, row_count, depth), (2, 0, 3, 1)
                ).reshape(row_count * col_count, depth * router_part),
            ],
            axis=1,
        )
        small_grads = small_grads.reshape(row_count, -1)
        small_grads = lax.all_to_all(small_grads, "rows", split_axis=0, concat_axis=0, tiled=True)
        small_grads = jnp.sum(small_grads, axis=0).reshape(col_count, -1)
        small_grads = lax.all_to_all(small_grads, "cols", split_axis=0, concat_axis=0, tiled=True)
        small_sums = jnp.sum(small_grads, axis=0)
        attention_gain_sum = small_sums[:gain_part]
        experts_gain_sum = small_sums[gain_part : 2 * gain_part]
        router_sum = small_sums[2 * gain_part :].reshape(depth, router_part)

    layer_output = (residual + sum_parts(mixture)).astype(LOW)
    key_at = query_part
    value_at = key_at + key_part
    out_at = value_at + key_part
    part = down_weight.shape[1]
    gate_grad, upward_grad, down_grad = (
        jnp.stack([sums_of[which * part : (which + 1) * part] for sums_of in expert_sums])
        for which in range(3)
    )
    return (
        layer_output,
        tokens_grad,
        sums[:, :key_at],
        sums[:, key_at:value_at],
        sums[:, value_at:out_at],
        sums[:, out_at:],
        router_sum,
        attention_gain_sum,
        experts_gain_sum,
        jnp.swapaxes(gate_grad, 1, 2),
        jnp.swapaxes(upward_grad, 1, 2),
        down_grad,
    )


def solution(mesh):
    in_specs = (
        P(("rows", "cols"), None),
        P("rows", "cols"),
        P("rows", "cols"),
        P("rows", "cols"),
        P("rows", "cols"),
        P("rows", "cols"),
        P(("rows", "cols")),
        P(("rows", "cols")),
        P("rows", None, "cols"),
        P("rows", None, "cols"),
        P("rows", "cols", None),
        P(("rows", "cols"), None),
        P(),
        P(("rows", "cols"), None),
    )
    out_specs = (
        P(("rows", "cols"), None),
        P(("rows", "cols"), None),
        P("rows", "cols"),
        P("rows", "cols"),
        P("rows", "cols"),
        P("rows", "cols"),
        P("rows", "cols"),
        P(("rows", "cols")),
        P(("rows", "cols")),
        P("rows", None, "cols"),
        P("rows", None, "cols"),
        P("rows", "cols", None),
    )
    return jax.shard_map(
        on_device, mesh=mesh, in_specs=in_specs, out_specs=out_specs, check_vma=False
    )
```

```python
import functools

import jax
import jax.numpy as jnp
from jax import lax
from jax.experimental import pallas as pl
from jax.experimental.pallas import tpu as pltpu
from jax.sharding import PartitionSpec as P

D = 1536
HEADS = 12
KV_HEADS = 2
HEAD_DIM = 128
TOP = 4
TOK_DEV = 512
BRANCHES = 4
LEAVES = 8
TRUNK = 256
BRANCH = 64

EPSILON = 1e-06
ROPE_BASE = 10000.0
MASKED = -1e30
LOW = jnp.bfloat16
WIDE = jnp.float32
KEY_WIDTH = KV_HEADS * HEAD_DIM
GROUP = HEADS // KV_HEADS
QUARTERS = 4
VMEM_LIMIT = 56 * 1024 * 1024

ANY = pl.BlockSpec(memory_space=pl.ANY)
SMEM = pl.BlockSpec(memory_space=pltpu.SMEM)


def nn(one, two):
    return lax.dot_general(one, two, (((1,), (0,)), ((), ())), preferred_element_type=WIDE)


def nt(one, two):
    return lax.dot_general(one, two, (((1,), (1,)), ((), ())), preferred_element_type=WIDE)


def tn(one, two):
    return lax.dot_general(one, two, (((0,), (0,)), ((), ())), preferred_element_type=WIDE)


def whole(shape):
    return pl.BlockSpec(shape, lambda *_: (0,) * len(shape))


LITTLE = pl.CostEstimate(flops=1, bytes_accessed=1, transcendentals=0)


def params():
    return pltpu.CompilerParams(vmem_limit_bytes=VMEM_LIMIT)


def turn(values, cosine, sine):
    return values * cosine + pltpu.roll(values, HEAD_DIM // 2, 1) * sine


def turn_back(values, cosine, sine):
    return values * cosine - pltpu.roll(values, HEAD_DIM // 2, 1) * sine


PIECES = (
    ((0, 0), (2, 0), (4, 0), (6, 0)),
    ((1, 0), (3, 0), (5, 0), (7, 0)),
    ((0, 1), (0, 2), (0, 3)),
    ((2, 1), (2, 2), (2, 3)),
    ((4, 1), (4, 2), (4, 3)),
    ((6, 1),),
    ((6, 2), (6, 3)),
    ((1, 1), (1, 2), (1, 3)),
    ((3, 1), (3, 2), (3, 3), (5, 1), (5, 2), (5, 3)),
    ((7, 1),),
    ((7, 2), (7, 3)),
)
EXTRA = 16


def weight_copies(info, refs, target, sem, start, width):
    if len(refs) == 1:
        return [pltpu.make_async_copy(refs[0], target, sem)]
    depth = refs[0].shape[1] - EXTRA
    copies = []
    for ref, parts in zip(refs, PIECES):
        for at, (flip_bits, slot) in enumerate(parts):
            row = pl.multiple_of((info[0] ^ flip_bits) * depth, depth)
            col = pl.multiple_of(info[2 + slot] * width, 128)
            copies.append(
                pltpu.make_async_copy(
                    ref.at[at, pl.ds(0, depth), pl.ds(start, width)],
                    target.at[pl.ds(row, depth), pl.ds(col, width)],
                    sem,
                )
            )
    return copies


def extras_kernel(info, *rest):
    refs, (out, sem) = rest[:-2], rest[-2:]
    depth = refs[0].shape[1] - EXTRA
    copies = []
    for ref, parts in zip(refs, PIECES):
        for at, (flip_bits, slot) in enumerate(parts):
            to = (info[0] ^ flip_bits) * QUARTERS + info[2 + slot]
            copies.append(pltpu.make_async_copy(ref.at[at, pl.ds(depth, EXTRA)], out.at[to], sem))
    run_all(copies)
    wait_all(copies)


def extras(info, refs):
    return pl.pallas_call(
        extras_kernel,
        out_shape=jax.ShapeDtypeStruct((8 * QUARTERS, EXTRA, refs[0].shape[2]), LOW),
        in_specs=[SMEM] + [ANY] * len(refs),
        out_specs=pl.BlockSpec(memory_space=pltpu.VMEM),
        scratch_shapes=[pltpu.SemaphoreType.DMA],
        compiler_params=params(),
        cost_estimate=LITTLE,
        name="extra_rows",
    )(info, *refs)


def run_all(copies):
    for copy in copies:
        copy.start()


def wait_all(copies):
    for copy in copies:
        copy.wait()


def key_value_kernel(info, tokens, gain, cosine, sine, *rest):
    count = len(rest) - 4
    refs, (normed, out, weight, sem) = rest[:count], rest[count:]
    copies = weight_copies(info, refs, weight, sem, D // QUARTERS, 128)
    run_all(copies)
    values = tokens[...].astype(WIDE)
    factor = lax.rsqrt(jnp.mean(values * values, axis=-1, keepdims=True) + EPSILON)
    low = (values * factor * gain[...]).astype(LOW)
    normed[...] = low
    wait_all(copies)
    both = nn(low, weight[...])
    half = HEAD_DIM // 2
    first = lax.broadcasted_iota(jnp.int32, (TOK_DEV, HEAD_DIM), 1) < half
    for g in range(KV_HEADS):
        one = both[:, 256 * g : 256 * g + 128]
        two = both[:, 256 * g + 128 : 256 * g + 256]
        key = jnp.where(first, one, pltpu.roll(two, half, 1))
        value = jnp.where(first, pltpu.roll(one, half, 1), two)
        out[:, 128 * g : 128 * g + 128] = turn(key, cosine[...], sine[...]).astype(LOW)
        out[:, KEY_WIDTH + 128 * g : KEY_WIDTH + 128 * g + 128] = value.astype(LOW)


def key_value(info, tokens, gain, cosine, sine, refs):
    return pl.pallas_call(
        key_value_kernel,
        out_shape=(
            jax.ShapeDtypeStruct((TOK_DEV, D), LOW),
            jax.ShapeDtypeStruct((TOK_DEV, 2 * KEY_WIDTH), LOW),
        ),
        in_specs=[SMEM] + [pl.BlockSpec(memory_space=pltpu.VMEM)] * 4 + [ANY] * len(refs),
        out_specs=(pl.BlockSpec(memory_space=pltpu.VMEM),) * 2,
        scratch_shapes=[pltpu.VMEM((D, 2 * KEY_WIDTH), LOW), pltpu.SemaphoreType.DMA],
        compiler_params=params(),
        cost_estimate=LITTLE,
        name="norm_key_value",
    )(info, tokens, gain, cosine, sine, *refs)


def query_kernel(info, normed, cosine, sine, *rest):
    count = len(rest) - 3
    refs, (out, weight, sem) = rest[:count], rest[count:]

    @pl.when(pl.program_id(0) == 0)
    def _():
        copies = weight_copies(info, refs, weight, sem, 0, D // QUARTERS)
        run_all(copies)
        wait_all(copies)

    at = pl.multiple_of(pl.program_id(0) * 256, 256)
    lin = nn(normed[...], weight[:, pl.ds(at, 256)])
    for h in range(2):
        out[:, 128 * h : 128 * h + 128] = turn(
            lin[:, 128 * h : 128 * h + 128], cosine[...], sine[...]
        ).astype(LOW)


def query(info, normed, cosine, sine, refs):
    return pl.pallas_call(
        query_kernel,
        grid=(D // 256,),
        out_shape=jax.ShapeDtypeStruct((TOK_DEV, D), LOW),
        in_specs=[SMEM, whole((TOK_DEV, D)), whole((TOK_DEV, 128)), whole((TOK_DEV, 128))]
        + [ANY] * len(refs),
        out_specs=pl.BlockSpec((TOK_DEV, 256), lambda i: (0, i)),
        scratch_shapes=[pltpu.VMEM((D, D), LOW), pltpu.SemaphoreType.DMA],
        compiler_params=params(),
        cost_estimate=LITTLE,
        name="query_projection",
    )(info, normed, cosine, sine, *refs)


KEYS = TRUNK + 2 * BRANCH
CHUNKS = TOK_DEV // BRANCH


def chunk_keys(info, source, own, column, chunk):
    at = pl.multiple_of(info[6 + chunk], BRANCH)
    rows = pl.multiple_of(chunk * BRANCH, BRANCH)
    columns = slice(column, column + HEAD_DIM)
    return jnp.concatenate(
        [
            source[0:TRUNK, columns],
            source[pl.ds(at, BRANCH), columns],
            own[pl.ds(rows, BRANCH), columns],
        ],
        axis=0,
    )


def chunk_allowed(info, chunk, query_axis, shape):
    query_row = lax.broadcasted_iota(jnp.int32, shape, query_axis) & (BRANCH - 1)
    key = lax.broadcasted_iota(jnp.int32, shape, 1 - query_axis)
    leaves = info[1] == 0
    trunk = jnp.logical_and(jnp.logical_not(leaves), chunk < TRUNK // BRANCH)
    limit = jnp.where(trunk, chunk * BRANCH + query_row, TRUNK - 1)
    branch_limit = jnp.where(leaves, TRUNK + BRANCH - 1, 0)
    own_limit = jnp.where(trunk, 0, query_row + TRUNK + BRANCH)
    top = jnp.where(key < TRUNK, limit, jnp.where(key < TRUNK + BRANCH, branch_limit, own_limit))
    return key <= top


def group_rows(ref, g):
    first = g * GROUP
    return jnp.concatenate(
        [ref[:, 128 * h : 128 * h + 128] for h in range(first, first + GROUP)], axis=0
    )


def keep_source(info, partner, own, source):
    @pl.when(pl.program_id(0) == 0)
    def _():
        @pl.when(info[1] == 0)
        def _():
            source[...] = partner[...]

        @pl.when(info[1] != 0)
        def _():
            source[...] = own[...]


def attention_kernel(info, queries, own, partner, out, source):
    keep_source(info, partner, own, source)
    chunk = pl.program_id(0)
    rows = GROUP * BRANCH
    allowed = chunk_allowed(info, chunk, 0, (rows, KEYS))
    for g in range(KV_HEADS):
        keys = chunk_keys(info, source, own, 128 * g, chunk)
        values = chunk_keys(info, source, own, KEY_WIDTH + 128 * g, chunk)
        scores = nt(group_rows(queries, g), keys) * HEAD_DIM**-0.5
        scores = jnp.where(allowed, scores, MASKED)
        weights = jnp.exp(scores - jnp.max(scores, axis=1, keepdims=True))
        total = jnp.sum(weights, axis=1, keepdims=True)
        mixed = nn((weights * (1.0 / total)).astype(LOW), values).astype(LOW)
        for h in range(GROUP):
            at = (g * GROUP + h) * 128
            out[:, at : at + 128] = mixed[h * BRANCH : (h + 1) * BRANCH]


def attention(info, queries, own, partner):
    return pl.pallas_call(
        attention_kernel,
        grid=(CHUNKS,),
        out_shape=jax.ShapeDtypeStruct((TOK_DEV, D), LOW),
        in_specs=[
            SMEM,
            pl.BlockSpec((BRANCH, D), lambda i: (i, 0)),
            whole((TOK_DEV, 2 * KEY_WIDTH)),
            whole((TOK_DEV, 2 * KEY_WIDTH)),
        ],
        out_specs=pl.BlockSpec((BRANCH, D), lambda i: (i, 0)),
        scratch_shapes=[pltpu.VMEM((TOK_DEV, 2 * KEY_WIDTH), LOW)],
        compiler_params=params(),
        cost_estimate=LITTLE,
        name="tree_attention",
    )(info, queries, own, partner)


def attention_back_kernel(
    info, queries, own, partner, grads, cosine, sine, grad_query, own_grad, source_grad, source
):
    keep_source(info, partner, own, source)
    chunk = pl.program_id(0)

    @pl.when(chunk == 0)
    def _():
        source_grad[...] = jnp.zeros_like(source_grad)

    rows = GROUP * BRANCH
    scale = HEAD_DIM**-0.5
    allowed = chunk_allowed(info, chunk, 1, (KEYS, rows))
    at = pl.multiple_of(info[6 + chunk], BRANCH)
    for g in range(KV_HEADS):
        keys = chunk_keys(info, source, own, 128 * g, chunk)
        values = chunk_keys(info, source, own, KEY_WIDTH + 128 * g, chunk)
        query_rows = group_rows(queries, g)
        grad_rows = group_rows(grads, g)
        scores = jnp.where(allowed, nt(keys, query_rows) * scale, MASKED)
        weights = jnp.exp(scores - jnp.max(scores, axis=0, keepdims=True))
        probs = weights * (1.0 / jnp.sum(weights, axis=0, keepdims=True))
        grad_probs = nt(values, grad_rows)
        mean = jnp.sum(probs * grad_probs, axis=0, keepdims=True)
        grad_scores = (probs * (grad_probs - mean)).astype(LOW)
        grad_values = nn(probs.astype(LOW), grad_rows)
        grad_keys = nn(grad_scores, query_rows) * scale
        grad_queries = tn(grad_scores, keys) * scale
        for h in range(GROUP):
            to = (g * GROUP + h) * 128
            grad_query[:, to : to + 128] = turn_back(
                grad_queries[h * BRANCH : (h + 1) * BRANCH], cosine[...], sine[...]
            ).astype(LOW)
        for column, grad in ((128 * g, grad_keys), (KEY_WIDTH + 128 * g, grad_values)):
            columns = slice(column, column + 128)
            source_grad[0:TRUNK, columns] += grad[0:TRUNK]
            source_grad[pl.ds(at, BRANCH), columns] += grad[TRUNK : TRUNK + BRANCH]
            own_grad[:, columns] = grad[TRUNK + BRANCH :]


def attention_back(info, queries, own, partner, grads, cosine, sine):
    chunked = pl.BlockSpec((BRANCH, D), lambda i: (i, 0))
    pair = (TOK_DEV, 2 * KEY_WIDTH)
    return pl.pallas_call(
        attention_back_kernel,
        grid=(CHUNKS,),
        out_shape=(
            jax.ShapeDtypeStruct((TOK_DEV, D), LOW),
            jax.ShapeDtypeStruct(pair, WIDE),
            jax.ShapeDtypeStruct(pair, WIDE),
        ),
        in_specs=[
            SMEM,
            chunked,
            whole(pair),
            whole(pair),
            chunked,
            pl.BlockSpec((BRANCH, 128), lambda i: (i, 0)),
            pl.BlockSpec((BRANCH, 128), lambda i: (i, 0)),
        ],
        out_specs=(
            chunked,
            pl.BlockSpec((BRANCH, 2 * KEY_WIDTH), lambda i: (i, 0)),
            whole(pair),
        ),
        scratch_shapes=[pltpu.VMEM(pair, LOW)],
        compiler_params=params(),
        cost_estimate=LITTLE,
        name="tree_attention_back",
    )(info, queries, own, partner, grads, cosine, sine)


def out_kernel(info, heads, tokens, gain, *rest):
    count = len(rest) - 4
    refs, (residual, normed, weight, sem) = rest[:count], rest[count:]

    @pl.when(pl.program_id(0) == 0)
    def _():
        copies = weight_copies(info, refs, weight, sem, D // QUARTERS + 128, D // QUARTERS)
        run_all(copies)
        wait_all(copies)

    at = pl.ds(pl.multiple_of(pl.program_id(0) * 256, 256), 256)
    residual[:, at] = tokens[:, at].astype(WIDE) + nn(heads[...], weight[:, at])

    @pl.when(pl.program_id(0) == pl.num_programs(0) - 1)
    def _():
        values = residual[...]
        factor = lax.rsqrt(jnp.mean(values * values, axis=-1, keepdims=True) + EPSILON)
        normed[...] = (values * factor * gain[...]).astype(LOW)


def out_projection(info, heads, tokens, gain, refs):
    full = (TOK_DEV, D)
    return pl.pallas_call(
        out_kernel,
        grid=(D // 256,),
        out_shape=(jax.ShapeDtypeStruct(full, WIDE), jax.ShapeDtypeStruct(full, LOW)),
        in_specs=[SMEM, whole(full), whole(full), whole((1, D))] + [ANY] * len(refs),
        out_specs=(whole(full), whole(full)),
        scratch_shapes=[pltpu.VMEM((D, D), LOW), pltpu.SemaphoreType.DMA],
        compiler_params=params(),
        cost_estimate=LITTLE,
        name="out_projection",
    )(info, heads, tokens, gain, *refs)


def hits_of(routes, ids):
    hit = ids == routes[0, 0:1]
    for k in range(1, TOP):
        hit = jnp.logical_or(hit, ids == routes[0, k : k + 1])
    return hit


def tables_kernel(capacity, local, total, order, info, routes, chosen_out, place_out, earlier):
    @pl.when(pl.program_id(0) == 0)
    def _():
        one = lax.broadcasted_iota(jnp.int32, (TOK_DEV, TOK_DEV), 0)
        two = lax.broadcasted_iota(jnp.int32, (TOK_DEV, TOK_DEV), 1)
        earlier[...] = jnp.where(one < two, 1.0, 0.0).astype(LOW)

    ids = lax.broadcasted_iota(jnp.int32, (total, TOK_DEV), 0)
    hit = hits_of(routes, ids)
    rank = nn(jnp.where(hit, 1.0, 0.0).astype(LOW), earlier[...])
    place = jnp.where(hit, rank, -1.0)
    spots = lax.broadcasted_iota(jnp.int32, (capacity, TOK_DEV), 0).astype(WIDE)
    place_out[0] = jnp.full(place_out.shape[1:], -1.0, WIDE)
    for e in range(local):
        mine = ids == info[0] * local + e
        place_row = jnp.sum(jnp.where(mine, place, 0.0), axis=0, keepdims=True)
        place_out[0, e : e + 1] = place_row
        chosen_out[0, e * capacity : (e + 1) * capacity] = jnp.where(
            spots == place_row, 1.0, 0.0
        ).astype(LOW)


def tables(order, info, routes, capacity, local, total):
    count = routes.shape[0]
    return pl.pallas_call(
        functools.partial(tables_kernel, capacity, local, total),
        grid_spec=pltpu.PrefetchScalarGridSpec(
            num_scalar_prefetch=2,
            grid=(count,),
            in_specs=[pl.BlockSpec((1, TOP, TOK_DEV), lambda i, order, info: (order[i], 0, 0))],
            out_specs=[
                pl.BlockSpec((1, local * capacity, TOK_DEV), lambda i, order, info: (i, 0, 0)),
                pl.BlockSpec((1, 8, TOK_DEV), lambda i, order, info: (i, 0, 0)),
            ],
            scratch_shapes=[pltpu.VMEM((TOK_DEV, TOK_DEV), LOW)],
        ),
        out_shape=[
            jax.ShapeDtypeStruct((count, local * capacity, TOK_DEV), LOW),
            jax.ShapeDtypeStruct((count, 8, TOK_DEV), WIDE),
        ],
        compiler_params=params(),
        cost_estimate=LITTLE,
        name="route_tables",
    )(order, info, routes)


def pick_kernel(local, order, chosen, blocks, *outs):
    rows_of = nn(chosen[0], blocks[0]).astype(LOW)
    capacity = outs[0].shape[1]
    for e in range(local):
        outs[e][0] = rows_of[e * capacity : (e + 1) * capacity]


def pick_rows(order, chosen, blocks, local):
    count, height, _ = chosen.shape
    capacity = height // local
    return pl.pallas_call(
        functools.partial(pick_kernel, local),
        grid_spec=pltpu.PrefetchScalarGridSpec(
            num_scalar_prefetch=1,
            grid=(count,),
            in_specs=[
                pl.BlockSpec((1, height, TOK_DEV), lambda i, order: (i, 0, 0)),
                pl.BlockSpec((1, TOK_DEV, D), lambda i, order: (order[i], 0, 0)),
            ],
            out_specs=[pl.BlockSpec((1, capacity, D), lambda i, order: (i, 0, 0))] * local,
        ),
        out_shape=[jax.ShapeDtypeStruct((count, capacity, D), LOW)] * local,
        compiler_params=params(),
        cost_estimate=LITTLE,
        name="pick_rows",
    )(order, chosen, blocks)


def dispatch_kernel(local, near, info, rows, chosen, routes, router, *rest):
    outs, logits = rest[2 * local : 4 * local], rest[-1]
    total = router.shape[1]
    step = pl.program_id(0)
    block = rows[...]
    rows_of = nn(chosen[0], block).astype(LOW)
    capacity = outs[0].shape[1]
    for e in range(local):
        outs[e][0] = rows_of[e * capacity : (e + 1) * capacity]
    part = nn(block, router[...])

    @pl.when(step == 0)
    def _():
        logits[...] = part

    @pl.when(step > 0)
    def _():
        logits[...] += part

    @pl.when(step == pl.num_programs(0) - 1)
    def _():
        values = logits[...].T
        ids = lax.broadcasted_iota(jnp.int32, (total, TOK_DEV), 0)
        weights = jnp.exp(values - jnp.max(values, axis=0, keepdims=True))
        hit = hits_of(routes, ids)
        share = weights / jnp.sum(jnp.where(hit, weights, 0.0), axis=0, keepdims=True)
        for e in range(local):
            mine = ids == info[0] * local + e
            share_row = jnp.sum(jnp.where(mine, share, 0.0), axis=0, keepdims=True)
            picked = chosen[0, e * capacity : (e + 1) * capacity].astype(WIDE)
            outs[local + e][0] = jnp.sum(picked * share_row, axis=1, keepdims=True)


def dispatch(at, near, info, rows, chosen, routes, router, local, earlier):
    count, height, _ = chosen.shape
    capacity = height // local
    total = router.shape[1]
    wide = 512
    out_shape = [jax.ShapeDtypeStruct((count, capacity, D), LOW)] * local + [
        jax.ShapeDtypeStruct((count, capacity, 1), WIDE)
    ] * local
    if earlier is None:
        earlier = [jnp.zeros((8, 128), shape.dtype) for shape in out_shape]
        aliases = {}
    else:
        aliases = {6 + i: i for i in range(len(out_shape))}
    return pl.pallas_call(
        functools.partial(dispatch_kernel, local),
        grid_spec=pltpu.PrefetchScalarGridSpec(
            num_scalar_prefetch=2,
            grid=(D // wide,),
            in_specs=[
                pl.BlockSpec((TOK_DEV, wide), lambda i, near, info: (0, i)),
                pl.BlockSpec((1, height, TOK_DEV), lambda i, near, info: (at, 0, 0)),
                pl.BlockSpec((1, TOP, TOK_DEV), lambda i, near, info: (near[at], 0, 0)),
                pl.BlockSpec((wide, total), lambda i, near, info: (i, 0)),
            ]
            + [ANY] * len(out_shape),
            out_specs=[
                pl.BlockSpec((1, capacity, wide), lambda i, near, info: (at, 0, i))
            ]
            * local
            + [pl.BlockSpec((1, capacity, 1), lambda i, near, info: (at, 0, 0))] * local,
            scratch_shapes=[pltpu.VMEM((TOK_DEV, total), WIDE)],
        ),
        out_shape=out_shape,
        input_output_aliases=aliases,
        compiler_params=params(),
        cost_estimate=LITTLE,
        name="dispatch",
    )(near, info, rows, chosen, routes, router, *earlier)


def spread_kernel(local, place, *rest):
    dots, out = rest[:local], rest[local]
    spots = lax.broadcasted_iota(jnp.int32, (dots[0].shape[1], TOK_DEV), 0).astype(WIDE)
    for e in range(local):
        chosen = spots == place[0, e : e + 1]
        out[0, e : e + 1] = jnp.sum(jnp.where(chosen, dots[e][0], 0.0), axis=0, keepdims=True)


def spread(place, dots):
    count, capacity, _ = dots[0].shape
    local = len(dots)
    return pl.pallas_call(
        functools.partial(spread_kernel, local),
        grid=(count,),
        out_shape=jax.ShapeDtypeStruct((count, local, TOK_DEV), WIDE),
        in_specs=[pl.BlockSpec((1, 8, TOK_DEV), lambda i: (i, 0, 0))]
        + [pl.BlockSpec((1, capacity, 1), lambda i: (i, 0, 0))] * local,
        out_specs=pl.BlockSpec((1, local, TOK_DEV), lambda i: (i, 0, 0)),
        compiler_params=params(),
        cost_estimate=LITTLE,
        name="spread",
    )(place, *dots)


def expert_kernel(slots, info, rows, grads, shares, *rest):
    count = len(rest) - 7
    refs = rest[:count]
    out_rows, back_rows, grad_rows, acts, dots, weight, sem = rest[count:]
    part = weight.shape[1] // slots

    @pl.when(pl.program_id(0) == 0)
    def _():
        def copies(ref, slot):
            return [
                pltpu.make_async_copy(
                    ref.at[pl.ds(which * part, part)],
                    weight.at[which, pl.ds(slot * part, part)],
                    sem,
                )
                for which in range(3)
            ]

        if count == slots:
            for slot in range(slots):
                run_all(copies(refs[slot], slot))
        else:
            block, second, above, below, far = refs
            low_end = info[2] == 0
            end = jnp.logical_or(low_end, info[2] == 3)
            run_all(copies(block, 0))
            run_all(copies(second, 1))

            @pl.when(low_end)
            def _():
                run_all(copies(above, 2))

            @pl.when(jnp.logical_not(low_end))
            def _():
                run_all(copies(below, 2))

            @pl.when(end)
            def _():
                run_all(copies(far, 3))

            @pl.when(jnp.logical_not(end))
            def _():
                run_all(copies(above, 3))

        for slot in range(slots):
            wait_all(copies(refs[0], slot))

    row_block = rows[...]
    share = shares[...]
    grad_float = grads[...].astype(WIDE)
    grad_low = (share * grad_float).astype(LOW)
    grad_rows[...] = grad_low
    gate_act = nt(row_block, weight[0])
    upward = nt(row_block, weight[1])
    sigmoid = 1.0 / (1.0 + jnp.exp(-gate_act))
    silu = gate_act * sigmoid
    hidden = (silu * upward).astype(LOW)
    expert_out = nn(hidden, weight[2]).astype(LOW).astype(WIDE)
    out_rows[...] = (share * expert_out).astype(LOW)
    dots[...] = jnp.sum(grad_float * expert_out, axis=1, keepdims=True)
    grad_hidden = nt(grad_low, weight[2])
    grad_gate = (grad_hidden * upward * sigmoid * (1.0 + gate_act * (1.0 - sigmoid))).astype(LOW)
    grad_up = (grad_hidden * silu).astype(LOW)
    back_rows[...] = (nn(grad_gate, weight[0]) + nn(grad_up, weight[1])).astype(LOW)
    for which, act in enumerate((grad_gate, grad_up, hidden)):
        turned = act.T
        for slot in range(slots):
            acts[slot, which * part : (which + 1) * part] = turned[
                slot * part : (slot + 1) * part
            ]


EXPERT_ROWS = 256


def expert(info, rows, grads, shares, refs, slots):
    height = rows.shape[0]
    part = refs[0].shape[0] // 3
    wide_block = pl.BlockSpec((EXPERT_ROWS, D), lambda i: (i, 0))
    thin_block = pl.BlockSpec((EXPERT_ROWS, 1), lambda i: (i, 0))
    return pl.pallas_call(
        functools.partial(expert_kernel, slots),
        grid=(height // EXPERT_ROWS,),
        out_shape=[jax.ShapeDtypeStruct((height, D), LOW)] * 3
        + [
            jax.ShapeDtypeStruct((slots, 3 * part, height), LOW),
            jax.ShapeDtypeStruct((height, 1), WIDE),
        ],
        in_specs=[SMEM, wide_block, wide_block, thin_block] + [ANY] * len(refs),
        out_specs=[wide_block] * 3
        + [pl.BlockSpec((slots, 3 * part, EXPERT_ROWS), lambda i: (0, 0, i)), thin_block],
        scratch_shapes=[pltpu.VMEM((3, slots * part, D), LOW), pltpu.SemaphoreType.DMA],
        compiler_params=params(),
        cost_estimate=LITTLE,
        name="expert",
    )(info, rows, grads, shares, *refs)


def expert_grads_kernel(slots, rows, grads, *rest):
    acts, outs = rest[: len(slots)], rest[len(slots) :]
    part = acts[0].shape[1] // 3
    for act, out in zip(acts, outs):
        out[: 2 * part, :] = nn(act[0, : 2 * part], rows[...]).astype(LOW)
        out[2 * part :, :] = nn(act[0, 2 * part :], grads[...]).astype(LOW)


def expert_grads(acts, rows, grads, slots):
    _, part, height = acts.shape
    return pl.pallas_call(
        functools.partial(expert_grads_kernel, slots),
        grid=(D // 256,),
        out_shape=[jax.ShapeDtypeStruct((part, D), LOW) for _ in slots],
        in_specs=[pl.BlockSpec((height, 256), lambda i: (0, i))] * 2
        + [pl.BlockSpec((1, part, height), lambda i, s=slot: (s, 0, 0)) for slot in slots],
        out_specs=[pl.BlockSpec((part, 256), lambda i: (0, i)) for _ in slots],
        compiler_params=params(),
        cost_estimate=LITTLE,
        name="expert_gradients",
    )(rows, grads, *[acts] * len(slots))


SHARE_ROWS = 32


def combine_kernel(local, info, chosen, *rest):
    rows, dots, out = rest[:local], rest[local:-1], rest[-1]
    both = jnp.concatenate([ref[0] for ref in rows], axis=0)
    out[0, :TOK_DEV] = tn(chosen[0], both).astype(LOW)
    if dots:
        capacity = rows[0].shape[1]
        row = lax.broadcasted_iota(jnp.int32, (SHARE_ROWS, D), 0)
        values = jnp.zeros((SHARE_ROWS, D), WIDE)
        for e in range(local):
            picked = chosen[0, e * capacity : (e + 1) * capacity].astype(WIDE)
            high, low = split(jnp.sum(picked * dots[e][0], axis=0, keepdims=True))
            pieces = [high.astype(WIDE), low.astype(WIDE)]
            pieces.append(jnp.zeros((1, D - 2 * TOK_DEV), WIDE))
            line = jnp.concatenate(pieces, axis=1)
            values = jnp.where(row == info[0] * local + e, line, values)
        out[0, TOK_DEV:] = values.astype(LOW)


def combine(info, chosen, rows, first, step, dots=()):
    count, capacity, _ = rows[0].shape
    number = (count - first + step - 1) // step
    height = TOK_DEV + (SHARE_ROWS if dots else 0)
    return pl.pallas_call(
        functools.partial(combine_kernel, len(rows)),
        grid=(number,),
        out_shape=jax.ShapeDtypeStruct((number, height, D), LOW),
        in_specs=[
            SMEM,
            pl.BlockSpec((1,) + chosen.shape[1:], lambda i: (first + step * i, 0, 0)),
        ]
        + [pl.BlockSpec((1, capacity, D), lambda i: (first + step * i, 0, 0))] * len(rows)
        + [pl.BlockSpec((1, capacity, 1), lambda i: (first + step * i, 0, 0))] * len(dots),
        out_specs=pl.BlockSpec((1, height, D), lambda i: (i, 0, 0)),
        compiler_params=params(),
        cost_estimate=LITTLE,
        name="combine",
    )(info, chosen, *rows, *dots)


def split(values):
    high = values.astype(LOW)
    return high, (values - high.astype(WIDE)).astype(LOW)


def norm_back(values, gain, grad):
    factor = lax.rsqrt(jnp.mean(values * values, axis=-1, keepdims=True) + EPSILON)
    scaled = gain * grad
    mean = jnp.mean(values * scaled, axis=-1, keepdims=True)
    grad_values = factor * scaled - values * (factor * factor * factor * mean)
    grad_gain = jnp.sum(grad * values * factor, axis=0, keepdims=True)
    return grad_values, grad_gain


def router_back(logits, routes, grad_shares):
    ids = lax.broadcasted_iota(jnp.int32, logits.shape, 0)
    hit = ids == routes[0:1]
    for k in range(1, TOP):
        hit = jnp.logical_or(hit, ids == routes[k : k + 1])
    weights = jnp.exp(logits - jnp.max(logits, axis=0, keepdims=True))
    probs = weights / jnp.sum(weights, axis=0, keepdims=True)
    chosen = jnp.sum(jnp.where(hit, probs, 0.0), axis=0, keepdims=True)
    grads = jnp.where(hit, grad_shares, 0.0)
    mean = jnp.sum(probs * grads, axis=0, keepdims=True) / chosen
    grad_probs = jnp.where(hit, (grads - mean) / chosen, 0.0)
    return probs * (grad_probs - jnp.sum(probs * grad_probs, axis=0, keepdims=True))


def branch_back_kernel(
    parts, info, residual, normed, cotangent, routes, router, gain, *rest
):
    sums, rest = rest[:parts], rest[parts:]
    experts = router.shape[0]
    count = len(rest) - 7
    refs = rest[:count]
    grad_residual, grad_branch, grad_heads, grad_gain, grad_router, weight, sem = rest[count:]

    @pl.when(pl.program_id(0) == 0)
    def _():
        copies = weight_copies(info, refs, weight, sem, D // QUARTERS + 128, D // QUARTERS)
        run_all(copies)
        logits = nt(router[...], normed[...])
        if parts == 2:
            back_sum, grad_shares = sums[0][...], sums[1][...]
        else:
            values = [ref[...].astype(WIDE) for ref in sums]
            upper = values[0] + values[1] + values[2]
            lower = values[3] + values[4] + values[5]
            last = lower.shape[0] - SHARE_ROWS
            shares = lower[last : last + experts]
            grad_shares = shares[:, :TOK_DEV] + shares[:, TOK_DEV : 2 * TOK_DEV]
            back_sum = jnp.concatenate([upper, lower[:last]], axis=0)
        high, low = split(router_back(logits, routes[...], grad_shares))
        grad_router[...] = nn(high, normed[...]) + nn(low, normed[...])
        grad_normed = tn(high, router[...]) + tn(low, router[...])
        grad_normed += back_sum
        grad_values, gain_grad = norm_back(residual[...], gain[...], grad_normed)
        grad_gain[...] = gain_grad
        total = cotangent[...].astype(WIDE) + grad_values
        grad_residual[...] = total
        grad_branch[...] = total.astype(LOW)
        wait_all(copies)

    at = pl.ds(pl.multiple_of(pl.program_id(0) * 256, 256), 256)
    grad_heads[...] = nt(grad_branch[...], weight[at, :]).astype(LOW)


def branch_back(info, residual, normed, sums, cotangent, routes, router, gain, refs):
    full = (TOK_DEV, D)
    total = router.shape[0]
    return pl.pallas_call(
        functools.partial(branch_back_kernel, len(sums)),
        grid=(D // 256,),
        out_shape=(
            jax.ShapeDtypeStruct(full, WIDE),
            jax.ShapeDtypeStruct(full, LOW),
            jax.ShapeDtypeStruct(full, LOW),
            jax.ShapeDtypeStruct((1, D), WIDE),
            jax.ShapeDtypeStruct((total, D), WIDE),
        ),
        in_specs=[SMEM]
        + [whole(full)] * 3
        + [whole((TOP, TOK_DEV)), whole((total, D)), whole((1, D))]
        + [whole(part.shape) for part in sums]
        + [ANY] * len(refs),
        out_specs=(
            whole(full),
            whole(full),
            pl.BlockSpec((TOK_DEV, 256), lambda i: (0, i)),
            whole((1, D)),
            whole((total, D)),
        ),
        scratch_shapes=[pltpu.VMEM((D, D), LOW), pltpu.SemaphoreType.DMA],
        compiler_params=params(),
        cost_estimate=LITTLE,
        name="experts_norm_back",
    )(info, residual, normed, cotangent, routes, router, gain, *sums, *refs)


def join_grads_kernel(info, own_grad, source_grad, arrived, cosine, sine, out):
    half = HEAD_DIM // 2
    first = lax.broadcasted_iota(jnp.int32, (TOK_DEV, HEAD_DIM), 1) < half
    leaves = info[1] == 0

    def total(column):
        columns = slice(column, column + 128)
        extra = source_grad[:, columns] + arrived[:, columns].astype(WIDE)
        return own_grad[:, columns] + jnp.where(leaves, 0.0, extra)

    for g in range(KV_HEADS):
        key = turn_back(total(128 * g), cosine[...], sine[...])
        value = total(KEY_WIDTH + 128 * g)
        out[:, 256 * g : 256 * g + 128] = jnp.where(
            first, key, pltpu.roll(value, half, 1)
        ).astype(LOW)
        out[:, 256 * g + 128 : 256 * g + 256] = jnp.where(
            first, pltpu.roll(key, half, 1), value
        ).astype(LOW)


def join_grads(info, own_grad, source_grad, arrived, cosine, sine):
    vmem = pl.BlockSpec(memory_space=pltpu.VMEM)
    return pl.pallas_call(
        join_grads_kernel,
        out_shape=jax.ShapeDtypeStruct((TOK_DEV, 2 * KEY_WIDTH), LOW),
        in_specs=[SMEM] + [vmem] * 5,
        out_specs=vmem,
        compiler_params=params(),
        cost_estimate=LITTLE,
        name="join_key_value_gradients",
    )(info, own_grad, source_grad, arrived, cosine, sine)


def token_back_kernel(info, grad_query, grad_pair, tokens, grad_residual, gain, *rest):
    count = (len(rest) - 6) // 2
    query_refs, pair_refs = rest[:count], rest[count : 2 * count]
    out, grad_gain, query_weight, pair_weight, grad_normed, sem = rest[2 * count :]

    @pl.when(pl.program_id(0) == 0)
    def _():
        copies = weight_copies(info, query_refs, query_weight, sem, 0, D // QUARTERS)
        copies += weight_copies(info, pair_refs, pair_weight, sem, D // QUARTERS, 128)
        run_all(copies)
        wait_all(copies)

    at = pl.ds(pl.multiple_of(pl.program_id(0) * 256, 256), 256)
    grad_normed[:, at] = nt(grad_query[...], query_weight[at, :]) + nt(
        grad_pair[...], pair_weight[at, :]
    )

    @pl.when(pl.program_id(0) == pl.num_programs(0) - 1)
    def _():
        grad_values, gain_grad = norm_back(
            tokens[...].astype(WIDE), gain[...], grad_normed[...]
        )
        grad_gain[...] = gain_grad
        out[...] = (grad_residual[...] + grad_values).astype(LOW)


def token_back(info, grad_query, grad_pair, tokens, grad_residual, gain, query_refs, pair_refs):
    full = (TOK_DEV, D)
    return pl.pallas_call(
        token_back_kernel,
        grid=(D // 256,),
        out_shape=(jax.ShapeDtypeStruct(full, LOW), jax.ShapeDtypeStruct((1, D), WIDE)),
        in_specs=[
            SMEM,
            whole(full),
            whole((TOK_DEV, 2 * KEY_WIDTH)),
            whole(full),
            whole(full),
            whole((1, D)),
        ]
        + [ANY] * (len(query_refs) + len(pair_refs)),
        out_specs=(whole(full), whole((1, D))),
        scratch_shapes=[
            pltpu.VMEM((D, D), LOW),
            pltpu.VMEM((D, 2 * KEY_WIDTH), LOW),
            pltpu.VMEM(full, WIDE),
            pltpu.SemaphoreType.DMA,
        ],
        compiler_params=params(),
        cost_estimate=LITTLE,
        name="token_gradient",
    )(info, grad_query, grad_pair, tokens, grad_residual, gain, *query_refs, *pair_refs)


def weight_grads_kernel(parts, info, *rest):
    ins, (keep, send) = rest[:-2], rest[-2:]
    depth = D // 8
    core = info[0] & 1
    chip = pl.program_id(0) ^ (info[0] >> 1)
    start = 0
    for strip_at, grads_at, width in parts:
        low = tn(ins[strip_at][...], ins[grads_at][...]).astype(LOW)
        columns = slice(start, start + width)
        start += width
        for slot in range(QUARTERS):
            for j in range(QUARTERS):

                @pl.when(info[2 + slot] == j)
                def _():
                    piece = low[:, j * width : (j + 1) * width]
                    upper, lower = piece[:depth], piece[depth:]
                    keep[0, slot, :depth, columns] = jnp.where(core == 0, upper, lower)
                    send[0, slot, :depth, columns] = jnp.where(core == 0, lower, upper)

    if keep.shape[2] > depth:
        extra = ins[-1]
        for slot in range(QUARTERS):
            to = info[2 + slot]
            keep[0, slot, depth:] = extra[(chip * 2 + core) * QUARTERS + to]
            send[0, slot, depth:] = extra[(chip * 2 + 1 - core) * QUARTERS + to]


def weight_grads(info, strips, grads, parts, extra):
    depth = D // 8
    width = sum(part[2] for part in parts)
    strip = pl.BlockSpec((TOK_DEV, 2 * depth), lambda i, info: (0, i ^ (info[0] >> 1)))
    more = [] if extra is None else [extra]
    shape = (4, QUARTERS, depth + EXTRA * len(more), width)
    out = pl.BlockSpec((1,) + shape[1:], lambda i, info: (i, 0, 0, 0))
    return pl.pallas_call(
        functools.partial(weight_grads_kernel, parts),
        grid_spec=pltpu.PrefetchScalarGridSpec(
            num_scalar_prefetch=1,
            grid=(4,),
            in_specs=[strip] * len(strips)
            + [
                pl.BlockSpec(a.shape, lambda i, info, n=a.ndim: (0,) * n)
                for a in (*grads, *more)
            ],
            out_specs=(out, out),
        ),
        out_shape=(jax.ShapeDtypeStruct(shape, LOW),) * 2,
        compiler_params=params(),
        cost_estimate=LITTLE,
        name="weight_gradients",
    )(info, *strips, *grads, *more)


def position_of(token_index):
    branch_place = TRUNK + (token_index - TRUNK) % BRANCH
    leaf_place = TRUNK + BRANCH + (token_index - TOK_DEV) % BRANCH
    return jnp.where(
        token_index < TRUNK, token_index, jnp.where(token_index < TOK_DEV, branch_place, leaf_place)
    )


def rotary_tables(positions):
    half_dim = HEAD_DIM // 2
    frequency = ROPE_BASE ** (-jnp.arange(half_dim, dtype=jnp.float32) / half_dim)
    angles = positions.astype(jnp.float32)[:, None] * frequency[None, :]
    cosine, sine = (jnp.cos(angles), jnp.sin(angles))
    return (
        jnp.concatenate([cosine, cosine], axis=1),
        jnp.concatenate([-sine, sine], axis=1),
    )


def after(values, *earlier):
    return lax.optimization_barrier((values, earlier))[0]


def fast_mesh():
    return lax.axis_size("rows") == 8 and lax.axis_size("cols") == 4


SLOT_SHARD = ((0, 2, 1, 3), (1, 3, 0, 2), (2, 0, 1, 3), (3, 1, 2, 0))
UP = [(0, 1), (1, 2), (2, 3)]
DOWN = [(1, 0), (2, 1), (3, 2)]
FAR = [(0, 3), (3, 0)]


def send_near(block):
    return lax.ppermute(block, "cols", DOWN), lax.ppermute(block, "cols", UP)


def send_far(block):
    return lax.ppermute(block, "cols", FAR)


def send_second(block, near):
    place = lax.axis_index("cols")
    above, below = near
    payload = jnp.where(place == 1, above, jnp.where(place == 2, below, block))
    return lax.ppermute(payload, "cols", [(3, 1), (1, 0), (0, 2), (2, 3)])


def slot_list(block, near, second, far):
    place = lax.axis_index("cols")
    above, below = near
    end = (place == 0) | (place == 3)
    return [
        block,
        second,
        jnp.where(place == 0, above, below),
        jnp.where(end, far, above),
    ]


def reduce_first(second, fourth, chain=False):
    relay = lax.ppermute(second, "cols", [(1, 3), (0, 1), (2, 0), (3, 2)])
    return relay, None if chain else lax.ppermute(fourth, "cols", FAR)


def reduce_second(third, fourth, relay):
    place = lax.axis_index("cols")
    relayed = relay.astype(WIDE)
    upward_load = (
        jnp.where(place == 0, third, fourth).astype(WIDE) + jnp.where(place == 1, relayed, 0.0)
    ).astype(LOW)
    downward_load = (third.astype(WIDE) + jnp.where(place == 2, relayed, 0.0)).astype(LOW)
    return (
        lax.ppermute(upward_load, "cols", UP),
        lax.ppermute(downward_load, "cols", DOWN),
    )


def reduce_last(own, first, second):
    place = lax.axis_index("cols")
    relay, far = first
    below, above = second
    end = (place == 0) | (place == 3)
    return (
        own.astype(WIDE)
        + below.astype(WIDE)
        + above.astype(WIDE)
        + jnp.where(end, relay.astype(WIDE) + far.astype(WIDE), 0.0)
    )


def flip(block, bit):
    count = lax.axis_size("rows")
    return lax.ppermute(block, "rows", [(i, i ^ bit) for i in range(count)])


def add_low(one, two):
    return (one.astype(WIDE) + two.astype(WIDE)).astype(LOW)


def chip_sums(keep, got, chips, part):
    return jnp.stack([add_low(keep[i][part], got[i][part]) for i in chips])


def halves(keep):
    half = keep.shape[1] // 2
    return slice(0, half), slice(half, None)


def chips_first(keep, got):
    one, two = halves(keep)
    return chip_sums(keep, got, (1, 3), one), chip_sums(keep, got, (2, 3), two)


def chips_second(keep, got, got_x, got_y):
    one, two = halves(keep)
    near_x = chip_sums(keep, got, (0, 2), one)
    near_y = chip_sums(keep, got, (0, 1), two)
    got_xy = flip(add_low(near_x[1], got_x[1]), 4)
    got_yx = flip(add_low(near_y[1], got_y[1]), 2)
    return (near_x[0], got_x[0], got_xy, near_y[0], got_y[0], got_yx)


def send_chips(sums):
    return flip(sums[0], 2), flip(sums[1], 4)


def sum_parts(parts):
    wide = [a.astype(WIDE) for a in parts]
    if len(wide) == 1:
        return wide[0]
    return jnp.concatenate([wide[0] + wide[1] + wide[2], wide[3] + wide[4] + wide[5]], axis=0)


def on_device(
    tokens,
    query_weight,
    key_weight,
    value_weight,
    out_weight,
    router_weight,
    attention_gain,
    experts_gain,
    gate_weight,
    upward_weight,
    down_weight,
    routes,
    leaf_parent,
    cotangent,
):
    row_count = lax.axis_size("rows")
    col_count = lax.axis_size("cols")
    row_place = lax.axis_index("rows")
    col_place = lax.axis_index("cols")
    fast = fast_mesh()
    parity = lax.rem(col_place, 2)
    tree_id = lax.div(row_place * col_count + col_place, 2)
    parent_row = lax.dynamic_slice_in_dim(leaf_parent, tree_id, 1, 0)[0]
    depth, query_part = query_weight.shape
    key_part = key_weight.shape[1]
    router_part = router_weight.shape[1]
    gain_part = attention_gain.shape[0]
    expert_total = router_part * col_count
    local_experts = gate_weight.shape[0]
    capacity = TOK_DEV * TOP // expert_total * 5 // 4

    shards = (
        jnp.asarray(SLOT_SHARD, jnp.int32)[col_place]
        if fast
        else jnp.arange(4, dtype=jnp.int32)
    )
    branch_rows = jnp.where(parity == 0, TRUNK + BRANCH * parent_row, TRUNK)
    info = jnp.concatenate(
        [jnp.stack([row_place, parity]), shards, branch_rows, jnp.zeros((2,), jnp.int32)]
    ).astype(jnp.int32)

    packed = jnp.concatenate([query_weight, key_weight, value_weight, out_weight], axis=1)
    local_index = (1 - parity) * TOK_DEV + jnp.arange(TOK_DEV, dtype=jnp.int32)
    cosine, sine = rotary_tables(position_of(local_index))
    shard_blocks = [
        jnp.concatenate(
            [gate_weight[expert].T, upward_weight[expert].T, down_weight[expert]], axis=0
        )
        for expert in range(local_experts)
    ]
    nears, seconds, fars = ([], [], [])
    routes_all = lax.all_gather(routes.T, "rows", axis=0)
    if fast:
        near_rows = row_place ^ jnp.arange(row_count, dtype=jnp.int32)
    else:
        near_rows = jnp.arange(row_count, dtype=jnp.int32)
    chosen, place_rows = tables(
        near_rows, info, routes_all, capacity, local_experts, expert_total
    )
    if fast:
        wide = packed.shape[1]
        gains = jnp.concatenate([attention_gain, experts_gain])[None, :]
        packed = jnp.concatenate(
            [
                packed,
                jnp.pad(router_weight.T, ((0, 0), (0, wide - depth))),
                jnp.pad(gains, ((0, 0), (0, wide - 2 * gain_part))),
                jnp.zeros((EXTRA - router_part - 1, wide), LOW),
            ],
            axis=0,
        )
        packed_near = send_near(packed)
        packed_far = send_far(packed)
        packed_second = send_second(packed, packed_near)
        slots = slot_list(packed, packed_near, packed_second, packed_far)

        def gather_expert(*earlier):
            expert_at = len(nears)
            block = after(shard_blocks[expert_at], *earlier)
            shard_blocks[expert_at] = block
            nears.append(send_near(block))
            seconds.append(send_second(block, nears[expert_at]))

        gather_expert(*packed_near)
        first = after(packed[None], routes_all)
        first_four = jnp.concatenate([first] + [flip(first, bits) for bits in (2, 4, 6)], axis=0)
        others = jnp.stack(slots[1:])
        others = after(others, info, cosine, sine, first_four)
        beside, across = flip(others, 2), flip(others, 4)
        first_in, others_in = flip(first_four, 1), flip(others, 1)
        beside, across = after((beside, across), first_in, others_in, chosen, *nears[0])
        corner = [flip(beside[:1], 4), flip(across[1:], 2)]
        pair_in = flip(jnp.concatenate([beside, across], axis=0), 1)
        corner_in = [flip(piece, 1) for piece in corner]
        pieces = [first_four, first_in, others, beside, across, *corner]
        pieces += [others_in, pair_in, *corner_in]
        query_refs = pair_refs = out_refs = pieces
        extra_rows = extras(info, pieces)
        router_all = extra_rows[:, :router_part, :depth]
        attention_scale = extra_rows[:, router_part, :gain_part]
        experts_scale = extra_rows[:, router_part, gain_part : 2 * gain_part]
    else:
        packed_all = lax.all_gather(lax.all_gather(packed, "cols", axis=0), "rows", axis=0)

        def unpack(start, width):
            part = packed_all[..., start : start + width]
            return jnp.swapaxes(part, 1, 2).reshape(row_count * depth, col_count * width)

        key_at = query_part
        query_refs = [unpack(0, query_part)]
        pair_refs = [
            jnp.concatenate(
                [
                    unpack(key_at, key_part).reshape(D, QUARTERS, -1),
                    unpack(key_at + key_part, key_part).reshape(D, QUARTERS, -1),
                ],
                axis=2,
            ).reshape(D, -1)
        ]
        out_refs = [unpack(key_at + 2 * key_part, query_part)]
        axes = ("rows", "cols")
        router_all = jnp.swapaxes(lax.all_gather(router_weight, axes, axis=0), 1, 2)
        attention_scale = lax.all_gather(attention_gain, axes, axis=0)
        experts_scale = lax.all_gather(experts_gain, axes, axis=0)
        expert_refs = [
            [lax.all_gather(block, "cols", axis=0)[i] for i in range(col_count)]
            for block in shard_blocks
        ]

    attention_scale = attention_scale.reshape(1, D).astype(WIDE)
    experts_scale = experts_scale.reshape(1, D).astype(WIDE)
    router_rows = jnp.transpose(
        router_all.reshape(row_count, col_count, router_part, depth), (1, 2, 0, 3)
    ).reshape(expert_total, D)
    router_cols = router_rows.T
    normed, own_pair = key_value(info, tokens, attention_scale, cosine, sine, pair_refs)
    grad_in = after(cotangent, *corner) if fast else cotangent
    grad_all = lax.all_gather(grad_in, "rows", axis=0)
    pairs = [(i + 1, i) for i in range(0, col_count, 2)]
    partner = lax.ppermute(own_pair, "cols", pairs)
    normed_in = after(normed, seconds[0]) if fast else normed
    queries = query(info, normed_in, cosine, sine, query_refs)
    if fast:
        fars.append(send_far(after(shard_blocks[0], seconds[0], partner, queries)))
    heads = attention(info, queries, own_pair, partner)
    residual, normed_two = out_projection(info, heads, tokens, experts_scale, out_refs)

    if fast:
        beside, across = flip(normed_two, 2), flip(normed_two, 4)
        beside_in = flip(normed_two, 1)
        gather_expert(fars[0], normed_two)
        grad_all = after(grad_all, normed_two)
    else:
        rows_all = lax.all_gather(normed_two, "rows", axis=0)
    grad_rows = pick_rows(near_rows, chosen, grad_all, local_experts)

    def place_block(q, block, picked):
        return dispatch(
            q, near_rows, info, block, chosen, routes_all, router_cols, local_experts, picked
        )

    if fast:
        half = TOK_DEV // 2
        picked = place_block(0, normed_two, None)
        picked = place_block(1, beside_in, picked)
        beside, across = after((beside, across), picked, grad_rows, *nears[1])
        corner = [flip(beside[:half], 4), flip(across[half:], 2)]
        picked = place_block(2, beside, picked)
        picked = place_block(4, across, picked)
        beside_in = flip(beside, 1)
        across_in = flip(after(across, beside_in), 1)
        picked = place_block(3, beside_in, picked)
        picked = place_block(5, across_in, picked)
        corner = jnp.concatenate(after(corner, picked), axis=0)
        corner_in = flip(corner, 1)
        picked = place_block(6, corner, picked)
        picked = place_block(7, corner_in, picked)
        fars.append(send_far(after(shard_blocks[1], seconds[1], picked)))
        expert_refs = [
            [shard_blocks[i], seconds[i], *nears[i], fars[i]] for i in range(local_experts)
        ]
    else:
        picked = None
        for q in range(row_count):
            picked = place_block(q, rows_all[q], picked)
    height = row_count * capacity
    token_rows = [a.reshape(height, D) for a in picked[:local_experts]]
    grad_rows = [a.reshape(height, D) for a in grad_rows]
    share_rows = [a.reshape(height, 1) for a in picked[local_experts:]]

    out_rows, back_rows, gate_dots, reduced, marks = ([], [], [], [], [])
    grad_slots = []
    for e in range(local_experts):
        rows_in = token_rows[e]
        if fast and e == 0:
            rows_in = after(rows_in, seconds[1])
        if fast and e == 1:
            rows_in = after(rows_in, fars[1], second, fourth, own_slot, third)
        out_row, back_row, grad_row, acts, dots = expert(
            info, rows_in, grad_rows[e], share_rows[e], expert_refs[e], col_count
        )
        out_rows.append(out_row.reshape(row_count, capacity, D))
        back_rows.append(back_row.reshape(row_count, capacity, D))
        gate_dots.append(dots.reshape(row_count, capacity, 1))
        if fast:
            if e == 1:
                back_rows = after(back_rows, marks[0][0])
                got = flip(combine(info, chosen, back_rows, 1, 2, gate_dots), 1)
                acts = after(acts, got)
            second, fourth = expert_grads(acts, token_rows[e], grad_row, (1, 3))
            if e == 0:
                relay, _ = reduce_first(second, fourth, chain=True)
                marks.append((relay,))
            own_slot, third = expert_grads(acts, token_rows[e], grad_row, (0, 2))
            grad_slots.append((own_slot, second, third, fourth))
        else:
            slots = expert_grads(acts, token_rows[e], grad_row, tuple(range(col_count)))
            reduced.append(
                lax.psum_scatter(jnp.stack(slots), "cols", scatter_dimension=0).astype(WIDE)
            )

    if fast:
        back_keep = combine(info, chosen, back_rows, 0, 2, gate_dots)
        back_first = chips_first(back_keep, got)
        sent_second = reduce_second(grad_slots[0][2], grad_slots[0][3], marks[0][0])
        back_parts = chips_second(back_keep, got, *send_chips(back_first))
        out_rows = [after(a, back_parts[1], back_parts[4]) for a in out_rows]
        out_got = flip(combine(info, chosen, out_rows, 1, 2), 1)
        out_keep = combine(info, chosen, out_rows, 0, 2)
        far_back = lax.ppermute(
            after(grad_slots[0][3], *sent_second, out_keep), "cols", FAR
        )
        reduced.append((grad_slots[0][0], (marks[0][0], far_back), sent_second))
        back_parts = after(back_parts, out_keep, out_got)
    else:
        spread_dots = spread(place_rows, gate_dots)
        grad_shares = lax.all_to_all(spread_dots, "rows", split_axis=0, concat_axis=0, tiled=True)

        def summed(rows):
            part = combine(info, chosen, rows, 0, 1)
            return lax.psum_scatter(part, "rows", scatter_dimension=0).astype(WIDE)

        back_parts = (summed(back_rows), grad_shares.reshape(expert_total, TOK_DEV))
        mixture = (summed(out_rows),)

    grad_residual, grad_branch, grad_heads, experts_gain_grad, router_grad = branch_back(
        info,
        residual,
        normed_two,
        back_parts,
        cotangent,
        routes.T,
        router_rows,
        experts_scale,
        out_refs,
    )
    if fast:
        relay, _ = reduce_first(after(grad_slots[1][1], far_back, grad_heads), fourth, chain=True)
        marks.append((relay,))
        out_first = chips_first(out_keep, out_got)
        out_flips = send_chips(out_first)
        grad_heads = after(grad_heads, *out_first)
        router_parts = jnp.transpose(
            router_grad.astype(LOW).reshape(col_count, router_part, row_count, depth),
            (2, 0, 1, 3),
        ).reshape(row_count * col_count, router_part, depth)
        gain_rows = experts_gain_grad.astype(LOW).reshape(row_count * col_count, 1, gain_part)
        extra = jnp.concatenate(
            [
                jnp.pad(router_parts, ((0, 0), (0, 0), (0, wide - depth))),
                jnp.pad(gain_rows, ((0, 0), (0, 0), (0, wide - gain_part))),
                jnp.zeros((row_count * col_count, EXTRA - router_part - 1, wide), LOW),
            ],
            axis=1,
        )
    grad_query, own_grad, source_grad = attention_back(
        info, queries, own_pair, partner, grad_heads, cosine, sine
    )
    arrived = lax.ppermute(source_grad.astype(LOW), "cols", [(j, i) for i, j in pairs])
    grad_pair = join_grads(info, own_grad, source_grad, arrived, cosine, sine)
    if fast:
        grad_branch = after(grad_branch, *out_flips)
        keep, send = weight_grads(
            info,
            [normed, heads],
            [grad_query, grad_pair, grad_branch],
            ((0, 2, query_part), (0, 3, 2 * key_part), (1, 4, query_part)),
            extra,
        )
        send = after(send, marks[1][0])
        sent = flip(send, 1)
        sent_second = reduce_second(grad_slots[1][2], grad_slots[1][3], marks[1][0])
        grad_pair = after(grad_pair, keep)
    tokens_grad, attention_gain_grad = token_back(
        info, grad_query, grad_pair, tokens, grad_residual, attention_scale, query_refs, pair_refs
    )

    if fast:
        sent_first = chips_first(keep, sent)
        sent_chips = send_chips(sent_first)
        far_back = lax.ppermute(
            after(grad_slots[1][3], *sent_second, tokens_grad, *sent_first), "cols", FAR
        )
        reduced.append((grad_slots[1][0], (marks[1][0], far_back), sent_second))
        mixture = chips_second(out_keep, out_got, *out_flips)
        slots = sum_parts(chips_second(keep, sent, *sent_chips))
        width = query_part + 2 * key_part
        own_slots = [packed, *others]
        gain_sums = sum(
            jnp.sum(own_slots[i][:depth, :width].astype(WIDE) * slots[i, :depth, :width], axis=1)
            for i in range(4)
        )
        own_gains = lax.dynamic_slice_in_dim(attention_scale[0], row_place * depth, depth, 0)
        gain_sums = (gain_sums / own_gains).reshape(col_count, 1, gain_part)
        gain_sums = jnp.pad(
            jnp.take(gain_sums, shards, axis=0),
            ((0, 0), (depth + router_part + 1, EXTRA - router_part - 2), (0, wide - gain_part)),
        )
        slots = (slots + gain_sums).astype(LOW)

        def cols_sum(slots):
            sent_first = reduce_first(slots[1], slots[3])
            sent_second = reduce_second(slots[2], slots[3], sent_first[0])
            return reduce_last(slots[0], sent_first, sent_second)

        sums = cols_sum(slots)
        expert_sums = [reduce_last(*parts) for parts in reduced]
        router_sum = sums[depth : depth + router_part, :depth].T
        experts_gain_sum = sums[depth + router_part, :gain_part]
        attention_gain_sum = sums[depth + router_part + 1, :gain_part]
        sums = sums[:depth]
    else:
        full_grads = [
            tn(normed, grad_query),
            *jnp.moveaxis(tn(normed, grad_pair).reshape(D, QUARTERS, 2, -1), 2, 0),
            tn(heads, grad_branch),
        ]
        packed_grad = jnp.concatenate(
            [
                grad.astype(LOW).reshape(row_count, depth, col_count, -1)
                for grad in full_grads
            ],
            axis=3,
        )
        row_sums = lax.psum_scatter(packed_grad, "rows", scatter_dimension=0)
        sums = lax.psum_scatter(row_sums, "cols", scatter_dimension=1).astype(WIDE)
        expert_sums = reduced
        small_grads = jnp.concatenate(
            [
                attention_gain_grad.reshape(-1, gain_part),
                experts_gain_grad.reshape(-1, gain_part),
                jnp.transpose(
                    router_grad.reshape(col_count, router_part, row_count, depth), (2, 0, 3, 1)
                ).reshape(row_count * col_count, depth * router_part),
            ],
            axis=1,
        )
        small_grads = small_grads.reshape(row_count, -1)
        small_grads = lax.all_to_all(small_grads, "rows", split_axis=0, concat_axis=0, tiled=True)
        small_grads = jnp.sum(small_grads, axis=0).reshape(col_count, -1)
        small_grads = lax.all_to_all(small_grads, "cols", split_axis=0, concat_axis=0, tiled=True)
        small_sums = jnp.sum(small_grads, axis=0)
        attention_gain_sum = small_sums[:gain_part]
        experts_gain_sum = small_sums[gain_part : 2 * gain_part]
        router_sum = small_sums[2 * gain_part :].reshape(depth, router_part)

    layer_output = (residual + sum_parts(mixture)).astype(LOW)
    key_at = query_part
    value_at = key_at + key_part
    out_at = value_at + key_part
    part = down_weight.shape[1]
    gate_grad, upward_grad, down_grad = (
        jnp.stack([sums_of[which * part : (which + 1) * part] for sums_of in expert_sums])
        for which in range(3)
    )
    return (
        layer_output,
        tokens_grad,
        sums[:, :key_at],
        sums[:, key_at:value_at],
        sums[:, value_at:out_at],
        sums[:, out_at:],
        router_sum,
        attention_gain_sum,
        experts_gain_sum,
        jnp.swapaxes(gate_grad, 1, 2),
        jnp.swapaxes(upward_grad, 1, 2),
        down_grad,
    )


def solution(mesh):
    in_specs = (
        P(("rows", "cols"), None),
        P("rows", "cols"),
        P("rows", "cols"),
        P("rows", "cols"),
        P("rows", "cols"),
        P("rows", "cols"),
        P(("rows", "cols")),
        P(("rows", "cols")),
        P("rows", None, "cols"),
        P("rows", None, "cols"),
        P("rows", "cols", None),
        P(("rows", "cols"), None),
        P(),
        P(("rows", "cols"), None),
    )
    out_specs = (
        P(("rows", "cols"), None),
        P(("rows", "cols"), None),
        P("rows", "cols"),
        P("rows", "cols"),
        P("rows", "cols"),
        P("rows", "cols"),
        P("rows", "cols"),
        P(("rows", "cols")),
        P(("rows", "cols")),
        P("rows", None, "cols"),
        P("rows", None, "cols"),
        P("rows", "cols", None),
    )
    return jax.shard_map(
        on_device, mesh=mesh, in_specs=in_specs, out_specs=out_specs, check_vma=False
    )
```

```python
import functools

import jax
import jax.numpy as jnp
from jax import lax
from jax.experimental import pallas as pl
from jax.experimental.pallas import tpu as pltpu
from jax.sharding import PartitionSpec as P

D = 1536
HEADS = 12
KV_HEADS = 2
HEAD_DIM = 128
TOP = 4
TOK_DEV = 512
BRANCHES = 4
LEAVES = 8
TRUNK = 256
BRANCH = 64

EPSILON = 1e-06
ROPE_BASE = 10000.0
MASKED = -1e30
LOW = jnp.bfloat16
WIDE = jnp.float32
KEY_WIDTH = KV_HEADS * HEAD_DIM
GROUP = HEADS // KV_HEADS
QUARTERS = 4
VMEM_LIMIT = 56 * 1024 * 1024

ANY = pl.BlockSpec(memory_space=pl.ANY)
SMEM = pl.BlockSpec(memory_space=pltpu.SMEM)


def nn(one, two):
    return lax.dot_general(one, two, (((1,), (0,)), ((), ())), preferred_element_type=WIDE)


def nt(one, two):
    return lax.dot_general(one, two, (((1,), (1,)), ((), ())), preferred_element_type=WIDE)


def tn(one, two):
    return lax.dot_general(one, two, (((0,), (0,)), ((), ())), preferred_element_type=WIDE)


def whole(shape):
    return pl.BlockSpec(shape, lambda *_: (0,) * len(shape))


LITTLE = pl.CostEstimate(flops=1, bytes_accessed=1, transcendentals=0)


def params():
    return pltpu.CompilerParams(vmem_limit_bytes=VMEM_LIMIT)


def turn(values, cosine, sine):
    return values * cosine + pltpu.roll(values, HEAD_DIM // 2, 1) * sine


def turn_back(values, cosine, sine):
    return values * cosine - pltpu.roll(values, HEAD_DIM // 2, 1) * sine


SLOTS = range(4)
PIECES = (
    tuple((0, slot) for slot in SLOTS),
    tuple((1, slot) for slot in SLOTS),
    tuple((2, slot) for slot in SLOTS),
    tuple((4, slot) for slot in SLOTS),
    ((6, 0), (6, 1)),
    ((6, 2), (6, 3)),
    tuple((flip_bits, slot) for flip_bits in (3, 5) for slot in SLOTS),
    ((7, 0), (7, 1)),
    ((7, 2), (7, 3)),
)
EXTRA = 16


def weight_copies(info, refs, target, sem, start, width):
    if len(refs) == 1:
        return [pltpu.make_async_copy(refs[0], target, sem)]
    depth = refs[0].shape[1] - EXTRA
    copies = []
    for ref, parts in zip(refs, PIECES):
        for at, (flip_bits, slot) in enumerate(parts):
            row = pl.multiple_of((info[0] ^ flip_bits) * depth, depth)
            col = pl.multiple_of(info[2 + slot] * width, 128)
            copies.append(
                pltpu.make_async_copy(
                    ref.at[at, pl.ds(0, depth), pl.ds(start, width)],
                    target.at[pl.ds(row, depth), pl.ds(col, width)],
                    sem,
                )
            )
    return copies


def extras_kernel(info, *rest):
    refs, (out, sem) = rest[:-2], rest[-2:]
    depth = refs[0].shape[1] - EXTRA
    copies = []
    for ref, parts in zip(refs, PIECES):
        for at, (flip_bits, slot) in enumerate(parts):
            to = (info[0] ^ flip_bits) * QUARTERS + info[2 + slot]
            copies.append(pltpu.make_async_copy(ref.at[at, pl.ds(depth, EXTRA)], out.at[to], sem))
    run_all(copies)
    wait_all(copies)


def extras(info, refs):
    return pl.pallas_call(
        extras_kernel,
        out_shape=jax.ShapeDtypeStruct((8 * QUARTERS, EXTRA, refs[0].shape[2]), LOW),
        in_specs=[SMEM] + [ANY] * len(refs),
        out_specs=pl.BlockSpec(memory_space=pltpu.VMEM),
        scratch_shapes=[pltpu.SemaphoreType.DMA],
        compiler_params=params(),
        cost_estimate=LITTLE,
        name="extra_rows",
    )(info, *refs)


def run_all(copies):
    for copy in copies:
        copy.start()


def wait_all(copies):
    for copy in copies:
        copy.wait()


def key_value_kernel(info, tokens, gain, cosine, sine, *rest):
    count = len(rest) - 4
    refs, (normed, out, weight, sem) = rest[:count], rest[count:]
    copies = weight_copies(info, refs, weight, sem, D // QUARTERS, 128)
    run_all(copies)
    values = tokens[...].astype(WIDE)
    factor = lax.rsqrt(jnp.mean(values * values, axis=-1, keepdims=True) + EPSILON)
    low = (values * factor * gain[...]).astype(LOW)
    normed[...] = low
    wait_all(copies)
    both = nn(low, weight[...])
    half = HEAD_DIM // 2
    first = lax.broadcasted_iota(jnp.int32, (TOK_DEV, HEAD_DIM), 1) < half
    for g in range(KV_HEADS):
        one = both[:, 256 * g : 256 * g + 128]
        two = both[:, 256 * g + 128 : 256 * g + 256]
        key = jnp.where(first, one, pltpu.roll(two, half, 1))
        value = jnp.where(first, pltpu.roll(one, half, 1), two)
        out[:, 128 * g : 128 * g + 128] = turn(key, cosine[...], sine[...]).astype(LOW)
        out[:, KEY_WIDTH + 128 * g : KEY_WIDTH + 128 * g + 128] = value.astype(LOW)


def key_value(info, tokens, gain, cosine, sine, refs):
    return pl.pallas_call(
        key_value_kernel,
        out_shape=(
            jax.ShapeDtypeStruct((TOK_DEV, D), LOW),
            jax.ShapeDtypeStruct((TOK_DEV, 2 * KEY_WIDTH), LOW),
        ),
        in_specs=[SMEM] + [pl.BlockSpec(memory_space=pltpu.VMEM)] * 4 + [ANY] * len(refs),
        out_specs=(pl.BlockSpec(memory_space=pltpu.VMEM),) * 2,
        scratch_shapes=[pltpu.VMEM((D, 2 * KEY_WIDTH), LOW), pltpu.SemaphoreType.DMA],
        compiler_params=params(),
        cost_estimate=LITTLE,
        name="norm_key_value",
    )(info, tokens, gain, cosine, sine, *refs)


def query_kernel(info, normed, cosine, sine, *rest):
    count = len(rest) - 3
    refs, (out, weight, sem) = rest[:count], rest[count:]

    @pl.when(pl.program_id(0) == 0)
    def _():
        copies = weight_copies(info, refs, weight, sem, 0, D // QUARTERS)
        run_all(copies)
        wait_all(copies)

    at = pl.multiple_of(pl.program_id(0) * 256, 256)
    lin = nn(normed[...], weight[:, pl.ds(at, 256)])
    for h in range(2):
        out[:, 128 * h : 128 * h + 128] = turn(
            lin[:, 128 * h : 128 * h + 128], cosine[...], sine[...]
        ).astype(LOW)


def query(info, normed, cosine, sine, refs):
    return pl.pallas_call(
        query_kernel,
        grid=(D // 256,),
        out_shape=jax.ShapeDtypeStruct((TOK_DEV, D), LOW),
        in_specs=[SMEM, whole((TOK_DEV, D)), whole((TOK_DEV, 128)), whole((TOK_DEV, 128))]
        + [ANY] * len(refs),
        out_specs=pl.BlockSpec((TOK_DEV, 256), lambda i: (0, i)),
        scratch_shapes=[pltpu.VMEM((D, D), LOW), pltpu.SemaphoreType.DMA],
        compiler_params=params(),
        cost_estimate=LITTLE,
        name="query_projection",
    )(info, normed, cosine, sine, *refs)


KEYS = TRUNK + 2 * BRANCH
CHUNKS = TOK_DEV // BRANCH


def chunk_keys(info, source, own, column, chunk):
    at = pl.multiple_of(info[6 + chunk], BRANCH)
    rows = pl.multiple_of(chunk * BRANCH, BRANCH)
    columns = slice(column, column + HEAD_DIM)
    return jnp.concatenate(
        [
            source[0:TRUNK, columns],
            source[pl.ds(at, BRANCH), columns],
            own[pl.ds(rows, BRANCH), columns],
        ],
        axis=0,
    )


def chunk_allowed(info, chunk, query_axis, shape):
    query_row = lax.broadcasted_iota(jnp.int32, shape, query_axis) & (BRANCH - 1)
    key = lax.broadcasted_iota(jnp.int32, shape, 1 - query_axis)
    leaves = info[1] == 0
    trunk = jnp.logical_and(jnp.logical_not(leaves), chunk < TRUNK // BRANCH)
    limit = jnp.where(trunk, chunk * BRANCH + query_row, TRUNK - 1)
    branch_limit = jnp.where(leaves, TRUNK + BRANCH - 1, 0)
    own_limit = jnp.where(trunk, 0, query_row + TRUNK + BRANCH)
    top = jnp.where(key < TRUNK, limit, jnp.where(key < TRUNK + BRANCH, branch_limit, own_limit))
    return key <= top


def group_rows(ref, g):
    first = g * GROUP
    return jnp.concatenate(
        [ref[:, 128 * h : 128 * h + 128] for h in range(first, first + GROUP)], axis=0
    )


def keep_source(info, partner, own, source):
    @pl.when(pl.program_id(0) == 0)
    def _():
        @pl.when(info[1] == 0)
        def _():
            source[...] = partner[...]

        @pl.when(info[1] != 0)
        def _():
            source[...] = own[...]


def attention_kernel(info, queries, own, partner, out, source):
    keep_source(info, partner, own, source)
    chunk = pl.program_id(0)
    rows = GROUP * BRANCH
    allowed = chunk_allowed(info, chunk, 0, (rows, KEYS))
    for g in range(KV_HEADS):
        keys = chunk_keys(info, source, own, 128 * g, chunk)
        values = chunk_keys(info, source, own, KEY_WIDTH + 128 * g, chunk)
        scores = nt(group_rows(queries, g), keys) * HEAD_DIM**-0.5
        scores = jnp.where(allowed, scores, MASKED)
        weights = jnp.exp(scores - jnp.max(scores, axis=1, keepdims=True))
        total = jnp.sum(weights, axis=1, keepdims=True)
        mixed = nn((weights * (1.0 / total)).astype(LOW), values).astype(LOW)
        for h in range(GROUP):
            at = (g * GROUP + h) * 128
            out[:, at : at + 128] = mixed[h * BRANCH : (h + 1) * BRANCH]


def attention(info, queries, own, partner):
    return pl.pallas_call(
        attention_kernel,
        grid=(CHUNKS,),
        out_shape=jax.ShapeDtypeStruct((TOK_DEV, D), LOW),
        in_specs=[
            SMEM,
            pl.BlockSpec((BRANCH, D), lambda i: (i, 0)),
            whole((TOK_DEV, 2 * KEY_WIDTH)),
            whole((TOK_DEV, 2 * KEY_WIDTH)),
        ],
        out_specs=pl.BlockSpec((BRANCH, D), lambda i: (i, 0)),
        scratch_shapes=[pltpu.VMEM((TOK_DEV, 2 * KEY_WIDTH), LOW)],
        compiler_params=params(),
        cost_estimate=LITTLE,
        name="tree_attention",
    )(info, queries, own, partner)


def attention_back_kernel(
    info, queries, own, partner, grads, cosine, sine, grad_query, own_grad, source_grad, source
):
    keep_source(info, partner, own, source)
    chunk = pl.program_id(0)

    @pl.when(chunk == 0)
    def _():
        source_grad[...] = jnp.zeros_like(source_grad)

    rows = GROUP * BRANCH
    scale = HEAD_DIM**-0.5
    allowed = chunk_allowed(info, chunk, 1, (KEYS, rows))
    at = pl.multiple_of(info[6 + chunk], BRANCH)
    for g in range(KV_HEADS):
        keys = chunk_keys(info, source, own, 128 * g, chunk)
        values = chunk_keys(info, source, own, KEY_WIDTH + 128 * g, chunk)
        query_rows = group_rows(queries, g)
        grad_rows = group_rows(grads, g)
        scores = jnp.where(allowed, nt(keys, query_rows) * scale, MASKED)
        weights = jnp.exp(scores - jnp.max(scores, axis=0, keepdims=True))
        probs = weights * (1.0 / jnp.sum(weights, axis=0, keepdims=True))
        grad_probs = nt(values, grad_rows)
        mean = jnp.sum(probs * grad_probs, axis=0, keepdims=True)
        grad_scores = (probs * (grad_probs - mean)).astype(LOW)
        grad_values = nn(probs.astype(LOW), grad_rows)
        grad_keys = nn(grad_scores, query_rows) * scale
        grad_queries = tn(grad_scores, keys) * scale
        for h in range(GROUP):
            to = (g * GROUP + h) * 128
            grad_query[:, to : to + 128] = turn_back(
                grad_queries[h * BRANCH : (h + 1) * BRANCH], cosine[...], sine[...]
            ).astype(LOW)
        for column, grad in ((128 * g, grad_keys), (KEY_WIDTH + 128 * g, grad_values)):
            columns = slice(column, column + 128)
            source_grad[0:TRUNK, columns] += grad[0:TRUNK]
            source_grad[pl.ds(at, BRANCH), columns] += grad[TRUNK : TRUNK + BRANCH]
            own_grad[:, columns] = grad[TRUNK + BRANCH :]


def attention_back(info, queries, own, partner, grads, cosine, sine):
    chunked = pl.BlockSpec((BRANCH, D), lambda i: (i, 0))
    pair = (TOK_DEV, 2 * KEY_WIDTH)
    return pl.pallas_call(
        attention_back_kernel,
        grid=(CHUNKS,),
        out_shape=(
            jax.ShapeDtypeStruct((TOK_DEV, D), LOW),
            jax.ShapeDtypeStruct(pair, WIDE),
            jax.ShapeDtypeStruct(pair, WIDE),
        ),
        in_specs=[
            SMEM,
            chunked,
            whole(pair),
            whole(pair),
            chunked,
            pl.BlockSpec((BRANCH, 128), lambda i: (i, 0)),
            pl.BlockSpec((BRANCH, 128), lambda i: (i, 0)),
        ],
        out_specs=(
            chunked,
            pl.BlockSpec((BRANCH, 2 * KEY_WIDTH), lambda i: (i, 0)),
            whole(pair),
        ),
        scratch_shapes=[pltpu.VMEM(pair, LOW)],
        compiler_params=params(),
        cost_estimate=LITTLE,
        name="tree_attention_back",
    )(info, queries, own, partner, grads, cosine, sine)


def out_kernel(info, heads, tokens, gain, *rest):
    count = len(rest) - 4
    refs, (residual, normed, weight, sem) = rest[:count], rest[count:]

    @pl.when(pl.program_id(0) == 0)
    def _():
        copies = weight_copies(info, refs, weight, sem, D // QUARTERS + 128, D // QUARTERS)
        run_all(copies)
        wait_all(copies)

    at = pl.ds(pl.multiple_of(pl.program_id(0) * 256, 256), 256)
    residual[:, at] = tokens[:, at].astype(WIDE) + nn(heads[...], weight[:, at])

    @pl.when(pl.program_id(0) == pl.num_programs(0) - 1)
    def _():
        values = residual[...]
        factor = lax.rsqrt(jnp.mean(values * values, axis=-1, keepdims=True) + EPSILON)
        normed[...] = (values * factor * gain[...]).astype(LOW)


def out_projection(info, heads, tokens, gain, refs):
    full = (TOK_DEV, D)
    return pl.pallas_call(
        out_kernel,
        grid=(D // 256,),
        out_shape=(jax.ShapeDtypeStruct(full, WIDE), jax.ShapeDtypeStruct(full, LOW)),
        in_specs=[SMEM, whole(full), whole(full), whole((1, D))] + [ANY] * len(refs),
        out_specs=(whole(full), whole(full)),
        scratch_shapes=[pltpu.VMEM((D, D), LOW), pltpu.SemaphoreType.DMA],
        compiler_params=params(),
        cost_estimate=LITTLE,
        name="out_projection",
    )(info, heads, tokens, gain, *refs)


def hits_of(routes, ids):
    hit = ids == routes[0, 0:1]
    for k in range(1, TOP):
        hit = jnp.logical_or(hit, ids == routes[0, k : k + 1])
    return hit


def tables_kernel(capacity, local, total, info, routes, chosen_out, place_out, earlier):
    @pl.when(pl.program_id(0) == 0)
    def _():
        one = lax.broadcasted_iota(jnp.int32, (TOK_DEV, TOK_DEV), 0)
        two = lax.broadcasted_iota(jnp.int32, (TOK_DEV, TOK_DEV), 1)
        earlier[...] = jnp.where(one < two, 1.0, 0.0).astype(LOW)

    ids = lax.broadcasted_iota(jnp.int32, (total, TOK_DEV), 0)
    hit = hits_of(routes, ids)
    rank = nn(jnp.where(hit, 1.0, 0.0).astype(LOW), earlier[...])
    place = jnp.where(hit, rank, -1.0)
    spots = lax.broadcasted_iota(jnp.int32, (capacity, TOK_DEV), 0).astype(WIDE)
    place_out[0] = jnp.full(place_out.shape[1:], -1.0, WIDE)
    for e in range(local):
        mine = ids == info[0] * local + e
        place_row = jnp.sum(jnp.where(mine, place, 0.0), axis=0, keepdims=True)
        place_out[0, e : e + 1] = place_row
        chosen_out[0, e * capacity : (e + 1) * capacity] = jnp.where(
            spots == place_row, 1.0, 0.0
        ).astype(LOW)


def tables(info, routes, capacity, local, total):
    count = routes.shape[0]
    return pl.pallas_call(
        functools.partial(tables_kernel, capacity, local, total),
        grid=(count,),
        in_specs=[SMEM, pl.BlockSpec((1, TOP, TOK_DEV), lambda i: (i, 0, 0))],
        out_specs=[
            pl.BlockSpec((1, local * capacity, TOK_DEV), lambda i: (i, 0, 0)),
            pl.BlockSpec((1, 8, TOK_DEV), lambda i: (i, 0, 0)),
        ],
        scratch_shapes=[pltpu.VMEM((TOK_DEV, TOK_DEV), LOW)],
        out_shape=[
            jax.ShapeDtypeStruct((count, local * capacity, TOK_DEV), LOW),
            jax.ShapeDtypeStruct((count, 8, TOK_DEV), WIDE),
        ],
        compiler_params=params(),
        cost_estimate=LITTLE,
        name="route_tables",
    )(info, routes)


def pick_kernel(local, chosen, *rest):
    count, height, _ = chosen.shape
    capacity = height // local
    for q in range(count):
        rows_of = nn(chosen[q], rest[q][...]).astype(LOW)
        for e in range(local):
            rest[count + e][q] = rows_of[e * capacity : (e + 1) * capacity]


def pick_rows(chosen, blocks, local):
    count, height, _ = chosen.shape
    capacity = height // local
    wide = 256
    return pl.pallas_call(
        functools.partial(pick_kernel, local),
        grid=(D // wide,),
        in_specs=[whole(chosen.shape)]
        + [pl.BlockSpec((TOK_DEV, wide), lambda i: (0, i))] * count,
        out_specs=[pl.BlockSpec((count, capacity, wide), lambda i: (0, 0, i))] * local,
        out_shape=[jax.ShapeDtypeStruct((count, capacity, D), LOW)] * local,
        compiler_params=params(),
        cost_estimate=LITTLE,
        name="pick_rows",
    )(chosen, *blocks)


def dispatch_kernel(local, info, rows, chosen, routes, router, *rest):
    outs, logits = rest[2 * local : 4 * local], rest[-1]
    total = router.shape[1]
    step = pl.program_id(0)
    block = rows[...]
    rows_of = nn(chosen[0], block).astype(LOW)
    capacity = outs[0].shape[1]
    for e in range(local):
        outs[e][0] = rows_of[e * capacity : (e + 1) * capacity]
    part = nn(block, router[...])

    @pl.when(step == 0)
    def _():
        logits[...] = part

    @pl.when(step > 0)
    def _():
        logits[...] += part

    @pl.when(step == pl.num_programs(0) - 1)
    def _():
        values = logits[...].T
        ids = lax.broadcasted_iota(jnp.int32, (total, TOK_DEV), 0)
        weights = jnp.exp(values - jnp.max(values, axis=0, keepdims=True))
        hit = hits_of(routes, ids)
        share = weights / jnp.sum(jnp.where(hit, weights, 0.0), axis=0, keepdims=True)
        for e in range(local):
            mine = ids == info[0] * local + e
            share_row = jnp.sum(jnp.where(mine, share, 0.0), axis=0, keepdims=True)
            picked = chosen[0, e * capacity : (e + 1) * capacity].astype(WIDE)
            outs[local + e][0] = jnp.sum(picked * share_row, axis=1, keepdims=True)


def dispatch(at, info, rows, chosen, routes, router, local, earlier):
    count, height, _ = chosen.shape
    capacity = height // local
    total = router.shape[1]
    wide = 512
    out_shape = [jax.ShapeDtypeStruct((count, capacity, D), LOW)] * local + [
        jax.ShapeDtypeStruct((count, capacity, 1), WIDE)
    ] * local
    if earlier is None:
        earlier = [jnp.zeros((8, 128), shape.dtype) for shape in out_shape]
        aliases = {}
    else:
        aliases = {5 + i: i for i in range(len(out_shape))}
    return pl.pallas_call(
        functools.partial(dispatch_kernel, local),
        grid=(D // wide,),
        in_specs=[
            SMEM,
            pl.BlockSpec((TOK_DEV, wide), lambda i: (0, i)),
            pl.BlockSpec((1, height, TOK_DEV), lambda i: (at, 0, 0)),
            pl.BlockSpec((1, TOP, TOK_DEV), lambda i: (at, 0, 0)),
            pl.BlockSpec((wide, total), lambda i: (i, 0)),
        ]
        + [ANY] * len(out_shape),
        out_specs=[pl.BlockSpec((1, capacity, wide), lambda i: (at, 0, i))] * local
        + [pl.BlockSpec((1, capacity, 1), lambda i: (at, 0, 0))] * local,
        scratch_shapes=[pltpu.VMEM((TOK_DEV, total), WIDE)],
        out_shape=out_shape,
        input_output_aliases=aliases,
        compiler_params=params(),
        cost_estimate=LITTLE,
        name="dispatch",
    )(info, rows, chosen, routes, router, *earlier)


def spread_kernel(local, place, *rest):
    dots, out = rest[:local], rest[local]
    spots = lax.broadcasted_iota(jnp.int32, (dots[0].shape[1], TOK_DEV), 0).astype(WIDE)
    for e in range(local):
        chosen = spots == place[0, e : e + 1]
        out[0, e : e + 1] = jnp.sum(jnp.where(chosen, dots[e][0], 0.0), axis=0, keepdims=True)


def spread(place, dots):
    count, capacity, _ = dots[0].shape
    local = len(dots)
    return pl.pallas_call(
        functools.partial(spread_kernel, local),
        grid=(count,),
        out_shape=jax.ShapeDtypeStruct((count, local, TOK_DEV), WIDE),
        in_specs=[pl.BlockSpec((1, 8, TOK_DEV), lambda i: (i, 0, 0))]
        + [pl.BlockSpec((1, capacity, 1), lambda i: (i, 0, 0))] * local,
        out_specs=pl.BlockSpec((1, local, TOK_DEV), lambda i: (i, 0, 0)),
        compiler_params=params(),
        cost_estimate=LITTLE,
        name="spread",
    )(place, *dots)


def expert_kernel(slots, rows, grads, shares, source, *rest):
    out_rows, back_rows, grad_rows, acts, dots, weight, sem = rest
    part = weight.shape[1] // slots

    @pl.when(pl.program_id(0) == 0)
    def _():
        copies = [
            pltpu.make_async_copy(
                source.at[slot, pl.ds(which * part, part)],
                weight.at[which, pl.ds(slot * part, part)],
                sem,
            )
            for slot in range(slots)
            for which in range(3)
        ]
        run_all(copies)
        wait_all(copies)

    row_block = rows[...]
    share = shares[...]
    grad_float = grads[...].astype(WIDE)
    grad_low = (share * grad_float).astype(LOW)
    grad_rows[...] = grad_low
    gate_act = nt(row_block, weight[0])
    upward = nt(row_block, weight[1])
    sigmoid = 1.0 / (1.0 + jnp.exp(-gate_act))
    silu = gate_act * sigmoid
    hidden = (silu * upward).astype(LOW)
    expert_out = nn(hidden, weight[2]).astype(LOW).astype(WIDE)
    out_rows[...] = (share * expert_out).astype(LOW)
    dots[...] = jnp.sum(grad_float * expert_out, axis=1, keepdims=True)
    grad_hidden = nt(grad_low, weight[2])
    grad_gate = (grad_hidden * upward * sigmoid * (1.0 + gate_act * (1.0 - sigmoid))).astype(LOW)
    grad_up = (grad_hidden * silu).astype(LOW)
    back_rows[...] = (nn(grad_gate, weight[0]) + nn(grad_up, weight[1])).astype(LOW)
    for which, act in enumerate((grad_gate, grad_up, hidden)):
        turned = act.T
        for slot in range(slots):
            acts[slot, which * part : (which + 1) * part] = turned[
                slot * part : (slot + 1) * part
            ]


EXPERT_ROWS = 256


def expert(rows, grads, shares, weights):
    height = rows.shape[0]
    slots, part = weights.shape[0], weights.shape[1] // 3
    wide_block = pl.BlockSpec((EXPERT_ROWS, D), lambda i: (i, 0))
    thin_block = pl.BlockSpec((EXPERT_ROWS, 1), lambda i: (i, 0))
    return pl.pallas_call(
        functools.partial(expert_kernel, slots),
        grid=(height // EXPERT_ROWS,),
        out_shape=[jax.ShapeDtypeStruct((height, D), LOW)] * 3
        + [
            jax.ShapeDtypeStruct((slots, 3 * part, height), LOW),
            jax.ShapeDtypeStruct((height, 1), WIDE),
        ],
        in_specs=[wide_block, wide_block, thin_block, ANY],
        out_specs=[wide_block] * 3
        + [pl.BlockSpec((slots, 3 * part, EXPERT_ROWS), lambda i: (0, 0, i)), thin_block],
        scratch_shapes=[pltpu.VMEM((3, slots * part, D), LOW), pltpu.SemaphoreType.DMA],
        compiler_params=params(),
        cost_estimate=LITTLE,
        name="expert",
    )(rows, grads, shares, weights)


def expert_grads_kernel(acts, rows, grads, out):
    slots, height, _ = acts.shape
    part = height // 3
    for slot in range(slots):
        out[slot, : 2 * part] = nn(acts[slot, : 2 * part], rows[...]).astype(LOW)
        out[slot, 2 * part :] = nn(acts[slot, 2 * part :], grads[...]).astype(LOW)


def expert_grads(acts, rows, grads):
    slots, part, height = acts.shape
    strip = pl.BlockSpec((height, 256), lambda i: (0, i))
    return pl.pallas_call(
        expert_grads_kernel,
        grid=(D // 256,),
        out_shape=jax.ShapeDtypeStruct((slots, part, D), LOW),
        in_specs=[whole(acts.shape), strip, strip],
        out_specs=pl.BlockSpec((slots, part, 256), lambda i: (0, 0, i)),
        compiler_params=params(),
        cost_estimate=LITTLE,
        name="expert_gradients",
    )(acts, rows, grads)


SHARE_ROWS = 32


def combine_kernel(local, info, chosen, *rest):
    rows, dots, out = rest[:local], rest[local:-1], rest[-1]
    both = jnp.concatenate([ref[0] for ref in rows], axis=0)
    out[0, :TOK_DEV] = tn(chosen[0], both).astype(LOW)
    if dots:
        capacity = rows[0].shape[1]
        row = lax.broadcasted_iota(jnp.int32, (SHARE_ROWS, D), 0)
        values = jnp.zeros((SHARE_ROWS, D), WIDE)
        for e in range(local):
            picked = chosen[0, e * capacity : (e + 1) * capacity].astype(WIDE)
            high, low = split(jnp.sum(picked * dots[e][0], axis=0, keepdims=True))
            pieces = [high.astype(WIDE), low.astype(WIDE)]
            pieces.append(jnp.zeros((1, D - 2 * TOK_DEV), WIDE))
            line = jnp.concatenate(pieces, axis=1)
            values = jnp.where(row == info[0] * local + e, line, values)
        out[0, TOK_DEV:] = values.astype(LOW)


def combine(info, chosen, rows, first, step, dots=()):
    count, capacity, _ = rows[0].shape
    number = (count - first + step - 1) // step
    height = TOK_DEV + (SHARE_ROWS if dots else 0)
    return pl.pallas_call(
        functools.partial(combine_kernel, len(rows)),
        grid=(number,),
        out_shape=jax.ShapeDtypeStruct((number, height, D), LOW),
        in_specs=[
            SMEM,
            pl.BlockSpec((1,) + chosen.shape[1:], lambda i: (first + step * i, 0, 0)),
        ]
        + [pl.BlockSpec((1, capacity, D), lambda i: (first + step * i, 0, 0))] * len(rows)
        + [pl.BlockSpec((1, capacity, 1), lambda i: (first + step * i, 0, 0))] * len(dots),
        out_specs=pl.BlockSpec((1, height, D), lambda i: (i, 0, 0)),
        compiler_params=params(),
        cost_estimate=LITTLE,
        name="combine",
    )(info, chosen, *rows, *dots)


def split(values):
    high = values.astype(LOW)
    return high, (values - high.astype(WIDE)).astype(LOW)


def norm_back(values, gain, grad):
    factor = lax.rsqrt(jnp.mean(values * values, axis=-1, keepdims=True) + EPSILON)
    scaled = gain * grad
    mean = jnp.mean(values * scaled, axis=-1, keepdims=True)
    grad_values = factor * scaled - values * (factor * factor * factor * mean)
    grad_gain = jnp.sum(grad * values * factor, axis=0, keepdims=True)
    return grad_values, grad_gain


def router_back(logits, routes, grad_shares):
    ids = lax.broadcasted_iota(jnp.int32, logits.shape, 0)
    hit = ids == routes[0:1]
    for k in range(1, TOP):
        hit = jnp.logical_or(hit, ids == routes[k : k + 1])
    weights = jnp.exp(logits - jnp.max(logits, axis=0, keepdims=True))
    probs = weights / jnp.sum(weights, axis=0, keepdims=True)
    chosen = jnp.sum(jnp.where(hit, probs, 0.0), axis=0, keepdims=True)
    grads = jnp.where(hit, grad_shares, 0.0)
    mean = jnp.sum(probs * grads, axis=0, keepdims=True) / chosen
    grad_probs = jnp.where(hit, (grads - mean) / chosen, 0.0)
    return probs * (grad_probs - jnp.sum(probs * grad_probs, axis=0, keepdims=True))


def branch_back_kernel(
    parts, info, residual, normed, cotangent, routes, router, gain, *rest
):
    sums, rest = rest[:parts], rest[parts:]
    experts = router.shape[0]
    count = len(rest) - 7
    refs = rest[:count]
    grad_residual, grad_branch, grad_heads, grad_gain, grad_router, weight, sem = rest[count:]

    @pl.when(pl.program_id(0) == 0)
    def _():
        copies = weight_copies(info, refs, weight, sem, D // QUARTERS + 128, D // QUARTERS)
        run_all(copies)
        logits = nt(router[...], normed[...])
        if parts == 2:
            back_sum, grad_shares = sums[0][...], sums[1][...]
        else:
            values = [ref[...].astype(WIDE) for ref in sums]
            upper = values[0] + values[1] + values[2]
            lower = values[3] + values[4] + values[5]
            last = lower.shape[0] - SHARE_ROWS
            shares = lower[last : last + experts]
            grad_shares = shares[:, :TOK_DEV] + shares[:, TOK_DEV : 2 * TOK_DEV]
            back_sum = jnp.concatenate([upper, lower[:last]], axis=0)
        high, low = split(router_back(logits, routes[...], grad_shares))
        grad_router[...] = nn(high, normed[...]) + nn(low, normed[...])
        grad_normed = tn(high, router[...]) + tn(low, router[...])
        grad_normed += back_sum
        grad_values, gain_grad = norm_back(residual[...], gain[...], grad_normed)
        grad_gain[...] = gain_grad
        total = cotangent[...].astype(WIDE) + grad_values
        grad_residual[...] = total
        grad_branch[...] = total.astype(LOW)
        wait_all(copies)

    at = pl.ds(pl.multiple_of(pl.program_id(0) * 256, 256), 256)
    grad_heads[...] = nt(grad_branch[...], weight[at, :]).astype(LOW)


def branch_back(info, residual, normed, sums, cotangent, routes, router, gain, refs):
    full = (TOK_DEV, D)
    total = router.shape[0]
    return pl.pallas_call(
        functools.partial(branch_back_kernel, len(sums)),
        grid=(D // 256,),
        out_shape=(
            jax.ShapeDtypeStruct(full, WIDE),
            jax.ShapeDtypeStruct(full, LOW),
            jax.ShapeDtypeStruct(full, LOW),
            jax.ShapeDtypeStruct((1, D), WIDE),
            jax.ShapeDtypeStruct((total, D), WIDE),
        ),
        in_specs=[SMEM]
        + [whole(full)] * 3
        + [whole((TOP, TOK_DEV)), whole((total, D)), whole((1, D))]
        + [whole(part.shape) for part in sums]
        + [ANY] * len(refs),
        out_specs=(
            whole(full),
            whole(full),
            pl.BlockSpec((TOK_DEV, 256), lambda i: (0, i)),
            whole((1, D)),
            whole((total, D)),
        ),
        scratch_shapes=[pltpu.VMEM((D, D), LOW), pltpu.SemaphoreType.DMA],
        compiler_params=params(),
        cost_estimate=LITTLE,
        name="experts_norm_back",
    )(info, residual, normed, cotangent, routes, router, gain, *sums, *refs)


def join_grads_kernel(info, own_grad, source_grad, arrived, cosine, sine, out):
    half = HEAD_DIM // 2
    first = lax.broadcasted_iota(jnp.int32, (TOK_DEV, HEAD_DIM), 1) < half
    leaves = info[1] == 0

    def total(column):
        columns = slice(column, column + 128)
        extra = source_grad[:, columns] + arrived[:, columns].astype(WIDE)
        return own_grad[:, columns] + jnp.where(leaves, 0.0, extra)

    for g in range(KV_HEADS):
        key = turn_back(total(128 * g), cosine[...], sine[...])
        value = total(KEY_WIDTH + 128 * g)
        out[:, 256 * g : 256 * g + 128] = jnp.where(
            first, key, pltpu.roll(value, half, 1)
        ).astype(LOW)
        out[:, 256 * g + 128 : 256 * g + 256] = jnp.where(
            first, pltpu.roll(key, half, 1), value
        ).astype(LOW)


def join_grads(info, own_grad, source_grad, arrived, cosine, sine):
    vmem = pl.BlockSpec(memory_space=pltpu.VMEM)
    return pl.pallas_call(
        join_grads_kernel,
        out_shape=jax.ShapeDtypeStruct((TOK_DEV, 2 * KEY_WIDTH), LOW),
        in_specs=[SMEM] + [vmem] * 5,
        out_specs=vmem,
        compiler_params=params(),
        cost_estimate=LITTLE,
        name="join_key_value_gradients",
    )(info, own_grad, source_grad, arrived, cosine, sine)


def token_back_kernel(info, grad_query, grad_pair, tokens, grad_residual, gain, *rest):
    count = (len(rest) - 6) // 2
    query_refs, pair_refs = rest[:count], rest[count : 2 * count]
    out, grad_gain, query_weight, pair_weight, grad_normed, sem = rest[2 * count :]

    @pl.when(pl.program_id(0) == 0)
    def _():
        copies = weight_copies(info, query_refs, query_weight, sem, 0, D // QUARTERS)
        copies += weight_copies(info, pair_refs, pair_weight, sem, D // QUARTERS, 128)
        run_all(copies)
        wait_all(copies)

    at = pl.ds(pl.multiple_of(pl.program_id(0) * 256, 256), 256)
    grad_normed[:, at] = nt(grad_query[...], query_weight[at, :]) + nt(
        grad_pair[...], pair_weight[at, :]
    )

    @pl.when(pl.program_id(0) == pl.num_programs(0) - 1)
    def _():
        grad_values, gain_grad = norm_back(
            tokens[...].astype(WIDE), gain[...], grad_normed[...]
        )
        grad_gain[...] = gain_grad
        out[...] = (grad_residual[...] + grad_values).astype(LOW)


def token_back(info, grad_query, grad_pair, tokens, grad_residual, gain, query_refs, pair_refs):
    full = (TOK_DEV, D)
    return pl.pallas_call(
        token_back_kernel,
        grid=(D // 256,),
        out_shape=(jax.ShapeDtypeStruct(full, LOW), jax.ShapeDtypeStruct((1, D), WIDE)),
        in_specs=[
            SMEM,
            whole(full),
            whole((TOK_DEV, 2 * KEY_WIDTH)),
            whole(full),
            whole(full),
            whole((1, D)),
        ]
        + [ANY] * (len(query_refs) + len(pair_refs)),
        out_specs=(whole(full), whole((1, D))),
        scratch_shapes=[
            pltpu.VMEM((D, D), LOW),
            pltpu.VMEM((D, 2 * KEY_WIDTH), LOW),
            pltpu.VMEM(full, WIDE),
            pltpu.SemaphoreType.DMA,
        ],
        compiler_params=params(),
        cost_estimate=LITTLE,
        name="token_gradient",
    )(info, grad_query, grad_pair, tokens, grad_residual, gain, *query_refs, *pair_refs)


def weight_grads_kernel(parts, info, *rest):
    ins, (keep, send) = rest[:-2], rest[-2:]
    depth = D // 8
    core = info[0] & 1
    chip = pl.program_id(0) ^ (info[0] >> 1)
    start = 0
    for strip_at, grads_at, width in parts:
        low = tn(ins[strip_at][...], ins[grads_at][...]).astype(LOW)
        columns = slice(start, start + width)
        start += width
        for slot in range(QUARTERS):
            for j in range(QUARTERS):

                @pl.when(info[2 + slot] == j)
                def _():
                    piece = low[:, j * width : (j + 1) * width]
                    upper, lower = piece[:depth], piece[depth:]
                    keep[0, slot, :depth, columns] = jnp.where(core == 0, upper, lower)
                    send[0, slot, :depth, columns] = jnp.where(core == 0, lower, upper)

    if keep.shape[2] > depth:
        extra = ins[-1]
        for slot in range(QUARTERS):
            to = info[2 + slot]
            keep[0, slot, depth:] = extra[(chip * 2 + core) * QUARTERS + to]
            send[0, slot, depth:] = extra[(chip * 2 + 1 - core) * QUARTERS + to]


def weight_grads(info, strips, grads, parts, extra):
    depth = D // 8
    width = sum(part[2] for part in parts)
    strip = pl.BlockSpec((TOK_DEV, 2 * depth), lambda i, info: (0, i ^ (info[0] >> 1)))
    more = [] if extra is None else [extra]
    shape = (4, QUARTERS, depth + EXTRA * len(more), width)
    out = pl.BlockSpec((1,) + shape[1:], lambda i, info: (i, 0, 0, 0))
    return pl.pallas_call(
        functools.partial(weight_grads_kernel, parts),
        grid_spec=pltpu.PrefetchScalarGridSpec(
            num_scalar_prefetch=1,
            grid=(4,),
            in_specs=[strip] * len(strips)
            + [
                pl.BlockSpec(a.shape, lambda i, info, n=a.ndim: (0,) * n)
                for a in (*grads, *more)
            ],
            out_specs=(out, out),
        ),
        out_shape=(jax.ShapeDtypeStruct(shape, LOW),) * 2,
        compiler_params=params(),
        cost_estimate=LITTLE,
        name="weight_gradients",
    )(info, *strips, *grads, *more)


def position_of(token_index):
    branch_place = TRUNK + (token_index - TRUNK) % BRANCH
    leaf_place = TRUNK + BRANCH + (token_index - TOK_DEV) % BRANCH
    return jnp.where(
        token_index < TRUNK, token_index, jnp.where(token_index < TOK_DEV, branch_place, leaf_place)
    )


def rotary_tables(positions):
    half_dim = HEAD_DIM // 2
    frequency = ROPE_BASE ** (-jnp.arange(half_dim, dtype=jnp.float32) / half_dim)
    angles = positions.astype(jnp.float32)[:, None] * frequency[None, :]
    cosine, sine = (jnp.cos(angles), jnp.sin(angles))
    return (
        jnp.concatenate([cosine, cosine], axis=1),
        jnp.concatenate([-sine, sine], axis=1),
    )


def after(values, *earlier):
    return lax.optimization_barrier((values, earlier))[0]


def fast_mesh():
    return lax.axis_size("rows") == 8 and lax.axis_size("cols") == 4


SLOT_SHARD = ((0, 2, 1, 3), (1, 3, 0, 2), (2, 0, 1, 3), (3, 1, 2, 0))
UP = [(0, 1), (1, 2), (2, 3)]
DOWN = [(1, 0), (2, 1), (3, 2)]
FAR = [(0, 3), (3, 0)]


def send_near(block):
    return lax.ppermute(block, "cols", DOWN), lax.ppermute(block, "cols", UP)


def send_far(block):
    return lax.ppermute(block, "cols", FAR)


def send_second(block, near):
    place = lax.axis_index("cols")
    above, below = near
    payload = jnp.where(place == 1, above, jnp.where(place == 2, below, block))
    return lax.ppermute(payload, "cols", [(3, 1), (1, 0), (0, 2), (2, 3)])


def slot_list(block, near, second, far):
    place = lax.axis_index("cols")
    above, below = near
    end = (place == 0) | (place == 3)
    return [
        block,
        second,
        jnp.where(place == 0, above, below),
        jnp.where(end, far, above),
    ]


def reduce_first(second, fourth):
    relay = lax.ppermute(second, "cols", [(1, 3), (0, 1), (2, 0), (3, 2)])
    return relay, lax.ppermute(fourth, "cols", FAR)


def reduce_second(third, fourth, relay):
    place = lax.axis_index("cols")
    relayed = relay.astype(WIDE)
    upward_load = (
        jnp.where(place == 0, third, fourth).astype(WIDE) + jnp.where(place == 1, relayed, 0.0)
    ).astype(LOW)
    downward_load = (third.astype(WIDE) + jnp.where(place == 2, relayed, 0.0)).astype(LOW)
    return (
        lax.ppermute(upward_load, "cols", UP),
        lax.ppermute(downward_load, "cols", DOWN),
    )


def reduce_last(own, first, second):
    place = lax.axis_index("cols")
    relay, far = first
    below, above = second
    end = (place == 0) | (place == 3)
    return (
        own.astype(WIDE)
        + below.astype(WIDE)
        + above.astype(WIDE)
        + jnp.where(end, relay.astype(WIDE) + far.astype(WIDE), 0.0)
    )


def flip(block, bit):
    count = lax.axis_size("rows")
    return lax.ppermute(block, "rows", [(i, i ^ bit) for i in range(count)])


def add_low(one, two):
    return (one.astype(WIDE) + two.astype(WIDE)).astype(LOW)


def chip_sums(keep, got, chips, part):
    return jnp.stack([add_low(keep[i][part], got[i][part]) for i in chips])


def halves(keep):
    half = keep.shape[1] // 2
    return slice(0, half), slice(half, None)


def chips_first(keep, got):
    one, two = halves(keep)
    return chip_sums(keep, got, (1, 3), one), chip_sums(keep, got, (2, 3), two)


def chips_second(keep, got, got_x, got_y):
    one, two = halves(keep)
    near_x = chip_sums(keep, got, (0, 2), one)
    near_y = chip_sums(keep, got, (0, 1), two)
    got_xy = flip(add_low(near_x[1], got_x[1]), 4)
    got_yx = flip(add_low(near_y[1], got_y[1]), 2)
    return (near_x[0], got_x[0], got_xy, near_y[0], got_y[0], got_yx)


def turn_corner(beside, across):
    half = beside.shape[0] // 2
    return jnp.concatenate([flip(beside[:half], 4), flip(across[half:], 2)], axis=0)


def send_chips(sums):
    return flip(sums[0], 2), flip(sums[1], 4)


def sum_parts(parts):
    wide = [a.astype(WIDE) for a in parts]
    if len(wide) == 1:
        return wide[0]
    return jnp.concatenate([wide[0] + wide[1] + wide[2], wide[3] + wide[4] + wide[5]], axis=0)


def on_device(
    tokens,
    query_weight,
    key_weight,
    value_weight,
    out_weight,
    router_weight,
    attention_gain,
    experts_gain,
    gate_weight,
    upward_weight,
    down_weight,
    routes,
    leaf_parent,
    cotangent,
):
    row_count = lax.axis_size("rows")
    col_count = lax.axis_size("cols")
    row_place = lax.axis_index("rows")
    col_place = lax.axis_index("cols")
    fast = fast_mesh()
    parity = lax.rem(col_place, 2)
    tree_id = lax.div(row_place * col_count + col_place, 2)
    parent_row = lax.dynamic_slice_in_dim(leaf_parent, tree_id, 1, 0)[0]
    depth, query_part = query_weight.shape
    key_part = key_weight.shape[1]
    router_part = router_weight.shape[1]
    gain_part = attention_gain.shape[0]
    expert_total = router_part * col_count
    local_experts = gate_weight.shape[0]
    capacity = TOK_DEV * TOP // expert_total * 5 // 4

    shards = (
        jnp.asarray(SLOT_SHARD, jnp.int32)[col_place]
        if fast
        else jnp.arange(4, dtype=jnp.int32)
    )
    branch_rows = jnp.where(parity == 0, TRUNK + BRANCH * parent_row, TRUNK)
    info = jnp.concatenate(
        [jnp.stack([row_place, parity]), shards, branch_rows, jnp.zeros((2,), jnp.int32)]
    ).astype(jnp.int32)

    packed = jnp.concatenate([query_weight, key_weight, value_weight, out_weight], axis=1)
    local_index = (1 - parity) * TOK_DEV + jnp.arange(TOK_DEV, dtype=jnp.int32)
    cosine, sine = rotary_tables(position_of(local_index))
    shard_blocks = [
        jnp.concatenate(
            [gate_weight[expert].T, upward_weight[expert].T, down_weight[expert]], axis=0
        )
        for expert in range(local_experts)
    ]
    expert_weights = []
    for block in shard_blocks:
        if expert_weights:
            block = after(block, expert_weights[-1])
        expert_weights.append(lax.all_gather(block, "cols", axis=0))
    if fast:
        wide = packed.shape[1]
        gains = jnp.concatenate([attention_gain, experts_gain])[None, :]
        packed = jnp.concatenate(
            [
                packed,
                jnp.pad(router_weight.T, ((0, 0), (0, wide - depth))),
                jnp.pad(gains, ((0, 0), (0, wide - 2 * gain_part))),
                jnp.pad(routes.T.astype(LOW), ((0, 0), (0, wide - TOK_DEV))),
                jnp.zeros((EXTRA - router_part - 1 - TOP, wide), LOW),
            ],
            axis=0,
        )
        packed_near = send_near(packed)
        packed_far = send_far(packed)
        packed_second = send_second(packed, packed_near)
        grad_flips = (flip(cotangent, 2), flip(cotangent, 4))
        own = jnp.stack(slot_list(packed, packed_near, packed_second, packed_far))
        own = after(own, info, cosine, sine, *grad_flips)
        beside, across = flip(own, 2), flip(own, 4)
        own_in = flip(own, 1)
        beside, across = after((beside, across), own_in)
        corner = [flip(beside[:2], 4), flip(across[2:], 2)]
        pair_in = flip(jnp.concatenate([beside, across], axis=0), 1)
        corner_in = [flip(piece, 1) for piece in corner]
        pieces = [own, own_in, beside, across, *corner, pair_in, *corner_in]
        at = depth + router_part + 1
        near_slots = [own, own_in, beside, pair_in, across, pair_in[4:], corner[0], corner_in[0]]
        routes_all = jnp.stack([part[0, at : at + TOP, :TOK_DEV] for part in near_slots])
        routes_all = routes_all.astype(jnp.int32)
        chosen, place_rows = tables(info, routes_all, capacity, local_experts, expert_total)
        query_refs = pair_refs = out_refs = pieces
        extra_rows = extras(info, pieces)
        router_all = extra_rows[:, :router_part, :depth]
        attention_scale = extra_rows[:, router_part, :gain_part]
        experts_scale = extra_rows[:, router_part, gain_part : 2 * gain_part]
    else:
        packed_all = lax.all_gather(lax.all_gather(packed, "cols", axis=0), "rows", axis=0)

        def unpack(start, width):
            part = packed_all[..., start : start + width]
            return jnp.swapaxes(part, 1, 2).reshape(row_count * depth, col_count * width)

        key_at = query_part
        query_refs = [unpack(0, query_part)]
        pair_refs = [
            jnp.concatenate(
                [
                    unpack(key_at, key_part).reshape(D, QUARTERS, -1),
                    unpack(key_at + key_part, key_part).reshape(D, QUARTERS, -1),
                ],
                axis=2,
            ).reshape(D, -1)
        ]
        out_refs = [unpack(key_at + 2 * key_part, query_part)]
        routes_all = lax.all_gather(routes.T, "rows", axis=0)
        chosen, place_rows = tables(info, routes_all, capacity, local_experts, expert_total)
        axes = ("rows", "cols")
        router_all = jnp.swapaxes(lax.all_gather(router_weight, axes, axis=0), 1, 2)
        attention_scale = lax.all_gather(attention_gain, axes, axis=0)
        experts_scale = lax.all_gather(experts_gain, axes, axis=0)

    attention_scale = attention_scale.reshape(1, D).astype(WIDE)
    experts_scale = experts_scale.reshape(1, D).astype(WIDE)
    router_rows = jnp.transpose(
        router_all.reshape(row_count, col_count, router_part, depth), (1, 2, 0, 3)
    ).reshape(expert_total, D)
    router_cols = router_rows.T
    normed, own_pair = key_value(info, tokens, attention_scale, cosine, sine, pair_refs)
    pairs = [(i + 1, i) for i in range(0, col_count, 2)]
    partner = lax.ppermute(own_pair, "cols", pairs)
    queries = query(info, normed, cosine, sine, query_refs)
    if fast:
        grad_flips = after(grad_flips, own_pair)
        grad_corner = turn_corner(*grad_flips)
        queries = after(queries, grad_corner)
    heads = attention(info, queries, own_pair, partner)
    if fast:
        grad_near = [cotangent, *grad_flips, grad_corner]
        grad_blocks = [block for one in grad_near for block in (one, flip(one, 1))]
        heads = after(heads, *grad_blocks, expert_weights[0])
    else:
        grad_all = lax.all_gather(cotangent, "rows", axis=0)
        grad_blocks = [grad_all[q] for q in range(row_count)]
    residual, normed_two = out_projection(info, heads, tokens, experts_scale, out_refs)

    if fast:
        beside, across = flip(normed_two, 2), flip(normed_two, 4)
        beside_in = flip(normed_two, 1)
    else:
        rows_all = lax.all_gather(normed_two, "rows", axis=0)
    grad_rows = pick_rows(chosen, grad_blocks, local_experts)

    def place_block(q, block, picked):
        return dispatch(
            q, info, block, chosen, routes_all, router_cols, local_experts, picked
        )

    if fast:
        half = TOK_DEV // 2
        picked = place_block(0, normed_two, None)
        picked = place_block(1, beside_in, picked)
        beside, across = after((beside, across), picked)
        corner = [flip(beside[:half], 4), flip(across[half:], 2)]
        picked = after(picked, *grad_rows)
        picked = place_block(2, beside, picked)
        picked = place_block(4, across, picked)
        beside_in = flip(beside, 1)
        across_in = flip(after(across, beside_in), 1)
        picked = place_block(3, beside_in, picked)
        picked = place_block(5, across_in, picked)
        corner = jnp.concatenate(after(corner, picked), axis=0)
        corner_in = flip(corner, 1)
        picked = place_block(6, corner, picked)
        picked = place_block(7, corner_in, picked)
    else:
        picked = None
        for q in range(row_count):
            picked = place_block(q, rows_all[q], picked)
    height = row_count * capacity
    token_rows = [a.reshape(height, D) for a in picked[:local_experts]]
    grad_rows = [a.reshape(height, D) for a in grad_rows]
    share_rows = [a.reshape(height, 1) for a in picked[local_experts:]]

    out_rows, back_rows, gate_dots, reduced = ([], [], [], [])
    for e in range(local_experts):
        rows_in = after(token_rows[e], *reduced_in) if e else token_rows[e]
        out_row, back_row, grad_row, acts, dots = expert(
            rows_in, grad_rows[e], share_rows[e], expert_weights[e]
        )
        out_rows.append(out_row.reshape(row_count, capacity, D))
        back_rows.append(back_row.reshape(row_count, capacity, D))
        gate_dots.append(dots.reshape(row_count, capacity, 1))
        if fast and e == 1:
            got = flip(combine(info, chosen, back_rows, 1, 2, gate_dots), 1)
            back_keep = combine(info, chosen, back_rows, 0, 2, gate_dots)
            back_first = chips_first(back_keep, got)
            acts = after(acts, *back_first)
            back_flips = send_chips(back_first)
        slots = expert_grads(acts, token_rows[e], grad_row)
        reduced_in = (slots,)
        if e:
            slots = after(slots, reduced[-1])
        reduced.append(lax.psum_scatter(slots, "cols", scatter_dimension=0, tiled=False))

    if fast:
        back_parts = chips_second(back_keep, got, *after(back_flips, slots))
        out_rows = [after(a, back_parts[1], back_parts[4]) for a in out_rows]
        out_got = flip(combine(info, chosen, out_rows, 1, 2), 1)
        out_keep = combine(info, chosen, out_rows, 0, 2)
        back_parts = after(back_parts, out_keep, out_got, slots, reduced[0])
    else:
        spread_dots = spread(place_rows, gate_dots)
        grad_shares = lax.all_to_all(spread_dots, "rows", split_axis=0, concat_axis=0, tiled=True)

        def summed(rows):
            part = combine(info, chosen, rows, 0, 1)
            return lax.psum_scatter(part, "rows", scatter_dimension=0).astype(WIDE)

        back_parts = (summed(back_rows), grad_shares.reshape(expert_total, TOK_DEV))
        mixture = (summed(out_rows),)

    grad_residual, grad_branch, grad_heads, experts_gain_grad, router_grad = branch_back(
        info,
        residual,
        normed_two,
        back_parts,
        cotangent,
        routes.T,
        router_rows,
        experts_scale,
        out_refs,
    )
    if fast:
        out_first = chips_first(out_keep, out_got)
        out_flips = send_chips(out_first)
        grad_heads = after(grad_heads, *out_first)
        router_parts = jnp.transpose(
            router_grad.astype(LOW).reshape(col_count, router_part, row_count, depth),
            (2, 0, 1, 3),
        ).reshape(row_count * col_count, router_part, depth)
        gain_rows = experts_gain_grad.astype(LOW).reshape(row_count * col_count, 1, gain_part)
        extra = jnp.concatenate(
            [
                jnp.pad(router_parts, ((0, 0), (0, 0), (0, wide - depth))),
                jnp.pad(gain_rows, ((0, 0), (0, 0), (0, wide - gain_part))),
                jnp.zeros((row_count * col_count, EXTRA - router_part - 1, wide), LOW),
            ],
            axis=1,
        )
    grad_query, own_grad, source_grad = attention_back(
        info, queries, own_pair, partner, grad_heads, cosine, sine
    )
    arrived = lax.ppermute(source_grad.astype(LOW), "cols", [(j, i) for i, j in pairs])
    grad_pair = join_grads(info, own_grad, source_grad, arrived, cosine, sine)
    if fast:
        grad_branch = after(grad_branch, *out_flips)
        keep, send = weight_grads(
            info,
            [normed, heads],
            [grad_query, grad_pair, grad_branch],
            ((0, 2, query_part), (0, 3, 2 * key_part), (1, 4, query_part)),
            extra,
        )
        sent = flip(send, 1)
        grad_pair = after(grad_pair, keep)
    tokens_grad, attention_gain_grad = token_back(
        info, grad_query, grad_pair, tokens, grad_residual, attention_scale, query_refs, pair_refs
    )

    if fast:
        sent_first = chips_first(keep, sent)
        sent_chips = send_chips(sent_first)
        mixture = chips_second(out_keep, out_got, *out_flips)
        slots = sum_parts(chips_second(keep, sent, *sent_chips))
        width = query_part + 2 * key_part
        own_slots = own
        gain_sums = sum(
            jnp.sum(own_slots[i][:depth, :width].astype(WIDE) * slots[i, :depth, :width], axis=1)
            for i in range(4)
        )
        own_gains = lax.dynamic_slice_in_dim(attention_scale[0], row_place * depth, depth, 0)
        gain_sums = (gain_sums / own_gains).reshape(col_count, 1, gain_part)
        gain_sums = jnp.pad(
            jnp.take(gain_sums, shards, axis=0),
            ((0, 0), (depth + router_part + 1, EXTRA - router_part - 2), (0, wide - gain_part)),
        )
        slots = (slots + gain_sums).astype(LOW)

        def cols_sum(slots):
            sent_first = reduce_first(slots[1], slots[3])
            sent_second = reduce_second(slots[2], slots[3], sent_first[0])
            return reduce_last(slots[0], sent_first, sent_second)

        sums = cols_sum(slots)
        router_sum = sums[depth : depth + router_part, :depth].T
        experts_gain_sum = sums[depth + router_part, :gain_part]
        attention_gain_sum = sums[depth + router_part + 1, :gain_part]
        sums = sums[:depth]
    else:
        full_grads = [
            tn(normed, grad_query),
            *jnp.moveaxis(tn(normed, grad_pair).reshape(D, QUARTERS, 2, -1), 2, 0),
            tn(heads, grad_branch),
        ]
        packed_grad = jnp.concatenate(
            [
                grad.astype(LOW).reshape(row_count, depth, col_count, -1)
                for grad in full_grads
            ],
            axis=3,
        )
        row_sums = lax.psum_scatter(packed_grad, "rows", scatter_dimension=0)
        sums = lax.psum_scatter(row_sums, "cols", scatter_dimension=1).astype(WIDE)
        small_grads = jnp.concatenate(
            [
                attention_gain_grad.reshape(-1, gain_part),
                experts_gain_grad.reshape(-1, gain_part),
                jnp.transpose(
                    router_grad.reshape(col_count, router_part, row_count, depth), (2, 0, 3, 1)
                ).reshape(row_count * col_count, depth * router_part),
            ],
            axis=1,
        )
        small_grads = small_grads.reshape(row_count, -1)
        small_grads = lax.all_to_all(small_grads, "rows", split_axis=0, concat_axis=0, tiled=True)
        small_grads = jnp.sum(small_grads, axis=0).reshape(col_count, -1)
        small_grads = lax.all_to_all(small_grads, "cols", split_axis=0, concat_axis=0, tiled=True)
        small_sums = jnp.sum(small_grads, axis=0)
        attention_gain_sum = small_sums[:gain_part]
        experts_gain_sum = small_sums[gain_part : 2 * gain_part]
        router_sum = small_sums[2 * gain_part :].reshape(depth, router_part)

    layer_output = (residual + sum_parts(mixture)).astype(LOW)
    key_at = query_part
    value_at = key_at + key_part
    out_at = value_at + key_part
    part = down_weight.shape[1]
    expert_sums = [block.astype(WIDE) for block in reduced]
    gate_grad, upward_grad, down_grad = (
        jnp.stack([sums_of[which * part : (which + 1) * part] for sums_of in expert_sums])
        for which in range(3)
    )
    return (
        layer_output,
        tokens_grad,
        sums[:, :key_at],
        sums[:, key_at:value_at],
        sums[:, value_at:out_at],
        sums[:, out_at:],
        router_sum,
        attention_gain_sum,
        experts_gain_sum,
        jnp.swapaxes(gate_grad, 1, 2),
        jnp.swapaxes(upward_grad, 1, 2),
        down_grad,
    )


def solution(mesh):
    in_specs = (
        P(("rows", "cols"), None),
        P("rows", "cols"),
        P("rows", "cols"),
        P("rows", "cols"),
        P("rows", "cols"),
        P("rows", "cols"),
        P(("rows", "cols")),
        P(("rows", "cols")),
        P("rows", None, "cols"),
        P("rows", None, "cols"),
        P("rows", "cols", None),
        P(("rows", "cols"), None),
        P(),
        P(("rows", "cols"), None),
    )
    out_specs = (
        P(("rows", "cols"), None),
        P(("rows", "cols"), None),
        P("rows", "cols"),
        P("rows", "cols"),
        P("rows", "cols"),
        P("rows", "cols"),
        P("rows", "cols"),
        P(("rows", "cols")),
        P(("rows", "cols")),
        P("rows", None, "cols"),
        P("rows", None, "cols"),
        P("rows", "cols", None),
    )
    return jax.shard_map(
        on_device, mesh=mesh, in_specs=in_specs, out_specs=out_specs, check_vma=False
    )
```

```python
import functools

import jax
import jax.numpy as jnp
from jax import lax
from jax.experimental import pallas as pl
from jax.experimental.pallas import tpu as pltpu
from jax.sharding import PartitionSpec as P

D = 1536
HEADS = 12
KV_HEADS = 2
HEAD_DIM = 128
TOP = 4
TOK_DEV = 512
BRANCHES = 4
LEAVES = 8
TRUNK = 256
BRANCH = 64

EPSILON = 1e-06
ROPE_BASE = 10000.0
MASKED = -1e30
LOW = jnp.bfloat16
WIDE = jnp.float32
KEY_WIDTH = KV_HEADS * HEAD_DIM
GROUP = HEADS // KV_HEADS
QUARTERS = 4
VMEM_LIMIT = 56 * 1024 * 1024

ANY = pl.BlockSpec(memory_space=pl.ANY)
SMEM = pl.BlockSpec(memory_space=pltpu.SMEM)


def nn(one, two):
    return lax.dot_general(one, two, (((1,), (0,)), ((), ())), preferred_element_type=WIDE)


def nt(one, two):
    return lax.dot_general(one, two, (((1,), (1,)), ((), ())), preferred_element_type=WIDE)


def tn(one, two):
    return lax.dot_general(one, two, (((0,), (0,)), ((), ())), preferred_element_type=WIDE)


def whole(shape):
    return pl.BlockSpec(shape, lambda *_: (0,) * len(shape))


LITTLE = pl.CostEstimate(flops=1, bytes_accessed=1, transcendentals=0)


def params():
    return pltpu.CompilerParams(vmem_limit_bytes=VMEM_LIMIT)


def turn(values, cosine, sine):
    return values * cosine + pltpu.roll(values, HEAD_DIM // 2, 1) * sine


def turn_back(values, cosine, sine):
    return values * cosine - pltpu.roll(values, HEAD_DIM // 2, 1) * sine


SLOTS = range(4)
PIECES = (
    tuple((0, slot) for slot in SLOTS),
    tuple((1, slot) for slot in SLOTS),
    tuple((2, slot) for slot in SLOTS),
    tuple((4, slot) for slot in SLOTS),
    ((6, 0), (6, 1)),
    ((6, 2), (6, 3)),
    tuple((flip_bits, slot) for flip_bits in (3, 5) for slot in SLOTS),
    ((7, 0), (7, 1)),
    ((7, 2), (7, 3)),
)
EXTRA = 16


STEP = 768


def weight_copies(info, refs, target, sem, start, width):
    if len(refs) == 1:
        return [pltpu.make_async_copy(refs[0], target, sem)]
    depth = refs[0].shape[1] - EXTRA
    copies = []
    for ref, parts in zip(refs, PIECES):
        for at, (flip_bits, slot) in enumerate(parts):
            row = pl.multiple_of((info[0] ^ flip_bits) * depth, depth)
            col = pl.multiple_of(info[2 + slot] * width, 128)
            copies.append(
                pltpu.make_async_copy(
                    ref.at[at, pl.ds(0, depth), pl.ds(start, width)],
                    target.at[pl.ds(row, depth), pl.ds(col, width)],
                    sem,
                )
            )
    return copies


def extras_kernel(info, *rest):
    refs, (out, sem) = rest[:-2], rest[-2:]
    depth = refs[0].shape[1] - EXTRA
    copies = []
    for ref, parts in zip(refs, PIECES):
        for at, (flip_bits, slot) in enumerate(parts):
            to = (info[0] ^ flip_bits) * QUARTERS + info[2 + slot]
            copies.append(pltpu.make_async_copy(ref.at[at, pl.ds(depth, EXTRA)], out.at[to], sem))
    run_all(copies)
    wait_all(copies)


def extras(info, refs):
    return pl.pallas_call(
        extras_kernel,
        out_shape=jax.ShapeDtypeStruct((8 * QUARTERS, EXTRA, refs[0].shape[2]), LOW),
        in_specs=[SMEM] + [ANY] * len(refs),
        out_specs=pl.BlockSpec(memory_space=pltpu.VMEM),
        scratch_shapes=[pltpu.SemaphoreType.DMA],
        compiler_params=params(),
        cost_estimate=LITTLE,
        name="extra_rows",
    )(info, *refs)


def run_all(copies):
    for copy in copies:
        copy.start()


def wait_all(copies):
    for copy in copies:
        copy.wait()


def key_value_kernel(info, tokens, gain, cosine, sine, *rest):
    count = len(rest) - 4
    refs, (normed, out, weight, sem) = rest[:count], rest[count:]
    copies = weight_copies(info, refs, weight, sem, D // QUARTERS, 128)
    run_all(copies)
    values = tokens[...].astype(WIDE)
    factor = lax.rsqrt(jnp.mean(values * values, axis=-1, keepdims=True) + EPSILON)
    low = (values * factor * gain[...]).astype(LOW)
    normed[...] = low
    wait_all(copies)
    both = nn(low, weight[...])
    half = HEAD_DIM // 2
    first = lax.broadcasted_iota(jnp.int32, (TOK_DEV, HEAD_DIM), 1) < half
    for g in range(KV_HEADS):
        one = both[:, 256 * g : 256 * g + 128]
        two = both[:, 256 * g + 128 : 256 * g + 256]
        key = jnp.where(first, one, pltpu.roll(two, half, 1))
        value = jnp.where(first, pltpu.roll(one, half, 1), two)
        out[:, 128 * g : 128 * g + 128] = turn(key, cosine[...], sine[...]).astype(LOW)
        out[:, KEY_WIDTH + 128 * g : KEY_WIDTH + 128 * g + 128] = value.astype(LOW)


def key_value(info, tokens, gain, cosine, sine, refs):
    return pl.pallas_call(
        key_value_kernel,
        out_shape=(
            jax.ShapeDtypeStruct((TOK_DEV, D), LOW),
            jax.ShapeDtypeStruct((TOK_DEV, 2 * KEY_WIDTH), LOW),
        ),
        in_specs=[SMEM] + [pl.BlockSpec(memory_space=pltpu.VMEM)] * 4 + [ANY] * len(refs),
        out_specs=(pl.BlockSpec(memory_space=pltpu.VMEM),) * 2,
        scratch_shapes=[pltpu.VMEM((D, 2 * KEY_WIDTH), LOW), pltpu.SemaphoreType.DMA],
        compiler_params=params(),
        cost_estimate=LITTLE,
        name="norm_key_value",
    )(info, tokens, gain, cosine, sine, *refs)


def query_kernel(info, normed, cosine, sine, *rest):
    count = len(rest) - 3
    refs, (out, weight, sem) = rest[:count], rest[count:]

    @pl.when(pl.program_id(0) == 0)
    def _():
        copies = weight_copies(info, refs, weight, sem, 0, D // QUARTERS)
        run_all(copies)
        wait_all(copies)

    at = pl.multiple_of(pl.program_id(0) * STEP, STEP)
    lin = nn(normed[...], weight[:, pl.ds(at, STEP)])
    for h in range(STEP // HEAD_DIM):
        out[:, 128 * h : 128 * h + 128] = turn(
            lin[:, 128 * h : 128 * h + 128], cosine[...], sine[...]
        ).astype(LOW)


def query(info, normed, cosine, sine, refs):
    return pl.pallas_call(
        query_kernel,
        grid=(D // STEP,),
        out_shape=jax.ShapeDtypeStruct((TOK_DEV, D), LOW),
        in_specs=[SMEM, whole((TOK_DEV, D)), whole((TOK_DEV, 128)), whole((TOK_DEV, 128))]
        + [ANY] * len(refs),
        out_specs=pl.BlockSpec((TOK_DEV, STEP), lambda i: (0, i)),
        scratch_shapes=[pltpu.VMEM((D, D), LOW), pltpu.SemaphoreType.DMA],
        compiler_params=params(),
        cost_estimate=LITTLE,
        name="query_projection",
    )(info, normed, cosine, sine, *refs)


KEYS = TRUNK + 2 * BRANCH
CHUNKS = TOK_DEV // BRANCH


def chunk_keys(info, source, own, column, chunk):
    at = pl.multiple_of(info[6 + chunk], BRANCH)
    rows = pl.multiple_of(chunk * BRANCH, BRANCH)
    columns = slice(column, column + HEAD_DIM)
    return jnp.concatenate(
        [
            source[0:TRUNK, columns],
            source[pl.ds(at, BRANCH), columns],
            own[pl.ds(rows, BRANCH), columns],
        ],
        axis=0,
    )


def chunk_allowed(info, chunk, query_axis, shape):
    query_row = lax.broadcasted_iota(jnp.int32, shape, query_axis) & (BRANCH - 1)
    key = lax.broadcasted_iota(jnp.int32, shape, 1 - query_axis)
    leaves = info[1] == 0
    trunk = jnp.logical_and(jnp.logical_not(leaves), chunk < TRUNK // BRANCH)
    limit = jnp.where(trunk, chunk * BRANCH + query_row, TRUNK - 1)
    branch_limit = jnp.where(leaves, TRUNK + BRANCH - 1, 0)
    own_limit = jnp.where(trunk, 0, query_row + TRUNK + BRANCH)
    top = jnp.where(key < TRUNK, limit, jnp.where(key < TRUNK + BRANCH, branch_limit, own_limit))
    return key <= top


def group_rows(ref, g):
    first = g * GROUP
    return jnp.concatenate(
        [ref[:, 128 * h : 128 * h + 128] for h in range(first, first + GROUP)], axis=0
    )


def keep_source(info, partner, own, source):
    @pl.when(pl.program_id(0) == 0)
    def _():
        @pl.when(info[1] == 0)
        def _():
            source[...] = partner[...]

        @pl.when(info[1] != 0)
        def _():
            source[...] = own[...]


def attention_kernel(info, queries, own, partner, out, source):
    keep_source(info, partner, own, source)
    chunk = pl.program_id(0)
    rows = GROUP * BRANCH
    allowed = chunk_allowed(info, chunk, 0, (rows, KEYS))
    for g in range(KV_HEADS):
        keys = chunk_keys(info, source, own, 128 * g, chunk)
        values = chunk_keys(info, source, own, KEY_WIDTH + 128 * g, chunk)
        scores = nt(group_rows(queries, g), keys) * HEAD_DIM**-0.5
        scores = jnp.where(allowed, scores, MASKED)
        weights = jnp.exp(scores - jnp.max(scores, axis=1, keepdims=True))
        total = jnp.sum(weights, axis=1, keepdims=True)
        mixed = nn((weights * (1.0 / total)).astype(LOW), values).astype(LOW)
        for h in range(GROUP):
            at = (g * GROUP + h) * 128
            out[:, at : at + 128] = mixed[h * BRANCH : (h + 1) * BRANCH]


def attention(info, queries, own, partner):
    return pl.pallas_call(
        attention_kernel,
        grid=(CHUNKS,),
        out_shape=jax.ShapeDtypeStruct((TOK_DEV, D), LOW),
        in_specs=[
            SMEM,
            pl.BlockSpec((BRANCH, D), lambda i: (i, 0)),
            whole((TOK_DEV, 2 * KEY_WIDTH)),
            whole((TOK_DEV, 2 * KEY_WIDTH)),
        ],
        out_specs=pl.BlockSpec((BRANCH, D), lambda i: (i, 0)),
        scratch_shapes=[pltpu.VMEM((TOK_DEV, 2 * KEY_WIDTH), LOW)],
        compiler_params=params(),
        cost_estimate=LITTLE,
        name="tree_attention",
    )(info, queries, own, partner)


def attention_back_kernel(
    info, queries, own, partner, grads, cosine, sine, grad_query, own_grad, source_grad, source
):
    keep_source(info, partner, own, source)
    chunk = pl.program_id(0)

    @pl.when(chunk == 0)
    def _():
        source_grad[...] = jnp.zeros_like(source_grad)

    rows = GROUP * BRANCH
    scale = HEAD_DIM**-0.5
    allowed = chunk_allowed(info, chunk, 1, (KEYS, rows))
    at = pl.multiple_of(info[6 + chunk], BRANCH)
    for g in range(KV_HEADS):
        keys = chunk_keys(info, source, own, 128 * g, chunk)
        values = chunk_keys(info, source, own, KEY_WIDTH + 128 * g, chunk)
        query_rows = group_rows(queries, g)
        grad_rows = group_rows(grads, g)
        scores = jnp.where(allowed, nt(keys, query_rows) * scale, MASKED)
        weights = jnp.exp(scores - jnp.max(scores, axis=0, keepdims=True))
        probs = weights * (1.0 / jnp.sum(weights, axis=0, keepdims=True))
        grad_probs = nt(values, grad_rows)
        mean = jnp.sum(probs * grad_probs, axis=0, keepdims=True)
        grad_scores = (probs * (grad_probs - mean)).astype(LOW)
        grad_values = nn(probs.astype(LOW), grad_rows)
        grad_keys = nn(grad_scores, query_rows) * scale
        grad_queries = tn(grad_scores, keys) * scale
        for h in range(GROUP):
            to = (g * GROUP + h) * 128
            grad_query[:, to : to + 128] = turn_back(
                grad_queries[h * BRANCH : (h + 1) * BRANCH], cosine[...], sine[...]
            ).astype(LOW)
        for column, grad in ((128 * g, grad_keys), (KEY_WIDTH + 128 * g, grad_values)):
            columns = slice(column, column + 128)
            source_grad[0:TRUNK, columns] += grad[0:TRUNK]
            source_grad[pl.ds(at, BRANCH), columns] += grad[TRUNK : TRUNK + BRANCH]
            own_grad[:, columns] = grad[TRUNK + BRANCH :]


def attention_back(info, queries, own, partner, grads, cosine, sine):
    chunked = pl.BlockSpec((BRANCH, D), lambda i: (i, 0))
    pair = (TOK_DEV, 2 * KEY_WIDTH)
    return pl.pallas_call(
        attention_back_kernel,
        grid=(CHUNKS,),
        out_shape=(
            jax.ShapeDtypeStruct((TOK_DEV, D), LOW),
            jax.ShapeDtypeStruct(pair, WIDE),
            jax.ShapeDtypeStruct(pair, WIDE),
        ),
        in_specs=[
            SMEM,
            chunked,
            whole(pair),
            whole(pair),
            chunked,
            pl.BlockSpec((BRANCH, 128), lambda i: (i, 0)),
            pl.BlockSpec((BRANCH, 128), lambda i: (i, 0)),
        ],
        out_specs=(
            chunked,
            pl.BlockSpec((BRANCH, 2 * KEY_WIDTH), lambda i: (i, 0)),
            whole(pair),
        ),
        scratch_shapes=[pltpu.VMEM(pair, LOW)],
        compiler_params=params(),
        cost_estimate=LITTLE,
        name="tree_attention_back",
    )(info, queries, own, partner, grads, cosine, sine)


def out_kernel(info, heads, tokens, gain, *rest):
    count = len(rest) - 4
    refs, (residual, normed, weight, sem) = rest[:count], rest[count:]

    @pl.when(pl.program_id(0) == 0)
    def _():
        copies = weight_copies(info, refs, weight, sem, D // QUARTERS + 128, D // QUARTERS)
        run_all(copies)
        wait_all(copies)

    at = pl.ds(pl.multiple_of(pl.program_id(0) * STEP, STEP), STEP)
    residual[:, at] = tokens[:, at].astype(WIDE) + nn(heads[...], weight[:, at])

    @pl.when(pl.program_id(0) == pl.num_programs(0) - 1)
    def _():
        values = residual[...]
        factor = lax.rsqrt(jnp.mean(values * values, axis=-1, keepdims=True) + EPSILON)
        normed[...] = (values * factor * gain[...]).astype(LOW)


def out_projection(info, heads, tokens, gain, refs):
    full = (TOK_DEV, D)
    return pl.pallas_call(
        out_kernel,
        grid=(D // STEP,),
        out_shape=(jax.ShapeDtypeStruct(full, WIDE), jax.ShapeDtypeStruct(full, LOW)),
        in_specs=[SMEM, whole(full), whole(full), whole((1, D))] + [ANY] * len(refs),
        out_specs=(whole(full), whole(full)),
        scratch_shapes=[pltpu.VMEM((D, D), LOW), pltpu.SemaphoreType.DMA],
        compiler_params=params(),
        cost_estimate=LITTLE,
        name="out_projection",
    )(info, heads, tokens, gain, *refs)


def hits_of(routes, ids):
    hit = ids == routes[0, 0:1]
    for k in range(1, TOP):
        hit = jnp.logical_or(hit, ids == routes[0, k : k + 1])
    return hit


def tables_kernel(capacity, local, total, info, routes, chosen_out, place_out, earlier):
    @pl.when(pl.program_id(0) == 0)
    def _():
        one = lax.broadcasted_iota(jnp.int32, (TOK_DEV, TOK_DEV), 0)
        two = lax.broadcasted_iota(jnp.int32, (TOK_DEV, TOK_DEV), 1)
        earlier[...] = jnp.where(one < two, 1.0, 0.0).astype(LOW)

    ids = lax.broadcasted_iota(jnp.int32, (total, TOK_DEV), 0)
    hit = hits_of(routes, ids)
    rank = nn(jnp.where(hit, 1.0, 0.0).astype(LOW), earlier[...])
    place = jnp.where(hit, rank, -1.0)
    spots = lax.broadcasted_iota(jnp.int32, (capacity, TOK_DEV), 0).astype(WIDE)
    place_out[0] = jnp.full(place_out.shape[1:], -1.0, WIDE)
    for e in range(local):
        mine = ids == info[0] * local + e
        place_row = jnp.sum(jnp.where(mine, place, 0.0), axis=0, keepdims=True)
        place_out[0, e : e + 1] = place_row
        chosen_out[0, e * capacity : (e + 1) * capacity] = jnp.where(
            spots == place_row, 1.0, 0.0
        ).astype(LOW)


def tables(info, routes, capacity, local, total):
    count = routes.shape[0]
    return pl.pallas_call(
        functools.partial(tables_kernel, capacity, local, total),
        grid=(count,),
        in_specs=[SMEM, pl.BlockSpec((1, TOP, TOK_DEV), lambda i: (i, 0, 0))],
        out_specs=[
            pl.BlockSpec((1, local * capacity, TOK_DEV), lambda i: (i, 0, 0)),
            pl.BlockSpec((1, 8, TOK_DEV), lambda i: (i, 0, 0)),
        ],
        scratch_shapes=[pltpu.VMEM((TOK_DEV, TOK_DEV), LOW)],
        out_shape=[
            jax.ShapeDtypeStruct((count, local * capacity, TOK_DEV), LOW),
            jax.ShapeDtypeStruct((count, 8, TOK_DEV), WIDE),
        ],
        compiler_params=params(),
        cost_estimate=LITTLE,
        name="route_tables",
    )(info, routes)


def pick_kernel(local, count, chosen, *rest):
    blocks, outs = rest[:count], rest[count : count + local]
    picks, block_in, out_block, sem_in, sem_out = rest[count + local :]
    capacity = outs[0].shape[1]
    copies = [
        (
            pltpu.make_async_copy(chosen.at[q], picks.at[q], sem_in.at[q, 0]),
            pltpu.make_async_copy(blocks[q], block_in.at[q], sem_in.at[q, 1]),
        )
        for q in range(count)
    ]
    for pair in copies:
        run_all(pair)
    sent = []
    for q in range(count):
        wait_all(copies[q])
        out_block[q] = nn(picks[q], block_in[q]).astype(LOW)
        for e in range(local):
            copy = pltpu.make_async_copy(
                out_block.at[q, pl.ds(e * capacity, capacity)], outs[e].at[q], sem_out.at[q, e]
            )
            copy.start()
            sent.append(copy)
    wait_all(sent)


def pick_rows(chosen, blocks, local):
    count, height, _ = chosen.shape
    return pl.pallas_call(
        functools.partial(pick_kernel, local, count),
        in_specs=[ANY] * (1 + count),
        out_specs=[ANY] * local,
        out_shape=[jax.ShapeDtypeStruct((count, height // local, D), LOW)] * local,
        scratch_shapes=[
            pltpu.VMEM((count, height, TOK_DEV), LOW),
            pltpu.VMEM((count, TOK_DEV, D), LOW),
            pltpu.VMEM((count, height, D), LOW),
            pltpu.SemaphoreType.DMA((count, 2)),
            pltpu.SemaphoreType.DMA((count, local)),
        ],
        compiler_params=params(),
        cost_estimate=LITTLE,
        name="pick_rows",
    )(chosen, *blocks)


def dispatch_kernel(local, info, rows, chosen, routes, router, *rest):
    outs, logits = rest[2 * local : 4 * local], rest[-1]
    total = router.shape[1]
    step = pl.program_id(0)
    block = rows[...]
    rows_of = nn(chosen[0], block).astype(LOW)
    capacity = outs[0].shape[1]
    for e in range(local):
        outs[e][0] = rows_of[e * capacity : (e + 1) * capacity]
    part = nn(block, router[...])

    @pl.when(step == 0)
    def _():
        logits[...] = part

    @pl.when(step > 0)
    def _():
        logits[...] += part

    @pl.when(step == pl.num_programs(0) - 1)
    def _():
        values = logits[...].T
        ids = lax.broadcasted_iota(jnp.int32, (total, TOK_DEV), 0)
        weights = jnp.exp(values - jnp.max(values, axis=0, keepdims=True))
        hit = hits_of(routes, ids)
        share = weights / jnp.sum(jnp.where(hit, weights, 0.0), axis=0, keepdims=True)
        for e in range(local):
            mine = ids == info[0] * local + e
            share_row = jnp.sum(jnp.where(mine, share, 0.0), axis=0, keepdims=True)
            picked = chosen[0, e * capacity : (e + 1) * capacity].astype(WIDE)
            outs[local + e][0] = jnp.sum(picked * share_row, axis=1, keepdims=True)


def dispatch(at, info, rows, chosen, routes, router, local, earlier):
    count, height, _ = chosen.shape
    capacity = height // local
    total = router.shape[1]
    wide = D
    out_shape = [jax.ShapeDtypeStruct((count, capacity, D), LOW)] * local + [
        jax.ShapeDtypeStruct((count, capacity, 1), WIDE)
    ] * local
    if earlier is None:
        earlier = [jnp.zeros((8, 128), shape.dtype) for shape in out_shape]
        aliases = {}
    else:
        aliases = {5 + i: i for i in range(len(out_shape))}
    return pl.pallas_call(
        functools.partial(dispatch_kernel, local),
        grid=(D // wide,),
        in_specs=[
            SMEM,
            pl.BlockSpec((TOK_DEV, wide), lambda i: (0, i)),
            pl.BlockSpec((1, height, TOK_DEV), lambda i: (at, 0, 0)),
            pl.BlockSpec((1, TOP, TOK_DEV), lambda i: (at, 0, 0)),
            pl.BlockSpec((wide, total), lambda i: (i, 0)),
        ]
        + [ANY] * len(out_shape),
        out_specs=[pl.BlockSpec((1, capacity, wide), lambda i: (at, 0, i))] * local
        + [pl.BlockSpec((1, capacity, 1), lambda i: (at, 0, 0))] * local,
        scratch_shapes=[pltpu.VMEM((TOK_DEV, total), WIDE)],
        out_shape=out_shape,
        input_output_aliases=aliases,
        compiler_params=params(),
        cost_estimate=LITTLE,
        name="dispatch",
    )(info, rows, chosen, routes, router, *earlier)


def spread_kernel(local, place, *rest):
    dots, out = rest[:local], rest[local]
    spots = lax.broadcasted_iota(jnp.int32, (dots[0].shape[1], TOK_DEV), 0).astype(WIDE)
    for e in range(local):
        chosen = spots == place[0, e : e + 1]
        out[0, e : e + 1] = jnp.sum(jnp.where(chosen, dots[e][0], 0.0), axis=0, keepdims=True)


def spread(place, dots):
    count, capacity, _ = dots[0].shape
    local = len(dots)
    return pl.pallas_call(
        functools.partial(spread_kernel, local),
        grid=(count,),
        out_shape=jax.ShapeDtypeStruct((count, local, TOK_DEV), WIDE),
        in_specs=[pl.BlockSpec((1, 8, TOK_DEV), lambda i: (i, 0, 0))]
        + [pl.BlockSpec((1, capacity, 1), lambda i: (i, 0, 0))] * local,
        out_specs=pl.BlockSpec((1, local, TOK_DEV), lambda i: (i, 0, 0)),
        compiler_params=params(),
        cost_estimate=LITTLE,
        name="spread",
    )(place, *dots)


def expert_kernel(slots, info, rows, grads, shares, *rest):
    refs, (out_rows, back_rows, grad_rows, acts, dots, weight, sem) = rest[:-7], rest[-7:]
    part = weight.shape[1] // slots

    @pl.when(pl.program_id(0) == 0)
    def _():
        def copies(ref, slot):
            return [
                pltpu.make_async_copy(
                    ref.at[pl.ds(which * part, part)],
                    weight.at[which, pl.ds(pl.multiple_of(slot * part, part), part)],
                    sem,
                )
                for which in range(3)
            ]

        if len(refs) == 1:
            for slot in range(slots):
                run_all(copies(refs[0].at[slot], slot))
            for slot in range(slots):
                wait_all(copies(refs[0].at[slot], slot))
        else:
            block, second, above, below, far = refs
            low_end = info[2] == 0
            end = jnp.logical_or(low_end, info[2] == 3)
            run_all(copies(block, info[2]))
            run_all(copies(second, info[3]))

            @pl.when(low_end)
            def _():
                run_all(copies(above, info[4]))

            @pl.when(jnp.logical_not(low_end))
            def _():
                run_all(copies(below, info[4]))

            @pl.when(end)
            def _():
                run_all(copies(far, info[5]))

            @pl.when(jnp.logical_not(end))
            def _():
                run_all(copies(above, info[5]))

            for slot in range(slots):
                wait_all(copies(block, slot))

    row_block = rows[...]
    share = shares[...]
    grad_float = grads[...].astype(WIDE)
    grad_low = (share * grad_float).astype(LOW)
    grad_rows[...] = grad_low
    gate_act = nt(row_block, weight[0])
    upward = nt(row_block, weight[1])
    sigmoid = 1.0 / (1.0 + jnp.exp(-gate_act))
    silu = gate_act * sigmoid
    hidden = (silu * upward).astype(LOW)
    expert_out = nn(hidden, weight[2]).astype(LOW).astype(WIDE)
    out_rows[...] = (share * expert_out).astype(LOW)
    dots[...] = jnp.sum(grad_float * expert_out, axis=1, keepdims=True)
    grad_hidden = nt(grad_low, weight[2])
    grad_gate = (grad_hidden * upward * sigmoid * (1.0 + gate_act * (1.0 - sigmoid))).astype(LOW)
    grad_up = (grad_hidden * silu).astype(LOW)
    back_rows[...] = (nn(grad_gate, weight[0]) + nn(grad_up, weight[1])).astype(LOW)
    for which, act in enumerate((grad_gate, grad_up, hidden)):
        turned = act.T
        for slot in range(slots):
            acts[slot, which * part : (which + 1) * part] = turned[
                slot * part : (slot + 1) * part
            ]


EXPERT_ROWS = 256


def expert(info, rows, grads, shares, refs, slots):
    height = rows.shape[0]
    part = refs[0].shape[-2] // 3
    wide_block = pl.BlockSpec((EXPERT_ROWS, D), lambda i: (i, 0))
    thin_block = pl.BlockSpec((EXPERT_ROWS, 1), lambda i: (i, 0))
    return pl.pallas_call(
        functools.partial(expert_kernel, slots),
        grid=(height // EXPERT_ROWS,),
        out_shape=[jax.ShapeDtypeStruct((height, D), LOW)] * 3
        + [
            jax.ShapeDtypeStruct((slots, 3 * part, height), LOW),
            jax.ShapeDtypeStruct((height, 1), WIDE),
        ],
        in_specs=[SMEM, wide_block, wide_block, thin_block] + [ANY] * len(refs),
        out_specs=[wide_block] * 3
        + [pl.BlockSpec((slots, 3 * part, EXPERT_ROWS), lambda i: (0, 0, i)), thin_block],
        scratch_shapes=[pltpu.VMEM((3, slots * part, D), LOW), pltpu.SemaphoreType.DMA],
        compiler_params=params(),
        cost_estimate=LITTLE,
        name="expert",
    )(info, rows, grads, shares, *refs)


def expert_grads_kernel(acts, rows, grads, out):
    slots, height, _ = acts.shape
    part = height // 3
    for slot in range(slots):
        out[slot, : 2 * part] = nn(acts[slot, : 2 * part], rows[...]).astype(LOW)
        out[slot, 2 * part :] = nn(acts[slot, 2 * part :], grads[...]).astype(LOW)


def expert_grads(acts, rows, grads):
    slots, part, height = acts.shape
    strip = pl.BlockSpec((height, 256), lambda i: (0, i))
    return pl.pallas_call(
        expert_grads_kernel,
        grid=(D // 256,),
        out_shape=jax.ShapeDtypeStruct((slots, part, D), LOW),
        in_specs=[whole(acts.shape), strip, strip],
        out_specs=pl.BlockSpec((slots, part, 256), lambda i: (0, 0, i)),
        compiler_params=params(),
        cost_estimate=LITTLE,
        name="expert_gradients",
    )(acts, rows, grads)


SHARE_ROWS = 32


def combine_kernel(local, first, step, info, chosen, *rest):
    rows, dots, out = rest[:local], rest[local:-6], rest[-6]
    picks, rows_in, out_block, sem_in, sem_out = rest[-5:]
    number = out.shape[0]
    capacity = rows[0].shape[1]
    copies = []
    for n in range(number):
        q = first + step * n
        copies.append(
            [pltpu.make_async_copy(chosen.at[q], picks.at[n], sem_in.at[n, local])]
            + [
                pltpu.make_async_copy(
                    rows[e].at[q],
                    rows_in.at[n, pl.ds(e * capacity, capacity)],
                    sem_in.at[n, e],
                )
                for e in range(local)
            ]
        )
    for group in copies:
        run_all(group)
    sent = []
    for n in range(number):
        wait_all(copies[n])
        out_block[n, :TOK_DEV] = tn(picks[n], rows_in[n]).astype(LOW)
        if dots:
            row = lax.broadcasted_iota(jnp.int32, (SHARE_ROWS, D), 0)
            values = jnp.zeros((SHARE_ROWS, D), WIDE)
            for e in range(local):
                picked = picks[n, e * capacity : (e + 1) * capacity].astype(WIDE)
                share = picked * dots[e][first + step * n]
                high, low = split(jnp.sum(share, axis=0, keepdims=True))
                pieces = [high.astype(WIDE), low.astype(WIDE)]
                pieces.append(jnp.zeros((1, D - 2 * TOK_DEV), WIDE))
                line = jnp.concatenate(pieces, axis=1)
                values = jnp.where(row == info[0] * local + e, line, values)
            out_block[n, TOK_DEV:] = values.astype(LOW)
        copy = pltpu.make_async_copy(out_block.at[n], out.at[n], sem_out.at[n])
        copy.start()
        sent.append(copy)
    wait_all(sent)


def combine(info, chosen, rows, first, step, dots=()):
    count, capacity, _ = rows[0].shape
    local = len(rows)
    number = (count - first + step - 1) // step
    height = TOK_DEV + (SHARE_ROWS if dots else 0)
    return pl.pallas_call(
        functools.partial(combine_kernel, local, first, step),
        out_shape=jax.ShapeDtypeStruct((number, height, D), LOW),
        in_specs=[SMEM, ANY]
        + [ANY] * local
        + [pl.BlockSpec(memory_space=pltpu.VMEM)] * len(dots),
        out_specs=ANY,
        scratch_shapes=[
            pltpu.VMEM((number, local * capacity, TOK_DEV), LOW),
            pltpu.VMEM((number, local * capacity, D), LOW),
            pltpu.VMEM((number, height, D), LOW),
            pltpu.SemaphoreType.DMA((number, local + 1)),
            pltpu.SemaphoreType.DMA((number,)),
        ],
        compiler_params=params(),
        cost_estimate=LITTLE,
        name="combine",
    )(info, chosen, *rows, *dots)


def chip_adds_kernel(keep, got, send_x, send_y, near_x, near_y, one, two, sem_in, sem_out):
    half = send_x.shape[1]
    copies = [
        (
            pltpu.make_async_copy(keep.at[i], one.at[i], sem_in.at[i, 0]),
            pltpu.make_async_copy(got.at[i], two.at[i], sem_in.at[i, 1]),
        )
        for i in range(4)
    ]
    for pair in copies:
        run_all(pair)
    sent = []
    for i in range(4):
        wait_all(copies[i])
        one[i] = (one[i].astype(WIDE) + two[i].astype(WIDE)).astype(LOW)
        upper = (near_x, send_x)[i % 2].at[i // 2]
        lower = (near_y, send_y)[i // 2].at[i % 2]
        for part, to in enumerate((upper, lower)):
            copy = pltpu.make_async_copy(
                one.at[i, pl.ds(part * half, half)], to, sem_out.at[i, part]
            )
            copy.start()
            sent.append(copy)
    wait_all(sent)


def chip_adds(keep, got):
    _, height, width = keep.shape
    shape = jax.ShapeDtypeStruct((2, height // 2, width), LOW)
    return pl.pallas_call(
        chip_adds_kernel,
        out_shape=(shape,) * 4,
        in_specs=[ANY, ANY],
        out_specs=(ANY,) * 4,
        scratch_shapes=[
            pltpu.VMEM(keep.shape, LOW),
            pltpu.VMEM(keep.shape, LOW),
            pltpu.SemaphoreType.DMA((4, 2)),
            pltpu.SemaphoreType.DMA((4, 2)),
        ],
        compiler_params=params(),
        cost_estimate=LITTLE,
        name="chip_sums",
    )(keep, got)


def corner_adds_kernel(near_x, got_x, near_y, got_y, send_y, send_x):
    send_y[...] = (near_x[0].astype(WIDE) + got_x[0].astype(WIDE)).astype(LOW)
    send_x[...] = (near_y[0].astype(WIDE) + got_y[0].astype(WIDE)).astype(LOW)


def corner_adds(near_x, got_x, near_y, got_y):
    _, half, width = near_x.shape
    rows = half
    block = pl.BlockSpec((1, rows, width), lambda i: (1, i, 0))
    out = pl.BlockSpec((rows, width), lambda i: (i, 0))
    return pl.pallas_call(
        corner_adds_kernel,
        grid=(half // rows,),
        out_shape=(jax.ShapeDtypeStruct((half, width), LOW),) * 2,
        in_specs=[block] * 4,
        out_specs=(out, out),
        compiler_params=params(),
        cost_estimate=LITTLE,
        name="corner_sums",
    )(near_x, got_x, near_y, got_y)


def split(values):
    high = values.astype(LOW)
    return high, (values - high.astype(WIDE)).astype(LOW)


def norm_back(values, gain, grad):
    factor = lax.rsqrt(jnp.mean(values * values, axis=-1, keepdims=True) + EPSILON)
    scaled = gain * grad
    mean = jnp.mean(values * scaled, axis=-1, keepdims=True)
    grad_values = factor * scaled - values * (factor * factor * factor * mean)
    grad_gain = jnp.sum(grad * values * factor, axis=0, keepdims=True)
    return grad_values, grad_gain


def router_back(logits, routes, grad_shares):
    ids = lax.broadcasted_iota(jnp.int32, logits.shape, 0)
    hit = ids == routes[0:1]
    for k in range(1, TOP):
        hit = jnp.logical_or(hit, ids == routes[k : k + 1])
    weights = jnp.exp(logits - jnp.max(logits, axis=0, keepdims=True))
    probs = weights / jnp.sum(weights, axis=0, keepdims=True)
    chosen = jnp.sum(jnp.where(hit, probs, 0.0), axis=0, keepdims=True)
    grads = jnp.where(hit, grad_shares, 0.0)
    mean = jnp.sum(probs * grads, axis=0, keepdims=True) / chosen
    grad_probs = jnp.where(hit, (grads - mean) / chosen, 0.0)
    return probs * (grad_probs - jnp.sum(probs * grad_probs, axis=0, keepdims=True))


def branch_back_kernel(
    parts, info, residual, normed, cotangent, routes, router, gain, *rest
):
    sums, rest = rest[:parts], rest[parts:]
    experts = router.shape[0]
    count = len(rest) - 7
    refs = rest[:count]
    grad_residual, grad_branch, grad_heads, grad_gain, grad_router, weight, sem = rest[count:]

    @pl.when(pl.program_id(0) == 0)
    def _():
        copies = weight_copies(info, refs, weight, sem, D // QUARTERS + 128, D // QUARTERS)
        run_all(copies)
        logits = nt(router[...], normed[...])
        if parts == 2:
            back_sum, grad_shares = sums[0][...], sums[1][...]
        else:
            values = [
                (ref[0] if len(ref.shape) == 3 else ref[...]).astype(WIDE) for ref in sums
            ]
            upper = values[0] + values[1] + values[2]
            lower = values[3] + values[4] + values[5]
            last = lower.shape[0] - SHARE_ROWS
            shares = lower[last : last + experts]
            grad_shares = shares[:, :TOK_DEV] + shares[:, TOK_DEV : 2 * TOK_DEV]
            back_sum = jnp.concatenate([upper, lower[:last]], axis=0)
        high, low = split(router_back(logits, routes[...], grad_shares))
        grad_router[...] = nn(high, normed[...]) + nn(low, normed[...])
        grad_normed = tn(high, router[...]) + tn(low, router[...])
        grad_normed += back_sum
        grad_values, gain_grad = norm_back(residual[...], gain[...], grad_normed)
        grad_gain[...] = gain_grad
        total = cotangent[...].astype(WIDE) + grad_values
        grad_residual[...] = total
        grad_branch[...] = total.astype(LOW)
        wait_all(copies)

    at = pl.ds(pl.multiple_of(pl.program_id(0) * STEP, STEP), STEP)
    grad_heads[...] = nt(grad_branch[...], weight[at, :]).astype(LOW)


def branch_back(info, residual, normed, sums, cotangent, routes, router, gain, refs):
    full = (TOK_DEV, D)
    total = router.shape[0]
    return pl.pallas_call(
        functools.partial(branch_back_kernel, len(sums)),
        grid=(D // STEP,),
        out_shape=(
            jax.ShapeDtypeStruct(full, WIDE),
            jax.ShapeDtypeStruct(full, LOW),
            jax.ShapeDtypeStruct(full, LOW),
            jax.ShapeDtypeStruct((1, D), WIDE),
            jax.ShapeDtypeStruct((total, D), WIDE),
        ),
        in_specs=[SMEM]
        + [whole(full)] * 3
        + [whole((TOP, TOK_DEV)), whole((total, D)), whole((1, D))]
        + [whole(part.shape if part.ndim == 2 else (1,) + part.shape[1:]) for part in sums]
        + [ANY] * len(refs),
        out_specs=(
            whole(full),
            whole(full),
            pl.BlockSpec((TOK_DEV, STEP), lambda i: (0, i)),
            whole((1, D)),
            whole((total, D)),
        ),
        scratch_shapes=[pltpu.VMEM((D, D), LOW), pltpu.SemaphoreType.DMA],
        compiler_params=params(),
        cost_estimate=LITTLE,
        name="experts_norm_back",
    )(info, residual, normed, cotangent, routes, router, gain, *sums, *refs)


def join_grads_kernel(info, own_grad, source_grad, arrived, cosine, sine, out):
    half = HEAD_DIM // 2
    first = lax.broadcasted_iota(jnp.int32, (TOK_DEV, HEAD_DIM), 1) < half
    leaves = info[1] == 0

    def total(column):
        columns = slice(column, column + 128)
        extra = source_grad[:, columns] + arrived[:, columns].astype(WIDE)
        return own_grad[:, columns] + jnp.where(leaves, 0.0, extra)

    for g in range(KV_HEADS):
        key = turn_back(total(128 * g), cosine[...], sine[...])
        value = total(KEY_WIDTH + 128 * g)
        out[:, 256 * g : 256 * g + 128] = jnp.where(
            first, key, pltpu.roll(value, half, 1)
        ).astype(LOW)
        out[:, 256 * g + 128 : 256 * g + 256] = jnp.where(
            first, pltpu.roll(key, half, 1), value
        ).astype(LOW)


def join_grads(info, own_grad, source_grad, arrived, cosine, sine):
    vmem = pl.BlockSpec(memory_space=pltpu.VMEM)
    return pl.pallas_call(
        join_grads_kernel,
        out_shape=jax.ShapeDtypeStruct((TOK_DEV, 2 * KEY_WIDTH), LOW),
        in_specs=[SMEM] + [vmem] * 5,
        out_specs=vmem,
        compiler_params=params(),
        cost_estimate=LITTLE,
        name="join_key_value_gradients",
    )(info, own_grad, source_grad, arrived, cosine, sine)


def token_back_kernel(info, grad_query, grad_pair, tokens, grad_residual, gain, *rest):
    count = (len(rest) - 6) // 2
    query_refs, pair_refs = rest[:count], rest[count : 2 * count]
    out, grad_gain, query_weight, pair_weight, grad_normed, sem = rest[2 * count :]

    @pl.when(pl.program_id(0) == 0)
    def _():
        copies = weight_copies(info, query_refs, query_weight, sem, 0, D // QUARTERS)
        copies += weight_copies(info, pair_refs, pair_weight, sem, D // QUARTERS, 128)
        run_all(copies)
        wait_all(copies)

    at = pl.ds(pl.multiple_of(pl.program_id(0) * STEP, STEP), STEP)
    grad_normed[:, at] = nt(grad_query[...], query_weight[at, :]) + nt(
        grad_pair[...], pair_weight[at, :]
    )

    @pl.when(pl.program_id(0) == pl.num_programs(0) - 1)
    def _():
        grad_values, gain_grad = norm_back(
            tokens[...].astype(WIDE), gain[...], grad_normed[...]
        )
        grad_gain[...] = gain_grad
        out[...] = (grad_residual[...] + grad_values).astype(LOW)


def token_back(info, grad_query, grad_pair, tokens, grad_residual, gain, query_refs, pair_refs):
    full = (TOK_DEV, D)
    return pl.pallas_call(
        token_back_kernel,
        grid=(D // STEP,),
        out_shape=(jax.ShapeDtypeStruct(full, LOW), jax.ShapeDtypeStruct((1, D), WIDE)),
        in_specs=[
            SMEM,
            whole(full),
            whole((TOK_DEV, 2 * KEY_WIDTH)),
            whole(full),
            whole(full),
            whole((1, D)),
        ]
        + [ANY] * (len(query_refs) + len(pair_refs)),
        out_specs=(whole(full), whole((1, D))),
        scratch_shapes=[
            pltpu.VMEM((D, D), LOW),
            pltpu.VMEM((D, 2 * KEY_WIDTH), LOW),
            pltpu.VMEM(full, WIDE),
            pltpu.SemaphoreType.DMA,
        ],
        compiler_params=params(),
        cost_estimate=LITTLE,
        name="token_gradient",
    )(info, grad_query, grad_pair, tokens, grad_residual, gain, *query_refs, *pair_refs)


def weight_grads_kernel(parts, whole_rows, info, *rest):
    ins, (keep, send) = rest[:-2], rest[-2:]
    depth = D // 8
    core = info[0] & 1
    chip = pl.program_id(0) ^ (info[0] >> 1)
    for strip_at, grads_at, start, width in parts:
        low = tn(ins[strip_at][...], ins[grads_at][...]).astype(LOW)
        columns = slice(start, start + width)
        for slot in range(QUARTERS):
            for j in range(QUARTERS):

                @pl.when(info[2 + slot] == j)
                def _():
                    piece = low[:, j * width : (j + 1) * width]
                    upper, lower = piece[:depth], piece[depth:]
                    keep[0, slot, :depth, columns] = jnp.where(core == 0, upper, lower)
                    send[0, slot, :depth, columns] = jnp.where(core == 0, lower, upper)
                    if not whole_rows:
                        blank = jnp.zeros((EXTRA, width), LOW)
                        keep[0, slot, depth:, columns] = blank
                        send[0, slot, depth:, columns] = blank

    if whole_rows:
        extra = ins[-1]
        for slot in range(QUARTERS):
            to = info[2 + slot]
            keep[0, slot, depth:] = extra[(chip * 2 + core) * QUARTERS + to]
            send[0, slot, depth:] = extra[(chip * 2 + 1 - core) * QUARTERS + to]


def weight_grads(info, strips, grads, parts, extra, earlier=()):
    depth = D // 8
    strip = pl.BlockSpec((TOK_DEV, 2 * depth), lambda i, info: (0, i ^ (info[0] >> 1)))
    more = [] if extra is None else [extra]
    width = 2 * D // QUARTERS + 128
    shape = (4, QUARTERS, depth + EXTRA, width)
    if earlier:
        out = pl.BlockSpec((1, QUARTERS, depth + EXTRA, 128), lambda i, info: (i, 0, 0, 3))
    else:
        out = pl.BlockSpec((1,) + shape[1:], lambda i, info: (i, 0, 0, 0))
    inputs = [*strips, *grads, *more]

    def kernel(info, *rest):
        count = len(inputs)
        weight_grads_kernel(
            parts, extra is not None, info, *rest[:count], *rest[count + len(earlier) :]
        )

    return pl.pallas_call(
        kernel,
        grid_spec=pltpu.PrefetchScalarGridSpec(
            num_scalar_prefetch=1,
            grid=(4,),
            in_specs=[strip] * len(strips)
            + [
                pl.BlockSpec(a.shape, lambda i, info, n=a.ndim: (0,) * n)
                for a in (*grads, *more)
            ]
            + [ANY] * len(earlier),
            out_specs=(out, out),
        ),
        out_shape=(jax.ShapeDtypeStruct(shape, LOW),) * 2,
        input_output_aliases={1 + len(inputs) + i: i for i in range(len(earlier))},
        compiler_params=params(),
        cost_estimate=LITTLE,
        name="weight_gradients",
    )(info, *inputs, *earlier)


def position_of(token_index):
    branch_place = TRUNK + (token_index - TRUNK) % BRANCH
    leaf_place = TRUNK + BRANCH + (token_index - TOK_DEV) % BRANCH
    return jnp.where(
        token_index < TRUNK, token_index, jnp.where(token_index < TOK_DEV, branch_place, leaf_place)
    )


def rotary_tables(positions):
    half_dim = HEAD_DIM // 2
    frequency = ROPE_BASE ** (-jnp.arange(half_dim, dtype=jnp.float32) / half_dim)
    angles = positions.astype(jnp.float32)[:, None] * frequency[None, :]
    cosine, sine = (jnp.cos(angles), jnp.sin(angles))
    return (
        jnp.concatenate([cosine, cosine], axis=1),
        jnp.concatenate([-sine, sine], axis=1),
    )


def after(values, *earlier):
    return lax.optimization_barrier((values, earlier))[0]


def fast_mesh():
    return lax.axis_size("rows") == 8 and lax.axis_size("cols") == 4


SLOT_SHARD = ((0, 2, 1, 3), (1, 3, 0, 2), (2, 0, 1, 3), (3, 1, 2, 0))
UP = [(0, 1), (1, 2), (2, 3)]
DOWN = [(1, 0), (2, 1), (3, 2)]
FAR = [(0, 3), (3, 0)]


def send_near(block):
    return lax.ppermute(block, "cols", DOWN), lax.ppermute(block, "cols", UP)


def send_far(block):
    return lax.ppermute(block, "cols", FAR)


def send_second(block, near):
    place = lax.axis_index("cols")
    above, below = near
    payload = jnp.where(place == 1, above, jnp.where(place == 2, below, block))
    return lax.ppermute(payload, "cols", [(3, 1), (1, 0), (0, 2), (2, 3)])


def slot_list(block, near, second, far):
    place = lax.axis_index("cols")
    above, below = near
    end = (place == 0) | (place == 3)
    return [
        block,
        second,
        jnp.where(place == 0, above, below),
        jnp.where(end, far, above),
    ]


def reduce_first(second, fourth):
    relay = lax.ppermute(second, "cols", [(1, 3), (0, 1), (2, 0), (3, 2)])
    return relay, lax.ppermute(fourth, "cols", FAR)


def reduce_second(third, fourth, relay):
    place = lax.axis_index("cols")
    relayed = relay.astype(WIDE)
    upward_load = (
        jnp.where(place == 0, third, fourth).astype(WIDE) + jnp.where(place == 1, relayed, 0.0)
    ).astype(LOW)
    downward_load = (third.astype(WIDE) + jnp.where(place == 2, relayed, 0.0)).astype(LOW)
    return (
        lax.ppermute(upward_load, "cols", UP),
        lax.ppermute(downward_load, "cols", DOWN),
    )


def reduce_last(own, first, second):
    place = lax.axis_index("cols")
    relay, far = first
    below, above = second
    end = (place == 0) | (place == 3)
    return (
        own.astype(WIDE)
        + below.astype(WIDE)
        + above.astype(WIDE)
        + jnp.where(end, relay.astype(WIDE) + far.astype(WIDE), 0.0)
    )


def flip(block, bit):
    count = lax.axis_size("rows")
    return lax.ppermute(block, "rows", [(i, i ^ bit) for i in range(count)])


def add_low(one, two):
    return (one.astype(WIDE) + two.astype(WIDE)).astype(LOW)


def chips_second(near_x, near_y, got_x, got_y):
    for_y, for_x = corner_adds(near_x, got_x, near_y, got_y)
    return (near_x, got_x, flip(for_y, 4), near_y, got_y, flip(for_x, 2))


def turn_corner(beside, across):
    half = beside.shape[0] // 2
    return jnp.concatenate([flip(beside[:half], 4), flip(across[half:], 2)], axis=0)


def send_chips(sums):
    return flip(sums[0], 2), flip(sums[1], 4)


def sum_parts(parts):
    wide = [(a[0] if a.ndim == 3 else a).astype(WIDE) for a in parts]
    if len(wide) == 1:
        return wide[0]
    return jnp.concatenate([wide[0] + wide[1] + wide[2], wide[3] + wide[4] + wide[5]], axis=0)


def on_device(
    tokens,
    query_weight,
    key_weight,
    value_weight,
    out_weight,
    router_weight,
    attention_gain,
    experts_gain,
    gate_weight,
    upward_weight,
    down_weight,
    routes,
    leaf_parent,
    cotangent,
):
    row_count = lax.axis_size("rows")
    col_count = lax.axis_size("cols")
    row_place = lax.axis_index("rows")
    col_place = lax.axis_index("cols")
    fast = fast_mesh()
    parity = lax.rem(col_place, 2)
    tree_id = lax.div(row_place * col_count + col_place, 2)
    parent_row = lax.dynamic_slice_in_dim(leaf_parent, tree_id, 1, 0)[0]
    depth, query_part = query_weight.shape
    key_part = key_weight.shape[1]
    router_part = router_weight.shape[1]
    gain_part = attention_gain.shape[0]
    expert_total = router_part * col_count
    local_experts = gate_weight.shape[0]
    capacity = TOK_DEV * TOP // expert_total * 5 // 4

    shards = (
        jnp.asarray(SLOT_SHARD, jnp.int32)[col_place]
        if fast
        else jnp.arange(4, dtype=jnp.int32)
    )
    branch_rows = jnp.where(parity == 0, TRUNK + BRANCH * parent_row, TRUNK)
    info = jnp.concatenate(
        [jnp.stack([row_place, parity]), shards, branch_rows, jnp.zeros((2,), jnp.int32)]
    ).astype(jnp.int32)

    packed = jnp.concatenate([query_weight, key_weight, value_weight, out_weight], axis=1)
    local_index = (1 - parity) * TOK_DEV + jnp.arange(TOK_DEV, dtype=jnp.int32)
    cosine, sine = rotary_tables(position_of(local_index))
    shard_blocks = [
        jnp.concatenate(
            [gate_weight[expert].T, upward_weight[expert].T, down_weight[expert]], axis=0
        )
        for expert in range(local_experts)
    ]
    expert_refs = []
    if fast:
        wide = packed.shape[1]
        gains = jnp.concatenate([attention_gain, experts_gain])[None, :]
        packed = jnp.concatenate(
            [
                packed,
                jnp.pad(router_weight.T, ((0, 0), (0, wide - depth))),
                jnp.pad(gains, ((0, 0), (0, wide - 2 * gain_part))),
                jnp.pad(routes.T.astype(LOW), ((0, 0), (0, wide - TOK_DEV))),
                jnp.zeros((EXTRA - router_part - 1 - TOP, wide), LOW),
            ],
            axis=0,
        )
        packed_near = send_near(packed)
        packed_far = send_far(packed)
        packed_second = send_second(packed, packed_near)
        first_block = after(shard_blocks[0], *packed_near)
        first_near = send_near(first_block)
        first_second = send_second(first_block, first_near)
        grad_flips = (flip(cotangent, 2), flip(cotangent, 4))
        own = jnp.stack(slot_list(packed, packed_near, packed_second, packed_far))
        own = after(own, info, cosine, sine, *grad_flips)
        beside, across = flip(own, 2), flip(own, 4)
        own_in = flip(own, 1)
        beside, across = after((beside, across), own_in, *first_near)
        corner = [flip(beside[:2], 4), flip(across[2:], 2)]
        pair_in = flip(jnp.concatenate([beside, across], axis=0), 1)
        corner_in = [flip(piece, 1) for piece in corner]
        pieces = [own, own_in, beside, across, *corner, pair_in, *corner_in]
        at = depth + router_part + 1
        near_slots = [own, own_in, beside, pair_in, across, pair_in[4:], corner[0], corner_in[0]]
        routes_all = jnp.stack([part[0, at : at + TOP, :TOK_DEV] for part in near_slots])
        routes_all = routes_all.astype(jnp.int32)
        chosen, place_rows = tables(info, routes_all, capacity, local_experts, expert_total)
        query_refs = pair_refs = out_refs = pieces
        extra_rows = extras(info, pieces)
        router_all = extra_rows[:, :router_part, :depth]
        attention_scale = extra_rows[:, router_part, :gain_part]
        experts_scale = extra_rows[:, router_part, gain_part : 2 * gain_part]
    else:
        packed_all = lax.all_gather(lax.all_gather(packed, "cols", axis=0), "rows", axis=0)

        def unpack(start, width):
            part = packed_all[..., start : start + width]
            return jnp.swapaxes(part, 1, 2).reshape(row_count * depth, col_count * width)

        key_at = query_part
        query_refs = [unpack(0, query_part)]
        pair_refs = [
            jnp.concatenate(
                [
                    unpack(key_at, key_part).reshape(D, QUARTERS, -1),
                    unpack(key_at + key_part, key_part).reshape(D, QUARTERS, -1),
                ],
                axis=2,
            ).reshape(D, -1)
        ]
        out_refs = [unpack(key_at + 2 * key_part, query_part)]
        routes_all = lax.all_gather(routes.T, "rows", axis=0)
        chosen, place_rows = tables(info, routes_all, capacity, local_experts, expert_total)
        axes = ("rows", "cols")
        router_all = jnp.swapaxes(lax.all_gather(router_weight, axes, axis=0), 1, 2)
        attention_scale = lax.all_gather(attention_gain, axes, axis=0)
        experts_scale = lax.all_gather(experts_gain, axes, axis=0)

    attention_scale = attention_scale.reshape(1, D).astype(WIDE)
    experts_scale = experts_scale.reshape(1, D).astype(WIDE)
    router_rows = jnp.transpose(
        router_all.reshape(row_count, col_count, router_part, depth), (1, 2, 0, 3)
    ).reshape(expert_total, D)
    router_cols = router_rows.T
    tokens_in = after(tokens, first_second, chosen) if fast else tokens
    normed, own_pair = key_value(info, tokens_in, attention_scale, cosine, sine, pair_refs)
    pairs = [(i + 1, i) for i in range(0, col_count, 2)]
    partner = lax.ppermute(own_pair, "cols", pairs)
    queries = query(info, normed, cosine, sine, query_refs)
    if fast:
        first_far = send_far(after(first_block, partner, queries))
        expert_refs.append([first_block, first_second, *first_near, first_far])
        grad_flips = after(grad_flips, own_pair)
        grad_corner = turn_corner(*grad_flips)
    heads = attention(info, queries, own_pair, partner)
    if fast:
        grad_near = [cotangent, *grad_flips, grad_corner]
        grad_blocks = [block for one in grad_near for block in (one, flip(one, 1))]
        heads = after(heads, grad_corner)
    else:
        grad_all = lax.all_gather(cotangent, "rows", axis=0)
        grad_blocks = [grad_all[q] for q in range(row_count)]
    residual, normed_two = out_projection(info, heads, tokens, experts_scale, out_refs)

    if fast:
        beside, across = flip(normed_two, 2), flip(normed_two, 4)
        beside_in = flip(normed_two, 1)
        later_block = after(shard_blocks[1], first_far, normed_two)
        expert_refs.append([lax.all_gather(later_block, "cols", axis=0)])
    else:
        rows_all = lax.all_gather(normed_two, "rows", axis=0)
        expert_refs = [[lax.all_gather(block, "cols", axis=0)] for block in shard_blocks]
    grad_rows = pick_rows(chosen, grad_blocks, local_experts)

    def place_block(q, block, picked):
        return dispatch(
            q, info, block, chosen, routes_all, router_cols, local_experts, picked
        )

    if fast:
        half = TOK_DEV // 2
        picked = place_block(0, normed_two, None)
        picked = place_block(1, beside_in, picked)
        beside, across = after((beside, across), picked)
        corner = [flip(beside[:half], 4), flip(across[half:], 2)]
        picked = after(picked, *grad_rows)
        picked = place_block(2, beside, picked)
        picked = place_block(4, across, picked)
        beside_in = flip(beside, 1)
        across_in = flip(after(across, beside_in), 1)
        picked = place_block(3, beside_in, picked)
        picked = place_block(5, across_in, picked)
        corner = jnp.concatenate(after(corner, picked), axis=0)
        corner_in = flip(corner, 1)
        picked = place_block(6, corner, picked)
        picked = place_block(7, corner_in, picked)
    else:
        picked = None
        for q in range(row_count):
            picked = place_block(q, rows_all[q], picked)
    height = row_count * capacity
    token_rows = [a.reshape(height, D) for a in picked[:local_experts]]
    grad_rows = [a.reshape(height, D) for a in grad_rows]
    share_rows = [a.reshape(height, 1) for a in picked[local_experts:]]

    out_rows, back_rows, gate_dots, reduced = ([], [], [], [])
    for e in range(local_experts):
        rows_in = after(token_rows[e], *reduced_in) if e else token_rows[e]
        out_row, back_row, grad_row, acts, dots = expert(
            info, rows_in, grad_rows[e], share_rows[e], expert_refs[e], col_count
        )
        out_rows.append(out_row.reshape(row_count, capacity, D))
        back_rows.append(back_row.reshape(row_count, capacity, D))
        gate_dots.append(dots.reshape(row_count, capacity, 1))
        if fast and e == 1:
            got = flip(combine(info, chosen, back_rows, 1, 2, gate_dots), 1)
            back_keep = combine(info, chosen, back_rows, 0, 2, gate_dots)
            for_x, for_y, near_x, near_y = chip_adds(back_keep, got)
            acts = after(acts, for_x)
            back_flips = send_chips((for_x, for_y))
        slots = expert_grads(acts, token_rows[e], grad_row)
        reduced_in = (slots,)
        if e and fast:
            back_parts = chips_second(near_x, near_y, *after(back_flips, slots))
        else:
            reduced.append(lax.psum_scatter(slots, "cols", scatter_dimension=0, tiled=False))

    if fast:
        out_rows = [after(a, back_parts[1], back_parts[4]) for a in out_rows]
        out_got = flip(combine(info, chosen, out_rows, 1, 2), 1)
        out_keep = combine(info, chosen, out_rows, 0, 2)
        back_parts = after(back_parts, out_keep, out_got, slots)
    else:
        spread_dots = spread(place_rows, gate_dots)
        grad_shares = lax.all_to_all(spread_dots, "rows", split_axis=0, concat_axis=0, tiled=True)

        def summed(rows):
            part = combine(info, chosen, rows, 0, 1)
            return lax.psum_scatter(part, "rows", scatter_dimension=0).astype(WIDE)

        back_parts = (summed(back_rows), grad_shares.reshape(expert_total, TOK_DEV))
        mixture = (summed(out_rows),)

    grad_residual, grad_branch, grad_heads, experts_gain_grad, router_grad = branch_back(
        info,
        residual,
        normed_two,
        back_parts,
        cotangent,
        routes.T,
        router_rows,
        experts_scale,
        out_refs,
    )
    if fast:
        out_keep = after(out_keep, back_parts[2], back_parts[5], reduced[0])
        out_first = chip_adds(out_keep, out_got)
        slots = after(slots, reduced[0], out_first[0])
        reduced.append(lax.psum_scatter(slots, "cols", scatter_dimension=0, tiled=False))
        out_flips = send_chips(out_first[:2])
        grad_heads = after(grad_heads, out_first[0])
        router_parts = jnp.transpose(
            router_grad.astype(LOW).reshape(col_count, router_part, row_count, depth),
            (2, 0, 1, 3),
        ).reshape(row_count * col_count, router_part, depth)
        gain_rows = experts_gain_grad.astype(LOW).reshape(row_count * col_count, 1, gain_part)
        extra = jnp.concatenate(
            [
                jnp.pad(router_parts, ((0, 0), (0, 0), (0, wide - depth))),
                jnp.pad(gain_rows, ((0, 0), (0, 0), (0, wide - gain_part))),
                jnp.zeros((row_count * col_count, EXTRA - router_part - 1, wide), LOW),
            ],
            axis=1,
        )
    grad_query, own_grad, source_grad = attention_back(
        info, queries, own_pair, partner, grad_heads, cosine, sine
    )
    arrived = lax.ppermute(source_grad.astype(LOW), "cols", [(j, i) for i, j in pairs])
    if fast:
        parts = ((0, 2, 0, query_part), (1, 3, query_part + 2 * key_part, query_part))
        out_flips = after(out_flips, grad_query)
        near_x, near_y = out_first[2:]
        for_y, for_x = corner_adds(near_x, out_flips[0], near_y, out_flips[1])
        mixture = (near_x, out_flips[0], flip(for_y, 4))
        mixture += (near_y, out_flips[1], flip(for_x, 2))
        grad_branch = after(grad_branch, for_y)
        keep_send = weight_grads(
            info, [normed, heads], [grad_query, grad_branch], parts, extra
        )
        arrived = after(arrived, *keep_send)
    grad_pair = join_grads(info, own_grad, source_grad, arrived, cosine, sine)
    if fast:
        keep, send = weight_grads(
            info, [normed], [grad_pair], ((0, 1, 0, 2 * key_part),), None, keep_send
        )
        sent = flip(send, 1)
        grad_pair = after(grad_pair, keep)
    tokens_grad, attention_gain_grad = token_back(
        info, grad_query, grad_pair, tokens, grad_residual, attention_scale, query_refs, pair_refs
    )

    if fast:
        flat = (4, col_count * (depth + EXTRA), wide)
        sent = after(sent, mixture[2], mixture[5])
        sent_first = chip_adds(keep.reshape(flat), sent.reshape(flat))
        sent_chips = send_chips(sent_first[:2])
        slots = sum_parts(chips_second(*sent_first[2:], *sent_chips))
        slots = slots.reshape(col_count, depth + EXTRA, wide)
        width = query_part + 2 * key_part
        own_slots = own
        gain_sums = sum(
            jnp.sum(own_slots[i][:depth, :width].astype(WIDE) * slots[i, :depth, :width], axis=1)
            for i in range(4)
        )
        own_gains = lax.dynamic_slice_in_dim(attention_scale[0], row_place * depth, depth, 0)
        gain_sums = (gain_sums / own_gains).reshape(col_count, 1, gain_part)
        gain_sums = jnp.pad(
            jnp.take(gain_sums, shards, axis=0),
            ((0, 0), (depth + router_part + 1, EXTRA - router_part - 2), (0, wide - gain_part)),
        )
        slots = (slots + gain_sums).astype(LOW)

        def cols_sum(slots):
            sent_first = reduce_first(slots[1], slots[3])
            sent_second = reduce_second(slots[2], slots[3], sent_first[0])
            return reduce_last(slots[0], sent_first, sent_second)

        sums = cols_sum(slots)
        router_sum = sums[depth : depth + router_part, :depth].T
        experts_gain_sum = sums[depth + router_part, :gain_part]
        attention_gain_sum = sums[depth + router_part + 1, :gain_part]
        sums = sums[:depth]
    else:
        full_grads = [
            tn(normed, grad_query),
            *jnp.moveaxis(tn(normed, grad_pair).reshape(D, QUARTERS, 2, -1), 2, 0),
            tn(heads, grad_branch),
        ]
        packed_grad = jnp.concatenate(
            [
                grad.astype(LOW).reshape(row_count, depth, col_count, -1)
                for grad in full_grads
            ],
            axis=3,
        )
        row_sums = lax.psum_scatter(packed_grad, "rows", scatter_dimension=0)
        sums = lax.psum_scatter(row_sums, "cols", scatter_dimension=1).astype(WIDE)
        small_grads = jnp.concatenate(
            [
                attention_gain_grad.reshape(-1, gain_part),
                experts_gain_grad.reshape(-1, gain_part),
                jnp.transpose(
                    router_grad.reshape(col_count, router_part, row_count, depth), (2, 0, 3, 1)
                ).reshape(row_count * col_count, depth * router_part),
            ],
            axis=1,
        )
        small_grads = small_grads.reshape(row_count, -1)
        small_grads = lax.all_to_all(small_grads, "rows", split_axis=0, concat_axis=0, tiled=True)
        small_grads = jnp.sum(small_grads, axis=0).reshape(col_count, -1)
        small_grads = lax.all_to_all(small_grads, "cols", split_axis=0, concat_axis=0, tiled=True)
        small_sums = jnp.sum(small_grads, axis=0)
        attention_gain_sum = small_sums[:gain_part]
        experts_gain_sum = small_sums[gain_part : 2 * gain_part]
        router_sum = small_sums[2 * gain_part :].reshape(depth, router_part)

    layer_output = (residual + sum_parts(mixture)).astype(LOW)
    key_at = query_part
    value_at = key_at + key_part
    out_at = value_at + key_part
    part = down_weight.shape[1]
    expert_sums = [block.astype(WIDE) for block in reduced]
    gate_grad, upward_grad, down_grad = (
        jnp.stack([sums_of[which * part : (which + 1) * part] for sums_of in expert_sums])
        for which in range(3)
    )
    return (
        layer_output,
        tokens_grad,
        sums[:, :key_at],
        sums[:, key_at:value_at],
        sums[:, value_at:out_at],
        sums[:, out_at:],
        router_sum,
        attention_gain_sum,
        experts_gain_sum,
        jnp.swapaxes(gate_grad, 1, 2),
        jnp.swapaxes(upward_grad, 1, 2),
        down_grad,
    )


def solution(mesh):
    in_specs = (
        P(("rows", "cols"), None),
        P("rows", "cols"),
        P("rows", "cols"),
        P("rows", "cols"),
        P("rows", "cols"),
        P("rows", "cols"),
        P(("rows", "cols")),
        P(("rows", "cols")),
        P("rows", None, "cols"),
        P("rows", None, "cols"),
        P("rows", "cols", None),
        P(("rows", "cols"), None),
        P(),
        P(("rows", "cols"), None),
    )
    out_specs = (
        P(("rows", "cols"), None),
        P(("rows", "cols"), None),
        P("rows", "cols"),
        P("rows", "cols"),
        P("rows", "cols"),
        P("rows", "cols"),
        P("rows", "cols"),
        P(("rows", "cols")),
        P(("rows", "cols")),
        P("rows", None, "cols"),
        P("rows", None, "cols"),
        P("rows", "cols", None),
    )
    return jax.shard_map(
        on_device, mesh=mesh, in_specs=in_specs, out_specs=out_specs, check_vma=False
    )
```

```python
import functools

import jax
import jax.numpy as jnp
from jax import lax
from jax.experimental import pallas as pl
from jax.experimental.pallas import tpu as pltpu
from jax.sharding import PartitionSpec as P

D = 1536
HEADS = 12
KV_HEADS = 2
HEAD_DIM = 128
TOP = 4
TOK_DEV = 512
BRANCHES = 4
LEAVES = 8
TRUNK = 256
BRANCH = 64

EPSILON = 1e-06
ROPE_BASE = 10000.0
MASKED = -1e30
LOW = jnp.bfloat16
WIDE = jnp.float32
KEY_WIDTH = KV_HEADS * HEAD_DIM
GROUP = HEADS // KV_HEADS
QUARTERS = 4
VMEM_LIMIT = 56 * 1024 * 1024

ANY = pl.BlockSpec(memory_space=pl.ANY)
SMEM = pl.BlockSpec(memory_space=pltpu.SMEM)


def nn(one, two):
    return lax.dot_general(one, two, (((1,), (0,)), ((), ())), preferred_element_type=WIDE)


def nt(one, two):
    return lax.dot_general(one, two, (((1,), (1,)), ((), ())), preferred_element_type=WIDE)


def tn(one, two):
    return lax.dot_general(one, two, (((0,), (0,)), ((), ())), preferred_element_type=WIDE)


def whole(shape):
    return pl.BlockSpec(shape, lambda *_: (0,) * len(shape))


LITTLE = pl.CostEstimate(flops=1, bytes_accessed=1, transcendentals=0)


def params():
    return pltpu.CompilerParams(vmem_limit_bytes=VMEM_LIMIT)


def turn(values, cosine, sine):
    return values * cosine + pltpu.roll(values, HEAD_DIM // 2, 1) * sine


def turn_back(values, cosine, sine):
    return values * cosine - pltpu.roll(values, HEAD_DIM // 2, 1) * sine


SLOTS = range(4)
PIECES = (
    tuple((0, slot) for slot in SLOTS),
    tuple((1, slot) for slot in SLOTS),
    tuple((2, slot) for slot in SLOTS),
    tuple((4, slot) for slot in SLOTS),
    ((6, 0), (6, 1)),
    ((6, 2), (6, 3)),
    tuple((flip_bits, slot) for flip_bits in (3, 5) for slot in SLOTS),
    ((7, 0), (7, 1)),
    ((7, 2), (7, 3)),
)
EXTRA = 16


STEP = 768


def weight_copies(info, refs, target, sem, start, width):
    if len(refs) == 1:
        return [pltpu.make_async_copy(refs[0], target, sem)]
    depth = refs[0].shape[1] - EXTRA
    copies = []
    for ref, parts in zip(refs, PIECES):
        for at, (flip_bits, slot) in enumerate(parts):
            row = pl.multiple_of((info[0] ^ flip_bits) * depth, depth)
            col = pl.multiple_of(info[2 + slot] * width, 128)
            copies.append(
                pltpu.make_async_copy(
                    ref.at[at, pl.ds(0, depth), pl.ds(start, width)],
                    target.at[pl.ds(row, depth), pl.ds(col, width)],
                    sem,
                )
            )
    return copies


def extras_kernel(info, *rest):
    refs, (out, sem) = rest[:-2], rest[-2:]
    depth = refs[0].shape[1] - EXTRA
    copies = []
    for ref, parts in zip(refs, PIECES):
        for at, (flip_bits, slot) in enumerate(parts):
            to = (info[0] ^ flip_bits) * QUARTERS + info[2 + slot]
            copies.append(pltpu.make_async_copy(ref.at[at, pl.ds(depth, EXTRA)], out.at[to], sem))
    run_all(copies)
    wait_all(copies)


def extras(info, refs):
    return pl.pallas_call(
        extras_kernel,
        out_shape=jax.ShapeDtypeStruct((8 * QUARTERS, EXTRA, refs[0].shape[2]), LOW),
        in_specs=[SMEM] + [ANY] * len(refs),
        out_specs=pl.BlockSpec(memory_space=pltpu.VMEM),
        scratch_shapes=[pltpu.SemaphoreType.DMA],
        compiler_params=params(),
        cost_estimate=LITTLE,
        name="extra_rows",
    )(info, *refs)


def run_all(copies):
    for copy in copies:
        copy.start()


def wait_all(copies):
    for copy in copies:
        copy.wait()


def key_value_kernel(info, tokens, gain, cosine, sine, *rest):
    count = len(rest) - 4
    refs, (normed, out, weight, sem) = rest[:count], rest[count:]
    copies = weight_copies(info, refs, weight, sem, D // QUARTERS, 128)
    run_all(copies)
    values = tokens[...].astype(WIDE)
    factor = lax.rsqrt(jnp.mean(values * values, axis=-1, keepdims=True) + EPSILON)
    low = (values * factor * gain[...]).astype(LOW)
    normed[...] = low
    wait_all(copies)
    both = nn(low, weight[...])
    half = HEAD_DIM // 2
    first = lax.broadcasted_iota(jnp.int32, (TOK_DEV, HEAD_DIM), 1) < half
    for g in range(KV_HEADS):
        one = both[:, 256 * g : 256 * g + 128]
        two = both[:, 256 * g + 128 : 256 * g + 256]
        key = jnp.where(first, one, pltpu.roll(two, half, 1))
        value = jnp.where(first, pltpu.roll(one, half, 1), two)
        out[:, 128 * g : 128 * g + 128] = turn(key, cosine[...], sine[...]).astype(LOW)
        out[:, KEY_WIDTH + 128 * g : KEY_WIDTH + 128 * g + 128] = value.astype(LOW)


def key_value(info, tokens, gain, cosine, sine, refs):
    return pl.pallas_call(
        key_value_kernel,
        out_shape=(
            jax.ShapeDtypeStruct((TOK_DEV, D), LOW),
            jax.ShapeDtypeStruct((TOK_DEV, 2 * KEY_WIDTH), LOW),
        ),
        in_specs=[SMEM] + [pl.BlockSpec(memory_space=pltpu.VMEM)] * 4 + [ANY] * len(refs),
        out_specs=(pl.BlockSpec(memory_space=pltpu.VMEM),) * 2,
        scratch_shapes=[pltpu.VMEM((D, 2 * KEY_WIDTH), LOW), pltpu.SemaphoreType.DMA],
        compiler_params=params(),
        cost_estimate=LITTLE,
        name="norm_key_value",
    )(info, tokens, gain, cosine, sine, *refs)


def query_kernel(info, normed, cosine, sine, *rest):
    count = len(rest) - 3
    refs, (out, weight, sem) = rest[:count], rest[count:]

    @pl.when(pl.program_id(0) == 0)
    def _():
        copies = weight_copies(info, refs, weight, sem, 0, D // QUARTERS)
        run_all(copies)
        wait_all(copies)

    at = pl.multiple_of(pl.program_id(0) * STEP, STEP)
    lin = nn(normed[...], weight[:, pl.ds(at, STEP)])
    for h in range(STEP // HEAD_DIM):
        out[:, 128 * h : 128 * h + 128] = turn(
            lin[:, 128 * h : 128 * h + 128], cosine[...], sine[...]
        ).astype(LOW)


def query(info, normed, cosine, sine, refs):
    return pl.pallas_call(
        query_kernel,
        grid=(D // STEP,),
        out_shape=jax.ShapeDtypeStruct((TOK_DEV, D), LOW),
        in_specs=[SMEM, whole((TOK_DEV, D)), whole((TOK_DEV, 128)), whole((TOK_DEV, 128))]
        + [ANY] * len(refs),
        out_specs=pl.BlockSpec((TOK_DEV, STEP), lambda i: (0, i)),
        scratch_shapes=[pltpu.VMEM((D, D), LOW), pltpu.SemaphoreType.DMA],
        compiler_params=params(),
        cost_estimate=LITTLE,
        name="query_projection",
    )(info, normed, cosine, sine, *refs)


KEYS = TRUNK + 2 * BRANCH
CHUNKS = TOK_DEV // BRANCH


def chunk_keys(info, source, own, column, chunk):
    at = pl.multiple_of(info[6 + chunk], BRANCH)
    rows = pl.multiple_of(chunk * BRANCH, BRANCH)
    columns = slice(column, column + HEAD_DIM)
    return jnp.concatenate(
        [
            source[0:TRUNK, columns],
            source[pl.ds(at, BRANCH), columns],
            own[pl.ds(rows, BRANCH), columns],
        ],
        axis=0,
    )


def chunk_allowed(info, chunk, query_axis, shape):
    query_row = lax.broadcasted_iota(jnp.int32, shape, query_axis) & (BRANCH - 1)
    key = lax.broadcasted_iota(jnp.int32, shape, 1 - query_axis)
    leaves = info[1] == 0
    trunk = jnp.logical_and(jnp.logical_not(leaves), chunk < TRUNK // BRANCH)
    limit = jnp.where(trunk, chunk * BRANCH + query_row, TRUNK - 1)
    branch_limit = jnp.where(leaves, TRUNK + BRANCH - 1, 0)
    own_limit = jnp.where(trunk, 0, query_row + TRUNK + BRANCH)
    top = jnp.where(key < TRUNK, limit, jnp.where(key < TRUNK + BRANCH, branch_limit, own_limit))
    return key <= top


def group_rows(ref, g):
    first = g * GROUP
    return jnp.concatenate(
        [ref[:, 128 * h : 128 * h + 128] for h in range(first, first + GROUP)], axis=0
    )


def keep_source(info, partner, own, source):
    @pl.when(pl.program_id(0) == 0)
    def _():
        @pl.when(info[1] == 0)
        def _():
            source[...] = partner[...]

        @pl.when(info[1] != 0)
        def _():
            source[...] = own[...]


def attention_kernel(info, queries, own, partner, out, source):
    keep_source(info, partner, own, source)
    chunk = pl.program_id(0)
    rows = GROUP * BRANCH
    allowed = chunk_allowed(info, chunk, 0, (rows, KEYS))
    for g in range(KV_HEADS):
        keys = chunk_keys(info, source, own, 128 * g, chunk)
        values = chunk_keys(info, source, own, KEY_WIDTH + 128 * g, chunk)
        scores = nt(group_rows(queries, g), keys) * HEAD_DIM**-0.5
        scores = jnp.where(allowed, scores, MASKED)
        weights = jnp.exp(scores - jnp.max(scores, axis=1, keepdims=True))
        total = jnp.sum(weights, axis=1, keepdims=True)
        mixed = nn((weights * (1.0 / total)).astype(LOW), values).astype(LOW)
        for h in range(GROUP):
            at = (g * GROUP + h) * 128
            out[:, at : at + 128] = mixed[h * BRANCH : (h + 1) * BRANCH]


def attention(info, queries, own, partner):
    return pl.pallas_call(
        attention_kernel,
        grid=(CHUNKS,),
        out_shape=jax.ShapeDtypeStruct((TOK_DEV, D), LOW),
        in_specs=[
            SMEM,
            pl.BlockSpec((BRANCH, D), lambda i: (i, 0)),
            whole((TOK_DEV, 2 * KEY_WIDTH)),
            whole((TOK_DEV, 2 * KEY_WIDTH)),
        ],
        out_specs=pl.BlockSpec((BRANCH, D), lambda i: (i, 0)),
        scratch_shapes=[pltpu.VMEM((TOK_DEV, 2 * KEY_WIDTH), LOW)],
        compiler_params=params(),
        cost_estimate=LITTLE,
        name="tree_attention",
    )(info, queries, own, partner)


def attention_back_kernel(
    info, queries, own, partner, grads, cosine, sine, grad_query, own_grad, source_grad, source
):
    keep_source(info, partner, own, source)
    chunk = pl.program_id(0)

    @pl.when(chunk == 0)
    def _():
        source_grad[...] = jnp.zeros_like(source_grad)

    rows = GROUP * BRANCH
    scale = HEAD_DIM**-0.5
    allowed = chunk_allowed(info, chunk, 1, (KEYS, rows))
    at = pl.multiple_of(info[6 + chunk], BRANCH)
    for g in range(KV_HEADS):
        keys = chunk_keys(info, source, own, 128 * g, chunk)
        values = chunk_keys(info, source, own, KEY_WIDTH + 128 * g, chunk)
        query_rows = group_rows(queries, g)
        grad_rows = group_rows(grads, g)
        scores = jnp.where(allowed, nt(keys, query_rows) * scale, MASKED)
        weights = jnp.exp(scores - jnp.max(scores, axis=0, keepdims=True))
        probs = weights * (1.0 / jnp.sum(weights, axis=0, keepdims=True))
        grad_probs = nt(values, grad_rows)
        mean = jnp.sum(probs * grad_probs, axis=0, keepdims=True)
        grad_scores = (probs * (grad_probs - mean)).astype(LOW)
        grad_values = nn(probs.astype(LOW), grad_rows)
        grad_keys = nn(grad_scores, query_rows) * scale
        grad_queries = tn(grad_scores, keys) * scale
        for h in range(GROUP):
            to = (g * GROUP + h) * 128
            grad_query[:, to : to + 128] = turn_back(
                grad_queries[h * BRANCH : (h + 1) * BRANCH], cosine[...], sine[...]
            ).astype(LOW)
        for column, grad in ((128 * g, grad_keys), (KEY_WIDTH + 128 * g, grad_values)):
            columns = slice(column, column + 128)
            source_grad[0:TRUNK, columns] += grad[0:TRUNK]
            source_grad[pl.ds(at, BRANCH), columns] += grad[TRUNK : TRUNK + BRANCH]
            own_grad[:, columns] = grad[TRUNK + BRANCH :]


def attention_back(info, queries, own, partner, grads, cosine, sine):
    chunked = pl.BlockSpec((BRANCH, D), lambda i: (i, 0))
    pair = (TOK_DEV, 2 * KEY_WIDTH)
    return pl.pallas_call(
        attention_back_kernel,
        grid=(CHUNKS,),
        out_shape=(
            jax.ShapeDtypeStruct((TOK_DEV, D), LOW),
            jax.ShapeDtypeStruct(pair, WIDE),
            jax.ShapeDtypeStruct(pair, WIDE),
        ),
        in_specs=[
            SMEM,
            chunked,
            whole(pair),
            whole(pair),
            chunked,
            pl.BlockSpec((BRANCH, 128), lambda i: (i, 0)),
            pl.BlockSpec((BRANCH, 128), lambda i: (i, 0)),
        ],
        out_specs=(
            chunked,
            pl.BlockSpec((BRANCH, 2 * KEY_WIDTH), lambda i: (i, 0)),
            whole(pair),
        ),
        scratch_shapes=[pltpu.VMEM(pair, LOW)],
        compiler_params=params(),
        cost_estimate=LITTLE,
        name="tree_attention_back",
    )(info, queries, own, partner, grads, cosine, sine)


def out_kernel(info, heads, tokens, gain, *rest):
    count = len(rest) - 4
    refs, (residual, normed, weight, sem) = rest[:count], rest[count:]

    @pl.when(pl.program_id(0) == 0)
    def _():
        copies = weight_copies(info, refs, weight, sem, D // QUARTERS + 128, D // QUARTERS)
        run_all(copies)
        wait_all(copies)

    at = pl.ds(pl.multiple_of(pl.program_id(0) * STEP, STEP), STEP)
    residual[:, at] = tokens[:, at].astype(WIDE) + nn(heads[...], weight[:, at])

    @pl.when(pl.program_id(0) == pl.num_programs(0) - 1)
    def _():
        values = residual[...]
        factor = lax.rsqrt(jnp.mean(values * values, axis=-1, keepdims=True) + EPSILON)
        normed[...] = (values * factor * gain[...]).astype(LOW)


def out_projection(info, heads, tokens, gain, refs):
    full = (TOK_DEV, D)
    return pl.pallas_call(
        out_kernel,
        grid=(D // STEP,),
        out_shape=(jax.ShapeDtypeStruct(full, WIDE), jax.ShapeDtypeStruct(full, LOW)),
        in_specs=[SMEM, whole(full), whole(full), whole((1, D))] + [ANY] * len(refs),
        out_specs=(whole(full), whole(full)),
        scratch_shapes=[pltpu.VMEM((D, D), LOW), pltpu.SemaphoreType.DMA],
        compiler_params=params(),
        cost_estimate=LITTLE,
        name="out_projection",
    )(info, heads, tokens, gain, *refs)


def hits_of(routes, ids):
    hit = ids == routes[0, 0:1]
    for k in range(1, TOP):
        hit = jnp.logical_or(hit, ids == routes[0, k : k + 1])
    return hit


def tables_kernel(capacity, local, total, info, routes, chosen_out, place_out, earlier):
    @pl.when(pl.program_id(0) == 0)
    def _():
        one = lax.broadcasted_iota(jnp.int32, (TOK_DEV, TOK_DEV), 0)
        two = lax.broadcasted_iota(jnp.int32, (TOK_DEV, TOK_DEV), 1)
        earlier[...] = jnp.where(one < two, 1.0, 0.0).astype(LOW)

    ids = lax.broadcasted_iota(jnp.int32, (total, TOK_DEV), 0)
    hit = hits_of(routes, ids)
    rank = nn(jnp.where(hit, 1.0, 0.0).astype(LOW), earlier[...])
    place = jnp.where(hit, rank, -1.0)
    spots = lax.broadcasted_iota(jnp.int32, (capacity, TOK_DEV), 0).astype(WIDE)
    place_out[0] = jnp.full(place_out.shape[1:], -1.0, WIDE)
    for e in range(local):
        mine = ids == info[0] * local + e
        place_row = jnp.sum(jnp.where(mine, place, 0.0), axis=0, keepdims=True)
        place_out[0, e : e + 1] = place_row
        chosen_out[0, e * capacity : (e + 1) * capacity] = jnp.where(
            spots == place_row, 1.0, 0.0
        ).astype(LOW)


def tables(info, routes, capacity, local, total):
    count = routes.shape[0]
    return pl.pallas_call(
        functools.partial(tables_kernel, capacity, local, total),
        grid=(count,),
        in_specs=[SMEM, pl.BlockSpec((1, TOP, TOK_DEV), lambda i: (i, 0, 0))],
        out_specs=[
            pl.BlockSpec((1, local * capacity, TOK_DEV), lambda i: (i, 0, 0)),
            pl.BlockSpec((1, 8, TOK_DEV), lambda i: (i, 0, 0)),
        ],
        scratch_shapes=[pltpu.VMEM((TOK_DEV, TOK_DEV), LOW)],
        out_shape=[
            jax.ShapeDtypeStruct((count, local * capacity, TOK_DEV), LOW),
            jax.ShapeDtypeStruct((count, 8, TOK_DEV), WIDE),
        ],
        compiler_params=params(),
        cost_estimate=LITTLE,
        name="route_tables",
    )(info, routes)


def pick_kernel(local, count, chosen, *rest):
    blocks, outs = rest[:count], rest[count : count + local]
    picks, block_in, out_block, sem_in, sem_out = rest[count + local :]
    capacity = outs[0].shape[1]
    copies = [
        (
            pltpu.make_async_copy(chosen.at[q], picks.at[q], sem_in.at[q, 0]),
            pltpu.make_async_copy(blocks[q], block_in.at[q], sem_in.at[q, 1]),
        )
        for q in range(count)
    ]
    for pair in copies:
        run_all(pair)
    sent = []
    for q in range(count):
        wait_all(copies[q])
        out_block[q] = nn(picks[q], block_in[q]).astype(LOW)
        for e in range(local):
            copy = pltpu.make_async_copy(
                out_block.at[q, pl.ds(e * capacity, capacity)], outs[e].at[q], sem_out.at[q, e]
            )
            copy.start()
            sent.append(copy)
    wait_all(sent)


def pick_rows(chosen, blocks, local):
    count, height, _ = chosen.shape
    return pl.pallas_call(
        functools.partial(pick_kernel, local, count),
        in_specs=[ANY] * (1 + count),
        out_specs=[ANY] * local,
        out_shape=[jax.ShapeDtypeStruct((count, height // local, D), LOW)] * local,
        scratch_shapes=[
            pltpu.VMEM((count, height, TOK_DEV), LOW),
            pltpu.VMEM((count, TOK_DEV, D), LOW),
            pltpu.VMEM((count, height, D), LOW),
            pltpu.SemaphoreType.DMA((count, 2)),
            pltpu.SemaphoreType.DMA((count, local)),
        ],
        compiler_params=params(),
        cost_estimate=LITTLE,
        name="pick_rows",
    )(chosen, *blocks)


def dispatch_kernel(local, info, rows, chosen, routes, router, *rest):
    outs, logits = rest[2 * local : 4 * local], rest[-1]
    total = router.shape[1]
    step = pl.program_id(0)
    block = rows[...]
    rows_of = nn(chosen[0], block).astype(LOW)
    capacity = outs[0].shape[1]
    for e in range(local):
        outs[e][0] = rows_of[e * capacity : (e + 1) * capacity]
    part = nn(block, router[...])

    @pl.when(step == 0)
    def _():
        logits[...] = part

    @pl.when(step > 0)
    def _():
        logits[...] += part

    @pl.when(step == pl.num_programs(0) - 1)
    def _():
        values = logits[...].T
        ids = lax.broadcasted_iota(jnp.int32, (total, TOK_DEV), 0)
        weights = jnp.exp(values - jnp.max(values, axis=0, keepdims=True))
        hit = hits_of(routes, ids)
        share = weights / jnp.sum(jnp.where(hit, weights, 0.0), axis=0, keepdims=True)
        for e in range(local):
            mine = ids == info[0] * local + e
            share_row = jnp.sum(jnp.where(mine, share, 0.0), axis=0, keepdims=True)
            picked = chosen[0, e * capacity : (e + 1) * capacity].astype(WIDE)
            outs[local + e][0] = jnp.sum(picked * share_row, axis=1, keepdims=True)


def dispatch(at, info, rows, chosen, routes, router, local, earlier):
    count, height, _ = chosen.shape
    capacity = height // local
    total = router.shape[1]
    wide = D
    out_shape = [jax.ShapeDtypeStruct((count, capacity, D), LOW)] * local + [
        jax.ShapeDtypeStruct((count, capacity, 1), WIDE)
    ] * local
    if earlier is None:
        earlier = [jnp.zeros((8, 128), shape.dtype) for shape in out_shape]
        aliases = {}
    else:
        aliases = {5 + i: i for i in range(len(out_shape))}
    return pl.pallas_call(
        functools.partial(dispatch_kernel, local),
        grid=(D // wide,),
        in_specs=[
            SMEM,
            pl.BlockSpec((TOK_DEV, wide), lambda i: (0, i)),
            pl.BlockSpec((1, height, TOK_DEV), lambda i: (at, 0, 0)),
            pl.BlockSpec((1, TOP, TOK_DEV), lambda i: (at, 0, 0)),
            pl.BlockSpec((wide, total), lambda i: (i, 0)),
        ]
        + [ANY] * len(out_shape),
        out_specs=[pl.BlockSpec((1, capacity, wide), lambda i: (at, 0, i))] * local
        + [pl.BlockSpec((1, capacity, 1), lambda i: (at, 0, 0))] * local,
        scratch_shapes=[pltpu.VMEM((TOK_DEV, total), WIDE)],
        out_shape=out_shape,
        input_output_aliases=aliases,
        compiler_params=params(),
        cost_estimate=LITTLE,
        name="dispatch",
    )(info, rows, chosen, routes, router, *earlier)


def spread_kernel(local, place, *rest):
    dots, out = rest[:local], rest[local]
    spots = lax.broadcasted_iota(jnp.int32, (dots[0].shape[1], TOK_DEV), 0).astype(WIDE)
    for e in range(local):
        chosen = spots == place[0, e : e + 1]
        out[0, e : e + 1] = jnp.sum(jnp.where(chosen, dots[e][0], 0.0), axis=0, keepdims=True)


def spread(place, dots):
    count, capacity, _ = dots[0].shape
    local = len(dots)
    return pl.pallas_call(
        functools.partial(spread_kernel, local),
        grid=(count,),
        out_shape=jax.ShapeDtypeStruct((count, local, TOK_DEV), WIDE),
        in_specs=[pl.BlockSpec((1, 8, TOK_DEV), lambda i: (i, 0, 0))]
        + [pl.BlockSpec((1, capacity, 1), lambda i: (i, 0, 0))] * local,
        out_specs=pl.BlockSpec((1, local, TOK_DEV), lambda i: (i, 0, 0)),
        compiler_params=params(),
        cost_estimate=LITTLE,
        name="spread",
    )(place, *dots)


def expert_kernel(slots, info, rows, grads, shares, *rest):
    refs, (out_rows, back_rows, grad_rows, acts, dots, weight, sem) = rest[:-7], rest[-7:]
    part = weight.shape[1] // slots

    @pl.when(pl.program_id(0) == 0)
    def _():
        def copies(ref, slot):
            return [
                pltpu.make_async_copy(
                    ref.at[pl.ds(which * part, part)],
                    weight.at[which, pl.ds(pl.multiple_of(slot * part, part), part)],
                    sem,
                )
                for which in range(3)
            ]

        if len(refs) == 1:
            for slot in range(slots):
                run_all(copies(refs[0].at[slot], slot))
            for slot in range(slots):
                wait_all(copies(refs[0].at[slot], slot))
        else:
            block, second, above, below, far = refs
            low_end = info[2] == 0
            end = jnp.logical_or(low_end, info[2] == 3)
            run_all(copies(block, info[2]))
            run_all(copies(second, info[3]))

            @pl.when(low_end)
            def _():
                run_all(copies(above, info[4]))

            @pl.when(jnp.logical_not(low_end))
            def _():
                run_all(copies(below, info[4]))

            @pl.when(end)
            def _():
                run_all(copies(far, info[5]))

            @pl.when(jnp.logical_not(end))
            def _():
                run_all(copies(above, info[5]))

            for slot in range(slots):
                wait_all(copies(block, slot))

    row_block = rows[...]
    share = shares[...]
    grad_float = grads[...].astype(WIDE)
    grad_low = (share * grad_float).astype(LOW)
    grad_rows[...] = grad_low
    gate_act = nt(row_block, weight[0])
    upward = nt(row_block, weight[1])
    sigmoid = 1.0 / (1.0 + jnp.exp(-gate_act))
    silu = gate_act * sigmoid
    hidden = (silu * upward).astype(LOW)
    expert_out = nn(hidden, weight[2]).astype(LOW).astype(WIDE)
    out_rows[...] = (share * expert_out).astype(LOW)
    dots[...] = jnp.sum(grad_float * expert_out, axis=1, keepdims=True)
    grad_hidden = nt(grad_low, weight[2])
    grad_gate = (grad_hidden * upward * sigmoid * (1.0 + gate_act * (1.0 - sigmoid))).astype(LOW)
    grad_up = (grad_hidden * silu).astype(LOW)
    back_rows[...] = (nn(grad_gate, weight[0]) + nn(grad_up, weight[1])).astype(LOW)
    for which, act in enumerate((grad_gate, grad_up, hidden)):
        turned = act.T
        for slot in range(slots):
            acts[slot, which * part : (which + 1) * part] = turned[
                slot * part : (slot + 1) * part
            ]


EXPERT_ROWS = 256


def expert(info, rows, grads, shares, refs, slots):
    height = rows.shape[0]
    part = refs[0].shape[-2] // 3
    wide_block = pl.BlockSpec((EXPERT_ROWS, D), lambda i: (i, 0))
    thin_block = pl.BlockSpec((EXPERT_ROWS, 1), lambda i: (i, 0))
    return pl.pallas_call(
        functools.partial(expert_kernel, slots),
        grid=(height // EXPERT_ROWS,),
        out_shape=[jax.ShapeDtypeStruct((height, D), LOW)] * 3
        + [
            jax.ShapeDtypeStruct((slots, 3 * part, height), LOW),
            jax.ShapeDtypeStruct((height, 1), WIDE),
        ],
        in_specs=[SMEM, wide_block, wide_block, thin_block] + [ANY] * len(refs),
        out_specs=[wide_block] * 3
        + [pl.BlockSpec((slots, 3 * part, EXPERT_ROWS), lambda i: (0, 0, i)), thin_block],
        scratch_shapes=[pltpu.VMEM((3, slots * part, D), LOW), pltpu.SemaphoreType.DMA],
        compiler_params=params(),
        cost_estimate=LITTLE,
        name="expert",
    )(info, rows, grads, shares, *refs)


def expert_grads_kernel(acts, rows, grads, out):
    slots, height, _ = acts.shape
    part = height // 3
    for slot in range(slots):
        out[slot, : 2 * part] = nn(acts[slot, : 2 * part], rows[...]).astype(LOW)
        out[slot, 2 * part :] = nn(acts[slot, 2 * part :], grads[...]).astype(LOW)


def expert_grads(acts, rows, grads):
    slots, part, height = acts.shape
    strip = pl.BlockSpec((height, 256), lambda i: (0, i))
    return pl.pallas_call(
        expert_grads_kernel,
        grid=(D // 256,),
        out_shape=jax.ShapeDtypeStruct((slots, part, D), LOW),
        in_specs=[whole(acts.shape), strip, strip],
        out_specs=pl.BlockSpec((slots, part, 256), lambda i: (0, 0, i)),
        compiler_params=params(),
        cost_estimate=LITTLE,
        name="expert_gradients",
    )(acts, rows, grads)


SHARE_ROWS = 32


def combine_kernel(local, first, step, info, chosen, *rest):
    rows, dots, out = rest[:local], rest[local:-6], rest[-6]
    picks, rows_in, out_block, sem_in, sem_out = rest[-5:]
    number = out.shape[0]
    capacity = rows[0].shape[1]
    copies = []
    for n in range(number):
        q = first + step * n
        copies.append(
            [pltpu.make_async_copy(chosen.at[q], picks.at[n], sem_in.at[n, local])]
            + [
                pltpu.make_async_copy(
                    rows[e].at[q],
                    rows_in.at[n, pl.ds(e * capacity, capacity)],
                    sem_in.at[n, e],
                )
                for e in range(local)
            ]
        )
    for group in copies:
        run_all(group)
    sent = []
    for n in range(number):
        wait_all(copies[n])
        out_block[n, :TOK_DEV] = tn(picks[n], rows_in[n]).astype(LOW)
        if dots:
            row = lax.broadcasted_iota(jnp.int32, (SHARE_ROWS, D), 0)
            values = jnp.zeros((SHARE_ROWS, D), WIDE)
            for e in range(local):
                picked = picks[n, e * capacity : (e + 1) * capacity].astype(WIDE)
                share = picked * dots[e][first + step * n]
                high, low = split(jnp.sum(share, axis=0, keepdims=True))
                pieces = [high.astype(WIDE), low.astype(WIDE)]
                pieces.append(jnp.zeros((1, D - 2 * TOK_DEV), WIDE))
                line = jnp.concatenate(pieces, axis=1)
                values = jnp.where(row == info[0] * local + e, line, values)
            out_block[n, TOK_DEV:] = values.astype(LOW)
        copy = pltpu.make_async_copy(out_block.at[n], out.at[n], sem_out.at[n])
        copy.start()
        sent.append(copy)
    wait_all(sent)


def combine(info, chosen, rows, first, step, dots=()):
    count, capacity, _ = rows[0].shape
    local = len(rows)
    number = (count - first + step - 1) // step
    height = TOK_DEV + (SHARE_ROWS if dots else 0)
    return pl.pallas_call(
        functools.partial(combine_kernel, local, first, step),
        out_shape=jax.ShapeDtypeStruct((number, height, D), LOW),
        in_specs=[SMEM, ANY]
        + [ANY] * local
        + [pl.BlockSpec(memory_space=pltpu.VMEM)] * len(dots),
        out_specs=ANY,
        scratch_shapes=[
            pltpu.VMEM((number, local * capacity, TOK_DEV), LOW),
            pltpu.VMEM((number, local * capacity, D), LOW),
            pltpu.VMEM((number, height, D), LOW),
            pltpu.SemaphoreType.DMA((number, local + 1)),
            pltpu.SemaphoreType.DMA((number,)),
        ],
        compiler_params=params(),
        cost_estimate=LITTLE,
        name="combine",
    )(info, chosen, *rows, *dots)


def chip_adds_kernel(keep, got, send_x, send_y, near_x, near_y, one, two, sem_in, sem_out):
    half = send_x.shape[1]
    copies = [
        (
            pltpu.make_async_copy(keep.at[i], one.at[i], sem_in.at[i, 0]),
            pltpu.make_async_copy(got.at[i], two.at[i], sem_in.at[i, 1]),
        )
        for i in range(4)
    ]
    for pair in copies:
        run_all(pair)
    sent = []
    for i in range(4):
        wait_all(copies[i])
        one[i] = (one[i].astype(WIDE) + two[i].astype(WIDE)).astype(LOW)
        upper = (near_x, send_x)[i % 2].at[i // 2]
        lower = (near_y, send_y)[i // 2].at[i % 2]
        for part, to in enumerate((upper, lower)):
            copy = pltpu.make_async_copy(
                one.at[i, pl.ds(part * half, half)], to, sem_out.at[i, part]
            )
            copy.start()
            sent.append(copy)
    wait_all(sent)


def chip_adds(keep, got):
    _, height, width = keep.shape
    shape = jax.ShapeDtypeStruct((2, height // 2, width), LOW)
    return pl.pallas_call(
        chip_adds_kernel,
        out_shape=(shape,) * 4,
        in_specs=[ANY, ANY],
        out_specs=(ANY,) * 4,
        scratch_shapes=[
            pltpu.VMEM(keep.shape, LOW),
            pltpu.VMEM(keep.shape, LOW),
            pltpu.SemaphoreType.DMA((4, 2)),
            pltpu.SemaphoreType.DMA((4, 2)),
        ],
        compiler_params=params(),
        cost_estimate=LITTLE,
        name="chip_sums",
    )(keep, got)


def corner_adds_kernel(near_x, got_x, near_y, got_y, send_y, send_x):
    send_y[...] = (near_x[0].astype(WIDE) + got_x[0].astype(WIDE)).astype(LOW)
    send_x[...] = (near_y[0].astype(WIDE) + got_y[0].astype(WIDE)).astype(LOW)


def corner_adds(near_x, got_x, near_y, got_y):
    _, half, width = near_x.shape
    rows = half
    block = pl.BlockSpec((1, rows, width), lambda i: (1, i, 0))
    out = pl.BlockSpec((rows, width), lambda i: (i, 0))
    return pl.pallas_call(
        corner_adds_kernel,
        grid=(half // rows,),
        out_shape=(jax.ShapeDtypeStruct((half, width), LOW),) * 2,
        in_specs=[block] * 4,
        out_specs=(out, out),
        compiler_params=params(),
        cost_estimate=LITTLE,
        name="corner_sums",
    )(near_x, got_x, near_y, got_y)


def split(values):
    high = values.astype(LOW)
    return high, (values - high.astype(WIDE)).astype(LOW)


def norm_back(values, gain, grad):
    factor = lax.rsqrt(jnp.mean(values * values, axis=-1, keepdims=True) + EPSILON)
    scaled = gain * grad
    mean = jnp.mean(values * scaled, axis=-1, keepdims=True)
    grad_values = factor * scaled - values * (factor * factor * factor * mean)
    grad_gain = jnp.sum(grad * values * factor, axis=0, keepdims=True)
    return grad_values, grad_gain


def router_back(logits, routes, grad_shares):
    ids = lax.broadcasted_iota(jnp.int32, logits.shape, 0)
    hit = ids == routes[0:1]
    for k in range(1, TOP):
        hit = jnp.logical_or(hit, ids == routes[k : k + 1])
    weights = jnp.exp(logits - jnp.max(logits, axis=0, keepdims=True))
    probs = weights / jnp.sum(weights, axis=0, keepdims=True)
    chosen = jnp.sum(jnp.where(hit, probs, 0.0), axis=0, keepdims=True)
    grads = jnp.where(hit, grad_shares, 0.0)
    mean = jnp.sum(probs * grads, axis=0, keepdims=True) / chosen
    grad_probs = jnp.where(hit, (grads - mean) / chosen, 0.0)
    return probs * (grad_probs - jnp.sum(probs * grad_probs, axis=0, keepdims=True))


def branch_back_kernel(
    parts, info, residual, normed, cotangent, routes, router, gain, *rest
):
    sums, rest = rest[:parts], rest[parts:]
    experts = router.shape[0]
    count = len(rest) - 7
    refs = rest[:count]
    grad_residual, grad_branch, grad_heads, grad_gain, grad_router, weight, sem = rest[count:]

    @pl.when(pl.program_id(0) == 0)
    def _():
        copies = weight_copies(info, refs, weight, sem, D // QUARTERS + 128, D // QUARTERS)
        run_all(copies)
        logits = nt(router[...], normed[...])
        if parts == 2:
            back_sum, grad_shares = sums[0][...], sums[1][...]
        else:
            values = [
                (ref[0] if len(ref.shape) == 3 else ref[...]).astype(WIDE) for ref in sums
            ]
            upper = values[0] + values[1] + values[2]
            lower = values[3] + values[4] + values[5]
            last = lower.shape[0] - SHARE_ROWS
            shares = lower[last : last + experts]
            grad_shares = shares[:, :TOK_DEV] + shares[:, TOK_DEV : 2 * TOK_DEV]
            back_sum = jnp.concatenate([upper, lower[:last]], axis=0)
        high, low = split(router_back(logits, routes[...], grad_shares))
        grad_router[...] = nn(high, normed[...]) + nn(low, normed[...])
        grad_normed = tn(high, router[...]) + tn(low, router[...])
        grad_normed += back_sum
        grad_values, gain_grad = norm_back(residual[...], gain[...], grad_normed)
        grad_gain[...] = gain_grad
        total = cotangent[...].astype(WIDE) + grad_values
        grad_residual[...] = total
        grad_branch[...] = total.astype(LOW)
        wait_all(copies)

    at = pl.ds(pl.multiple_of(pl.program_id(0) * STEP, STEP), STEP)
    grad_heads[...] = nt(grad_branch[...], weight[at, :]).astype(LOW)


def branch_back(info, residual, normed, sums, cotangent, routes, router, gain, refs):
    full = (TOK_DEV, D)
    total = router.shape[0]
    return pl.pallas_call(
        functools.partial(branch_back_kernel, len(sums)),
        grid=(D // STEP,),
        out_shape=(
            jax.ShapeDtypeStruct(full, WIDE),
            jax.ShapeDtypeStruct(full, LOW),
            jax.ShapeDtypeStruct(full, LOW),
            jax.ShapeDtypeStruct((1, D), WIDE),
            jax.ShapeDtypeStruct((total, D), WIDE),
        ),
        in_specs=[SMEM]
        + [whole(full)] * 3
        + [whole((TOP, TOK_DEV)), whole((total, D)), whole((1, D))]
        + [whole(part.shape if part.ndim == 2 else (1,) + part.shape[1:]) for part in sums]
        + [ANY] * len(refs),
        out_specs=(
            whole(full),
            whole(full),
            pl.BlockSpec((TOK_DEV, STEP), lambda i: (0, i)),
            whole((1, D)),
            whole((total, D)),
        ),
        scratch_shapes=[pltpu.VMEM((D, D), LOW), pltpu.SemaphoreType.DMA],
        compiler_params=params(),
        cost_estimate=LITTLE,
        name="experts_norm_back",
    )(info, residual, normed, cotangent, routes, router, gain, *sums, *refs)


def join_grads_kernel(info, own_grad, source_grad, arrived, cosine, sine, out):
    half = HEAD_DIM // 2
    first = lax.broadcasted_iota(jnp.int32, (TOK_DEV, HEAD_DIM), 1) < half
    leaves = info[1] == 0

    def total(column):
        columns = slice(column, column + 128)
        extra = source_grad[:, columns] + arrived[:, columns].astype(WIDE)
        return own_grad[:, columns] + jnp.where(leaves, 0.0, extra)

    for g in range(KV_HEADS):
        key = turn_back(total(128 * g), cosine[...], sine[...])
        value = total(KEY_WIDTH + 128 * g)
        out[:, 256 * g : 256 * g + 128] = jnp.where(
            first, key, pltpu.roll(value, half, 1)
        ).astype(LOW)
        out[:, 256 * g + 128 : 256 * g + 256] = jnp.where(
            first, pltpu.roll(key, half, 1), value
        ).astype(LOW)


def join_grads(info, own_grad, source_grad, arrived, cosine, sine):
    vmem = pl.BlockSpec(memory_space=pltpu.VMEM)
    return pl.pallas_call(
        join_grads_kernel,
        out_shape=jax.ShapeDtypeStruct((TOK_DEV, 2 * KEY_WIDTH), LOW),
        in_specs=[SMEM] + [vmem] * 5,
        out_specs=vmem,
        compiler_params=params(),
        cost_estimate=LITTLE,
        name="join_key_value_gradients",
    )(info, own_grad, source_grad, arrived, cosine, sine)


def token_back_kernel(info, grad_query, grad_pair, tokens, grad_residual, gain, *rest):
    count = (len(rest) - 6) // 2
    query_refs, pair_refs = rest[:count], rest[count : 2 * count]
    out, grad_gain, query_weight, pair_weight, grad_normed, sem = rest[2 * count :]

    @pl.when(pl.program_id(0) == 0)
    def _():
        copies = weight_copies(info, query_refs, query_weight, sem, 0, D // QUARTERS)
        copies += weight_copies(info, pair_refs, pair_weight, sem, D // QUARTERS, 128)
        run_all(copies)
        wait_all(copies)

    at = pl.ds(pl.multiple_of(pl.program_id(0) * STEP, STEP), STEP)
    grad_normed[:, at] = nt(grad_query[...], query_weight[at, :]) + nt(
        grad_pair[...], pair_weight[at, :]
    )

    @pl.when(pl.program_id(0) == pl.num_programs(0) - 1)
    def _():
        grad_values, gain_grad = norm_back(
            tokens[...].astype(WIDE), gain[...], grad_normed[...]
        )
        grad_gain[...] = gain_grad
        out[...] = (grad_residual[...] + grad_values).astype(LOW)


def token_back(info, grad_query, grad_pair, tokens, grad_residual, gain, query_refs, pair_refs):
    full = (TOK_DEV, D)
    return pl.pallas_call(
        token_back_kernel,
        grid=(D // STEP,),
        out_shape=(jax.ShapeDtypeStruct(full, LOW), jax.ShapeDtypeStruct((1, D), WIDE)),
        in_specs=[
            SMEM,
            whole(full),
            whole((TOK_DEV, 2 * KEY_WIDTH)),
            whole(full),
            whole(full),
            whole((1, D)),
        ]
        + [ANY] * (len(query_refs) + len(pair_refs)),
        out_specs=(whole(full), whole((1, D))),
        scratch_shapes=[
            pltpu.VMEM((D, D), LOW),
            pltpu.VMEM((D, 2 * KEY_WIDTH), LOW),
            pltpu.VMEM(full, WIDE),
            pltpu.SemaphoreType.DMA,
        ],
        compiler_params=params(),
        cost_estimate=LITTLE,
        name="token_gradient",
    )(info, grad_query, grad_pair, tokens, grad_residual, gain, *query_refs, *pair_refs)


def weight_grads_kernel(parts, whole_rows, info, *rest):
    ins, (keep, send) = rest[:-2], rest[-2:]
    depth = D // 8
    core = info[0] & 1
    chip = pl.program_id(0) ^ (info[0] >> 1)
    for strip_at, grads_at, start, width in parts:
        low = tn(ins[strip_at][...], ins[grads_at][...]).astype(LOW)
        columns = slice(start, start + width)
        for slot in range(QUARTERS):
            for j in range(QUARTERS):

                @pl.when(info[2 + slot] == j)
                def _():
                    piece = low[:, j * width : (j + 1) * width]
                    upper, lower = piece[:depth], piece[depth:]
                    keep[0, slot, :depth, columns] = jnp.where(core == 0, upper, lower)
                    send[0, slot, :depth, columns] = jnp.where(core == 0, lower, upper)
                    if not whole_rows:
                        blank = jnp.zeros((EXTRA, width), LOW)
                        keep[0, slot, depth:, columns] = blank
                        send[0, slot, depth:, columns] = blank

    if whole_rows:
        extra = ins[-1]
        for slot in range(QUARTERS):
            to = info[2 + slot]
            keep[0, slot, depth:] = extra[(chip * 2 + core) * QUARTERS + to]
            send[0, slot, depth:] = extra[(chip * 2 + 1 - core) * QUARTERS + to]


def weight_grads(info, strips, grads, parts, extra, earlier=()):
    depth = D // 8
    strip = pl.BlockSpec((TOK_DEV, 2 * depth), lambda i, info: (0, i ^ (info[0] >> 1)))
    more = [] if extra is None else [extra]
    width = 2 * D // QUARTERS + 128
    shape = (4, QUARTERS, depth + EXTRA, width)
    if earlier:
        out = pl.BlockSpec((1, QUARTERS, depth + EXTRA, 128), lambda i, info: (i, 0, 0, 3))
    else:
        out = pl.BlockSpec((1,) + shape[1:], lambda i, info: (i, 0, 0, 0))
    inputs = [*strips, *grads, *more]

    def kernel(info, *rest):
        count = len(inputs)
        weight_grads_kernel(
            parts, extra is not None, info, *rest[:count], *rest[count + len(earlier) :]
        )

    return pl.pallas_call(
        kernel,
        grid_spec=pltpu.PrefetchScalarGridSpec(
            num_scalar_prefetch=1,
            grid=(4,),
            in_specs=[strip] * len(strips)
            + [
                pl.BlockSpec(a.shape, lambda i, info, n=a.ndim: (0,) * n)
                for a in (*grads, *more)
            ]
            + [ANY] * len(earlier),
            out_specs=(out, out),
        ),
        out_shape=(jax.ShapeDtypeStruct(shape, LOW),) * 2,
        input_output_aliases={1 + len(inputs) + i: i for i in range(len(earlier))},
        compiler_params=params(),
        cost_estimate=LITTLE,
        name="weight_gradients",
    )(info, *inputs, *earlier)


def position_of(token_index):
    branch_place = TRUNK + (token_index - TRUNK) % BRANCH
    leaf_place = TRUNK + BRANCH + (token_index - TOK_DEV) % BRANCH
    return jnp.where(
        token_index < TRUNK, token_index, jnp.where(token_index < TOK_DEV, branch_place, leaf_place)
    )


def rotary_tables(positions):
    half_dim = HEAD_DIM // 2
    frequency = ROPE_BASE ** (-jnp.arange(half_dim, dtype=jnp.float32) / half_dim)
    angles = positions.astype(jnp.float32)[:, None] * frequency[None, :]
    cosine, sine = (jnp.cos(angles), jnp.sin(angles))
    return (
        jnp.concatenate([cosine, cosine], axis=1),
        jnp.concatenate([-sine, sine], axis=1),
    )


def after(values, *earlier):
    return lax.optimization_barrier((values, earlier))[0]


def fast_mesh():
    return lax.axis_size("rows") == 8 and lax.axis_size("cols") == 4


SLOT_SHARD = ((0, 2, 1, 3), (1, 3, 0, 2), (2, 0, 1, 3), (3, 1, 2, 0))
UP = [(0, 1), (1, 2), (2, 3)]
DOWN = [(1, 0), (2, 1), (3, 2)]
FAR = [(0, 3), (3, 0)]


def send_near(block):
    return lax.ppermute(block, "cols", DOWN), lax.ppermute(block, "cols", UP)


def send_far(block):
    return lax.ppermute(block, "cols", FAR)


def send_over(block):
    return lax.ppermute(block, "cols", [(0, 2), (1, 3), (2, 0), (3, 1)])


def send_second(block, near):
    place = lax.axis_index("cols")
    above, below = near
    payload = jnp.where(place == 1, above, jnp.where(place == 2, below, block))
    return lax.ppermute(payload, "cols", [(3, 1), (1, 0), (0, 2), (2, 3)])


def slot_list(block, near, second, far):
    place = lax.axis_index("cols")
    above, below = near
    end = (place == 0) | (place == 3)
    return [
        block,
        second,
        jnp.where(place == 0, above, below),
        jnp.where(end, far, above),
    ]


def reduce_slots(slots):
    place = lax.axis_index("cols")
    own, second, third, fourth = slots
    arrived = (
        lax.ppermute(jnp.where(place == 0, third, fourth), "cols", UP),
        lax.ppermute(third, "cols", DOWN),
        send_over(second),
        send_far(fourth),
    )
    return own.astype(WIDE) + sum(block.astype(WIDE) for block in arrived)


def flip(block, bit):
    count = lax.axis_size("rows")
    return lax.ppermute(block, "rows", [(i, i ^ bit) for i in range(count)])


def add_low(one, two):
    return (one.astype(WIDE) + two.astype(WIDE)).astype(LOW)


def chips_second(near_x, near_y, got_x, got_y):
    for_y, for_x = corner_adds(near_x, got_x, near_y, got_y)
    return (near_x, got_x, flip(for_y, 4), near_y, got_y, flip(for_x, 2))


def turn_corner(beside, across):
    half = beside.shape[0] // 2
    return jnp.concatenate([flip(beside[:half], 4), flip(across[half:], 2)], axis=0)


def send_chips(sums):
    return flip(sums[0], 2), flip(sums[1], 4)


def sum_parts(parts):
    wide = [(a[0] if a.ndim == 3 else a).astype(WIDE) for a in parts]
    if len(wide) == 1:
        return wide[0]
    return jnp.concatenate([wide[0] + wide[1] + wide[2], wide[3] + wide[4] + wide[5]], axis=0)


def on_device(
    tokens,
    query_weight,
    key_weight,
    value_weight,
    out_weight,
    router_weight,
    attention_gain,
    experts_gain,
    gate_weight,
    upward_weight,
    down_weight,
    routes,
    leaf_parent,
    cotangent,
):
    row_count = lax.axis_size("rows")
    col_count = lax.axis_size("cols")
    row_place = lax.axis_index("rows")
    col_place = lax.axis_index("cols")
    fast = fast_mesh()
    parity = lax.rem(col_place, 2)
    tree_id = lax.div(row_place * col_count + col_place, 2)
    parent_row = lax.dynamic_slice_in_dim(leaf_parent, tree_id, 1, 0)[0]
    depth, query_part = query_weight.shape
    key_part = key_weight.shape[1]
    router_part = router_weight.shape[1]
    gain_part = attention_gain.shape[0]
    expert_total = router_part * col_count
    local_experts = gate_weight.shape[0]
    capacity = TOK_DEV * TOP // expert_total * 5 // 4

    shards = (
        jnp.asarray(SLOT_SHARD, jnp.int32)[col_place]
        if fast
        else jnp.arange(4, dtype=jnp.int32)
    )
    branch_rows = jnp.where(parity == 0, TRUNK + BRANCH * parent_row, TRUNK)
    info = jnp.concatenate(
        [jnp.stack([row_place, parity]), shards, branch_rows, jnp.zeros((2,), jnp.int32)]
    ).astype(jnp.int32)

    packed = jnp.concatenate([query_weight, key_weight, value_weight, out_weight], axis=1)
    local_index = (1 - parity) * TOK_DEV + jnp.arange(TOK_DEV, dtype=jnp.int32)
    cosine, sine = rotary_tables(position_of(local_index))
    shard_blocks = [
        jnp.concatenate(
            [gate_weight[expert].T, upward_weight[expert].T, down_weight[expert]], axis=0
        )
        for expert in range(local_experts)
    ]
    expert_refs = []
    if fast:
        wide = packed.shape[1]
        gains = jnp.concatenate([attention_gain, experts_gain])[None, :]
        packed = jnp.concatenate(
            [
                packed,
                jnp.pad(router_weight.T, ((0, 0), (0, wide - depth))),
                jnp.pad(gains, ((0, 0), (0, wide - 2 * gain_part))),
                jnp.pad(routes.T.astype(LOW), ((0, 0), (0, wide - TOK_DEV))),
                jnp.zeros((EXTRA - router_part - 1 - TOP, wide), LOW),
            ],
            axis=0,
        )
        packed_near = send_near(packed)
        packed_far = send_far(packed)
        packed_second = send_over(packed)
        first_block = after(shard_blocks[0], *packed_near)
        first_near = send_near(first_block)
        first_second = send_second(first_block, first_near)
        own = jnp.stack(slot_list(packed, packed_near, packed_second, packed_far))
        own = after(own, info, cosine, sine)
        beside, across = flip(own, 2), flip(own, 4)
        own_in = flip(own, 1)
        beside, across = after((beside, across), own_in, *first_near)
        corner = [flip(beside[:2], 4), flip(across[2:], 2)]
        pair_in = flip(jnp.concatenate([beside, across], axis=0), 1)
        corner_in = [flip(piece, 1) for piece in corner]
        grad_in = after(cotangent, *corner)
        grad_flips = (flip(grad_in, 2), flip(grad_in, 4))
        pieces = [own, own_in, beside, across, *corner, pair_in, *corner_in]
        at = depth + router_part + 1
        near_slots = [own, own_in, beside, pair_in, across, pair_in[4:], corner[0], corner_in[0]]
        routes_all = jnp.stack([part[0, at : at + TOP, :TOK_DEV] for part in near_slots])
        routes_all = routes_all.astype(jnp.int32)
        chosen, place_rows = tables(info, routes_all, capacity, local_experts, expert_total)
        query_refs = pair_refs = out_refs = pieces
        extra_rows = extras(info, pieces)
        router_all = extra_rows[:, :router_part, :depth]
        attention_scale = extra_rows[:, router_part, :gain_part]
        experts_scale = extra_rows[:, router_part, gain_part : 2 * gain_part]
    else:
        packed_all = lax.all_gather(lax.all_gather(packed, "cols", axis=0), "rows", axis=0)

        def unpack(start, width):
            part = packed_all[..., start : start + width]
            return jnp.swapaxes(part, 1, 2).reshape(row_count * depth, col_count * width)

        key_at = query_part
        query_refs = [unpack(0, query_part)]
        pair_refs = [
            jnp.concatenate(
                [
                    unpack(key_at, key_part).reshape(D, QUARTERS, -1),
                    unpack(key_at + key_part, key_part).reshape(D, QUARTERS, -1),
                ],
                axis=2,
            ).reshape(D, -1)
        ]
        out_refs = [unpack(key_at + 2 * key_part, query_part)]
        routes_all = lax.all_gather(routes.T, "rows", axis=0)
        chosen, place_rows = tables(info, routes_all, capacity, local_experts, expert_total)
        axes = ("rows", "cols")
        router_all = jnp.swapaxes(lax.all_gather(router_weight, axes, axis=0), 1, 2)
        attention_scale = lax.all_gather(attention_gain, axes, axis=0)
        experts_scale = lax.all_gather(experts_gain, axes, axis=0)

    attention_scale = attention_scale.reshape(1, D).astype(WIDE)
    experts_scale = experts_scale.reshape(1, D).astype(WIDE)
    router_rows = jnp.transpose(
        router_all.reshape(row_count, col_count, router_part, depth), (1, 2, 0, 3)
    ).reshape(expert_total, D)
    router_cols = router_rows.T
    tokens_in = after(tokens, first_second, chosen) if fast else tokens
    normed, own_pair = key_value(info, tokens_in, attention_scale, cosine, sine, pair_refs)
    pairs = [(i + 1, i) for i in range(0, col_count, 2)]
    partner = lax.ppermute(own_pair, "cols", pairs)
    queries = query(info, normed, cosine, sine, query_refs)
    if fast:
        first_far = send_far(after(first_block, partner, queries))
        expert_refs.append([first_block, first_second, *first_near, first_far])
        grad_flips = after(grad_flips, queries)
        grad_corner = turn_corner(*grad_flips)
    heads = attention(info, queries, own_pair, partner)
    if fast:
        heads = after(heads, grad_corner)
        grad_near = [cotangent, *grad_flips, grad_corner]
        grad_blocks = [block for one in grad_near for block in (one, flip(one, 1))]
    else:
        grad_all = lax.all_gather(cotangent, "rows", axis=0)
        grad_blocks = [grad_all[q] for q in range(row_count)]
    residual, normed_two = out_projection(info, heads, tokens, experts_scale, out_refs)

    if fast:
        beside, across = flip(normed_two, 2), flip(normed_two, 4)
        beside_in = flip(normed_two, 1)
        later_block = after(shard_blocks[1], first_far, normed_two)
        expert_refs.append([lax.all_gather(later_block, "cols", axis=0)])
    else:
        rows_all = lax.all_gather(normed_two, "rows", axis=0)
        expert_refs = [[lax.all_gather(block, "cols", axis=0)] for block in shard_blocks]
    grad_rows = pick_rows(chosen, grad_blocks, local_experts)

    def place_block(q, block, picked):
        return dispatch(
            q, info, block, chosen, routes_all, router_cols, local_experts, picked
        )

    if fast:
        half = TOK_DEV // 2
        picked = place_block(0, normed_two, None)
        picked = place_block(1, beside_in, picked)
        beside, across = after((beside, across), picked, *grad_rows)
        corner = [flip(beside[:half], 4), flip(across[half:], 2)]
        picked = place_block(2, beside, picked)
        picked = place_block(4, across, picked)
        beside_in = flip(beside, 1)
        across_in = flip(across, 1)
        picked = place_block(3, beside_in, picked)
        picked = place_block(5, across_in, picked)
        corner = jnp.concatenate(after(corner, picked), axis=0)
        corner_in = flip(corner, 1)
        picked = place_block(6, corner, picked)
        picked = place_block(7, corner_in, picked)
    else:
        picked = None
        for q in range(row_count):
            picked = place_block(q, rows_all[q], picked)
    height = row_count * capacity
    token_rows = [a.reshape(height, D) for a in picked[:local_experts]]
    grad_rows = [a.reshape(height, D) for a in grad_rows]
    share_rows = [a.reshape(height, 1) for a in picked[local_experts:]]

    out_rows, back_rows, gate_dots, reduced = ([], [], [], [])
    for e in range(local_experts):
        rows_in = after(token_rows[e], *reduced_in) if e else token_rows[e]
        out_row, back_row, grad_row, acts, dots = expert(
            info, rows_in, grad_rows[e], share_rows[e], expert_refs[e], col_count
        )
        out_rows.append(out_row.reshape(row_count, capacity, D))
        back_rows.append(back_row.reshape(row_count, capacity, D))
        gate_dots.append(dots.reshape(row_count, capacity, 1))
        if fast and e == 1:
            got = flip(combine(info, chosen, back_rows, 1, 2, gate_dots), 1)
            back_keep = combine(info, chosen, back_rows, 0, 2, gate_dots)
            for_x, for_y, near_x, near_y = chip_adds(back_keep, got)
            acts = after(acts, for_x)
            back_flips = send_chips((for_x, for_y))
        slots = expert_grads(acts, token_rows[e], grad_row)
        reduced_in = (slots,)
        if e and fast:
            out_got = flip(combine(info, chosen, out_rows, 1, 2), 1)
            out_keep = combine(info, chosen, out_rows, 0, 2)
            back_flips = after(back_flips, slots, out_keep)
            back_parts = chips_second(near_x, near_y, *back_flips)
        else:
            reduced.append(lax.psum_scatter(slots, "cols", scatter_dimension=0, tiled=False))

    if fast:
        out_first = chip_adds(out_keep, out_got)
        back_parts = after(back_parts, out_first[0])
    else:
        spread_dots = spread(place_rows, gate_dots)
        grad_shares = lax.all_to_all(spread_dots, "rows", split_axis=0, concat_axis=0, tiled=True)

        def summed(rows):
            part = combine(info, chosen, rows, 0, 1)
            return lax.psum_scatter(part, "rows", scatter_dimension=0).astype(WIDE)

        back_parts = (summed(back_rows), grad_shares.reshape(expert_total, TOK_DEV))
        mixture = (summed(out_rows),)

    grad_residual, grad_branch, grad_heads, experts_gain_grad, router_grad = branch_back(
        info,
        residual,
        normed_two,
        back_parts,
        cotangent,
        routes.T,
        router_rows,
        experts_scale,
        out_refs,
    )
    if fast:
        out_flips = send_chips(after(out_first[:2], back_parts[2], back_parts[5]))
        router_parts = jnp.transpose(
            router_grad.astype(LOW).reshape(col_count, router_part, row_count, depth),
            (2, 0, 1, 3),
        ).reshape(row_count * col_count, router_part, depth)
        gain_rows = experts_gain_grad.astype(LOW).reshape(row_count * col_count, 1, gain_part)
        extra = jnp.concatenate(
            [
                jnp.pad(router_parts, ((0, 0), (0, 0), (0, wide - depth))),
                jnp.pad(gain_rows, ((0, 0), (0, 0), (0, wide - gain_part))),
                jnp.zeros((row_count * col_count, EXTRA - router_part - 1, wide), LOW),
            ],
            axis=1,
        )
    grad_query, own_grad, source_grad = attention_back(
        info, queries, own_pair, partner, grad_heads, cosine, sine
    )
    arrived = lax.ppermute(source_grad.astype(LOW), "cols", [(j, i) for i, j in pairs])
    if fast:
        parts = ((0, 2, 0, query_part), (1, 3, query_part + 2 * key_part, query_part))
        slots = after(slots, reduced[0], grad_query)
        reduced.append(lax.psum_scatter(slots, "cols", scatter_dimension=0, tiled=False))
        out_flips = after(out_flips, grad_query)
        near_x, near_y = out_first[2:]
        for_y, for_x = corner_adds(near_x, out_flips[0], near_y, out_flips[1])
        mixture = (near_x, out_flips[0], flip(for_y, 4))
        mixture += (near_y, out_flips[1], flip(for_x, 2))
        grad_branch = after(grad_branch, for_y)
        keep_send = weight_grads(
            info, [normed, heads], [grad_query, grad_branch], parts, extra
        )
        arrived = after(arrived, *keep_send, mixture[2], mixture[5])
    grad_pair = join_grads(info, own_grad, source_grad, arrived, cosine, sine)
    if fast:
        keep, send = weight_grads(
            info, [normed], [grad_pair], ((0, 1, 0, 2 * key_part),), None, keep_send
        )
        sent = flip(send, 1)
        grad_pair = after(grad_pair, keep)
    tokens_grad, attention_gain_grad = token_back(
        info, grad_query, grad_pair, tokens, grad_residual, attention_scale, query_refs, pair_refs
    )

    if fast:
        flat = (4, col_count * (depth + EXTRA), wide)
        sent_first = chip_adds(keep.reshape(flat), sent.reshape(flat))
        sent_chips = after(send_chips(sent_first[:2]), tokens_grad)
        slots = sum_parts(chips_second(*sent_first[2:], *sent_chips))
        slots = slots.reshape(col_count, depth + EXTRA, wide)
        width = query_part + 2 * key_part
        own_slots = own
        gain_sums = sum(
            jnp.sum(own_slots[i][:depth, :width].astype(WIDE) * slots[i, :depth, :width], axis=1)
            for i in range(4)
        )
        own_gains = lax.dynamic_slice_in_dim(attention_scale[0], row_place * depth, depth, 0)
        gain_sums = (gain_sums / own_gains).reshape(col_count, 1, gain_part)
        gain_sums = jnp.pad(
            jnp.take(gain_sums, shards, axis=0),
            ((0, 0), (depth + router_part + 1, EXTRA - router_part - 2), (0, wide - gain_part)),
        )
        slots = after((slots + gain_sums).astype(LOW), reduced[1])

        sums = reduce_slots(slots)
        router_sum = sums[depth : depth + router_part, :depth].T
        experts_gain_sum = sums[depth + router_part, :gain_part]
        attention_gain_sum = sums[depth + router_part + 1, :gain_part]
        sums = sums[:depth]
    else:
        full_grads = [
            tn(normed, grad_query),
            *jnp.moveaxis(tn(normed, grad_pair).reshape(D, QUARTERS, 2, -1), 2, 0),
            tn(heads, grad_branch),
        ]
        packed_grad = jnp.concatenate(
            [
                grad.astype(LOW).reshape(row_count, depth, col_count, -1)
                for grad in full_grads
            ],
            axis=3,
        )
        row_sums = lax.psum_scatter(packed_grad, "rows", scatter_dimension=0)
        sums = lax.psum_scatter(row_sums, "cols", scatter_dimension=1).astype(WIDE)
        small_grads = jnp.concatenate(
            [
                attention_gain_grad.reshape(-1, gain_part),
                experts_gain_grad.reshape(-1, gain_part),
                jnp.transpose(
                    router_grad.reshape(col_count, router_part, row_count, depth), (2, 0, 3, 1)
                ).reshape(row_count * col_count, depth * router_part),
            ],
            axis=1,
        )
        small_grads = small_grads.reshape(row_count, -1)
        small_grads = lax.all_to_all(small_grads, "rows", split_axis=0, concat_axis=0, tiled=True)
        small_grads = jnp.sum(small_grads, axis=0).reshape(col_count, -1)
        small_grads = lax.all_to_all(small_grads, "cols", split_axis=0, concat_axis=0, tiled=True)
        small_sums = jnp.sum(small_grads, axis=0)
        attention_gain_sum = small_sums[:gain_part]
        experts_gain_sum = small_sums[gain_part : 2 * gain_part]
        router_sum = small_sums[2 * gain_part :].reshape(depth, router_part)

    layer_output = (residual + sum_parts(mixture)).astype(LOW)
    key_at = query_part
    value_at = key_at + key_part
    out_at = value_at + key_part
    part = down_weight.shape[1]
    expert_sums = [block.astype(WIDE) for block in reduced]
    gate_grad, upward_grad, down_grad = (
        jnp.stack([sums_of[which * part : (which + 1) * part] for sums_of in expert_sums])
        for which in range(3)
    )
    return (
        layer_output,
        tokens_grad,
        sums[:, :key_at],
        sums[:, key_at:value_at],
        sums[:, value_at:out_at],
        sums[:, out_at:],
        router_sum,
        attention_gain_sum,
        experts_gain_sum,
        jnp.swapaxes(gate_grad, 1, 2),
        jnp.swapaxes(upward_grad, 1, 2),
        down_grad,
    )


def solution(mesh):
    in_specs = (
        P(("rows", "cols"), None),
        P("rows", "cols"),
        P("rows", "cols"),
        P("rows", "cols"),
        P("rows", "cols"),
        P("rows", "cols"),
        P(("rows", "cols")),
        P(("rows", "cols")),
        P("rows", None, "cols"),
        P("rows", None, "cols"),
        P("rows", "cols", None),
        P(("rows", "cols"), None),
        P(),
        P(("rows", "cols"), None),
    )
    out_specs = (
        P(("rows", "cols"), None),
        P(("rows", "cols"), None),
        P("rows", "cols"),
        P("rows", "cols"),
        P("rows", "cols"),
        P("rows", "cols"),
        P("rows", "cols"),
        P(("rows", "cols")),
        P(("rows", "cols")),
        P("rows", None, "cols"),
        P("rows", None, "cols"),
        P("rows", "cols", None),
    )
    return jax.shard_map(
        on_device, mesh=mesh, in_specs=in_specs, out_specs=out_specs, check_vma=False
    )
```

```python
import functools

import jax
import jax.numpy as jnp
from jax import lax
from jax.experimental import pallas as pl
from jax.experimental.pallas import tpu as pltpu
from jax.sharding import PartitionSpec as P

D = 1536
HEADS = 12
KV_HEADS = 2
HEAD_DIM = 128
TOP = 4
TOK_DEV = 512
BRANCHES = 4
LEAVES = 8
TRUNK = 256
BRANCH = 64

EPSILON = 1e-06
ROPE_BASE = 10000.0
MASKED = -1e30
LOW = jnp.bfloat16
WIDE = jnp.float32
KEY_WIDTH = KV_HEADS * HEAD_DIM
GROUP = HEADS // KV_HEADS
QUARTERS = 4
VMEM_LIMIT = 56 * 1024 * 1024

ANY = pl.BlockSpec(memory_space=pl.ANY)
SMEM = pl.BlockSpec(memory_space=pltpu.SMEM)


def nn(one, two):
    return lax.dot_general(one, two, (((1,), (0,)), ((), ())), preferred_element_type=WIDE)


def nt(one, two):
    return lax.dot_general(one, two, (((1,), (1,)), ((), ())), preferred_element_type=WIDE)


def tn(one, two):
    return lax.dot_general(one, two, (((0,), (0,)), ((), ())), preferred_element_type=WIDE)


def whole(shape):
    return pl.BlockSpec(shape, lambda *_: (0,) * len(shape))


LITTLE = pl.CostEstimate(flops=1, bytes_accessed=1, transcendentals=0)


def params():
    return pltpu.CompilerParams(vmem_limit_bytes=VMEM_LIMIT)


def turn(values, cosine, sine):
    return values * cosine + pltpu.roll(values, HEAD_DIM // 2, 1) * sine


def turn_back(values, cosine, sine):
    return values * cosine - pltpu.roll(values, HEAD_DIM // 2, 1) * sine


PIECES = (
    ((0, 0), (2, 0), (4, 0), (6, 0)),
    ((1, 0), (3, 0), (5, 0), (7, 0)),
    ((0, 1), (0, 2), (0, 3)),
    ((2, 1), (2, 2), (2, 3)),
    ((4, 1), (4, 2), (4, 3)),
    ((6, 1),),
    ((6, 2), (6, 3)),
    ((1, 1), (1, 2), (1, 3)),
    ((3, 1), (3, 2), (3, 3), (5, 1), (5, 2), (5, 3)),
    ((7, 1),),
    ((7, 2), (7, 3)),
)
EXTRA = 16


STEP = 768


def weight_copies(info, refs, target, sem, start, width):
    if len(refs) == 1:
        return [pltpu.make_async_copy(refs[0], target, sem)]
    depth = refs[0].shape[1] - EXTRA
    copies = []
    for ref, parts in zip(refs, PIECES):
        for at, (flip_bits, slot) in enumerate(parts):
            row = pl.multiple_of((info[0] ^ flip_bits) * depth, depth)
            col = pl.multiple_of(info[2 + slot] * width, 128)
            copies.append(
                pltpu.make_async_copy(
                    ref.at[at, pl.ds(0, depth), pl.ds(start, width)],
                    target.at[pl.ds(row, depth), pl.ds(col, width)],
                    sem,
                )
            )
    return copies


def extras_kernel(info, *rest):
    refs, (out, sem) = rest[:-2], rest[-2:]
    depth = refs[0].shape[1] - EXTRA
    copies = []
    for ref, parts in zip(refs, PIECES):
        for at, (flip_bits, slot) in enumerate(parts):
            to = (info[0] ^ flip_bits) * QUARTERS + info[2 + slot]
            copies.append(pltpu.make_async_copy(ref.at[at, pl.ds(depth, EXTRA)], out.at[to], sem))
    run_all(copies)
    wait_all(copies)


def extras(info, refs):
    return pl.pallas_call(
        extras_kernel,
        out_shape=jax.ShapeDtypeStruct((8 * QUARTERS, EXTRA, refs[0].shape[2]), LOW),
        in_specs=[SMEM] + [ANY] * len(refs),
        out_specs=pl.BlockSpec(memory_space=pltpu.VMEM),
        scratch_shapes=[pltpu.SemaphoreType.DMA],
        compiler_params=params(),
        cost_estimate=LITTLE,
        name="extra_rows",
    )(info, *refs)


def run_all(copies):
    for copy in copies:
        copy.start()


def wait_all(copies):
    for copy in copies:
        copy.wait()


def key_value_kernel(info, tokens, gain, cosine, sine, *rest):
    count = len(rest) - 4
    refs, (normed, out, weight, sem) = rest[:count], rest[count:]
    copies = weight_copies(info, refs, weight, sem, D // QUARTERS, 128)
    run_all(copies)
    values = tokens[...].astype(WIDE)
    factor = lax.rsqrt(jnp.mean(values * values, axis=-1, keepdims=True) + EPSILON)
    low = (values * factor * gain[...]).astype(LOW)
    normed[...] = low
    wait_all(copies)
    both = nn(low, weight[...])
    half = HEAD_DIM // 2
    first = lax.broadcasted_iota(jnp.int32, (TOK_DEV, HEAD_DIM), 1) < half
    for g in range(KV_HEADS):
        one = both[:, 256 * g : 256 * g + 128]
        two = both[:, 256 * g + 128 : 256 * g + 256]
        key = jnp.where(first, one, pltpu.roll(two, half, 1))
        value = jnp.where(first, pltpu.roll(one, half, 1), two)
        out[:, 128 * g : 128 * g + 128] = turn(key, cosine[...], sine[...]).astype(LOW)
        out[:, KEY_WIDTH + 128 * g : KEY_WIDTH + 128 * g + 128] = value.astype(LOW)


def key_value(info, tokens, gain, cosine, sine, refs):
    return pl.pallas_call(
        key_value_kernel,
        out_shape=(
            jax.ShapeDtypeStruct((TOK_DEV, D), LOW),
            jax.ShapeDtypeStruct((TOK_DEV, 2 * KEY_WIDTH), LOW),
        ),
        in_specs=[SMEM] + [pl.BlockSpec(memory_space=pltpu.VMEM)] * 4 + [ANY] * len(refs),
        out_specs=(pl.BlockSpec(memory_space=pltpu.VMEM),) * 2,
        scratch_shapes=[pltpu.VMEM((D, 2 * KEY_WIDTH), LOW), pltpu.SemaphoreType.DMA],
        compiler_params=params(),
        cost_estimate=LITTLE,
        name="norm_key_value",
    )(info, tokens, gain, cosine, sine, *refs)


def query_kernel(info, normed, cosine, sine, *rest):
    count = len(rest) - 3
    refs, (out, weight, sem) = rest[:count], rest[count:]

    @pl.when(pl.program_id(0) == 0)
    def _():
        copies = weight_copies(info, refs, weight, sem, 0, D // QUARTERS)
        run_all(copies)
        wait_all(copies)

    at = pl.multiple_of(pl.program_id(0) * STEP, STEP)
    lin = nn(normed[...], weight[:, pl.ds(at, STEP)])
    for h in range(STEP // HEAD_DIM):
        out[:, 128 * h : 128 * h + 128] = turn(
            lin[:, 128 * h : 128 * h + 128], cosine[...], sine[...]
        ).astype(LOW)


def query(info, normed, cosine, sine, refs):
    return pl.pallas_call(
        query_kernel,
        grid=(D // STEP,),
        out_shape=jax.ShapeDtypeStruct((TOK_DEV, D), LOW),
        in_specs=[SMEM, whole((TOK_DEV, D)), whole((TOK_DEV, 128)), whole((TOK_DEV, 128))]
        + [ANY] * len(refs),
        out_specs=pl.BlockSpec((TOK_DEV, STEP), lambda i: (0, i)),
        scratch_shapes=[pltpu.VMEM((D, D), LOW), pltpu.SemaphoreType.DMA],
        compiler_params=params(),
        cost_estimate=LITTLE,
        name="query_projection",
    )(info, normed, cosine, sine, *refs)


KEYS = TRUNK + 2 * BRANCH
CHUNKS = TOK_DEV // BRANCH


def chunk_keys(info, source, own, column, chunk):
    at = pl.multiple_of(info[6 + chunk], BRANCH)
    rows = pl.multiple_of(chunk * BRANCH, BRANCH)
    columns = slice(column, column + HEAD_DIM)
    return jnp.concatenate(
        [
            source[0:TRUNK, columns],
            source[pl.ds(at, BRANCH), columns],
            own[pl.ds(rows, BRANCH), columns],
        ],
        axis=0,
    )


def chunk_allowed(info, chunk, query_axis, shape):
    query_row = lax.broadcasted_iota(jnp.int32, shape, query_axis) & (BRANCH - 1)
    key = lax.broadcasted_iota(jnp.int32, shape, 1 - query_axis)
    leaves = info[1] == 0
    trunk = jnp.logical_and(jnp.logical_not(leaves), chunk < TRUNK // BRANCH)
    limit = jnp.where(trunk, chunk * BRANCH + query_row, TRUNK - 1)
    branch_limit = jnp.where(leaves, TRUNK + BRANCH - 1, 0)
    own_limit = jnp.where(trunk, 0, query_row + TRUNK + BRANCH)
    top = jnp.where(key < TRUNK, limit, jnp.where(key < TRUNK + BRANCH, branch_limit, own_limit))
    return key <= top


def group_rows(ref, g):
    first = g * GROUP
    return jnp.concatenate(
        [ref[:, 128 * h : 128 * h + 128] for h in range(first, first + GROUP)], axis=0
    )


def keep_source(info, partner, own, source):
    @pl.when(pl.program_id(0) == 0)
    def _():
        @pl.when(info[1] == 0)
        def _():
            source[...] = partner[...]

        @pl.when(info[1] != 0)
        def _():
            source[...] = own[...]


def attention_kernel(info, queries, own, partner, out, source):
    keep_source(info, partner, own, source)
    chunk = pl.program_id(0)
    rows = GROUP * BRANCH
    allowed = chunk_allowed(info, chunk, 0, (rows, KEYS))
    for g in range(KV_HEADS):
        keys = chunk_keys(info, source, own, 128 * g, chunk)
        values = chunk_keys(info, source, own, KEY_WIDTH + 128 * g, chunk)
        scores = nt(group_rows(queries, g), keys) * HEAD_DIM**-0.5
        scores = jnp.where(allowed, scores, MASKED)
        weights = jnp.exp(scores - jnp.max(scores, axis=1, keepdims=True))
        total = jnp.sum(weights, axis=1, keepdims=True)
        mixed = nn((weights * (1.0 / total)).astype(LOW), values).astype(LOW)
        for h in range(GROUP):
            at = (g * GROUP + h) * 128
            out[:, at : at + 128] = mixed[h * BRANCH : (h + 1) * BRANCH]


def attention(info, queries, own, partner):
    return pl.pallas_call(
        attention_kernel,
        grid=(CHUNKS,),
        out_shape=jax.ShapeDtypeStruct((TOK_DEV, D), LOW),
        in_specs=[
            SMEM,
            pl.BlockSpec((BRANCH, D), lambda i: (i, 0)),
            whole((TOK_DEV, 2 * KEY_WIDTH)),
            whole((TOK_DEV, 2 * KEY_WIDTH)),
        ],
        out_specs=pl.BlockSpec((BRANCH, D), lambda i: (i, 0)),
        scratch_shapes=[pltpu.VMEM((TOK_DEV, 2 * KEY_WIDTH), LOW)],
        compiler_params=params(),
        cost_estimate=LITTLE,
        name="tree_attention",
    )(info, queries, own, partner)


def attention_back_kernel(
    info, queries, own, partner, grads, cosine, sine, grad_query, own_grad, source_grad, source
):
    keep_source(info, partner, own, source)
    chunk = pl.program_id(0)

    @pl.when(chunk == 0)
    def _():
        source_grad[...] = jnp.zeros_like(source_grad)

    rows = GROUP * BRANCH
    scale = HEAD_DIM**-0.5
    allowed = chunk_allowed(info, chunk, 1, (KEYS, rows))
    at = pl.multiple_of(info[6 + chunk], BRANCH)
    for g in range(KV_HEADS):
        keys = chunk_keys(info, source, own, 128 * g, chunk)
        values = chunk_keys(info, source, own, KEY_WIDTH + 128 * g, chunk)
        query_rows = group_rows(queries, g)
        grad_rows = group_rows(grads, g)
        scores = jnp.where(allowed, nt(keys, query_rows) * scale, MASKED)
        weights = jnp.exp(scores - jnp.max(scores, axis=0, keepdims=True))
        probs = weights * (1.0 / jnp.sum(weights, axis=0, keepdims=True))
        grad_probs = nt(values, grad_rows)
        mean = jnp.sum(probs * grad_probs, axis=0, keepdims=True)
        grad_scores = (probs * (grad_probs - mean)).astype(LOW)
        grad_values = nn(probs.astype(LOW), grad_rows)
        grad_keys = nn(grad_scores, query_rows) * scale
        grad_queries = tn(grad_scores, keys) * scale
        for h in range(GROUP):
            to = (g * GROUP + h) * 128
            grad_query[:, to : to + 128] = turn_back(
                grad_queries[h * BRANCH : (h + 1) * BRANCH], cosine[...], sine[...]
            ).astype(LOW)
        for column, grad in ((128 * g, grad_keys), (KEY_WIDTH + 128 * g, grad_values)):
            columns = slice(column, column + 128)
            source_grad[0:TRUNK, columns] += grad[0:TRUNK]
            source_grad[pl.ds(at, BRANCH), columns] += grad[TRUNK : TRUNK + BRANCH]
            own_grad[:, columns] = grad[TRUNK + BRANCH :]


def attention_back(info, queries, own, partner, grads, cosine, sine):
    chunked = pl.BlockSpec((BRANCH, D), lambda i: (i, 0))
    pair = (TOK_DEV, 2 * KEY_WIDTH)
    return pl.pallas_call(
        attention_back_kernel,
        grid=(CHUNKS,),
        out_shape=(
            jax.ShapeDtypeStruct((TOK_DEV, D), LOW),
            jax.ShapeDtypeStruct(pair, WIDE),
            jax.ShapeDtypeStruct(pair, WIDE),
        ),
        in_specs=[
            SMEM,
            chunked,
            whole(pair),
            whole(pair),
            chunked,
            pl.BlockSpec((BRANCH, 128), lambda i: (i, 0)),
            pl.BlockSpec((BRANCH, 128), lambda i: (i, 0)),
        ],
        out_specs=(
            chunked,
            pl.BlockSpec((BRANCH, 2 * KEY_WIDTH), lambda i: (i, 0)),
            whole(pair),
        ),
        scratch_shapes=[pltpu.VMEM(pair, LOW)],
        compiler_params=params(),
        cost_estimate=LITTLE,
        name="tree_attention_back",
    )(info, queries, own, partner, grads, cosine, sine)


def out_kernel(info, heads, tokens, gain, *rest):
    count = len(rest) - 4
    refs, (residual, normed, weight, sem) = rest[:count], rest[count:]

    @pl.when(pl.program_id(0) == 0)
    def _():
        copies = weight_copies(info, refs, weight, sem, D // QUARTERS + 128, D // QUARTERS)
        run_all(copies)
        wait_all(copies)

    at = pl.ds(pl.multiple_of(pl.program_id(0) * STEP, STEP), STEP)
    residual[:, at] = tokens[:, at].astype(WIDE) + nn(heads[...], weight[:, at])

    @pl.when(pl.program_id(0) == pl.num_programs(0) - 1)
    def _():
        values = residual[...]
        factor = lax.rsqrt(jnp.mean(values * values, axis=-1, keepdims=True) + EPSILON)
        normed[...] = (values * factor * gain[...]).astype(LOW)


def out_projection(info, heads, tokens, gain, refs):
    full = (TOK_DEV, D)
    return pl.pallas_call(
        out_kernel,
        grid=(D // STEP,),
        out_shape=(jax.ShapeDtypeStruct(full, WIDE), jax.ShapeDtypeStruct(full, LOW)),
        in_specs=[SMEM, whole(full), whole(full), whole((1, D))] + [ANY] * len(refs),
        out_specs=(whole(full), whole(full)),
        scratch_shapes=[pltpu.VMEM((D, D), LOW), pltpu.SemaphoreType.DMA],
        compiler_params=params(),
        cost_estimate=LITTLE,
        name="out_projection",
    )(info, heads, tokens, gain, *refs)


def hits_of(routes, ids):
    hit = ids == routes[0, 0:1]
    for k in range(1, TOP):
        hit = jnp.logical_or(hit, ids == routes[0, k : k + 1])
    return hit


def tables_kernel(capacity, local, total, info, routes, chosen_out, place_out, earlier):
    @pl.when(pl.program_id(0) == 0)
    def _():
        one = lax.broadcasted_iota(jnp.int32, (TOK_DEV, TOK_DEV), 0)
        two = lax.broadcasted_iota(jnp.int32, (TOK_DEV, TOK_DEV), 1)
        earlier[...] = jnp.where(one < two, 1.0, 0.0).astype(LOW)

    ids = lax.broadcasted_iota(jnp.int32, (total, TOK_DEV), 0)
    hit = hits_of(routes, ids)
    rank = nn(jnp.where(hit, 1.0, 0.0).astype(LOW), earlier[...])
    place = jnp.where(hit, rank, -1.0)
    spots = lax.broadcasted_iota(jnp.int32, (capacity, TOK_DEV), 0).astype(WIDE)
    place_out[0] = jnp.full(place_out.shape[1:], -1.0, WIDE)
    for e in range(local):
        mine = ids == info[0] * local + e
        place_row = jnp.sum(jnp.where(mine, place, 0.0), axis=0, keepdims=True)
        place_out[0, e : e + 1] = place_row
        chosen_out[0, e * capacity : (e + 1) * capacity] = jnp.where(
            spots == place_row, 1.0, 0.0
        ).astype(LOW)


def tables(info, routes, capacity, local, total):
    count = routes.shape[0]
    return pl.pallas_call(
        functools.partial(tables_kernel, capacity, local, total),
        grid=(count,),
        in_specs=[SMEM, pl.BlockSpec((1, TOP, TOK_DEV), lambda i: (i, 0, 0))],
        out_specs=[
            pl.BlockSpec((1, local * capacity, TOK_DEV), lambda i: (i, 0, 0)),
            pl.BlockSpec((1, 8, TOK_DEV), lambda i: (i, 0, 0)),
        ],
        scratch_shapes=[pltpu.VMEM((TOK_DEV, TOK_DEV), LOW)],
        out_shape=[
            jax.ShapeDtypeStruct((count, local * capacity, TOK_DEV), LOW),
            jax.ShapeDtypeStruct((count, 8, TOK_DEV), WIDE),
        ],
        compiler_params=params(),
        cost_estimate=LITTLE,
        name="route_tables",
    )(info, routes)


def pick_kernel(local, count, chosen, *rest):
    blocks, outs = rest[:count], rest[count : count + local]
    picks, block_in, out_block, sem_in, sem_out = rest[count + local :]
    capacity = outs[0].shape[1]
    copies = [
        (
            pltpu.make_async_copy(chosen.at[q], picks.at[q], sem_in.at[q, 0]),
            pltpu.make_async_copy(blocks[q], block_in.at[q], sem_in.at[q, 1]),
        )
        for q in range(count)
    ]
    for pair in copies:
        run_all(pair)
    sent = []
    for q in range(count):
        wait_all(copies[q])
        out_block[q] = nn(picks[q], block_in[q]).astype(LOW)
        for e in range(local):
            copy = pltpu.make_async_copy(
                out_block.at[q, pl.ds(e * capacity, capacity)], outs[e].at[q], sem_out.at[q, e]
            )
            copy.start()
            sent.append(copy)
    wait_all(sent)


def pick_rows(chosen, blocks, local):
    count, height, _ = chosen.shape
    return pl.pallas_call(
        functools.partial(pick_kernel, local, count),
        in_specs=[ANY] * (1 + count),
        out_specs=[ANY] * local,
        out_shape=[jax.ShapeDtypeStruct((count, height // local, D), LOW)] * local,
        scratch_shapes=[
            pltpu.VMEM((count, height, TOK_DEV), LOW),
            pltpu.VMEM((count, TOK_DEV, D), LOW),
            pltpu.VMEM((count, height, D), LOW),
            pltpu.SemaphoreType.DMA((count, 2)),
            pltpu.SemaphoreType.DMA((count, local)),
        ],
        compiler_params=params(),
        cost_estimate=LITTLE,
        name="pick_rows",
    )(chosen, *blocks)


def dispatch_kernel(local, info, rows, chosen, routes, router, *rest):
    outs, logits = rest[2 * local : 4 * local], rest[-1]
    total = router.shape[1]
    step = pl.program_id(0)
    block = rows[...]
    rows_of = nn(chosen[0], block).astype(LOW)
    capacity = outs[0].shape[1]
    for e in range(local):
        outs[e][0] = rows_of[e * capacity : (e + 1) * capacity]
    part = nn(block, router[...])

    @pl.when(step == 0)
    def _():
        logits[...] = part

    @pl.when(step > 0)
    def _():
        logits[...] += part

    @pl.when(step == pl.num_programs(0) - 1)
    def _():
        values = logits[...].T
        ids = lax.broadcasted_iota(jnp.int32, (total, TOK_DEV), 0)
        weights = jnp.exp(values - jnp.max(values, axis=0, keepdims=True))
        hit = hits_of(routes, ids)
        share = weights / jnp.sum(jnp.where(hit, weights, 0.0), axis=0, keepdims=True)
        for e in range(local):
            mine = ids == info[0] * local + e
            share_row = jnp.sum(jnp.where(mine, share, 0.0), axis=0, keepdims=True)
            picked = chosen[0, e * capacity : (e + 1) * capacity].astype(WIDE)
            outs[local + e][0] = jnp.sum(picked * share_row, axis=1, keepdims=True)


def dispatch(at, info, rows, chosen, routes, router, local, earlier):
    count, height, _ = chosen.shape
    capacity = height // local
    total = router.shape[1]
    wide = D
    out_shape = [jax.ShapeDtypeStruct((count, capacity, D), LOW)] * local + [
        jax.ShapeDtypeStruct((count, capacity, 1), WIDE)
    ] * local
    if earlier is None:
        earlier = [jnp.zeros((8, 128), shape.dtype) for shape in out_shape]
        aliases = {}
    else:
        aliases = {5 + i: i for i in range(len(out_shape))}
    return pl.pallas_call(
        functools.partial(dispatch_kernel, local),
        grid=(D // wide,),
        in_specs=[
            SMEM,
            pl.BlockSpec((TOK_DEV, wide), lambda i: (0, i)),
            pl.BlockSpec((1, height, TOK_DEV), lambda i: (at, 0, 0)),
            pl.BlockSpec((1, TOP, TOK_DEV), lambda i: (at, 0, 0)),
            pl.BlockSpec((wide, total), lambda i: (i, 0)),
        ]
        + [ANY] * len(out_shape),
        out_specs=[pl.BlockSpec((1, capacity, wide), lambda i: (at, 0, i))] * local
        + [pl.BlockSpec((1, capacity, 1), lambda i: (at, 0, 0))] * local,
        scratch_shapes=[pltpu.VMEM((TOK_DEV, total), WIDE)],
        out_shape=out_shape,
        input_output_aliases=aliases,
        compiler_params=params(),
        cost_estimate=LITTLE,
        name="dispatch",
    )(info, rows, chosen, routes, router, *earlier)


def spread_kernel(local, place, *rest):
    dots, out = rest[:local], rest[local]
    spots = lax.broadcasted_iota(jnp.int32, (dots[0].shape[1], TOK_DEV), 0).astype(WIDE)
    for e in range(local):
        chosen = spots == place[0, e : e + 1]
        out[0, e : e + 1] = jnp.sum(jnp.where(chosen, dots[e][0], 0.0), axis=0, keepdims=True)


def spread(place, dots):
    count, capacity, _ = dots[0].shape
    local = len(dots)
    return pl.pallas_call(
        functools.partial(spread_kernel, local),
        grid=(count,),
        out_shape=jax.ShapeDtypeStruct((count, local, TOK_DEV), WIDE),
        in_specs=[pl.BlockSpec((1, 8, TOK_DEV), lambda i: (i, 0, 0))]
        + [pl.BlockSpec((1, capacity, 1), lambda i: (i, 0, 0))] * local,
        out_specs=pl.BlockSpec((1, local, TOK_DEV), lambda i: (i, 0, 0)),
        compiler_params=params(),
        cost_estimate=LITTLE,
        name="spread",
    )(place, *dots)


def expert_kernel(slots, info, rows, grads, shares, *rest):
    refs, (out_rows, back_rows, grad_rows, acts, dots, weight, sem) = rest[:-7], rest[-7:]
    part = weight.shape[1] // slots

    @pl.when(pl.program_id(0) == 0)
    def _():
        def copies(ref, slot):
            return [
                pltpu.make_async_copy(
                    ref.at[pl.ds(which * part, part)],
                    weight.at[which, pl.ds(pl.multiple_of(slot * part, part), part)],
                    sem,
                )
                for which in range(3)
            ]

        if len(refs) == 1:
            for slot in range(slots):
                run_all(copies(refs[0].at[slot], slot))
            for slot in range(slots):
                wait_all(copies(refs[0].at[slot], slot))
        else:
            block, second, above, below, far = refs
            low_end = info[2] == 0
            end = jnp.logical_or(low_end, info[2] == 3)
            run_all(copies(block, info[2]))
            run_all(copies(second, info[3]))

            @pl.when(low_end)
            def _():
                run_all(copies(above, info[4]))

            @pl.when(jnp.logical_not(low_end))
            def _():
                run_all(copies(below, info[4]))

            @pl.when(end)
            def _():
                run_all(copies(far, info[5]))

            @pl.when(jnp.logical_not(end))
            def _():
                run_all(copies(above, info[5]))

            for slot in range(slots):
                wait_all(copies(block, slot))

    row_block = rows[...]
    share = shares[...]
    grad_float = grads[...].astype(WIDE)
    grad_low = (share * grad_float).astype(LOW)
    grad_rows[...] = grad_low
    gate_act = nt(row_block, weight[0])
    upward = nt(row_block, weight[1])
    sigmoid = 1.0 / (1.0 + jnp.exp(-gate_act))
    silu = gate_act * sigmoid
    hidden = (silu * upward).astype(LOW)
    expert_out = nn(hidden, weight[2]).astype(LOW).astype(WIDE)
    out_rows[...] = (share * expert_out).astype(LOW)
    dots[...] = jnp.sum(grad_float * expert_out, axis=1, keepdims=True)
    grad_hidden = nt(grad_low, weight[2])
    grad_gate = (grad_hidden * upward * sigmoid * (1.0 + gate_act * (1.0 - sigmoid))).astype(LOW)
    grad_up = (grad_hidden * silu).astype(LOW)
    back_rows[...] = (nn(grad_gate, weight[0]) + nn(grad_up, weight[1])).astype(LOW)
    for which, act in enumerate((grad_gate, grad_up, hidden)):
        turned = act.T
        for slot in range(slots):
            acts[slot, which * part : (which + 1) * part] = turned[
                slot * part : (slot + 1) * part
            ]


EXPERT_ROWS = 256


def expert(info, rows, grads, shares, refs, slots):
    height = rows.shape[0]
    part = refs[0].shape[-2] // 3
    wide_block = pl.BlockSpec((EXPERT_ROWS, D), lambda i: (i, 0))
    thin_block = pl.BlockSpec((EXPERT_ROWS, 1), lambda i: (i, 0))
    return pl.pallas_call(
        functools.partial(expert_kernel, slots),
        grid=(height // EXPERT_ROWS,),
        out_shape=[jax.ShapeDtypeStruct((height, D), LOW)] * 3
        + [
            jax.ShapeDtypeStruct((slots, 3 * part, height), LOW),
            jax.ShapeDtypeStruct((height, 1), WIDE),
        ],
        in_specs=[SMEM, wide_block, wide_block, thin_block] + [ANY] * len(refs),
        out_specs=[wide_block] * 3
        + [pl.BlockSpec((slots, 3 * part, EXPERT_ROWS), lambda i: (0, 0, i)), thin_block],
        scratch_shapes=[pltpu.VMEM((3, slots * part, D), LOW), pltpu.SemaphoreType.DMA],
        compiler_params=params(),
        cost_estimate=LITTLE,
        name="expert",
    )(info, rows, grads, shares, *refs)


def expert_grads_kernel(acts, rows, grads, out):
    slots, height, _ = acts.shape
    part = height // 3
    for slot in range(slots):
        out[slot, : 2 * part] = nn(acts[slot, : 2 * part], rows[...]).astype(LOW)
        out[slot, 2 * part :] = nn(acts[slot, 2 * part :], grads[...]).astype(LOW)


def expert_grads(acts, rows, grads):
    slots, part, height = acts.shape
    strip = pl.BlockSpec((height, 256), lambda i: (0, i))
    return pl.pallas_call(
        expert_grads_kernel,
        grid=(D // 256,),
        out_shape=jax.ShapeDtypeStruct((slots, part, D), LOW),
        in_specs=[whole(acts.shape), strip, strip],
        out_specs=pl.BlockSpec((slots, part, 256), lambda i: (0, 0, i)),
        compiler_params=params(),
        cost_estimate=LITTLE,
        name="expert_gradients",
    )(acts, rows, grads)


SHARE_ROWS = 32


def combine_kernel(local, first, step, info, chosen, *rest):
    rows, dots, out = rest[:local], rest[local:-6], rest[-6]
    picks, rows_in, out_block, sem_in, sem_out = rest[-5:]
    number = out.shape[0]
    capacity = rows[0].shape[1]
    copies = []
    for n in range(number):
        q = first + step * n
        copies.append(
            [pltpu.make_async_copy(chosen.at[q], picks.at[n], sem_in.at[n, local])]
            + [
                pltpu.make_async_copy(
                    rows[e].at[q],
                    rows_in.at[n, pl.ds(e * capacity, capacity)],
                    sem_in.at[n, e],
                )
                for e in range(local)
            ]
        )
    for group in copies:
        run_all(group)
    sent = []
    for n in range(number):
        wait_all(copies[n])
        out_block[n, :TOK_DEV] = tn(picks[n], rows_in[n]).astype(LOW)
        if dots:
            row = lax.broadcasted_iota(jnp.int32, (SHARE_ROWS, D), 0)
            values = jnp.zeros((SHARE_ROWS, D), WIDE)
            for e in range(local):
                picked = picks[n, e * capacity : (e + 1) * capacity].astype(WIDE)
                share = picked * dots[e][first + step * n]
                high, low = split(jnp.sum(share, axis=0, keepdims=True))
                pieces = [high.astype(WIDE), low.astype(WIDE)]
                pieces.append(jnp.zeros((1, D - 2 * TOK_DEV), WIDE))
                line = jnp.concatenate(pieces, axis=1)
                values = jnp.where(row == info[0] * local + e, line, values)
            out_block[n, TOK_DEV:] = values.astype(LOW)
        copy = pltpu.make_async_copy(out_block.at[n], out.at[n], sem_out.at[n])
        copy.start()
        sent.append(copy)
    wait_all(sent)


def combine(info, chosen, rows, first, step, dots=()):
    count, capacity, _ = rows[0].shape
    local = len(rows)
    number = (count - first + step - 1) // step
    height = TOK_DEV + (SHARE_ROWS if dots else 0)
    return pl.pallas_call(
        functools.partial(combine_kernel, local, first, step),
        out_shape=jax.ShapeDtypeStruct((number, height, D), LOW),
        in_specs=[SMEM, ANY]
        + [ANY] * local
        + [pl.BlockSpec(memory_space=pltpu.VMEM)] * len(dots),
        out_specs=ANY,
        scratch_shapes=[
            pltpu.VMEM((number, local * capacity, TOK_DEV), LOW),
            pltpu.VMEM((number, local * capacity, D), LOW),
            pltpu.VMEM((number, height, D), LOW),
            pltpu.SemaphoreType.DMA((number, local + 1)),
            pltpu.SemaphoreType.DMA((number,)),
        ],
        compiler_params=params(),
        cost_estimate=LITTLE,
        name="combine",
    )(info, chosen, *rows, *dots)


def chip_adds_kernel(keep, got, send_x, send_y, near_x, near_y, one, two, sem_in, sem_out):
    half = send_x.shape[1]
    copies = [
        (
            pltpu.make_async_copy(keep.at[i], one.at[i], sem_in.at[i, 0]),
            pltpu.make_async_copy(got.at[i], two.at[i], sem_in.at[i, 1]),
        )
        for i in range(4)
    ]
    for pair in copies:
        run_all(pair)
    sent = []
    for i in range(4):
        wait_all(copies[i])
        one[i] = (one[i].astype(WIDE) + two[i].astype(WIDE)).astype(LOW)
        upper = (near_x, send_x)[i % 2].at[i // 2]
        lower = (near_y, send_y)[i // 2].at[i % 2]
        for part, to in enumerate((upper, lower)):
            copy = pltpu.make_async_copy(
                one.at[i, pl.ds(part * half, half)], to, sem_out.at[i, part]
            )
            copy.start()
            sent.append(copy)
    wait_all(sent)


def chip_adds(keep, got):
    _, height, width = keep.shape
    shape = jax.ShapeDtypeStruct((2, height // 2, width), LOW)
    return pl.pallas_call(
        chip_adds_kernel,
        out_shape=(shape,) * 4,
        in_specs=[ANY, ANY],
        out_specs=(ANY,) * 4,
        scratch_shapes=[
            pltpu.VMEM(keep.shape, LOW),
            pltpu.VMEM(keep.shape, LOW),
            pltpu.SemaphoreType.DMA((4, 2)),
            pltpu.SemaphoreType.DMA((4, 2)),
        ],
        compiler_params=params(),
        cost_estimate=LITTLE,
        name="chip_sums",
    )(keep, got)


def corner_adds_kernel(near_x, got_x, near_y, got_y, send_y, send_x):
    send_y[...] = (near_x[0].astype(WIDE) + got_x[0].astype(WIDE)).astype(LOW)
    send_x[...] = (near_y[0].astype(WIDE) + got_y[0].astype(WIDE)).astype(LOW)


def corner_adds(near_x, got_x, near_y, got_y):
    _, half, width = near_x.shape
    rows = half
    block = pl.BlockSpec((1, rows, width), lambda i: (1, i, 0))
    out = pl.BlockSpec((rows, width), lambda i: (i, 0))
    return pl.pallas_call(
        corner_adds_kernel,
        grid=(half // rows,),
        out_shape=(jax.ShapeDtypeStruct((half, width), LOW),) * 2,
        in_specs=[block] * 4,
        out_specs=(out, out),
        compiler_params=params(),
        cost_estimate=LITTLE,
        name="corner_sums",
    )(near_x, got_x, near_y, got_y)


def split(values):
    high = values.astype(LOW)
    return high, (values - high.astype(WIDE)).astype(LOW)


def norm_back(values, gain, grad):
    factor = lax.rsqrt(jnp.mean(values * values, axis=-1, keepdims=True) + EPSILON)
    scaled = gain * grad
    mean = jnp.mean(values * scaled, axis=-1, keepdims=True)
    grad_values = factor * scaled - values * (factor * factor * factor * mean)
    grad_gain = jnp.sum(grad * values * factor, axis=0, keepdims=True)
    return grad_values, grad_gain


def router_back(logits, routes, grad_shares):
    ids = lax.broadcasted_iota(jnp.int32, logits.shape, 0)
    hit = ids == routes[0:1]
    for k in range(1, TOP):
        hit = jnp.logical_or(hit, ids == routes[k : k + 1])
    weights = jnp.exp(logits - jnp.max(logits, axis=0, keepdims=True))
    probs = weights / jnp.sum(weights, axis=0, keepdims=True)
    chosen = jnp.sum(jnp.where(hit, probs, 0.0), axis=0, keepdims=True)
    grads = jnp.where(hit, grad_shares, 0.0)
    mean = jnp.sum(probs * grads, axis=0, keepdims=True) / chosen
    grad_probs = jnp.where(hit, (grads - mean) / chosen, 0.0)
    return probs * (grad_probs - jnp.sum(probs * grad_probs, axis=0, keepdims=True))


def branch_back_kernel(
    parts, info, residual, normed, cotangent, routes, router, gain, *rest
):
    sums, rest = rest[:parts], rest[parts:]
    experts = router.shape[0]
    count = len(rest) - 7
    refs = rest[:count]
    grad_residual, grad_branch, grad_heads, grad_gain, grad_router, weight, sem = rest[count:]

    @pl.when(pl.program_id(0) == 0)
    def _():
        copies = weight_copies(info, refs, weight, sem, D // QUARTERS + 128, D // QUARTERS)
        run_all(copies)
        logits = nt(router[...], normed[...])
        if parts == 2:
            back_sum, grad_shares = sums[0][...], sums[1][...]
        else:
            values = [
                (ref[0] if len(ref.shape) == 3 else ref[...]).astype(WIDE) for ref in sums
            ]
            upper = values[0] + values[1] + values[2]
            lower = values[3] + values[4] + values[5]
            last = lower.shape[0] - SHARE_ROWS
            shares = lower[last : last + experts]
            grad_shares = shares[:, :TOK_DEV] + shares[:, TOK_DEV : 2 * TOK_DEV]
            back_sum = jnp.concatenate([upper, lower[:last]], axis=0)
        high, low = split(router_back(logits, routes[...], grad_shares))
        grad_router[...] = nn(high, normed[...]) + nn(low, normed[...])
        grad_normed = tn(high, router[...]) + tn(low, router[...])
        grad_normed += back_sum
        grad_values, gain_grad = norm_back(residual[...], gain[...], grad_normed)
        grad_gain[...] = gain_grad
        total = cotangent[...].astype(WIDE) + grad_values
        grad_residual[...] = total
        grad_branch[...] = total.astype(LOW)
        wait_all(copies)

    at = pl.ds(pl.multiple_of(pl.program_id(0) * STEP, STEP), STEP)
    grad_heads[...] = nt(grad_branch[...], weight[at, :]).astype(LOW)


def branch_back(info, residual, normed, sums, cotangent, routes, router, gain, refs):
    full = (TOK_DEV, D)
    total = router.shape[0]
    return pl.pallas_call(
        functools.partial(branch_back_kernel, len(sums)),
        grid=(D // STEP,),
        out_shape=(
            jax.ShapeDtypeStruct(full, WIDE),
            jax.ShapeDtypeStruct(full, LOW),
            jax.ShapeDtypeStruct(full, LOW),
            jax.ShapeDtypeStruct((1, D), WIDE),
            jax.ShapeDtypeStruct((total, D), WIDE),
        ),
        in_specs=[SMEM]
        + [whole(full)] * 3
        + [whole((TOP, TOK_DEV)), whole((total, D)), whole((1, D))]
        + [whole(part.shape if part.ndim == 2 else (1,) + part.shape[1:]) for part in sums]
        + [ANY] * len(refs),
        out_specs=(
            whole(full),
            whole(full),
            pl.BlockSpec((TOK_DEV, STEP), lambda i: (0, i)),
            whole((1, D)),
            whole((total, D)),
        ),
        scratch_shapes=[pltpu.VMEM((D, D), LOW), pltpu.SemaphoreType.DMA],
        compiler_params=params(),
        cost_estimate=LITTLE,
        name="experts_norm_back",
    )(info, residual, normed, cotangent, routes, router, gain, *sums, *refs)


def join_grads_kernel(info, own_grad, source_grad, arrived, cosine, sine, out):
    half = HEAD_DIM // 2
    first = lax.broadcasted_iota(jnp.int32, (TOK_DEV, HEAD_DIM), 1) < half
    leaves = info[1] == 0

    def total(column):
        columns = slice(column, column + 128)
        extra = source_grad[:, columns] + arrived[:, columns].astype(WIDE)
        return own_grad[:, columns] + jnp.where(leaves, 0.0, extra)

    for g in range(KV_HEADS):
        key = turn_back(total(128 * g), cosine[...], sine[...])
        value = total(KEY_WIDTH + 128 * g)
        out[:, 256 * g : 256 * g + 128] = jnp.where(
            first, key, pltpu.roll(value, half, 1)
        ).astype(LOW)
        out[:, 256 * g + 128 : 256 * g + 256] = jnp.where(
            first, pltpu.roll(key, half, 1), value
        ).astype(LOW)


def join_grads(info, own_grad, source_grad, arrived, cosine, sine):
    vmem = pl.BlockSpec(memory_space=pltpu.VMEM)
    return pl.pallas_call(
        join_grads_kernel,
        out_shape=jax.ShapeDtypeStruct((TOK_DEV, 2 * KEY_WIDTH), LOW),
        in_specs=[SMEM] + [vmem] * 5,
        out_specs=vmem,
        compiler_params=params(),
        cost_estimate=LITTLE,
        name="join_key_value_gradients",
    )(info, own_grad, source_grad, arrived, cosine, sine)


def token_back_kernel(info, grad_query, grad_pair, tokens, grad_residual, gain, *rest):
    count = (len(rest) - 6) // 2
    query_refs, pair_refs = rest[:count], rest[count : 2 * count]
    out, grad_gain, query_weight, pair_weight, grad_normed, sem = rest[2 * count :]

    @pl.when(pl.program_id(0) == 0)
    def _():
        copies = weight_copies(info, query_refs, query_weight, sem, 0, D // QUARTERS)
        copies += weight_copies(info, pair_refs, pair_weight, sem, D // QUARTERS, 128)
        run_all(copies)
        wait_all(copies)

    at = pl.ds(pl.multiple_of(pl.program_id(0) * STEP, STEP), STEP)
    grad_normed[:, at] = nt(grad_query[...], query_weight[at, :]) + nt(
        grad_pair[...], pair_weight[at, :]
    )

    @pl.when(pl.program_id(0) == pl.num_programs(0) - 1)
    def _():
        grad_values, gain_grad = norm_back(
            tokens[...].astype(WIDE), gain[...], grad_normed[...]
        )
        grad_gain[...] = gain_grad
        out[...] = (grad_residual[...] + grad_values).astype(LOW)


def token_back(info, grad_query, grad_pair, tokens, grad_residual, gain, query_refs, pair_refs):
    full = (TOK_DEV, D)
    return pl.pallas_call(
        token_back_kernel,
        grid=(D // STEP,),
        out_shape=(jax.ShapeDtypeStruct(full, LOW), jax.ShapeDtypeStruct((1, D), WIDE)),
        in_specs=[
            SMEM,
            whole(full),
            whole((TOK_DEV, 2 * KEY_WIDTH)),
            whole(full),
            whole(full),
            whole((1, D)),
        ]
        + [ANY] * (len(query_refs) + len(pair_refs)),
        out_specs=(whole(full), whole((1, D))),
        scratch_shapes=[
            pltpu.VMEM((D, D), LOW),
            pltpu.VMEM((D, 2 * KEY_WIDTH), LOW),
            pltpu.VMEM(full, WIDE),
            pltpu.SemaphoreType.DMA,
        ],
        compiler_params=params(),
        cost_estimate=LITTLE,
        name="token_gradient",
    )(info, grad_query, grad_pair, tokens, grad_residual, gain, *query_refs, *pair_refs)


def weight_grads_kernel(parts, whole_rows, info, *rest):
    ins, (keep, send) = rest[:-2], rest[-2:]
    depth = D // 8
    core = info[0] & 1
    chip = pl.program_id(0) ^ (info[0] >> 1)
    for strip_at, grads_at, start, width in parts:
        low = tn(ins[strip_at][...], ins[grads_at][...]).astype(LOW)
        columns = slice(start, start + width)
        for slot in range(QUARTERS):
            for j in range(QUARTERS):

                @pl.when(info[2 + slot] == j)
                def _():
                    piece = low[:, j * width : (j + 1) * width]
                    upper, lower = piece[:depth], piece[depth:]
                    keep[0, slot, :depth, columns] = jnp.where(core == 0, upper, lower)
                    send[0, slot, :depth, columns] = jnp.where(core == 0, lower, upper)
                    if not whole_rows:
                        blank = jnp.zeros((EXTRA, width), LOW)
                        keep[0, slot, depth:, columns] = blank
                        send[0, slot, depth:, columns] = blank

    if whole_rows:
        extra = ins[-1]
        for slot in range(QUARTERS):
            to = info[2 + slot]
            keep[0, slot, depth:] = extra[(chip * 2 + core) * QUARTERS + to]
            send[0, slot, depth:] = extra[(chip * 2 + 1 - core) * QUARTERS + to]


def weight_grads(info, strips, grads, parts, extra, earlier=()):
    depth = D // 8
    strip = pl.BlockSpec((TOK_DEV, 2 * depth), lambda i, info: (0, i ^ (info[0] >> 1)))
    more = [] if extra is None else [extra]
    width = 2 * D // QUARTERS + 128
    shape = (4, QUARTERS, depth + EXTRA, width)
    if earlier:
        out = pl.BlockSpec((1, QUARTERS, depth + EXTRA, 128), lambda i, info: (i, 0, 0, 3))
    else:
        out = pl.BlockSpec((1,) + shape[1:], lambda i, info: (i, 0, 0, 0))
    inputs = [*strips, *grads, *more]

    def kernel(info, *rest):
        count = len(inputs)
        weight_grads_kernel(
            parts, extra is not None, info, *rest[:count], *rest[count + len(earlier) :]
        )

    return pl.pallas_call(
        kernel,
        grid_spec=pltpu.PrefetchScalarGridSpec(
            num_scalar_prefetch=1,
            grid=(4,),
            in_specs=[strip] * len(strips)
            + [
                pl.BlockSpec(a.shape, lambda i, info, n=a.ndim: (0,) * n)
                for a in (*grads, *more)
            ]
            + [ANY] * len(earlier),
            out_specs=(out, out),
        ),
        out_shape=(jax.ShapeDtypeStruct(shape, LOW),) * 2,
        input_output_aliases={1 + len(inputs) + i: i for i in range(len(earlier))},
        compiler_params=params(),
        cost_estimate=LITTLE,
        name="weight_gradients",
    )(info, *inputs, *earlier)


def position_of(token_index):
    branch_place = TRUNK + (token_index - TRUNK) % BRANCH
    leaf_place = TRUNK + BRANCH + (token_index - TOK_DEV) % BRANCH
    return jnp.where(
        token_index < TRUNK, token_index, jnp.where(token_index < TOK_DEV, branch_place, leaf_place)
    )


def rotary_tables(positions):
    half_dim = HEAD_DIM // 2
    frequency = ROPE_BASE ** (-jnp.arange(half_dim, dtype=jnp.float32) / half_dim)
    angles = positions.astype(jnp.float32)[:, None] * frequency[None, :]
    cosine, sine = (jnp.cos(angles), jnp.sin(angles))
    return (
        jnp.concatenate([cosine, cosine], axis=1),
        jnp.concatenate([-sine, sine], axis=1),
    )


def after(values, *earlier):
    return lax.optimization_barrier((values, earlier))[0]


def fast_mesh():
    return lax.axis_size("rows") == 8 and lax.axis_size("cols") == 4


SLOT_SHARD = ((0, 2, 1, 3), (1, 3, 0, 2), (2, 0, 1, 3), (3, 1, 2, 0))
UP = [(0, 1), (1, 2), (2, 3)]
DOWN = [(1, 0), (2, 1), (3, 2)]
FAR = [(0, 3), (3, 0)]


def send_near(block):
    return lax.ppermute(block, "cols", DOWN), lax.ppermute(block, "cols", UP)


def send_far(block):
    return lax.ppermute(block, "cols", FAR)


def send_over(block):
    return lax.ppermute(block, "cols", [(0, 2), (1, 3), (2, 0), (3, 1)])


def send_second(block, near):
    place = lax.axis_index("cols")
    above, below = near
    payload = jnp.where(place == 1, above, jnp.where(place == 2, below, block))
    return lax.ppermute(payload, "cols", [(3, 1), (1, 0), (0, 2), (2, 3)])


def slot_list(block, near, second, far):
    place = lax.axis_index("cols")
    above, below = near
    end = (place == 0) | (place == 3)
    return [
        block,
        second,
        jnp.where(place == 0, above, below),
        jnp.where(end, far, above),
    ]


def reduce_slots(slots, *earlier):
    place = lax.axis_index("cols")
    own, second, third, fourth = slots
    arrived = (
        lax.ppermute(jnp.where(place == 0, third, fourth), "cols", UP),
        lax.ppermute(third, "cols", DOWN),
        send_over(second),
        send_far(fourth),
    )
    arrived = after(arrived, *earlier)
    return own.astype(WIDE) + sum(block.astype(WIDE) for block in arrived)


def flip(block, bit):
    count = lax.axis_size("rows")
    return lax.ppermute(block, "rows", [(i, i ^ bit) for i in range(count)])


def add_low(one, two):
    return (one.astype(WIDE) + two.astype(WIDE)).astype(LOW)


def chips_second(near_x, near_y, got_x, got_y):
    for_y, for_x = corner_adds(near_x, got_x, near_y, got_y)
    return (near_x, got_x, flip(for_y, 4), near_y, got_y, flip(for_x, 2))


def send_chips(sums):
    return flip(sums[0], 2), flip(sums[1], 4)


def sum_parts(parts):
    wide = [(a[0] if a.ndim == 3 else a).astype(WIDE) for a in parts]
    if len(wide) == 1:
        return wide[0]
    return jnp.concatenate([wide[0] + wide[1] + wide[2], wide[3] + wide[4] + wide[5]], axis=0)


def on_device(
    tokens,
    query_weight,
    key_weight,
    value_weight,
    out_weight,
    router_weight,
    attention_gain,
    experts_gain,
    gate_weight,
    upward_weight,
    down_weight,
    routes,
    leaf_parent,
    cotangent,
):
    row_count = lax.axis_size("rows")
    col_count = lax.axis_size("cols")
    row_place = lax.axis_index("rows")
    col_place = lax.axis_index("cols")
    fast = fast_mesh()
    parity = lax.rem(col_place, 2)
    tree_id = lax.div(row_place * col_count + col_place, 2)
    parent_row = lax.dynamic_slice_in_dim(leaf_parent, tree_id, 1, 0)[0]
    depth, query_part = query_weight.shape
    key_part = key_weight.shape[1]
    router_part = router_weight.shape[1]
    gain_part = attention_gain.shape[0]
    expert_total = router_part * col_count
    local_experts = gate_weight.shape[0]
    capacity = TOK_DEV * TOP // expert_total * 5 // 4

    shards = (
        jnp.asarray(SLOT_SHARD, jnp.int32)[col_place]
        if fast
        else jnp.arange(4, dtype=jnp.int32)
    )
    branch_rows = jnp.where(parity == 0, TRUNK + BRANCH * parent_row, TRUNK)
    info = jnp.concatenate(
        [jnp.stack([row_place, parity]), shards, branch_rows, jnp.zeros((2,), jnp.int32)]
    ).astype(jnp.int32)

    packed = jnp.concatenate([query_weight, key_weight, value_weight, out_weight], axis=1)
    local_index = (1 - parity) * TOK_DEV + jnp.arange(TOK_DEV, dtype=jnp.int32)
    cosine, sine = rotary_tables(position_of(local_index))
    shard_blocks = [
        jnp.concatenate(
            [gate_weight[expert].T, upward_weight[expert].T, down_weight[expert]], axis=0
        )
        for expert in range(local_experts)
    ]
    expert_refs = []
    if fast:
        wide = packed.shape[1]
        gains = jnp.concatenate([attention_gain, experts_gain])[None, :]
        packed = jnp.concatenate(
            [
                packed,
                jnp.pad(router_weight.T, ((0, 0), (0, wide - depth))),
                jnp.pad(gains, ((0, 0), (0, wide - 2 * gain_part))),
                jnp.pad(routes.T.astype(LOW), ((0, 0), (0, wide - TOK_DEV))),
                jnp.zeros((EXTRA - router_part - 1 - TOP, wide), LOW),
            ],
            axis=0,
        )
        packed_near = send_near(packed)
        packed_far = send_far(packed)
        packed_second = send_over(packed)
        first_block = after(shard_blocks[0], *packed_near)
        first_near = send_near(first_block)
        first_second = send_second(first_block, first_near)
        slots = slot_list(packed, packed_near, packed_second, packed_far)
        first = packed[None]
        first_four = jnp.concatenate([first] + [flip(first, bits) for bits in (2, 4, 6)], axis=0)
        others = after(jnp.stack(slots[1:]), info, cosine, sine, first_four)
        beside, across = flip(others, 2), flip(others, 4)
        first_in, others_in = flip(first_four, 1), flip(others, 1)
        at = depth + router_part + 1
        routes_all = jnp.stack(
            [part[:, at : at + TOP, :TOK_DEV] for part in (first_four, first_in)], axis=1
        )
        routes_all = routes_all.reshape(row_count, TOP, TOK_DEV).astype(jnp.int32)
        chosen, place_rows = tables(info, routes_all, capacity, local_experts, expert_total)
        beside, across = after((beside, across), others_in, chosen, *first_near)
        corner = [flip(beside[:1], 4), flip(across[1:], 2)]
        pair_in = flip(jnp.concatenate([beside, across], axis=0), 1)
        corner_in = [flip(piece, 1) for piece in corner]
        pieces = [first_four, first_in, others, beside, across, *corner]
        pieces += [others_in, pair_in, *corner_in]
        grad_in = after(cotangent, *corner)
        grad_flips = [flip(grad_in, 2), flip(grad_in, 4)]
        query_refs = pair_refs = out_refs = pieces
        extra_rows = extras(info, pieces)
        router_all = extra_rows[:, :router_part, :depth]
        attention_scale = extra_rows[:, router_part, :gain_part]
        experts_scale = extra_rows[:, router_part, gain_part : 2 * gain_part]
    else:
        packed_all = lax.all_gather(lax.all_gather(packed, "cols", axis=0), "rows", axis=0)

        def unpack(start, width):
            part = packed_all[..., start : start + width]
            return jnp.swapaxes(part, 1, 2).reshape(row_count * depth, col_count * width)

        key_at = query_part
        query_refs = [unpack(0, query_part)]
        pair_refs = [
            jnp.concatenate(
                [
                    unpack(key_at, key_part).reshape(D, QUARTERS, -1),
                    unpack(key_at + key_part, key_part).reshape(D, QUARTERS, -1),
                ],
                axis=2,
            ).reshape(D, -1)
        ]
        out_refs = [unpack(key_at + 2 * key_part, query_part)]
        routes_all = lax.all_gather(routes.T, "rows", axis=0)
        chosen, place_rows = tables(info, routes_all, capacity, local_experts, expert_total)
        axes = ("rows", "cols")
        router_all = jnp.swapaxes(lax.all_gather(router_weight, axes, axis=0), 1, 2)
        attention_scale = lax.all_gather(attention_gain, axes, axis=0)
        experts_scale = lax.all_gather(experts_gain, axes, axis=0)

    attention_scale = attention_scale.reshape(1, D).astype(WIDE)
    experts_scale = experts_scale.reshape(1, D).astype(WIDE)
    router_rows = jnp.transpose(
        router_all.reshape(row_count, col_count, router_part, depth), (1, 2, 0, 3)
    ).reshape(expert_total, D)
    router_cols = router_rows.T
    tokens_in = after(tokens, first_second) if fast else tokens
    normed, own_pair = key_value(info, tokens_in, attention_scale, cosine, sine, pair_refs)
    pairs = [(i + 1, i) for i in range(0, col_count, 2)]
    partner = lax.ppermute(own_pair, "cols", pairs)
    queries = query(info, normed, cosine, sine, query_refs)
    if fast:
        first_far = send_far(after(first_block, partner, queries))
        expert_refs.append([first_block, first_second, *first_near, first_far])
    if fast:
        queries = after(queries, *grad_flips)
        grad_in = after(cotangent, *grad_flips)
        grad_flips.append(flip(grad_in, 6))
    heads = attention(info, queries, own_pair, partner)
    if fast:
        grad_near = [grad_in, *grad_flips]
        grad_blocks = [block for one in grad_near for block in (one, flip(one, 1))]
        heads = after(heads, *grad_blocks[1:6])
    else:
        grad_all = lax.all_gather(cotangent, "rows", axis=0)
        grad_blocks = [grad_all[q] for q in range(row_count)]
    residual, normed_two = out_projection(info, heads, tokens, experts_scale, out_refs)

    if fast:
        beside, across = flip(normed_two, 2), flip(normed_two, 4)
        beside_in = flip(after(normed_two, *grad_blocks), 1)
        later_block = after(shard_blocks[1], first_far, normed_two)
        expert_refs.append([lax.all_gather(later_block, "cols", axis=0)])
    else:
        rows_all = lax.all_gather(normed_two, "rows", axis=0)
        expert_refs = [[lax.all_gather(block, "cols", axis=0)] for block in shard_blocks]
    grad_rows = pick_rows(chosen, grad_blocks, local_experts)

    def place_block(q, block, picked):
        return dispatch(
            q, info, block, chosen, routes_all, router_cols, local_experts, picked
        )

    if fast:
        half = TOK_DEV // 2
        picked = place_block(0, normed_two, None)
        beside, across = after((beside, across), picked, *grad_rows)
        corner = [flip(beside[:half], 4), flip(across[half:], 2)]
        picked = place_block(1, beside_in, picked)
        picked = place_block(2, beside, picked)
        picked = place_block(4, across, picked)
        beside_in = flip(beside, 1)
        across_in = flip(across, 1)
        picked = place_block(3, beside_in, picked)
        picked = place_block(5, across_in, picked)
        corner = jnp.concatenate(after(corner, picked), axis=0)
        corner_in = flip(corner, 1)
        picked = place_block(6, corner, picked)
        picked = place_block(7, corner_in, picked)
    else:
        picked = None
        for q in range(row_count):
            picked = place_block(q, rows_all[q], picked)
    height = row_count * capacity
    token_rows = [a.reshape(height, D) for a in picked[:local_experts]]
    grad_rows = [a.reshape(height, D) for a in grad_rows]
    share_rows = [a.reshape(height, 1) for a in picked[local_experts:]]

    out_rows, back_rows, gate_dots, reduced = ([], [], [], [])
    for e in range(local_experts):
        rows_in = after(token_rows[e], *reduced_in) if e else token_rows[e]
        out_row, back_row, grad_row, acts, dots = expert(
            info, rows_in, grad_rows[e], share_rows[e], expert_refs[e], col_count
        )
        out_rows.append(out_row.reshape(row_count, capacity, D))
        back_rows.append(back_row.reshape(row_count, capacity, D))
        gate_dots.append(dots.reshape(row_count, capacity, 1))
        if fast and e == 1:
            got = flip(combine(info, chosen, back_rows, 1, 2, gate_dots), 1)
            back_keep = combine(info, chosen, back_rows, 0, 2, gate_dots)
            for_x, for_y, near_x, near_y = chip_adds(back_keep, got)
            acts = after(acts, for_x)
            back_flips = send_chips((for_x, for_y))
        slots = expert_grads(acts, token_rows[e], grad_row)
        reduced_in = (slots,)
        if e and fast:
            out_got = flip(combine(info, chosen, out_rows, 1, 2), 1)
            out_keep = combine(info, chosen, out_rows, 0, 2)
            back_flips = after(back_flips, slots, out_keep)
            back_parts = chips_second(near_x, near_y, *back_flips)
        else:
            reduced.append(lax.psum_scatter(slots, "cols", scatter_dimension=0, tiled=False))

    if fast:
        out_first = chip_adds(out_keep, out_got)
        back_parts = after(back_parts, out_first[0])
    else:
        spread_dots = spread(place_rows, gate_dots)
        grad_shares = lax.all_to_all(spread_dots, "rows", split_axis=0, concat_axis=0, tiled=True)

        def summed(rows):
            part = combine(info, chosen, rows, 0, 1)
            return lax.psum_scatter(part, "rows", scatter_dimension=0).astype(WIDE)

        back_parts = (summed(back_rows), grad_shares.reshape(expert_total, TOK_DEV))
        mixture = (summed(out_rows),)

    grad_residual, grad_branch, grad_heads, experts_gain_grad, router_grad = branch_back(
        info,
        residual,
        normed_two,
        back_parts,
        cotangent,
        routes.T,
        router_rows,
        experts_scale,
        out_refs,
    )
    if fast:
        out_flips = send_chips(after(out_first[:2], back_parts[2], back_parts[5]))
        slots = after(slots, reduced[0], back_parts[2])
        reduced.append(lax.psum_scatter(slots, "cols", scatter_dimension=0, tiled=False))
        router_parts = jnp.transpose(
            router_grad.astype(LOW).reshape(col_count, router_part, row_count, depth),
            (2, 0, 1, 3),
        ).reshape(row_count * col_count, router_part, depth)
        gain_rows = experts_gain_grad.astype(LOW).reshape(row_count * col_count, 1, gain_part)
        extra = jnp.concatenate(
            [
                jnp.pad(router_parts, ((0, 0), (0, 0), (0, wide - depth))),
                jnp.pad(gain_rows, ((0, 0), (0, 0), (0, wide - gain_part))),
                jnp.zeros((row_count * col_count, EXTRA - router_part - 1, wide), LOW),
            ],
            axis=1,
        )
    grad_query, own_grad, source_grad = attention_back(
        info, queries, own_pair, partner, grad_heads, cosine, sine
    )
    arrived = lax.ppermute(source_grad.astype(LOW), "cols", [(j, i) for i, j in pairs])
    if fast:
        parts = ((0, 2, 0, query_part), (1, 3, query_part + 2 * key_part, query_part))
        keep_send = weight_grads(
            info, [normed, heads], [grad_query, grad_branch], parts, extra
        )
        arrived = after(arrived, *keep_send, *out_flips)
    grad_pair = join_grads(info, own_grad, source_grad, arrived, cosine, sine)
    if fast:
        keep, send = weight_grads(
            info, [normed], [grad_pair], ((0, 1, 0, 2 * key_part),), None, keep_send
        )
        flat = (4, col_count * (depth + EXTRA), wide)
        sent = flip(send, 1)
        sent_first = chip_adds(keep.reshape(flat), sent.reshape(flat))
        sent_chips = send_chips(sent_first[:2])
        grad_pair = after(grad_pair, sent_first[0])
    tokens_grad, attention_gain_grad = token_back(
        info, grad_query, grad_pair, tokens, grad_residual, attention_scale, query_refs, pair_refs
    )

    if fast:
        sent_chips = after(sent_chips, tokens_grad)
        sent_parts = chips_second(*sent_first[2:], *sent_chips)
        near_x, near_y = out_first[2:]
        mixture = chips_second(near_x, near_y, *after(out_flips, *sent_chips))
    layer_output = (residual + sum_parts(mixture)).astype(LOW)
    part = down_weight.shape[1]
    expert_sums = [block.astype(WIDE) for block in reduced]
    gate_grad, upward_grad, down_grad = (
        jnp.stack([sums_of[which * part : (which + 1) * part] for sums_of in expert_sums])
        for which in range(3)
    )
    if fast:
        slots = sum_parts(sent_parts)
        slots = slots.reshape(col_count, depth + EXTRA, wide)
        width = query_part + 2 * key_part
        own_slots = [packed, *others]
        gain_sums = sum(
            jnp.sum(own_slots[i][:depth, :width].astype(WIDE) * slots[i, :depth, :width], axis=1)
            for i in range(4)
        )
        own_gains = lax.dynamic_slice_in_dim(attention_scale[0], row_place * depth, depth, 0)
        gain_sums = (gain_sums / own_gains).reshape(col_count, 1, gain_part)
        gain_sums = jnp.pad(
            jnp.take(gain_sums, shards, axis=0),
            ((0, 0), (depth + router_part + 1, EXTRA - router_part - 2), (0, wide - gain_part)),
        )
        slots = after((slots + gain_sums).astype(LOW), reduced[1])

        sums = reduce_slots(slots, gate_grad, upward_grad, down_grad, layer_output)
        router_sum = sums[depth : depth + router_part, :depth].T
        experts_gain_sum = sums[depth + router_part, :gain_part]
        attention_gain_sum = sums[depth + router_part + 1, :gain_part]
        sums = sums[:depth]
    else:
        full_grads = [
            tn(normed, grad_query),
            *jnp.moveaxis(tn(normed, grad_pair).reshape(D, QUARTERS, 2, -1), 2, 0),
            tn(heads, grad_branch),
        ]
        packed_grad = jnp.concatenate(
            [
                grad.astype(LOW).reshape(row_count, depth, col_count, -1)
                for grad in full_grads
            ],
            axis=3,
        )
        row_sums = lax.psum_scatter(packed_grad, "rows", scatter_dimension=0)
        sums = lax.psum_scatter(row_sums, "cols", scatter_dimension=1).astype(WIDE)
        small_grads = jnp.concatenate(
            [
                attention_gain_grad.reshape(-1, gain_part),
                experts_gain_grad.reshape(-1, gain_part),
                jnp.transpose(
                    router_grad.reshape(col_count, router_part, row_count, depth), (2, 0, 3, 1)
                ).reshape(row_count * col_count, depth * router_part),
            ],
            axis=1,
        )
        small_grads = small_grads.reshape(row_count, -1)
        small_grads = lax.all_to_all(small_grads, "rows", split_axis=0, concat_axis=0, tiled=True)
        small_grads = jnp.sum(small_grads, axis=0).reshape(col_count, -1)
        small_grads = lax.all_to_all(small_grads, "cols", split_axis=0, concat_axis=0, tiled=True)
        small_sums = jnp.sum(small_grads, axis=0)
        attention_gain_sum = small_sums[:gain_part]
        experts_gain_sum = small_sums[gain_part : 2 * gain_part]
        router_sum = small_sums[2 * gain_part :].reshape(depth, router_part)

    key_at = query_part
    value_at = key_at + key_part
    out_at = value_at + key_part
    return (
        layer_output,
        tokens_grad,
        sums[:, :key_at],
        sums[:, key_at:value_at],
        sums[:, value_at:out_at],
        sums[:, out_at:],
        router_sum,
        attention_gain_sum,
        experts_gain_sum,
        jnp.swapaxes(gate_grad, 1, 2),
        jnp.swapaxes(upward_grad, 1, 2),
        down_grad,
    )


def solution(mesh):
    in_specs = (
        P(("rows", "cols"), None),
        P("rows", "cols"),
        P("rows", "cols"),
        P("rows", "cols"),
        P("rows", "cols"),
        P("rows", "cols"),
        P(("rows", "cols")),
        P(("rows", "cols")),
        P("rows", None, "cols"),
        P("rows", None, "cols"),
        P("rows", "cols", None),
        P(("rows", "cols"), None),
        P(),
        P(("rows", "cols"), None),
    )
    out_specs = (
        P(("rows", "cols"), None),
        P(("rows", "cols"), None),
        P("rows", "cols"),
        P("rows", "cols"),
        P("rows", "cols"),
        P("rows", "cols"),
        P("rows", "cols"),
        P(("rows", "cols")),
        P(("rows", "cols")),
        P("rows", None, "cols"),
        P("rows", None, "cols"),
        P("rows", "cols", None),
    )
    return jax.shard_map(
        on_device, mesh=mesh, in_specs=in_specs, out_specs=out_specs, check_vma=False
    )
```

```python
import functools

import jax
import jax.numpy as jnp
from jax import lax
from jax.experimental import pallas as pl
from jax.experimental.pallas import tpu as pltpu
from jax.sharding import PartitionSpec as P

D = 1536
HEADS = 12
KV_HEADS = 2
HEAD_DIM = 128
TOP = 4
TOK_DEV = 512
BRANCHES = 4
LEAVES = 8
TRUNK = 256
BRANCH = 64

EPSILON = 1e-06
ROPE_BASE = 10000.0
MASKED = -1e30
LOW = jnp.bfloat16
WIDE = jnp.float32
KEY_WIDTH = KV_HEADS * HEAD_DIM
GROUP = HEADS // KV_HEADS
QUARTERS = 4
VMEM_LIMIT = 56 * 1024 * 1024

ANY = pl.BlockSpec(memory_space=pl.ANY)
SMEM = pl.BlockSpec(memory_space=pltpu.SMEM)


def nn(one, two):
    return lax.dot_general(one, two, (((1,), (0,)), ((), ())), preferred_element_type=WIDE)


def nt(one, two):
    return lax.dot_general(one, two, (((1,), (1,)), ((), ())), preferred_element_type=WIDE)


def tn(one, two):
    return lax.dot_general(one, two, (((0,), (0,)), ((), ())), preferred_element_type=WIDE)


def whole(shape):
    return pl.BlockSpec(shape, lambda *_: (0,) * len(shape))


LITTLE = pl.CostEstimate(flops=1, bytes_accessed=1, transcendentals=0)


def params():
    return pltpu.CompilerParams(vmem_limit_bytes=VMEM_LIMIT)


def turn(values, cosine, sine):
    return values * cosine + pltpu.roll(values, HEAD_DIM // 2, 1) * sine


def turn_back(values, cosine, sine):
    return values * cosine - pltpu.roll(values, HEAD_DIM // 2, 1) * sine


SLOTS = range(4)
PIECES = (
    tuple((0, slot) for slot in SLOTS),
    tuple((1, slot) for slot in SLOTS),
    tuple((2, slot) for slot in SLOTS),
    tuple((4, slot) for slot in SLOTS),
    ((6, 0), (6, 1)),
    ((6, 2), (6, 3)),
    tuple((flip_bits, slot) for flip_bits in (3, 5) for slot in SLOTS),
    ((7, 0), (7, 1)),
    ((7, 2), (7, 3)),
)
EXTRA = 16


STEP = 768


def weight_copies(info, refs, target, sem, start, width):
    if len(refs) == 1:
        return [pltpu.make_async_copy(refs[0], target, sem)]
    depth = refs[0].shape[1] - EXTRA
    copies = []
    for ref, parts in zip(refs, PIECES):
        for at, (flip_bits, slot) in enumerate(parts):
            row = pl.multiple_of((info[0] ^ flip_bits) * depth, depth)
            col = pl.multiple_of(info[2 + slot] * width, 128)
            copies.append(
                pltpu.make_async_copy(
                    ref.at[at, pl.ds(0, depth), pl.ds(start, width)],
                    target.at[pl.ds(row, depth), pl.ds(col, width)],
                    sem,
                )
            )
    return copies


def extras_kernel(info, *rest):
    refs, (out, sem) = rest[:-2], rest[-2:]
    depth = refs[0].shape[1] - EXTRA
    copies = []
    for ref, parts in zip(refs, PIECES):
        for at, (flip_bits, slot) in enumerate(parts):
            to = (info[0] ^ flip_bits) * QUARTERS + info[2 + slot]
            copies.append(pltpu.make_async_copy(ref.at[at, pl.ds(depth, EXTRA)], out.at[to], sem))
    run_all(copies)
    wait_all(copies)


def extras(info, refs):
    return pl.pallas_call(
        extras_kernel,
        out_shape=jax.ShapeDtypeStruct((8 * QUARTERS, EXTRA, refs[0].shape[2]), LOW),
        in_specs=[SMEM] + [ANY] * len(refs),
        out_specs=pl.BlockSpec(memory_space=pltpu.VMEM),
        scratch_shapes=[pltpu.SemaphoreType.DMA],
        compiler_params=params(),
        cost_estimate=LITTLE,
        name="extra_rows",
    )(info, *refs)


def run_all(copies):
    for copy in copies:
        copy.start()


def wait_all(copies):
    for copy in copies:
        copy.wait()


def key_value_kernel(info, tokens, gain, cosine, sine, *rest):
    count = len(rest) - 4
    refs, (normed, out, weight, sem) = rest[:count], rest[count:]
    copies = weight_copies(info, refs, weight, sem, D // QUARTERS, 128)
    run_all(copies)
    values = tokens[...].astype(WIDE)
    factor = lax.rsqrt(jnp.mean(values * values, axis=-1, keepdims=True) + EPSILON)
    low = (values * factor * gain[...]).astype(LOW)
    normed[...] = low
    wait_all(copies)
    both = nn(low, weight[...])
    half = HEAD_DIM // 2
    first = lax.broadcasted_iota(jnp.int32, (TOK_DEV, HEAD_DIM), 1) < half
    for g in range(KV_HEADS):
        one = both[:, 256 * g : 256 * g + 128]
        two = both[:, 256 * g + 128 : 256 * g + 256]
        key = jnp.where(first, one, pltpu.roll(two, half, 1))
        value = jnp.where(first, pltpu.roll(one, half, 1), two)
        out[:, 128 * g : 128 * g + 128] = turn(key, cosine[...], sine[...]).astype(LOW)
        out[:, KEY_WIDTH + 128 * g : KEY_WIDTH + 128 * g + 128] = value.astype(LOW)


def key_value(info, tokens, gain, cosine, sine, refs):
    return pl.pallas_call(
        key_value_kernel,
        out_shape=(
            jax.ShapeDtypeStruct((TOK_DEV, D), LOW),
            jax.ShapeDtypeStruct((TOK_DEV, 2 * KEY_WIDTH), LOW),
        ),
        in_specs=[SMEM] + [pl.BlockSpec(memory_space=pltpu.VMEM)] * 4 + [ANY] * len(refs),
        out_specs=(pl.BlockSpec(memory_space=pltpu.VMEM),) * 2,
        scratch_shapes=[pltpu.VMEM((D, 2 * KEY_WIDTH), LOW), pltpu.SemaphoreType.DMA],
        compiler_params=params(),
        cost_estimate=LITTLE,
        name="norm_key_value",
    )(info, tokens, gain, cosine, sine, *refs)


def query_kernel(info, normed, cosine, sine, *rest):
    count = len(rest) - 3
    refs, (out, weight, sem) = rest[:count], rest[count:]

    @pl.when(pl.program_id(0) == 0)
    def _():
        copies = weight_copies(info, refs, weight, sem, 0, D // QUARTERS)
        run_all(copies)
        wait_all(copies)

    at = pl.multiple_of(pl.program_id(0) * STEP, STEP)
    lin = nn(normed[...], weight[:, pl.ds(at, STEP)])
    for h in range(STEP // HEAD_DIM):
        out[:, 128 * h : 128 * h + 128] = turn(
            lin[:, 128 * h : 128 * h + 128], cosine[...], sine[...]
        ).astype(LOW)


def query(info, normed, cosine, sine, refs):
    return pl.pallas_call(
        query_kernel,
        grid=(D // STEP,),
        out_shape=jax.ShapeDtypeStruct((TOK_DEV, D), LOW),
        in_specs=[SMEM, whole((TOK_DEV, D)), whole((TOK_DEV, 128)), whole((TOK_DEV, 128))]
        + [ANY] * len(refs),
        out_specs=pl.BlockSpec((TOK_DEV, STEP), lambda i: (0, i)),
        scratch_shapes=[pltpu.VMEM((D, D), LOW), pltpu.SemaphoreType.DMA],
        compiler_params=params(),
        cost_estimate=LITTLE,
        name="query_projection",
    )(info, normed, cosine, sine, *refs)


KEYS = TRUNK + 2 * BRANCH
CHUNKS = TOK_DEV // BRANCH


def chunk_keys(info, source, own, column, chunk):
    at = pl.multiple_of(info[6 + chunk], BRANCH)
    rows = pl.multiple_of(chunk * BRANCH, BRANCH)
    columns = slice(column, column + HEAD_DIM)
    return jnp.concatenate(
        [
            source[0:TRUNK, columns],
            source[pl.ds(at, BRANCH), columns],
            own[pl.ds(rows, BRANCH), columns],
        ],
        axis=0,
    )


def chunk_allowed(info, chunk, query_axis, shape):
    query_row = lax.broadcasted_iota(jnp.int32, shape, query_axis) & (BRANCH - 1)
    key = lax.broadcasted_iota(jnp.int32, shape, 1 - query_axis)
    leaves = info[1] == 0
    trunk = jnp.logical_and(jnp.logical_not(leaves), chunk < TRUNK // BRANCH)
    limit = jnp.where(trunk, chunk * BRANCH + query_row, TRUNK - 1)
    branch_limit = jnp.where(leaves, TRUNK + BRANCH - 1, 0)
    own_limit = jnp.where(trunk, 0, query_row + TRUNK + BRANCH)
    top = jnp.where(key < TRUNK, limit, jnp.where(key < TRUNK + BRANCH, branch_limit, own_limit))
    return key <= top


def group_rows(ref, g):
    first = g * GROUP
    return jnp.concatenate(
        [ref[:, 128 * h : 128 * h + 128] for h in range(first, first + GROUP)], axis=0
    )


def keep_source(info, partner, own, source):
    @pl.when(pl.program_id(0) == 0)
    def _():
        @pl.when(info[1] == 0)
        def _():
            source[...] = partner[...]

        @pl.when(info[1] != 0)
        def _():
            source[...] = own[...]


def attention_kernel(info, queries, own, partner, out, source):
    keep_source(info, partner, own, source)
    chunk = pl.program_id(0)
    rows = GROUP * BRANCH
    allowed = chunk_allowed(info, chunk, 0, (rows, KEYS))
    for g in range(KV_HEADS):
        keys = chunk_keys(info, source, own, 128 * g, chunk)
        values = chunk_keys(info, source, own, KEY_WIDTH + 128 * g, chunk)
        scores = nt(group_rows(queries, g), keys) * HEAD_DIM**-0.5
        scores = jnp.where(allowed, scores, MASKED)
        weights = jnp.exp(scores - jnp.max(scores, axis=1, keepdims=True))
        total = jnp.sum(weights, axis=1, keepdims=True)
        mixed = nn((weights * (1.0 / total)).astype(LOW), values).astype(LOW)
        for h in range(GROUP):
            at = (g * GROUP + h) * 128
            out[:, at : at + 128] = mixed[h * BRANCH : (h + 1) * BRANCH]


def attention(info, queries, own, partner):
    return pl.pallas_call(
        attention_kernel,
        grid=(CHUNKS,),
        out_shape=jax.ShapeDtypeStruct((TOK_DEV, D), LOW),
        in_specs=[
            SMEM,
            pl.BlockSpec((BRANCH, D), lambda i: (i, 0)),
            whole((TOK_DEV, 2 * KEY_WIDTH)),
            whole((TOK_DEV, 2 * KEY_WIDTH)),
        ],
        out_specs=pl.BlockSpec((BRANCH, D), lambda i: (i, 0)),
        scratch_shapes=[pltpu.VMEM((TOK_DEV, 2 * KEY_WIDTH), LOW)],
        compiler_params=params(),
        cost_estimate=LITTLE,
        name="tree_attention",
    )(info, queries, own, partner)


def attention_back_kernel(
    info, queries, own, partner, grads, cosine, sine, grad_query, own_grad, source_grad, source
):
    keep_source(info, partner, own, source)
    chunk = pl.program_id(0)

    @pl.when(chunk == 0)
    def _():
        source_grad[...] = jnp.zeros_like(source_grad)

    rows = GROUP * BRANCH
    scale = HEAD_DIM**-0.5
    allowed = chunk_allowed(info, chunk, 1, (KEYS, rows))
    at = pl.multiple_of(info[6 + chunk], BRANCH)
    for g in range(KV_HEADS):
        keys = chunk_keys(info, source, own, 128 * g, chunk)
        values = chunk_keys(info, source, own, KEY_WIDTH + 128 * g, chunk)
        query_rows = group_rows(queries, g)
        grad_rows = group_rows(grads, g)
        scores = jnp.where(allowed, nt(keys, query_rows) * scale, MASKED)
        weights = jnp.exp(scores - jnp.max(scores, axis=0, keepdims=True))
        probs = weights * (1.0 / jnp.sum(weights, axis=0, keepdims=True))
        grad_probs = nt(values, grad_rows)
        mean = jnp.sum(probs * grad_probs, axis=0, keepdims=True)
        grad_scores = (probs * (grad_probs - mean)).astype(LOW)
        grad_values = nn(probs.astype(LOW), grad_rows)
        grad_keys = nn(grad_scores, query_rows) * scale
        grad_queries = tn(grad_scores, keys) * scale
        for h in range(GROUP):
            to = (g * GROUP + h) * 128
            grad_query[:, to : to + 128] = turn_back(
                grad_queries[h * BRANCH : (h + 1) * BRANCH], cosine[...], sine[...]
            ).astype(LOW)
        for column, grad in ((128 * g, grad_keys), (KEY_WIDTH + 128 * g, grad_values)):
            columns = slice(column, column + 128)
            source_grad[0:TRUNK, columns] += grad[0:TRUNK]
            source_grad[pl.ds(at, BRANCH), columns] += grad[TRUNK : TRUNK + BRANCH]
            own_grad[:, columns] = grad[TRUNK + BRANCH :]


def attention_back(info, queries, own, partner, grads, cosine, sine):
    chunked = pl.BlockSpec((BRANCH, D), lambda i: (i, 0))
    pair = (TOK_DEV, 2 * KEY_WIDTH)
    return pl.pallas_call(
        attention_back_kernel,
        grid=(CHUNKS,),
        out_shape=(
            jax.ShapeDtypeStruct((TOK_DEV, D), LOW),
            jax.ShapeDtypeStruct(pair, WIDE),
            jax.ShapeDtypeStruct(pair, WIDE),
        ),
        in_specs=[
            SMEM,
            chunked,
            whole(pair),
            whole(pair),
            chunked,
            pl.BlockSpec((BRANCH, 128), lambda i: (i, 0)),
            pl.BlockSpec((BRANCH, 128), lambda i: (i, 0)),
        ],
        out_specs=(
            chunked,
            pl.BlockSpec((BRANCH, 2 * KEY_WIDTH), lambda i: (i, 0)),
            whole(pair),
        ),
        scratch_shapes=[pltpu.VMEM(pair, LOW)],
        compiler_params=params(),
        cost_estimate=LITTLE,
        name="tree_attention_back",
    )(info, queries, own, partner, grads, cosine, sine)


def out_kernel(info, heads, tokens, gain, *rest):
    count = len(rest) - 4
    refs, (residual, normed, weight, sem) = rest[:count], rest[count:]

    @pl.when(pl.program_id(0) == 0)
    def _():
        copies = weight_copies(info, refs, weight, sem, D // QUARTERS + 128, D // QUARTERS)
        run_all(copies)
        wait_all(copies)

    at = pl.ds(pl.multiple_of(pl.program_id(0) * STEP, STEP), STEP)
    residual[:, at] = tokens[:, at].astype(WIDE) + nn(heads[...], weight[:, at])

    @pl.when(pl.program_id(0) == pl.num_programs(0) - 1)
    def _():
        values = residual[...]
        factor = lax.rsqrt(jnp.mean(values * values, axis=-1, keepdims=True) + EPSILON)
        normed[...] = (values * factor * gain[...]).astype(LOW)


def out_projection(info, heads, tokens, gain, refs):
    full = (TOK_DEV, D)
    return pl.pallas_call(
        out_kernel,
        grid=(D // STEP,),
        out_shape=(jax.ShapeDtypeStruct(full, WIDE), jax.ShapeDtypeStruct(full, LOW)),
        in_specs=[SMEM, whole(full), whole(full), whole((1, D))] + [ANY] * len(refs),
        out_specs=(whole(full), whole(full)),
        scratch_shapes=[pltpu.VMEM((D, D), LOW), pltpu.SemaphoreType.DMA],
        compiler_params=params(),
        cost_estimate=LITTLE,
        name="out_projection",
    )(info, heads, tokens, gain, *refs)


def hits_of(routes, ids):
    hit = ids == routes[0, 0:1]
    for k in range(1, TOP):
        hit = jnp.logical_or(hit, ids == routes[0, k : k + 1])
    return hit


def tables_kernel(capacity, local, total, info, routes, chosen_out, place_out, earlier):
    @pl.when(pl.program_id(0) == 0)
    def _():
        one = lax.broadcasted_iota(jnp.int32, (TOK_DEV, TOK_DEV), 0)
        two = lax.broadcasted_iota(jnp.int32, (TOK_DEV, TOK_DEV), 1)
        earlier[...] = jnp.where(one < two, 1.0, 0.0).astype(LOW)

    ids = lax.broadcasted_iota(jnp.int32, (total, TOK_DEV), 0)
    hit = hits_of(routes, ids)
    rank = nn(jnp.where(hit, 1.0, 0.0).astype(LOW), earlier[...])
    place = jnp.where(hit, rank, -1.0)
    spots = lax.broadcasted_iota(jnp.int32, (capacity, TOK_DEV), 0).astype(WIDE)
    place_out[0] = jnp.full(place_out.shape[1:], -1.0, WIDE)
    for e in range(local):
        mine = ids == info[0] * local + e
        place_row = jnp.sum(jnp.where(mine, place, 0.0), axis=0, keepdims=True)
        place_out[0, e : e + 1] = place_row
        chosen_out[0, e * capacity : (e + 1) * capacity] = jnp.where(
            spots == place_row, 1.0, 0.0
        ).astype(LOW)


def tables(info, routes, capacity, local, total):
    count = routes.shape[0]
    return pl.pallas_call(
        functools.partial(tables_kernel, capacity, local, total),
        grid=(count,),
        in_specs=[SMEM, pl.BlockSpec((1, TOP, TOK_DEV), lambda i: (i, 0, 0))],
        out_specs=[
            pl.BlockSpec((1, local * capacity, TOK_DEV), lambda i: (i, 0, 0)),
            pl.BlockSpec((1, 8, TOK_DEV), lambda i: (i, 0, 0)),
        ],
        scratch_shapes=[pltpu.VMEM((TOK_DEV, TOK_DEV), LOW)],
        out_shape=[
            jax.ShapeDtypeStruct((count, local * capacity, TOK_DEV), LOW),
            jax.ShapeDtypeStruct((count, 8, TOK_DEV), WIDE),
        ],
        compiler_params=params(),
        cost_estimate=LITTLE,
        name="route_tables",
    )(info, routes)


def pick_kernel(local, count, chosen, *rest):
    blocks, outs = rest[:count], rest[count : count + local]
    picks, block_in, out_block, sem_in, sem_out = rest[count + local :]
    capacity = outs[0].shape[1]
    copies = [
        (
            pltpu.make_async_copy(chosen.at[q], picks.at[q], sem_in.at[q, 0]),
            pltpu.make_async_copy(blocks[q], block_in.at[q], sem_in.at[q, 1]),
        )
        for q in range(count)
    ]
    for pair in copies:
        run_all(pair)
    sent = []
    for q in range(count):
        wait_all(copies[q])
        out_block[q] = nn(picks[q], block_in[q]).astype(LOW)
        for e in range(local):
            copy = pltpu.make_async_copy(
                out_block.at[q, pl.ds(e * capacity, capacity)], outs[e].at[q], sem_out.at[q, e]
            )
            copy.start()
            sent.append(copy)
    wait_all(sent)


def pick_rows(chosen, blocks, local):
    count, height, _ = chosen.shape
    return pl.pallas_call(
        functools.partial(pick_kernel, local, count),
        in_specs=[ANY] * (1 + count),
        out_specs=[ANY] * local,
        out_shape=[jax.ShapeDtypeStruct((count, height // local, D), LOW)] * local,
        scratch_shapes=[
            pltpu.VMEM((count, height, TOK_DEV), LOW),
            pltpu.VMEM((count, TOK_DEV, D), LOW),
            pltpu.VMEM((count, height, D), LOW),
            pltpu.SemaphoreType.DMA((count, 2)),
            pltpu.SemaphoreType.DMA((count, local)),
        ],
        compiler_params=params(),
        cost_estimate=LITTLE,
        name="pick_rows",
    )(chosen, *blocks)


def dispatch_kernel(local, info, rows, chosen, routes, router, *rest):
    outs, logits = rest[2 * local : 4 * local], rest[-1]
    total = router.shape[1]
    step = pl.program_id(0)
    block = rows[...]
    rows_of = nn(chosen[0], block).astype(LOW)
    capacity = outs[0].shape[1]
    for e in range(local):
        outs[e][0] = rows_of[e * capacity : (e + 1) * capacity]
    part = nn(block, router[...])

    @pl.when(step == 0)
    def _():
        logits[...] = part

    @pl.when(step > 0)
    def _():
        logits[...] += part

    @pl.when(step == pl.num_programs(0) - 1)
    def _():
        values = logits[...].T
        ids = lax.broadcasted_iota(jnp.int32, (total, TOK_DEV), 0)
        weights = jnp.exp(values - jnp.max(values, axis=0, keepdims=True))
        hit = hits_of(routes, ids)
        share = weights / jnp.sum(jnp.where(hit, weights, 0.0), axis=0, keepdims=True)
        for e in range(local):
            mine = ids == info[0] * local + e
            share_row = jnp.sum(jnp.where(mine, share, 0.0), axis=0, keepdims=True)
            picked = chosen[0, e * capacity : (e + 1) * capacity].astype(WIDE)
            outs[local + e][0] = jnp.sum(picked * share_row, axis=1, keepdims=True)


def dispatch(at, info, rows, chosen, routes, router, local, earlier):
    count, height, _ = chosen.shape
    capacity = height // local
    total = router.shape[1]
    wide = D
    out_shape = [jax.ShapeDtypeStruct((count, capacity, D), LOW)] * local + [
        jax.ShapeDtypeStruct((count, capacity, 1), WIDE)
    ] * local
    if earlier is None:
        earlier = [jnp.zeros((8, 128), shape.dtype) for shape in out_shape]
        aliases = {}
    else:
        aliases = {5 + i: i for i in range(len(out_shape))}
    return pl.pallas_call(
        functools.partial(dispatch_kernel, local),
        grid=(D // wide,),
        in_specs=[
            SMEM,
            pl.BlockSpec((TOK_DEV, wide), lambda i: (0, i)),
            pl.BlockSpec((1, height, TOK_DEV), lambda i: (at, 0, 0)),
            pl.BlockSpec((1, TOP, TOK_DEV), lambda i: (at, 0, 0)),
            pl.BlockSpec((wide, total), lambda i: (i, 0)),
        ]
        + [ANY] * len(out_shape),
        out_specs=[pl.BlockSpec((1, capacity, wide), lambda i: (at, 0, i))] * local
        + [pl.BlockSpec((1, capacity, 1), lambda i: (at, 0, 0))] * local,
        scratch_shapes=[pltpu.VMEM((TOK_DEV, total), WIDE)],
        out_shape=out_shape,
        input_output_aliases=aliases,
        compiler_params=params(),
        cost_estimate=LITTLE,
        name="dispatch",
    )(info, rows, chosen, routes, router, *earlier)


def spread_kernel(local, place, *rest):
    dots, out = rest[:local], rest[local]
    spots = lax.broadcasted_iota(jnp.int32, (dots[0].shape[1], TOK_DEV), 0).astype(WIDE)
    for e in range(local):
        chosen = spots == place[0, e : e + 1]
        out[0, e : e + 1] = jnp.sum(jnp.where(chosen, dots[e][0], 0.0), axis=0, keepdims=True)


def spread(place, dots):
    count, capacity, _ = dots[0].shape
    local = len(dots)
    return pl.pallas_call(
        functools.partial(spread_kernel, local),
        grid=(count,),
        out_shape=jax.ShapeDtypeStruct((count, local, TOK_DEV), WIDE),
        in_specs=[pl.BlockSpec((1, 8, TOK_DEV), lambda i: (i, 0, 0))]
        + [pl.BlockSpec((1, capacity, 1), lambda i: (i, 0, 0))] * local,
        out_specs=pl.BlockSpec((1, local, TOK_DEV), lambda i: (i, 0, 0)),
        compiler_params=params(),
        cost_estimate=LITTLE,
        name="spread",
    )(place, *dots)


def expert_kernel(slots, info, rows, grads, shares, *rest):
    refs, (out_rows, back_rows, grad_rows, acts, dots, weight, sem) = rest[:-7], rest[-7:]
    part = weight.shape[1] // slots

    @pl.when(pl.program_id(0) == 0)
    def _():
        def copies(ref, slot):
            return [
                pltpu.make_async_copy(
                    ref.at[pl.ds(which * part, part)],
                    weight.at[which, pl.ds(pl.multiple_of(slot * part, part), part)],
                    sem,
                )
                for which in range(3)
            ]

        if len(refs) == 1:
            for slot in range(slots):
                run_all(copies(refs[0].at[slot], slot))
            for slot in range(slots):
                wait_all(copies(refs[0].at[slot], slot))
        else:
            block, second, above, below, far = refs
            low_end = info[2] == 0
            end = jnp.logical_or(low_end, info[2] == 3)
            run_all(copies(block, info[2]))
            run_all(copies(second, info[3]))

            @pl.when(low_end)
            def _():
                run_all(copies(above, info[4]))

            @pl.when(jnp.logical_not(low_end))
            def _():
                run_all(copies(below, info[4]))

            @pl.when(end)
            def _():
                run_all(copies(far, info[5]))

            @pl.when(jnp.logical_not(end))
            def _():
                run_all(copies(above, info[5]))

            for slot in range(slots):
                wait_all(copies(block, slot))

    row_block = rows[...]
    share = shares[...]
    grad_float = grads[...].astype(WIDE)
    grad_low = (share * grad_float).astype(LOW)
    grad_rows[...] = grad_low
    gate_act = nt(row_block, weight[0])
    upward = nt(row_block, weight[1])
    sigmoid = 1.0 / (1.0 + jnp.exp(-gate_act))
    silu = gate_act * sigmoid
    hidden = (silu * upward).astype(LOW)
    expert_out = nn(hidden, weight[2]).astype(LOW).astype(WIDE)
    out_rows[...] = (share * expert_out).astype(LOW)
    dots[...] = jnp.sum(grad_float * expert_out, axis=1, keepdims=True)
    grad_hidden = nt(grad_low, weight[2])
    grad_gate = (grad_hidden * upward * sigmoid * (1.0 + gate_act * (1.0 - sigmoid))).astype(LOW)
    grad_up = (grad_hidden * silu).astype(LOW)
    back_rows[...] = (nn(grad_gate, weight[0]) + nn(grad_up, weight[1])).astype(LOW)
    for which, act in enumerate((grad_gate, grad_up, hidden)):
        turned = act.T
        for slot in range(slots):
            acts[slot, which * part : (which + 1) * part] = turned[
                slot * part : (slot + 1) * part
            ]


EXPERT_ROWS = 256


def expert(info, rows, grads, shares, refs, slots):
    height = rows.shape[0]
    part = refs[0].shape[-2] // 3
    wide_block = pl.BlockSpec((EXPERT_ROWS, D), lambda i: (i, 0))
    thin_block = pl.BlockSpec((EXPERT_ROWS, 1), lambda i: (i, 0))
    return pl.pallas_call(
        functools.partial(expert_kernel, slots),
        grid=(height // EXPERT_ROWS,),
        out_shape=[jax.ShapeDtypeStruct((height, D), LOW)] * 3
        + [
            jax.ShapeDtypeStruct((slots, 3 * part, height), LOW),
            jax.ShapeDtypeStruct((height, 1), WIDE),
        ],
        in_specs=[SMEM, wide_block, wide_block, thin_block] + [ANY] * len(refs),
        out_specs=[wide_block] * 3
        + [pl.BlockSpec((slots, 3 * part, EXPERT_ROWS), lambda i: (0, 0, i)), thin_block],
        scratch_shapes=[pltpu.VMEM((3, slots * part, D), LOW), pltpu.SemaphoreType.DMA],
        compiler_params=params(),
        cost_estimate=LITTLE,
        name="expert",
    )(info, rows, grads, shares, *refs)


def expert_grads_kernel(acts, rows, grads, out):
    slots, height, _ = acts.shape
    part = height // 3
    for slot in range(slots):
        out[slot, : 2 * part] = nn(acts[slot, : 2 * part], rows[...]).astype(LOW)
        out[slot, 2 * part :] = nn(acts[slot, 2 * part :], grads[...]).astype(LOW)


def expert_grads(acts, rows, grads):
    slots, part, height = acts.shape
    strip = pl.BlockSpec((height, 256), lambda i: (0, i))
    return pl.pallas_call(
        expert_grads_kernel,
        grid=(D // 256,),
        out_shape=jax.ShapeDtypeStruct((slots, part, D), LOW),
        in_specs=[whole(acts.shape), strip, strip],
        out_specs=pl.BlockSpec((slots, part, 256), lambda i: (0, 0, i)),
        compiler_params=params(),
        cost_estimate=LITTLE,
        name="expert_gradients",
    )(acts, rows, grads)


SHARE_ROWS = 32


def combine_kernel(local, first, step, info, chosen, *rest):
    rows, dots, out = rest[:local], rest[local:-6], rest[-6]
    picks, rows_in, out_block, sem_in, sem_out = rest[-5:]
    number = out.shape[0]
    capacity = rows[0].shape[1]
    copies = []
    for n in range(number):
        q = first + step * n
        copies.append(
            [pltpu.make_async_copy(chosen.at[q], picks.at[n], sem_in.at[n, local])]
            + [
                pltpu.make_async_copy(
                    rows[e].at[q],
                    rows_in.at[n, pl.ds(e * capacity, capacity)],
                    sem_in.at[n, e],
                )
                for e in range(local)
            ]
        )
    for group in copies:
        run_all(group)
    sent = []
    for n in range(number):
        wait_all(copies[n])
        out_block[n, :TOK_DEV] = tn(picks[n], rows_in[n]).astype(LOW)
        if dots:
            row = lax.broadcasted_iota(jnp.int32, (SHARE_ROWS, D), 0)
            values = jnp.zeros((SHARE_ROWS, D), WIDE)
            for e in range(local):
                picked = picks[n, e * capacity : (e + 1) * capacity].astype(WIDE)
                share = picked * dots[e][first + step * n]
                high, low = split(jnp.sum(share, axis=0, keepdims=True))
                pieces = [high.astype(WIDE), low.astype(WIDE)]
                pieces.append(jnp.zeros((1, D - 2 * TOK_DEV), WIDE))
                line = jnp.concatenate(pieces, axis=1)
                values = jnp.where(row == info[0] * local + e, line, values)
            out_block[n, TOK_DEV:] = values.astype(LOW)
        copy = pltpu.make_async_copy(out_block.at[n], out.at[n], sem_out.at[n])
        copy.start()
        sent.append(copy)
    wait_all(sent)


def combine(info, chosen, rows, first, step, dots=()):
    count, capacity, _ = rows[0].shape
    local = len(rows)
    number = (count - first + step - 1) // step
    height = TOK_DEV + (SHARE_ROWS if dots else 0)
    return pl.pallas_call(
        functools.partial(combine_kernel, local, first, step),
        out_shape=jax.ShapeDtypeStruct((number, height, D), LOW),
        in_specs=[SMEM, ANY]
        + [ANY] * local
        + [pl.BlockSpec(memory_space=pltpu.VMEM)] * len(dots),
        out_specs=ANY,
        scratch_shapes=[
            pltpu.VMEM((number, local * capacity, TOK_DEV), LOW),
            pltpu.VMEM((number, local * capacity, D), LOW),
            pltpu.VMEM((number, height, D), LOW),
            pltpu.SemaphoreType.DMA((number, local + 1)),
            pltpu.SemaphoreType.DMA((number,)),
        ],
        compiler_params=params(),
        cost_estimate=LITTLE,
        name="combine",
    )(info, chosen, *rows, *dots)


def chip_adds_kernel(keep, got, send_x, send_y, near_x, near_y, one, two, sem_in, sem_out):
    half = send_x.shape[1]
    copies = [
        (
            pltpu.make_async_copy(keep.at[i], one.at[i], sem_in.at[i, 0]),
            pltpu.make_async_copy(got.at[i], two.at[i], sem_in.at[i, 1]),
        )
        for i in range(4)
    ]
    for pair in copies:
        run_all(pair)
    sent = []
    for i in range(4):
        wait_all(copies[i])
        one[i] = (one[i].astype(WIDE) + two[i].astype(WIDE)).astype(LOW)
        upper = (near_x, send_x)[i % 2].at[i // 2]
        lower = (near_y, send_y)[i // 2].at[i % 2]
        for part, to in enumerate((upper, lower)):
            copy = pltpu.make_async_copy(
                one.at[i, pl.ds(part * half, half)], to, sem_out.at[i, part]
            )
            copy.start()
            sent.append(copy)
    wait_all(sent)


def chip_adds(keep, got):
    _, height, width = keep.shape
    shape = jax.ShapeDtypeStruct((2, height // 2, width), LOW)
    return pl.pallas_call(
        chip_adds_kernel,
        out_shape=(shape,) * 4,
        in_specs=[ANY, ANY],
        out_specs=(ANY,) * 4,
        scratch_shapes=[
            pltpu.VMEM(keep.shape, LOW),
            pltpu.VMEM(keep.shape, LOW),
            pltpu.SemaphoreType.DMA((4, 2)),
            pltpu.SemaphoreType.DMA((4, 2)),
        ],
        compiler_params=params(),
        cost_estimate=LITTLE,
        name="chip_sums",
    )(keep, got)


def corner_adds_kernel(near_x, got_x, near_y, got_y, send_y, send_x):
    send_y[...] = (near_x[0].astype(WIDE) + got_x[0].astype(WIDE)).astype(LOW)
    send_x[...] = (near_y[0].astype(WIDE) + got_y[0].astype(WIDE)).astype(LOW)


def corner_adds(near_x, got_x, near_y, got_y):
    _, half, width = near_x.shape
    rows = half
    block = pl.BlockSpec((1, rows, width), lambda i: (1, i, 0))
    out = pl.BlockSpec((rows, width), lambda i: (i, 0))
    return pl.pallas_call(
        corner_adds_kernel,
        grid=(half // rows,),
        out_shape=(jax.ShapeDtypeStruct((half, width), LOW),) * 2,
        in_specs=[block] * 4,
        out_specs=(out, out),
        compiler_params=params(),
        cost_estimate=LITTLE,
        name="corner_sums",
    )(near_x, got_x, near_y, got_y)


def split(values):
    high = values.astype(LOW)
    return high, (values - high.astype(WIDE)).astype(LOW)


def norm_back(values, gain, grad):
    factor = lax.rsqrt(jnp.mean(values * values, axis=-1, keepdims=True) + EPSILON)
    scaled = gain * grad
    mean = jnp.mean(values * scaled, axis=-1, keepdims=True)
    grad_values = factor * scaled - values * (factor * factor * factor * mean)
    grad_gain = jnp.sum(grad * values * factor, axis=0, keepdims=True)
    return grad_values, grad_gain


def router_back(logits, routes, grad_shares):
    ids = lax.broadcasted_iota(jnp.int32, logits.shape, 0)
    hit = ids == routes[0:1]
    for k in range(1, TOP):
        hit = jnp.logical_or(hit, ids == routes[k : k + 1])
    weights = jnp.exp(logits - jnp.max(logits, axis=0, keepdims=True))
    probs = weights / jnp.sum(weights, axis=0, keepdims=True)
    chosen = jnp.sum(jnp.where(hit, probs, 0.0), axis=0, keepdims=True)
    grads = jnp.where(hit, grad_shares, 0.0)
    mean = jnp.sum(probs * grads, axis=0, keepdims=True) / chosen
    grad_probs = jnp.where(hit, (grads - mean) / chosen, 0.0)
    return probs * (grad_probs - jnp.sum(probs * grad_probs, axis=0, keepdims=True))


def branch_back_kernel(
    parts, info, residual, normed, cotangent, routes, router, gain, *rest
):
    sums, rest = rest[:parts], rest[parts:]
    experts = router.shape[0]
    count = len(rest) - 7
    refs = rest[:count]
    grad_residual, grad_branch, grad_heads, grad_gain, grad_router, weight, sem = rest[count:]

    @pl.when(pl.program_id(0) == 0)
    def _():
        copies = weight_copies(info, refs, weight, sem, D // QUARTERS + 128, D // QUARTERS)
        run_all(copies)
        logits = nt(router[...], normed[...])
        if parts == 2:
            back_sum, grad_shares = sums[0][...], sums[1][...]
        else:
            values = [
                (ref[0] if len(ref.shape) == 3 else ref[...]).astype(WIDE) for ref in sums
            ]
            upper = values[0] + values[1] + values[2]
            lower = values[3] + values[4] + values[5]
            last = lower.shape[0] - SHARE_ROWS
            shares = lower[last : last + experts]
            grad_shares = shares[:, :TOK_DEV] + shares[:, TOK_DEV : 2 * TOK_DEV]
            back_sum = jnp.concatenate([upper, lower[:last]], axis=0)
        high, low = split(router_back(logits, routes[...], grad_shares))
        grad_router[...] = nn(high, normed[...]) + nn(low, normed[...])
        grad_normed = tn(high, router[...]) + tn(low, router[...])
        grad_normed += back_sum
        grad_values, gain_grad = norm_back(residual[...], gain[...], grad_normed)
        grad_gain[...] = gain_grad
        total = cotangent[...].astype(WIDE) + grad_values
        grad_residual[...] = total
        grad_branch[...] = total.astype(LOW)
        wait_all(copies)

    at = pl.ds(pl.multiple_of(pl.program_id(0) * STEP, STEP), STEP)
    grad_heads[...] = nt(grad_branch[...], weight[at, :]).astype(LOW)


def branch_back(info, residual, normed, sums, cotangent, routes, router, gain, refs):
    full = (TOK_DEV, D)
    total = router.shape[0]
    return pl.pallas_call(
        functools.partial(branch_back_kernel, len(sums)),
        grid=(D // STEP,),
        out_shape=(
            jax.ShapeDtypeStruct(full, WIDE),
            jax.ShapeDtypeStruct(full, LOW),
            jax.ShapeDtypeStruct(full, LOW),
            jax.ShapeDtypeStruct((1, D), WIDE),
            jax.ShapeDtypeStruct((total, D), WIDE),
        ),
        in_specs=[SMEM]
        + [whole(full)] * 3
        + [whole((TOP, TOK_DEV)), whole((total, D)), whole((1, D))]
        + [whole(part.shape if part.ndim == 2 else (1,) + part.shape[1:]) for part in sums]
        + [ANY] * len(refs),
        out_specs=(
            whole(full),
            whole(full),
            pl.BlockSpec((TOK_DEV, STEP), lambda i: (0, i)),
            whole((1, D)),
            whole((total, D)),
        ),
        scratch_shapes=[pltpu.VMEM((D, D), LOW), pltpu.SemaphoreType.DMA],
        compiler_params=params(),
        cost_estimate=LITTLE,
        name="experts_norm_back",
    )(info, residual, normed, cotangent, routes, router, gain, *sums, *refs)


def join_grads_kernel(info, own_grad, source_grad, arrived, cosine, sine, out):
    half = HEAD_DIM // 2
    first = lax.broadcasted_iota(jnp.int32, (TOK_DEV, HEAD_DIM), 1) < half
    leaves = info[1] == 0

    def total(column):
        columns = slice(column, column + 128)
        extra = source_grad[:, columns] + arrived[:, columns].astype(WIDE)
        return own_grad[:, columns] + jnp.where(leaves, 0.0, extra)

    for g in range(KV_HEADS):
        key = turn_back(total(128 * g), cosine[...], sine[...])
        value = total(KEY_WIDTH + 128 * g)
        out[:, 256 * g : 256 * g + 128] = jnp.where(
            first, key, pltpu.roll(value, half, 1)
        ).astype(LOW)
        out[:, 256 * g + 128 : 256 * g + 256] = jnp.where(
            first, pltpu.roll(key, half, 1), value
        ).astype(LOW)


def join_grads(info, own_grad, source_grad, arrived, cosine, sine):
    vmem = pl.BlockSpec(memory_space=pltpu.VMEM)
    return pl.pallas_call(
        join_grads_kernel,
        out_shape=jax.ShapeDtypeStruct((TOK_DEV, 2 * KEY_WIDTH), LOW),
        in_specs=[SMEM] + [vmem] * 5,
        out_specs=vmem,
        compiler_params=params(),
        cost_estimate=LITTLE,
        name="join_key_value_gradients",
    )(info, own_grad, source_grad, arrived, cosine, sine)


def token_back_kernel(info, grad_query, grad_pair, tokens, grad_residual, gain, *rest):
    count = (len(rest) - 6) // 2
    query_refs, pair_refs = rest[:count], rest[count : 2 * count]
    out, grad_gain, query_weight, pair_weight, grad_normed, sem = rest[2 * count :]

    @pl.when(pl.program_id(0) == 0)
    def _():
        copies = weight_copies(info, query_refs, query_weight, sem, 0, D // QUARTERS)
        copies += weight_copies(info, pair_refs, pair_weight, sem, D // QUARTERS, 128)
        run_all(copies)
        wait_all(copies)

    at = pl.ds(pl.multiple_of(pl.program_id(0) * STEP, STEP), STEP)
    grad_normed[:, at] = nt(grad_query[...], query_weight[at, :]) + nt(
        grad_pair[...], pair_weight[at, :]
    )

    @pl.when(pl.program_id(0) == pl.num_programs(0) - 1)
    def _():
        grad_values, gain_grad = norm_back(
            tokens[...].astype(WIDE), gain[...], grad_normed[...]
        )
        grad_gain[...] = gain_grad
        out[...] = (grad_residual[...] + grad_values).astype(LOW)


def token_back(info, grad_query, grad_pair, tokens, grad_residual, gain, query_refs, pair_refs):
    full = (TOK_DEV, D)
    return pl.pallas_call(
        token_back_kernel,
        grid=(D // STEP,),
        out_shape=(jax.ShapeDtypeStruct(full, LOW), jax.ShapeDtypeStruct((1, D), WIDE)),
        in_specs=[
            SMEM,
            whole(full),
            whole((TOK_DEV, 2 * KEY_WIDTH)),
            whole(full),
            whole(full),
            whole((1, D)),
        ]
        + [ANY] * (len(query_refs) + len(pair_refs)),
        out_specs=(whole(full), whole((1, D))),
        scratch_shapes=[
            pltpu.VMEM((D, D), LOW),
            pltpu.VMEM((D, 2 * KEY_WIDTH), LOW),
            pltpu.VMEM(full, WIDE),
            pltpu.SemaphoreType.DMA,
        ],
        compiler_params=params(),
        cost_estimate=LITTLE,
        name="token_gradient",
    )(info, grad_query, grad_pair, tokens, grad_residual, gain, *query_refs, *pair_refs)


def weight_grads_kernel(parts, whole_rows, info, *rest):
    ins, (keep, send) = rest[:-2], rest[-2:]
    depth = D // 8
    core = info[0] & 1
    chip = pl.program_id(0) ^ (info[0] >> 1)
    for strip_at, grads_at, start, width in parts:
        low = tn(ins[strip_at][...], ins[grads_at][...]).astype(LOW)
        columns = slice(start, start + width)
        for slot in range(QUARTERS):
            for j in range(QUARTERS):

                @pl.when(info[2 + slot] == j)
                def _():
                    piece = low[:, j * width : (j + 1) * width]
                    upper, lower = piece[:depth], piece[depth:]
                    keep[0, slot, :depth, columns] = jnp.where(core == 0, upper, lower)
                    send[0, slot, :depth, columns] = jnp.where(core == 0, lower, upper)
                    if not whole_rows:
                        blank = jnp.zeros((EXTRA, width), LOW)
                        keep[0, slot, depth:, columns] = blank
                        send[0, slot, depth:, columns] = blank

    if whole_rows:
        extra = ins[-1]
        for slot in range(QUARTERS):
            to = info[2 + slot]
            keep[0, slot, depth:] = extra[(chip * 2 + core) * QUARTERS + to]
            send[0, slot, depth:] = extra[(chip * 2 + 1 - core) * QUARTERS + to]


def weight_grads(info, strips, grads, parts, extra, earlier=()):
    depth = D // 8
    strip = pl.BlockSpec((TOK_DEV, 2 * depth), lambda i, info: (0, i ^ (info[0] >> 1)))
    more = [] if extra is None else [extra]
    width = 2 * D // QUARTERS + 128
    shape = (4, QUARTERS, depth + EXTRA, width)
    if earlier:
        out = pl.BlockSpec((1, QUARTERS, depth + EXTRA, 128), lambda i, info: (i, 0, 0, 3))
    else:
        out = pl.BlockSpec((1,) + shape[1:], lambda i, info: (i, 0, 0, 0))
    inputs = [*strips, *grads, *more]

    def kernel(info, *rest):
        count = len(inputs)
        weight_grads_kernel(
            parts, extra is not None, info, *rest[:count], *rest[count + len(earlier) :]
        )

    return pl.pallas_call(
        kernel,
        grid_spec=pltpu.PrefetchScalarGridSpec(
            num_scalar_prefetch=1,
            grid=(4,),
            in_specs=[strip] * len(strips)
            + [
                pl.BlockSpec(a.shape, lambda i, info, n=a.ndim: (0,) * n)
                for a in (*grads, *more)
            ]
            + [ANY] * len(earlier),
            out_specs=(out, out),
        ),
        out_shape=(jax.ShapeDtypeStruct(shape, LOW),) * 2,
        input_output_aliases={1 + len(inputs) + i: i for i in range(len(earlier))},
        compiler_params=params(),
        cost_estimate=LITTLE,
        name="weight_gradients",
    )(info, *inputs, *earlier)


def position_of(token_index):
    branch_place = TRUNK + (token_index - TRUNK) % BRANCH
    leaf_place = TRUNK + BRANCH + (token_index - TOK_DEV) % BRANCH
    return jnp.where(
        token_index < TRUNK, token_index, jnp.where(token_index < TOK_DEV, branch_place, leaf_place)
    )


def rotary_tables(positions):
    half_dim = HEAD_DIM // 2
    frequency = ROPE_BASE ** (-jnp.arange(half_dim, dtype=jnp.float32) / half_dim)
    angles = positions.astype(jnp.float32)[:, None] * frequency[None, :]
    cosine, sine = (jnp.cos(angles), jnp.sin(angles))
    return (
        jnp.concatenate([cosine, cosine], axis=1),
        jnp.concatenate([-sine, sine], axis=1),
    )


def after(values, *earlier):
    return lax.optimization_barrier((values, earlier))[0]


def fast_mesh():
    return lax.axis_size("rows") == 8 and lax.axis_size("cols") == 4


SLOT_SHARD = ((0, 2, 1, 3), (1, 3, 0, 2), (2, 0, 1, 3), (3, 1, 2, 0))
UP = [(0, 1), (1, 2), (2, 3)]
DOWN = [(1, 0), (2, 1), (3, 2)]
FAR = [(0, 3), (3, 0)]


def send_near(block):
    return lax.ppermute(block, "cols", DOWN), lax.ppermute(block, "cols", UP)


def send_far(block):
    return lax.ppermute(block, "cols", FAR)


def send_over(block):
    return lax.ppermute(block, "cols", [(0, 2), (1, 3), (2, 0), (3, 1)])


def send_second(block, near):
    place = lax.axis_index("cols")
    above, below = near
    payload = jnp.where(place == 1, above, jnp.where(place == 2, below, block))
    return lax.ppermute(payload, "cols", [(3, 1), (1, 0), (0, 2), (2, 3)])


def slot_list(block, near, second, far):
    place = lax.axis_index("cols")
    above, below = near
    end = (place == 0) | (place == 3)
    return [
        block,
        second,
        jnp.where(place == 0, above, below),
        jnp.where(end, far, above),
    ]


def reduce_slots(slots, *earlier):
    place = lax.axis_index("cols")
    own, second, third, fourth = slots
    end = (place == 0) | (place == 3)
    relay = lax.ppermute(second, "cols", [(1, 3), (0, 1), (2, 0), (3, 2)])
    relayed = relay.astype(WIDE)
    upward_load = (
        jnp.where(place == 0, third, fourth).astype(WIDE) + jnp.where(place == 1, relayed, 0.0)
    ).astype(LOW)
    downward_load = (third.astype(WIDE) + jnp.where(place == 2, relayed, 0.0)).astype(LOW)
    arrived = (
        lax.ppermute(upward_load, "cols", UP),
        lax.ppermute(downward_load, "cols", DOWN),
        send_far(after(fourth, upward_load, downward_load)),
        jnp.where(end, relay, jnp.zeros_like(relay)),
    )
    arrived = after(arrived, *earlier)
    return own.astype(WIDE) + sum(block.astype(WIDE) for block in arrived)


def flip(block, bit):
    count = lax.axis_size("rows")
    return lax.ppermute(block, "rows", [(i, i ^ bit) for i in range(count)])


def add_low(one, two):
    return (one.astype(WIDE) + two.astype(WIDE)).astype(LOW)


def chips_second(near_x, near_y, got_x, got_y):
    for_y, for_x = corner_adds(near_x, got_x, near_y, got_y)
    return (near_x, got_x, flip(for_y, 4), near_y, got_y, flip(for_x, 2))


def turn_corner(beside, across):
    half = beside.shape[0] // 2
    return jnp.concatenate([flip(beside[:half], 4), flip(across[half:], 2)], axis=0)


def send_chips(sums):
    return flip(sums[0], 2), flip(sums[1], 4)


def sum_parts(parts):
    wide = [(a[0] if a.ndim == 3 else a).astype(WIDE) for a in parts]
    if len(wide) == 1:
        return wide[0]
    return jnp.concatenate([wide[0] + wide[1] + wide[2], wide[3] + wide[4] + wide[5]], axis=0)


def on_device(
    tokens,
    query_weight,
    key_weight,
    value_weight,
    out_weight,
    router_weight,
    attention_gain,
    experts_gain,
    gate_weight,
    upward_weight,
    down_weight,
    routes,
    leaf_parent,
    cotangent,
):
    row_count = lax.axis_size("rows")
    col_count = lax.axis_size("cols")
    row_place = lax.axis_index("rows")
    col_place = lax.axis_index("cols")
    fast = fast_mesh()
    parity = lax.rem(col_place, 2)
    tree_id = lax.div(row_place * col_count + col_place, 2)
    parent_row = lax.dynamic_slice_in_dim(leaf_parent, tree_id, 1, 0)[0]
    depth, query_part = query_weight.shape
    key_part = key_weight.shape[1]
    router_part = router_weight.shape[1]
    gain_part = attention_gain.shape[0]
    expert_total = router_part * col_count
    local_experts = gate_weight.shape[0]
    capacity = TOK_DEV * TOP // expert_total * 5 // 4

    shards = (
        jnp.asarray(SLOT_SHARD, jnp.int32)[col_place]
        if fast
        else jnp.arange(4, dtype=jnp.int32)
    )
    branch_rows = jnp.where(parity == 0, TRUNK + BRANCH * parent_row, TRUNK)
    info = jnp.concatenate(
        [jnp.stack([row_place, parity]), shards, branch_rows, jnp.zeros((2,), jnp.int32)]
    ).astype(jnp.int32)

    packed = jnp.concatenate([query_weight, key_weight, value_weight, out_weight], axis=1)
    local_index = (1 - parity) * TOK_DEV + jnp.arange(TOK_DEV, dtype=jnp.int32)
    cosine, sine = rotary_tables(position_of(local_index))
    shard_blocks = [
        jnp.concatenate(
            [gate_weight[expert].T, upward_weight[expert].T, down_weight[expert]], axis=0
        )
        for expert in range(local_experts)
    ]
    expert_refs = []
    if fast:
        wide = packed.shape[1]
        gains = jnp.concatenate([attention_gain, experts_gain])[None, :]
        packed = jnp.concatenate(
            [
                packed,
                jnp.pad(router_weight.T, ((0, 0), (0, wide - depth))),
                jnp.pad(gains, ((0, 0), (0, wide - 2 * gain_part))),
                jnp.pad(routes.T.astype(LOW), ((0, 0), (0, wide - TOK_DEV))),
                jnp.zeros((EXTRA - router_part - 1 - TOP, wide), LOW),
            ],
            axis=0,
        )
        packed_near = send_near(packed)
        packed_far = send_far(packed)
        packed_second = send_over(packed)
        first_block = after(shard_blocks[0], *packed_near)
        first_near = send_near(first_block)
        first_second = send_second(first_block, first_near)
        own = jnp.stack(slot_list(packed, packed_near, packed_second, packed_far))
        own = after(own, info, cosine, sine)
        beside, across = flip(own, 2), flip(own, 4)
        own_in = flip(own, 1)
        beside, across = after((beside, across), own_in, *first_near)
        corner = [flip(beside[:2], 4), flip(across[2:], 2)]
        pair_in = flip(jnp.concatenate([beside, across], axis=0), 1)
        corner_in = [flip(piece, 1) for piece in corner]
        grad_in = after(cotangent, *corner)
        grad_flips = [flip(grad_in, 2), flip(grad_in, 4)]
        pieces = [own, own_in, beside, across, *corner, pair_in, *corner_in]
        at = depth + router_part + 1
        near_slots = [own, own_in, beside, pair_in, across, pair_in[4:], corner[0], corner_in[0]]
        routes_all = jnp.stack([part[0, at : at + TOP, :TOK_DEV] for part in near_slots])
        routes_all = routes_all.astype(jnp.int32)
        chosen, place_rows = tables(info, routes_all, capacity, local_experts, expert_total)
        query_refs = pair_refs = out_refs = pieces
        extra_rows = extras(info, pieces)
        router_all = extra_rows[:, :router_part, :depth]
        attention_scale = extra_rows[:, router_part, :gain_part]
        experts_scale = extra_rows[:, router_part, gain_part : 2 * gain_part]
    else:
        packed_all = lax.all_gather(lax.all_gather(packed, "cols", axis=0), "rows", axis=0)

        def unpack(start, width):
            part = packed_all[..., start : start + width]
            return jnp.swapaxes(part, 1, 2).reshape(row_count * depth, col_count * width)

        key_at = query_part
        query_refs = [unpack(0, query_part)]
        pair_refs = [
            jnp.concatenate(
                [
                    unpack(key_at, key_part).reshape(D, QUARTERS, -1),
                    unpack(key_at + key_part, key_part).reshape(D, QUARTERS, -1),
                ],
                axis=2,
            ).reshape(D, -1)
        ]
        out_refs = [unpack(key_at + 2 * key_part, query_part)]
        routes_all = lax.all_gather(routes.T, "rows", axis=0)
        chosen, place_rows = tables(info, routes_all, capacity, local_experts, expert_total)
        axes = ("rows", "cols")
        router_all = jnp.swapaxes(lax.all_gather(router_weight, axes, axis=0), 1, 2)
        attention_scale = lax.all_gather(attention_gain, axes, axis=0)
        experts_scale = lax.all_gather(experts_gain, axes, axis=0)

    attention_scale = attention_scale.reshape(1, D).astype(WIDE)
    experts_scale = experts_scale.reshape(1, D).astype(WIDE)
    router_rows = jnp.transpose(
        router_all.reshape(row_count, col_count, router_part, depth), (1, 2, 0, 3)
    ).reshape(expert_total, D)
    router_cols = router_rows.T
    tokens_in = after(tokens, first_second, chosen) if fast else tokens
    normed, own_pair = key_value(info, tokens_in, attention_scale, cosine, sine, pair_refs)
    pairs = [(i + 1, i) for i in range(0, col_count, 2)]
    partner = lax.ppermute(own_pair, "cols", pairs)
    if fast:
        own_grad_in = flip(grad_in, 1)
        normed_in = after(normed, own_grad_in)
    else:
        normed_in = normed
    queries = query(info, normed_in, cosine, sine, query_refs)
    if fast:
        first_far = send_far(after(first_block, partner, queries))
        expert_refs.append([first_block, first_second, *first_near, first_far])
    if fast:
        grad_flips = after(grad_flips, queries)
        grad_corner = turn_corner(*grad_flips)
    heads = attention(info, queries, own_pair, partner)
    if fast:
        grad_near = [*grad_flips, grad_corner]
        grad_blocks = [cotangent, own_grad_in]
        grad_blocks += [block for one in grad_near for block in (one, flip(one, 1))]
        heads = after(heads, grad_corner, grad_blocks[3], grad_blocks[5])
    else:
        grad_all = lax.all_gather(cotangent, "rows", axis=0)
        grad_blocks = [grad_all[q] for q in range(row_count)]
    residual, normed_two = out_projection(info, heads, tokens, experts_scale, out_refs)

    if fast:
        beside, across = flip(normed_two, 2), flip(normed_two, 4)
        beside_in = flip(after(normed_two, *grad_blocks), 1)
        later_block = after(shard_blocks[1], first_far, normed_two)
        expert_refs.append([lax.all_gather(later_block, "cols", axis=0)])
    else:
        rows_all = lax.all_gather(normed_two, "rows", axis=0)
        expert_refs = [[lax.all_gather(block, "cols", axis=0)] for block in shard_blocks]
    grad_rows = pick_rows(chosen, grad_blocks, local_experts)

    def place_block(q, block, picked):
        return dispatch(
            q, info, block, chosen, routes_all, router_cols, local_experts, picked
        )

    if fast:
        half = TOK_DEV // 2
        picked = place_block(0, normed_two, None)
        beside, across = after((beside, across), picked, *grad_rows)
        corner = [flip(beside[:half], 4), flip(across[half:], 2)]
        picked = place_block(1, beside_in, picked)
        picked = place_block(2, beside, picked)
        picked = place_block(4, across, picked)
        beside_in = flip(beside, 1)
        across_in = flip(across, 1)
        picked = place_block(3, beside_in, picked)
        picked = place_block(5, across_in, picked)
        corner = jnp.concatenate(after(corner, picked), axis=0)
        corner_in = flip(corner, 1)
        picked = place_block(6, corner, picked)
        picked = place_block(7, corner_in, picked)
    else:
        picked = None
        for q in range(row_count):
            picked = place_block(q, rows_all[q], picked)
    height = row_count * capacity
    token_rows = [a.reshape(height, D) for a in picked[:local_experts]]
    grad_rows = [a.reshape(height, D) for a in grad_rows]
    share_rows = [a.reshape(height, 1) for a in picked[local_experts:]]

    out_rows, back_rows, gate_dots, reduced = ([], [], [], [])
    for e in range(local_experts):
        rows_in = after(token_rows[e], *reduced_in) if e else token_rows[e]
        out_row, back_row, grad_row, acts, dots = expert(
            info, rows_in, grad_rows[e], share_rows[e], expert_refs[e], col_count
        )
        out_rows.append(out_row.reshape(row_count, capacity, D))
        back_rows.append(back_row.reshape(row_count, capacity, D))
        gate_dots.append(dots.reshape(row_count, capacity, 1))
        if fast and e == 1:
            got = flip(combine(info, chosen, back_rows, 1, 2, gate_dots), 1)
            back_keep = combine(info, chosen, back_rows, 0, 2, gate_dots)
            for_x, for_y, near_x, near_y = chip_adds(back_keep, got)
            acts = after(acts, for_x)
            back_flips = send_chips((for_x, for_y))
        slots = expert_grads(acts, token_rows[e], grad_row)
        reduced_in = (slots,)
        if e and fast:
            out_got = flip(combine(info, chosen, out_rows, 1, 2), 1)
            out_keep = combine(info, chosen, out_rows, 0, 2)
            back_flips = after(back_flips, slots, out_keep)
            back_parts = chips_second(near_x, near_y, *back_flips)
        else:
            reduced.append(lax.psum_scatter(slots, "cols", scatter_dimension=0, tiled=False))

    if fast:
        out_first = chip_adds(out_keep, out_got)
        back_parts = after(back_parts, out_first[0])
    else:
        spread_dots = spread(place_rows, gate_dots)
        grad_shares = lax.all_to_all(spread_dots, "rows", split_axis=0, concat_axis=0, tiled=True)

        def summed(rows):
            part = combine(info, chosen, rows, 0, 1)
            return lax.psum_scatter(part, "rows", scatter_dimension=0).astype(WIDE)

        back_parts = (summed(back_rows), grad_shares.reshape(expert_total, TOK_DEV))
        mixture = (summed(out_rows),)

    grad_residual, grad_branch, grad_heads, experts_gain_grad, router_grad = branch_back(
        info,
        residual,
        normed_two,
        back_parts,
        cotangent,
        routes.T,
        router_rows,
        experts_scale,
        out_refs,
    )
    if fast:
        out_flips = send_chips(after(out_first[:2], back_parts[2], back_parts[5]))
        slots = after(slots, reduced[0], back_parts[2])
        reduced.append(lax.psum_scatter(slots, "cols", scatter_dimension=0, tiled=False))
        router_parts = jnp.transpose(
            router_grad.astype(LOW).reshape(col_count, router_part, row_count, depth),
            (2, 0, 1, 3),
        ).reshape(row_count * col_count, router_part, depth)
        gain_rows = experts_gain_grad.astype(LOW).reshape(row_count * col_count, 1, gain_part)
        extra = jnp.concatenate(
            [
                jnp.pad(router_parts, ((0, 0), (0, 0), (0, wide - depth))),
                jnp.pad(gain_rows, ((0, 0), (0, 0), (0, wide - gain_part))),
                jnp.zeros((row_count * col_count, EXTRA - router_part - 1, wide), LOW),
            ],
            axis=1,
        )
    grad_query, own_grad, source_grad = attention_back(
        info, queries, own_pair, partner, grad_heads, cosine, sine
    )
    arrived = lax.ppermute(source_grad.astype(LOW), "cols", [(j, i) for i, j in pairs])
    if fast:
        parts = ((0, 2, 0, query_part), (1, 3, query_part + 2 * key_part, query_part))
        keep_send = weight_grads(
            info, [normed, heads], [grad_query, grad_branch], parts, extra
        )
        arrived = after(arrived, *keep_send, *out_flips)
    grad_pair = join_grads(info, own_grad, source_grad, arrived, cosine, sine)
    if fast:
        keep, send = weight_grads(
            info, [normed], [grad_pair], ((0, 1, 0, 2 * key_part),), None, keep_send
        )
        flat = (4, col_count * (depth + EXTRA), wide)
        sent = flip(send, 1)
        sent_first = chip_adds(keep.reshape(flat), sent.reshape(flat))
        sent_chips = send_chips(sent_first[:2])
        grad_pair = after(grad_pair, sent_first[0])
    tokens_grad, attention_gain_grad = token_back(
        info, grad_query, grad_pair, tokens, grad_residual, attention_scale, query_refs, pair_refs
    )

    if fast:
        sent_chips = after(sent_chips, tokens_grad)
        sent_parts = chips_second(*sent_first[2:], *sent_chips)
        near_x, near_y = out_first[2:]
        mixture = chips_second(near_x, near_y, *after(out_flips, *sent_chips))
    layer_output = (residual + sum_parts(mixture)).astype(LOW)
    part = down_weight.shape[1]
    expert_sums = [block.astype(WIDE) for block in reduced]
    gate_grad, upward_grad, down_grad = (
        jnp.stack([sums_of[which * part : (which + 1) * part] for sums_of in expert_sums])
        for which in range(3)
    )
    if fast:
        slots = sum_parts(sent_parts)
        slots = slots.reshape(col_count, depth + EXTRA, wide)
        width = query_part + 2 * key_part
        own_slots = own
        gain_sums = sum(
            jnp.sum(own_slots[i][:depth, :width].astype(WIDE) * slots[i, :depth, :width], axis=1)
            for i in range(4)
        )
        own_gains = lax.dynamic_slice_in_dim(attention_scale[0], row_place * depth, depth, 0)
        gain_sums = (gain_sums / own_gains).reshape(col_count, 1, gain_part)
        gain_sums = jnp.pad(
            jnp.take(gain_sums, shards, axis=0),
            ((0, 0), (depth + router_part + 1, EXTRA - router_part - 2), (0, wide - gain_part)),
        )
        slots = after((slots + gain_sums).astype(LOW), reduced[1])

        sums = reduce_slots(slots, gate_grad, upward_grad, down_grad, layer_output)
        router_sum = sums[depth : depth + router_part, :depth].T
        experts_gain_sum = sums[depth + router_part, :gain_part]
        attention_gain_sum = sums[depth + router_part + 1, :gain_part]
        sums = sums[:depth]
    else:
        full_grads = [
            tn(normed, grad_query),
            *jnp.moveaxis(tn(normed, grad_pair).reshape(D, QUARTERS, 2, -1), 2, 0),
            tn(heads, grad_branch),
        ]
        packed_grad = jnp.concatenate(
            [
                grad.astype(LOW).reshape(row_count, depth, col_count, -1)
                for grad in full_grads
            ],
            axis=3,
        )
        row_sums = lax.psum_scatter(packed_grad, "rows", scatter_dimension=0)
        sums = lax.psum_scatter(row_sums, "cols", scatter_dimension=1).astype(WIDE)
        small_grads = jnp.concatenate(
            [
                attention_gain_grad.reshape(-1, gain_part),
                experts_gain_grad.reshape(-1, gain_part),
                jnp.transpose(
                    router_grad.reshape(col_count, router_part, row_count, depth), (2, 0, 3, 1)
                ).reshape(row_count * col_count, depth * router_part),
            ],
            axis=1,
        )
        small_grads = small_grads.reshape(row_count, -1)
        small_grads = lax.all_to_all(small_grads, "rows", split_axis=0, concat_axis=0, tiled=True)
        small_grads = jnp.sum(small_grads, axis=0).reshape(col_count, -1)
        small_grads = lax.all_to_all(small_grads, "cols", split_axis=0, concat_axis=0, tiled=True)
        small_sums = jnp.sum(small_grads, axis=0)
        attention_gain_sum = small_sums[:gain_part]
        experts_gain_sum = small_sums[gain_part : 2 * gain_part]
        router_sum = small_sums[2 * gain_part :].reshape(depth, router_part)

    key_at = query_part
    value_at = key_at + key_part
    out_at = value_at + key_part
    return (
        layer_output,
        tokens_grad,
        sums[:, :key_at],
        sums[:, key_at:value_at],
        sums[:, value_at:out_at],
        sums[:, out_at:],
        router_sum,
        attention_gain_sum,
        experts_gain_sum,
        jnp.swapaxes(gate_grad, 1, 2),
        jnp.swapaxes(upward_grad, 1, 2),
        down_grad,
    )


def solution(mesh):
    in_specs = (
        P(("rows", "cols"), None),
        P("rows", "cols"),
        P("rows", "cols"),
        P("rows", "cols"),
        P("rows", "cols"),
        P("rows", "cols"),
        P(("rows", "cols")),
        P(("rows", "cols")),
        P("rows", None, "cols"),
        P("rows", None, "cols"),
        P("rows", "cols", None),
        P(("rows", "cols"), None),
        P(),
        P(("rows", "cols"), None),
    )
    out_specs = (
        P(("rows", "cols"), None),
        P(("rows", "cols"), None),
        P("rows", "cols"),
        P("rows", "cols"),
        P("rows", "cols"),
        P("rows", "cols"),
        P("rows", "cols"),
        P(("rows", "cols")),
        P(("rows", "cols")),
        P("rows", None, "cols"),
        P("rows", None, "cols"),
        P("rows", "cols", None),
    )
    return jax.shard_map(
        on_device, mesh=mesh, in_specs=in_specs, out_specs=out_specs, check_vma=False
    )
```

```python
import functools

import jax
import jax.numpy as jnp
from jax import lax
from jax.experimental import pallas as pl
from jax.experimental.pallas import tpu as pltpu
from jax.sharding import PartitionSpec as P

D = 1536
HEADS = 12
KV_HEADS = 2
HEAD_DIM = 128
TOP = 4
TOK_DEV = 512
BRANCHES = 4
LEAVES = 8
TRUNK = 256
BRANCH = 64

EPSILON = 1e-06
ROPE_BASE = 10000.0
MASKED = -1e30
LOW = jnp.bfloat16
WIDE = jnp.float32
KEY_WIDTH = KV_HEADS * HEAD_DIM
GROUP = HEADS // KV_HEADS
QUARTERS = 4
VMEM_LIMIT = 56 * 1024 * 1024

ANY = pl.BlockSpec(memory_space=pl.ANY)
SMEM = pl.BlockSpec(memory_space=pltpu.SMEM)


def nn(one, two):
    return lax.dot_general(one, two, (((1,), (0,)), ((), ())), preferred_element_type=WIDE)


def nt(one, two):
    return lax.dot_general(one, two, (((1,), (1,)), ((), ())), preferred_element_type=WIDE)


def tn(one, two):
    return lax.dot_general(one, two, (((0,), (0,)), ((), ())), preferred_element_type=WIDE)


def whole(shape):
    return pl.BlockSpec(shape, lambda *_: (0,) * len(shape))


LITTLE = pl.CostEstimate(flops=1, bytes_accessed=1, transcendentals=0)


def params():
    return pltpu.CompilerParams(vmem_limit_bytes=VMEM_LIMIT)


def turn(values, cosine, sine):
    return values * cosine + pltpu.roll(values, HEAD_DIM // 2, 1) * sine


def turn_back(values, cosine, sine):
    return values * cosine - pltpu.roll(values, HEAD_DIM // 2, 1) * sine


SLOTS = range(4)
PIECES = (
    tuple((0, slot) for slot in SLOTS),
    tuple((1, slot) for slot in SLOTS),
    tuple((2, slot) for slot in SLOTS),
    tuple((4, slot) for slot in SLOTS),
    ((6, 0), (6, 1)),
    ((6, 2), (6, 3)),
    tuple((flip_bits, slot) for flip_bits in (3, 5) for slot in SLOTS),
    ((7, 0), (7, 1)),
    ((7, 2), (7, 3)),
)
EXTRA = 16


STEP = 768


def weight_copies(info, refs, target, sem, start, width):
    if len(refs) == 1:
        return [pltpu.make_async_copy(refs[0], target, sem)]
    depth = refs[0].shape[1] - EXTRA
    copies = []
    for ref, parts in zip(refs, PIECES):
        for at, (flip_bits, slot) in enumerate(parts):
            row = pl.multiple_of((info[0] ^ flip_bits) * depth, depth)
            col = pl.multiple_of(info[2 + slot] * width, 128)
            copies.append(
                pltpu.make_async_copy(
                    ref.at[at, pl.ds(0, depth), pl.ds(start, width)],
                    target.at[pl.ds(row, depth), pl.ds(col, width)],
                    sem,
                )
            )
    return copies


def extras_kernel(info, *rest):
    refs, (out, sem) = rest[:-2], rest[-2:]
    depth = refs[0].shape[1] - EXTRA
    copies = []
    for ref, parts in zip(refs, PIECES):
        for at, (flip_bits, slot) in enumerate(parts):
            to = (info[0] ^ flip_bits) * QUARTERS + info[2 + slot]
            copies.append(pltpu.make_async_copy(ref.at[at, pl.ds(depth, EXTRA)], out.at[to], sem))
    run_all(copies)
    wait_all(copies)


def extras(info, refs):
    return pl.pallas_call(
        extras_kernel,
        out_shape=jax.ShapeDtypeStruct((8 * QUARTERS, EXTRA, refs[0].shape[2]), LOW),
        in_specs=[SMEM] + [ANY] * len(refs),
        out_specs=pl.BlockSpec(memory_space=pltpu.VMEM),
        scratch_shapes=[pltpu.SemaphoreType.DMA],
        compiler_params=params(),
        cost_estimate=LITTLE,
        name="extra_rows",
    )(info, *refs)


def run_all(copies):
    for copy in copies:
        copy.start()


def wait_all(copies):
    for copy in copies:
        copy.wait()


def key_value_kernel(info, tokens, gain, cosine, sine, *rest):
    count = len(rest) - 4
    refs, (normed, out, weight, sem) = rest[:count], rest[count:]
    copies = weight_copies(info, refs, weight, sem, D // QUARTERS, 128)
    run_all(copies)
    values = tokens[...].astype(WIDE)
    factor = lax.rsqrt(jnp.mean(values * values, axis=-1, keepdims=True) + EPSILON)
    low = (values * factor * gain[...]).astype(LOW)
    normed[...] = low
    wait_all(copies)
    both = nn(low, weight[...])
    half = HEAD_DIM // 2
    first = lax.broadcasted_iota(jnp.int32, (TOK_DEV, HEAD_DIM), 1) < half
    for g in range(KV_HEADS):
        one = both[:, 256 * g : 256 * g + 128]
        two = both[:, 256 * g + 128 : 256 * g + 256]
        key = jnp.where(first, one, pltpu.roll(two, half, 1))
        value = jnp.where(first, pltpu.roll(one, half, 1), two)
        out[:, 128 * g : 128 * g + 128] = turn(key, cosine[...], sine[...]).astype(LOW)
        out[:, KEY_WIDTH + 128 * g : KEY_WIDTH + 128 * g + 128] = value.astype(LOW)


def key_value(info, tokens, gain, cosine, sine, refs):
    return pl.pallas_call(
        key_value_kernel,
        out_shape=(
            jax.ShapeDtypeStruct((TOK_DEV, D), LOW),
            jax.ShapeDtypeStruct((TOK_DEV, 2 * KEY_WIDTH), LOW),
        ),
        in_specs=[SMEM] + [pl.BlockSpec(memory_space=pltpu.VMEM)] * 4 + [ANY] * len(refs),
        out_specs=(pl.BlockSpec(memory_space=pltpu.VMEM),) * 2,
        scratch_shapes=[pltpu.VMEM((D, 2 * KEY_WIDTH), LOW), pltpu.SemaphoreType.DMA],
        compiler_params=params(),
        cost_estimate=LITTLE,
        name="norm_key_value",
    )(info, tokens, gain, cosine, sine, *refs)


def query_kernel(info, normed, cosine, sine, *rest):
    count = len(rest) - 3
    refs, (out, weight, sem) = rest[:count], rest[count:]

    @pl.when(pl.program_id(0) == 0)
    def _():
        copies = weight_copies(info, refs, weight, sem, 0, D // QUARTERS)
        run_all(copies)
        wait_all(copies)

    at = pl.multiple_of(pl.program_id(0) * STEP, STEP)
    lin = nn(normed[...], weight[:, pl.ds(at, STEP)])
    for h in range(STEP // HEAD_DIM):
        out[:, 128 * h : 128 * h + 128] = turn(
            lin[:, 128 * h : 128 * h + 128], cosine[...], sine[...]
        ).astype(LOW)


def query(info, normed, cosine, sine, refs):
    return pl.pallas_call(
        query_kernel,
        grid=(D // STEP,),
        out_shape=jax.ShapeDtypeStruct((TOK_DEV, D), LOW),
        in_specs=[SMEM, whole((TOK_DEV, D)), whole((TOK_DEV, 128)), whole((TOK_DEV, 128))]
        + [ANY] * len(refs),
        out_specs=pl.BlockSpec((TOK_DEV, STEP), lambda i: (0, i)),
        scratch_shapes=[pltpu.VMEM((D, D), LOW), pltpu.SemaphoreType.DMA],
        compiler_params=params(),
        cost_estimate=LITTLE,
        name="query_projection",
    )(info, normed, cosine, sine, *refs)


KEYS = TRUNK + 2 * BRANCH
CHUNKS = TOK_DEV // BRANCH


def chunk_keys(info, source, own, column, chunk):
    at = pl.multiple_of(info[6 + chunk], BRANCH)
    rows = pl.multiple_of(chunk * BRANCH, BRANCH)
    columns = slice(column, column + HEAD_DIM)
    return jnp.concatenate(
        [
            source[0:TRUNK, columns],
            source[pl.ds(at, BRANCH), columns],
            own[pl.ds(rows, BRANCH), columns],
        ],
        axis=0,
    )


def chunk_allowed(info, chunk, query_axis, shape):
    query_row = lax.broadcasted_iota(jnp.int32, shape, query_axis) & (BRANCH - 1)
    key = lax.broadcasted_iota(jnp.int32, shape, 1 - query_axis)
    leaves = info[1] == 0
    trunk = jnp.logical_and(jnp.logical_not(leaves), chunk < TRUNK // BRANCH)
    limit = jnp.where(trunk, chunk * BRANCH + query_row, TRUNK - 1)
    branch_limit = jnp.where(leaves, TRUNK + BRANCH - 1, 0)
    own_limit = jnp.where(trunk, 0, query_row + TRUNK + BRANCH)
    top = jnp.where(key < TRUNK, limit, jnp.where(key < TRUNK + BRANCH, branch_limit, own_limit))
    return key <= top


def group_rows(ref, g):
    first = g * GROUP
    return jnp.concatenate(
        [ref[:, 128 * h : 128 * h + 128] for h in range(first, first + GROUP)], axis=0
    )


def keep_source(info, partner, own, source):
    @pl.when(pl.program_id(0) == 0)
    def _():
        @pl.when(info[1] == 0)
        def _():
            source[...] = partner[...]

        @pl.when(info[1] != 0)
        def _():
            source[...] = own[...]


def attention_kernel(info, queries, own, partner, out, source):
    keep_source(info, partner, own, source)
    chunk = pl.program_id(0)
    rows = GROUP * BRANCH
    allowed = chunk_allowed(info, chunk, 0, (rows, KEYS))
    for g in range(KV_HEADS):
        keys = chunk_keys(info, source, own, 128 * g, chunk)
        values = chunk_keys(info, source, own, KEY_WIDTH + 128 * g, chunk)
        scores = nt(group_rows(queries, g), keys) * HEAD_DIM**-0.5
        scores = jnp.where(allowed, scores, MASKED)
        weights = jnp.exp(scores - jnp.max(scores, axis=1, keepdims=True))
        total = jnp.sum(weights, axis=1, keepdims=True)
        mixed = nn((weights * (1.0 / total)).astype(LOW), values).astype(LOW)
        for h in range(GROUP):
            at = (g * GROUP + h) * 128
            out[:, at : at + 128] = mixed[h * BRANCH : (h + 1) * BRANCH]


def attention(info, queries, own, partner):
    return pl.pallas_call(
        attention_kernel,
        grid=(CHUNKS,),
        out_shape=jax.ShapeDtypeStruct((TOK_DEV, D), LOW),
        in_specs=[
            SMEM,
            pl.BlockSpec((BRANCH, D), lambda i: (i, 0)),
            whole((TOK_DEV, 2 * KEY_WIDTH)),
            whole((TOK_DEV, 2 * KEY_WIDTH)),
        ],
        out_specs=pl.BlockSpec((BRANCH, D), lambda i: (i, 0)),
        scratch_shapes=[pltpu.VMEM((TOK_DEV, 2 * KEY_WIDTH), LOW)],
        compiler_params=params(),
        cost_estimate=LITTLE,
        name="tree_attention",
    )(info, queries, own, partner)


def attention_back_kernel(
    info, queries, own, partner, grads, cosine, sine, grad_query, own_grad, source_grad, source
):
    keep_source(info, partner, own, source)
    chunk = pl.program_id(0)

    @pl.when(chunk == 0)
    def _():
        source_grad[...] = jnp.zeros_like(source_grad)

    rows = GROUP * BRANCH
    scale = HEAD_DIM**-0.5
    allowed = chunk_allowed(info, chunk, 1, (KEYS, rows))
    at = pl.multiple_of(info[6 + chunk], BRANCH)
    for g in range(KV_HEADS):
        keys = chunk_keys(info, source, own, 128 * g, chunk)
        values = chunk_keys(info, source, own, KEY_WIDTH + 128 * g, chunk)
        query_rows = group_rows(queries, g)
        grad_rows = group_rows(grads, g)
        scores = jnp.where(allowed, nt(keys, query_rows) * scale, MASKED)
        weights = jnp.exp(scores - jnp.max(scores, axis=0, keepdims=True))
        probs = weights * (1.0 / jnp.sum(weights, axis=0, keepdims=True))
        grad_probs = nt(values, grad_rows)
        mean = jnp.sum(probs * grad_probs, axis=0, keepdims=True)
        grad_scores = (probs * (grad_probs - mean)).astype(LOW)
        grad_values = nn(probs.astype(LOW), grad_rows)
        grad_keys = nn(grad_scores, query_rows) * scale
        grad_queries = tn(grad_scores, keys) * scale
        for h in range(GROUP):
            to = (g * GROUP + h) * 128
            grad_query[:, to : to + 128] = turn_back(
                grad_queries[h * BRANCH : (h + 1) * BRANCH], cosine[...], sine[...]
            ).astype(LOW)
        for column, grad in ((128 * g, grad_keys), (KEY_WIDTH + 128 * g, grad_values)):
            columns = slice(column, column + 128)
            source_grad[0:TRUNK, columns] += grad[0:TRUNK]
            source_grad[pl.ds(at, BRANCH), columns] += grad[TRUNK : TRUNK + BRANCH]
            own_grad[:, columns] = grad[TRUNK + BRANCH :]


def attention_back(info, queries, own, partner, grads, cosine, sine):
    chunked = pl.BlockSpec((BRANCH, D), lambda i: (i, 0))
    pair = (TOK_DEV, 2 * KEY_WIDTH)
    return pl.pallas_call(
        attention_back_kernel,
        grid=(CHUNKS,),
        out_shape=(
            jax.ShapeDtypeStruct((TOK_DEV, D), LOW),
            jax.ShapeDtypeStruct(pair, WIDE),
            jax.ShapeDtypeStruct(pair, WIDE),
        ),
        in_specs=[
            SMEM,
            chunked,
            whole(pair),
            whole(pair),
            chunked,
            pl.BlockSpec((BRANCH, 128), lambda i: (i, 0)),
            pl.BlockSpec((BRANCH, 128), lambda i: (i, 0)),
        ],
        out_specs=(
            chunked,
            pl.BlockSpec((BRANCH, 2 * KEY_WIDTH), lambda i: (i, 0)),
            whole(pair),
        ),
        scratch_shapes=[pltpu.VMEM(pair, LOW)],
        compiler_params=params(),
        cost_estimate=LITTLE,
        name="tree_attention_back",
    )(info, queries, own, partner, grads, cosine, sine)


def out_kernel(info, heads, tokens, gain, *rest):
    count = len(rest) - 4
    refs, (residual, normed, weight, sem) = rest[:count], rest[count:]

    @pl.when(pl.program_id(0) == 0)
    def _():
        copies = weight_copies(info, refs, weight, sem, D // QUARTERS + 128, D // QUARTERS)
        run_all(copies)
        wait_all(copies)

    at = pl.ds(pl.multiple_of(pl.program_id(0) * STEP, STEP), STEP)
    residual[:, at] = tokens[:, at].astype(WIDE) + nn(heads[...], weight[:, at])

    @pl.when(pl.program_id(0) == pl.num_programs(0) - 1)
    def _():
        values = residual[...]
        factor = lax.rsqrt(jnp.mean(values * values, axis=-1, keepdims=True) + EPSILON)
        normed[...] = (values * factor * gain[...]).astype(LOW)


def out_projection(info, heads, tokens, gain, refs):
    full = (TOK_DEV, D)
    return pl.pallas_call(
        out_kernel,
        grid=(D // STEP,),
        out_shape=(jax.ShapeDtypeStruct(full, WIDE), jax.ShapeDtypeStruct(full, LOW)),
        in_specs=[SMEM, whole(full), whole(full), whole((1, D))] + [ANY] * len(refs),
        out_specs=(whole(full), whole(full)),
        scratch_shapes=[pltpu.VMEM((D, D), LOW), pltpu.SemaphoreType.DMA],
        compiler_params=params(),
        cost_estimate=LITTLE,
        name="out_projection",
    )(info, heads, tokens, gain, *refs)


def hits_of(routes, ids):
    hit = ids == routes[0, 0:1]
    for k in range(1, TOP):
        hit = jnp.logical_or(hit, ids == routes[0, k : k + 1])
    return hit


def tables_kernel(capacity, local, total, info, routes, chosen_out, place_out, earlier):
    @pl.when(pl.program_id(0) == 0)
    def _():
        one = lax.broadcasted_iota(jnp.int32, (TOK_DEV, TOK_DEV), 0)
        two = lax.broadcasted_iota(jnp.int32, (TOK_DEV, TOK_DEV), 1)
        earlier[...] = jnp.where(one < two, 1.0, 0.0).astype(LOW)

    ids = lax.broadcasted_iota(jnp.int32, (total, TOK_DEV), 0)
    hit = hits_of(routes, ids)
    rank = nn(jnp.where(hit, 1.0, 0.0).astype(LOW), earlier[...])
    place = jnp.where(hit, rank, -1.0)
    spots = lax.broadcasted_iota(jnp.int32, (capacity, TOK_DEV), 0).astype(WIDE)
    place_out[0] = jnp.full(place_out.shape[1:], -1.0, WIDE)
    for e in range(local):
        mine = ids == info[0] * local + e
        place_row = jnp.sum(jnp.where(mine, place, 0.0), axis=0, keepdims=True)
        place_out[0, e : e + 1] = place_row
        chosen_out[0, e * capacity : (e + 1) * capacity] = jnp.where(
            spots == place_row, 1.0, 0.0
        ).astype(LOW)


def tables(info, routes, capacity, local, total):
    count = routes.shape[0]
    return pl.pallas_call(
        functools.partial(tables_kernel, capacity, local, total),
        grid=(count,),
        in_specs=[SMEM, pl.BlockSpec((1, TOP, TOK_DEV), lambda i: (i, 0, 0))],
        out_specs=[
            pl.BlockSpec((1, local * capacity, TOK_DEV), lambda i: (i, 0, 0)),
            pl.BlockSpec((1, 8, TOK_DEV), lambda i: (i, 0, 0)),
        ],
        scratch_shapes=[pltpu.VMEM((TOK_DEV, TOK_DEV), LOW)],
        out_shape=[
            jax.ShapeDtypeStruct((count, local * capacity, TOK_DEV), LOW),
            jax.ShapeDtypeStruct((count, 8, TOK_DEV), WIDE),
        ],
        compiler_params=params(),
        cost_estimate=LITTLE,
        name="route_tables",
    )(info, routes)


def pick_kernel(local, count, chosen, *rest):
    blocks, outs = rest[:count], rest[count : count + local]
    picks, block_in, out_block, sem_in, sem_out = rest[count + local :]
    capacity = outs[0].shape[1]
    copies = [
        (
            pltpu.make_async_copy(chosen.at[q], picks.at[q], sem_in.at[q, 0]),
            pltpu.make_async_copy(blocks[q], block_in.at[q], sem_in.at[q, 1]),
        )
        for q in range(count)
    ]
    for pair in copies:
        run_all(pair)
    sent = []
    for q in range(count):
        wait_all(copies[q])
        out_block[q] = nn(picks[q], block_in[q]).astype(LOW)
        for e in range(local):
            copy = pltpu.make_async_copy(
                out_block.at[q, pl.ds(e * capacity, capacity)], outs[e].at[q], sem_out.at[q, e]
            )
            copy.start()
            sent.append(copy)
    wait_all(sent)


def pick_rows(chosen, blocks, local):
    count, height, _ = chosen.shape
    return pl.pallas_call(
        functools.partial(pick_kernel, local, count),
        in_specs=[ANY] * (1 + count),
        out_specs=[ANY] * local,
        out_shape=[jax.ShapeDtypeStruct((count, height // local, D), LOW)] * local,
        scratch_shapes=[
            pltpu.VMEM((count, height, TOK_DEV), LOW),
            pltpu.VMEM((count, TOK_DEV, D), LOW),
            pltpu.VMEM((count, height, D), LOW),
            pltpu.SemaphoreType.DMA((count, 2)),
            pltpu.SemaphoreType.DMA((count, local)),
        ],
        compiler_params=params(),
        cost_estimate=LITTLE,
        name="pick_rows",
    )(chosen, *blocks)


def dispatch_kernel(local, info, rows, chosen, routes, router, *rest):
    outs, logits = rest[2 * local : 4 * local], rest[-1]
    total = router.shape[1]
    step = pl.program_id(0)
    block = rows[...]
    rows_of = nn(chosen[0], block).astype(LOW)
    capacity = outs[0].shape[1]
    for e in range(local):
        outs[e][0] = rows_of[e * capacity : (e + 1) * capacity]
    part = nn(block, router[...])

    @pl.when(step == 0)
    def _():
        logits[...] = part

    @pl.when(step > 0)
    def _():
        logits[...] += part

    @pl.when(step == pl.num_programs(0) - 1)
    def _():
        values = logits[...].T
        ids = lax.broadcasted_iota(jnp.int32, (total, TOK_DEV), 0)
        weights = jnp.exp(values - jnp.max(values, axis=0, keepdims=True))
        hit = hits_of(routes, ids)
        share = weights / jnp.sum(jnp.where(hit, weights, 0.0), axis=0, keepdims=True)
        for e in range(local):
            mine = ids == info[0] * local + e
            share_row = jnp.sum(jnp.where(mine, share, 0.0), axis=0, keepdims=True)
            picked = chosen[0, e * capacity : (e + 1) * capacity].astype(WIDE)
            outs[local + e][0] = jnp.sum(picked * share_row, axis=1, keepdims=True)


def dispatch(at, info, rows, chosen, routes, router, local, earlier):
    count, height, _ = chosen.shape
    capacity = height // local
    total = router.shape[1]
    wide = D
    out_shape = [jax.ShapeDtypeStruct((count, capacity, D), LOW)] * local + [
        jax.ShapeDtypeStruct((count, capacity, 1), WIDE)
    ] * local
    if earlier is None:
        earlier = [jnp.zeros((8, 128), shape.dtype) for shape in out_shape]
        aliases = {}
    else:
        aliases = {5 + i: i for i in range(len(out_shape))}
    return pl.pallas_call(
        functools.partial(dispatch_kernel, local),
        grid=(D // wide,),
        in_specs=[
            SMEM,
            pl.BlockSpec((TOK_DEV, wide), lambda i: (0, i)),
            pl.BlockSpec((1, height, TOK_DEV), lambda i: (at, 0, 0)),
            pl.BlockSpec((1, TOP, TOK_DEV), lambda i: (at, 0, 0)),
            pl.BlockSpec((wide, total), lambda i: (i, 0)),
        ]
        + [ANY] * len(out_shape),
        out_specs=[pl.BlockSpec((1, capacity, wide), lambda i: (at, 0, i))] * local
        + [pl.BlockSpec((1, capacity, 1), lambda i: (at, 0, 0))] * local,
        scratch_shapes=[pltpu.VMEM((TOK_DEV, total), WIDE)],
        out_shape=out_shape,
        input_output_aliases=aliases,
        compiler_params=params(),
        cost_estimate=LITTLE,
        name="dispatch",
    )(info, rows, chosen, routes, router, *earlier)


def spread_kernel(local, place, *rest):
    dots, out = rest[:local], rest[local]
    spots = lax.broadcasted_iota(jnp.int32, (dots[0].shape[1], TOK_DEV), 0).astype(WIDE)
    for e in range(local):
        chosen = spots == place[0, e : e + 1]
        out[0, e : e + 1] = jnp.sum(jnp.where(chosen, dots[e][0], 0.0), axis=0, keepdims=True)


def spread(place, dots):
    count, capacity, _ = dots[0].shape
    local = len(dots)
    return pl.pallas_call(
        functools.partial(spread_kernel, local),
        grid=(count,),
        out_shape=jax.ShapeDtypeStruct((count, local, TOK_DEV), WIDE),
        in_specs=[pl.BlockSpec((1, 8, TOK_DEV), lambda i: (i, 0, 0))]
        + [pl.BlockSpec((1, capacity, 1), lambda i: (i, 0, 0))] * local,
        out_specs=pl.BlockSpec((1, local, TOK_DEV), lambda i: (i, 0, 0)),
        compiler_params=params(),
        cost_estimate=LITTLE,
        name="spread",
    )(place, *dots)


def expert_kernel(slots, info, rows, grads, shares, *rest):
    refs, (out_rows, back_rows, grad_rows, acts, dots, weight, sem) = rest[:-7], rest[-7:]
    part = weight.shape[1] // slots

    @pl.when(pl.program_id(0) == 0)
    def _():
        def copies(ref, slot):
            return [
                pltpu.make_async_copy(
                    ref.at[pl.ds(which * part, part)],
                    weight.at[which, pl.ds(pl.multiple_of(slot * part, part), part)],
                    sem,
                )
                for which in range(3)
            ]

        if len(refs) == 1:
            for slot in range(slots):
                run_all(copies(refs[0].at[slot], slot))
            for slot in range(slots):
                wait_all(copies(refs[0].at[slot], slot))
        else:
            block, second, above, below, far = refs
            low_end = info[2] == 0
            end = jnp.logical_or(low_end, info[2] == 3)
            run_all(copies(block, info[2]))
            run_all(copies(second, info[3]))

            @pl.when(low_end)
            def _():
                run_all(copies(above, info[4]))

            @pl.when(jnp.logical_not(low_end))
            def _():
                run_all(copies(below, info[4]))

            @pl.when(end)
            def _():
                run_all(copies(far, info[5]))

            @pl.when(jnp.logical_not(end))
            def _():
                run_all(copies(above, info[5]))

            for slot in range(slots):
                wait_all(copies(block, slot))

    row_block = rows[...]
    share = shares[...]
    grad_float = grads[...].astype(WIDE)
    grad_low = (share * grad_float).astype(LOW)
    grad_rows[...] = grad_low
    gate_act = nt(row_block, weight[0])
    upward = nt(row_block, weight[1])
    sigmoid = 1.0 / (1.0 + jnp.exp(-gate_act))
    silu = gate_act * sigmoid
    hidden = (silu * upward).astype(LOW)
    expert_out = nn(hidden, weight[2]).astype(LOW).astype(WIDE)
    out_rows[...] = (share * expert_out).astype(LOW)
    dots[...] = jnp.sum(grad_float * expert_out, axis=1, keepdims=True)
    grad_hidden = nt(grad_low, weight[2])
    grad_gate = (grad_hidden * upward * sigmoid * (1.0 + gate_act * (1.0 - sigmoid))).astype(LOW)
    grad_up = (grad_hidden * silu).astype(LOW)
    back_rows[...] = (nn(grad_gate, weight[0]) + nn(grad_up, weight[1])).astype(LOW)
    for which, act in enumerate((grad_gate, grad_up, hidden)):
        turned = act.T
        for slot in range(slots):
            acts[slot, which * part : (which + 1) * part] = turned[
                slot * part : (slot + 1) * part
            ]


EXPERT_ROWS = 256


def expert(info, rows, grads, shares, refs, slots):
    height = rows.shape[0]
    part = refs[0].shape[-2] // 3
    wide_block = pl.BlockSpec((EXPERT_ROWS, D), lambda i: (i, 0))
    thin_block = pl.BlockSpec((EXPERT_ROWS, 1), lambda i: (i, 0))
    return pl.pallas_call(
        functools.partial(expert_kernel, slots),
        grid=(height // EXPERT_ROWS,),
        out_shape=[jax.ShapeDtypeStruct((height, D), LOW)] * 3
        + [
            jax.ShapeDtypeStruct((slots, 3 * part, height), LOW),
            jax.ShapeDtypeStruct((height, 1), WIDE),
        ],
        in_specs=[SMEM, wide_block, wide_block, thin_block] + [ANY] * len(refs),
        out_specs=[wide_block] * 3
        + [pl.BlockSpec((slots, 3 * part, EXPERT_ROWS), lambda i: (0, 0, i)), thin_block],
        scratch_shapes=[pltpu.VMEM((3, slots * part, D), LOW), pltpu.SemaphoreType.DMA],
        compiler_params=params(),
        cost_estimate=LITTLE,
        name="expert",
    )(info, rows, grads, shares, *refs)


def expert_grads_kernel(acts, rows, grads, out):
    slots, height, _ = acts.shape
    part = height // 3
    for slot in range(slots):
        out[slot, : 2 * part] = nn(acts[slot, : 2 * part], rows[...]).astype(LOW)
        out[slot, 2 * part :] = nn(acts[slot, 2 * part :], grads[...]).astype(LOW)


def expert_grads(acts, rows, grads):
    slots, part, height = acts.shape
    strip = pl.BlockSpec((height, 256), lambda i: (0, i))
    return pl.pallas_call(
        expert_grads_kernel,
        grid=(D // 256,),
        out_shape=jax.ShapeDtypeStruct((slots, part, D), LOW),
        in_specs=[whole(acts.shape), strip, strip],
        out_specs=pl.BlockSpec((slots, part, 256), lambda i: (0, 0, i)),
        compiler_params=params(),
        cost_estimate=LITTLE,
        name="expert_gradients",
    )(acts, rows, grads)


SHARE_ROWS = 32


def combine_kernel(local, first, step, info, chosen, *rest):
    rows, dots, out = rest[:local], rest[local:-6], rest[-6]
    picks, rows_in, out_block, sem_in, sem_out = rest[-5:]
    number = out.shape[0]
    capacity = rows[0].shape[1]
    copies = []
    for n in range(number):
        q = first + step * n
        copies.append(
            [pltpu.make_async_copy(chosen.at[q], picks.at[n], sem_in.at[n, local])]
            + [
                pltpu.make_async_copy(
                    rows[e].at[q],
                    rows_in.at[n, pl.ds(e * capacity, capacity)],
                    sem_in.at[n, e],
                )
                for e in range(local)
            ]
        )
    for group in copies:
        run_all(group)
    sent = []
    for n in range(number):
        wait_all(copies[n])
        out_block[n, :TOK_DEV] = tn(picks[n], rows_in[n]).astype(LOW)
        if dots:
            row = lax.broadcasted_iota(jnp.int32, (SHARE_ROWS, D), 0)
            values = jnp.zeros((SHARE_ROWS, D), WIDE)
            for e in range(local):
                picked = picks[n, e * capacity : (e + 1) * capacity].astype(WIDE)
                share = picked * dots[e][first + step * n]
                high, low = split(jnp.sum(share, axis=0, keepdims=True))
                pieces = [high.astype(WIDE), low.astype(WIDE)]
                pieces.append(jnp.zeros((1, D - 2 * TOK_DEV), WIDE))
                line = jnp.concatenate(pieces, axis=1)
                values = jnp.where(row == info[0] * local + e, line, values)
            out_block[n, TOK_DEV:] = values.astype(LOW)
        copy = pltpu.make_async_copy(out_block.at[n], out.at[n], sem_out.at[n])
        copy.start()
        sent.append(copy)
    wait_all(sent)


def combine(info, chosen, rows, first, step, dots=()):
    count, capacity, _ = rows[0].shape
    local = len(rows)
    number = (count - first + step - 1) // step
    height = TOK_DEV + (SHARE_ROWS if dots else 0)
    return pl.pallas_call(
        functools.partial(combine_kernel, local, first, step),
        out_shape=jax.ShapeDtypeStruct((number, height, D), LOW),
        in_specs=[SMEM, ANY]
        + [ANY] * local
        + [pl.BlockSpec(memory_space=pltpu.VMEM)] * len(dots),
        out_specs=ANY,
        scratch_shapes=[
            pltpu.VMEM((number, local * capacity, TOK_DEV), LOW),
            pltpu.VMEM((number, local * capacity, D), LOW),
            pltpu.VMEM((number, height, D), LOW),
            pltpu.SemaphoreType.DMA((number, local + 1)),
            pltpu.SemaphoreType.DMA((number,)),
        ],
        compiler_params=params(),
        cost_estimate=LITTLE,
        name="combine",
    )(info, chosen, *rows, *dots)


def chip_adds_kernel(keep, got, send_x, send_y, near_x, near_y, one, two, sem_in, sem_out):
    half = send_x.shape[1]
    copies = [
        (
            pltpu.make_async_copy(keep.at[i], one.at[i], sem_in.at[i, 0]),
            pltpu.make_async_copy(got.at[i], two.at[i], sem_in.at[i, 1]),
        )
        for i in range(4)
    ]
    for pair in copies:
        run_all(pair)
    sent = []
    for i in range(4):
        wait_all(copies[i])
        one[i] = (one[i].astype(WIDE) + two[i].astype(WIDE)).astype(LOW)
        upper = (near_x, send_x)[i % 2].at[i // 2]
        lower = (near_y, send_y)[i // 2].at[i % 2]
        for part, to in enumerate((upper, lower)):
            copy = pltpu.make_async_copy(
                one.at[i, pl.ds(part * half, half)], to, sem_out.at[i, part]
            )
            copy.start()
            sent.append(copy)
    wait_all(sent)


def chip_adds(keep, got):
    _, height, width = keep.shape
    shape = jax.ShapeDtypeStruct((2, height // 2, width), LOW)
    return pl.pallas_call(
        chip_adds_kernel,
        out_shape=(shape,) * 4,
        in_specs=[ANY, ANY],
        out_specs=(ANY,) * 4,
        scratch_shapes=[
            pltpu.VMEM(keep.shape, LOW),
            pltpu.VMEM(keep.shape, LOW),
            pltpu.SemaphoreType.DMA((4, 2)),
            pltpu.SemaphoreType.DMA((4, 2)),
        ],
        compiler_params=params(),
        cost_estimate=LITTLE,
        name="chip_sums",
    )(keep, got)


def corner_adds_kernel(near_x, got_x, near_y, got_y, send_y, send_x):
    send_y[...] = (near_x[0].astype(WIDE) + got_x[0].astype(WIDE)).astype(LOW)
    send_x[...] = (near_y[0].astype(WIDE) + got_y[0].astype(WIDE)).astype(LOW)


def corner_adds(near_x, got_x, near_y, got_y):
    _, half, width = near_x.shape
    rows = half
    block = pl.BlockSpec((1, rows, width), lambda i: (1, i, 0))
    out = pl.BlockSpec((rows, width), lambda i: (i, 0))
    return pl.pallas_call(
        corner_adds_kernel,
        grid=(half // rows,),
        out_shape=(jax.ShapeDtypeStruct((half, width), LOW),) * 2,
        in_specs=[block] * 4,
        out_specs=(out, out),
        compiler_params=params(),
        cost_estimate=LITTLE,
        name="corner_sums",
    )(near_x, got_x, near_y, got_y)


def split(values):
    high = values.astype(LOW)
    return high, (values - high.astype(WIDE)).astype(LOW)


def norm_back(values, gain, grad):
    factor = lax.rsqrt(jnp.mean(values * values, axis=-1, keepdims=True) + EPSILON)
    scaled = gain * grad
    mean = jnp.mean(values * scaled, axis=-1, keepdims=True)
    grad_values = factor * scaled - values * (factor * factor * factor * mean)
    grad_gain = jnp.sum(grad * values * factor, axis=0, keepdims=True)
    return grad_values, grad_gain


def router_back(logits, routes, grad_shares):
    ids = lax.broadcasted_iota(jnp.int32, logits.shape, 0)
    hit = ids == routes[0:1]
    for k in range(1, TOP):
        hit = jnp.logical_or(hit, ids == routes[k : k + 1])
    weights = jnp.exp(logits - jnp.max(logits, axis=0, keepdims=True))
    probs = weights / jnp.sum(weights, axis=0, keepdims=True)
    chosen = jnp.sum(jnp.where(hit, probs, 0.0), axis=0, keepdims=True)
    grads = jnp.where(hit, grad_shares, 0.0)
    mean = jnp.sum(probs * grads, axis=0, keepdims=True) / chosen
    grad_probs = jnp.where(hit, (grads - mean) / chosen, 0.0)
    return probs * (grad_probs - jnp.sum(probs * grad_probs, axis=0, keepdims=True))


def branch_back_kernel(
    parts, info, residual, normed, cotangent, routes, router, gain, *rest
):
    sums, rest = rest[:parts], rest[parts:]
    experts = router.shape[0]
    count = len(rest) - 7
    refs = rest[:count]
    grad_residual, grad_branch, grad_heads, grad_gain, grad_router, weight, sem = rest[count:]

    @pl.when(pl.program_id(0) == 0)
    def _():
        copies = weight_copies(info, refs, weight, sem, D // QUARTERS + 128, D // QUARTERS)
        run_all(copies)
        logits = nt(router[...], normed[...])
        if parts == 2:
            back_sum, grad_shares = sums[0][...], sums[1][...]
        else:
            values = [
                (ref[0] if len(ref.shape) == 3 else ref[...]).astype(WIDE) for ref in sums
            ]
            upper = values[0] + values[1] + values[2]
            lower = values[3] + values[4] + values[5]
            last = lower.shape[0] - SHARE_ROWS
            shares = lower[last : last + experts]
            grad_shares = shares[:, :TOK_DEV] + shares[:, TOK_DEV : 2 * TOK_DEV]
            back_sum = jnp.concatenate([upper, lower[:last]], axis=0)
        high, low = split(router_back(logits, routes[...], grad_shares))
        grad_router[...] = nn(high, normed[...]) + nn(low, normed[...])
        grad_normed = tn(high, router[...]) + tn(low, router[...])
        grad_normed += back_sum
        grad_values, gain_grad = norm_back(residual[...], gain[...], grad_normed)
        grad_gain[...] = gain_grad
        total = cotangent[...].astype(WIDE) + grad_values
        grad_residual[...] = total
        grad_branch[...] = total.astype(LOW)
        wait_all(copies)

    at = pl.ds(pl.multiple_of(pl.program_id(0) * STEP, STEP), STEP)
    grad_heads[...] = nt(grad_branch[...], weight[at, :]).astype(LOW)


def branch_back(info, residual, normed, sums, cotangent, routes, router, gain, refs):
    full = (TOK_DEV, D)
    total = router.shape[0]
    return pl.pallas_call(
        functools.partial(branch_back_kernel, len(sums)),
        grid=(D // STEP,),
        out_shape=(
            jax.ShapeDtypeStruct(full, WIDE),
            jax.ShapeDtypeStruct(full, LOW),
            jax.ShapeDtypeStruct(full, LOW),
            jax.ShapeDtypeStruct((1, D), WIDE),
            jax.ShapeDtypeStruct((total, D), WIDE),
        ),
        in_specs=[SMEM]
        + [whole(full)] * 3
        + [whole((TOP, TOK_DEV)), whole((total, D)), whole((1, D))]
        + [whole(part.shape if part.ndim == 2 else (1,) + part.shape[1:]) for part in sums]
        + [ANY] * len(refs),
        out_specs=(
            whole(full),
            whole(full),
            pl.BlockSpec((TOK_DEV, STEP), lambda i: (0, i)),
            whole((1, D)),
            whole((total, D)),
        ),
        scratch_shapes=[pltpu.VMEM((D, D), LOW), pltpu.SemaphoreType.DMA],
        compiler_params=params(),
        cost_estimate=LITTLE,
        name="experts_norm_back",
    )(info, residual, normed, cotangent, routes, router, gain, *sums, *refs)


def join_grads_kernel(info, own_grad, source_grad, arrived, cosine, sine, out):
    half = HEAD_DIM // 2
    first = lax.broadcasted_iota(jnp.int32, (TOK_DEV, HEAD_DIM), 1) < half
    leaves = info[1] == 0

    def total(column):
        columns = slice(column, column + 128)
        extra = source_grad[:, columns] + arrived[:, columns].astype(WIDE)
        return own_grad[:, columns] + jnp.where(leaves, 0.0, extra)

    for g in range(KV_HEADS):
        key = turn_back(total(128 * g), cosine[...], sine[...])
        value = total(KEY_WIDTH + 128 * g)
        out[:, 256 * g : 256 * g + 128] = jnp.where(
            first, key, pltpu.roll(value, half, 1)
        ).astype(LOW)
        out[:, 256 * g + 128 : 256 * g + 256] = jnp.where(
            first, pltpu.roll(key, half, 1), value
        ).astype(LOW)


def join_grads(info, own_grad, source_grad, arrived, cosine, sine):
    vmem = pl.BlockSpec(memory_space=pltpu.VMEM)
    return pl.pallas_call(
        join_grads_kernel,
        out_shape=jax.ShapeDtypeStruct((TOK_DEV, 2 * KEY_WIDTH), LOW),
        in_specs=[SMEM] + [vmem] * 5,
        out_specs=vmem,
        compiler_params=params(),
        cost_estimate=LITTLE,
        name="join_key_value_gradients",
    )(info, own_grad, source_grad, arrived, cosine, sine)


def normed_grad_kernel(info, grad_query, *rest):
    refs, (out, weight, sem) = rest[:-3], rest[-3:]

    @pl.when(pl.program_id(0) == 0)
    def _():
        copies = weight_copies(info, refs, weight, sem, 0, D // QUARTERS)
        run_all(copies)
        wait_all(copies)

    at = pl.ds(pl.multiple_of(pl.program_id(0) * STEP, STEP), STEP)
    out[...] = nt(grad_query[...], weight[at, :])


def normed_grad(info, grad_query, refs):
    return pl.pallas_call(
        normed_grad_kernel,
        grid=(D // STEP,),
        out_shape=jax.ShapeDtypeStruct((TOK_DEV, D), WIDE),
        in_specs=[SMEM, whole((TOK_DEV, D))] + [ANY] * len(refs),
        out_specs=pl.BlockSpec((TOK_DEV, STEP), lambda i: (0, i)),
        scratch_shapes=[pltpu.VMEM((D, D), LOW), pltpu.SemaphoreType.DMA],
        compiler_params=params(),
        cost_estimate=LITTLE,
        name="normed_gradient",
    )(info, grad_query, *refs)


def token_back_kernel(info, query_part, grad_pair, tokens, grad_residual, gain, *rest):
    refs, (out, grad_gain, weight, sem) = rest[:-4], rest[-4:]
    copies = weight_copies(info, refs, weight, sem, D // QUARTERS, 128)
    run_all(copies)
    wait_all(copies)
    grad_normed = query_part[...] + nt(grad_pair[...], weight[...])
    grad_values, gain_grad = norm_back(tokens[...].astype(WIDE), gain[...], grad_normed)
    grad_gain[...] = gain_grad
    out[...] = (grad_residual[...] + grad_values).astype(LOW)


def token_back(info, query_part, grad_pair, tokens, grad_residual, gain, refs):
    full = (TOK_DEV, D)
    vmem = pl.BlockSpec(memory_space=pltpu.VMEM)
    return pl.pallas_call(
        token_back_kernel,
        out_shape=(jax.ShapeDtypeStruct(full, LOW), jax.ShapeDtypeStruct((1, D), WIDE)),
        in_specs=[SMEM] + [vmem] * 5 + [ANY] * len(refs),
        out_specs=(vmem, vmem),
        scratch_shapes=[
            pltpu.VMEM((D, 2 * KEY_WIDTH), LOW),
            pltpu.SemaphoreType.DMA,
        ],
        compiler_params=params(),
        cost_estimate=LITTLE,
        name="token_gradient",
    )(info, query_part, grad_pair, tokens, grad_residual, gain, *refs)


def weight_grads_kernel(parts, whole_rows, info, *rest):
    ins, (keep, send) = rest[:-2], rest[-2:]
    depth = D // 8
    core = info[0] & 1
    chip = pl.program_id(0) ^ (info[0] >> 1)
    for strip_at, grads_at, start, width in parts:
        low = tn(ins[strip_at][...], ins[grads_at][...]).astype(LOW)
        columns = slice(start, start + width)
        for slot in range(QUARTERS):
            for j in range(QUARTERS):

                @pl.when(info[2 + slot] == j)
                def _():
                    piece = low[:, j * width : (j + 1) * width]
                    upper, lower = piece[:depth], piece[depth:]
                    keep[0, slot, :depth, columns] = jnp.where(core == 0, upper, lower)
                    send[0, slot, :depth, columns] = jnp.where(core == 0, lower, upper)
                    if not whole_rows:
                        blank = jnp.zeros((EXTRA, width), LOW)
                        keep[0, slot, depth:, columns] = blank
                        send[0, slot, depth:, columns] = blank

    if whole_rows:
        extra = ins[-1]
        for slot in range(QUARTERS):
            to = info[2 + slot]
            keep[0, slot, depth:] = extra[(chip * 2 + core) * QUARTERS + to]
            send[0, slot, depth:] = extra[(chip * 2 + 1 - core) * QUARTERS + to]


def weight_grads(info, strips, grads, parts, extra, earlier=()):
    depth = D // 8
    strip = pl.BlockSpec((TOK_DEV, 2 * depth), lambda i, info: (0, i ^ (info[0] >> 1)))
    more = [] if extra is None else [extra]
    width = 2 * D // QUARTERS + 128
    shape = (4, QUARTERS, depth + EXTRA, width)
    if earlier:
        out = pl.BlockSpec((1, QUARTERS, depth + EXTRA, 128), lambda i, info: (i, 0, 0, 3))
    else:
        out = pl.BlockSpec((1,) + shape[1:], lambda i, info: (i, 0, 0, 0))
    inputs = [*strips, *grads, *more]

    def kernel(info, *rest):
        count = len(inputs)
        weight_grads_kernel(
            parts, extra is not None, info, *rest[:count], *rest[count + len(earlier) :]
        )

    return pl.pallas_call(
        kernel,
        grid_spec=pltpu.PrefetchScalarGridSpec(
            num_scalar_prefetch=1,
            grid=(4,),
            in_specs=[strip] * len(strips)
            + [
                pl.BlockSpec(a.shape, lambda i, info, n=a.ndim: (0,) * n)
                for a in (*grads, *more)
            ]
            + [ANY] * len(earlier),
            out_specs=(out, out),
        ),
        out_shape=(jax.ShapeDtypeStruct(shape, LOW),) * 2,
        input_output_aliases={1 + len(inputs) + i: i for i in range(len(earlier))},
        compiler_params=params(),
        cost_estimate=LITTLE,
        name="weight_gradients",
    )(info, *inputs, *earlier)


def last_sums_kernel(part, info, own, *rest):
    arrived, (query_out, key_out, value_out, out_out, extra_out) = rest[:-5], rest[-5:]
    total = own[...].astype(WIDE)
    for ref in arrived[:-1]:
        total += ref[...].astype(WIDE)
    end = jnp.logical_or(info[2] == 0, info[2] == 3)
    total += jnp.where(end, arrived[-1][...].astype(WIDE), 0.0)
    depth = query_out.shape[0]
    quarter = query_out.shape[1]
    query_out[...] = total[:depth, :quarter]
    pair = total[:depth, quarter : quarter + 2 * part].T
    key_out[...] = pair[:part]
    value_out[...] = pair[part:]
    out_out[...] = total[:depth, quarter + 2 * part :]
    extra_out[...] = total[depth:]


def last_sums(info, own, arrived, depth, part):
    height, width = own.shape
    quarter = D // QUARTERS
    vmem = pl.BlockSpec(memory_space=pltpu.VMEM)
    return pl.pallas_call(
        functools.partial(last_sums_kernel, part),
        out_shape=(
            jax.ShapeDtypeStruct((depth, quarter), WIDE),
            jax.ShapeDtypeStruct((part, depth), WIDE),
            jax.ShapeDtypeStruct((part, depth), WIDE),
            jax.ShapeDtypeStruct((depth, quarter), WIDE),
            jax.ShapeDtypeStruct((height - depth, width), WIDE),
        ),
        in_specs=[SMEM] + [vmem] * (1 + len(arrived)),
        out_specs=(vmem,) * 5,
        compiler_params=params(),
        cost_estimate=LITTLE,
        name="last_sums",
    )(info, own, *arrived)


def position_of(token_index):
    branch_place = TRUNK + (token_index - TRUNK) % BRANCH
    leaf_place = TRUNK + BRANCH + (token_index - TOK_DEV) % BRANCH
    return jnp.where(
        token_index < TRUNK, token_index, jnp.where(token_index < TOK_DEV, branch_place, leaf_place)
    )


def rotary_tables(positions):
    half_dim = HEAD_DIM // 2
    frequency = ROPE_BASE ** (-jnp.arange(half_dim, dtype=jnp.float32) / half_dim)
    angles = positions.astype(jnp.float32)[:, None] * frequency[None, :]
    cosine, sine = (jnp.cos(angles), jnp.sin(angles))
    return (
        jnp.concatenate([cosine, cosine], axis=1),
        jnp.concatenate([-sine, sine], axis=1),
    )


def after(values, *earlier):
    return lax.optimization_barrier((values, earlier))[0]


def fast_mesh():
    return lax.axis_size("rows") == 8 and lax.axis_size("cols") == 4


SLOT_SHARD = ((0, 2, 1, 3), (1, 3, 0, 2), (2, 0, 1, 3), (3, 1, 2, 0))
UP = [(0, 1), (1, 2), (2, 3)]
DOWN = [(1, 0), (2, 1), (3, 2)]
FAR = [(0, 3), (3, 0)]


def send_near(block):
    return lax.ppermute(block, "cols", DOWN), lax.ppermute(block, "cols", UP)


def send_far(block):
    return lax.ppermute(block, "cols", FAR)


def send_over(block):
    return lax.ppermute(block, "cols", [(0, 2), (1, 3), (2, 0), (3, 1)])


def send_second(block, near):
    place = lax.axis_index("cols")
    above, below = near
    payload = jnp.where(place == 1, above, jnp.where(place == 2, below, block))
    return lax.ppermute(payload, "cols", [(3, 1), (1, 0), (0, 2), (2, 3)])


def slot_list(block, near, second, far):
    place = lax.axis_index("cols")
    above, below = near
    end = (place == 0) | (place == 3)
    return [
        block,
        second,
        jnp.where(place == 0, above, below),
        jnp.where(end, far, above),
    ]


def send_slots(slots):
    place = lax.axis_index("cols")
    _, second, third, fourth = slots
    relay = lax.ppermute(second, "cols", [(1, 3), (0, 1), (2, 0), (3, 2)])
    relayed = relay.astype(WIDE)
    upward_load = (
        jnp.where(place == 0, third, fourth).astype(WIDE) + jnp.where(place == 1, relayed, 0.0)
    ).astype(LOW)
    downward_load = (third.astype(WIDE) + jnp.where(place == 2, relayed, 0.0)).astype(LOW)
    return (
        lax.ppermute(upward_load, "cols", UP),
        lax.ppermute(downward_load, "cols", DOWN),
        send_far(after(fourth, upward_load, downward_load)),
        relay,
    )


def flip(block, bit):
    count = lax.axis_size("rows")
    return lax.ppermute(block, "rows", [(i, i ^ bit) for i in range(count)])


def add_low(one, two):
    return (one.astype(WIDE) + two.astype(WIDE)).astype(LOW)


def chips_second(near_x, near_y, got_x, got_y):
    for_y, for_x = corner_adds(near_x, got_x, near_y, got_y)
    return (near_x, got_x, flip(for_y, 4), near_y, got_y, flip(for_x, 2))


def turn_corner(beside, across):
    half = beside.shape[0] // 2
    return jnp.concatenate([flip(beside[:half], 4), flip(across[half:], 2)], axis=0)


def send_chips(sums):
    return flip(sums[0], 2), flip(sums[1], 4)


def sum_parts(parts):
    wide = [(a[0] if a.ndim == 3 else a).astype(WIDE) for a in parts]
    if len(wide) == 1:
        return wide[0]
    return jnp.concatenate([wide[0] + wide[1] + wide[2], wide[3] + wide[4] + wide[5]], axis=0)


def on_device(
    tokens,
    query_weight,
    key_weight,
    value_weight,
    out_weight,
    router_weight,
    attention_gain,
    experts_gain,
    gate_weight,
    upward_weight,
    down_weight,
    routes,
    leaf_parent,
    cotangent,
):
    row_count = lax.axis_size("rows")
    col_count = lax.axis_size("cols")
    row_place = lax.axis_index("rows")
    col_place = lax.axis_index("cols")
    fast = fast_mesh()
    parity = lax.rem(col_place, 2)
    tree_id = lax.div(row_place * col_count + col_place, 2)
    parent_row = lax.dynamic_slice_in_dim(leaf_parent, tree_id, 1, 0)[0]
    depth, query_part = query_weight.shape
    key_part = key_weight.shape[1]
    router_part = router_weight.shape[1]
    gain_part = attention_gain.shape[0]
    expert_total = router_part * col_count
    local_experts = gate_weight.shape[0]
    capacity = TOK_DEV * TOP // expert_total * 5 // 4

    shards = (
        jnp.asarray(SLOT_SHARD, jnp.int32)[col_place]
        if fast
        else jnp.arange(4, dtype=jnp.int32)
    )
    branch_rows = jnp.where(parity == 0, TRUNK + BRANCH * parent_row, TRUNK)
    info = jnp.concatenate(
        [jnp.stack([row_place, parity]), shards, branch_rows, jnp.zeros((2,), jnp.int32)]
    ).astype(jnp.int32)

    packed = jnp.concatenate([query_weight, key_weight, value_weight, out_weight], axis=1)
    local_index = (1 - parity) * TOK_DEV + jnp.arange(TOK_DEV, dtype=jnp.int32)
    cosine, sine = rotary_tables(position_of(local_index))
    shard_blocks = [
        jnp.concatenate(
            [gate_weight[expert].T, upward_weight[expert].T, down_weight[expert]], axis=0
        )
        for expert in range(local_experts)
    ]
    expert_refs = []
    if fast:
        wide = packed.shape[1]
        gains = jnp.concatenate([attention_gain, experts_gain])[None, :]
        packed = jnp.concatenate(
            [
                packed,
                jnp.pad(router_weight.T, ((0, 0), (0, wide - depth))),
                jnp.pad(gains, ((0, 0), (0, wide - 2 * gain_part))),
                jnp.pad(routes.T.astype(LOW), ((0, 0), (0, wide - TOK_DEV))),
                jnp.zeros((EXTRA - router_part - 1 - TOP, wide), LOW),
            ],
            axis=0,
        )
        packed_near = send_near(packed)
        packed_far = send_far(packed)
        packed_second = send_over(packed)
        first_block = after(shard_blocks[0], *packed_near)
        first_near = send_near(first_block)
        first_second = send_second(first_block, first_near)
        own = jnp.stack(slot_list(packed, packed_near, packed_second, packed_far))
        own = after(own, info, cosine, sine)
        beside, across = flip(own, 2), flip(own, 4)
        own_in = flip(own, 1)
        beside, across = after((beside, across), own_in, *first_near)
        corner = [flip(beside[:2], 4), flip(across[2:], 2)]
        pair_in = flip(jnp.concatenate([beside, across], axis=0), 1)
        corner_in = [flip(piece, 1) for piece in corner]
        grad_in = after(cotangent, *corner)
        grad_flips = [flip(grad_in, 2), flip(grad_in, 4)]
        pieces = [own, own_in, beside, across, *corner, pair_in, *corner_in]
        at = depth + router_part + 1
        near_slots = [own, own_in, beside, pair_in, across, pair_in[4:], corner[0], corner_in[0]]
        routes_all = jnp.stack([part[0, at : at + TOP, :TOK_DEV] for part in near_slots])
        routes_all = routes_all.astype(jnp.int32)
        chosen, place_rows = tables(info, routes_all, capacity, local_experts, expert_total)
        query_refs = pair_refs = out_refs = pieces
        extra_rows = extras(info, pieces)
        router_all = extra_rows[:, :router_part, :depth]
        attention_scale = extra_rows[:, router_part, :gain_part]
        experts_scale = extra_rows[:, router_part, gain_part : 2 * gain_part]
    else:
        packed_all = lax.all_gather(lax.all_gather(packed, "cols", axis=0), "rows", axis=0)

        def unpack(start, width):
            part = packed_all[..., start : start + width]
            return jnp.swapaxes(part, 1, 2).reshape(row_count * depth, col_count * width)

        key_at = query_part
        query_refs = [unpack(0, query_part)]
        pair_refs = [
            jnp.concatenate(
                [
                    unpack(key_at, key_part).reshape(D, QUARTERS, -1),
                    unpack(key_at + key_part, key_part).reshape(D, QUARTERS, -1),
                ],
                axis=2,
            ).reshape(D, -1)
        ]
        out_refs = [unpack(key_at + 2 * key_part, query_part)]
        routes_all = lax.all_gather(routes.T, "rows", axis=0)
        chosen, place_rows = tables(info, routes_all, capacity, local_experts, expert_total)
        axes = ("rows", "cols")
        router_all = jnp.swapaxes(lax.all_gather(router_weight, axes, axis=0), 1, 2)
        attention_scale = lax.all_gather(attention_gain, axes, axis=0)
        experts_scale = lax.all_gather(experts_gain, axes, axis=0)

    attention_scale = attention_scale.reshape(1, D).astype(WIDE)
    experts_scale = experts_scale.reshape(1, D).astype(WIDE)
    router_rows = jnp.transpose(
        router_all.reshape(row_count, col_count, router_part, depth), (1, 2, 0, 3)
    ).reshape(expert_total, D)
    router_cols = router_rows.T
    tokens_in = after(tokens, first_second, chosen) if fast else tokens
    normed, own_pair = key_value(info, tokens_in, attention_scale, cosine, sine, pair_refs)
    pairs = [(i + 1, i) for i in range(0, col_count, 2)]
    partner = lax.ppermute(own_pair, "cols", pairs)
    if fast:
        own_grad_in = flip(grad_in, 1)
        normed_in = after(normed, own_grad_in)
    else:
        normed_in = normed
    queries = query(info, normed_in, cosine, sine, query_refs)
    if fast:
        first_far = send_far(after(first_block, partner, queries))
        expert_refs.append([first_block, first_second, *first_near, first_far])
    if fast:
        grad_flips = after(grad_flips, queries)
        grad_corner = turn_corner(*grad_flips)
    heads = attention(info, queries, own_pair, partner)
    if fast:
        grad_near = [*grad_flips, grad_corner]
        grad_blocks = [cotangent, own_grad_in]
        grad_blocks += [block for one in grad_near for block in (one, flip(one, 1))]
        heads = after(heads, grad_corner, grad_blocks[3], grad_blocks[5])
    else:
        grad_all = lax.all_gather(cotangent, "rows", axis=0)
        grad_blocks = [grad_all[q] for q in range(row_count)]
    residual, normed_two = out_projection(info, heads, tokens, experts_scale, out_refs)

    if fast:
        beside, across = flip(normed_two, 2), flip(normed_two, 4)
        beside_in = flip(after(normed_two, *grad_blocks), 1)
        later_block = after(shard_blocks[1], first_far, normed_two)
        expert_refs.append([lax.all_gather(later_block, "cols", axis=0)])
    else:
        rows_all = lax.all_gather(normed_two, "rows", axis=0)
        expert_refs = [[lax.all_gather(block, "cols", axis=0)] for block in shard_blocks]
    grad_rows = pick_rows(chosen, grad_blocks, local_experts)

    def place_block(q, block, picked):
        return dispatch(
            q, info, block, chosen, routes_all, router_cols, local_experts, picked
        )

    if fast:
        half = TOK_DEV // 2
        picked = place_block(0, normed_two, None)
        picked = place_block(1, beside_in, after(picked, *grad_rows))
        beside, across = after((beside, across), picked)
        corner = [flip(beside[:half], 4), flip(across[half:], 2)]
        picked = place_block(2, beside, picked)
        picked = place_block(4, across, picked)
        beside_in = flip(beside, 1)
        across_in = flip(across, 1)
        picked = place_block(3, beside_in, picked)
        picked = place_block(5, across_in, picked)
        corner = jnp.concatenate(after(corner, picked), axis=0)
        corner_in = flip(corner, 1)
        picked = place_block(6, corner, picked)
        picked = place_block(7, corner_in, picked)
    else:
        picked = None
        for q in range(row_count):
            picked = place_block(q, rows_all[q], picked)
    height = row_count * capacity
    token_rows = [a.reshape(height, D) for a in picked[:local_experts]]
    grad_rows = [a.reshape(height, D) for a in grad_rows]
    share_rows = [a.reshape(height, 1) for a in picked[local_experts:]]

    out_rows, back_rows, gate_dots, reduced = ([], [], [], [])
    for e in range(local_experts):
        rows_in = after(token_rows[e], *reduced_in) if e else token_rows[e]
        out_row, back_row, grad_row, acts, dots = expert(
            info, rows_in, grad_rows[e], share_rows[e], expert_refs[e], col_count
        )
        out_rows.append(out_row.reshape(row_count, capacity, D))
        back_rows.append(back_row.reshape(row_count, capacity, D))
        gate_dots.append(dots.reshape(row_count, capacity, 1))
        if fast and e == 1:
            got = flip(combine(info, chosen, back_rows, 1, 2, gate_dots), 1)
            back_keep = combine(info, chosen, back_rows, 0, 2, gate_dots)
            for_x, for_y, near_x, near_y = chip_adds(back_keep, got)
            acts = after(acts, for_x)
            back_flips = send_chips((for_x, for_y))
        slots = expert_grads(acts, token_rows[e], grad_row)
        reduced_in = (slots,)
        if e and fast:
            out_got = flip(combine(info, chosen, out_rows, 1, 2), 1)
            out_keep = combine(info, chosen, out_rows, 0, 2)
            back_flips = after(back_flips, slots, out_keep)
            back_parts = chips_second(near_x, near_y, *back_flips)
        else:
            reduced.append(lax.psum_scatter(slots, "cols", scatter_dimension=0, tiled=False))

    if fast:
        out_first = chip_adds(out_keep, out_got)
        back_parts = after(back_parts, out_first[0])
    else:
        spread_dots = spread(place_rows, gate_dots)
        grad_shares = lax.all_to_all(spread_dots, "rows", split_axis=0, concat_axis=0, tiled=True)

        def summed(rows):
            part = combine(info, chosen, rows, 0, 1)
            return lax.psum_scatter(part, "rows", scatter_dimension=0).astype(WIDE)

        back_parts = (summed(back_rows), grad_shares.reshape(expert_total, TOK_DEV))
        mixture = (summed(out_rows),)

    grad_residual, grad_branch, grad_heads, experts_gain_grad, router_grad = branch_back(
        info,
        residual,
        normed_two,
        back_parts,
        cotangent,
        routes.T,
        router_rows,
        experts_scale,
        out_refs,
    )
    if fast:
        out_flips = send_chips(after(out_first[:2], back_parts[2], back_parts[5]))
        slots = after(slots, reduced[0], back_parts[2])
        reduced.append(lax.psum_scatter(slots, "cols", scatter_dimension=0, tiled=False))
        router_parts = jnp.transpose(
            router_grad.astype(LOW).reshape(col_count, router_part, row_count, depth),
            (2, 0, 1, 3),
        ).reshape(row_count * col_count, router_part, depth)
        gain_rows = experts_gain_grad.astype(LOW).reshape(row_count * col_count, 1, gain_part)
        extra = jnp.concatenate(
            [
                jnp.pad(router_parts, ((0, 0), (0, 0), (0, wide - depth))),
                jnp.pad(gain_rows, ((0, 0), (0, 0), (0, wide - gain_part))),
                jnp.zeros((row_count * col_count, EXTRA - router_part - 1, wide), LOW),
            ],
            axis=1,
        )
    grad_query, own_grad, source_grad = attention_back(
        info, queries, own_pair, partner, grad_heads, cosine, sine
    )
    arrived = lax.ppermute(source_grad.astype(LOW), "cols", [(j, i) for i, j in pairs])
    if fast:
        parts = ((0, 2, 0, query_part), (1, 3, query_part + 2 * key_part, query_part))
        keep_send = weight_grads(
            info, [normed, heads], [grad_query, grad_branch], parts, extra
        )
        near_x, near_y = out_first[2:]
        for_y, for_x = corner_adds(
            near_x, after(out_flips[0], *keep_send), near_y, out_flips[1]
        )
        mixture = (near_x, out_flips[0], flip(for_y, 4))
        mixture += (near_y, out_flips[1], flip(for_x, 2))
        query_back = normed_grad(info, after(grad_query, for_y), query_refs)
        arrived = after(arrived, query_back)
    else:
        query_back = normed_grad(info, grad_query, query_refs)
    grad_pair = join_grads(info, own_grad, source_grad, arrived, cosine, sine)
    if fast:
        keep, send = weight_grads(
            info, [normed], [grad_pair], ((0, 1, 0, 2 * key_part),), None, keep_send
        )
        flat = (4, col_count * (depth + EXTRA), wide)
        sent = flip(send, 1)
        sent_first = chip_adds(keep.reshape(flat), sent.reshape(flat))
        sent_chips = send_chips(sent_first[:2])
        grad_pair = after(grad_pair, sent_first[0])
    tokens_grad, attention_gain_grad = token_back(
        info, query_back, grad_pair, tokens, grad_residual, attention_scale, pair_refs
    )

    if fast:
        sent_chips = after(sent_chips, tokens_grad)
        sent_parts = chips_second(*sent_first[2:], *sent_chips)
    layer_output = (residual + sum_parts(mixture)).astype(LOW)
    part = down_weight.shape[1]
    expert_sums = [block.astype(WIDE) for block in reduced]
    gate_grad, upward_grad, down_grad = (
        jnp.stack([sums_of[which * part : (which + 1) * part] for sums_of in expert_sums])
        for which in range(3)
    )
    gate_grad, upward_grad = jnp.swapaxes(gate_grad, 1, 2), jnp.swapaxes(upward_grad, 1, 2)
    if fast:
        slots = sum_parts(sent_parts)
        slots = slots.reshape(col_count, depth + EXTRA, wide)
        width = query_part + 2 * key_part
        own_slots = own
        gain_sums = sum(
            jnp.sum(own_slots[i][:depth, :width].astype(WIDE) * slots[i, :depth, :width], axis=1)
            for i in range(4)
        )
        own_gains = lax.dynamic_slice_in_dim(attention_scale[0], row_place * depth, depth, 0)
        gain_sums = (gain_sums / own_gains).reshape(col_count, 1, gain_part)
        gain_sums = jnp.pad(
            jnp.take(gain_sums, shards, axis=0),
            ((0, 0), (depth + router_part + 1, EXTRA - router_part - 2), (0, wide - gain_part)),
        )
        slots = after((slots + gain_sums).astype(LOW), reduced[1])

        arrived = send_slots(slots)
        earlier = (gate_grad, upward_grad, down_grad, layer_output)
        query_sum, key_sum, value_sum, out_sum, extra_sum = last_sums(
            info, slots[0], after(arrived, *earlier), depth, key_part
        )
        key_sum, value_sum = key_sum.T, value_sum.T
        router_sum = extra_sum[:router_part, :depth].T
        experts_gain_sum = extra_sum[router_part, :gain_part]
        attention_gain_sum = extra_sum[router_part + 1, :gain_part]
    else:
        full_grads = [
            tn(normed, grad_query),
            *jnp.moveaxis(tn(normed, grad_pair).reshape(D, QUARTERS, 2, -1), 2, 0),
            tn(heads, grad_branch),
        ]
        packed_grad = jnp.concatenate(
            [
                grad.astype(LOW).reshape(row_count, depth, col_count, -1)
                for grad in full_grads
            ],
            axis=3,
        )
        row_sums = lax.psum_scatter(packed_grad, "rows", scatter_dimension=0)
        sums = lax.psum_scatter(row_sums, "cols", scatter_dimension=1).astype(WIDE)
        key_at = query_part
        value_at = key_at + key_part
        out_at = value_at + key_part
        query_sum, out_sum = sums[:, :key_at], sums[:, out_at:]
        key_sum, value_sum = sums[:, key_at:value_at], sums[:, value_at:out_at]
        small_grads = jnp.concatenate(
            [
                attention_gain_grad.reshape(-1, gain_part),
                experts_gain_grad.reshape(-1, gain_part),
                jnp.transpose(
                    router_grad.reshape(col_count, router_part, row_count, depth), (2, 0, 3, 1)
                ).reshape(row_count * col_count, depth * router_part),
            ],
            axis=1,
        )
        small_grads = small_grads.reshape(row_count, -1)
        small_grads = lax.all_to_all(small_grads, "rows", split_axis=0, concat_axis=0, tiled=True)
        small_grads = jnp.sum(small_grads, axis=0).reshape(col_count, -1)
        small_grads = lax.all_to_all(small_grads, "cols", split_axis=0, concat_axis=0, tiled=True)
        small_sums = jnp.sum(small_grads, axis=0)
        attention_gain_sum = small_sums[:gain_part]
        experts_gain_sum = small_sums[gain_part : 2 * gain_part]
        router_sum = small_sums[2 * gain_part :].reshape(depth, router_part)

    return (
        layer_output,
        tokens_grad,
        query_sum,
        key_sum,
        value_sum,
        out_sum,
        router_sum,
        attention_gain_sum,
        experts_gain_sum,
        gate_grad,
        upward_grad,
        down_grad,
    )


def solution(mesh):
    in_specs = (
        P(("rows", "cols"), None),
        P("rows", "cols"),
        P("rows", "cols"),
        P("rows", "cols"),
        P("rows", "cols"),
        P("rows", "cols"),
        P(("rows", "cols")),
        P(("rows", "cols")),
        P("rows", None, "cols"),
        P("rows", None, "cols"),
        P("rows", "cols", None),
        P(("rows", "cols"), None),
        P(),
        P(("rows", "cols"), None),
    )
    out_specs = (
        P(("rows", "cols"), None),
        P(("rows", "cols"), None),
        P("rows", "cols"),
        P("rows", "cols"),
        P("rows", "cols"),
        P("rows", "cols"),
        P("rows", "cols"),
        P(("rows", "cols")),
        P(("rows", "cols")),
        P("rows", None, "cols"),
        P("rows", None, "cols"),
        P("rows", "cols", None),
    )
    return jax.shard_map(
        on_device, mesh=mesh, in_specs=in_specs, out_specs=out_specs, check_vma=False
    )
```

```python
import functools

import jax
import jax.numpy as jnp
from jax import lax
from jax.experimental import pallas as pl
from jax.experimental.pallas import tpu as pltpu
from jax.sharding import PartitionSpec as P

D = 1536
HEADS = 12
KV_HEADS = 2
HEAD_DIM = 128
TOP = 4
TOK_DEV = 512
BRANCHES = 4
LEAVES = 8
TRUNK = 256
BRANCH = 64

EPSILON = 1e-06
ROPE_BASE = 10000.0
MASKED = -1e30
LOW = jnp.bfloat16
WIDE = jnp.float32
KEY_WIDTH = KV_HEADS * HEAD_DIM
GROUP = HEADS // KV_HEADS
QUARTERS = 4
VMEM_LIMIT = 56 * 1024 * 1024

ANY = pl.BlockSpec(memory_space=pl.ANY)
SMEM = pl.BlockSpec(memory_space=pltpu.SMEM)


def nn(one, two):
    return lax.dot_general(one, two, (((1,), (0,)), ((), ())), preferred_element_type=WIDE)


def nt(one, two):
    return lax.dot_general(one, two, (((1,), (1,)), ((), ())), preferred_element_type=WIDE)


def tn(one, two):
    return lax.dot_general(one, two, (((0,), (0,)), ((), ())), preferred_element_type=WIDE)


def whole(shape):
    return pl.BlockSpec(shape, lambda *_: (0,) * len(shape))


LITTLE = pl.CostEstimate(flops=1, bytes_accessed=1, transcendentals=0)


def params():
    return pltpu.CompilerParams(vmem_limit_bytes=VMEM_LIMIT)


def turn(values, cosine, sine):
    return values * cosine + pltpu.roll(values, HEAD_DIM // 2, 1) * sine


def turn_back(values, cosine, sine):
    return values * cosine - pltpu.roll(values, HEAD_DIM // 2, 1) * sine


SLOTS = range(4)
PIECES = (
    tuple((0, slot) for slot in SLOTS),
    tuple((1, slot) for slot in SLOTS),
    tuple((2, slot) for slot in SLOTS),
    tuple((4, slot) for slot in SLOTS),
    ((6, 0), (6, 1)),
    ((6, 2), (6, 3)),
    tuple((flip_bits, slot) for flip_bits in (3, 5) for slot in SLOTS),
    ((7, 0), (7, 1)),
    ((7, 2), (7, 3)),
)
EXTRA = 16


STEP = 768


def weight_copies(info, refs, target, sem, start, width):
    if len(refs) == 1:
        return [pltpu.make_async_copy(refs[0], target, sem)]
    depth = refs[0].shape[1] - EXTRA
    copies = []
    for ref, parts in zip(refs, PIECES):
        for at, (flip_bits, slot) in enumerate(parts):
            row = pl.multiple_of((info[0] ^ flip_bits) * depth, depth)
            col = pl.multiple_of(info[2 + slot] * width, 128)
            copies.append(
                pltpu.make_async_copy(
                    ref.at[at, pl.ds(0, depth), pl.ds(start, width)],
                    target.at[pl.ds(row, depth), pl.ds(col, width)],
                    sem,
                )
            )
    return copies


def extras_kernel(info, *rest):
    refs, (out, sem) = rest[:-2], rest[-2:]
    depth = refs[0].shape[1] - EXTRA
    copies = []
    for ref, parts in zip(refs, PIECES):
        for at, (flip_bits, slot) in enumerate(parts):
            to = (info[0] ^ flip_bits) * QUARTERS + info[2 + slot]
            copies.append(pltpu.make_async_copy(ref.at[at, pl.ds(depth, EXTRA)], out.at[to], sem))
    run_all(copies)
    wait_all(copies)


def extras(info, refs):
    return pl.pallas_call(
        extras_kernel,
        out_shape=jax.ShapeDtypeStruct((8 * QUARTERS, EXTRA, refs[0].shape[2]), LOW),
        in_specs=[SMEM] + [ANY] * len(refs),
        out_specs=pl.BlockSpec(memory_space=pltpu.VMEM),
        scratch_shapes=[pltpu.SemaphoreType.DMA],
        compiler_params=params(),
        cost_estimate=LITTLE,
        name="extra_rows",
    )(info, *refs)


def run_all(copies):
    for copy in copies:
        copy.start()


def wait_all(copies):
    for copy in copies:
        copy.wait()


def key_value_kernel(info, tokens, gain, cosine, sine, *rest):
    count = len(rest) - 4
    refs, (normed, out, weight, sem) = rest[:count], rest[count:]
    copies = weight_copies(info, refs, weight, sem, D // QUARTERS, 128)
    run_all(copies)
    values = tokens[...].astype(WIDE)
    factor = lax.rsqrt(jnp.mean(values * values, axis=-1, keepdims=True) + EPSILON)
    low = (values * factor * gain[...]).astype(LOW)
    normed[...] = low
    wait_all(copies)
    both = nn(low, weight[...])
    half = HEAD_DIM // 2
    first = lax.broadcasted_iota(jnp.int32, (TOK_DEV, HEAD_DIM), 1) < half
    for g in range(KV_HEADS):
        one = both[:, 256 * g : 256 * g + 128]
        two = both[:, 256 * g + 128 : 256 * g + 256]
        key = jnp.where(first, one, pltpu.roll(two, half, 1))
        value = jnp.where(first, pltpu.roll(one, half, 1), two)
        out[:, 128 * g : 128 * g + 128] = turn(key, cosine[...], sine[...]).astype(LOW)
        out[:, KEY_WIDTH + 128 * g : KEY_WIDTH + 128 * g + 128] = value.astype(LOW)


def key_value(info, tokens, gain, cosine, sine, refs):
    return pl.pallas_call(
        key_value_kernel,
        out_shape=(
            jax.ShapeDtypeStruct((TOK_DEV, D), LOW),
            jax.ShapeDtypeStruct((TOK_DEV, 2 * KEY_WIDTH), LOW),
        ),
        in_specs=[SMEM] + [pl.BlockSpec(memory_space=pltpu.VMEM)] * 4 + [ANY] * len(refs),
        out_specs=(pl.BlockSpec(memory_space=pltpu.VMEM),) * 2,
        scratch_shapes=[pltpu.VMEM((D, 2 * KEY_WIDTH), LOW), pltpu.SemaphoreType.DMA],
        compiler_params=params(),
        cost_estimate=LITTLE,
        name="norm_key_value",
    )(info, tokens, gain, cosine, sine, *refs)


def query_kernel(info, normed, cosine, sine, *rest):
    count = len(rest) - 3
    refs, (out, weight, sem) = rest[:count], rest[count:]

    @pl.when(pl.program_id(0) == 0)
    def _():
        copies = weight_copies(info, refs, weight, sem, 0, D // QUARTERS)
        run_all(copies)
        wait_all(copies)

    at = pl.multiple_of(pl.program_id(0) * STEP, STEP)
    lin = nn(normed[...], weight[:, pl.ds(at, STEP)])
    for h in range(STEP // HEAD_DIM):
        out[:, 128 * h : 128 * h + 128] = turn(
            lin[:, 128 * h : 128 * h + 128], cosine[...], sine[...]
        ).astype(LOW)


def query(info, normed, cosine, sine, refs):
    return pl.pallas_call(
        query_kernel,
        grid=(D // STEP,),
        out_shape=jax.ShapeDtypeStruct((TOK_DEV, D), LOW),
        in_specs=[SMEM, whole((TOK_DEV, D)), whole((TOK_DEV, 128)), whole((TOK_DEV, 128))]
        + [ANY] * len(refs),
        out_specs=pl.BlockSpec((TOK_DEV, STEP), lambda i: (0, i)),
        scratch_shapes=[pltpu.VMEM((D, D), LOW), pltpu.SemaphoreType.DMA],
        compiler_params=params(),
        cost_estimate=LITTLE,
        name="query_projection",
    )(info, normed, cosine, sine, *refs)


KEYS = TRUNK + 2 * BRANCH
CHUNKS = TOK_DEV // BRANCH


def chunk_keys(info, source, own, column, chunk):
    at = pl.multiple_of(info[6 + chunk], BRANCH)
    rows = pl.multiple_of(chunk * BRANCH, BRANCH)
    columns = slice(column, column + HEAD_DIM)
    return jnp.concatenate(
        [
            source[0:TRUNK, columns],
            source[pl.ds(at, BRANCH), columns],
            own[pl.ds(rows, BRANCH), columns],
        ],
        axis=0,
    )


def chunk_allowed(info, chunk, query_axis, shape):
    query_row = lax.broadcasted_iota(jnp.int32, shape, query_axis) & (BRANCH - 1)
    key = lax.broadcasted_iota(jnp.int32, shape, 1 - query_axis)
    leaves = info[1] == 0
    trunk = jnp.logical_and(jnp.logical_not(leaves), chunk < TRUNK // BRANCH)
    limit = jnp.where(trunk, chunk * BRANCH + query_row, TRUNK - 1)
    branch_limit = jnp.where(leaves, TRUNK + BRANCH - 1, 0)
    own_limit = jnp.where(trunk, 0, query_row + TRUNK + BRANCH)
    top = jnp.where(key < TRUNK, limit, jnp.where(key < TRUNK + BRANCH, branch_limit, own_limit))
    return key <= top


def group_rows(ref, g):
    first = g * GROUP
    return jnp.concatenate(
        [ref[:, 128 * h : 128 * h + 128] for h in range(first, first + GROUP)], axis=0
    )


def keep_source(info, partner, own, source):
    @pl.when(pl.program_id(0) == 0)
    def _():
        @pl.when(info[1] == 0)
        def _():
            source[...] = partner[...]

        @pl.when(info[1] != 0)
        def _():
            source[...] = own[...]


def attention_kernel(info, queries, own, partner, out, source):
    keep_source(info, partner, own, source)
    chunk = pl.program_id(0)
    rows = GROUP * BRANCH
    allowed = chunk_allowed(info, chunk, 0, (rows, KEYS))
    for g in range(KV_HEADS):
        keys = chunk_keys(info, source, own, 128 * g, chunk)
        values = chunk_keys(info, source, own, KEY_WIDTH + 128 * g, chunk)
        scores = nt(group_rows(queries, g), keys) * HEAD_DIM**-0.5
        scores = jnp.where(allowed, scores, MASKED)
        weights = jnp.exp(scores - jnp.max(scores, axis=1, keepdims=True))
        total = jnp.sum(weights, axis=1, keepdims=True)
        mixed = nn((weights * (1.0 / total)).astype(LOW), values).astype(LOW)
        for h in range(GROUP):
            at = (g * GROUP + h) * 128
            out[:, at : at + 128] = mixed[h * BRANCH : (h + 1) * BRANCH]


def attention(info, queries, own, partner):
    return pl.pallas_call(
        attention_kernel,
        grid=(CHUNKS,),
        out_shape=jax.ShapeDtypeStruct((TOK_DEV, D), LOW),
        in_specs=[
            SMEM,
            pl.BlockSpec((BRANCH, D), lambda i: (i, 0)),
            whole((TOK_DEV, 2 * KEY_WIDTH)),
            whole((TOK_DEV, 2 * KEY_WIDTH)),
        ],
        out_specs=pl.BlockSpec((BRANCH, D), lambda i: (i, 0)),
        scratch_shapes=[pltpu.VMEM((TOK_DEV, 2 * KEY_WIDTH), LOW)],
        compiler_params=params(),
        cost_estimate=LITTLE,
        name="tree_attention",
    )(info, queries, own, partner)


def attention_back_kernel(
    info, queries, own, partner, grads, cosine, sine, grad_query, own_grad, source_grad, source
):
    keep_source(info, partner, own, source)
    chunk = pl.program_id(0)

    @pl.when(chunk == 0)
    def _():
        source_grad[...] = jnp.zeros_like(source_grad)

    rows = GROUP * BRANCH
    scale = HEAD_DIM**-0.5
    allowed = chunk_allowed(info, chunk, 1, (KEYS, rows))
    at = pl.multiple_of(info[6 + chunk], BRANCH)
    for g in range(KV_HEADS):
        keys = chunk_keys(info, source, own, 128 * g, chunk)
        values = chunk_keys(info, source, own, KEY_WIDTH + 128 * g, chunk)
        query_rows = group_rows(queries, g)
        grad_rows = group_rows(grads, g)
        scores = jnp.where(allowed, nt(keys, query_rows) * scale, MASKED)
        weights = jnp.exp(scores - jnp.max(scores, axis=0, keepdims=True))
        probs = weights * (1.0 / jnp.sum(weights, axis=0, keepdims=True))
        grad_probs = nt(values, grad_rows)
        mean = jnp.sum(probs * grad_probs, axis=0, keepdims=True)
        grad_scores = (probs * (grad_probs - mean)).astype(LOW)
        grad_values = nn(probs.astype(LOW), grad_rows)
        grad_keys = nn(grad_scores, query_rows) * scale
        grad_queries = tn(grad_scores, keys) * scale
        for h in range(GROUP):
            to = (g * GROUP + h) * 128
            grad_query[:, to : to + 128] = turn_back(
                grad_queries[h * BRANCH : (h + 1) * BRANCH], cosine[...], sine[...]
            ).astype(LOW)
        for column, grad in ((128 * g, grad_keys), (KEY_WIDTH + 128 * g, grad_values)):
            columns = slice(column, column + 128)
            source_grad[0:TRUNK, columns] += grad[0:TRUNK]
            source_grad[pl.ds(at, BRANCH), columns] += grad[TRUNK : TRUNK + BRANCH]
            own_grad[:, columns] = grad[TRUNK + BRANCH :]


def attention_back(info, queries, own, partner, grads, cosine, sine):
    chunked = pl.BlockSpec((BRANCH, D), lambda i: (i, 0))
    pair = (TOK_DEV, 2 * KEY_WIDTH)
    return pl.pallas_call(
        attention_back_kernel,
        grid=(CHUNKS,),
        out_shape=(
            jax.ShapeDtypeStruct((TOK_DEV, D), LOW),
            jax.ShapeDtypeStruct(pair, WIDE),
            jax.ShapeDtypeStruct(pair, WIDE),
        ),
        in_specs=[
            SMEM,
            chunked,
            whole(pair),
            whole(pair),
            chunked,
            pl.BlockSpec((BRANCH, 128), lambda i: (i, 0)),
            pl.BlockSpec((BRANCH, 128), lambda i: (i, 0)),
        ],
        out_specs=(
            chunked,
            pl.BlockSpec((BRANCH, 2 * KEY_WIDTH), lambda i: (i, 0)),
            whole(pair),
        ),
        scratch_shapes=[pltpu.VMEM(pair, LOW)],
        compiler_params=params(),
        cost_estimate=LITTLE,
        name="tree_attention_back",
    )(info, queries, own, partner, grads, cosine, sine)


def out_kernel(info, heads, tokens, gain, *rest):
    count = len(rest) - 4
    refs, (residual, normed, weight, sem) = rest[:count], rest[count:]

    @pl.when(pl.program_id(0) == 0)
    def _():
        copies = weight_copies(info, refs, weight, sem, D // QUARTERS + 128, D // QUARTERS)
        run_all(copies)
        wait_all(copies)

    at = pl.ds(pl.multiple_of(pl.program_id(0) * STEP, STEP), STEP)
    residual[:, at] = tokens[:, at].astype(WIDE) + nn(heads[...], weight[:, at])

    @pl.when(pl.program_id(0) == pl.num_programs(0) - 1)
    def _():
        values = residual[...]
        factor = lax.rsqrt(jnp.mean(values * values, axis=-1, keepdims=True) + EPSILON)
        normed[...] = (values * factor * gain[...]).astype(LOW)


def out_projection(info, heads, tokens, gain, refs):
    full = (TOK_DEV, D)
    return pl.pallas_call(
        out_kernel,
        grid=(D // STEP,),
        out_shape=(jax.ShapeDtypeStruct(full, WIDE), jax.ShapeDtypeStruct(full, LOW)),
        in_specs=[SMEM, whole(full), whole(full), whole((1, D))] + [ANY] * len(refs),
        out_specs=(whole(full), whole(full)),
        scratch_shapes=[pltpu.VMEM((D, D), LOW), pltpu.SemaphoreType.DMA],
        compiler_params=params(),
        cost_estimate=LITTLE,
        name="out_projection",
    )(info, heads, tokens, gain, *refs)


def hits_of(routes, ids):
    hit = ids == routes[0, 0:1]
    for k in range(1, TOP):
        hit = jnp.logical_or(hit, ids == routes[0, k : k + 1])
    return hit


def tables_kernel(capacity, local, total, info, routes, chosen_out, place_out, earlier):
    @pl.when(pl.program_id(0) == 0)
    def _():
        one = lax.broadcasted_iota(jnp.int32, (TOK_DEV, TOK_DEV), 0)
        two = lax.broadcasted_iota(jnp.int32, (TOK_DEV, TOK_DEV), 1)
        earlier[...] = jnp.where(one < two, 1.0, 0.0).astype(LOW)

    ids = lax.broadcasted_iota(jnp.int32, (total, TOK_DEV), 0)
    hit = hits_of(routes, ids)
    rank = nn(jnp.where(hit, 1.0, 0.0).astype(LOW), earlier[...])
    place = jnp.where(hit, rank, -1.0)
    spots = lax.broadcasted_iota(jnp.int32, (capacity, TOK_DEV), 0).astype(WIDE)
    place_out[0] = jnp.full(place_out.shape[1:], -1.0, WIDE)
    for e in range(local):
        mine = ids == info[0] * local + e
        place_row = jnp.sum(jnp.where(mine, place, 0.0), axis=0, keepdims=True)
        place_out[0, e : e + 1] = place_row
        chosen_out[0, e * capacity : (e + 1) * capacity] = jnp.where(
            spots == place_row, 1.0, 0.0
        ).astype(LOW)


def tables(info, routes, capacity, local, total):
    count = routes.shape[0]
    return pl.pallas_call(
        functools.partial(tables_kernel, capacity, local, total),
        grid=(count,),
        in_specs=[SMEM, pl.BlockSpec((1, TOP, TOK_DEV), lambda i: (i, 0, 0))],
        out_specs=[
            pl.BlockSpec((1, local * capacity, TOK_DEV), lambda i: (i, 0, 0)),
            pl.BlockSpec((1, 8, TOK_DEV), lambda i: (i, 0, 0)),
        ],
        scratch_shapes=[pltpu.VMEM((TOK_DEV, TOK_DEV), LOW)],
        out_shape=[
            jax.ShapeDtypeStruct((count, local * capacity, TOK_DEV), LOW),
            jax.ShapeDtypeStruct((count, 8, TOK_DEV), WIDE),
        ],
        compiler_params=params(),
        cost_estimate=LITTLE,
        name="route_tables",
    )(info, routes)


def pick_kernel(local, count, chosen, *rest):
    blocks, outs = rest[:count], rest[count : count + local]
    picks, block_in, out_block, sem_in, sem_out = rest[count + local :]
    capacity = outs[0].shape[1]
    copies = [
        (
            pltpu.make_async_copy(chosen.at[q], picks.at[q], sem_in.at[q, 0]),
            pltpu.make_async_copy(blocks[q], block_in.at[q], sem_in.at[q, 1]),
        )
        for q in range(count)
    ]
    for pair in copies:
        run_all(pair)
    sent = []
    for q in range(count):
        wait_all(copies[q])
        out_block[q] = nn(picks[q], block_in[q]).astype(LOW)
        for e in range(local):
            copy = pltpu.make_async_copy(
                out_block.at[q, pl.ds(e * capacity, capacity)], outs[e].at[q], sem_out.at[q, e]
            )
            copy.start()
            sent.append(copy)
    wait_all(sent)


def pick_rows(chosen, blocks, local):
    count, height, _ = chosen.shape
    return pl.pallas_call(
        functools.partial(pick_kernel, local, count),
        in_specs=[ANY] * (1 + count),
        out_specs=[ANY] * local,
        out_shape=[jax.ShapeDtypeStruct((count, height // local, D), LOW)] * local,
        scratch_shapes=[
            pltpu.VMEM((count, height, TOK_DEV), LOW),
            pltpu.VMEM((count, TOK_DEV, D), LOW),
            pltpu.VMEM((count, height, D), LOW),
            pltpu.SemaphoreType.DMA((count, 2)),
            pltpu.SemaphoreType.DMA((count, local)),
        ],
        compiler_params=params(),
        cost_estimate=LITTLE,
        name="pick_rows",
    )(chosen, *blocks)


def dispatch_kernel(local, info, rows, chosen, routes, router, *rest):
    outs, logits = rest[2 * local : 4 * local], rest[-1]
    total = router.shape[1]
    step = pl.program_id(0)
    block = rows[...]
    rows_of = nn(chosen[0], block).astype(LOW)
    capacity = outs[0].shape[1]
    for e in range(local):
        outs[e][0] = rows_of[e * capacity : (e + 1) * capacity]
    part = nn(block, router[...])

    @pl.when(step == 0)
    def _():
        logits[...] = part

    @pl.when(step > 0)
    def _():
        logits[...] += part

    @pl.when(step == pl.num_programs(0) - 1)
    def _():
        values = logits[...].T
        ids = lax.broadcasted_iota(jnp.int32, (total, TOK_DEV), 0)
        weights = jnp.exp(values - jnp.max(values, axis=0, keepdims=True))
        hit = hits_of(routes, ids)
        share = weights / jnp.sum(jnp.where(hit, weights, 0.0), axis=0, keepdims=True)
        for e in range(local):
            mine = ids == info[0] * local + e
            share_row = jnp.sum(jnp.where(mine, share, 0.0), axis=0, keepdims=True)
            picked = chosen[0, e * capacity : (e + 1) * capacity].astype(WIDE)
            outs[local + e][0] = jnp.sum(picked * share_row, axis=1, keepdims=True)


def dispatch(at, info, rows, chosen, routes, router, local, earlier):
    count, height, _ = chosen.shape
    capacity = height // local
    total = router.shape[1]
    wide = D
    out_shape = [jax.ShapeDtypeStruct((count, capacity, D), LOW)] * local + [
        jax.ShapeDtypeStruct((count, capacity, 1), WIDE)
    ] * local
    if earlier is None:
        earlier = [jnp.zeros((8, 128), shape.dtype) for shape in out_shape]
        aliases = {}
    else:
        aliases = {5 + i: i for i in range(len(out_shape))}
    return pl.pallas_call(
        functools.partial(dispatch_kernel, local),
        grid=(D // wide,),
        in_specs=[
            SMEM,
            pl.BlockSpec((TOK_DEV, wide), lambda i: (0, i)),
            pl.BlockSpec((1, height, TOK_DEV), lambda i: (at, 0, 0)),
            pl.BlockSpec((1, TOP, TOK_DEV), lambda i: (at, 0, 0)),
            pl.BlockSpec((wide, total), lambda i: (i, 0)),
        ]
        + [ANY] * len(out_shape),
        out_specs=[pl.BlockSpec((1, capacity, wide), lambda i: (at, 0, i))] * local
        + [pl.BlockSpec((1, capacity, 1), lambda i: (at, 0, 0))] * local,
        scratch_shapes=[pltpu.VMEM((TOK_DEV, total), WIDE)],
        out_shape=out_shape,
        input_output_aliases=aliases,
        compiler_params=params(),
        cost_estimate=LITTLE,
        name="dispatch",
    )(info, rows, chosen, routes, router, *earlier)


def spread_kernel(local, place, *rest):
    dots, out = rest[:local], rest[local]
    spots = lax.broadcasted_iota(jnp.int32, (dots[0].shape[1], TOK_DEV), 0).astype(WIDE)
    for e in range(local):
        chosen = spots == place[0, e : e + 1]
        out[0, e : e + 1] = jnp.sum(jnp.where(chosen, dots[e][0], 0.0), axis=0, keepdims=True)


def spread(place, dots):
    count, capacity, _ = dots[0].shape
    local = len(dots)
    return pl.pallas_call(
        functools.partial(spread_kernel, local),
        grid=(count,),
        out_shape=jax.ShapeDtypeStruct((count, local, TOK_DEV), WIDE),
        in_specs=[pl.BlockSpec((1, 8, TOK_DEV), lambda i: (i, 0, 0))]
        + [pl.BlockSpec((1, capacity, 1), lambda i: (i, 0, 0))] * local,
        out_specs=pl.BlockSpec((1, local, TOK_DEV), lambda i: (i, 0, 0)),
        compiler_params=params(),
        cost_estimate=LITTLE,
        name="spread",
    )(place, *dots)


def expert_kernel(slots, info, rows, grads, shares, *rest):
    refs, (out_rows, back_rows, grad_rows, acts, dots, weight, sem) = rest[:-7], rest[-7:]
    part = weight.shape[1] // slots

    @pl.when(pl.program_id(0) == 0)
    def _():
        def copies(ref, slot):
            return [
                pltpu.make_async_copy(
                    ref.at[pl.ds(which * part, part)],
                    weight.at[which, pl.ds(pl.multiple_of(slot * part, part), part)],
                    sem,
                )
                for which in range(3)
            ]

        if len(refs) == 1:
            for slot in range(slots):
                run_all(copies(refs[0].at[slot], slot))
            for slot in range(slots):
                wait_all(copies(refs[0].at[slot], slot))
        else:
            block, second, above, below, far = refs
            low_end = info[2] == 0
            end = jnp.logical_or(low_end, info[2] == 3)
            run_all(copies(block, info[2]))
            run_all(copies(second, info[3]))

            @pl.when(low_end)
            def _():
                run_all(copies(above, info[4]))

            @pl.when(jnp.logical_not(low_end))
            def _():
                run_all(copies(below, info[4]))

            @pl.when(end)
            def _():
                run_all(copies(far, info[5]))

            @pl.when(jnp.logical_not(end))
            def _():
                run_all(copies(above, info[5]))

            for slot in range(slots):
                wait_all(copies(block, slot))

    row_block = rows[...]
    share = shares[...]
    grad_float = grads[...].astype(WIDE)
    grad_low = (share * grad_float).astype(LOW)
    grad_rows[...] = grad_low
    gate_act = nt(row_block, weight[0])
    upward = nt(row_block, weight[1])
    sigmoid = 1.0 / (1.0 + jnp.exp(-gate_act))
    silu = gate_act * sigmoid
    hidden = (silu * upward).astype(LOW)
    expert_out = nn(hidden, weight[2]).astype(LOW).astype(WIDE)
    out_rows[...] = (share * expert_out).astype(LOW)
    dots[...] = jnp.sum(grad_float * expert_out, axis=1, keepdims=True)
    grad_hidden = nt(grad_low, weight[2])
    grad_gate = (grad_hidden * upward * sigmoid * (1.0 + gate_act * (1.0 - sigmoid))).astype(LOW)
    grad_up = (grad_hidden * silu).astype(LOW)
    back_rows[...] = (nn(grad_gate, weight[0]) + nn(grad_up, weight[1])).astype(LOW)
    for which, act in enumerate((grad_gate, grad_up, hidden)):
        turned = act.T
        for slot in range(slots):
            acts[slot, which * part : (which + 1) * part] = turned[
                slot * part : (slot + 1) * part
            ]


EXPERT_ROWS = 256


def expert(info, rows, grads, shares, refs, slots):
    height = rows.shape[0]
    part = refs[0].shape[-2] // 3
    wide_block = pl.BlockSpec((EXPERT_ROWS, D), lambda i: (i, 0))
    thin_block = pl.BlockSpec((EXPERT_ROWS, 1), lambda i: (i, 0))
    return pl.pallas_call(
        functools.partial(expert_kernel, slots),
        grid=(height // EXPERT_ROWS,),
        out_shape=[jax.ShapeDtypeStruct((height, D), LOW)] * 3
        + [
            jax.ShapeDtypeStruct((slots, 3 * part, height), LOW),
            jax.ShapeDtypeStruct((height, 1), WIDE),
        ],
        in_specs=[SMEM, wide_block, wide_block, thin_block] + [ANY] * len(refs),
        out_specs=[wide_block] * 3
        + [pl.BlockSpec((slots, 3 * part, EXPERT_ROWS), lambda i: (0, 0, i)), thin_block],
        scratch_shapes=[pltpu.VMEM((3, slots * part, D), LOW), pltpu.SemaphoreType.DMA],
        compiler_params=params(),
        cost_estimate=LITTLE,
        name="expert",
    )(info, rows, grads, shares, *refs)


def expert_grads_kernel(acts, rows, grads, out):
    slots, height, _ = acts.shape
    part = height // 3
    for slot in range(slots):
        out[slot, : 2 * part] = nn(acts[slot, : 2 * part], rows[...]).astype(LOW)
        out[slot, 2 * part :] = nn(acts[slot, 2 * part :], grads[...]).astype(LOW)


def expert_grads(acts, rows, grads):
    slots, part, height = acts.shape
    strip = pl.BlockSpec((height, 256), lambda i: (0, i))
    return pl.pallas_call(
        expert_grads_kernel,
        grid=(D // 256,),
        out_shape=jax.ShapeDtypeStruct((slots, part, D), LOW),
        in_specs=[whole(acts.shape), strip, strip],
        out_specs=pl.BlockSpec((slots, part, 256), lambda i: (0, 0, i)),
        compiler_params=params(),
        cost_estimate=LITTLE,
        name="expert_gradients",
    )(acts, rows, grads)


SHARE_ROWS = 32


def combine_kernel(local, first, step, info, chosen, *rest):
    rows, dots, out = rest[:local], rest[local:-6], rest[-6]
    picks, rows_in, out_block, sem_in, sem_out = rest[-5:]
    number = out.shape[0]
    capacity = rows[0].shape[1]
    copies = []
    for n in range(number):
        q = first + step * n
        copies.append(
            [pltpu.make_async_copy(chosen.at[q], picks.at[n], sem_in.at[n, local])]
            + [
                pltpu.make_async_copy(
                    rows[e].at[q],
                    rows_in.at[n, pl.ds(e * capacity, capacity)],
                    sem_in.at[n, e],
                )
                for e in range(local)
            ]
        )
    for group in copies:
        run_all(group)
    sent = []
    for n in range(number):
        wait_all(copies[n])
        out_block[n, :TOK_DEV] = tn(picks[n], rows_in[n]).astype(LOW)
        if dots:
            row = lax.broadcasted_iota(jnp.int32, (SHARE_ROWS, D), 0)
            values = jnp.zeros((SHARE_ROWS, D), WIDE)
            for e in range(local):
                picked = picks[n, e * capacity : (e + 1) * capacity].astype(WIDE)
                share = picked * dots[e][first + step * n]
                high, low = split(jnp.sum(share, axis=0, keepdims=True))
                pieces = [high.astype(WIDE), low.astype(WIDE)]
                pieces.append(jnp.zeros((1, D - 2 * TOK_DEV), WIDE))
                line = jnp.concatenate(pieces, axis=1)
                values = jnp.where(row == info[0] * local + e, line, values)
            out_block[n, TOK_DEV:] = values.astype(LOW)
        copy = pltpu.make_async_copy(out_block.at[n], out.at[n], sem_out.at[n])
        copy.start()
        sent.append(copy)
    wait_all(sent)


def combine(info, chosen, rows, first, step, dots=()):
    count, capacity, _ = rows[0].shape
    local = len(rows)
    number = (count - first + step - 1) // step
    height = TOK_DEV + (SHARE_ROWS if dots else 0)
    return pl.pallas_call(
        functools.partial(combine_kernel, local, first, step),
        out_shape=jax.ShapeDtypeStruct((number, height, D), LOW),
        in_specs=[SMEM, ANY]
        + [ANY] * local
        + [pl.BlockSpec(memory_space=pltpu.VMEM)] * len(dots),
        out_specs=ANY,
        scratch_shapes=[
            pltpu.VMEM((number, local * capacity, TOK_DEV), LOW),
            pltpu.VMEM((number, local * capacity, D), LOW),
            pltpu.VMEM((number, height, D), LOW),
            pltpu.SemaphoreType.DMA((number, local + 1)),
            pltpu.SemaphoreType.DMA((number,)),
        ],
        compiler_params=params(),
        cost_estimate=LITTLE,
        name="combine",
    )(info, chosen, *rows, *dots)


def chip_adds_kernel(keep, got, send_x, send_y, near_x, near_y, one, two, sem_in, sem_out):
    half = send_x.shape[1]
    copies = [
        (
            pltpu.make_async_copy(keep.at[i], one.at[i], sem_in.at[i, 0]),
            pltpu.make_async_copy(got.at[i], two.at[i], sem_in.at[i, 1]),
        )
        for i in range(4)
    ]
    for pair in copies:
        run_all(pair)
    sent = []
    for i in range(4):
        wait_all(copies[i])
        one[i] = (one[i].astype(WIDE) + two[i].astype(WIDE)).astype(LOW)
        upper = (near_x, send_x)[i % 2].at[i // 2]
        lower = (near_y, send_y)[i // 2].at[i % 2]
        for part, to in enumerate((upper, lower)):
            copy = pltpu.make_async_copy(
                one.at[i, pl.ds(part * half, half)], to, sem_out.at[i, part]
            )
            copy.start()
            sent.append(copy)
    wait_all(sent)


def chip_adds(keep, got):
    _, height, width = keep.shape
    shape = jax.ShapeDtypeStruct((2, height // 2, width), LOW)
    return pl.pallas_call(
        chip_adds_kernel,
        out_shape=(shape,) * 4,
        in_specs=[ANY, ANY],
        out_specs=(ANY,) * 4,
        scratch_shapes=[
            pltpu.VMEM(keep.shape, LOW),
            pltpu.VMEM(keep.shape, LOW),
            pltpu.SemaphoreType.DMA((4, 2)),
            pltpu.SemaphoreType.DMA((4, 2)),
        ],
        compiler_params=params(),
        cost_estimate=LITTLE,
        name="chip_sums",
    )(keep, got)


def corner_adds_kernel(near_x, got_x, near_y, got_y, send_y, send_x):
    send_y[...] = (near_x[0].astype(WIDE) + got_x[0].astype(WIDE)).astype(LOW)
    send_x[...] = (near_y[0].astype(WIDE) + got_y[0].astype(WIDE)).astype(LOW)


def corner_adds(near_x, got_x, near_y, got_y):
    _, half, width = near_x.shape
    rows = half
    block = pl.BlockSpec((1, rows, width), lambda i: (1, i, 0))
    out = pl.BlockSpec((rows, width), lambda i: (i, 0))
    return pl.pallas_call(
        corner_adds_kernel,
        grid=(half // rows,),
        out_shape=(jax.ShapeDtypeStruct((half, width), LOW),) * 2,
        in_specs=[block] * 4,
        out_specs=(out, out),
        compiler_params=params(),
        cost_estimate=LITTLE,
        name="corner_sums",
    )(near_x, got_x, near_y, got_y)


def split(values):
    high = values.astype(LOW)
    return high, (values - high.astype(WIDE)).astype(LOW)


def norm_back(values, gain, grad):
    factor = lax.rsqrt(jnp.mean(values * values, axis=-1, keepdims=True) + EPSILON)
    scaled = gain * grad
    mean = jnp.mean(values * scaled, axis=-1, keepdims=True)
    grad_values = factor * scaled - values * (factor * factor * factor * mean)
    grad_gain = jnp.sum(grad * values * factor, axis=0, keepdims=True)
    return grad_values, grad_gain


def router_back(logits, routes, grad_shares):
    ids = lax.broadcasted_iota(jnp.int32, logits.shape, 0)
    hit = ids == routes[0:1]
    for k in range(1, TOP):
        hit = jnp.logical_or(hit, ids == routes[k : k + 1])
    weights = jnp.exp(logits - jnp.max(logits, axis=0, keepdims=True))
    probs = weights / jnp.sum(weights, axis=0, keepdims=True)
    chosen = jnp.sum(jnp.where(hit, probs, 0.0), axis=0, keepdims=True)
    grads = jnp.where(hit, grad_shares, 0.0)
    mean = jnp.sum(probs * grads, axis=0, keepdims=True) / chosen
    grad_probs = jnp.where(hit, (grads - mean) / chosen, 0.0)
    return probs * (grad_probs - jnp.sum(probs * grad_probs, axis=0, keepdims=True))


def branch_back_kernel(
    parts, info, residual, normed, cotangent, routes, router, gain, *rest
):
    sums, rest = rest[:parts], rest[parts:]
    experts = router.shape[0]
    count = len(rest) - 7
    refs = rest[:count]
    grad_residual, grad_branch, grad_heads, grad_gain, grad_router, weight, sem = rest[count:]

    @pl.when(pl.program_id(0) == 0)
    def _():
        copies = weight_copies(info, refs, weight, sem, D // QUARTERS + 128, D // QUARTERS)
        run_all(copies)
        logits = nt(router[...], normed[...])
        if parts == 2:
            back_sum, grad_shares = sums[0][...], sums[1][...]
        else:
            values = [
                (ref[0] if len(ref.shape) == 3 else ref[...]).astype(WIDE) for ref in sums
            ]
            upper = values[0] + values[1] + values[2]
            lower = values[3] + values[4] + values[5]
            last = lower.shape[0] - SHARE_ROWS
            shares = lower[last : last + experts]
            grad_shares = shares[:, :TOK_DEV] + shares[:, TOK_DEV : 2 * TOK_DEV]
            back_sum = jnp.concatenate([upper, lower[:last]], axis=0)
        high, low = split(router_back(logits, routes[...], grad_shares))
        grad_router[...] = nn(high, normed[...]) + nn(low, normed[...])
        grad_normed = tn(high, router[...]) + tn(low, router[...])
        grad_normed += back_sum
        grad_values, gain_grad = norm_back(residual[...], gain[...], grad_normed)
        grad_gain[...] = gain_grad
        total = cotangent[...].astype(WIDE) + grad_values
        grad_residual[...] = total
        grad_branch[...] = total.astype(LOW)
        wait_all(copies)

    at = pl.ds(pl.multiple_of(pl.program_id(0) * STEP, STEP), STEP)
    grad_heads[...] = nt(grad_branch[...], weight[at, :]).astype(LOW)


def branch_back(info, residual, normed, sums, cotangent, routes, router, gain, refs):
    full = (TOK_DEV, D)
    total = router.shape[0]
    return pl.pallas_call(
        functools.partial(branch_back_kernel, len(sums)),
        grid=(D // STEP,),
        out_shape=(
            jax.ShapeDtypeStruct(full, WIDE),
            jax.ShapeDtypeStruct(full, LOW),
            jax.ShapeDtypeStruct(full, LOW),
            jax.ShapeDtypeStruct((1, D), WIDE),
            jax.ShapeDtypeStruct((total, D), WIDE),
        ),
        in_specs=[SMEM]
        + [whole(full)] * 3
        + [whole((TOP, TOK_DEV)), whole((total, D)), whole((1, D))]
        + [whole(part.shape if part.ndim == 2 else (1,) + part.shape[1:]) for part in sums]
        + [ANY] * len(refs),
        out_specs=(
            whole(full),
            whole(full),
            pl.BlockSpec((TOK_DEV, STEP), lambda i: (0, i)),
            whole((1, D)),
            whole((total, D)),
        ),
        scratch_shapes=[pltpu.VMEM((D, D), LOW), pltpu.SemaphoreType.DMA],
        compiler_params=params(),
        cost_estimate=LITTLE,
        name="experts_norm_back",
    )(info, residual, normed, cotangent, routes, router, gain, *sums, *refs)


def join_grads_kernel(info, own_grad, source_grad, arrived, cosine, sine, out):
    half = HEAD_DIM // 2
    first = lax.broadcasted_iota(jnp.int32, (TOK_DEV, HEAD_DIM), 1) < half
    leaves = info[1] == 0

    def total(column):
        columns = slice(column, column + 128)
        extra = source_grad[:, columns] + arrived[:, columns].astype(WIDE)
        return own_grad[:, columns] + jnp.where(leaves, 0.0, extra)

    for g in range(KV_HEADS):
        key = turn_back(total(128 * g), cosine[...], sine[...])
        value = total(KEY_WIDTH + 128 * g)
        out[:, 256 * g : 256 * g + 128] = jnp.where(
            first, key, pltpu.roll(value, half, 1)
        ).astype(LOW)
        out[:, 256 * g + 128 : 256 * g + 256] = jnp.where(
            first, pltpu.roll(key, half, 1), value
        ).astype(LOW)


def join_grads(info, own_grad, source_grad, arrived, cosine, sine):
    vmem = pl.BlockSpec(memory_space=pltpu.VMEM)
    return pl.pallas_call(
        join_grads_kernel,
        out_shape=jax.ShapeDtypeStruct((TOK_DEV, 2 * KEY_WIDTH), LOW),
        in_specs=[SMEM] + [vmem] * 5,
        out_specs=vmem,
        compiler_params=params(),
        cost_estimate=LITTLE,
        name="join_key_value_gradients",
    )(info, own_grad, source_grad, arrived, cosine, sine)


def normed_grad_kernel(info, grad_query, *rest):
    refs, (out, weight, sem) = rest[:-3], rest[-3:]

    @pl.when(pl.program_id(0) == 0)
    def _():
        copies = weight_copies(info, refs, weight, sem, 0, D // QUARTERS)
        run_all(copies)
        wait_all(copies)

    at = pl.ds(pl.multiple_of(pl.program_id(0) * STEP, STEP), STEP)
    out[...] = nt(grad_query[...], weight[at, :])


def normed_grad(info, grad_query, refs):
    return pl.pallas_call(
        normed_grad_kernel,
        grid=(D // STEP,),
        out_shape=jax.ShapeDtypeStruct((TOK_DEV, D), WIDE),
        in_specs=[SMEM, whole((TOK_DEV, D))] + [ANY] * len(refs),
        out_specs=pl.BlockSpec((TOK_DEV, STEP), lambda i: (0, i)),
        scratch_shapes=[pltpu.VMEM((D, D), LOW), pltpu.SemaphoreType.DMA],
        compiler_params=params(),
        cost_estimate=LITTLE,
        name="normed_gradient",
    )(info, grad_query, *refs)


def token_back_kernel(info, query_part, grad_pair, tokens, grad_residual, gain, *rest):
    refs, (out, grad_gain, weight, sem) = rest[:-4], rest[-4:]
    copies = weight_copies(info, refs, weight, sem, D // QUARTERS, 128)
    run_all(copies)
    wait_all(copies)
    grad_normed = query_part[...] + nt(grad_pair[...], weight[...])
    grad_values, gain_grad = norm_back(tokens[...].astype(WIDE), gain[...], grad_normed)
    grad_gain[...] = gain_grad
    out[...] = (grad_residual[...] + grad_values).astype(LOW)


def token_back(info, query_part, grad_pair, tokens, grad_residual, gain, refs):
    full = (TOK_DEV, D)
    vmem = pl.BlockSpec(memory_space=pltpu.VMEM)
    return pl.pallas_call(
        token_back_kernel,
        out_shape=(jax.ShapeDtypeStruct(full, LOW), jax.ShapeDtypeStruct((1, D), WIDE)),
        in_specs=[SMEM] + [vmem] * 5 + [ANY] * len(refs),
        out_specs=(vmem, vmem),
        scratch_shapes=[
            pltpu.VMEM((D, 2 * KEY_WIDTH), LOW),
            pltpu.SemaphoreType.DMA,
        ],
        compiler_params=params(),
        cost_estimate=LITTLE,
        name="token_gradient",
    )(info, query_part, grad_pair, tokens, grad_residual, gain, *refs)


def weight_grads_kernel(parts, whole_rows, info, *rest):
    ins, (keep, send) = rest[:-2], rest[-2:]
    depth = D // 8
    core = info[0] & 1
    chip = pl.program_id(0) ^ (info[0] >> 1)
    for strip_at, grads_at, start, width in parts:
        low = tn(ins[strip_at][...], ins[grads_at][...]).astype(LOW)
        columns = slice(start, start + width)
        for slot in range(QUARTERS):
            for j in range(QUARTERS):

                @pl.when(info[2 + slot] == j)
                def _():
                    piece = low[:, j * width : (j + 1) * width]
                    upper, lower = piece[:depth], piece[depth:]
                    keep[0, slot, :depth, columns] = jnp.where(core == 0, upper, lower)
                    send[0, slot, :depth, columns] = jnp.where(core == 0, lower, upper)
                    if not whole_rows:
                        blank = jnp.zeros((EXTRA, width), LOW)
                        keep[0, slot, depth:, columns] = blank
                        send[0, slot, depth:, columns] = blank

    if whole_rows:
        extra = ins[-1]
        for slot in range(QUARTERS):
            to = info[2 + slot]
            keep[0, slot, depth:] = extra[(chip * 2 + core) * QUARTERS + to]
            send[0, slot, depth:] = extra[(chip * 2 + 1 - core) * QUARTERS + to]


def weight_grads(info, strips, grads, parts, extra, earlier=()):
    depth = D // 8
    strip = pl.BlockSpec((TOK_DEV, 2 * depth), lambda i, info: (0, i ^ (info[0] >> 1)))
    more = [] if extra is None else [extra]
    width = 2 * D // QUARTERS + 128
    shape = (4, QUARTERS, depth + EXTRA, width)
    if earlier:
        out = pl.BlockSpec((1, QUARTERS, depth + EXTRA, 128), lambda i, info: (i, 0, 0, 3))
    else:
        out = pl.BlockSpec((1,) + shape[1:], lambda i, info: (i, 0, 0, 0))
    inputs = [*strips, *grads, *more]

    def kernel(info, *rest):
        count = len(inputs)
        weight_grads_kernel(
            parts, extra is not None, info, *rest[:count], *rest[count + len(earlier) :]
        )

    return pl.pallas_call(
        kernel,
        grid_spec=pltpu.PrefetchScalarGridSpec(
            num_scalar_prefetch=1,
            grid=(4,),
            in_specs=[strip] * len(strips)
            + [
                pl.BlockSpec(a.shape, lambda i, info, n=a.ndim: (0,) * n)
                for a in (*grads, *more)
            ]
            + [ANY] * len(earlier),
            out_specs=(out, out),
        ),
        out_shape=(jax.ShapeDtypeStruct(shape, LOW),) * 2,
        input_output_aliases={1 + len(inputs) + i: i for i in range(len(earlier))},
        compiler_params=params(),
        cost_estimate=LITTLE,
        name="weight_gradients",
    )(info, *inputs, *earlier)


def last_sums_kernel(part, info, own, *rest):
    arrived, (query_out, key_out, value_out, out_out, extra_out) = rest[:-5], rest[-5:]
    total = own[...].astype(WIDE)
    for ref in arrived[:-1]:
        total += ref[...].astype(WIDE)
    end = jnp.logical_or(info[2] == 0, info[2] == 3)
    total += jnp.where(end, arrived[-1][...].astype(WIDE), 0.0)
    depth = query_out.shape[0]
    quarter = query_out.shape[1]
    query_out[...] = total[:depth, :quarter]
    pair = total[:depth, quarter : quarter + 2 * part].T
    key_out[...] = pair[:part]
    value_out[...] = pair[part:]
    out_out[...] = total[:depth, quarter + 2 * part :]
    extra_out[...] = total[depth:]


def last_sums(info, own, arrived, depth, part):
    height, width = own.shape
    quarter = D // QUARTERS
    vmem = pl.BlockSpec(memory_space=pltpu.VMEM)
    return pl.pallas_call(
        functools.partial(last_sums_kernel, part),
        out_shape=(
            jax.ShapeDtypeStruct((depth, quarter), WIDE),
            jax.ShapeDtypeStruct((part, depth), WIDE),
            jax.ShapeDtypeStruct((part, depth), WIDE),
            jax.ShapeDtypeStruct((depth, quarter), WIDE),
            jax.ShapeDtypeStruct((height - depth, width), WIDE),
        ),
        in_specs=[SMEM] + [vmem] * (1 + len(arrived)),
        out_specs=(vmem,) * 5,
        compiler_params=params(),
        cost_estimate=LITTLE,
        name="last_sums",
    )(info, own, *arrived)


def position_of(token_index):
    branch_place = TRUNK + (token_index - TRUNK) % BRANCH
    leaf_place = TRUNK + BRANCH + (token_index - TOK_DEV) % BRANCH
    return jnp.where(
        token_index < TRUNK, token_index, jnp.where(token_index < TOK_DEV, branch_place, leaf_place)
    )


def rotary_tables(positions):
    half_dim = HEAD_DIM // 2
    frequency = ROPE_BASE ** (-jnp.arange(half_dim, dtype=jnp.float32) / half_dim)
    angles = positions.astype(jnp.float32)[:, None] * frequency[None, :]
    cosine, sine = (jnp.cos(angles), jnp.sin(angles))
    return (
        jnp.concatenate([cosine, cosine], axis=1),
        jnp.concatenate([-sine, sine], axis=1),
    )


def after(values, *earlier):
    return lax.optimization_barrier((values, earlier))[0]


def fast_mesh():
    return lax.axis_size("rows") == 8 and lax.axis_size("cols") == 4


SLOT_SHARD = ((0, 2, 1, 3), (1, 3, 0, 2), (2, 0, 1, 3), (3, 1, 2, 0))
UP = [(0, 1), (1, 2), (2, 3)]
DOWN = [(1, 0), (2, 1), (3, 2)]
FAR = [(0, 3), (3, 0)]


def send_near(block):
    return lax.ppermute(block, "cols", DOWN), lax.ppermute(block, "cols", UP)


def send_far(block):
    return lax.ppermute(block, "cols", FAR)


def send_over(block):
    return lax.ppermute(block, "cols", [(0, 2), (1, 3), (2, 0), (3, 1)])


def send_second(block, near):
    place = lax.axis_index("cols")
    above, below = near
    payload = jnp.where(place == 1, above, jnp.where(place == 2, below, block))
    return lax.ppermute(payload, "cols", [(3, 1), (1, 0), (0, 2), (2, 3)])


def slot_list(block, near, second, far):
    place = lax.axis_index("cols")
    above, below = near
    end = (place == 0) | (place == 3)
    return [
        block,
        second,
        jnp.where(place == 0, above, below),
        jnp.where(end, far, above),
    ]


def send_slots(slots):
    place = lax.axis_index("cols")
    _, second, third, fourth = slots
    relay = lax.ppermute(second, "cols", [(1, 3), (0, 1), (2, 0), (3, 2)])
    relayed = relay.astype(WIDE)
    upward_load = (
        jnp.where(place == 0, third, fourth).astype(WIDE) + jnp.where(place == 1, relayed, 0.0)
    ).astype(LOW)
    downward_load = (third.astype(WIDE) + jnp.where(place == 2, relayed, 0.0)).astype(LOW)
    return (
        lax.ppermute(upward_load, "cols", UP),
        lax.ppermute(downward_load, "cols", DOWN),
        send_far(after(fourth, upward_load, downward_load)),
        relay,
    )


def flip(block, bit):
    count = lax.axis_size("rows")
    return lax.ppermute(block, "rows", [(i, i ^ bit) for i in range(count)])


def add_low(one, two):
    return (one.astype(WIDE) + two.astype(WIDE)).astype(LOW)


def chips_second(near_x, near_y, got_x, got_y):
    for_y, for_x = corner_adds(near_x, got_x, near_y, got_y)
    return (near_x, got_x, flip(for_y, 4), near_y, got_y, flip(for_x, 2))


def turn_corner(beside, across):
    half = beside.shape[0] // 2
    return jnp.concatenate([flip(beside[:half], 4), flip(across[half:], 2)], axis=0)


def send_chips(sums):
    return flip(sums[0], 2), flip(sums[1], 4)


def sum_parts(parts):
    wide = [(a[0] if a.ndim == 3 else a).astype(WIDE) for a in parts]
    if len(wide) == 1:
        return wide[0]
    return jnp.concatenate([wide[0] + wide[1] + wide[2], wide[3] + wide[4] + wide[5]], axis=0)


def on_device(
    tokens,
    query_weight,
    key_weight,
    value_weight,
    out_weight,
    router_weight,
    attention_gain,
    experts_gain,
    gate_weight,
    upward_weight,
    down_weight,
    routes,
    leaf_parent,
    cotangent,
):
    row_count = lax.axis_size("rows")
    col_count = lax.axis_size("cols")
    row_place = lax.axis_index("rows")
    col_place = lax.axis_index("cols")
    fast = fast_mesh()
    parity = lax.rem(col_place, 2)
    tree_id = lax.div(row_place * col_count + col_place, 2)
    parent_row = lax.dynamic_slice_in_dim(leaf_parent, tree_id, 1, 0)[0]
    depth, query_part = query_weight.shape
    key_part = key_weight.shape[1]
    router_part = router_weight.shape[1]
    gain_part = attention_gain.shape[0]
    expert_total = router_part * col_count
    local_experts = gate_weight.shape[0]
    capacity = TOK_DEV * TOP // expert_total * 5 // 4

    shards = (
        jnp.asarray(SLOT_SHARD, jnp.int32)[col_place]
        if fast
        else jnp.arange(4, dtype=jnp.int32)
    )
    branch_rows = jnp.where(parity == 0, TRUNK + BRANCH * parent_row, TRUNK)
    info = jnp.concatenate(
        [jnp.stack([row_place, parity]), shards, branch_rows, jnp.zeros((2,), jnp.int32)]
    ).astype(jnp.int32)

    packed = jnp.concatenate([query_weight, key_weight, value_weight, out_weight], axis=1)
    local_index = (1 - parity) * TOK_DEV + jnp.arange(TOK_DEV, dtype=jnp.int32)
    cosine, sine = rotary_tables(position_of(local_index))
    shard_blocks = [
        jnp.concatenate(
            [gate_weight[expert].T, upward_weight[expert].T, down_weight[expert]], axis=0
        )
        for expert in range(local_experts)
    ]
    expert_refs = []
    if fast:
        wide = packed.shape[1]
        gains = jnp.concatenate([attention_gain, experts_gain])[None, :]
        packed = jnp.concatenate(
            [
                packed,
                jnp.pad(router_weight.T, ((0, 0), (0, wide - depth))),
                jnp.pad(gains, ((0, 0), (0, wide - 2 * gain_part))),
                jnp.pad(routes.T.astype(LOW), ((0, 0), (0, wide - TOK_DEV))),
                jnp.zeros((EXTRA - router_part - 1 - TOP, wide), LOW),
            ],
            axis=0,
        )
        packed_near = send_near(packed)
        packed_far = send_far(packed)
        packed_second = send_over(packed)
        first_block = after(shard_blocks[0], *packed_near)
        first_near = send_near(first_block)
        first_far = send_far(first_block)
        own = jnp.stack(slot_list(packed, packed_near, packed_second, packed_far))
        own = after(own, info, cosine, sine)
        beside, across = flip(own, 2), flip(own, 4)
        own_in = flip(own, 1)
        beside, across = after((beside, across), own_in, *first_near)
        corner = [flip(beside[:2], 4), flip(across[2:], 2)]
        pair_in = flip(jnp.concatenate([beside, across], axis=0), 1)
        corner_in = [flip(piece, 1) for piece in corner]
        grad_in = after(cotangent, *corner)
        grad_flips = [flip(grad_in, 2), flip(grad_in, 4)]
        pieces = [own, own_in, beside, across, *corner, pair_in, *corner_in]
        at = depth + router_part + 1
        near_slots = [own, own_in, beside, pair_in, across, pair_in[4:], corner[0], corner_in[0]]
        routes_all = jnp.stack([part[0, at : at + TOP, :TOK_DEV] for part in near_slots])
        routes_all = routes_all.astype(jnp.int32)
        chosen, place_rows = tables(info, routes_all, capacity, local_experts, expert_total)
        query_refs = pair_refs = out_refs = pieces
        extra_rows = extras(info, pieces)
        router_all = extra_rows[:, :router_part, :depth]
        attention_scale = extra_rows[:, router_part, :gain_part]
        experts_scale = extra_rows[:, router_part, gain_part : 2 * gain_part]
    else:
        packed_all = lax.all_gather(lax.all_gather(packed, "cols", axis=0), "rows", axis=0)

        def unpack(start, width):
            part = packed_all[..., start : start + width]
            return jnp.swapaxes(part, 1, 2).reshape(row_count * depth, col_count * width)

        key_at = query_part
        query_refs = [unpack(0, query_part)]
        pair_refs = [
            jnp.concatenate(
                [
                    unpack(key_at, key_part).reshape(D, QUARTERS, -1),
                    unpack(key_at + key_part, key_part).reshape(D, QUARTERS, -1),
                ],
                axis=2,
            ).reshape(D, -1)
        ]
        out_refs = [unpack(key_at + 2 * key_part, query_part)]
        routes_all = lax.all_gather(routes.T, "rows", axis=0)
        chosen, place_rows = tables(info, routes_all, capacity, local_experts, expert_total)
        axes = ("rows", "cols")
        router_all = jnp.swapaxes(lax.all_gather(router_weight, axes, axis=0), 1, 2)
        attention_scale = lax.all_gather(attention_gain, axes, axis=0)
        experts_scale = lax.all_gather(experts_gain, axes, axis=0)

    attention_scale = attention_scale.reshape(1, D).astype(WIDE)
    experts_scale = experts_scale.reshape(1, D).astype(WIDE)
    router_rows = jnp.transpose(
        router_all.reshape(row_count, col_count, router_part, depth), (1, 2, 0, 3)
    ).reshape(expert_total, D)
    router_cols = router_rows.T
    tokens_in = after(tokens, first_far, chosen) if fast else tokens
    normed, own_pair = key_value(info, tokens_in, attention_scale, cosine, sine, pair_refs)
    pairs = [(i + 1, i) for i in range(0, col_count, 2)]
    partner = lax.ppermute(own_pair, "cols", pairs)
    if fast:
        own_grad_in = flip(grad_in, 1)
        normed_in = after(normed, own_grad_in)
    else:
        normed_in = normed
    queries = query(info, normed_in, cosine, sine, query_refs)
    if fast:
        first_second = send_second(after(first_block, partner, queries), first_near)
        expert_refs.append([first_block, first_second, *first_near, first_far])
    if fast:
        grad_flips = after(grad_flips, queries)
        grad_corner = turn_corner(*grad_flips)
    heads = attention(info, queries, own_pair, partner)
    if fast:
        grad_near = [*grad_flips, grad_corner]
        grad_blocks = [cotangent, own_grad_in]
        grad_blocks += [block for one in grad_near for block in (one, flip(one, 1))]
        heads = after(heads, grad_corner, grad_blocks[3], grad_blocks[5])
    else:
        grad_all = lax.all_gather(cotangent, "rows", axis=0)
        grad_blocks = [grad_all[q] for q in range(row_count)]
    residual, normed_two = out_projection(info, heads, tokens, experts_scale, out_refs)

    if fast:
        beside, across = flip(normed_two, 2), flip(normed_two, 4)
        beside_in = flip(normed_two, 1)
        later_block = after(shard_blocks[1], first_second, normed_two)
        expert_refs.append([lax.all_gather(later_block, "cols", axis=0)])
    else:
        rows_all = lax.all_gather(normed_two, "rows", axis=0)
        expert_refs = [[lax.all_gather(block, "cols", axis=0)] for block in shard_blocks]
    grad_rows = pick_rows(chosen, grad_blocks, local_experts)

    def place_block(q, block, picked):
        return dispatch(
            q, info, block, chosen, routes_all, router_cols, local_experts, picked
        )

    if fast:
        half = TOK_DEV // 2
        picked = place_block(0, normed_two, None)
        picked = place_block(1, beside_in, after(picked, *grad_rows))
        beside, across = after((beside, across), picked)
        corner = [flip(beside[:half], 4), flip(across[half:], 2)]
        picked = place_block(2, beside, picked)
        picked = place_block(4, across, picked)
        beside_in = flip(beside, 1)
        across_in = flip(across, 1)
        picked = place_block(3, beside_in, picked)
        picked = place_block(5, across_in, picked)
        corner = jnp.concatenate(after(corner, picked), axis=0)
        corner_in = flip(corner, 1)
        picked = place_block(6, corner, picked)
        picked = place_block(7, corner_in, picked)
    else:
        picked = None
        for q in range(row_count):
            picked = place_block(q, rows_all[q], picked)
    height = row_count * capacity
    token_rows = [a.reshape(height, D) for a in picked[:local_experts]]
    grad_rows = [a.reshape(height, D) for a in grad_rows]
    share_rows = [a.reshape(height, 1) for a in picked[local_experts:]]

    out_rows, back_rows, gate_dots, reduced = ([], [], [], [])
    for e in range(local_experts):
        rows_in = after(token_rows[e], *reduced_in) if e else token_rows[e]
        out_row, back_row, grad_row, acts, dots = expert(
            info, rows_in, grad_rows[e], share_rows[e], expert_refs[e], col_count
        )
        out_rows.append(out_row.reshape(row_count, capacity, D))
        back_rows.append(back_row.reshape(row_count, capacity, D))
        gate_dots.append(dots.reshape(row_count, capacity, 1))
        if fast and e == 1:
            got = flip(combine(info, chosen, back_rows, 1, 2, gate_dots), 1)
            back_keep = combine(info, chosen, back_rows, 0, 2, gate_dots)
            for_x, for_y, near_x, near_y = chip_adds(back_keep, got)
            acts = after(acts, for_x)
            back_flips = send_chips((for_x, for_y))
        slots = expert_grads(acts, token_rows[e], grad_row)
        reduced_in = (slots,)
        if e and fast:
            out_got = flip(combine(info, chosen, out_rows, 1, 2), 1)
            out_keep = combine(info, chosen, out_rows, 0, 2)
            back_flips = after(back_flips, slots, out_keep)
            back_parts = chips_second(near_x, near_y, *back_flips)
        else:
            reduced.append(lax.psum_scatter(slots, "cols", scatter_dimension=0, tiled=False))

    if fast:
        out_first = chip_adds(out_keep, out_got)
        back_parts = after(back_parts, out_first[0])
    else:
        spread_dots = spread(place_rows, gate_dots)
        grad_shares = lax.all_to_all(spread_dots, "rows", split_axis=0, concat_axis=0, tiled=True)

        def summed(rows):
            part = combine(info, chosen, rows, 0, 1)
            return lax.psum_scatter(part, "rows", scatter_dimension=0).astype(WIDE)

        back_parts = (summed(back_rows), grad_shares.reshape(expert_total, TOK_DEV))
        mixture = (summed(out_rows),)

    grad_residual, grad_branch, grad_heads, experts_gain_grad, router_grad = branch_back(
        info,
        residual,
        normed_two,
        back_parts,
        cotangent,
        routes.T,
        router_rows,
        experts_scale,
        out_refs,
    )
    if fast:
        out_flips = send_chips(after(out_first[:2], back_parts[2], back_parts[5]))
        slots = after(slots, reduced[0], back_parts[2])
        reduced.append(lax.psum_scatter(slots, "cols", scatter_dimension=0, tiled=False))
        router_parts = jnp.transpose(
            router_grad.astype(LOW).reshape(col_count, router_part, row_count, depth),
            (2, 0, 1, 3),
        ).reshape(row_count * col_count, router_part, depth)
        gain_rows = experts_gain_grad.astype(LOW).reshape(row_count * col_count, 1, gain_part)
        extra = jnp.concatenate(
            [
                jnp.pad(router_parts, ((0, 0), (0, 0), (0, wide - depth))),
                jnp.pad(gain_rows, ((0, 0), (0, 0), (0, wide - gain_part))),
                jnp.zeros((row_count * col_count, EXTRA - router_part - 1, wide), LOW),
            ],
            axis=1,
        )
    grad_query, own_grad, source_grad = attention_back(
        info, queries, own_pair, partner, grad_heads, cosine, sine
    )
    arrived = lax.ppermute(source_grad.astype(LOW), "cols", [(j, i) for i, j in pairs])
    if fast:
        parts = ((0, 2, 0, query_part), (1, 3, query_part + 2 * key_part, query_part))
        keep_send = weight_grads(
            info, [normed, heads], [grad_query, grad_branch], parts, extra
        )
        query_back = normed_grad(info, after(grad_query, *keep_send), query_refs)
        arrived = after(arrived, query_back, *out_flips)
    else:
        query_back = normed_grad(info, grad_query, query_refs)
    grad_pair = join_grads(info, own_grad, source_grad, arrived, cosine, sine)
    if fast:
        keep, send = weight_grads(
            info, [normed], [grad_pair], ((0, 1, 0, 2 * key_part),), None, keep_send
        )
        flat = (4, col_count * (depth + EXTRA), wide)
        sent = flip(send, 1)
        sent_first = chip_adds(keep.reshape(flat), sent.reshape(flat))
        sent_chips = send_chips(sent_first[:2])
        grad_pair = after(grad_pair, sent_first[0])
    tokens_grad, attention_gain_grad = token_back(
        info, query_back, grad_pair, tokens, grad_residual, attention_scale, pair_refs
    )

    if fast:
        sent_chips = after(sent_chips, tokens_grad)
        sent_parts = chips_second(*sent_first[2:], *sent_chips)
        near_x, near_y = out_first[2:]
        mixture = chips_second(near_x, near_y, *after(out_flips, *sent_chips))
    layer_output = (residual + sum_parts(mixture)).astype(LOW)
    part = down_weight.shape[1]
    expert_sums = [block.astype(WIDE) for block in reduced]
    gate_grad, upward_grad, down_grad = (
        jnp.stack([sums_of[which * part : (which + 1) * part] for sums_of in expert_sums])
        for which in range(3)
    )
    gate_grad, upward_grad = jnp.swapaxes(gate_grad, 1, 2), jnp.swapaxes(upward_grad, 1, 2)
    if fast:
        slots = sum_parts(sent_parts)
        slots = slots.reshape(col_count, depth + EXTRA, wide)
        width = query_part + 2 * key_part
        own_slots = own
        gain_sums = sum(
            jnp.sum(own_slots[i][:depth, :width].astype(WIDE) * slots[i, :depth, :width], axis=1)
            for i in range(4)
        )
        own_gains = lax.dynamic_slice_in_dim(attention_scale[0], row_place * depth, depth, 0)
        gain_sums = (gain_sums / own_gains).reshape(col_count, 1, gain_part)
        gain_sums = jnp.pad(
            jnp.take(gain_sums, shards, axis=0),
            ((0, 0), (depth + router_part + 1, EXTRA - router_part - 2), (0, wide - gain_part)),
        )
        slots = after((slots + gain_sums).astype(LOW), reduced[1])

        arrived = send_slots(slots)
        earlier = (gate_grad, upward_grad, down_grad, layer_output)
        query_sum, key_sum, value_sum, out_sum, extra_sum = last_sums(
            info, slots[0], after(arrived, *earlier), depth, key_part
        )
        key_sum, value_sum = key_sum.T, value_sum.T
        router_sum = extra_sum[:router_part, :depth].T
        experts_gain_sum = extra_sum[router_part, :gain_part]
        attention_gain_sum = extra_sum[router_part + 1, :gain_part]
    else:
        full_grads = [
            tn(normed, grad_query),
            *jnp.moveaxis(tn(normed, grad_pair).reshape(D, QUARTERS, 2, -1), 2, 0),
            tn(heads, grad_branch),
        ]
        packed_grad = jnp.concatenate(
            [
                grad.astype(LOW).reshape(row_count, depth, col_count, -1)
                for grad in full_grads
            ],
            axis=3,
        )
        row_sums = lax.psum_scatter(packed_grad, "rows", scatter_dimension=0)
        sums = lax.psum_scatter(row_sums, "cols", scatter_dimension=1).astype(WIDE)
        key_at = query_part
        value_at = key_at + key_part
        out_at = value_at + key_part
        query_sum, out_sum = sums[:, :key_at], sums[:, out_at:]
        key_sum, value_sum = sums[:, key_at:value_at], sums[:, value_at:out_at]
        small_grads = jnp.concatenate(
            [
                attention_gain_grad.reshape(-1, gain_part),
                experts_gain_grad.reshape(-1, gain_part),
                jnp.transpose(
                    router_grad.reshape(col_count, router_part, row_count, depth), (2, 0, 3, 1)
                ).reshape(row_count * col_count, depth * router_part),
            ],
            axis=1,
        )
        small_grads = small_grads.reshape(row_count, -1)
        small_grads = lax.all_to_all(small_grads, "rows", split_axis=0, concat_axis=0, tiled=True)
        small_grads = jnp.sum(small_grads, axis=0).reshape(col_count, -1)
        small_grads = lax.all_to_all(small_grads, "cols", split_axis=0, concat_axis=0, tiled=True)
        small_sums = jnp.sum(small_grads, axis=0)
        attention_gain_sum = small_sums[:gain_part]
        experts_gain_sum = small_sums[gain_part : 2 * gain_part]
        router_sum = small_sums[2 * gain_part :].reshape(depth, router_part)

    return (
        layer_output,
        tokens_grad,
        query_sum,
        key_sum,
        value_sum,
        out_sum,
        router_sum,
        attention_gain_sum,
        experts_gain_sum,
        gate_grad,
        upward_grad,
        down_grad,
    )


def solution(mesh):
    in_specs = (
        P(("rows", "cols"), None),
        P("rows", "cols"),
        P("rows", "cols"),
        P("rows", "cols"),
        P("rows", "cols"),
        P("rows", "cols"),
        P(("rows", "cols")),
        P(("rows", "cols")),
        P("rows", None, "cols"),
        P("rows", None, "cols"),
        P("rows", "cols", None),
        P(("rows", "cols"), None),
        P(),
        P(("rows", "cols"), None),
    )
    out_specs = (
        P(("rows", "cols"), None),
        P(("rows", "cols"), None),
        P("rows", "cols"),
        P("rows", "cols"),
        P("rows", "cols"),
        P("rows", "cols"),
        P("rows", "cols"),
        P(("rows", "cols")),
        P(("rows", "cols")),
        P("rows", None, "cols"),
        P("rows", None, "cols"),
        P("rows", "cols", None),
    )
    return jax.shard_map(
        on_device, mesh=mesh, in_specs=in_specs, out_specs=out_specs, check_vma=False
    )
```

```python
import functools

import jax
import jax.numpy as jnp
from jax import lax
from jax.experimental import pallas as pl
from jax.experimental.pallas import tpu as pltpu
from jax.sharding import PartitionSpec as P

D = 1536
HEADS = 12
KV_HEADS = 2
HEAD_DIM = 128
TOP = 4
TOK_DEV = 512
BRANCHES = 4
LEAVES = 8
TRUNK = 256
BRANCH = 64

EPSILON = 1e-06
ROPE_BASE = 10000.0
MASKED = -1e30
LOW = jnp.bfloat16
WIDE = jnp.float32
KEY_WIDTH = KV_HEADS * HEAD_DIM
GROUP = HEADS // KV_HEADS
QUARTERS = 4
VMEM_LIMIT = 56 * 1024 * 1024

ANY = pl.BlockSpec(memory_space=pl.ANY)
SMEM = pl.BlockSpec(memory_space=pltpu.SMEM)


def nn(one, two):
    return lax.dot_general(one, two, (((1,), (0,)), ((), ())), preferred_element_type=WIDE)


def nt(one, two):
    return lax.dot_general(one, two, (((1,), (1,)), ((), ())), preferred_element_type=WIDE)


def tn(one, two):
    return lax.dot_general(one, two, (((0,), (0,)), ((), ())), preferred_element_type=WIDE)


def whole(shape):
    return pl.BlockSpec(shape, lambda *_: (0,) * len(shape))


LITTLE = pl.CostEstimate(flops=1, bytes_accessed=1, transcendentals=0)


def params():
    return pltpu.CompilerParams(vmem_limit_bytes=VMEM_LIMIT)


def turn(values, cosine, sine):
    return values * cosine + pltpu.roll(values, HEAD_DIM // 2, 1) * sine


def turn_back(values, cosine, sine):
    return values * cosine - pltpu.roll(values, HEAD_DIM // 2, 1) * sine


SLOTS = range(4)
PIECES = (
    tuple((0, slot) for slot in SLOTS),
    tuple((1, slot) for slot in SLOTS),
    tuple((2, slot) for slot in SLOTS),
    tuple((4, slot) for slot in SLOTS),
    ((6, 0), (6, 1)),
    ((6, 2), (6, 3)),
    tuple((flip_bits, slot) for flip_bits in (3, 5) for slot in SLOTS),
    ((7, 0), (7, 1)),
    ((7, 2), (7, 3)),
)
EXTRA = 16


STEP = 768


def weight_copies(info, refs, target, sem, start, width):
    if len(refs) == 1:
        return [pltpu.make_async_copy(refs[0], target, sem)]
    depth = refs[0].shape[1] - EXTRA
    copies = []
    for ref, parts in zip(refs, PIECES):
        for at, (flip_bits, slot) in enumerate(parts):
            row = pl.multiple_of((info[0] ^ flip_bits) * depth, depth)
            col = pl.multiple_of(info[2 + slot] * width, 128)
            copies.append(
                pltpu.make_async_copy(
                    ref.at[at, pl.ds(0, depth), pl.ds(start, width)],
                    target.at[pl.ds(row, depth), pl.ds(col, width)],
                    sem,
                )
            )
    return copies


def extras_kernel(info, *rest):
    refs, (out, sem) = rest[:-2], rest[-2:]
    depth = refs[0].shape[1] - EXTRA
    copies = []
    for ref, parts in zip(refs, PIECES):
        for at, (flip_bits, slot) in enumerate(parts):
            to = (info[0] ^ flip_bits) * QUARTERS + info[2 + slot]
            copies.append(pltpu.make_async_copy(ref.at[at, pl.ds(depth, EXTRA)], out.at[to], sem))
    run_all(copies)
    wait_all(copies)


def extras(info, refs):
    return pl.pallas_call(
        extras_kernel,
        out_shape=jax.ShapeDtypeStruct((8 * QUARTERS, EXTRA, refs[0].shape[2]), LOW),
        in_specs=[SMEM] + [ANY] * len(refs),
        out_specs=pl.BlockSpec(memory_space=pltpu.VMEM),
        scratch_shapes=[pltpu.SemaphoreType.DMA],
        compiler_params=params(),
        cost_estimate=LITTLE,
        name="extra_rows",
    )(info, *refs)


def run_all(copies):
    for copy in copies:
        copy.start()


def wait_all(copies):
    for copy in copies:
        copy.wait()


def key_value_kernel(info, tokens, gain, cosine, sine, *rest):
    count = len(rest) - 4
    refs, (normed, out, weight, sem) = rest[:count], rest[count:]
    copies = weight_copies(info, refs, weight, sem, D // QUARTERS, 128)
    run_all(copies)
    values = tokens[...].astype(WIDE)
    factor = lax.rsqrt(jnp.mean(values * values, axis=-1, keepdims=True) + EPSILON)
    low = (values * factor * gain[...]).astype(LOW)
    normed[...] = low
    wait_all(copies)
    both = nn(low, weight[...])
    half = HEAD_DIM // 2
    first = lax.broadcasted_iota(jnp.int32, (TOK_DEV, HEAD_DIM), 1) < half
    for g in range(KV_HEADS):
        one = both[:, 256 * g : 256 * g + 128]
        two = both[:, 256 * g + 128 : 256 * g + 256]
        key = jnp.where(first, one, pltpu.roll(two, half, 1))
        value = jnp.where(first, pltpu.roll(one, half, 1), two)
        out[:, 128 * g : 128 * g + 128] = turn(key, cosine[...], sine[...]).astype(LOW)
        out[:, KEY_WIDTH + 128 * g : KEY_WIDTH + 128 * g + 128] = value.astype(LOW)


def key_value(info, tokens, gain, cosine, sine, refs):
    return pl.pallas_call(
        key_value_kernel,
        out_shape=(
            jax.ShapeDtypeStruct((TOK_DEV, D), LOW),
            jax.ShapeDtypeStruct((TOK_DEV, 2 * KEY_WIDTH), LOW),
        ),
        in_specs=[SMEM] + [pl.BlockSpec(memory_space=pltpu.VMEM)] * 4 + [ANY] * len(refs),
        out_specs=(pl.BlockSpec(memory_space=pltpu.VMEM),) * 2,
        scratch_shapes=[pltpu.VMEM((D, 2 * KEY_WIDTH), LOW), pltpu.SemaphoreType.DMA],
        compiler_params=params(),
        cost_estimate=LITTLE,
        name="norm_key_value",
    )(info, tokens, gain, cosine, sine, *refs)


def query_kernel(info, normed, cosine, sine, *rest):
    count = len(rest) - 3
    refs, (out, weight, sem) = rest[:count], rest[count:]

    @pl.when(pl.program_id(0) == 0)
    def _():
        copies = weight_copies(info, refs, weight, sem, 0, D // QUARTERS)
        run_all(copies)
        wait_all(copies)

    at = pl.multiple_of(pl.program_id(0) * STEP, STEP)
    lin = nn(normed[...], weight[:, pl.ds(at, STEP)])
    for h in range(STEP // HEAD_DIM):
        out[:, 128 * h : 128 * h + 128] = turn(
            lin[:, 128 * h : 128 * h + 128], cosine[...], sine[...]
        ).astype(LOW)


def query(info, normed, cosine, sine, refs):
    return pl.pallas_call(
        query_kernel,
        grid=(D // STEP,),
        out_shape=jax.ShapeDtypeStruct((TOK_DEV, D), LOW),
        in_specs=[SMEM, whole((TOK_DEV, D)), whole((TOK_DEV, 128)), whole((TOK_DEV, 128))]
        + [ANY] * len(refs),
        out_specs=pl.BlockSpec((TOK_DEV, STEP), lambda i: (0, i)),
        scratch_shapes=[pltpu.VMEM((D, D), LOW), pltpu.SemaphoreType.DMA],
        compiler_params=params(),
        cost_estimate=LITTLE,
        name="query_projection",
    )(info, normed, cosine, sine, *refs)


KEYS = TRUNK + 2 * BRANCH
CHUNKS = TOK_DEV // BRANCH


def chunk_keys(info, source, own, column, chunk):
    at = pl.multiple_of(info[6 + chunk], BRANCH)
    rows = pl.multiple_of(chunk * BRANCH, BRANCH)
    columns = slice(column, column + HEAD_DIM)
    return jnp.concatenate(
        [
            source[0:TRUNK, columns],
            source[pl.ds(at, BRANCH), columns],
            own[pl.ds(rows, BRANCH), columns],
        ],
        axis=0,
    )


def chunk_allowed(info, chunk, query_axis, shape):
    query_row = lax.broadcasted_iota(jnp.int32, shape, query_axis) & (BRANCH - 1)
    key = lax.broadcasted_iota(jnp.int32, shape, 1 - query_axis)
    leaves = info[1] == 0
    trunk = jnp.logical_and(jnp.logical_not(leaves), chunk < TRUNK // BRANCH)
    limit = jnp.where(trunk, chunk * BRANCH + query_row, TRUNK - 1)
    branch_limit = jnp.where(leaves, TRUNK + BRANCH - 1, 0)
    own_limit = jnp.where(trunk, 0, query_row + TRUNK + BRANCH)
    top = jnp.where(key < TRUNK, limit, jnp.where(key < TRUNK + BRANCH, branch_limit, own_limit))
    return key <= top


def group_rows(ref, g):
    first = g * GROUP
    return jnp.concatenate(
        [ref[:, 128 * h : 128 * h + 128] for h in range(first, first + GROUP)], axis=0
    )


def keep_source(info, partner, own, source):
    @pl.when(pl.program_id(0) == 0)
    def _():
        @pl.when(info[1] == 0)
        def _():
            source[...] = partner[...]

        @pl.when(info[1] != 0)
        def _():
            source[...] = own[...]


def attention_kernel(info, queries, own, partner, out, source):
    keep_source(info, partner, own, source)
    chunk = pl.program_id(0)
    rows = GROUP * BRANCH
    allowed = chunk_allowed(info, chunk, 0, (rows, KEYS))
    for g in range(KV_HEADS):
        keys = chunk_keys(info, source, own, 128 * g, chunk)
        values = chunk_keys(info, source, own, KEY_WIDTH + 128 * g, chunk)
        scores = nt(group_rows(queries, g), keys) * HEAD_DIM**-0.5
        scores = jnp.where(allowed, scores, MASKED)
        weights = jnp.exp(scores - jnp.max(scores, axis=1, keepdims=True))
        total = jnp.sum(weights, axis=1, keepdims=True)
        mixed = nn((weights * (1.0 / total)).astype(LOW), values).astype(LOW)
        for h in range(GROUP):
            at = (g * GROUP + h) * 128
            out[:, at : at + 128] = mixed[h * BRANCH : (h + 1) * BRANCH]


def attention(info, queries, own, partner):
    return pl.pallas_call(
        attention_kernel,
        grid=(CHUNKS,),
        out_shape=jax.ShapeDtypeStruct((TOK_DEV, D), LOW),
        in_specs=[
            SMEM,
            pl.BlockSpec((BRANCH, D), lambda i: (i, 0)),
            whole((TOK_DEV, 2 * KEY_WIDTH)),
            whole((TOK_DEV, 2 * KEY_WIDTH)),
        ],
        out_specs=pl.BlockSpec((BRANCH, D), lambda i: (i, 0)),
        scratch_shapes=[pltpu.VMEM((TOK_DEV, 2 * KEY_WIDTH), LOW)],
        compiler_params=params(),
        cost_estimate=LITTLE,
        name="tree_attention",
    )(info, queries, own, partner)


def attention_back_kernel(
    info, queries, own, partner, grads, cosine, sine, grad_query, own_grad, source_grad, source
):
    keep_source(info, partner, own, source)
    chunk = pl.program_id(0)

    @pl.when(chunk == 0)
    def _():
        source_grad[...] = jnp.zeros_like(source_grad)

    rows = GROUP * BRANCH
    scale = HEAD_DIM**-0.5
    allowed = chunk_allowed(info, chunk, 1, (KEYS, rows))
    at = pl.multiple_of(info[6 + chunk], BRANCH)
    for g in range(KV_HEADS):
        keys = chunk_keys(info, source, own, 128 * g, chunk)
        values = chunk_keys(info, source, own, KEY_WIDTH + 128 * g, chunk)
        query_rows = group_rows(queries, g)
        grad_rows = group_rows(grads, g)
        scores = jnp.where(allowed, nt(keys, query_rows) * scale, MASKED)
        weights = jnp.exp(scores - jnp.max(scores, axis=0, keepdims=True))
        probs = weights * (1.0 / jnp.sum(weights, axis=0, keepdims=True))
        grad_probs = nt(values, grad_rows)
        mean = jnp.sum(probs * grad_probs, axis=0, keepdims=True)
        grad_scores = (probs * (grad_probs - mean)).astype(LOW)
        grad_values = nn(probs.astype(LOW), grad_rows)
        grad_keys = nn(grad_scores, query_rows) * scale
        grad_queries = tn(grad_scores, keys) * scale
        for h in range(GROUP):
            to = (g * GROUP + h) * 128
            grad_query[:, to : to + 128] = turn_back(
                grad_queries[h * BRANCH : (h + 1) * BRANCH], cosine[...], sine[...]
            ).astype(LOW)
        for column, grad in ((128 * g, grad_keys), (KEY_WIDTH + 128 * g, grad_values)):
            columns = slice(column, column + 128)
            source_grad[0:TRUNK, columns] += grad[0:TRUNK]
            source_grad[pl.ds(at, BRANCH), columns] += grad[TRUNK : TRUNK + BRANCH]
            own_grad[:, columns] = grad[TRUNK + BRANCH :]


def attention_back(info, queries, own, partner, grads, cosine, sine):
    chunked = pl.BlockSpec((BRANCH, D), lambda i: (i, 0))
    pair = (TOK_DEV, 2 * KEY_WIDTH)
    return pl.pallas_call(
        attention_back_kernel,
        grid=(CHUNKS,),
        out_shape=(
            jax.ShapeDtypeStruct((TOK_DEV, D), LOW),
            jax.ShapeDtypeStruct(pair, WIDE),
            jax.ShapeDtypeStruct(pair, WIDE),
        ),
        in_specs=[
            SMEM,
            chunked,
            whole(pair),
            whole(pair),
            chunked,
            pl.BlockSpec((BRANCH, 128), lambda i: (i, 0)),
            pl.BlockSpec((BRANCH, 128), lambda i: (i, 0)),
        ],
        out_specs=(
            chunked,
            pl.BlockSpec((BRANCH, 2 * KEY_WIDTH), lambda i: (i, 0)),
            whole(pair),
        ),
        scratch_shapes=[pltpu.VMEM(pair, LOW)],
        compiler_params=params(),
        cost_estimate=LITTLE,
        name="tree_attention_back",
    )(info, queries, own, partner, grads, cosine, sine)


def out_kernel(info, heads, tokens, gain, *rest):
    count = len(rest) - 4
    refs, (residual, normed, weight, sem) = rest[:count], rest[count:]

    @pl.when(pl.program_id(0) == 0)
    def _():
        copies = weight_copies(info, refs, weight, sem, D // QUARTERS + 128, D // QUARTERS)
        run_all(copies)
        wait_all(copies)

    at = pl.ds(pl.multiple_of(pl.program_id(0) * STEP, STEP), STEP)
    residual[:, at] = tokens[:, at].astype(WIDE) + nn(heads[...], weight[:, at])

    @pl.when(pl.program_id(0) == pl.num_programs(0) - 1)
    def _():
        values = residual[...]
        factor = lax.rsqrt(jnp.mean(values * values, axis=-1, keepdims=True) + EPSILON)
        normed[...] = (values * factor * gain[...]).astype(LOW)


def out_projection(info, heads, tokens, gain, refs):
    full = (TOK_DEV, D)
    return pl.pallas_call(
        out_kernel,
        grid=(D // STEP,),
        out_shape=(jax.ShapeDtypeStruct(full, WIDE), jax.ShapeDtypeStruct(full, LOW)),
        in_specs=[SMEM, whole(full), whole(full), whole((1, D))] + [ANY] * len(refs),
        out_specs=(whole(full), whole(full)),
        scratch_shapes=[pltpu.VMEM((D, D), LOW), pltpu.SemaphoreType.DMA],
        compiler_params=params(),
        cost_estimate=LITTLE,
        name="out_projection",
    )(info, heads, tokens, gain, *refs)


def hits_of(routes, ids):
    hit = ids == routes[0, 0:1]
    for k in range(1, TOP):
        hit = jnp.logical_or(hit, ids == routes[0, k : k + 1])
    return hit


def tables_kernel(capacity, local, total, info, routes, chosen_out, place_out, earlier):
    @pl.when(pl.program_id(0) == 0)
    def _():
        one = lax.broadcasted_iota(jnp.int32, (TOK_DEV, TOK_DEV), 0)
        two = lax.broadcasted_iota(jnp.int32, (TOK_DEV, TOK_DEV), 1)
        earlier[...] = jnp.where(one < two, 1.0, 0.0).astype(LOW)

    ids = lax.broadcasted_iota(jnp.int32, (total, TOK_DEV), 0)
    hit = hits_of(routes, ids)
    rank = nn(jnp.where(hit, 1.0, 0.0).astype(LOW), earlier[...])
    place = jnp.where(hit, rank, -1.0)
    spots = lax.broadcasted_iota(jnp.int32, (capacity, TOK_DEV), 0).astype(WIDE)
    place_out[0] = jnp.full(place_out.shape[1:], -1.0, WIDE)
    for e in range(local):
        mine = ids == info[0] * local + e
        place_row = jnp.sum(jnp.where(mine, place, 0.0), axis=0, keepdims=True)
        place_out[0, e : e + 1] = place_row
        chosen_out[0, e * capacity : (e + 1) * capacity] = jnp.where(
            spots == place_row, 1.0, 0.0
        ).astype(LOW)


def tables(info, routes, capacity, local, total):
    count = routes.shape[0]
    return pl.pallas_call(
        functools.partial(tables_kernel, capacity, local, total),
        grid=(count,),
        in_specs=[SMEM, pl.BlockSpec((1, TOP, TOK_DEV), lambda i: (i, 0, 0))],
        out_specs=[
            pl.BlockSpec((1, local * capacity, TOK_DEV), lambda i: (i, 0, 0)),
            pl.BlockSpec((1, 8, TOK_DEV), lambda i: (i, 0, 0)),
        ],
        scratch_shapes=[pltpu.VMEM((TOK_DEV, TOK_DEV), LOW)],
        out_shape=[
            jax.ShapeDtypeStruct((count, local * capacity, TOK_DEV), LOW),
            jax.ShapeDtypeStruct((count, 8, TOK_DEV), WIDE),
        ],
        compiler_params=params(),
        cost_estimate=LITTLE,
        name="route_tables",
    )(info, routes)


def pick_kernel(local, count, chosen, *rest):
    blocks, outs = rest[:count], rest[count : count + local]
    picks, block_in, out_block, sem_in, sem_out = rest[count + local :]
    capacity = outs[0].shape[1]
    copies = [
        (
            pltpu.make_async_copy(chosen.at[q], picks.at[q], sem_in.at[q, 0]),
            pltpu.make_async_copy(blocks[q], block_in.at[q], sem_in.at[q, 1]),
        )
        for q in range(count)
    ]
    for pair in copies:
        run_all(pair)
    sent = []
    for q in range(count):
        wait_all(copies[q])
        out_block[q] = nn(picks[q], block_in[q]).astype(LOW)
        for e in range(local):
            copy = pltpu.make_async_copy(
                out_block.at[q, pl.ds(e * capacity, capacity)], outs[e].at[q], sem_out.at[q, e]
            )
            copy.start()
            sent.append(copy)
    wait_all(sent)


def pick_rows(chosen, blocks, local):
    count, height, _ = chosen.shape
    return pl.pallas_call(
        functools.partial(pick_kernel, local, count),
        in_specs=[ANY] * (1 + count),
        out_specs=[ANY] * local,
        out_shape=[jax.ShapeDtypeStruct((count, height // local, D), LOW)] * local,
        scratch_shapes=[
            pltpu.VMEM((count, height, TOK_DEV), LOW),
            pltpu.VMEM((count, TOK_DEV, D), LOW),
            pltpu.VMEM((count, height, D), LOW),
            pltpu.SemaphoreType.DMA((count, 2)),
            pltpu.SemaphoreType.DMA((count, local)),
        ],
        compiler_params=params(),
        cost_estimate=LITTLE,
        name="pick_rows",
    )(chosen, *blocks)


def dispatch_kernel(local, info, rows, chosen, routes, router, *rest):
    outs, logits = rest[2 * local : 4 * local], rest[-1]
    total = router.shape[1]
    step = pl.program_id(0)
    block = rows[...]
    rows_of = nn(chosen[0], block).astype(LOW)
    capacity = outs[0].shape[1]
    for e in range(local):
        outs[e][0] = rows_of[e * capacity : (e + 1) * capacity]
    part = nn(block, router[...])

    @pl.when(step == 0)
    def _():
        logits[...] = part

    @pl.when(step > 0)
    def _():
        logits[...] += part

    @pl.when(step == pl.num_programs(0) - 1)
    def _():
        values = logits[...].T
        ids = lax.broadcasted_iota(jnp.int32, (total, TOK_DEV), 0)
        weights = jnp.exp(values - jnp.max(values, axis=0, keepdims=True))
        hit = hits_of(routes, ids)
        share = weights / jnp.sum(jnp.where(hit, weights, 0.0), axis=0, keepdims=True)
        for e in range(local):
            mine = ids == info[0] * local + e
            share_row = jnp.sum(jnp.where(mine, share, 0.0), axis=0, keepdims=True)
            picked = chosen[0, e * capacity : (e + 1) * capacity].astype(WIDE)
            outs[local + e][0] = jnp.sum(picked * share_row, axis=1, keepdims=True)


def dispatch(at, info, rows, chosen, routes, router, local, earlier):
    count, height, _ = chosen.shape
    capacity = height // local
    total = router.shape[1]
    wide = D
    out_shape = [jax.ShapeDtypeStruct((count, capacity, D), LOW)] * local + [
        jax.ShapeDtypeStruct((count, capacity, 1), WIDE)
    ] * local
    if earlier is None:
        earlier = [jnp.zeros((8, 128), shape.dtype) for shape in out_shape]
        aliases = {}
    else:
        aliases = {5 + i: i for i in range(len(out_shape))}
    return pl.pallas_call(
        functools.partial(dispatch_kernel, local),
        grid=(D // wide,),
        in_specs=[
            SMEM,
            pl.BlockSpec((TOK_DEV, wide), lambda i: (0, i)),
            pl.BlockSpec((1, height, TOK_DEV), lambda i: (at, 0, 0)),
            pl.BlockSpec((1, TOP, TOK_DEV), lambda i: (at, 0, 0)),
            pl.BlockSpec((wide, total), lambda i: (i, 0)),
        ]
        + [ANY] * len(out_shape),
        out_specs=[pl.BlockSpec((1, capacity, wide), lambda i: (at, 0, i))] * local
        + [pl.BlockSpec((1, capacity, 1), lambda i: (at, 0, 0))] * local,
        scratch_shapes=[pltpu.VMEM((TOK_DEV, total), WIDE)],
        out_shape=out_shape,
        input_output_aliases=aliases,
        compiler_params=params(),
        cost_estimate=LITTLE,
        name="dispatch",
    )(info, rows, chosen, routes, router, *earlier)


def spread_kernel(local, place, *rest):
    dots, out = rest[:local], rest[local]
    spots = lax.broadcasted_iota(jnp.int32, (dots[0].shape[1], TOK_DEV), 0).astype(WIDE)
    for e in range(local):
        chosen = spots == place[0, e : e + 1]
        out[0, e : e + 1] = jnp.sum(jnp.where(chosen, dots[e][0], 0.0), axis=0, keepdims=True)


def spread(place, dots):
    count, capacity, _ = dots[0].shape
    local = len(dots)
    return pl.pallas_call(
        functools.partial(spread_kernel, local),
        grid=(count,),
        out_shape=jax.ShapeDtypeStruct((count, local, TOK_DEV), WIDE),
        in_specs=[pl.BlockSpec((1, 8, TOK_DEV), lambda i: (i, 0, 0))]
        + [pl.BlockSpec((1, capacity, 1), lambda i: (i, 0, 0))] * local,
        out_specs=pl.BlockSpec((1, local, TOK_DEV), lambda i: (i, 0, 0)),
        compiler_params=params(),
        cost_estimate=LITTLE,
        name="spread",
    )(place, *dots)


def expert_kernel(slots, info, rows, grads, shares, *rest):
    refs, (out_rows, back_rows, grad_rows, acts, dots, weight, sem) = rest[:-7], rest[-7:]
    part = weight.shape[1] // slots

    @pl.when(pl.program_id(0) == 0)
    def _():
        def copies(ref, slot):
            return [
                pltpu.make_async_copy(
                    ref.at[pl.ds(which * part, part)],
                    weight.at[which, pl.ds(pl.multiple_of(slot * part, part), part)],
                    sem,
                )
                for which in range(3)
            ]

        if len(refs) == 1:
            for slot in range(slots):
                run_all(copies(refs[0].at[slot], slot))
            for slot in range(slots):
                wait_all(copies(refs[0].at[slot], slot))
        else:
            block, second, above, below, far = refs
            low_end = info[2] == 0
            end = jnp.logical_or(low_end, info[2] == 3)
            run_all(copies(block, info[2]))
            run_all(copies(second, info[3]))

            @pl.when(low_end)
            def _():
                run_all(copies(above, info[4]))

            @pl.when(jnp.logical_not(low_end))
            def _():
                run_all(copies(below, info[4]))

            @pl.when(end)
            def _():
                run_all(copies(far, info[5]))

            @pl.when(jnp.logical_not(end))
            def _():
                run_all(copies(above, info[5]))

            for slot in range(slots):
                wait_all(copies(block, slot))

    row_block = rows[...]
    share = shares[...]
    grad_float = grads[...].astype(WIDE)
    grad_low = (share * grad_float).astype(LOW)
    grad_rows[...] = grad_low
    gate_act = nt(row_block, weight[0])
    upward = nt(row_block, weight[1])
    sigmoid = 1.0 / (1.0 + jnp.exp(-gate_act))
    silu = gate_act * sigmoid
    hidden = (silu * upward).astype(LOW)
    expert_out = nn(hidden, weight[2]).astype(LOW).astype(WIDE)
    out_rows[...] = (share * expert_out).astype(LOW)
    dots[...] = jnp.sum(grad_float * expert_out, axis=1, keepdims=True)
    grad_hidden = nt(grad_low, weight[2])
    grad_gate = (grad_hidden * upward * sigmoid * (1.0 + gate_act * (1.0 - sigmoid))).astype(LOW)
    grad_up = (grad_hidden * silu).astype(LOW)
    back_rows[...] = (nn(grad_gate, weight[0]) + nn(grad_up, weight[1])).astype(LOW)
    for which, act in enumerate((grad_gate, grad_up, hidden)):
        turned = act.T
        for slot in range(slots):
            acts[slot, which * part : (which + 1) * part] = turned[
                slot * part : (slot + 1) * part
            ]


EXPERT_ROWS = 256


def expert(info, rows, grads, shares, refs, slots):
    height = rows.shape[0]
    part = refs[0].shape[-2] // 3
    wide_block = pl.BlockSpec((EXPERT_ROWS, D), lambda i: (i, 0))
    thin_block = pl.BlockSpec((EXPERT_ROWS, 1), lambda i: (i, 0))
    return pl.pallas_call(
        functools.partial(expert_kernel, slots),
        grid=(height // EXPERT_ROWS,),
        out_shape=[jax.ShapeDtypeStruct((height, D), LOW)] * 3
        + [
            jax.ShapeDtypeStruct((slots, 3 * part, height), LOW),
            jax.ShapeDtypeStruct((height, 1), WIDE),
        ],
        in_specs=[SMEM, wide_block, wide_block, thin_block] + [ANY] * len(refs),
        out_specs=[wide_block] * 3
        + [pl.BlockSpec((slots, 3 * part, EXPERT_ROWS), lambda i: (0, 0, i)), thin_block],
        scratch_shapes=[pltpu.VMEM((3, slots * part, D), LOW), pltpu.SemaphoreType.DMA],
        compiler_params=params(),
        cost_estimate=LITTLE,
        name="expert",
    )(info, rows, grads, shares, *refs)


def expert_grads_kernel(acts, rows, grads, out):
    slots, height, _ = acts.shape
    part = height // 3
    for slot in range(slots):
        out[slot, : 2 * part] = nn(acts[slot, : 2 * part], rows[...]).astype(LOW)
        out[slot, 2 * part :] = nn(acts[slot, 2 * part :], grads[...]).astype(LOW)


def expert_grads(acts, rows, grads):
    slots, part, height = acts.shape
    strip = pl.BlockSpec((height, 256), lambda i: (0, i))
    return pl.pallas_call(
        expert_grads_kernel,
        grid=(D // 256,),
        out_shape=jax.ShapeDtypeStruct((slots, part, D), LOW),
        in_specs=[whole(acts.shape), strip, strip],
        out_specs=pl.BlockSpec((slots, part, 256), lambda i: (0, 0, i)),
        compiler_params=params(),
        cost_estimate=LITTLE,
        name="expert_gradients",
    )(acts, rows, grads)


SHARE_ROWS = 32


def combine_kernel(local, first, step, info, chosen, *rest):
    rows, dots, out = rest[:local], rest[local:-6], rest[-6]
    picks, rows_in, out_block, sem_in, sem_out = rest[-5:]
    number = out.shape[0]
    capacity = rows[0].shape[1]
    copies = []
    for n in range(number):
        q = first + step * n
        copies.append(
            [pltpu.make_async_copy(chosen.at[q], picks.at[n], sem_in.at[n, local])]
            + [
                pltpu.make_async_copy(
                    rows[e].at[q],
                    rows_in.at[n, pl.ds(e * capacity, capacity)],
                    sem_in.at[n, e],
                )
                for e in range(local)
            ]
        )
    for group in copies:
        run_all(group)
    sent = []
    for n in range(number):
        wait_all(copies[n])
        out_block[n, :TOK_DEV] = tn(picks[n], rows_in[n]).astype(LOW)
        if dots:
            row = lax.broadcasted_iota(jnp.int32, (SHARE_ROWS, D), 0)
            values = jnp.zeros((SHARE_ROWS, D), WIDE)
            for e in range(local):
                picked = picks[n, e * capacity : (e + 1) * capacity].astype(WIDE)
                share = picked * dots[e][first + step * n]
                high, low = split(jnp.sum(share, axis=0, keepdims=True))
                pieces = [high.astype(WIDE), low.astype(WIDE)]
                pieces.append(jnp.zeros((1, D - 2 * TOK_DEV), WIDE))
                line = jnp.concatenate(pieces, axis=1)
                values = jnp.where(row == info[0] * local + e, line, values)
            out_block[n, TOK_DEV:] = values.astype(LOW)
        copy = pltpu.make_async_copy(out_block.at[n], out.at[n], sem_out.at[n])
        copy.start()
        sent.append(copy)
    wait_all(sent)


def combine(info, chosen, rows, first, step, dots=()):
    count, capacity, _ = rows[0].shape
    local = len(rows)
    number = (count - first + step - 1) // step
    height = TOK_DEV + (SHARE_ROWS if dots else 0)
    return pl.pallas_call(
        functools.partial(combine_kernel, local, first, step),
        out_shape=jax.ShapeDtypeStruct((number, height, D), LOW),
        in_specs=[SMEM, ANY]
        + [ANY] * local
        + [pl.BlockSpec(memory_space=pltpu.VMEM)] * len(dots),
        out_specs=ANY,
        scratch_shapes=[
            pltpu.VMEM((number, local * capacity, TOK_DEV), LOW),
            pltpu.VMEM((number, local * capacity, D), LOW),
            pltpu.VMEM((number, height, D), LOW),
            pltpu.SemaphoreType.DMA((number, local + 1)),
            pltpu.SemaphoreType.DMA((number,)),
        ],
        compiler_params=params(),
        cost_estimate=LITTLE,
        name="combine",
    )(info, chosen, *rows, *dots)


def chip_adds_kernel(keep, got, send_x, send_y, near_x, near_y, one, two, sem_in, sem_out):
    half = send_x.shape[1]
    copies = [
        (
            pltpu.make_async_copy(keep.at[i], one.at[i], sem_in.at[i, 0]),
            pltpu.make_async_copy(got.at[i], two.at[i], sem_in.at[i, 1]),
        )
        for i in range(4)
    ]
    for pair in copies:
        run_all(pair)
    sent = []
    for i in range(4):
        wait_all(copies[i])
        one[i] = (one[i].astype(WIDE) + two[i].astype(WIDE)).astype(LOW)
        upper = (near_x, send_x)[i % 2].at[i // 2]
        lower = (near_y, send_y)[i // 2].at[i % 2]
        for part, to in enumerate((upper, lower)):
            copy = pltpu.make_async_copy(
                one.at[i, pl.ds(part * half, half)], to, sem_out.at[i, part]
            )
            copy.start()
            sent.append(copy)
    wait_all(sent)


def chip_adds(keep, got):
    _, height, width = keep.shape
    shape = jax.ShapeDtypeStruct((2, height // 2, width), LOW)
    return pl.pallas_call(
        chip_adds_kernel,
        out_shape=(shape,) * 4,
        in_specs=[ANY, ANY],
        out_specs=(ANY,) * 4,
        scratch_shapes=[
            pltpu.VMEM(keep.shape, LOW),
            pltpu.VMEM(keep.shape, LOW),
            pltpu.SemaphoreType.DMA((4, 2)),
            pltpu.SemaphoreType.DMA((4, 2)),
        ],
        compiler_params=params(),
        cost_estimate=LITTLE,
        name="chip_sums",
    )(keep, got)


def corner_adds_kernel(near_x, got_x, near_y, got_y, send_y, send_x):
    send_y[...] = (near_x[0].astype(WIDE) + got_x[0].astype(WIDE)).astype(LOW)
    send_x[...] = (near_y[0].astype(WIDE) + got_y[0].astype(WIDE)).astype(LOW)


def corner_adds(near_x, got_x, near_y, got_y):
    _, half, width = near_x.shape
    rows = half
    block = pl.BlockSpec((1, rows, width), lambda i: (1, i, 0))
    out = pl.BlockSpec((rows, width), lambda i: (i, 0))
    return pl.pallas_call(
        corner_adds_kernel,
        grid=(half // rows,),
        out_shape=(jax.ShapeDtypeStruct((half, width), LOW),) * 2,
        in_specs=[block] * 4,
        out_specs=(out, out),
        compiler_params=params(),
        cost_estimate=LITTLE,
        name="corner_sums",
    )(near_x, got_x, near_y, got_y)


def split(values):
    high = values.astype(LOW)
    return high, (values - high.astype(WIDE)).astype(LOW)


def norm_back(values, gain, grad):
    factor = lax.rsqrt(jnp.mean(values * values, axis=-1, keepdims=True) + EPSILON)
    scaled = gain * grad
    mean = jnp.mean(values * scaled, axis=-1, keepdims=True)
    grad_values = factor * scaled - values * (factor * factor * factor * mean)
    grad_gain = jnp.sum(grad * values * factor, axis=0, keepdims=True)
    return grad_values, grad_gain


def router_back(logits, routes, grad_shares):
    ids = lax.broadcasted_iota(jnp.int32, logits.shape, 0)
    hit = ids == routes[0:1]
    for k in range(1, TOP):
        hit = jnp.logical_or(hit, ids == routes[k : k + 1])
    weights = jnp.exp(logits - jnp.max(logits, axis=0, keepdims=True))
    probs = weights / jnp.sum(weights, axis=0, keepdims=True)
    chosen = jnp.sum(jnp.where(hit, probs, 0.0), axis=0, keepdims=True)
    grads = jnp.where(hit, grad_shares, 0.0)
    mean = jnp.sum(probs * grads, axis=0, keepdims=True) / chosen
    grad_probs = jnp.where(hit, (grads - mean) / chosen, 0.0)
    return probs * (grad_probs - jnp.sum(probs * grad_probs, axis=0, keepdims=True))


def branch_back_kernel(
    parts, info, residual, normed, cotangent, routes, router, gain, *rest
):
    sums, rest = rest[:parts], rest[parts:]
    experts = router.shape[0]
    count = len(rest) - 7
    refs = rest[:count]
    grad_residual, grad_branch, grad_heads, grad_gain, grad_router, weight, sem = rest[count:]

    @pl.when(pl.program_id(0) == 0)
    def _():
        copies = weight_copies(info, refs, weight, sem, D // QUARTERS + 128, D // QUARTERS)
        run_all(copies)
        logits = nt(router[...], normed[...])
        if parts == 2:
            back_sum, grad_shares = sums[0][...], sums[1][...]
        else:
            values = [
                (ref[0] if len(ref.shape) == 3 else ref[...]).astype(WIDE) for ref in sums
            ]
            upper = values[0] + values[1] + values[2]
            lower = values[3] + values[4] + values[5]
            last = lower.shape[0] - SHARE_ROWS
            shares = lower[last : last + experts]
            grad_shares = shares[:, :TOK_DEV] + shares[:, TOK_DEV : 2 * TOK_DEV]
            back_sum = jnp.concatenate([upper, lower[:last]], axis=0)
        high, low = split(router_back(logits, routes[...], grad_shares))
        grad_router[...] = nn(high, normed[...]) + nn(low, normed[...])
        grad_normed = tn(high, router[...]) + tn(low, router[...])
        grad_normed += back_sum
        grad_values, gain_grad = norm_back(residual[...], gain[...], grad_normed)
        grad_gain[...] = gain_grad
        total = cotangent[...].astype(WIDE) + grad_values
        grad_residual[...] = total
        grad_branch[...] = total.astype(LOW)
        wait_all(copies)

    at = pl.ds(pl.multiple_of(pl.program_id(0) * STEP, STEP), STEP)
    grad_heads[...] = nt(grad_branch[...], weight[at, :]).astype(LOW)


def branch_back(info, residual, normed, sums, cotangent, routes, router, gain, refs):
    full = (TOK_DEV, D)
    total = router.shape[0]
    return pl.pallas_call(
        functools.partial(branch_back_kernel, len(sums)),
        grid=(D // STEP,),
        out_shape=(
            jax.ShapeDtypeStruct(full, WIDE),
            jax.ShapeDtypeStruct(full, LOW),
            jax.ShapeDtypeStruct(full, LOW),
            jax.ShapeDtypeStruct((1, D), WIDE),
            jax.ShapeDtypeStruct((total, D), WIDE),
        ),
        in_specs=[SMEM]
        + [whole(full)] * 3
        + [whole((TOP, TOK_DEV)), whole((total, D)), whole((1, D))]
        + [whole(part.shape if part.ndim == 2 else (1,) + part.shape[1:]) for part in sums]
        + [ANY] * len(refs),
        out_specs=(
            whole(full),
            whole(full),
            pl.BlockSpec((TOK_DEV, STEP), lambda i: (0, i)),
            whole((1, D)),
            whole((total, D)),
        ),
        scratch_shapes=[pltpu.VMEM((D, D), LOW), pltpu.SemaphoreType.DMA],
        compiler_params=params(),
        cost_estimate=LITTLE,
        name="experts_norm_back",
    )(info, residual, normed, cotangent, routes, router, gain, *sums, *refs)


def join_grads_kernel(info, own_grad, source_grad, arrived, cosine, sine, out):
    half = HEAD_DIM // 2
    first = lax.broadcasted_iota(jnp.int32, (TOK_DEV, HEAD_DIM), 1) < half
    leaves = info[1] == 0

    def total(column):
        columns = slice(column, column + 128)
        extra = source_grad[:, columns] + arrived[:, columns].astype(WIDE)
        return own_grad[:, columns] + jnp.where(leaves, 0.0, extra)

    for g in range(KV_HEADS):
        key = turn_back(total(128 * g), cosine[...], sine[...])
        value = total(KEY_WIDTH + 128 * g)
        out[:, 256 * g : 256 * g + 128] = jnp.where(
            first, key, pltpu.roll(value, half, 1)
        ).astype(LOW)
        out[:, 256 * g + 128 : 256 * g + 256] = jnp.where(
            first, pltpu.roll(key, half, 1), value
        ).astype(LOW)


def join_grads(info, own_grad, source_grad, arrived, cosine, sine):
    vmem = pl.BlockSpec(memory_space=pltpu.VMEM)
    return pl.pallas_call(
        join_grads_kernel,
        out_shape=jax.ShapeDtypeStruct((TOK_DEV, 2 * KEY_WIDTH), LOW),
        in_specs=[SMEM] + [vmem] * 5,
        out_specs=vmem,
        compiler_params=params(),
        cost_estimate=LITTLE,
        name="join_key_value_gradients",
    )(info, own_grad, source_grad, arrived, cosine, sine)


def normed_grad_kernel(info, grad_query, *rest):
    refs, (out, weight, sem) = rest[:-3], rest[-3:]

    @pl.when(pl.program_id(0) == 0)
    def _():
        copies = weight_copies(info, refs, weight, sem, 0, D // QUARTERS)
        run_all(copies)
        wait_all(copies)

    at = pl.ds(pl.multiple_of(pl.program_id(0) * STEP, STEP), STEP)
    out[...] = nt(grad_query[...], weight[at, :])


def normed_grad(info, grad_query, refs):
    return pl.pallas_call(
        normed_grad_kernel,
        grid=(D // STEP,),
        out_shape=jax.ShapeDtypeStruct((TOK_DEV, D), WIDE),
        in_specs=[SMEM, whole((TOK_DEV, D))] + [ANY] * len(refs),
        out_specs=pl.BlockSpec((TOK_DEV, STEP), lambda i: (0, i)),
        scratch_shapes=[pltpu.VMEM((D, D), LOW), pltpu.SemaphoreType.DMA],
        compiler_params=params(),
        cost_estimate=LITTLE,
        name="normed_gradient",
    )(info, grad_query, *refs)


def token_back_kernel(info, query_part, grad_pair, tokens, grad_residual, gain, *rest):
    refs, (out, grad_gain, weight, sem) = rest[:-4], rest[-4:]
    copies = weight_copies(info, refs, weight, sem, D // QUARTERS, 128)
    run_all(copies)
    wait_all(copies)
    grad_normed = query_part[...] + nt(grad_pair[...], weight[...])
    grad_values, gain_grad = norm_back(tokens[...].astype(WIDE), gain[...], grad_normed)
    grad_gain[...] = gain_grad
    out[...] = (grad_residual[...] + grad_values).astype(LOW)


def token_back(info, query_part, grad_pair, tokens, grad_residual, gain, refs):
    full = (TOK_DEV, D)
    vmem = pl.BlockSpec(memory_space=pltpu.VMEM)
    return pl.pallas_call(
        token_back_kernel,
        out_shape=(jax.ShapeDtypeStruct(full, LOW), jax.ShapeDtypeStruct((1, D), WIDE)),
        in_specs=[SMEM] + [vmem] * 5 + [ANY] * len(refs),
        out_specs=(vmem, vmem),
        scratch_shapes=[
            pltpu.VMEM((D, 2 * KEY_WIDTH), LOW),
            pltpu.SemaphoreType.DMA,
        ],
        compiler_params=params(),
        cost_estimate=LITTLE,
        name="token_gradient",
    )(info, query_part, grad_pair, tokens, grad_residual, gain, *refs)


def weight_grads_kernel(parts, info, *rest):
    ins, (keep, send) = rest[:-2], rest[-2:]
    depth = D // 8
    core = info[0] & 1
    chip = pl.program_id(0) ^ (info[0] >> 1)
    for strip_at, grads_at, start, width in parts:
        low = tn(ins[strip_at][...], ins[grads_at][...]).astype(LOW)
        columns = slice(start, start + width)
        for slot in range(QUARTERS):
            for j in range(QUARTERS):

                @pl.when(info[2 + slot] == j)
                def _():
                    piece = low[:, j * width : (j + 1) * width]
                    upper, lower = piece[:depth], piece[depth:]
                    keep[0, slot, :depth, columns] = jnp.where(core == 0, upper, lower)
                    send[0, slot, :depth, columns] = jnp.where(core == 0, lower, upper)

    if keep.shape[2] > depth:
        extra = ins[-1]
        for slot in range(QUARTERS):
            to = info[2 + slot]
            keep[0, slot, depth:] = extra[(chip * 2 + core) * QUARTERS + to]
            send[0, slot, depth:] = extra[(chip * 2 + 1 - core) * QUARTERS + to]


def weight_grads(info, strips, grads, parts, extra=None):
    depth = D // 8
    strip = pl.BlockSpec((TOK_DEV, 2 * depth), lambda i, info: (0, i ^ (info[0] >> 1)))
    more = [] if extra is None else [extra]
    width = sum(part[3] for part in parts)
    shape = (4, QUARTERS, depth + EXTRA * len(more), width)
    out = pl.BlockSpec((1,) + shape[1:], lambda i, info: (i, 0, 0, 0))
    return pl.pallas_call(
        functools.partial(weight_grads_kernel, parts),
        grid_spec=pltpu.PrefetchScalarGridSpec(
            num_scalar_prefetch=1,
            grid=(4,),
            in_specs=[strip] * len(strips)
            + [
                pl.BlockSpec(a.shape, lambda i, info, n=a.ndim: (0,) * n)
                for a in (*grads, *more)
            ],
            out_specs=(out, out),
        ),
        out_shape=(jax.ShapeDtypeStruct(shape, LOW),) * 2,
        compiler_params=params(),
        cost_estimate=LITTLE,
        name="weight_gradients",
    )(info, *strips, *grads, *more)


def last_sums_kernel(part, info, own, *rest):
    arrived, (query_out, key_out, value_out, out_out, extra_out) = rest[:-5], rest[-5:]
    total = own[...].astype(WIDE)
    for ref in arrived[:-1]:
        total += ref[...].astype(WIDE)
    end = jnp.logical_or(info[2] == 0, info[2] == 3)
    total += jnp.where(end, arrived[-1][...].astype(WIDE), 0.0)
    depth = query_out.shape[0]
    quarter = query_out.shape[1]
    query_out[...] = total[:depth, :quarter]
    pair = total[:depth, 2 * quarter :].T
    key_out[...] = pair[:part]
    value_out[...] = pair[part:]
    out_out[...] = total[:depth, quarter : 2 * quarter]
    extra_out[...] = total[depth:]


def last_sums(info, own, arrived, depth, part):
    height, width = own.shape
    quarter = D // QUARTERS
    vmem = pl.BlockSpec(memory_space=pltpu.VMEM)
    return pl.pallas_call(
        functools.partial(last_sums_kernel, part),
        out_shape=(
            jax.ShapeDtypeStruct((depth, quarter), WIDE),
            jax.ShapeDtypeStruct((part, depth), WIDE),
            jax.ShapeDtypeStruct((part, depth), WIDE),
            jax.ShapeDtypeStruct((depth, quarter), WIDE),
            jax.ShapeDtypeStruct((height - depth, width), WIDE),
        ),
        in_specs=[SMEM] + [vmem] * (1 + len(arrived)),
        out_specs=(vmem,) * 5,
        compiler_params=params(),
        cost_estimate=LITTLE,
        name="last_sums",
    )(info, own, *arrived)


def position_of(token_index):
    branch_place = TRUNK + (token_index - TRUNK) % BRANCH
    leaf_place = TRUNK + BRANCH + (token_index - TOK_DEV) % BRANCH
    return jnp.where(
        token_index < TRUNK, token_index, jnp.where(token_index < TOK_DEV, branch_place, leaf_place)
    )


def rotary_tables(positions):
    half_dim = HEAD_DIM // 2
    frequency = ROPE_BASE ** (-jnp.arange(half_dim, dtype=jnp.float32) / half_dim)
    angles = positions.astype(jnp.float32)[:, None] * frequency[None, :]
    cosine, sine = (jnp.cos(angles), jnp.sin(angles))
    return (
        jnp.concatenate([cosine, cosine], axis=1),
        jnp.concatenate([-sine, sine], axis=1),
    )


def after(values, *earlier):
    return lax.optimization_barrier((values, earlier))[0]


def fast_mesh():
    return lax.axis_size("rows") == 8 and lax.axis_size("cols") == 4


SLOT_SHARD = ((0, 2, 1, 3), (1, 3, 0, 2), (2, 0, 1, 3), (3, 1, 2, 0))
UP = [(0, 1), (1, 2), (2, 3)]
DOWN = [(1, 0), (2, 1), (3, 2)]
FAR = [(0, 3), (3, 0)]


def send_near(block):
    return lax.ppermute(block, "cols", DOWN), lax.ppermute(block, "cols", UP)


def send_far(block):
    return lax.ppermute(block, "cols", FAR)


def send_over(block):
    return lax.ppermute(block, "cols", [(0, 2), (1, 3), (2, 0), (3, 1)])


def send_second(block, near):
    place = lax.axis_index("cols")
    above, below = near
    payload = jnp.where(place == 1, above, jnp.where(place == 2, below, block))
    return lax.ppermute(payload, "cols", [(3, 1), (1, 0), (0, 2), (2, 3)])


def slot_list(block, near, second, far):
    place = lax.axis_index("cols")
    above, below = near
    end = (place == 0) | (place == 3)
    return [
        block,
        second,
        jnp.where(place == 0, above, below),
        jnp.where(end, far, above),
    ]


def send_slots(slots):
    place = lax.axis_index("cols")
    _, second, third, fourth = slots
    relay = lax.ppermute(second, "cols", [(1, 3), (0, 1), (2, 0), (3, 2)])
    relayed = relay.astype(WIDE)
    upward_load = (
        jnp.where(place == 0, third, fourth).astype(WIDE) + jnp.where(place == 1, relayed, 0.0)
    ).astype(LOW)
    downward_load = (third.astype(WIDE) + jnp.where(place == 2, relayed, 0.0)).astype(LOW)
    return (
        lax.ppermute(upward_load, "cols", UP),
        lax.ppermute(downward_load, "cols", DOWN),
        send_far(after(fourth, upward_load, downward_load)),
        relay,
    )


def flip(block, bit):
    count = lax.axis_size("rows")
    return lax.ppermute(block, "rows", [(i, i ^ bit) for i in range(count)])


def add_low(one, two):
    return (one.astype(WIDE) + two.astype(WIDE)).astype(LOW)


def chips_second(near_x, near_y, got_x, got_y):
    for_y, for_x = corner_adds(near_x, got_x, near_y, got_y)
    return (near_x, got_x, flip(for_y, 4), near_y, got_y, flip(for_x, 2))


def turn_corner(beside, across):
    half = beside.shape[0] // 2
    return jnp.concatenate([flip(beside[:half], 4), flip(across[half:], 2)], axis=0)


def send_chips(sums):
    return flip(sums[0], 2), flip(sums[1], 4)


def sum_parts(parts):
    wide = [(a[0] if a.ndim == 3 else a).astype(WIDE) for a in parts]
    if len(wide) == 1:
        return wide[0]
    return jnp.concatenate([wide[0] + wide[1] + wide[2], wide[3] + wide[4] + wide[5]], axis=0)


def on_device(
    tokens,
    query_weight,
    key_weight,
    value_weight,
    out_weight,
    router_weight,
    attention_gain,
    experts_gain,
    gate_weight,
    upward_weight,
    down_weight,
    routes,
    leaf_parent,
    cotangent,
):
    row_count = lax.axis_size("rows")
    col_count = lax.axis_size("cols")
    row_place = lax.axis_index("rows")
    col_place = lax.axis_index("cols")
    fast = fast_mesh()
    parity = lax.rem(col_place, 2)
    tree_id = lax.div(row_place * col_count + col_place, 2)
    parent_row = lax.dynamic_slice_in_dim(leaf_parent, tree_id, 1, 0)[0]
    depth, query_part = query_weight.shape
    key_part = key_weight.shape[1]
    router_part = router_weight.shape[1]
    gain_part = attention_gain.shape[0]
    expert_total = router_part * col_count
    local_experts = gate_weight.shape[0]
    capacity = TOK_DEV * TOP // expert_total * 5 // 4

    shards = (
        jnp.asarray(SLOT_SHARD, jnp.int32)[col_place]
        if fast
        else jnp.arange(4, dtype=jnp.int32)
    )
    branch_rows = jnp.where(parity == 0, TRUNK + BRANCH * parent_row, TRUNK)
    info = jnp.concatenate(
        [jnp.stack([row_place, parity]), shards, branch_rows, jnp.zeros((2,), jnp.int32)]
    ).astype(jnp.int32)

    packed = jnp.concatenate([query_weight, key_weight, value_weight, out_weight], axis=1)
    local_index = (1 - parity) * TOK_DEV + jnp.arange(TOK_DEV, dtype=jnp.int32)
    cosine, sine = rotary_tables(position_of(local_index))
    shard_blocks = [
        jnp.concatenate(
            [gate_weight[expert].T, upward_weight[expert].T, down_weight[expert]], axis=0
        )
        for expert in range(local_experts)
    ]
    expert_refs = []
    if fast:
        wide = packed.shape[1]
        gains = jnp.concatenate([attention_gain, experts_gain])[None, :]
        packed = jnp.concatenate(
            [
                packed,
                jnp.pad(router_weight.T, ((0, 0), (0, wide - depth))),
                jnp.pad(gains, ((0, 0), (0, wide - 2 * gain_part))),
                jnp.pad(routes.T.astype(LOW), ((0, 0), (0, wide - TOK_DEV))),
                jnp.zeros((EXTRA - router_part - 1 - TOP, wide), LOW),
            ],
            axis=0,
        )
        packed_near = send_near(packed)
        packed_far = send_far(packed)
        packed_second = send_over(packed)
        first_block = after(shard_blocks[0], *packed_near)
        first_near = send_near(first_block)
        first_far = send_far(first_block)
        own = jnp.stack(slot_list(packed, packed_near, packed_second, packed_far))
        own = after(own, info, cosine, sine)
        beside, across = flip(own, 2), flip(own, 4)
        own_in = flip(own, 1)
        beside, across = after((beside, across), own_in, *first_near)
        corner = [flip(beside[:2], 4), flip(across[2:], 2)]
        pair_in = flip(jnp.concatenate([beside, across], axis=0), 1)
        corner_in = [flip(piece, 1) for piece in corner]
        grad_in = after(cotangent, *corner)
        grad_flips = [flip(grad_in, 2), flip(grad_in, 4)]
        pieces = [own, own_in, beside, across, *corner, pair_in, *corner_in]
        at = depth + router_part + 1
        near_slots = [own, own_in, beside, pair_in, across, pair_in[4:], corner[0], corner_in[0]]
        routes_all = jnp.stack([part[0, at : at + TOP, :TOK_DEV] for part in near_slots])
        routes_all = routes_all.astype(jnp.int32)
        chosen, place_rows = tables(info, routes_all, capacity, local_experts, expert_total)
        query_refs = pair_refs = out_refs = pieces
        extra_rows = extras(info, pieces)
        router_all = extra_rows[:, :router_part, :depth]
        attention_scale = extra_rows[:, router_part, :gain_part]
        experts_scale = extra_rows[:, router_part, gain_part : 2 * gain_part]
    else:
        packed_all = lax.all_gather(lax.all_gather(packed, "cols", axis=0), "rows", axis=0)

        def unpack(start, width):
            part = packed_all[..., start : start + width]
            return jnp.swapaxes(part, 1, 2).reshape(row_count * depth, col_count * width)

        key_at = query_part
        query_refs = [unpack(0, query_part)]
        pair_refs = [
            jnp.concatenate(
                [
                    unpack(key_at, key_part).reshape(D, QUARTERS, -1),
                    unpack(key_at + key_part, key_part).reshape(D, QUARTERS, -1),
                ],
                axis=2,
            ).reshape(D, -1)
        ]
        out_refs = [unpack(key_at + 2 * key_part, query_part)]
        routes_all = lax.all_gather(routes.T, "rows", axis=0)
        chosen, place_rows = tables(info, routes_all, capacity, local_experts, expert_total)
        axes = ("rows", "cols")
        router_all = jnp.swapaxes(lax.all_gather(router_weight, axes, axis=0), 1, 2)
        attention_scale = lax.all_gather(attention_gain, axes, axis=0)
        experts_scale = lax.all_gather(experts_gain, axes, axis=0)

    attention_scale = attention_scale.reshape(1, D).astype(WIDE)
    experts_scale = experts_scale.reshape(1, D).astype(WIDE)
    router_rows = jnp.transpose(
        router_all.reshape(row_count, col_count, router_part, depth), (1, 2, 0, 3)
    ).reshape(expert_total, D)
    router_cols = router_rows.T
    tokens_in = after(tokens, first_far, chosen) if fast else tokens
    normed, own_pair = key_value(info, tokens_in, attention_scale, cosine, sine, pair_refs)
    pairs = [(i + 1, i) for i in range(0, col_count, 2)]
    partner = lax.ppermute(own_pair, "cols", pairs)
    if fast:
        own_grad_in = flip(grad_in, 1)
        normed_in = after(normed, own_grad_in)
    else:
        normed_in = normed
    queries = query(info, normed_in, cosine, sine, query_refs)
    if fast:
        first_second = send_second(after(first_block, partner, queries), first_near)
        expert_refs.append([first_block, first_second, *first_near, first_far])
    if fast:
        grad_flips = after(grad_flips, queries)
        grad_corner = turn_corner(*grad_flips)
    heads = attention(info, queries, own_pair, partner)
    if fast:
        grad_near = [*grad_flips, grad_corner]
        grad_blocks = [cotangent, own_grad_in]
        grad_blocks += [block for one in grad_near for block in (one, flip(one, 1))]
        heads = after(heads, grad_corner, grad_blocks[3], grad_blocks[5])
    else:
        grad_all = lax.all_gather(cotangent, "rows", axis=0)
        grad_blocks = [grad_all[q] for q in range(row_count)]
    residual, normed_two = out_projection(info, heads, tokens, experts_scale, out_refs)

    if fast:
        beside, across = flip(normed_two, 2), flip(normed_two, 4)
        beside_in = flip(normed_two, 1)
        later_block = after(shard_blocks[1], first_second, normed_two)
        expert_refs.append([lax.all_gather(later_block, "cols", axis=0)])
    else:
        rows_all = lax.all_gather(normed_two, "rows", axis=0)
        expert_refs = [[lax.all_gather(block, "cols", axis=0)] for block in shard_blocks]
    grad_rows = pick_rows(chosen, grad_blocks, local_experts)

    def place_block(q, block, picked):
        return dispatch(
            q, info, block, chosen, routes_all, router_cols, local_experts, picked
        )

    if fast:
        half = TOK_DEV // 2
        picked = place_block(0, normed_two, None)
        picked = place_block(1, beside_in, after(picked, *grad_rows))
        beside, across = after((beside, across), picked)
        corner = [flip(beside[:half], 4), flip(across[half:], 2)]
        picked = place_block(2, beside, picked)
        picked = place_block(4, across, picked)
        beside_in = flip(beside, 1)
        across_in = flip(across, 1)
        picked = place_block(3, beside_in, picked)
        picked = place_block(5, across_in, picked)
        corner = jnp.concatenate(after(corner, picked), axis=0)
        corner_in = flip(corner, 1)
        picked = place_block(6, corner, picked)
        picked = place_block(7, corner_in, picked)
    else:
        picked = None
        for q in range(row_count):
            picked = place_block(q, rows_all[q], picked)
    height = row_count * capacity
    token_rows = [a.reshape(height, D) for a in picked[:local_experts]]
    grad_rows = [a.reshape(height, D) for a in grad_rows]
    share_rows = [a.reshape(height, 1) for a in picked[local_experts:]]

    out_rows, back_rows, gate_dots, reduced = ([], [], [], [])
    for e in range(local_experts):
        rows_in = after(token_rows[e], *reduced_in) if e else token_rows[e]
        out_row, back_row, grad_row, acts, dots = expert(
            info, rows_in, grad_rows[e], share_rows[e], expert_refs[e], col_count
        )
        out_rows.append(out_row.reshape(row_count, capacity, D))
        back_rows.append(back_row.reshape(row_count, capacity, D))
        gate_dots.append(dots.reshape(row_count, capacity, 1))
        if fast and e == 1:
            got = flip(combine(info, chosen, back_rows, 1, 2, gate_dots), 1)
            back_keep = combine(info, chosen, back_rows, 0, 2, gate_dots)
            for_x, for_y, near_x, near_y = chip_adds(back_keep, got)
            acts = after(acts, for_x)
            back_flips = send_chips((for_x, for_y))
        slots = expert_grads(acts, token_rows[e], grad_row)
        reduced_in = (slots,)
        if e and fast:
            out_got = flip(combine(info, chosen, out_rows, 1, 2), 1)
            out_keep = combine(info, chosen, out_rows, 0, 2)
            back_flips = after(back_flips, slots, out_keep)
            back_parts = chips_second(near_x, near_y, *back_flips)
        else:
            reduced.append(lax.psum_scatter(slots, "cols", scatter_dimension=0, tiled=False))

    if fast:
        out_first = chip_adds(out_keep, out_got)
        back_parts = after(back_parts, out_first[0])
    else:
        spread_dots = spread(place_rows, gate_dots)
        grad_shares = lax.all_to_all(spread_dots, "rows", split_axis=0, concat_axis=0, tiled=True)

        def summed(rows):
            part = combine(info, chosen, rows, 0, 1)
            return lax.psum_scatter(part, "rows", scatter_dimension=0).astype(WIDE)

        back_parts = (summed(back_rows), grad_shares.reshape(expert_total, TOK_DEV))
        mixture = (summed(out_rows),)

    grad_residual, grad_branch, grad_heads, experts_gain_grad, router_grad = branch_back(
        info,
        residual,
        normed_two,
        back_parts,
        cotangent,
        routes.T,
        router_rows,
        experts_scale,
        out_refs,
    )
    if fast:
        out_flips = send_chips(after(out_first[:2], back_parts[2], back_parts[5]))
        slots = after(slots, reduced[0], back_parts[2])
        reduced.append(lax.psum_scatter(slots, "cols", scatter_dimension=0, tiled=False))
        main_width = 2 * query_part
        router_parts = jnp.transpose(
            router_grad.astype(LOW).reshape(col_count, router_part, row_count, depth),
            (2, 0, 1, 3),
        ).reshape(row_count * col_count, router_part, depth)
        gain_rows = experts_gain_grad.astype(LOW).reshape(row_count * col_count, 1, gain_part)
        extra = jnp.concatenate(
            [
                jnp.pad(router_parts, ((0, 0), (0, 0), (0, main_width - depth))),
                jnp.pad(gain_rows, ((0, 0), (0, 0), (0, main_width - gain_part))),
                jnp.zeros((row_count * col_count, EXTRA - router_part - 1, main_width), LOW),
            ],
            axis=1,
        )
    grad_query, own_grad, source_grad = attention_back(
        info, queries, own_pair, partner, grad_heads, cosine, sine
    )
    arrived = lax.ppermute(source_grad.astype(LOW), "cols", [(j, i) for i, j in pairs])
    if fast:
        parts = ((0, 2, 0, query_part), (1, 3, query_part, query_part))
        grad_branch = after(grad_branch, *out_flips)
        keep, send = weight_grads(
            info, [normed, heads], [grad_query, grad_branch], parts, extra
        )
        flat = (4, col_count * (depth + EXTRA), main_width)
        sent = flip(send, 1)
        main_first = chip_adds(keep.reshape(flat), sent.reshape(flat))
        main_chips = send_chips(main_first[:2])
        query_back = normed_grad(info, after(grad_query, main_first[0]), query_refs)
        main_chips = after(main_chips, query_back)
        main_x, main_y = main_first[2:]
        for_y, for_x = corner_adds(main_x, main_chips[0], main_y, main_chips[1])
        main_parts = (main_x, main_chips[0], flip(for_y, 4), main_y, main_chips[1])
        main_parts += (flip(for_x, 2),)
        arrived = after(arrived, for_y)
    else:
        query_back = normed_grad(info, grad_query, query_refs)
    grad_pair = join_grads(info, own_grad, source_grad, arrived, cosine, sine)
    if fast:
        keep, send = weight_grads(info, [normed], [grad_pair], ((0, 1, 0, 2 * key_part),))
        flat = (4, col_count * depth, 2 * key_part)
        pair_first = chip_adds(keep.reshape(flat), flip(send, 1).reshape(flat))
        pair_chips = send_chips(pair_first[:2])
        grad_pair = after(grad_pair, pair_first[0])
    tokens_grad, attention_gain_grad = token_back(
        info, query_back, grad_pair, tokens, grad_residual, attention_scale, pair_refs
    )

    if fast:
        pair_parts = chips_second(*pair_first[2:], *after(pair_chips, tokens_grad))
        near_x, near_y = out_first[2:]
        mixture = chips_second(near_x, near_y, *after(out_flips, pair_parts[2], pair_parts[5]))
    layer_output = (residual + sum_parts(mixture)).astype(LOW)
    part = down_weight.shape[1]
    expert_sums = [block.astype(WIDE) for block in reduced]
    gate_grad, upward_grad, down_grad = (
        jnp.stack([sums_of[which * part : (which + 1) * part] for sums_of in expert_sums])
        for which in range(3)
    )
    gate_grad, upward_grad = jnp.swapaxes(gate_grad, 1, 2), jnp.swapaxes(upward_grad, 1, 2)
    if fast:
        slots = sum_parts(main_parts).reshape(col_count, depth + EXTRA, main_width)
        pairs_sum = sum_parts(pair_parts).reshape(col_count, depth, 2 * key_part)
        width = query_part + 2 * key_part
        weights_own = jnp.stack([own[i, :depth, :width].astype(WIDE) for i in range(4)])
        gain_sums = jnp.sum(
            weights_own[..., :query_part] * slots[:, :depth, :query_part], axis=(0, 2)
        ) + jnp.sum(weights_own[..., query_part:] * pairs_sum, axis=(0, 2))
        own_gains = lax.dynamic_slice_in_dim(attention_scale[0], row_place * depth, depth, 0)
        gain_sums = (gain_sums / own_gains).reshape(col_count, 1, gain_part)
        gain_sums = jnp.pad(
            jnp.take(gain_sums, shards, axis=0),
            (
                (0, 0),
                (depth + router_part + 1, EXTRA - router_part - 2),
                (0, main_width - gain_part),
            ),
        )
        pairs_sum = jnp.pad(pairs_sum, ((0, 0), (0, EXTRA), (0, 0)))
        slots = jnp.concatenate([slots + gain_sums, pairs_sum], axis=2).astype(LOW)
        slots = after(slots, reduced[1])

        arrived = send_slots(slots)
        earlier = (gate_grad, upward_grad, down_grad, layer_output)
        query_sum, key_sum, value_sum, out_sum, extra_sum = last_sums(
            info, slots[0], after(arrived, *earlier), depth, key_part
        )
        key_sum, value_sum = key_sum.T, value_sum.T
        router_sum = extra_sum[:router_part, :depth].T
        experts_gain_sum = extra_sum[router_part, :gain_part]
        attention_gain_sum = extra_sum[router_part + 1, :gain_part]
    else:
        full_grads = [
            tn(normed, grad_query),
            *jnp.moveaxis(tn(normed, grad_pair).reshape(D, QUARTERS, 2, -1), 2, 0),
            tn(heads, grad_branch),
        ]
        packed_grad = jnp.concatenate(
            [
                grad.astype(LOW).reshape(row_count, depth, col_count, -1)
                for grad in full_grads
            ],
            axis=3,
        )
        row_sums = lax.psum_scatter(packed_grad, "rows", scatter_dimension=0)
        sums = lax.psum_scatter(row_sums, "cols", scatter_dimension=1).astype(WIDE)
        key_at = query_part
        value_at = key_at + key_part
        out_at = value_at + key_part
        query_sum, out_sum = sums[:, :key_at], sums[:, out_at:]
        key_sum, value_sum = sums[:, key_at:value_at], sums[:, value_at:out_at]
        small_grads = jnp.concatenate(
            [
                attention_gain_grad.reshape(-1, gain_part),
                experts_gain_grad.reshape(-1, gain_part),
                jnp.transpose(
                    router_grad.reshape(col_count, router_part, row_count, depth), (2, 0, 3, 1)
                ).reshape(row_count * col_count, depth * router_part),
            ],
            axis=1,
        )
        small_grads = small_grads.reshape(row_count, -1)
        small_grads = lax.all_to_all(small_grads, "rows", split_axis=0, concat_axis=0, tiled=True)
        small_grads = jnp.sum(small_grads, axis=0).reshape(col_count, -1)
        small_grads = lax.all_to_all(small_grads, "cols", split_axis=0, concat_axis=0, tiled=True)
        small_sums = jnp.sum(small_grads, axis=0)
        attention_gain_sum = small_sums[:gain_part]
        experts_gain_sum = small_sums[gain_part : 2 * gain_part]
        router_sum = small_sums[2 * gain_part :].reshape(depth, router_part)

    return (
        layer_output,
        tokens_grad,
        query_sum,
        key_sum,
        value_sum,
        out_sum,
        router_sum,
        attention_gain_sum,
        experts_gain_sum,
        gate_grad,
        upward_grad,
        down_grad,
    )


def solution(mesh):
    in_specs = (
        P(("rows", "cols"), None),
        P("rows", "cols"),
        P("rows", "cols"),
        P("rows", "cols"),
        P("rows", "cols"),
        P("rows", "cols"),
        P(("rows", "cols")),
        P(("rows", "cols")),
        P("rows", None, "cols"),
        P("rows", None, "cols"),
        P("rows", "cols", None),
        P(("rows", "cols"), None),
        P(),
        P(("rows", "cols"), None),
    )
    out_specs = (
        P(("rows", "cols"), None),
        P(("rows", "cols"), None),
        P("rows", "cols"),
        P("rows", "cols"),
        P("rows", "cols"),
        P("rows", "cols"),
        P("rows", "cols"),
        P(("rows", "cols")),
        P(("rows", "cols")),
        P("rows", None, "cols"),
        P("rows", None, "cols"),
        P("rows", "cols", None),
    )
    return jax.shard_map(
        on_device, mesh=mesh, in_specs=in_specs, out_specs=out_specs, check_vma=False
    )
```

```python
import functools

import jax
import jax.numpy as jnp
from jax import lax
from jax.experimental import pallas as pl
from jax.experimental.pallas import tpu as pltpu
from jax.sharding import PartitionSpec as P

D = 1536
HEADS = 12
KV_HEADS = 2
HEAD_DIM = 128
TOP = 4
TOK_DEV = 512
BRANCHES = 4
LEAVES = 8
TRUNK = 256
BRANCH = 64

EPSILON = 1e-06
ROPE_BASE = 10000.0
MASKED = -1e30
LOW = jnp.bfloat16
WIDE = jnp.float32
KEY_WIDTH = KV_HEADS * HEAD_DIM
GROUP = HEADS // KV_HEADS
QUARTERS = 4
VMEM_LIMIT = 56 * 1024 * 1024

ANY = pl.BlockSpec(memory_space=pl.ANY)
SMEM = pl.BlockSpec(memory_space=pltpu.SMEM)


def nn(one, two):
    return lax.dot_general(one, two, (((1,), (0,)), ((), ())), preferred_element_type=WIDE)


def nt(one, two):
    return lax.dot_general(one, two, (((1,), (1,)), ((), ())), preferred_element_type=WIDE)


def tn(one, two):
    return lax.dot_general(one, two, (((0,), (0,)), ((), ())), preferred_element_type=WIDE)


def whole(shape):
    return pl.BlockSpec(shape, lambda *_: (0,) * len(shape))


LITTLE = pl.CostEstimate(flops=1, bytes_accessed=1, transcendentals=0)


def params():
    return pltpu.CompilerParams(vmem_limit_bytes=VMEM_LIMIT)


def turn(values, cosine, sine):
    return values * cosine + pltpu.roll(values, HEAD_DIM // 2, 1) * sine


def turn_back(values, cosine, sine):
    return values * cosine - pltpu.roll(values, HEAD_DIM // 2, 1) * sine


SLOTS = range(4)
PIECES = (
    tuple((0, slot) for slot in SLOTS),
    tuple((1, slot) for slot in SLOTS),
    tuple((2, slot) for slot in SLOTS),
    tuple((4, slot) for slot in SLOTS),
    ((6, 0), (6, 1)),
    ((6, 2), (6, 3)),
    tuple((flip_bits, slot) for flip_bits in (3, 5) for slot in SLOTS),
    ((7, 0), (7, 1)),
    ((7, 2), (7, 3)),
)
EXTRA = 16


STEP = 768


def weight_copies(info, refs, target, sem, start, width):
    if len(refs) == 1:
        return [pltpu.make_async_copy(refs[0], target, sem)]
    depth = refs[0].shape[1] - EXTRA
    copies = []
    for ref, parts in zip(refs, PIECES):
        for at, (flip_bits, slot) in enumerate(parts):
            row = pl.multiple_of((info[0] ^ flip_bits) * depth, depth)
            col = pl.multiple_of(info[2 + slot] * width, 128)
            copies.append(
                pltpu.make_async_copy(
                    ref.at[at, pl.ds(0, depth), pl.ds(start, width)],
                    target.at[pl.ds(row, depth), pl.ds(col, width)],
                    sem,
                )
            )
    return copies


def extras_kernel(info, *rest):
    refs, (out, sem) = rest[:-2], rest[-2:]
    depth = refs[0].shape[1] - EXTRA
    copies = []
    for ref, parts in zip(refs, PIECES):
        for at, (flip_bits, slot) in enumerate(parts):
            to = (info[0] ^ flip_bits) * QUARTERS + info[2 + slot]
            copies.append(pltpu.make_async_copy(ref.at[at, pl.ds(depth, EXTRA)], out.at[to], sem))
    run_all(copies)
    wait_all(copies)


def extras(info, refs):
    return pl.pallas_call(
        extras_kernel,
        out_shape=jax.ShapeDtypeStruct((8 * QUARTERS, EXTRA, refs[0].shape[2]), LOW),
        in_specs=[SMEM] + [ANY] * len(refs),
        out_specs=pl.BlockSpec(memory_space=pltpu.VMEM),
        scratch_shapes=[pltpu.SemaphoreType.DMA],
        compiler_params=params(),
        cost_estimate=LITTLE,
        name="extra_rows",
    )(info, *refs)


def run_all(copies):
    for copy in copies:
        copy.start()


def wait_all(copies):
    for copy in copies:
        copy.wait()


def key_value_kernel(info, tokens, gain, cosine, sine, *rest):
    count = len(rest) - 4
    refs, (normed, out, weight, sem) = rest[:count], rest[count:]
    copies = weight_copies(info, refs, weight, sem, D // QUARTERS, 128)
    run_all(copies)
    values = tokens[...].astype(WIDE)
    factor = lax.rsqrt(jnp.mean(values * values, axis=-1, keepdims=True) + EPSILON)
    low = (values * factor * gain[...]).astype(LOW)
    normed[...] = low
    wait_all(copies)
    both = nn(low, weight[...])
    half = HEAD_DIM // 2
    first = lax.broadcasted_iota(jnp.int32, (TOK_DEV, HEAD_DIM), 1) < half
    for g in range(KV_HEADS):
        one = both[:, 256 * g : 256 * g + 128]
        two = both[:, 256 * g + 128 : 256 * g + 256]
        key = jnp.where(first, one, pltpu.roll(two, half, 1))
        value = jnp.where(first, pltpu.roll(one, half, 1), two)
        out[:, 128 * g : 128 * g + 128] = turn(key, cosine[...], sine[...]).astype(LOW)
        out[:, KEY_WIDTH + 128 * g : KEY_WIDTH + 128 * g + 128] = value.astype(LOW)


def key_value(info, tokens, gain, cosine, sine, refs):
    return pl.pallas_call(
        key_value_kernel,
        out_shape=(
            jax.ShapeDtypeStruct((TOK_DEV, D), LOW),
            jax.ShapeDtypeStruct((TOK_DEV, 2 * KEY_WIDTH), LOW),
        ),
        in_specs=[SMEM] + [pl.BlockSpec(memory_space=pltpu.VMEM)] * 4 + [ANY] * len(refs),
        out_specs=(pl.BlockSpec(memory_space=pltpu.VMEM),) * 2,
        scratch_shapes=[pltpu.VMEM((D, 2 * KEY_WIDTH), LOW), pltpu.SemaphoreType.DMA],
        compiler_params=params(),
        cost_estimate=LITTLE,
        name="norm_key_value",
    )(info, tokens, gain, cosine, sine, *refs)


def query_kernel(info, normed, cosine, sine, *rest):
    count = len(rest) - 3
    refs, (out, weight, sem) = rest[:count], rest[count:]

    @pl.when(pl.program_id(0) == 0)
    def _():
        copies = weight_copies(info, refs, weight, sem, 0, D // QUARTERS)
        run_all(copies)
        wait_all(copies)

    at = pl.multiple_of(pl.program_id(0) * STEP, STEP)
    lin = nn(normed[...], weight[:, pl.ds(at, STEP)])
    for h in range(STEP // HEAD_DIM):
        out[:, 128 * h : 128 * h + 128] = turn(
            lin[:, 128 * h : 128 * h + 128], cosine[...], sine[...]
        ).astype(LOW)


def query(info, normed, cosine, sine, refs):
    return pl.pallas_call(
        query_kernel,
        grid=(D // STEP,),
        out_shape=jax.ShapeDtypeStruct((TOK_DEV, D), LOW),
        in_specs=[SMEM, whole((TOK_DEV, D)), whole((TOK_DEV, 128)), whole((TOK_DEV, 128))]
        + [ANY] * len(refs),
        out_specs=pl.BlockSpec((TOK_DEV, STEP), lambda i: (0, i)),
        scratch_shapes=[pltpu.VMEM((D, D), LOW), pltpu.SemaphoreType.DMA],
        compiler_params=params(),
        cost_estimate=LITTLE,
        name="query_projection",
    )(info, normed, cosine, sine, *refs)


KEYS = TRUNK + 2 * BRANCH
CHUNKS = TOK_DEV // BRANCH


def chunk_keys(info, source, own, column, chunk):
    at = pl.multiple_of(info[6 + chunk], BRANCH)
    rows = pl.multiple_of(chunk * BRANCH, BRANCH)
    columns = slice(column, column + HEAD_DIM)
    return jnp.concatenate(
        [
            source[0:TRUNK, columns],
            source[pl.ds(at, BRANCH), columns],
            own[pl.ds(rows, BRANCH), columns],
        ],
        axis=0,
    )


def chunk_allowed(info, chunk, query_axis, shape):
    query_row = lax.broadcasted_iota(jnp.int32, shape, query_axis) & (BRANCH - 1)
    key = lax.broadcasted_iota(jnp.int32, shape, 1 - query_axis)
    leaves = info[1] == 0
    trunk = jnp.logical_and(jnp.logical_not(leaves), chunk < TRUNK // BRANCH)
    limit = jnp.where(trunk, chunk * BRANCH + query_row, TRUNK - 1)
    branch_limit = jnp.where(leaves, TRUNK + BRANCH - 1, 0)
    own_limit = jnp.where(trunk, 0, query_row + TRUNK + BRANCH)
    top = jnp.where(key < TRUNK, limit, jnp.where(key < TRUNK + BRANCH, branch_limit, own_limit))
    return key <= top


def group_rows(ref, g):
    first = g * GROUP
    return jnp.concatenate(
        [ref[:, 128 * h : 128 * h + 128] for h in range(first, first + GROUP)], axis=0
    )


def keep_source(info, partner, own, source):
    @pl.when(pl.program_id(0) == 0)
    def _():
        @pl.when(info[1] == 0)
        def _():
            source[...] = partner[...]

        @pl.when(info[1] != 0)
        def _():
            source[...] = own[...]


def attention_kernel(info, queries, own, partner, out, source):
    keep_source(info, partner, own, source)
    chunk = pl.program_id(0)
    rows = GROUP * BRANCH
    allowed = chunk_allowed(info, chunk, 0, (rows, KEYS))
    for g in range(KV_HEADS):
        keys = chunk_keys(info, source, own, 128 * g, chunk)
        values = chunk_keys(info, source, own, KEY_WIDTH + 128 * g, chunk)
        scores = nt(group_rows(queries, g), keys) * HEAD_DIM**-0.5
        scores = jnp.where(allowed, scores, MASKED)
        weights = jnp.exp(scores - jnp.max(scores, axis=1, keepdims=True))
        total = jnp.sum(weights, axis=1, keepdims=True)
        mixed = nn((weights * (1.0 / total)).astype(LOW), values).astype(LOW)
        for h in range(GROUP):
            at = (g * GROUP + h) * 128
            out[:, at : at + 128] = mixed[h * BRANCH : (h + 1) * BRANCH]


def attention(info, queries, own, partner):
    return pl.pallas_call(
        attention_kernel,
        grid=(CHUNKS,),
        out_shape=jax.ShapeDtypeStruct((TOK_DEV, D), LOW),
        in_specs=[
            SMEM,
            pl.BlockSpec((BRANCH, D), lambda i: (i, 0)),
            whole((TOK_DEV, 2 * KEY_WIDTH)),
            whole((TOK_DEV, 2 * KEY_WIDTH)),
        ],
        out_specs=pl.BlockSpec((BRANCH, D), lambda i: (i, 0)),
        scratch_shapes=[pltpu.VMEM((TOK_DEV, 2 * KEY_WIDTH), LOW)],
        compiler_params=params(),
        cost_estimate=LITTLE,
        name="tree_attention",
    )(info, queries, own, partner)


def attention_back_kernel(
    info, queries, own, partner, grads, cosine, sine, grad_query, own_grad, source_grad, source
):
    keep_source(info, partner, own, source)
    chunk = pl.program_id(0)

    @pl.when(chunk == 0)
    def _():
        source_grad[...] = jnp.zeros_like(source_grad)

    rows = GROUP * BRANCH
    scale = HEAD_DIM**-0.5
    allowed = chunk_allowed(info, chunk, 1, (KEYS, rows))
    at = pl.multiple_of(info[6 + chunk], BRANCH)
    for g in range(KV_HEADS):
        keys = chunk_keys(info, source, own, 128 * g, chunk)
        values = chunk_keys(info, source, own, KEY_WIDTH + 128 * g, chunk)
        query_rows = group_rows(queries, g)
        grad_rows = group_rows(grads, g)
        scores = jnp.where(allowed, nt(keys, query_rows) * scale, MASKED)
        weights = jnp.exp(scores - jnp.max(scores, axis=0, keepdims=True))
        probs = weights * (1.0 / jnp.sum(weights, axis=0, keepdims=True))
        grad_probs = nt(values, grad_rows)
        mean = jnp.sum(probs * grad_probs, axis=0, keepdims=True)
        grad_scores = (probs * (grad_probs - mean)).astype(LOW)
        grad_values = nn(probs.astype(LOW), grad_rows)
        grad_keys = nn(grad_scores, query_rows) * scale
        grad_queries = tn(grad_scores, keys) * scale
        for h in range(GROUP):
            to = (g * GROUP + h) * 128
            grad_query[:, to : to + 128] = turn_back(
                grad_queries[h * BRANCH : (h + 1) * BRANCH], cosine[...], sine[...]
            ).astype(LOW)
        for column, grad in ((128 * g, grad_keys), (KEY_WIDTH + 128 * g, grad_values)):
            columns = slice(column, column + 128)
            source_grad[0:TRUNK, columns] += grad[0:TRUNK]
            source_grad[pl.ds(at, BRANCH), columns] += grad[TRUNK : TRUNK + BRANCH]
            own_grad[:, columns] = grad[TRUNK + BRANCH :]


def attention_back(info, queries, own, partner, grads, cosine, sine):
    chunked = pl.BlockSpec((BRANCH, D), lambda i: (i, 0))
    pair = (TOK_DEV, 2 * KEY_WIDTH)
    return pl.pallas_call(
        attention_back_kernel,
        grid=(CHUNKS,),
        out_shape=(
            jax.ShapeDtypeStruct((TOK_DEV, D), LOW),
            jax.ShapeDtypeStruct(pair, WIDE),
            jax.ShapeDtypeStruct(pair, WIDE),
        ),
        in_specs=[
            SMEM,
            chunked,
            whole(pair),
            whole(pair),
            chunked,
            pl.BlockSpec((BRANCH, 128), lambda i: (i, 0)),
            pl.BlockSpec((BRANCH, 128), lambda i: (i, 0)),
        ],
        out_specs=(
            chunked,
            pl.BlockSpec((BRANCH, 2 * KEY_WIDTH), lambda i: (i, 0)),
            whole(pair),
        ),
        scratch_shapes=[pltpu.VMEM(pair, LOW)],
        compiler_params=params(),
        cost_estimate=LITTLE,
        name="tree_attention_back",
    )(info, queries, own, partner, grads, cosine, sine)


def out_kernel(info, heads, tokens, gain, *rest):
    count = len(rest) - 4
    refs, (residual, normed, weight, sem) = rest[:count], rest[count:]

    @pl.when(pl.program_id(0) == 0)
    def _():
        copies = weight_copies(info, refs, weight, sem, D // QUARTERS + 128, D // QUARTERS)
        run_all(copies)
        wait_all(copies)

    at = pl.ds(pl.multiple_of(pl.program_id(0) * STEP, STEP), STEP)
    residual[:, at] = tokens[:, at].astype(WIDE) + nn(heads[...], weight[:, at])

    @pl.when(pl.program_id(0) == pl.num_programs(0) - 1)
    def _():
        values = residual[...]
        factor = lax.rsqrt(jnp.mean(values * values, axis=-1, keepdims=True) + EPSILON)
        normed[...] = (values * factor * gain[...]).astype(LOW)


def out_projection(info, heads, tokens, gain, refs):
    full = (TOK_DEV, D)
    return pl.pallas_call(
        out_kernel,
        grid=(D // STEP,),
        out_shape=(jax.ShapeDtypeStruct(full, WIDE), jax.ShapeDtypeStruct(full, LOW)),
        in_specs=[SMEM, whole(full), whole(full), whole((1, D))] + [ANY] * len(refs),
        out_specs=(whole(full), whole(full)),
        scratch_shapes=[pltpu.VMEM((D, D), LOW), pltpu.SemaphoreType.DMA],
        compiler_params=params(),
        cost_estimate=LITTLE,
        name="out_projection",
    )(info, heads, tokens, gain, *refs)


def hits_of(routes, ids):
    hit = ids == routes[0, 0:1]
    for k in range(1, TOP):
        hit = jnp.logical_or(hit, ids == routes[0, k : k + 1])
    return hit


def tables_kernel(capacity, local, total, info, routes, chosen_out, place_out, earlier):
    @pl.when(pl.program_id(0) == 0)
    def _():
        one = lax.broadcasted_iota(jnp.int32, (TOK_DEV, TOK_DEV), 0)
        two = lax.broadcasted_iota(jnp.int32, (TOK_DEV, TOK_DEV), 1)
        earlier[...] = jnp.where(one < two, 1.0, 0.0).astype(LOW)

    ids = lax.broadcasted_iota(jnp.int32, (total, TOK_DEV), 0)
    hit = hits_of(routes, ids)
    rank = nn(jnp.where(hit, 1.0, 0.0).astype(LOW), earlier[...])
    place = jnp.where(hit, rank, -1.0)
    spots = lax.broadcasted_iota(jnp.int32, (capacity, TOK_DEV), 0).astype(WIDE)
    place_out[0] = jnp.full(place_out.shape[1:], -1.0, WIDE)
    for e in range(local):
        mine = ids == info[0] * local + e
        place_row = jnp.sum(jnp.where(mine, place, 0.0), axis=0, keepdims=True)
        place_out[0, e : e + 1] = place_row
        chosen_out[0, e * capacity : (e + 1) * capacity] = jnp.where(
            spots == place_row, 1.0, 0.0
        ).astype(LOW)


def tables(info, routes, capacity, local, total):
    count = routes.shape[0]
    return pl.pallas_call(
        functools.partial(tables_kernel, capacity, local, total),
        grid=(count,),
        in_specs=[SMEM, pl.BlockSpec((1, TOP, TOK_DEV), lambda i: (i, 0, 0))],
        out_specs=[
            pl.BlockSpec((1, local * capacity, TOK_DEV), lambda i: (i, 0, 0)),
            pl.BlockSpec((1, 8, TOK_DEV), lambda i: (i, 0, 0)),
        ],
        scratch_shapes=[pltpu.VMEM((TOK_DEV, TOK_DEV), LOW)],
        out_shape=[
            jax.ShapeDtypeStruct((count, local * capacity, TOK_DEV), LOW),
            jax.ShapeDtypeStruct((count, 8, TOK_DEV), WIDE),
        ],
        compiler_params=params(),
        cost_estimate=LITTLE,
        name="route_tables",
    )(info, routes)


def pick_kernel(local, count, chosen, *rest):
    blocks, outs = rest[:count], rest[count : count + local]
    picks, block_in, out_block, sem_in, sem_out = rest[count + local :]
    capacity = outs[0].shape[1]
    copies = [
        (
            pltpu.make_async_copy(chosen.at[q], picks.at[q], sem_in.at[q, 0]),
            pltpu.make_async_copy(blocks[q], block_in.at[q], sem_in.at[q, 1]),
        )
        for q in range(count)
    ]
    for pair in copies:
        run_all(pair)
    sent = []
    for q in range(count):
        wait_all(copies[q])
        out_block[q] = nn(picks[q], block_in[q]).astype(LOW)
        for e in range(local):
            copy = pltpu.make_async_copy(
                out_block.at[q, pl.ds(e * capacity, capacity)], outs[e].at[q], sem_out.at[q, e]
            )
            copy.start()
            sent.append(copy)
    wait_all(sent)


def pick_rows(chosen, blocks, local):
    count, height, _ = chosen.shape
    return pl.pallas_call(
        functools.partial(pick_kernel, local, count),
        in_specs=[ANY] * (1 + count),
        out_specs=[ANY] * local,
        out_shape=[jax.ShapeDtypeStruct((count, height // local, D), LOW)] * local,
        scratch_shapes=[
            pltpu.VMEM((count, height, TOK_DEV), LOW),
            pltpu.VMEM((count, TOK_DEV, D), LOW),
            pltpu.VMEM((count, height, D), LOW),
            pltpu.SemaphoreType.DMA((count, 2)),
            pltpu.SemaphoreType.DMA((count, local)),
        ],
        compiler_params=params(),
        cost_estimate=LITTLE,
        name="pick_rows",
    )(chosen, *blocks)


def dispatch_kernel(local, info, rows, chosen, routes, router, *rest):
    outs, logits = rest[2 * local : 4 * local], rest[-1]
    total = router.shape[1]
    step = pl.program_id(0)
    block = rows[...]
    rows_of = nn(chosen[0], block).astype(LOW)
    capacity = outs[0].shape[1]
    for e in range(local):
        outs[e][0] = rows_of[e * capacity : (e + 1) * capacity]
    part = nn(block, router[...])

    @pl.when(step == 0)
    def _():
        logits[...] = part

    @pl.when(step > 0)
    def _():
        logits[...] += part

    @pl.when(step == pl.num_programs(0) - 1)
    def _():
        values = logits[...].T
        ids = lax.broadcasted_iota(jnp.int32, (total, TOK_DEV), 0)
        weights = jnp.exp(values - jnp.max(values, axis=0, keepdims=True))
        hit = hits_of(routes, ids)
        share = weights / jnp.sum(jnp.where(hit, weights, 0.0), axis=0, keepdims=True)
        for e in range(local):
            mine = ids == info[0] * local + e
            share_row = jnp.sum(jnp.where(mine, share, 0.0), axis=0, keepdims=True)
            picked = chosen[0, e * capacity : (e + 1) * capacity].astype(WIDE)
            outs[local + e][0] = jnp.sum(picked * share_row, axis=1, keepdims=True)


def dispatch(at, info, rows, chosen, routes, router, local, earlier):
    count, height, _ = chosen.shape
    capacity = height // local
    total = router.shape[1]
    wide = D
    out_shape = [jax.ShapeDtypeStruct((count, capacity, D), LOW)] * local + [
        jax.ShapeDtypeStruct((count, capacity, 1), WIDE)
    ] * local
    if earlier is None:
        earlier = [jnp.zeros((8, 128), shape.dtype) for shape in out_shape]
        aliases = {}
    else:
        aliases = {5 + i: i for i in range(len(out_shape))}
    return pl.pallas_call(
        functools.partial(dispatch_kernel, local),
        grid=(D // wide,),
        in_specs=[
            SMEM,
            pl.BlockSpec((TOK_DEV, wide), lambda i: (0, i)),
            pl.BlockSpec((1, height, TOK_DEV), lambda i: (at, 0, 0)),
            pl.BlockSpec((1, TOP, TOK_DEV), lambda i: (at, 0, 0)),
            pl.BlockSpec((wide, total), lambda i: (i, 0)),
        ]
        + [ANY] * len(out_shape),
        out_specs=[pl.BlockSpec((1, capacity, wide), lambda i: (at, 0, i))] * local
        + [pl.BlockSpec((1, capacity, 1), lambda i: (at, 0, 0))] * local,
        scratch_shapes=[pltpu.VMEM((TOK_DEV, total), WIDE)],
        out_shape=out_shape,
        input_output_aliases=aliases,
        compiler_params=params(),
        cost_estimate=LITTLE,
        name="dispatch",
    )(info, rows, chosen, routes, router, *earlier)


def spread_kernel(local, place, *rest):
    dots, out = rest[:local], rest[local]
    spots = lax.broadcasted_iota(jnp.int32, (dots[0].shape[1], TOK_DEV), 0).astype(WIDE)
    for e in range(local):
        chosen = spots == place[0, e : e + 1]
        out[0, e : e + 1] = jnp.sum(jnp.where(chosen, dots[e][0], 0.0), axis=0, keepdims=True)


def spread(place, dots):
    count, capacity, _ = dots[0].shape
    local = len(dots)
    return pl.pallas_call(
        functools.partial(spread_kernel, local),
        grid=(count,),
        out_shape=jax.ShapeDtypeStruct((count, local, TOK_DEV), WIDE),
        in_specs=[pl.BlockSpec((1, 8, TOK_DEV), lambda i: (i, 0, 0))]
        + [pl.BlockSpec((1, capacity, 1), lambda i: (i, 0, 0))] * local,
        out_specs=pl.BlockSpec((1, local, TOK_DEV), lambda i: (i, 0, 0)),
        compiler_params=params(),
        cost_estimate=LITTLE,
        name="spread",
    )(place, *dots)


def expert_kernel(slots, info, rows, grads, shares, *rest):
    refs, (out_rows, back_rows, grad_rows, acts, dots, weight, sem) = rest[:-7], rest[-7:]
    part = weight.shape[1] // slots

    @pl.when(pl.program_id(0) == 0)
    def _():
        def copies(ref, slot):
            return [
                pltpu.make_async_copy(
                    ref.at[pl.ds(which * part, part)],
                    weight.at[which, pl.ds(pl.multiple_of(slot * part, part), part)],
                    sem,
                )
                for which in range(3)
            ]

        if len(refs) == 1:
            for slot in range(slots):
                run_all(copies(refs[0].at[slot], slot))
            for slot in range(slots):
                wait_all(copies(refs[0].at[slot], slot))
        else:
            block, second, above, below, far = refs
            low_end = info[2] == 0
            end = jnp.logical_or(low_end, info[2] == 3)
            run_all(copies(block, info[2]))
            run_all(copies(second, info[3]))

            @pl.when(low_end)
            def _():
                run_all(copies(above, info[4]))

            @pl.when(jnp.logical_not(low_end))
            def _():
                run_all(copies(below, info[4]))

            @pl.when(end)
            def _():
                run_all(copies(far, info[5]))

            @pl.when(jnp.logical_not(end))
            def _():
                run_all(copies(above, info[5]))

            for slot in range(slots):
                wait_all(copies(block, slot))

    row_block = rows[...]
    share = shares[...]
    grad_float = grads[...].astype(WIDE)
    grad_low = (share * grad_float).astype(LOW)
    grad_rows[...] = grad_low
    gate_act = nt(row_block, weight[0])
    upward = nt(row_block, weight[1])
    sigmoid = 1.0 / (1.0 + jnp.exp(-gate_act))
    silu = gate_act * sigmoid
    hidden = (silu * upward).astype(LOW)
    expert_out = nn(hidden, weight[2]).astype(LOW).astype(WIDE)
    out_rows[...] = (share * expert_out).astype(LOW)
    dots[...] = jnp.sum(grad_float * expert_out, axis=1, keepdims=True)
    grad_hidden = nt(grad_low, weight[2])
    grad_gate = (grad_hidden * upward * sigmoid * (1.0 + gate_act * (1.0 - sigmoid))).astype(LOW)
    grad_up = (grad_hidden * silu).astype(LOW)
    back_rows[...] = (nn(grad_gate, weight[0]) + nn(grad_up, weight[1])).astype(LOW)
    for which, act in enumerate((grad_gate, grad_up, hidden)):
        turned = act.T
        for slot in range(slots):
            acts[slot, which * part : (which + 1) * part] = turned[
                slot * part : (slot + 1) * part
            ]


EXPERT_ROWS = 256


def expert(info, rows, grads, shares, refs, slots):
    height = rows.shape[0]
    part = refs[0].shape[-2] // 3
    wide_block = pl.BlockSpec((EXPERT_ROWS, D), lambda i: (i, 0))
    thin_block = pl.BlockSpec((EXPERT_ROWS, 1), lambda i: (i, 0))
    return pl.pallas_call(
        functools.partial(expert_kernel, slots),
        grid=(height // EXPERT_ROWS,),
        out_shape=[jax.ShapeDtypeStruct((height, D), LOW)] * 3
        + [
            jax.ShapeDtypeStruct((slots, 3 * part, height), LOW),
            jax.ShapeDtypeStruct((height, 1), WIDE),
        ],
        in_specs=[SMEM, wide_block, wide_block, thin_block] + [ANY] * len(refs),
        out_specs=[wide_block] * 3
        + [pl.BlockSpec((slots, 3 * part, EXPERT_ROWS), lambda i: (0, 0, i)), thin_block],
        scratch_shapes=[pltpu.VMEM((3, slots * part, D), LOW), pltpu.SemaphoreType.DMA],
        compiler_params=params(),
        cost_estimate=LITTLE,
        name="expert",
    )(info, rows, grads, shares, *refs)


def expert_grads_kernel(acts, rows, grads, out):
    slots, height, _ = acts.shape
    part = height // 3
    for slot in range(slots):
        out[slot, : 2 * part] = nn(acts[slot, : 2 * part], rows[...]).astype(LOW)
        out[slot, 2 * part :] = nn(acts[slot, 2 * part :], grads[...]).astype(LOW)


def expert_grads(acts, rows, grads):
    slots, part, height = acts.shape
    strip = pl.BlockSpec((height, 256), lambda i: (0, i))
    return pl.pallas_call(
        expert_grads_kernel,
        grid=(D // 256,),
        out_shape=jax.ShapeDtypeStruct((slots, part, D), LOW),
        in_specs=[whole(acts.shape), strip, strip],
        out_specs=pl.BlockSpec((slots, part, 256), lambda i: (0, 0, i)),
        compiler_params=params(),
        cost_estimate=LITTLE,
        name="expert_gradients",
    )(acts, rows, grads)


SHARE_ROWS = 32


def combine_kernel(local, first, step, info, chosen, *rest):
    rows, dots, out = rest[:local], rest[local:-6], rest[-6]
    picks, rows_in, out_block, sem_in, sem_out = rest[-5:]
    number = out.shape[0]
    capacity = rows[0].shape[1]
    copies = []
    for n in range(number):
        q = first + step * n
        copies.append(
            [pltpu.make_async_copy(chosen.at[q], picks.at[n], sem_in.at[n, local])]
            + [
                pltpu.make_async_copy(
                    rows[e].at[q],
                    rows_in.at[n, pl.ds(e * capacity, capacity)],
                    sem_in.at[n, e],
                )
                for e in range(local)
            ]
        )
    for group in copies:
        run_all(group)
    sent = []
    for n in range(number):
        wait_all(copies[n])
        out_block[n, :TOK_DEV] = tn(picks[n], rows_in[n]).astype(LOW)
        if dots:
            row = lax.broadcasted_iota(jnp.int32, (SHARE_ROWS, D), 0)
            values = jnp.zeros((SHARE_ROWS, D), WIDE)
            for e in range(local):
                picked = picks[n, e * capacity : (e + 1) * capacity].astype(WIDE)
                share = picked * dots[e][first + step * n]
                high, low = split(jnp.sum(share, axis=0, keepdims=True))
                pieces = [high.astype(WIDE), low.astype(WIDE)]
                pieces.append(jnp.zeros((1, D - 2 * TOK_DEV), WIDE))
                line = jnp.concatenate(pieces, axis=1)
                values = jnp.where(row == info[0] * local + e, line, values)
            out_block[n, TOK_DEV:] = values.astype(LOW)
        copy = pltpu.make_async_copy(out_block.at[n], out.at[n], sem_out.at[n])
        copy.start()
        sent.append(copy)
    wait_all(sent)


def combine(info, chosen, rows, first, step, dots=()):
    count, capacity, _ = rows[0].shape
    local = len(rows)
    number = (count - first + step - 1) // step
    height = TOK_DEV + (SHARE_ROWS if dots else 0)
    return pl.pallas_call(
        functools.partial(combine_kernel, local, first, step),
        out_shape=jax.ShapeDtypeStruct((number, height, D), LOW),
        in_specs=[SMEM, ANY]
        + [ANY] * local
        + [pl.BlockSpec(memory_space=pltpu.VMEM)] * len(dots),
        out_specs=ANY,
        scratch_shapes=[
            pltpu.VMEM((number, local * capacity, TOK_DEV), LOW),
            pltpu.VMEM((number, local * capacity, D), LOW),
            pltpu.VMEM((number, height, D), LOW),
            pltpu.SemaphoreType.DMA((number, local + 1)),
            pltpu.SemaphoreType.DMA((number,)),
        ],
        compiler_params=params(),
        cost_estimate=LITTLE,
        name="combine",
    )(info, chosen, *rows, *dots)


def chip_adds_kernel(keep, got, send_x, send_y, near_x, near_y, one, two, sem_in, sem_out):
    half = send_x.shape[1]
    copies = [
        (
            pltpu.make_async_copy(keep.at[i], one.at[i], sem_in.at[i, 0]),
            pltpu.make_async_copy(got.at[i], two.at[i], sem_in.at[i, 1]),
        )
        for i in range(4)
    ]
    for pair in copies:
        run_all(pair)
    sent = []
    for i in range(4):
        wait_all(copies[i])
        one[i] = (one[i].astype(WIDE) + two[i].astype(WIDE)).astype(LOW)
        upper = (near_x, send_x)[i % 2].at[i // 2]
        lower = (near_y, send_y)[i // 2].at[i % 2]
        for part, to in enumerate((upper, lower)):
            copy = pltpu.make_async_copy(
                one.at[i, pl.ds(part * half, half)], to, sem_out.at[i, part]
            )
            copy.start()
            sent.append(copy)
    wait_all(sent)


def chip_adds(keep, got):
    _, height, width = keep.shape
    shape = jax.ShapeDtypeStruct((2, height // 2, width), LOW)
    return pl.pallas_call(
        chip_adds_kernel,
        out_shape=(shape,) * 4,
        in_specs=[ANY, ANY],
        out_specs=(ANY,) * 4,
        scratch_shapes=[
            pltpu.VMEM(keep.shape, LOW),
            pltpu.VMEM(keep.shape, LOW),
            pltpu.SemaphoreType.DMA((4, 2)),
            pltpu.SemaphoreType.DMA((4, 2)),
        ],
        compiler_params=params(),
        cost_estimate=LITTLE,
        name="chip_sums",
    )(keep, got)


def corner_adds_kernel(near_x, got_x, near_y, got_y, send_y, send_x):
    send_y[...] = (near_x[0].astype(WIDE) + got_x[0].astype(WIDE)).astype(LOW)
    send_x[...] = (near_y[0].astype(WIDE) + got_y[0].astype(WIDE)).astype(LOW)


def corner_adds(near_x, got_x, near_y, got_y):
    _, half, width = near_x.shape
    rows = half
    block = pl.BlockSpec((1, rows, width), lambda i: (1, i, 0))
    out = pl.BlockSpec((rows, width), lambda i: (i, 0))
    return pl.pallas_call(
        corner_adds_kernel,
        grid=(half // rows,),
        out_shape=(jax.ShapeDtypeStruct((half, width), LOW),) * 2,
        in_specs=[block] * 4,
        out_specs=(out, out),
        compiler_params=params(),
        cost_estimate=LITTLE,
        name="corner_sums",
    )(near_x, got_x, near_y, got_y)


def split(values):
    high = values.astype(LOW)
    return high, (values - high.astype(WIDE)).astype(LOW)


def norm_back(values, gain, grad):
    factor = lax.rsqrt(jnp.mean(values * values, axis=-1, keepdims=True) + EPSILON)
    scaled = gain * grad
    mean = jnp.mean(values * scaled, axis=-1, keepdims=True)
    grad_values = factor * scaled - values * (factor * factor * factor * mean)
    grad_gain = jnp.sum(grad * values * factor, axis=0, keepdims=True)
    return grad_values, grad_gain


def router_back(logits, routes, grad_shares):
    ids = lax.broadcasted_iota(jnp.int32, logits.shape, 0)
    hit = ids == routes[0:1]
    for k in range(1, TOP):
        hit = jnp.logical_or(hit, ids == routes[k : k + 1])
    weights = jnp.exp(logits - jnp.max(logits, axis=0, keepdims=True))
    probs = weights / jnp.sum(weights, axis=0, keepdims=True)
    chosen = jnp.sum(jnp.where(hit, probs, 0.0), axis=0, keepdims=True)
    grads = jnp.where(hit, grad_shares, 0.0)
    mean = jnp.sum(probs * grads, axis=0, keepdims=True) / chosen
    grad_probs = jnp.where(hit, (grads - mean) / chosen, 0.0)
    return probs * (grad_probs - jnp.sum(probs * grad_probs, axis=0, keepdims=True))


def branch_back_kernel(
    parts, info, residual, normed, cotangent, routes, router, gain, *rest
):
    sums, rest = rest[:parts], rest[parts:]
    experts = router.shape[0]
    count = len(rest) - 7
    refs = rest[:count]
    grad_residual, grad_branch, grad_heads, grad_gain, grad_router, weight, sem = rest[count:]

    @pl.when(pl.program_id(0) == 0)
    def _():
        copies = weight_copies(info, refs, weight, sem, D // QUARTERS + 128, D // QUARTERS)
        run_all(copies)
        logits = nt(router[...], normed[...])
        if parts == 2:
            back_sum, grad_shares = sums[0][...], sums[1][...]
        else:
            values = [
                (ref[0] if len(ref.shape) == 3 else ref[...]).astype(WIDE) for ref in sums
            ]
            upper = values[0] + values[1] + values[2]
            lower = values[3] + values[4] + values[5]
            last = lower.shape[0] - SHARE_ROWS
            shares = lower[last : last + experts]
            grad_shares = shares[:, :TOK_DEV] + shares[:, TOK_DEV : 2 * TOK_DEV]
            back_sum = jnp.concatenate([upper, lower[:last]], axis=0)
        high, low = split(router_back(logits, routes[...], grad_shares))
        grad_router[...] = nn(high, normed[...]) + nn(low, normed[...])
        grad_normed = tn(high, router[...]) + tn(low, router[...])
        grad_normed += back_sum
        grad_values, gain_grad = norm_back(residual[...], gain[...], grad_normed)
        grad_gain[...] = gain_grad
        total = cotangent[...].astype(WIDE) + grad_values
        grad_residual[...] = total
        grad_branch[...] = total.astype(LOW)
        wait_all(copies)

    at = pl.ds(pl.multiple_of(pl.program_id(0) * STEP, STEP), STEP)
    grad_heads[...] = nt(grad_branch[...], weight[at, :]).astype(LOW)


def branch_back(info, residual, normed, sums, cotangent, routes, router, gain, refs):
    full = (TOK_DEV, D)
    total = router.shape[0]
    return pl.pallas_call(
        functools.partial(branch_back_kernel, len(sums)),
        grid=(D // STEP,),
        out_shape=(
            jax.ShapeDtypeStruct(full, WIDE),
            jax.ShapeDtypeStruct(full, LOW),
            jax.ShapeDtypeStruct(full, LOW),
            jax.ShapeDtypeStruct((1, D), WIDE),
            jax.ShapeDtypeStruct((total, D), WIDE),
        ),
        in_specs=[SMEM]
        + [whole(full)] * 3
        + [whole((TOP, TOK_DEV)), whole((total, D)), whole((1, D))]
        + [whole(part.shape if part.ndim == 2 else (1,) + part.shape[1:]) for part in sums]
        + [ANY] * len(refs),
        out_specs=(
            whole(full),
            whole(full),
            pl.BlockSpec((TOK_DEV, STEP), lambda i: (0, i)),
            whole((1, D)),
            whole((total, D)),
        ),
        scratch_shapes=[pltpu.VMEM((D, D), LOW), pltpu.SemaphoreType.DMA],
        compiler_params=params(),
        cost_estimate=LITTLE,
        name="experts_norm_back",
    )(info, residual, normed, cotangent, routes, router, gain, *sums, *refs)


def join_grads_kernel(info, own_grad, source_grad, arrived, cosine, sine, out):
    half = HEAD_DIM // 2
    first = lax.broadcasted_iota(jnp.int32, (TOK_DEV, HEAD_DIM), 1) < half
    leaves = info[1] == 0

    def total(column):
        columns = slice(column, column + 128)
        extra = source_grad[:, columns] + arrived[:, columns].astype(WIDE)
        return own_grad[:, columns] + jnp.where(leaves, 0.0, extra)

    for g in range(KV_HEADS):
        key = turn_back(total(128 * g), cosine[...], sine[...])
        value = total(KEY_WIDTH + 128 * g)
        out[:, 256 * g : 256 * g + 128] = jnp.where(
            first, key, pltpu.roll(value, half, 1)
        ).astype(LOW)
        out[:, 256 * g + 128 : 256 * g + 256] = jnp.where(
            first, pltpu.roll(key, half, 1), value
        ).astype(LOW)


def join_grads(info, own_grad, source_grad, arrived, cosine, sine):
    vmem = pl.BlockSpec(memory_space=pltpu.VMEM)
    return pl.pallas_call(
        join_grads_kernel,
        out_shape=jax.ShapeDtypeStruct((TOK_DEV, 2 * KEY_WIDTH), LOW),
        in_specs=[SMEM] + [vmem] * 5,
        out_specs=vmem,
        compiler_params=params(),
        cost_estimate=LITTLE,
        name="join_key_value_gradients",
    )(info, own_grad, source_grad, arrived, cosine, sine)


def normed_grad_kernel(info, grad_query, *rest):
    refs, (out, weight, sem) = rest[:-3], rest[-3:]

    @pl.when(pl.program_id(0) == 0)
    def _():
        copies = weight_copies(info, refs, weight, sem, 0, D // QUARTERS)
        run_all(copies)
        wait_all(copies)

    at = pl.ds(pl.multiple_of(pl.program_id(0) * STEP, STEP), STEP)
    out[...] = nt(grad_query[...], weight[at, :])


def normed_grad(info, grad_query, refs):
    return pl.pallas_call(
        normed_grad_kernel,
        grid=(D // STEP,),
        out_shape=jax.ShapeDtypeStruct((TOK_DEV, D), WIDE),
        in_specs=[SMEM, whole((TOK_DEV, D))] + [ANY] * len(refs),
        out_specs=pl.BlockSpec((TOK_DEV, STEP), lambda i: (0, i)),
        scratch_shapes=[pltpu.VMEM((D, D), LOW), pltpu.SemaphoreType.DMA],
        compiler_params=params(),
        cost_estimate=LITTLE,
        name="normed_gradient",
    )(info, grad_query, *refs)


def token_back_kernel(info, query_part, grad_pair, tokens, grad_residual, gain, *rest):
    refs, (out, grad_gain, weight, sem) = rest[:-4], rest[-4:]
    copies = weight_copies(info, refs, weight, sem, D // QUARTERS, 128)
    run_all(copies)
    wait_all(copies)
    grad_normed = query_part[...] + nt(grad_pair[...], weight[...])
    grad_values, gain_grad = norm_back(tokens[...].astype(WIDE), gain[...], grad_normed)
    grad_gain[...] = gain_grad
    out[...] = (grad_residual[...] + grad_values).astype(LOW)


def token_back(info, query_part, grad_pair, tokens, grad_residual, gain, refs):
    full = (TOK_DEV, D)
    vmem = pl.BlockSpec(memory_space=pltpu.VMEM)
    return pl.pallas_call(
        token_back_kernel,
        out_shape=(jax.ShapeDtypeStruct(full, LOW), jax.ShapeDtypeStruct((1, D), WIDE)),
        in_specs=[SMEM] + [vmem] * 5 + [ANY] * len(refs),
        out_specs=(vmem, vmem),
        scratch_shapes=[
            pltpu.VMEM((D, 2 * KEY_WIDTH), LOW),
            pltpu.SemaphoreType.DMA,
        ],
        compiler_params=params(),
        cost_estimate=LITTLE,
        name="token_gradient",
    )(info, query_part, grad_pair, tokens, grad_residual, gain, *refs)


def weight_grads_kernel(parts, info, *rest):
    ins, (keep, send) = rest[:-2], rest[-2:]
    depth = D // 8
    core = info[0] & 1
    chip = pl.program_id(0) ^ (info[0] >> 1)
    for strip_at, grads_at, start, width in parts:
        low = tn(ins[strip_at][...], ins[grads_at][...]).astype(LOW)
        columns = slice(start, start + width)
        for slot in range(QUARTERS):
            for j in range(QUARTERS):

                @pl.when(info[2 + slot] == j)
                def _():
                    piece = low[:, j * width : (j + 1) * width]
                    upper, lower = piece[:depth], piece[depth:]
                    keep[0, slot, :depth, columns] = jnp.where(core == 0, upper, lower)
                    send[0, slot, :depth, columns] = jnp.where(core == 0, lower, upper)

    if keep.shape[2] > depth:
        extra = ins[-1]
        for slot in range(QUARTERS):
            to = info[2 + slot]
            keep[0, slot, depth:] = extra[(chip * 2 + core) * QUARTERS + to]
            send[0, slot, depth:] = extra[(chip * 2 + 1 - core) * QUARTERS + to]


def weight_grads(info, strips, grads, parts, extra=None):
    depth = D // 8
    strip = pl.BlockSpec((TOK_DEV, 2 * depth), lambda i, info: (0, i ^ (info[0] >> 1)))
    more = [] if extra is None else [extra]
    width = sum(part[3] for part in parts)
    shape = (4, QUARTERS, depth + EXTRA * len(more), width)
    out = pl.BlockSpec((1,) + shape[1:], lambda i, info: (i, 0, 0, 0))
    return pl.pallas_call(
        functools.partial(weight_grads_kernel, parts),
        grid_spec=pltpu.PrefetchScalarGridSpec(
            num_scalar_prefetch=1,
            grid=(4,),
            in_specs=[strip] * len(strips)
            + [
                pl.BlockSpec(a.shape, lambda i, info, n=a.ndim: (0,) * n)
                for a in (*grads, *more)
            ],
            out_specs=(out, out),
        ),
        out_shape=(jax.ShapeDtypeStruct(shape, LOW),) * 2,
        compiler_params=params(),
        cost_estimate=LITTLE,
        name="weight_gradients",
    )(info, *strips, *grads, *more)


def last_sums_kernel(part, info, own, *rest):
    arrived, (query_out, key_out, value_out, out_out, extra_out) = rest[:-5], rest[-5:]
    total = own[...].astype(WIDE)
    for ref in arrived[:-1]:
        total += ref[...].astype(WIDE)
    end = jnp.logical_or(info[2] == 0, info[2] == 3)
    total += jnp.where(end, arrived[-1][...].astype(WIDE), 0.0)
    depth = query_out.shape[0]
    quarter = query_out.shape[1]
    query_out[...] = total[:depth, :quarter]
    pair = total[:depth, 2 * quarter :].T
    key_out[...] = pair[:part]
    value_out[...] = pair[part:]
    out_out[...] = total[:depth, quarter : 2 * quarter]
    extra_out[...] = total[depth:]


def last_sums(info, own, arrived, depth, part):
    height, width = own.shape
    quarter = D // QUARTERS
    vmem = pl.BlockSpec(memory_space=pltpu.VMEM)
    return pl.pallas_call(
        functools.partial(last_sums_kernel, part),
        out_shape=(
            jax.ShapeDtypeStruct((depth, quarter), WIDE),
            jax.ShapeDtypeStruct((part, depth), WIDE),
            jax.ShapeDtypeStruct((part, depth), WIDE),
            jax.ShapeDtypeStruct((depth, quarter), WIDE),
            jax.ShapeDtypeStruct((height - depth, width), WIDE),
        ),
        in_specs=[SMEM] + [vmem] * (1 + len(arrived)),
        out_specs=(vmem,) * 5,
        compiler_params=params(),
        cost_estimate=LITTLE,
        name="last_sums",
    )(info, own, *arrived)


def expert_sums_kernel(count, *rest):
    blocks, outs = rest[:count], rest[count:]
    part = outs[0].shape[1]
    for e in range(count):
        for which, out in enumerate(outs):
            out[e] = blocks[e][which * part : (which + 1) * part].astype(WIDE)


def expert_sums(blocks):
    count, part = len(blocks), blocks[0].shape[0] // 3
    vmem = pl.BlockSpec(memory_space=pltpu.VMEM)
    return pl.pallas_call(
        functools.partial(expert_sums_kernel, count),
        out_shape=(jax.ShapeDtypeStruct((count, part, D), WIDE),) * 3,
        in_specs=[vmem] * count,
        out_specs=(vmem,) * 3,
        compiler_params=params(),
        cost_estimate=LITTLE,
        name="expert_sums",
    )(*blocks)


def position_of(token_index):
    branch_place = TRUNK + (token_index - TRUNK) % BRANCH
    leaf_place = TRUNK + BRANCH + (token_index - TOK_DEV) % BRANCH
    return jnp.where(
        token_index < TRUNK, token_index, jnp.where(token_index < TOK_DEV, branch_place, leaf_place)
    )


def rotary_tables(positions):
    half_dim = HEAD_DIM // 2
    frequency = ROPE_BASE ** (-jnp.arange(half_dim, dtype=jnp.float32) / half_dim)
    angles = positions.astype(jnp.float32)[:, None] * frequency[None, :]
    cosine, sine = (jnp.cos(angles), jnp.sin(angles))
    return (
        jnp.concatenate([cosine, cosine], axis=1),
        jnp.concatenate([-sine, sine], axis=1),
    )


def after(values, *earlier):
    return lax.optimization_barrier((values, earlier))[0]


def fast_mesh():
    return lax.axis_size("rows") == 8 and lax.axis_size("cols") == 4


SLOT_SHARD = ((0, 2, 1, 3), (1, 3, 0, 2), (2, 0, 1, 3), (3, 1, 2, 0))
UP = [(0, 1), (1, 2), (2, 3)]
DOWN = [(1, 0), (2, 1), (3, 2)]
FAR = [(0, 3), (3, 0)]


def send_near(block):
    return lax.ppermute(block, "cols", DOWN), lax.ppermute(block, "cols", UP)


def send_far(block):
    return lax.ppermute(block, "cols", FAR)


def send_over(block):
    return lax.ppermute(block, "cols", [(0, 2), (1, 3), (2, 0), (3, 1)])


def send_second(block, near):
    place = lax.axis_index("cols")
    above, below = near
    payload = jnp.where(place == 1, above, jnp.where(place == 2, below, block))
    return lax.ppermute(payload, "cols", [(3, 1), (1, 0), (0, 2), (2, 3)])


def slot_list(block, near, second, far):
    place = lax.axis_index("cols")
    above, below = near
    end = (place == 0) | (place == 3)
    return [
        block,
        second,
        jnp.where(place == 0, above, below),
        jnp.where(end, far, above),
    ]


def send_slots(slots):
    place = lax.axis_index("cols")
    _, second, third, fourth = slots
    relay = lax.ppermute(second, "cols", [(1, 3), (0, 1), (2, 0), (3, 2)])
    relayed = relay.astype(WIDE)
    upward_load = (
        jnp.where(place == 0, third, fourth).astype(WIDE) + jnp.where(place == 1, relayed, 0.0)
    ).astype(LOW)
    downward_load = (third.astype(WIDE) + jnp.where(place == 2, relayed, 0.0)).astype(LOW)
    return (
        lax.ppermute(upward_load, "cols", UP),
        lax.ppermute(downward_load, "cols", DOWN),
        send_far(after(fourth, upward_load, downward_load)),
        relay,
    )


def flip(block, bit):
    count = lax.axis_size("rows")
    return lax.ppermute(block, "rows", [(i, i ^ bit) for i in range(count)])


def add_low(one, two):
    return (one.astype(WIDE) + two.astype(WIDE)).astype(LOW)


def chips_second(near_x, near_y, got_x, got_y):
    for_y, for_x = corner_adds(near_x, got_x, near_y, got_y)
    return (near_x, got_x, flip(for_y, 4), near_y, got_y, flip(for_x, 2))


def turn_corner(beside, across):
    half = beside.shape[0] // 2
    return jnp.concatenate([flip(beside[:half], 4), flip(across[half:], 2)], axis=0)


def send_chips(sums):
    return flip(sums[0], 2), flip(sums[1], 4)


def sum_parts(parts):
    wide = [(a[0] if a.ndim == 3 else a).astype(WIDE) for a in parts]
    if len(wide) == 1:
        return wide[0]
    return jnp.concatenate([wide[0] + wide[1] + wide[2], wide[3] + wide[4] + wide[5]], axis=0)


def on_device(
    tokens,
    query_weight,
    key_weight,
    value_weight,
    out_weight,
    router_weight,
    attention_gain,
    experts_gain,
    gate_weight,
    upward_weight,
    down_weight,
    routes,
    leaf_parent,
    cotangent,
):
    row_count = lax.axis_size("rows")
    col_count = lax.axis_size("cols")
    row_place = lax.axis_index("rows")
    col_place = lax.axis_index("cols")
    fast = fast_mesh()
    parity = lax.rem(col_place, 2)
    tree_id = lax.div(row_place * col_count + col_place, 2)
    parent_row = lax.dynamic_slice_in_dim(leaf_parent, tree_id, 1, 0)[0]
    depth, query_part = query_weight.shape
    key_part = key_weight.shape[1]
    router_part = router_weight.shape[1]
    gain_part = attention_gain.shape[0]
    expert_total = router_part * col_count
    local_experts = gate_weight.shape[0]
    capacity = TOK_DEV * TOP // expert_total * 5 // 4

    shards = (
        jnp.asarray(SLOT_SHARD, jnp.int32)[col_place]
        if fast
        else jnp.arange(4, dtype=jnp.int32)
    )
    branch_rows = jnp.where(parity == 0, TRUNK + BRANCH * parent_row, TRUNK)
    info = jnp.concatenate(
        [jnp.stack([row_place, parity]), shards, branch_rows, jnp.zeros((2,), jnp.int32)]
    ).astype(jnp.int32)

    packed = jnp.concatenate([query_weight, key_weight, value_weight, out_weight], axis=1)
    local_index = (1 - parity) * TOK_DEV + jnp.arange(TOK_DEV, dtype=jnp.int32)
    cosine, sine = rotary_tables(position_of(local_index))
    shard_blocks = [
        jnp.concatenate(
            [gate_weight[expert].T, upward_weight[expert].T, down_weight[expert]], axis=0
        )
        for expert in range(local_experts)
    ]
    expert_refs = []
    if fast:
        wide = packed.shape[1]
        gains = jnp.concatenate([attention_gain, experts_gain])[None, :]
        packed = jnp.concatenate(
            [
                packed,
                jnp.pad(router_weight.T, ((0, 0), (0, wide - depth))),
                jnp.pad(gains, ((0, 0), (0, wide - 2 * gain_part))),
                jnp.pad(routes.T.astype(LOW), ((0, 0), (0, wide - TOK_DEV))),
                jnp.zeros((EXTRA - router_part - 1 - TOP, wide), LOW),
            ],
            axis=0,
        )
        packed_near = send_near(packed)
        packed_far = send_far(packed)
        packed_second = send_over(packed)
        first_block = after(shard_blocks[0], *packed_near)
        first_near = send_near(first_block)
        first_far = send_far(first_block)
        own = jnp.stack(slot_list(packed, packed_near, packed_second, packed_far))
        own = after(own, info, cosine, sine)
        beside, across = flip(own, 2), flip(own, 4)
        own_in = flip(own, 1)
        beside, across = after((beside, across), own_in, *first_near)
        corner = [flip(beside[:2], 4), flip(across[2:], 2)]
        pair_in = flip(jnp.concatenate([beside, across], axis=0), 1)
        corner_in = [flip(piece, 1) for piece in corner]
        grad_in = after(cotangent, *corner)
        grad_flips = [flip(grad_in, 2), flip(grad_in, 4)]
        pieces = [own, own_in, beside, across, *corner, pair_in, *corner_in]
        at = depth + router_part + 1
        near_slots = [own, own_in, beside, pair_in, across, pair_in[4:], corner[0], corner_in[0]]
        routes_all = jnp.stack([part[0, at : at + TOP, :TOK_DEV] for part in near_slots])
        routes_all = routes_all.astype(jnp.int32)
        chosen, place_rows = tables(info, routes_all, capacity, local_experts, expert_total)
        query_refs = pair_refs = out_refs = pieces
        extra_rows = extras(info, pieces)
        router_all = extra_rows[:, :router_part, :depth]
        attention_scale = extra_rows[:, router_part, :gain_part]
        experts_scale = extra_rows[:, router_part, gain_part : 2 * gain_part]
    else:
        packed_all = lax.all_gather(lax.all_gather(packed, "cols", axis=0), "rows", axis=0)

        def unpack(start, width):
            part = packed_all[..., start : start + width]
            return jnp.swapaxes(part, 1, 2).reshape(row_count * depth, col_count * width)

        key_at = query_part
        query_refs = [unpack(0, query_part)]
        pair_refs = [
            jnp.concatenate(
                [
                    unpack(key_at, key_part).reshape(D, QUARTERS, -1),
                    unpack(key_at + key_part, key_part).reshape(D, QUARTERS, -1),
                ],
                axis=2,
            ).reshape(D, -1)
        ]
        out_refs = [unpack(key_at + 2 * key_part, query_part)]
        routes_all = lax.all_gather(routes.T, "rows", axis=0)
        chosen, place_rows = tables(info, routes_all, capacity, local_experts, expert_total)
        axes = ("rows", "cols")
        router_all = jnp.swapaxes(lax.all_gather(router_weight, axes, axis=0), 1, 2)
        attention_scale = lax.all_gather(attention_gain, axes, axis=0)
        experts_scale = lax.all_gather(experts_gain, axes, axis=0)

    attention_scale = attention_scale.reshape(1, D).astype(WIDE)
    experts_scale = experts_scale.reshape(1, D).astype(WIDE)
    router_rows = jnp.transpose(
        router_all.reshape(row_count, col_count, router_part, depth), (1, 2, 0, 3)
    ).reshape(expert_total, D)
    router_cols = router_rows.T
    tokens_in = after(tokens, first_far, chosen) if fast else tokens
    normed, own_pair = key_value(info, tokens_in, attention_scale, cosine, sine, pair_refs)
    pairs = [(i + 1, i) for i in range(0, col_count, 2)]
    partner = lax.ppermute(own_pair, "cols", pairs)
    if fast:
        own_grad_in = flip(grad_in, 1)
        normed_in = after(normed, own_grad_in)
    else:
        normed_in = normed
    queries = query(info, normed_in, cosine, sine, query_refs)
    if fast:
        first_second = send_second(after(first_block, partner, queries), first_near)
        expert_refs.append([first_block, first_second, *first_near, first_far])
    if fast:
        grad_flips = after(grad_flips, queries)
        grad_corner = turn_corner(*grad_flips)
    heads = attention(info, queries, own_pair, partner)
    if fast:
        grad_near = [*grad_flips, grad_corner]
        grad_blocks = [cotangent, own_grad_in]
        grad_blocks += [block for one in grad_near for block in (one, flip(one, 1))]
        heads = after(heads, grad_corner, grad_blocks[3], grad_blocks[5])
    else:
        grad_all = lax.all_gather(cotangent, "rows", axis=0)
        grad_blocks = [grad_all[q] for q in range(row_count)]
    residual, normed_two = out_projection(info, heads, tokens, experts_scale, out_refs)

    if fast:
        beside, across = flip(normed_two, 2), flip(normed_two, 4)
        beside_in = flip(normed_two, 1)
        later_block = after(shard_blocks[1], first_second, normed_two)
        expert_refs.append([lax.all_gather(later_block, "cols", axis=0)])
    else:
        rows_all = lax.all_gather(normed_two, "rows", axis=0)
        expert_refs = [[lax.all_gather(block, "cols", axis=0)] for block in shard_blocks]
    grad_rows = pick_rows(chosen, grad_blocks, local_experts)

    def place_block(q, block, picked):
        return dispatch(
            q, info, block, chosen, routes_all, router_cols, local_experts, picked
        )

    if fast:
        half = TOK_DEV // 2
        picked = place_block(0, normed_two, None)
        picked = place_block(1, beside_in, after(picked, *grad_rows))
        beside, across = after((beside, across), picked)
        corner = [flip(beside[:half], 4), flip(across[half:], 2)]
        picked = place_block(2, beside, picked)
        picked = place_block(4, across, picked)
        beside_in = flip(beside, 1)
        across_in = flip(across, 1)
        picked = place_block(3, beside_in, picked)
        picked = place_block(5, across_in, picked)
        corner = jnp.concatenate(after(corner, picked), axis=0)
        corner_in = flip(corner, 1)
        picked = place_block(6, corner, picked)
        picked = place_block(7, corner_in, picked)
    else:
        picked = None
        for q in range(row_count):
            picked = place_block(q, rows_all[q], picked)
    height = row_count * capacity
    token_rows = [a.reshape(height, D) for a in picked[:local_experts]]
    grad_rows = [a.reshape(height, D) for a in grad_rows]
    share_rows = [a.reshape(height, 1) for a in picked[local_experts:]]

    out_rows, back_rows, gate_dots, reduced = ([], [], [], [])
    for e in range(local_experts):
        rows_in = after(token_rows[e], *reduced_in) if e else token_rows[e]
        out_row, back_row, grad_row, acts, dots = expert(
            info, rows_in, grad_rows[e], share_rows[e], expert_refs[e], col_count
        )
        out_rows.append(out_row.reshape(row_count, capacity, D))
        back_rows.append(back_row.reshape(row_count, capacity, D))
        gate_dots.append(dots.reshape(row_count, capacity, 1))
        if fast and e == 1:
            got = flip(combine(info, chosen, back_rows, 1, 2, gate_dots), 1)
            back_keep = combine(info, chosen, back_rows, 0, 2, gate_dots)
            for_x, for_y, near_x, near_y = chip_adds(back_keep, got)
            acts = after(acts, for_x)
            back_flips = send_chips((for_x, for_y))
        slots = expert_grads(acts, token_rows[e], grad_row)
        reduced_in = (slots,)
        if e and fast:
            out_got = flip(combine(info, chosen, out_rows, 1, 2), 1)
            out_keep = combine(info, chosen, out_rows, 0, 2)
            back_flips = after(back_flips, slots, out_keep)
            back_parts = chips_second(near_x, near_y, *back_flips)
        else:
            reduced.append(lax.psum_scatter(slots, "cols", scatter_dimension=0, tiled=False))

    if fast:
        out_first = chip_adds(out_keep, out_got)
        back_parts = after(back_parts, out_first[0])
    else:
        spread_dots = spread(place_rows, gate_dots)
        grad_shares = lax.all_to_all(spread_dots, "rows", split_axis=0, concat_axis=0, tiled=True)

        def summed(rows):
            part = combine(info, chosen, rows, 0, 1)
            return lax.psum_scatter(part, "rows", scatter_dimension=0).astype(WIDE)

        back_parts = (summed(back_rows), grad_shares.reshape(expert_total, TOK_DEV))
        mixture = (summed(out_rows),)

    grad_residual, grad_branch, grad_heads, experts_gain_grad, router_grad = branch_back(
        info,
        residual,
        normed_two,
        back_parts,
        cotangent,
        routes.T,
        router_rows,
        experts_scale,
        out_refs,
    )
    if fast:
        out_flips = send_chips(after(out_first[:2], back_parts[2], back_parts[5]))
        slots = after(slots, reduced[0], back_parts[2])
        reduced.append(lax.psum_scatter(slots, "cols", scatter_dimension=0, tiled=False))
        main_width = 2 * query_part
        router_parts = jnp.transpose(
            router_grad.astype(LOW).reshape(col_count, router_part, row_count, depth),
            (2, 0, 1, 3),
        ).reshape(row_count * col_count, router_part, depth)
        gain_rows = experts_gain_grad.astype(LOW).reshape(row_count * col_count, 1, gain_part)
        extra = jnp.concatenate(
            [
                jnp.pad(router_parts, ((0, 0), (0, 0), (0, main_width - depth))),
                jnp.pad(gain_rows, ((0, 0), (0, 0), (0, main_width - gain_part))),
                jnp.zeros((row_count * col_count, EXTRA - router_part - 1, main_width), LOW),
            ],
            axis=1,
        )
    grad_query, own_grad, source_grad = attention_back(
        info, queries, own_pair, partner, grad_heads, cosine, sine
    )
    arrived = lax.ppermute(source_grad.astype(LOW), "cols", [(j, i) for i, j in pairs])
    if fast:
        parts = ((0, 2, 0, query_part), (1, 3, query_part, query_part))
        grad_branch = after(grad_branch, *out_flips)
        keep, send = weight_grads(
            info, [normed, heads], [grad_query, grad_branch], parts, extra
        )
        flat = (4, col_count * (depth + EXTRA), main_width)
        sent = flip(send, 1)
        main_first = chip_adds(keep.reshape(flat), sent.reshape(flat))
        main_chips = send_chips(main_first[:2])
        query_back = normed_grad(info, after(grad_query, main_first[0]), query_refs)
        main_chips = after(main_chips, query_back)
        main_x, main_y = main_first[2:]
        for_y, for_x = corner_adds(main_x, main_chips[0], main_y, main_chips[1])
        main_parts = (main_x, main_chips[0], flip(for_y, 4), main_y, main_chips[1])
        main_parts += (flip(for_x, 2),)
        arrived = after(arrived, for_y)
    else:
        query_back = normed_grad(info, grad_query, query_refs)
    grad_pair = join_grads(info, own_grad, source_grad, arrived, cosine, sine)
    if fast:
        keep, send = weight_grads(info, [normed], [grad_pair], ((0, 1, 0, 2 * key_part),))
        flat = (4, col_count * depth, 2 * key_part)
        pair_first = chip_adds(keep.reshape(flat), flip(send, 1).reshape(flat))
        pair_chips = send_chips(pair_first[:2])
        grad_pair = after(grad_pair, pair_first[0])
    tokens_grad, attention_gain_grad = token_back(
        info, query_back, grad_pair, tokens, grad_residual, attention_scale, pair_refs
    )

    if fast:
        pair_parts = chips_second(*pair_first[2:], *after(pair_chips, tokens_grad))
        near_x, near_y = out_first[2:]
        mixture = chips_second(near_x, near_y, *after(out_flips, pair_parts[2], pair_parts[5]))
    layer_output = (residual + sum_parts(mixture)).astype(LOW)
    gate_grad, upward_grad, down_grad = expert_sums(reduced)
    gate_grad, upward_grad = jnp.swapaxes(gate_grad, 1, 2), jnp.swapaxes(upward_grad, 1, 2)
    if fast:
        main_parts = after(main_parts, tokens_grad)
        slots = sum_parts(main_parts).reshape(col_count, depth + EXTRA, main_width)
        pairs_sum = sum_parts(pair_parts).reshape(col_count, depth, 2 * key_part)
        width = query_part + 2 * key_part
        weights_own = jnp.stack([own[i, :depth, :width].astype(WIDE) for i in range(4)])
        gain_sums = jnp.sum(
            weights_own[..., :query_part] * slots[:, :depth, :query_part], axis=(0, 2)
        ) + jnp.sum(weights_own[..., query_part:] * pairs_sum, axis=(0, 2))
        own_gains = lax.dynamic_slice_in_dim(attention_scale[0], row_place * depth, depth, 0)
        gain_sums = (gain_sums / own_gains).reshape(col_count, 1, gain_part)
        gain_sums = jnp.pad(
            jnp.take(gain_sums, shards, axis=0),
            (
                (0, 0),
                (depth + router_part + 1, EXTRA - router_part - 2),
                (0, main_width - gain_part),
            ),
        )
        pairs_sum = jnp.pad(pairs_sum, ((0, 0), (0, EXTRA), (0, 0)))
        slots = jnp.concatenate([slots + gain_sums, pairs_sum], axis=2).astype(LOW)
        slots = after(slots, reduced[1])

        arrived = send_slots(slots)
        earlier = (gate_grad, upward_grad, down_grad, layer_output)
        query_sum, key_sum, value_sum, out_sum, extra_sum = last_sums(
            info, slots[0], after(arrived, *earlier), depth, key_part
        )
        key_sum, value_sum = key_sum.T, value_sum.T
        router_sum = extra_sum[:router_part, :depth].T
        experts_gain_sum = extra_sum[router_part, :gain_part]
        attention_gain_sum = extra_sum[router_part + 1, :gain_part]
    else:
        full_grads = [
            tn(normed, grad_query),
            *jnp.moveaxis(tn(normed, grad_pair).reshape(D, QUARTERS, 2, -1), 2, 0),
            tn(heads, grad_branch),
        ]
        packed_grad = jnp.concatenate(
            [
                grad.astype(LOW).reshape(row_count, depth, col_count, -1)
                for grad in full_grads
            ],
            axis=3,
        )
        row_sums = lax.psum_scatter(packed_grad, "rows", scatter_dimension=0)
        sums = lax.psum_scatter(row_sums, "cols", scatter_dimension=1).astype(WIDE)
        key_at = query_part
        value_at = key_at + key_part
        out_at = value_at + key_part
        query_sum, out_sum = sums[:, :key_at], sums[:, out_at:]
        key_sum, value_sum = sums[:, key_at:value_at], sums[:, value_at:out_at]
        small_grads = jnp.concatenate(
            [
                attention_gain_grad.reshape(-1, gain_part),
                experts_gain_grad.reshape(-1, gain_part),
                jnp.transpose(
                    router_grad.reshape(col_count, router_part, row_count, depth), (2, 0, 3, 1)
                ).reshape(row_count * col_count, depth * router_part),
            ],
            axis=1,
        )
        small_grads = small_grads.reshape(row_count, -1)
        small_grads = lax.all_to_all(small_grads, "rows", split_axis=0, concat_axis=0, tiled=True)
        small_grads = jnp.sum(small_grads, axis=0).reshape(col_count, -1)
        small_grads = lax.all_to_all(small_grads, "cols", split_axis=0, concat_axis=0, tiled=True)
        small_sums = jnp.sum(small_grads, axis=0)
        attention_gain_sum = small_sums[:gain_part]
        experts_gain_sum = small_sums[gain_part : 2 * gain_part]
        router_sum = small_sums[2 * gain_part :].reshape(depth, router_part)

    return (
        layer_output,
        tokens_grad,
        query_sum,
        key_sum,
        value_sum,
        out_sum,
        router_sum,
        attention_gain_sum,
        experts_gain_sum,
        gate_grad,
        upward_grad,
        down_grad,
    )


def solution(mesh):
    in_specs = (
        P(("rows", "cols"), None),
        P("rows", "cols"),
        P("rows", "cols"),
        P("rows", "cols"),
        P("rows", "cols"),
        P("rows", "cols"),
        P(("rows", "cols")),
        P(("rows", "cols")),
        P("rows", None, "cols"),
        P("rows", None, "cols"),
        P("rows", "cols", None),
        P(("rows", "cols"), None),
        P(),
        P(("rows", "cols"), None),
    )
    out_specs = (
        P(("rows", "cols"), None),
        P(("rows", "cols"), None),
        P("rows", "cols"),
        P("rows", "cols"),
        P("rows", "cols"),
        P("rows", "cols"),
        P("rows", "cols"),
        P(("rows", "cols")),
        P(("rows", "cols")),
        P("rows", None, "cols"),
        P("rows", None, "cols"),
        P("rows", "cols", None),
    )
    return jax.shard_map(
        on_device, mesh=mesh, in_specs=in_specs, out_specs=out_specs, check_vma=False
    )
```

```python
import functools

import jax
import jax.numpy as jnp
from jax import lax
from jax.experimental import pallas as pl
from jax.experimental.pallas import tpu as pltpu
from jax.sharding import PartitionSpec as P

D = 1536
HEADS = 12
KV_HEADS = 2
HEAD_DIM = 128
TOP = 4
TOK_DEV = 512
BRANCHES = 4
LEAVES = 8
TRUNK = 256
BRANCH = 64

EPSILON = 1e-06
ROPE_BASE = 10000.0
MASKED = -1e30
LOW = jnp.bfloat16
WIDE = jnp.float32
KEY_WIDTH = KV_HEADS * HEAD_DIM
GROUP = HEADS // KV_HEADS
QUARTERS = 4
VMEM_LIMIT = 56 * 1024 * 1024

ANY = pl.BlockSpec(memory_space=pl.ANY)
SMEM = pl.BlockSpec(memory_space=pltpu.SMEM)


def nn(one, two):
    return lax.dot_general(one, two, (((1,), (0,)), ((), ())), preferred_element_type=WIDE)


def nt(one, two):
    return lax.dot_general(one, two, (((1,), (1,)), ((), ())), preferred_element_type=WIDE)


def tn(one, two):
    return lax.dot_general(one, two, (((0,), (0,)), ((), ())), preferred_element_type=WIDE)


def whole(shape):
    return pl.BlockSpec(shape, lambda *_: (0,) * len(shape))


LITTLE = pl.CostEstimate(flops=1, bytes_accessed=1, transcendentals=0)


def params():
    return pltpu.CompilerParams(vmem_limit_bytes=VMEM_LIMIT)


def turn(values, cosine, sine):
    return values * cosine + pltpu.roll(values, HEAD_DIM // 2, 1) * sine


def turn_back(values, cosine, sine):
    return values * cosine - pltpu.roll(values, HEAD_DIM // 2, 1) * sine


SLOTS = range(4)
PIECES = (
    tuple((0, slot) for slot in SLOTS),
    tuple((1, slot) for slot in SLOTS),
    tuple((2, slot) for slot in SLOTS),
    tuple((4, slot) for slot in SLOTS),
    ((6, 0), (6, 1)),
    ((6, 2), (6, 3)),
    tuple((flip_bits, slot) for flip_bits in (3, 5) for slot in SLOTS),
    ((7, 0), (7, 1)),
    ((7, 2), (7, 3)),
)
EXTRA = 16


STEP = 768


def weight_copies(info, refs, target, sem, start, width):
    if len(refs) == 1:
        return [pltpu.make_async_copy(refs[0], target, sem)]
    depth = refs[0].shape[1] - EXTRA
    copies = []
    for ref, parts in zip(refs, PIECES):
        for at, (flip_bits, slot) in enumerate(parts):
            row = pl.multiple_of((info[0] ^ flip_bits) * depth, depth)
            col = pl.multiple_of(info[2 + slot] * width, 128)
            copies.append(
                pltpu.make_async_copy(
                    ref.at[at, pl.ds(0, depth), pl.ds(start, width)],
                    target.at[pl.ds(row, depth), pl.ds(col, width)],
                    sem,
                )
            )
    return copies


def extras_kernel(info, *rest):
    refs, (out, sem) = rest[:-2], rest[-2:]
    depth = refs[0].shape[1] - EXTRA
    copies = []
    for ref, parts in zip(refs, PIECES):
        for at, (flip_bits, slot) in enumerate(parts):
            to = (info[0] ^ flip_bits) * QUARTERS + info[2 + slot]
            copies.append(pltpu.make_async_copy(ref.at[at, pl.ds(depth, EXTRA)], out.at[to], sem))
    run_all(copies)
    wait_all(copies)


def extras(info, refs):
    return pl.pallas_call(
        extras_kernel,
        out_shape=jax.ShapeDtypeStruct((8 * QUARTERS, EXTRA, refs[0].shape[2]), LOW),
        in_specs=[SMEM] + [ANY] * len(refs),
        out_specs=pl.BlockSpec(memory_space=pltpu.VMEM),
        scratch_shapes=[pltpu.SemaphoreType.DMA],
        compiler_params=params(),
        cost_estimate=LITTLE,
        name="extra_rows",
    )(info, *refs)


def run_all(copies):
    for copy in copies:
        copy.start()


def wait_all(copies):
    for copy in copies:
        copy.wait()


def key_value_kernel(info, tokens, gain, cosine, sine, *rest):
    count = len(rest) - 4
    refs, (normed, out, weight, sem) = rest[:count], rest[count:]
    copies = weight_copies(info, refs, weight, sem, D // QUARTERS, 128)
    run_all(copies)
    values = tokens[...].astype(WIDE)
    factor = lax.rsqrt(jnp.mean(values * values, axis=-1, keepdims=True) + EPSILON)
    low = (values * factor * gain[...]).astype(LOW)
    normed[...] = low
    wait_all(copies)
    both = nn(low, weight[...])
    half = HEAD_DIM // 2
    first = lax.broadcasted_iota(jnp.int32, (TOK_DEV, HEAD_DIM), 1) < half
    for g in range(KV_HEADS):
        one = both[:, 256 * g : 256 * g + 128]
        two = both[:, 256 * g + 128 : 256 * g + 256]
        key = jnp.where(first, one, pltpu.roll(two, half, 1))
        value = jnp.where(first, pltpu.roll(one, half, 1), two)
        out[:, 128 * g : 128 * g + 128] = turn(key, cosine[...], sine[...]).astype(LOW)
        out[:, KEY_WIDTH + 128 * g : KEY_WIDTH + 128 * g + 128] = value.astype(LOW)


def key_value(info, tokens, gain, cosine, sine, refs):
    return pl.pallas_call(
        key_value_kernel,
        out_shape=(
            jax.ShapeDtypeStruct((TOK_DEV, D), LOW),
            jax.ShapeDtypeStruct((TOK_DEV, 2 * KEY_WIDTH), LOW),
        ),
        in_specs=[SMEM] + [pl.BlockSpec(memory_space=pltpu.VMEM)] * 4 + [ANY] * len(refs),
        out_specs=(pl.BlockSpec(memory_space=pltpu.VMEM),) * 2,
        scratch_shapes=[pltpu.VMEM((D, 2 * KEY_WIDTH), LOW), pltpu.SemaphoreType.DMA],
        compiler_params=params(),
        cost_estimate=LITTLE,
        name="norm_key_value",
    )(info, tokens, gain, cosine, sine, *refs)


def query_kernel(info, normed, cosine, sine, *rest):
    count = len(rest) - 3
    refs, (out, weight, sem) = rest[:count], rest[count:]

    @pl.when(pl.program_id(0) == 0)
    def _():
        copies = weight_copies(info, refs, weight, sem, 0, D // QUARTERS)
        run_all(copies)
        wait_all(copies)

    at = pl.multiple_of(pl.program_id(0) * STEP, STEP)
    lin = nn(normed[...], weight[:, pl.ds(at, STEP)])
    for h in range(STEP // HEAD_DIM):
        out[:, 128 * h : 128 * h + 128] = turn(
            lin[:, 128 * h : 128 * h + 128], cosine[...], sine[...]
        ).astype(LOW)


def query(info, normed, cosine, sine, refs):
    return pl.pallas_call(
        query_kernel,
        grid=(D // STEP,),
        out_shape=jax.ShapeDtypeStruct((TOK_DEV, D), LOW),
        in_specs=[SMEM, whole((TOK_DEV, D)), whole((TOK_DEV, 128)), whole((TOK_DEV, 128))]
        + [ANY] * len(refs),
        out_specs=pl.BlockSpec((TOK_DEV, STEP), lambda i: (0, i)),
        scratch_shapes=[pltpu.VMEM((D, D), LOW), pltpu.SemaphoreType.DMA],
        compiler_params=params(),
        cost_estimate=LITTLE,
        name="query_projection",
    )(info, normed, cosine, sine, *refs)


KEYS = TRUNK + 2 * BRANCH
CHUNKS = TOK_DEV // BRANCH


def chunk_keys(info, source, own, column, chunk):
    at = pl.multiple_of(info[6 + chunk], BRANCH)
    rows = pl.multiple_of(chunk * BRANCH, BRANCH)
    columns = slice(column, column + HEAD_DIM)
    return jnp.concatenate(
        [
            source[0:TRUNK, columns],
            source[pl.ds(at, BRANCH), columns],
            own[pl.ds(rows, BRANCH), columns],
        ],
        axis=0,
    )


def chunk_allowed(info, chunk, query_axis, shape):
    query_row = lax.broadcasted_iota(jnp.int32, shape, query_axis) & (BRANCH - 1)
    key = lax.broadcasted_iota(jnp.int32, shape, 1 - query_axis)
    leaves = info[1] == 0
    trunk = jnp.logical_and(jnp.logical_not(leaves), chunk < TRUNK // BRANCH)
    limit = jnp.where(trunk, chunk * BRANCH + query_row, TRUNK - 1)
    branch_limit = jnp.where(leaves, TRUNK + BRANCH - 1, 0)
    own_limit = jnp.where(trunk, 0, query_row + TRUNK + BRANCH)
    top = jnp.where(key < TRUNK, limit, jnp.where(key < TRUNK + BRANCH, branch_limit, own_limit))
    return key <= top


def group_rows(ref, g):
    first = g * GROUP
    return jnp.concatenate(
        [ref[:, 128 * h : 128 * h + 128] for h in range(first, first + GROUP)], axis=0
    )


def keep_source(info, partner, own, source):
    @pl.when(pl.program_id(0) == 0)
    def _():
        @pl.when(info[1] == 0)
        def _():
            source[...] = partner[...]

        @pl.when(info[1] != 0)
        def _():
            source[...] = own[...]


def attention_kernel(info, queries, own, partner, out, source):
    keep_source(info, partner, own, source)
    chunk = pl.program_id(0)
    rows = GROUP * BRANCH
    allowed = chunk_allowed(info, chunk, 0, (rows, KEYS))
    for g in range(KV_HEADS):
        keys = chunk_keys(info, source, own, 128 * g, chunk)
        values = chunk_keys(info, source, own, KEY_WIDTH + 128 * g, chunk)
        scores = nt(group_rows(queries, g), keys) * HEAD_DIM**-0.5
        scores = jnp.where(allowed, scores, MASKED)
        weights = jnp.exp(scores - jnp.max(scores, axis=1, keepdims=True))
        total = jnp.sum(weights, axis=1, keepdims=True)
        mixed = nn((weights * (1.0 / total)).astype(LOW), values).astype(LOW)
        for h in range(GROUP):
            at = (g * GROUP + h) * 128
            out[:, at : at + 128] = mixed[h * BRANCH : (h + 1) * BRANCH]


def attention(info, queries, own, partner):
    return pl.pallas_call(
        attention_kernel,
        grid=(CHUNKS,),
        out_shape=jax.ShapeDtypeStruct((TOK_DEV, D), LOW),
        in_specs=[
            SMEM,
            pl.BlockSpec((BRANCH, D), lambda i: (i, 0)),
            whole((TOK_DEV, 2 * KEY_WIDTH)),
            whole((TOK_DEV, 2 * KEY_WIDTH)),
        ],
        out_specs=pl.BlockSpec((BRANCH, D), lambda i: (i, 0)),
        scratch_shapes=[pltpu.VMEM((TOK_DEV, 2 * KEY_WIDTH), LOW)],
        compiler_params=params(),
        cost_estimate=LITTLE,
        name="tree_attention",
    )(info, queries, own, partner)


def attention_back_kernel(
    info, queries, own, partner, grads, cosine, sine, grad_query, own_grad, source_grad, source
):
    keep_source(info, partner, own, source)
    chunk = pl.program_id(0)

    @pl.when(chunk == 0)
    def _():
        source_grad[...] = jnp.zeros_like(source_grad)

    rows = GROUP * BRANCH
    scale = HEAD_DIM**-0.5
    allowed = chunk_allowed(info, chunk, 1, (KEYS, rows))
    at = pl.multiple_of(info[6 + chunk], BRANCH)
    for g in range(KV_HEADS):
        keys = chunk_keys(info, source, own, 128 * g, chunk)
        values = chunk_keys(info, source, own, KEY_WIDTH + 128 * g, chunk)
        query_rows = group_rows(queries, g)
        grad_rows = group_rows(grads, g)
        scores = jnp.where(allowed, nt(keys, query_rows) * scale, MASKED)
        weights = jnp.exp(scores - jnp.max(scores, axis=0, keepdims=True))
        probs = weights * (1.0 / jnp.sum(weights, axis=0, keepdims=True))
        grad_probs = nt(values, grad_rows)
        mean = jnp.sum(probs * grad_probs, axis=0, keepdims=True)
        grad_scores = (probs * (grad_probs - mean)).astype(LOW)
        grad_values = nn(probs.astype(LOW), grad_rows)
        grad_keys = nn(grad_scores, query_rows) * scale
        grad_queries = tn(grad_scores, keys) * scale
        for h in range(GROUP):
            to = (g * GROUP + h) * 128
            grad_query[:, to : to + 128] = turn_back(
                grad_queries[h * BRANCH : (h + 1) * BRANCH], cosine[...], sine[...]
            ).astype(LOW)
        for column, grad in ((128 * g, grad_keys), (KEY_WIDTH + 128 * g, grad_values)):
            columns = slice(column, column + 128)
            source_grad[0:TRUNK, columns] += grad[0:TRUNK]
            source_grad[pl.ds(at, BRANCH), columns] += grad[TRUNK : TRUNK + BRANCH]
            own_grad[:, columns] = grad[TRUNK + BRANCH :]


def attention_back(info, queries, own, partner, grads, cosine, sine):
    chunked = pl.BlockSpec((BRANCH, D), lambda i: (i, 0))
    pair = (TOK_DEV, 2 * KEY_WIDTH)
    return pl.pallas_call(
        attention_back_kernel,
        grid=(CHUNKS,),
        out_shape=(
            jax.ShapeDtypeStruct((TOK_DEV, D), LOW),
            jax.ShapeDtypeStruct(pair, WIDE),
            jax.ShapeDtypeStruct(pair, WIDE),
        ),
        in_specs=[
            SMEM,
            chunked,
            whole(pair),
            whole(pair),
            chunked,
            pl.BlockSpec((BRANCH, 128), lambda i: (i, 0)),
            pl.BlockSpec((BRANCH, 128), lambda i: (i, 0)),
        ],
        out_specs=(
            chunked,
            pl.BlockSpec((BRANCH, 2 * KEY_WIDTH), lambda i: (i, 0)),
            whole(pair),
        ),
        scratch_shapes=[pltpu.VMEM(pair, LOW)],
        compiler_params=params(),
        cost_estimate=LITTLE,
        name="tree_attention_back",
    )(info, queries, own, partner, grads, cosine, sine)


def out_kernel(info, heads, tokens, gain, *rest):
    count = len(rest) - 4
    refs, (residual, normed, weight, sem) = rest[:count], rest[count:]

    @pl.when(pl.program_id(0) == 0)
    def _():
        copies = weight_copies(info, refs, weight, sem, D // QUARTERS + 128, D // QUARTERS)
        run_all(copies)
        wait_all(copies)

    at = pl.ds(pl.multiple_of(pl.program_id(0) * STEP, STEP), STEP)
    residual[:, at] = tokens[:, at].astype(WIDE) + nn(heads[...], weight[:, at])

    @pl.when(pl.program_id(0) == pl.num_programs(0) - 1)
    def _():
        values = residual[...]
        factor = lax.rsqrt(jnp.mean(values * values, axis=-1, keepdims=True) + EPSILON)
        normed[...] = (values * factor * gain[...]).astype(LOW)


def out_projection(info, heads, tokens, gain, refs):
    full = (TOK_DEV, D)
    return pl.pallas_call(
        out_kernel,
        grid=(D // STEP,),
        out_shape=(jax.ShapeDtypeStruct(full, WIDE), jax.ShapeDtypeStruct(full, LOW)),
        in_specs=[SMEM, whole(full), whole(full), whole((1, D))] + [ANY] * len(refs),
        out_specs=(whole(full), whole(full)),
        scratch_shapes=[pltpu.VMEM((D, D), LOW), pltpu.SemaphoreType.DMA],
        compiler_params=params(),
        cost_estimate=LITTLE,
        name="out_projection",
    )(info, heads, tokens, gain, *refs)


def hits_of(routes, ids):
    hit = ids == routes[0, 0:1]
    for k in range(1, TOP):
        hit = jnp.logical_or(hit, ids == routes[0, k : k + 1])
    return hit


def tables_kernel(capacity, local, total, info, routes, chosen_out, place_out, earlier):
    @pl.when(pl.program_id(0) == 0)
    def _():
        one = lax.broadcasted_iota(jnp.int32, (TOK_DEV, TOK_DEV), 0)
        two = lax.broadcasted_iota(jnp.int32, (TOK_DEV, TOK_DEV), 1)
        earlier[...] = jnp.where(one < two, 1.0, 0.0).astype(LOW)

    ids = lax.broadcasted_iota(jnp.int32, (total, TOK_DEV), 0)
    hit = hits_of(routes, ids)
    rank = nn(jnp.where(hit, 1.0, 0.0).astype(LOW), earlier[...])
    place = jnp.where(hit, rank, -1.0)
    spots = lax.broadcasted_iota(jnp.int32, (capacity, TOK_DEV), 0).astype(WIDE)
    place_out[0] = jnp.full(place_out.shape[1:], -1.0, WIDE)
    for e in range(local):
        mine = ids == info[0] * local + e
        place_row = jnp.sum(jnp.where(mine, place, 0.0), axis=0, keepdims=True)
        place_out[0, e : e + 1] = place_row
        chosen_out[0, e * capacity : (e + 1) * capacity] = jnp.where(
            spots == place_row, 1.0, 0.0
        ).astype(LOW)


def tables(info, routes, capacity, local, total):
    count = routes.shape[0]
    return pl.pallas_call(
        functools.partial(tables_kernel, capacity, local, total),
        grid=(count,),
        in_specs=[SMEM, pl.BlockSpec((1, TOP, TOK_DEV), lambda i: (i, 0, 0))],
        out_specs=[
            pl.BlockSpec((1, local * capacity, TOK_DEV), lambda i: (i, 0, 0)),
            pl.BlockSpec((1, 8, TOK_DEV), lambda i: (i, 0, 0)),
        ],
        scratch_shapes=[pltpu.VMEM((TOK_DEV, TOK_DEV), LOW)],
        out_shape=[
            jax.ShapeDtypeStruct((count, local * capacity, TOK_DEV), LOW),
            jax.ShapeDtypeStruct((count, 8, TOK_DEV), WIDE),
        ],
        compiler_params=params(),
        cost_estimate=LITTLE,
        name="route_tables",
    )(info, routes)


def pick_kernel(local, count, chosen, *rest):
    blocks, outs = rest[:count], rest[count : count + local]
    picks, block_in, out_block, sem_in, sem_out = rest[count + local :]
    capacity = outs[0].shape[1]
    copies = [
        (
            pltpu.make_async_copy(chosen.at[q], picks.at[q], sem_in.at[q, 0]),
            pltpu.make_async_copy(blocks[q], block_in.at[q], sem_in.at[q, 1]),
        )
        for q in range(count)
    ]
    for pair in copies:
        run_all(pair)
    sent = []
    for q in range(count):
        wait_all(copies[q])
        out_block[q] = nn(picks[q], block_in[q]).astype(LOW)
        for e in range(local):
            copy = pltpu.make_async_copy(
                out_block.at[q, pl.ds(e * capacity, capacity)], outs[e].at[q], sem_out.at[q, e]
            )
            copy.start()
            sent.append(copy)
    wait_all(sent)


def pick_rows(chosen, blocks, local):
    count, height, _ = chosen.shape
    return pl.pallas_call(
        functools.partial(pick_kernel, local, count),
        in_specs=[ANY] * (1 + count),
        out_specs=[ANY] * local,
        out_shape=[jax.ShapeDtypeStruct((count, height // local, D), LOW)] * local,
        scratch_shapes=[
            pltpu.VMEM((count, height, TOK_DEV), LOW),
            pltpu.VMEM((count, TOK_DEV, D), LOW),
            pltpu.VMEM((count, height, D), LOW),
            pltpu.SemaphoreType.DMA((count, 2)),
            pltpu.SemaphoreType.DMA((count, local)),
        ],
        compiler_params=params(),
        cost_estimate=LITTLE,
        name="pick_rows",
    )(chosen, *blocks)


def dispatch_kernel(local, info, rows, chosen, routes, router, *rest):
    outs, logits = rest[2 * local : 4 * local], rest[-1]
    total = router.shape[1]
    step = pl.program_id(0)
    block = rows[...]
    rows_of = nn(chosen[0], block).astype(LOW)
    capacity = outs[0].shape[1]
    for e in range(local):
        outs[e][0] = rows_of[e * capacity : (e + 1) * capacity]
    part = nn(block, router[...])

    @pl.when(step == 0)
    def _():
        logits[...] = part

    @pl.when(step > 0)
    def _():
        logits[...] += part

    @pl.when(step == pl.num_programs(0) - 1)
    def _():
        values = logits[...].T
        ids = lax.broadcasted_iota(jnp.int32, (total, TOK_DEV), 0)
        weights = jnp.exp(values - jnp.max(values, axis=0, keepdims=True))
        hit = hits_of(routes, ids)
        share = weights / jnp.sum(jnp.where(hit, weights, 0.0), axis=0, keepdims=True)
        for e in range(local):
            mine = ids == info[0] * local + e
            share_row = jnp.sum(jnp.where(mine, share, 0.0), axis=0, keepdims=True)
            picked = chosen[0, e * capacity : (e + 1) * capacity].astype(WIDE)
            outs[local + e][0] = jnp.sum(picked * share_row, axis=1, keepdims=True)


def dispatch(at, info, rows, chosen, routes, router, local, earlier):
    count, height, _ = chosen.shape
    capacity = height // local
    total = router.shape[1]
    wide = D
    out_shape = [jax.ShapeDtypeStruct((count, capacity, D), LOW)] * local + [
        jax.ShapeDtypeStruct((count, capacity, 1), WIDE)
    ] * local
    if earlier is None:
        earlier = [jnp.zeros((8, 128), shape.dtype) for shape in out_shape]
        aliases = {}
    else:
        aliases = {5 + i: i for i in range(len(out_shape))}
    return pl.pallas_call(
        functools.partial(dispatch_kernel, local),
        grid=(D // wide,),
        in_specs=[
            SMEM,
            pl.BlockSpec((TOK_DEV, wide), lambda i: (0, i)),
            pl.BlockSpec((1, height, TOK_DEV), lambda i: (at, 0, 0)),
            pl.BlockSpec((1, TOP, TOK_DEV), lambda i: (at, 0, 0)),
            pl.BlockSpec((wide, total), lambda i: (i, 0)),
        ]
        + [ANY] * len(out_shape),
        out_specs=[pl.BlockSpec((1, capacity, wide), lambda i: (at, 0, i))] * local
        + [pl.BlockSpec((1, capacity, 1), lambda i: (at, 0, 0))] * local,
        scratch_shapes=[pltpu.VMEM((TOK_DEV, total), WIDE)],
        out_shape=out_shape,
        input_output_aliases=aliases,
        compiler_params=params(),
        cost_estimate=LITTLE,
        name="dispatch",
    )(info, rows, chosen, routes, router, *earlier)


def spread_kernel(local, place, *rest):
    dots, out = rest[:local], rest[local]
    spots = lax.broadcasted_iota(jnp.int32, (dots[0].shape[1], TOK_DEV), 0).astype(WIDE)
    for e in range(local):
        chosen = spots == place[0, e : e + 1]
        out[0, e : e + 1] = jnp.sum(jnp.where(chosen, dots[e][0], 0.0), axis=0, keepdims=True)


def spread(place, dots):
    count, capacity, _ = dots[0].shape
    local = len(dots)
    return pl.pallas_call(
        functools.partial(spread_kernel, local),
        grid=(count,),
        out_shape=jax.ShapeDtypeStruct((count, local, TOK_DEV), WIDE),
        in_specs=[pl.BlockSpec((1, 8, TOK_DEV), lambda i: (i, 0, 0))]
        + [pl.BlockSpec((1, capacity, 1), lambda i: (i, 0, 0))] * local,
        out_specs=pl.BlockSpec((1, local, TOK_DEV), lambda i: (i, 0, 0)),
        compiler_params=params(),
        cost_estimate=LITTLE,
        name="spread",
    )(place, *dots)


def expert_kernel(slots, info, rows, grads, shares, *rest):
    refs, (out_rows, back_rows, grad_rows, acts, dots, weight, sem) = rest[:-7], rest[-7:]
    part = weight.shape[1] // slots

    @pl.when(pl.program_id(0) == 0)
    def _():
        def copies(ref, slot):
            return [
                pltpu.make_async_copy(
                    ref.at[pl.ds(which * part, part)],
                    weight.at[which, pl.ds(pl.multiple_of(slot * part, part), part)],
                    sem,
                )
                for which in range(3)
            ]

        if len(refs) == 1:
            for slot in range(slots):
                run_all(copies(refs[0].at[slot], slot))
            for slot in range(slots):
                wait_all(copies(refs[0].at[slot], slot))
        else:
            block, second, above, below, far = refs
            low_end = info[2] == 0
            end = jnp.logical_or(low_end, info[2] == 3)
            run_all(copies(block, info[2]))
            run_all(copies(second, info[3]))

            @pl.when(low_end)
            def _():
                run_all(copies(above, info[4]))

            @pl.when(jnp.logical_not(low_end))
            def _():
                run_all(copies(below, info[4]))

            @pl.when(end)
            def _():
                run_all(copies(far, info[5]))

            @pl.when(jnp.logical_not(end))
            def _():
                run_all(copies(above, info[5]))

            for slot in range(slots):
                wait_all(copies(block, slot))

    row_block = rows[...]
    share = shares[...]
    grad_float = grads[...].astype(WIDE)
    grad_low = (share * grad_float).astype(LOW)
    grad_rows[...] = grad_low
    gate_act = nt(row_block, weight[0])
    upward = nt(row_block, weight[1])
    sigmoid = 1.0 / (1.0 + jnp.exp(-gate_act))
    silu = gate_act * sigmoid
    hidden = (silu * upward).astype(LOW)
    expert_out = nn(hidden, weight[2]).astype(LOW).astype(WIDE)
    out_rows[...] = (share * expert_out).astype(LOW)
    dots[...] = jnp.sum(grad_float * expert_out, axis=1, keepdims=True)
    grad_hidden = nt(grad_low, weight[2])
    grad_gate = (grad_hidden * upward * sigmoid * (1.0 + gate_act * (1.0 - sigmoid))).astype(LOW)
    grad_up = (grad_hidden * silu).astype(LOW)
    back_rows[...] = (nn(grad_gate, weight[0]) + nn(grad_up, weight[1])).astype(LOW)
    for which, act in enumerate((grad_gate, grad_up, hidden)):
        turned = act.T
        for slot in range(slots):
            acts[slot, which * part : (which + 1) * part] = turned[
                slot * part : (slot + 1) * part
            ]


EXPERT_ROWS = 256


def expert(info, rows, grads, shares, refs, slots):
    height = rows.shape[0]
    part = refs[0].shape[-2] // 3
    wide_block = pl.BlockSpec((EXPERT_ROWS, D), lambda i: (i, 0))
    thin_block = pl.BlockSpec((EXPERT_ROWS, 1), lambda i: (i, 0))
    return pl.pallas_call(
        functools.partial(expert_kernel, slots),
        grid=(height // EXPERT_ROWS,),
        out_shape=[jax.ShapeDtypeStruct((height, D), LOW)] * 3
        + [
            jax.ShapeDtypeStruct((slots, 3 * part, height), LOW),
            jax.ShapeDtypeStruct((height, 1), WIDE),
        ],
        in_specs=[SMEM, wide_block, wide_block, thin_block] + [ANY] * len(refs),
        out_specs=[wide_block] * 3
        + [pl.BlockSpec((slots, 3 * part, EXPERT_ROWS), lambda i: (0, 0, i)), thin_block],
        scratch_shapes=[pltpu.VMEM((3, slots * part, D), LOW), pltpu.SemaphoreType.DMA],
        compiler_params=params(),
        cost_estimate=LITTLE,
        name="expert",
    )(info, rows, grads, shares, *refs)


def expert_grads_kernel(acts, rows, grads, out):
    slots, height, _ = acts.shape
    part = height // 3
    for slot in range(slots):
        out[slot, : 2 * part] = nn(acts[slot, : 2 * part], rows[...]).astype(LOW)
        out[slot, 2 * part :] = nn(acts[slot, 2 * part :], grads[...]).astype(LOW)


def expert_grads(acts, rows, grads):
    slots, part, height = acts.shape
    strip = pl.BlockSpec((height, 256), lambda i: (0, i))
    return pl.pallas_call(
        expert_grads_kernel,
        grid=(D // 256,),
        out_shape=jax.ShapeDtypeStruct((slots, part, D), LOW),
        in_specs=[whole(acts.shape), strip, strip],
        out_specs=pl.BlockSpec((slots, part, 256), lambda i: (0, 0, i)),
        compiler_params=params(),
        cost_estimate=LITTLE,
        name="expert_gradients",
    )(acts, rows, grads)


SHARE_ROWS = 32


def combine_kernel(local, first, step, info, chosen, *rest):
    rows, dots, out = rest[:local], rest[local:-6], rest[-6]
    picks, rows_in, out_block, sem_in, sem_out = rest[-5:]
    number = out.shape[0]
    capacity = rows[0].shape[1]
    copies = []
    for n in range(number):
        q = first + step * n
        copies.append(
            [pltpu.make_async_copy(chosen.at[q], picks.at[n], sem_in.at[n, local])]
            + [
                pltpu.make_async_copy(
                    rows[e].at[q],
                    rows_in.at[n, pl.ds(e * capacity, capacity)],
                    sem_in.at[n, e],
                )
                for e in range(local)
            ]
        )
    for group in copies:
        run_all(group)
    sent = []
    for n in range(number):
        wait_all(copies[n])
        out_block[n, :TOK_DEV] = tn(picks[n], rows_in[n]).astype(LOW)
        if dots:
            row = lax.broadcasted_iota(jnp.int32, (SHARE_ROWS, D), 0)
            values = jnp.zeros((SHARE_ROWS, D), WIDE)
            for e in range(local):
                picked = picks[n, e * capacity : (e + 1) * capacity].astype(WIDE)
                share = picked * dots[e][first + step * n]
                high, low = split(jnp.sum(share, axis=0, keepdims=True))
                pieces = [high.astype(WIDE), low.astype(WIDE)]
                pieces.append(jnp.zeros((1, D - 2 * TOK_DEV), WIDE))
                line = jnp.concatenate(pieces, axis=1)
                values = jnp.where(row == info[0] * local + e, line, values)
            out_block[n, TOK_DEV:] = values.astype(LOW)
        copy = pltpu.make_async_copy(out_block.at[n], out.at[n], sem_out.at[n])
        copy.start()
        sent.append(copy)
    wait_all(sent)


def combine(info, chosen, rows, first, step, dots=()):
    count, capacity, _ = rows[0].shape
    local = len(rows)
    number = (count - first + step - 1) // step
    height = TOK_DEV + (SHARE_ROWS if dots else 0)
    return pl.pallas_call(
        functools.partial(combine_kernel, local, first, step),
        out_shape=jax.ShapeDtypeStruct((number, height, D), LOW),
        in_specs=[SMEM, ANY]
        + [ANY] * local
        + [pl.BlockSpec(memory_space=pltpu.VMEM)] * len(dots),
        out_specs=ANY,
        scratch_shapes=[
            pltpu.VMEM((number, local * capacity, TOK_DEV), LOW),
            pltpu.VMEM((number, local * capacity, D), LOW),
            pltpu.VMEM((number, height, D), LOW),
            pltpu.SemaphoreType.DMA((number, local + 1)),
            pltpu.SemaphoreType.DMA((number,)),
        ],
        compiler_params=params(),
        cost_estimate=LITTLE,
        name="combine",
    )(info, chosen, *rows, *dots)


def chip_adds_kernel(keep, got, send_x, send_y, near_x, near_y, one, two, sem_in, sem_out):
    half = send_x.shape[1]
    copies = [
        (
            pltpu.make_async_copy(keep.at[i], one.at[i], sem_in.at[i, 0]),
            pltpu.make_async_copy(got.at[i], two.at[i], sem_in.at[i, 1]),
        )
        for i in range(4)
    ]
    for pair in copies:
        run_all(pair)
    sent = []
    for i in range(4):
        wait_all(copies[i])
        one[i] = (one[i].astype(WIDE) + two[i].astype(WIDE)).astype(LOW)
        upper = (near_x, send_x)[i % 2].at[i // 2]
        lower = (near_y, send_y)[i // 2].at[i % 2]
        for part, to in enumerate((upper, lower)):
            copy = pltpu.make_async_copy(
                one.at[i, pl.ds(part * half, half)], to, sem_out.at[i, part]
            )
            copy.start()
            sent.append(copy)
    wait_all(sent)


def chip_adds(keep, got):
    _, height, width = keep.shape
    shape = jax.ShapeDtypeStruct((2, height // 2, width), LOW)
    return pl.pallas_call(
        chip_adds_kernel,
        out_shape=(shape,) * 4,
        in_specs=[ANY, ANY],
        out_specs=(ANY,) * 4,
        scratch_shapes=[
            pltpu.VMEM(keep.shape, LOW),
            pltpu.VMEM(keep.shape, LOW),
            pltpu.SemaphoreType.DMA((4, 2)),
            pltpu.SemaphoreType.DMA((4, 2)),
        ],
        compiler_params=params(),
        cost_estimate=LITTLE,
        name="chip_sums",
    )(keep, got)


def corner_adds_kernel(near_x, got_x, near_y, got_y, send_y, send_x):
    send_y[...] = (near_x[0].astype(WIDE) + got_x[0].astype(WIDE)).astype(LOW)
    send_x[...] = (near_y[0].astype(WIDE) + got_y[0].astype(WIDE)).astype(LOW)


def corner_adds(near_x, got_x, near_y, got_y):
    _, half, width = near_x.shape
    rows = half
    block = pl.BlockSpec((1, rows, width), lambda i: (1, i, 0))
    out = pl.BlockSpec((rows, width), lambda i: (i, 0))
    return pl.pallas_call(
        corner_adds_kernel,
        grid=(half // rows,),
        out_shape=(jax.ShapeDtypeStruct((half, width), LOW),) * 2,
        in_specs=[block] * 4,
        out_specs=(out, out),
        compiler_params=params(),
        cost_estimate=LITTLE,
        name="corner_sums",
    )(near_x, got_x, near_y, got_y)


def split(values):
    high = values.astype(LOW)
    return high, (values - high.astype(WIDE)).astype(LOW)


def norm_back(values, gain, grad):
    factor = lax.rsqrt(jnp.mean(values * values, axis=-1, keepdims=True) + EPSILON)
    scaled = gain * grad
    mean = jnp.mean(values * scaled, axis=-1, keepdims=True)
    grad_values = factor * scaled - values * (factor * factor * factor * mean)
    grad_gain = jnp.sum(grad * values * factor, axis=0, keepdims=True)
    return grad_values, grad_gain


def router_back(logits, routes, grad_shares):
    ids = lax.broadcasted_iota(jnp.int32, logits.shape, 0)
    hit = ids == routes[0:1]
    for k in range(1, TOP):
        hit = jnp.logical_or(hit, ids == routes[k : k + 1])
    weights = jnp.exp(logits - jnp.max(logits, axis=0, keepdims=True))
    probs = weights / jnp.sum(weights, axis=0, keepdims=True)
    chosen = jnp.sum(jnp.where(hit, probs, 0.0), axis=0, keepdims=True)
    grads = jnp.where(hit, grad_shares, 0.0)
    mean = jnp.sum(probs * grads, axis=0, keepdims=True) / chosen
    grad_probs = jnp.where(hit, (grads - mean) / chosen, 0.0)
    return probs * (grad_probs - jnp.sum(probs * grad_probs, axis=0, keepdims=True))


def branch_back_kernel(
    parts, info, residual, normed, cotangent, routes, router, gain, *rest
):
    sums, rest = rest[:parts], rest[parts:]
    experts = router.shape[0]
    count = len(rest) - 7
    refs = rest[:count]
    grad_residual, grad_branch, grad_heads, grad_gain, grad_router, weight, sem = rest[count:]

    @pl.when(pl.program_id(0) == 0)
    def _():
        copies = weight_copies(info, refs, weight, sem, D // QUARTERS + 128, D // QUARTERS)
        run_all(copies)
        logits = nt(router[...], normed[...])
        if parts == 2:
            back_sum, grad_shares = sums[0][...], sums[1][...]
        else:
            values = [
                (ref[0] if len(ref.shape) == 3 else ref[...]).astype(WIDE) for ref in sums
            ]
            upper = values[0] + values[1] + values[2]
            lower = values[3] + values[4] + values[5]
            last = lower.shape[0] - SHARE_ROWS
            shares = lower[last : last + experts]
            grad_shares = shares[:, :TOK_DEV] + shares[:, TOK_DEV : 2 * TOK_DEV]
            back_sum = jnp.concatenate([upper, lower[:last]], axis=0)
        high, low = split(router_back(logits, routes[...], grad_shares))
        grad_router[...] = nn(high, normed[...]) + nn(low, normed[...])
        grad_normed = tn(high, router[...]) + tn(low, router[...])
        grad_normed += back_sum
        grad_values, gain_grad = norm_back(residual[...], gain[...], grad_normed)
        grad_gain[...] = gain_grad
        total = cotangent[...].astype(WIDE) + grad_values
        grad_residual[...] = total
        grad_branch[...] = total.astype(LOW)
        wait_all(copies)

    at = pl.ds(pl.multiple_of(pl.program_id(0) * STEP, STEP), STEP)
    grad_heads[...] = nt(grad_branch[...], weight[at, :]).astype(LOW)


def branch_back(info, residual, normed, sums, cotangent, routes, router, gain, refs):
    full = (TOK_DEV, D)
    total = router.shape[0]
    return pl.pallas_call(
        functools.partial(branch_back_kernel, len(sums)),
        grid=(D // STEP,),
        out_shape=(
            jax.ShapeDtypeStruct(full, WIDE),
            jax.ShapeDtypeStruct(full, LOW),
            jax.ShapeDtypeStruct(full, LOW),
            jax.ShapeDtypeStruct((1, D), WIDE),
            jax.ShapeDtypeStruct((total, D), WIDE),
        ),
        in_specs=[SMEM]
        + [whole(full)] * 3
        + [whole((TOP, TOK_DEV)), whole((total, D)), whole((1, D))]
        + [whole(part.shape if part.ndim == 2 else (1,) + part.shape[1:]) for part in sums]
        + [ANY] * len(refs),
        out_specs=(
            whole(full),
            whole(full),
            pl.BlockSpec((TOK_DEV, STEP), lambda i: (0, i)),
            whole((1, D)),
            whole((total, D)),
        ),
        scratch_shapes=[pltpu.VMEM((D, D), LOW), pltpu.SemaphoreType.DMA],
        compiler_params=params(),
        cost_estimate=LITTLE,
        name="experts_norm_back",
    )(info, residual, normed, cotangent, routes, router, gain, *sums, *refs)


def join_grads_kernel(info, own_grad, source_grad, arrived, cosine, sine, out):
    half = HEAD_DIM // 2
    first = lax.broadcasted_iota(jnp.int32, (TOK_DEV, HEAD_DIM), 1) < half
    leaves = info[1] == 0

    def total(column):
        columns = slice(column, column + 128)
        extra = source_grad[:, columns] + arrived[:, columns].astype(WIDE)
        return own_grad[:, columns] + jnp.where(leaves, 0.0, extra)

    for g in range(KV_HEADS):
        key = turn_back(total(128 * g), cosine[...], sine[...])
        value = total(KEY_WIDTH + 128 * g)
        out[:, 256 * g : 256 * g + 128] = jnp.where(
            first, key, pltpu.roll(value, half, 1)
        ).astype(LOW)
        out[:, 256 * g + 128 : 256 * g + 256] = jnp.where(
            first, pltpu.roll(key, half, 1), value
        ).astype(LOW)


def join_grads(info, own_grad, source_grad, arrived, cosine, sine):
    vmem = pl.BlockSpec(memory_space=pltpu.VMEM)
    return pl.pallas_call(
        join_grads_kernel,
        out_shape=jax.ShapeDtypeStruct((TOK_DEV, 2 * KEY_WIDTH), LOW),
        in_specs=[SMEM] + [vmem] * 5,
        out_specs=vmem,
        compiler_params=params(),
        cost_estimate=LITTLE,
        name="join_key_value_gradients",
    )(info, own_grad, source_grad, arrived, cosine, sine)


def normed_grad_kernel(info, grad_query, *rest):
    refs, (out, weight, sem) = rest[:-3], rest[-3:]

    @pl.when(pl.program_id(0) == 0)
    def _():
        copies = weight_copies(info, refs, weight, sem, 0, D // QUARTERS)
        run_all(copies)
        wait_all(copies)

    at = pl.ds(pl.multiple_of(pl.program_id(0) * STEP, STEP), STEP)
    out[...] = nt(grad_query[...], weight[at, :])


def normed_grad(info, grad_query, refs):
    return pl.pallas_call(
        normed_grad_kernel,
        grid=(D // STEP,),
        out_shape=jax.ShapeDtypeStruct((TOK_DEV, D), WIDE),
        in_specs=[SMEM, whole((TOK_DEV, D))] + [ANY] * len(refs),
        out_specs=pl.BlockSpec((TOK_DEV, STEP), lambda i: (0, i)),
        scratch_shapes=[pltpu.VMEM((D, D), LOW), pltpu.SemaphoreType.DMA],
        compiler_params=params(),
        cost_estimate=LITTLE,
        name="normed_gradient",
    )(info, grad_query, *refs)


def token_back_kernel(info, query_part, grad_pair, tokens, grad_residual, gain, *rest):
    refs, (out, grad_gain, weight, sem) = rest[:-4], rest[-4:]
    copies = weight_copies(info, refs, weight, sem, D // QUARTERS, 128)
    run_all(copies)
    wait_all(copies)
    grad_normed = query_part[...] + nt(grad_pair[...], weight[...])
    grad_values, gain_grad = norm_back(tokens[...].astype(WIDE), gain[...], grad_normed)
    grad_gain[...] = gain_grad
    out[...] = (grad_residual[...] + grad_values).astype(LOW)


def token_back(info, query_part, grad_pair, tokens, grad_residual, gain, refs):
    full = (TOK_DEV, D)
    vmem = pl.BlockSpec(memory_space=pltpu.VMEM)
    return pl.pallas_call(
        token_back_kernel,
        out_shape=(jax.ShapeDtypeStruct(full, LOW), jax.ShapeDtypeStruct((1, D), WIDE)),
        in_specs=[SMEM] + [vmem] * 5 + [ANY] * len(refs),
        out_specs=(vmem, vmem),
        scratch_shapes=[
            pltpu.VMEM((D, 2 * KEY_WIDTH), LOW),
            pltpu.SemaphoreType.DMA,
        ],
        compiler_params=params(),
        cost_estimate=LITTLE,
        name="token_gradient",
    )(info, query_part, grad_pair, tokens, grad_residual, gain, *refs)


def weight_grads_kernel(parts, info, *rest):
    ins, (keep, send) = rest[:-2], rest[-2:]
    depth = D // 8
    core = info[0] & 1
    chip = pl.program_id(0) ^ (info[0] >> 1)
    for strip_at, grads_at, start, width in parts:
        low = tn(ins[strip_at][...], ins[grads_at][...]).astype(LOW)
        columns = slice(start, start + width)
        for slot in range(QUARTERS):
            for j in range(QUARTERS):

                @pl.when(info[2 + slot] == j)
                def _():
                    piece = low[:, j * width : (j + 1) * width]
                    upper, lower = piece[:depth], piece[depth:]
                    keep[0, slot, :depth, columns] = jnp.where(core == 0, upper, lower)
                    send[0, slot, :depth, columns] = jnp.where(core == 0, lower, upper)

    if keep.shape[2] > depth:
        extra = ins[-1]
        for slot in range(QUARTERS):
            to = info[2 + slot]
            keep[0, slot, depth:] = extra[(chip * 2 + core) * QUARTERS + to]
            send[0, slot, depth:] = extra[(chip * 2 + 1 - core) * QUARTERS + to]


def weight_grads(info, strips, grads, parts, extra=None):
    depth = D // 8
    strip = pl.BlockSpec((TOK_DEV, 2 * depth), lambda i, info: (0, i ^ (info[0] >> 1)))
    more = [] if extra is None else [extra]
    width = sum(part[3] for part in parts)
    shape = (4, QUARTERS, depth + EXTRA * len(more), width)
    out = pl.BlockSpec((1,) + shape[1:], lambda i, info: (i, 0, 0, 0))
    return pl.pallas_call(
        functools.partial(weight_grads_kernel, parts),
        grid_spec=pltpu.PrefetchScalarGridSpec(
            num_scalar_prefetch=1,
            grid=(4,),
            in_specs=[strip] * len(strips)
            + [
                pl.BlockSpec(a.shape, lambda i, info, n=a.ndim: (0,) * n)
                for a in (*grads, *more)
            ],
            out_specs=(out, out),
        ),
        out_shape=(jax.ShapeDtypeStruct(shape, LOW),) * 2,
        compiler_params=params(),
        cost_estimate=LITTLE,
        name="weight_gradients",
    )(info, *strips, *grads, *more)


def last_sums_kernel(part, info, own, *rest):
    arrived, (query_out, key_out, value_out, out_out, extra_out) = rest[:-5], rest[-5:]
    total = own[...].astype(WIDE)
    for ref in arrived[:-1]:
        total += ref[...].astype(WIDE)
    end = jnp.logical_or(info[2] == 0, info[2] == 3)
    total += jnp.where(end, arrived[-1][...].astype(WIDE), 0.0)
    depth = query_out.shape[0]
    quarter = query_out.shape[1]
    query_out[...] = total[:depth, :quarter]
    pair = total[:depth, 2 * quarter :].T
    key_out[...] = pair[:part]
    value_out[...] = pair[part:]
    out_out[...] = total[:depth, quarter : 2 * quarter]
    extra_out[...] = total[depth:]


def last_sums(info, own, arrived, depth, part):
    height, width = own.shape
    quarter = D // QUARTERS
    vmem = pl.BlockSpec(memory_space=pltpu.VMEM)
    return pl.pallas_call(
        functools.partial(last_sums_kernel, part),
        out_shape=(
            jax.ShapeDtypeStruct((depth, quarter), WIDE),
            jax.ShapeDtypeStruct((part, depth), WIDE),
            jax.ShapeDtypeStruct((part, depth), WIDE),
            jax.ShapeDtypeStruct((depth, quarter), WIDE),
            jax.ShapeDtypeStruct((height - depth, width), WIDE),
        ),
        in_specs=[SMEM] + [vmem] * (1 + len(arrived)),
        out_specs=(vmem,) * 5,
        compiler_params=params(),
        cost_estimate=LITTLE,
        name="last_sums",
    )(info, own, *arrived)


def expert_sums_kernel(count, *rest):
    blocks, outs = rest[:count], rest[count:]
    part = outs[0].shape[1]
    for e in range(count):
        for which, out in enumerate(outs):
            out[e] = blocks[e][which * part : (which + 1) * part].astype(WIDE)


def expert_sums(blocks):
    count, part = len(blocks), blocks[0].shape[0] // 3
    vmem = pl.BlockSpec(memory_space=pltpu.VMEM)
    return pl.pallas_call(
        functools.partial(expert_sums_kernel, count),
        out_shape=(jax.ShapeDtypeStruct((count, part, D), WIDE),) * 3,
        in_specs=[vmem] * count,
        out_specs=(vmem,) * 3,
        compiler_params=params(),
        cost_estimate=LITTLE,
        name="expert_sums",
    )(*blocks)


def position_of(token_index):
    branch_place = TRUNK + (token_index - TRUNK) % BRANCH
    leaf_place = TRUNK + BRANCH + (token_index - TOK_DEV) % BRANCH
    return jnp.where(
        token_index < TRUNK, token_index, jnp.where(token_index < TOK_DEV, branch_place, leaf_place)
    )


def rotary_tables(positions):
    half_dim = HEAD_DIM // 2
    frequency = ROPE_BASE ** (-jnp.arange(half_dim, dtype=jnp.float32) / half_dim)
    angles = positions.astype(jnp.float32)[:, None] * frequency[None, :]
    cosine, sine = (jnp.cos(angles), jnp.sin(angles))
    return (
        jnp.concatenate([cosine, cosine], axis=1),
        jnp.concatenate([-sine, sine], axis=1),
    )


def after(values, *earlier):
    return lax.optimization_barrier((values, earlier))[0]


def fast_mesh():
    return lax.axis_size("rows") == 8 and lax.axis_size("cols") == 4


SLOT_SHARD = ((0, 2, 1, 3), (1, 3, 0, 2), (2, 0, 1, 3), (3, 1, 2, 0))
UP = [(0, 1), (1, 2), (2, 3)]
DOWN = [(1, 0), (2, 1), (3, 2)]
FAR = [(0, 3), (3, 0)]


def send_near(block):
    return lax.ppermute(block, "cols", DOWN), lax.ppermute(block, "cols", UP)


def send_far(block):
    return lax.ppermute(block, "cols", FAR)


def send_over(block):
    return lax.ppermute(block, "cols", [(0, 2), (1, 3), (2, 0), (3, 1)])


def send_second(block, near):
    place = lax.axis_index("cols")
    above, below = near
    payload = jnp.where(place == 1, above, jnp.where(place == 2, below, block))
    return lax.ppermute(payload, "cols", [(3, 1), (1, 0), (0, 2), (2, 3)])


def slot_list(block, near, second, far):
    place = lax.axis_index("cols")
    above, below = near
    end = (place == 0) | (place == 3)
    return [
        block,
        second,
        jnp.where(place == 0, above, below),
        jnp.where(end, far, above),
    ]


def send_slots(slots):
    place = lax.axis_index("cols")
    _, second, third, fourth = slots
    relay = lax.ppermute(second, "cols", [(1, 3), (0, 1), (2, 0), (3, 2)])
    relayed = relay.astype(WIDE)
    upward_load = (
        jnp.where(place == 0, third, fourth).astype(WIDE) + jnp.where(place == 1, relayed, 0.0)
    ).astype(LOW)
    downward_load = (third.astype(WIDE) + jnp.where(place == 2, relayed, 0.0)).astype(LOW)
    arrived = (
        lax.ppermute(upward_load, "cols", UP),
        lax.ppermute(downward_load, "cols", DOWN),
        send_far(after(fourth, upward_load, downward_load)),
        relay,
    )
    return arrived, upward_load


def flip(block, bit):
    count = lax.axis_size("rows")
    return lax.ppermute(block, "rows", [(i, i ^ bit) for i in range(count)])


def add_low(one, two):
    return (one.astype(WIDE) + two.astype(WIDE)).astype(LOW)


def chips_second(near_x, near_y, got_x, got_y):
    for_y, for_x = corner_adds(near_x, got_x, near_y, got_y)
    return (near_x, got_x, flip(for_y, 4), near_y, got_y, flip(for_x, 2))


def turn_corner(beside, across):
    half = beside.shape[0] // 2
    return jnp.concatenate([flip(beside[:half], 4), flip(across[half:], 2)], axis=0)


def send_chips(sums):
    return flip(sums[0], 2), flip(sums[1], 4)


def sum_parts(parts):
    wide = [(a[0] if a.ndim == 3 else a).astype(WIDE) for a in parts]
    if len(wide) == 1:
        return wide[0]
    return jnp.concatenate([wide[0] + wide[1] + wide[2], wide[3] + wide[4] + wide[5]], axis=0)


def on_device(
    tokens,
    query_weight,
    key_weight,
    value_weight,
    out_weight,
    router_weight,
    attention_gain,
    experts_gain,
    gate_weight,
    upward_weight,
    down_weight,
    routes,
    leaf_parent,
    cotangent,
):
    row_count = lax.axis_size("rows")
    col_count = lax.axis_size("cols")
    row_place = lax.axis_index("rows")
    col_place = lax.axis_index("cols")
    fast = fast_mesh()
    parity = lax.rem(col_place, 2)
    tree_id = lax.div(row_place * col_count + col_place, 2)
    parent_row = lax.dynamic_slice_in_dim(leaf_parent, tree_id, 1, 0)[0]
    depth, query_part = query_weight.shape
    key_part = key_weight.shape[1]
    router_part = router_weight.shape[1]
    gain_part = attention_gain.shape[0]
    expert_total = router_part * col_count
    local_experts = gate_weight.shape[0]
    capacity = TOK_DEV * TOP // expert_total * 5 // 4

    shards = (
        jnp.asarray(SLOT_SHARD, jnp.int32)[col_place]
        if fast
        else jnp.arange(4, dtype=jnp.int32)
    )
    branch_rows = jnp.where(parity == 0, TRUNK + BRANCH * parent_row, TRUNK)
    info = jnp.concatenate(
        [jnp.stack([row_place, parity]), shards, branch_rows, jnp.zeros((2,), jnp.int32)]
    ).astype(jnp.int32)

    packed = jnp.concatenate([query_weight, key_weight, value_weight, out_weight], axis=1)
    local_index = (1 - parity) * TOK_DEV + jnp.arange(TOK_DEV, dtype=jnp.int32)
    cosine, sine = rotary_tables(position_of(local_index))
    shard_blocks = [
        jnp.concatenate(
            [gate_weight[expert].T, upward_weight[expert].T, down_weight[expert]], axis=0
        )
        for expert in range(local_experts)
    ]
    expert_refs = []
    if fast:
        wide = packed.shape[1]
        gains = jnp.concatenate([attention_gain, experts_gain])[None, :]
        packed = jnp.concatenate(
            [
                packed,
                jnp.pad(router_weight.T, ((0, 0), (0, wide - depth))),
                jnp.pad(gains, ((0, 0), (0, wide - 2 * gain_part))),
                jnp.pad(routes.T.astype(LOW), ((0, 0), (0, wide - TOK_DEV))),
                jnp.zeros((EXTRA - router_part - 1 - TOP, wide), LOW),
            ],
            axis=0,
        )
        packed_near = send_near(packed)
        packed_far = send_far(packed)
        packed_second = send_over(packed)
        first_block = after(shard_blocks[0], *packed_near)
        first_near = send_near(first_block)
        first_far = send_far(first_block)
        own = jnp.stack(slot_list(packed, packed_near, packed_second, packed_far))
        own = after(own, info, cosine, sine)
        beside, across = flip(own, 2), flip(own, 4)
        own_in = flip(own, 1)
        beside, across = after((beside, across), own_in, *first_near)
        corner = [flip(beside[:2], 4), flip(across[2:], 2)]
        pair_in = flip(jnp.concatenate([beside, across], axis=0), 1)
        corner_in = [flip(piece, 1) for piece in corner]
        grad_in = after(cotangent, *corner)
        grad_flips = [flip(grad_in, 2), flip(grad_in, 4)]
        pieces = [own, own_in, beside, across, *corner, pair_in, *corner_in]
        at = depth + router_part + 1
        near_slots = [own, own_in, beside, pair_in, across, pair_in[4:], corner[0], corner_in[0]]
        routes_all = jnp.stack([part[0, at : at + TOP, :TOK_DEV] for part in near_slots])
        routes_all = routes_all.astype(jnp.int32)
        chosen, place_rows = tables(info, routes_all, capacity, local_experts, expert_total)
        query_refs = pair_refs = out_refs = pieces
        extra_rows = extras(info, pieces)
        router_all = extra_rows[:, :router_part, :depth]
        attention_scale = extra_rows[:, router_part, :gain_part]
        experts_scale = extra_rows[:, router_part, gain_part : 2 * gain_part]
    else:
        packed_all = lax.all_gather(lax.all_gather(packed, "cols", axis=0), "rows", axis=0)

        def unpack(start, width):
            part = packed_all[..., start : start + width]
            return jnp.swapaxes(part, 1, 2).reshape(row_count * depth, col_count * width)

        key_at = query_part
        query_refs = [unpack(0, query_part)]
        pair_refs = [
            jnp.concatenate(
                [
                    unpack(key_at, key_part).reshape(D, QUARTERS, -1),
                    unpack(key_at + key_part, key_part).reshape(D, QUARTERS, -1),
                ],
                axis=2,
            ).reshape(D, -1)
        ]
        out_refs = [unpack(key_at + 2 * key_part, query_part)]
        routes_all = lax.all_gather(routes.T, "rows", axis=0)
        chosen, place_rows = tables(info, routes_all, capacity, local_experts, expert_total)
        axes = ("rows", "cols")
        router_all = jnp.swapaxes(lax.all_gather(router_weight, axes, axis=0), 1, 2)
        attention_scale = lax.all_gather(attention_gain, axes, axis=0)
        experts_scale = lax.all_gather(experts_gain, axes, axis=0)

    attention_scale = attention_scale.reshape(1, D).astype(WIDE)
    experts_scale = experts_scale.reshape(1, D).astype(WIDE)
    router_rows = jnp.transpose(
        router_all.reshape(row_count, col_count, router_part, depth), (1, 2, 0, 3)
    ).reshape(expert_total, D)
    router_cols = router_rows.T
    tokens_in = after(tokens, first_far, chosen) if fast else tokens
    normed, own_pair = key_value(info, tokens_in, attention_scale, cosine, sine, pair_refs)
    pairs = [(i + 1, i) for i in range(0, col_count, 2)]
    partner = lax.ppermute(own_pair, "cols", pairs)
    if fast:
        own_grad_in = flip(grad_in, 1)
        normed_in = after(normed, own_grad_in)
    else:
        normed_in = normed
    queries = query(info, normed_in, cosine, sine, query_refs)
    if fast:
        first_second = send_second(after(first_block, partner, queries), first_near)
        expert_refs.append([first_block, first_second, *first_near, first_far])
    if fast:
        grad_flips = after(grad_flips, queries)
        grad_corner = turn_corner(*grad_flips)
    heads = attention(info, queries, own_pair, partner)
    if fast:
        grad_near = [*grad_flips, grad_corner]
        grad_blocks = [cotangent, own_grad_in]
        grad_blocks += [block for one in grad_near for block in (one, flip(one, 1))]
        heads = after(heads, grad_corner, grad_blocks[3], grad_blocks[5])
    else:
        grad_all = lax.all_gather(cotangent, "rows", axis=0)
        grad_blocks = [grad_all[q] for q in range(row_count)]
    residual, normed_two = out_projection(info, heads, tokens, experts_scale, out_refs)

    if fast:
        beside, across = flip(normed_two, 2), flip(normed_two, 4)
        beside_in = flip(normed_two, 1)
        later_block = after(shard_blocks[1], first_second, normed_two)
        expert_refs.append([lax.all_gather(later_block, "cols", axis=0)])
    else:
        rows_all = lax.all_gather(normed_two, "rows", axis=0)
        expert_refs = [[lax.all_gather(block, "cols", axis=0)] for block in shard_blocks]
    grad_rows = pick_rows(chosen, grad_blocks, local_experts)

    def place_block(q, block, picked):
        return dispatch(
            q, info, block, chosen, routes_all, router_cols, local_experts, picked
        )

    if fast:
        half = TOK_DEV // 2
        picked = place_block(0, normed_two, None)
        picked = place_block(1, beside_in, after(picked, *grad_rows))
        beside, across = after((beside, across), picked)
        corner = [flip(beside[:half], 4), flip(across[half:], 2)]
        picked = place_block(2, beside, picked)
        picked = place_block(4, across, picked)
        beside_in = flip(beside, 1)
        across_in = flip(across, 1)
        picked = place_block(3, beside_in, picked)
        picked = place_block(5, across_in, picked)
        corner = jnp.concatenate(after(corner, picked), axis=0)
        corner_in = flip(corner, 1)
        picked = place_block(6, corner, picked)
        picked = place_block(7, corner_in, picked)
    else:
        picked = None
        for q in range(row_count):
            picked = place_block(q, rows_all[q], picked)
    height = row_count * capacity
    token_rows = [a.reshape(height, D) for a in picked[:local_experts]]
    grad_rows = [a.reshape(height, D) for a in grad_rows]
    share_rows = [a.reshape(height, 1) for a in picked[local_experts:]]

    out_rows, back_rows, gate_dots, reduced = ([], [], [], [])
    for e in range(local_experts):
        rows_in = after(token_rows[e], *reduced_in) if e else token_rows[e]
        out_row, back_row, grad_row, acts, dots = expert(
            info, rows_in, grad_rows[e], share_rows[e], expert_refs[e], col_count
        )
        out_rows.append(out_row.reshape(row_count, capacity, D))
        back_rows.append(back_row.reshape(row_count, capacity, D))
        gate_dots.append(dots.reshape(row_count, capacity, 1))
        if fast and e == 1:
            got = flip(combine(info, chosen, back_rows, 1, 2, gate_dots), 1)
            back_keep = combine(info, chosen, back_rows, 0, 2, gate_dots)
            for_x, for_y, near_x, near_y = chip_adds(back_keep, got)
            acts = after(acts, for_x)
            back_flips = send_chips((for_x, for_y))
        slots = expert_grads(acts, token_rows[e], grad_row)
        reduced_in = (slots,)
        if e and fast:
            out_got = flip(combine(info, chosen, out_rows, 1, 2), 1)
            out_keep = combine(info, chosen, out_rows, 0, 2)
            back_flips = after(back_flips, slots, out_keep)
            back_parts = chips_second(near_x, near_y, *back_flips)
        else:
            reduced.append(lax.psum_scatter(slots, "cols", scatter_dimension=0, tiled=False))

    if fast:
        out_first = chip_adds(out_keep, out_got)
        back_parts = after(back_parts, out_first[0])
    else:
        spread_dots = spread(place_rows, gate_dots)
        grad_shares = lax.all_to_all(spread_dots, "rows", split_axis=0, concat_axis=0, tiled=True)

        def summed(rows):
            part = combine(info, chosen, rows, 0, 1)
            return lax.psum_scatter(part, "rows", scatter_dimension=0).astype(WIDE)

        back_parts = (summed(back_rows), grad_shares.reshape(expert_total, TOK_DEV))
        mixture = (summed(out_rows),)

    grad_residual, grad_branch, grad_heads, experts_gain_grad, router_grad = branch_back(
        info,
        residual,
        normed_two,
        back_parts,
        cotangent,
        routes.T,
        router_rows,
        experts_scale,
        out_refs,
    )
    if fast:
        out_flips = send_chips(after(out_first[:2], back_parts[2], back_parts[5]))
        slots = after(slots, reduced[0], back_parts[2])
        reduced.append(lax.psum_scatter(slots, "cols", scatter_dimension=0, tiled=False))
        main_width = 2 * query_part
        router_parts = jnp.transpose(
            router_grad.astype(LOW).reshape(col_count, router_part, row_count, depth),
            (2, 0, 1, 3),
        ).reshape(row_count * col_count, router_part, depth)
        gain_rows = experts_gain_grad.astype(LOW).reshape(row_count * col_count, 1, gain_part)
        extra = jnp.concatenate(
            [
                jnp.pad(router_parts, ((0, 0), (0, 0), (0, main_width - depth))),
                jnp.pad(gain_rows, ((0, 0), (0, 0), (0, main_width - gain_part))),
                jnp.zeros((row_count * col_count, EXTRA - router_part - 1, main_width), LOW),
            ],
            axis=1,
        )
    grad_query, own_grad, source_grad = attention_back(
        info, queries, own_pair, partner, grad_heads, cosine, sine
    )
    arrived = lax.ppermute(source_grad.astype(LOW), "cols", [(j, i) for i, j in pairs])
    if fast:
        parts = ((0, 2, 0, query_part), (1, 3, query_part, query_part))
        grad_branch = after(grad_branch, *out_flips)
        keep, send = weight_grads(
            info, [normed, heads], [grad_query, grad_branch], parts, extra
        )
        flat = (4, col_count * (depth + EXTRA), main_width)
        sent = flip(send, 1)
        main_first = chip_adds(keep.reshape(flat), sent.reshape(flat))
        main_chips = send_chips(main_first[:2])
        query_back = normed_grad(info, after(grad_query, main_first[0]), query_refs)
        main_chips = after(main_chips, query_back)
        main_x, main_y = main_first[2:]
        for_y, for_x = corner_adds(main_x, main_chips[0], main_y, main_chips[1])
        main_parts = (main_x, main_chips[0], flip(for_y, 4), main_y, main_chips[1])
        main_parts += (flip(for_x, 2),)
        arrived = after(arrived, for_y)
    else:
        query_back = normed_grad(info, grad_query, query_refs)
    grad_pair = join_grads(info, own_grad, source_grad, arrived, cosine, sine)
    if fast:
        keep, send = weight_grads(info, [normed], [grad_pair], ((0, 1, 0, 2 * key_part),))
        flat = (4, col_count * depth, 2 * key_part)
        pair_first = chip_adds(keep.reshape(flat), flip(send, 1).reshape(flat))
        pair_chips = send_chips(pair_first[:2])
        grad_pair = after(grad_pair, pair_first[0])
    tokens_grad, attention_gain_grad = token_back(
        info, query_back, grad_pair, tokens, grad_residual, attention_scale, pair_refs
    )

    if fast:
        pair_parts = chips_second(*pair_first[2:], *after(pair_chips, tokens_grad))
    gate_grad, upward_grad, down_grad = expert_sums(reduced)
    gate_grad, upward_grad = jnp.swapaxes(gate_grad, 1, 2), jnp.swapaxes(upward_grad, 1, 2)
    if fast:
        main_parts = after(main_parts, tokens_grad)
        slots = sum_parts(main_parts).reshape(col_count, depth + EXTRA, main_width)
        pairs_sum = sum_parts(pair_parts).reshape(col_count, depth, 2 * key_part)
        width = query_part + 2 * key_part
        weights_own = jnp.stack([own[i, :depth, :width].astype(WIDE) for i in range(4)])
        gain_sums = jnp.sum(
            weights_own[..., :query_part] * slots[:, :depth, :query_part], axis=(0, 2)
        ) + jnp.sum(weights_own[..., query_part:] * pairs_sum, axis=(0, 2))
        own_gains = lax.dynamic_slice_in_dim(attention_scale[0], row_place * depth, depth, 0)
        gain_sums = (gain_sums / own_gains).reshape(col_count, 1, gain_part)
        gain_sums = jnp.pad(
            jnp.take(gain_sums, shards, axis=0),
            (
                (0, 0),
                (depth + router_part + 1, EXTRA - router_part - 2),
                (0, main_width - gain_part),
            ),
        )
        pairs_sum = jnp.pad(pairs_sum, ((0, 0), (0, EXTRA), (0, 0)))
        slots = jnp.concatenate([slots + gain_sums, pairs_sum], axis=2).astype(LOW)
        slots = after(slots, reduced[1])

        arrived, sent_load = send_slots(slots)
        near_x, near_y = out_first[2:]
        mixture = chips_second(near_x, near_y, *after(out_flips, sent_load))
        layer_output = (residual + sum_parts(mixture)).astype(LOW)
        earlier = (gate_grad, upward_grad, down_grad, layer_output)
        query_sum, key_sum, value_sum, out_sum, extra_sum = last_sums(
            info, slots[0], after(arrived, *earlier), depth, key_part
        )
        key_sum, value_sum = key_sum.T, value_sum.T
        router_sum = extra_sum[:router_part, :depth].T
        experts_gain_sum = extra_sum[router_part, :gain_part]
        attention_gain_sum = extra_sum[router_part + 1, :gain_part]
    else:
        layer_output = (residual + sum_parts(mixture)).astype(LOW)
        full_grads = [
            tn(normed, grad_query),
            *jnp.moveaxis(tn(normed, grad_pair).reshape(D, QUARTERS, 2, -1), 2, 0),
            tn(heads, grad_branch),
        ]
        packed_grad = jnp.concatenate(
            [
                grad.astype(LOW).reshape(row_count, depth, col_count, -1)
                for grad in full_grads
            ],
            axis=3,
        )
        row_sums = lax.psum_scatter(packed_grad, "rows", scatter_dimension=0)
        sums = lax.psum_scatter(row_sums, "cols", scatter_dimension=1).astype(WIDE)
        key_at = query_part
        value_at = key_at + key_part
        out_at = value_at + key_part
        query_sum, out_sum = sums[:, :key_at], sums[:, out_at:]
        key_sum, value_sum = sums[:, key_at:value_at], sums[:, value_at:out_at]
        small_grads = jnp.concatenate(
            [
                attention_gain_grad.reshape(-1, gain_part),
                experts_gain_grad.reshape(-1, gain_part),
                jnp.transpose(
                    router_grad.reshape(col_count, router_part, row_count, depth), (2, 0, 3, 1)
                ).reshape(row_count * col_count, depth * router_part),
            ],
            axis=1,
        )
        small_grads = small_grads.reshape(row_count, -1)
        small_grads = lax.all_to_all(small_grads, "rows", split_axis=0, concat_axis=0, tiled=True)
        small_grads = jnp.sum(small_grads, axis=0).reshape(col_count, -1)
        small_grads = lax.all_to_all(small_grads, "cols", split_axis=0, concat_axis=0, tiled=True)
        small_sums = jnp.sum(small_grads, axis=0)
        attention_gain_sum = small_sums[:gain_part]
        experts_gain_sum = small_sums[gain_part : 2 * gain_part]
        router_sum = small_sums[2 * gain_part :].reshape(depth, router_part)

    return (
        layer_output,
        tokens_grad,
        query_sum,
        key_sum,
        value_sum,
        out_sum,
        router_sum,
        attention_gain_sum,
        experts_gain_sum,
        gate_grad,
        upward_grad,
        down_grad,
    )


def solution(mesh):
    in_specs = (
        P(("rows", "cols"), None),
        P("rows", "cols"),
        P("rows", "cols"),
        P("rows", "cols"),
        P("rows", "cols"),
        P("rows", "cols"),
        P(("rows", "cols")),
        P(("rows", "cols")),
        P("rows", None, "cols"),
        P("rows", None, "cols"),
        P("rows", "cols", None),
        P(("rows", "cols"), None),
        P(),
        P(("rows", "cols"), None),
    )
    out_specs = (
        P(("rows", "cols"), None),
        P(("rows", "cols"), None),
        P("rows", "cols"),
        P("rows", "cols"),
        P("rows", "cols"),
        P("rows", "cols"),
        P("rows", "cols"),
        P(("rows", "cols")),
        P(("rows", "cols")),
        P("rows", None, "cols"),
        P("rows", None, "cols"),
        P("rows", "cols", None),
    )
    return jax.shard_map(
        on_device, mesh=mesh, in_specs=in_specs, out_specs=out_specs, check_vma=False
    )
```

```python
import functools

import jax
import jax.numpy as jnp
from jax import lax
from jax.experimental import pallas as pl
from jax.experimental.pallas import tpu as pltpu
from jax.sharding import PartitionSpec as P

D = 1536
HEADS = 12
KV_HEADS = 2
HEAD_DIM = 128
TOP = 4
TOK_DEV = 512
BRANCHES = 4
LEAVES = 8
TRUNK = 256
BRANCH = 64

EPSILON = 1e-06
ROPE_BASE = 10000.0
MASKED = -1e30
LOW = jnp.bfloat16
WIDE = jnp.float32
KEY_WIDTH = KV_HEADS * HEAD_DIM
GROUP = HEADS // KV_HEADS
QUARTERS = 4
VMEM_LIMIT = 56 * 1024 * 1024

ANY = pl.BlockSpec(memory_space=pl.ANY)
SMEM = pl.BlockSpec(memory_space=pltpu.SMEM)


def nn(one, two):
    return lax.dot_general(one, two, (((1,), (0,)), ((), ())), preferred_element_type=WIDE)


def nt(one, two):
    return lax.dot_general(one, two, (((1,), (1,)), ((), ())), preferred_element_type=WIDE)


def tn(one, two):
    return lax.dot_general(one, two, (((0,), (0,)), ((), ())), preferred_element_type=WIDE)


def whole(shape):
    return pl.BlockSpec(shape, lambda *_: (0,) * len(shape))


LITTLE = pl.CostEstimate(flops=1, bytes_accessed=1, transcendentals=0)


def params():
    return pltpu.CompilerParams(vmem_limit_bytes=VMEM_LIMIT)


def turn(values, cosine, sine):
    return values * cosine + pltpu.roll(values, HEAD_DIM // 2, 1) * sine


def turn_back(values, cosine, sine):
    return values * cosine - pltpu.roll(values, HEAD_DIM // 2, 1) * sine


SLOTS = range(4)
PIECES = (
    tuple((0, slot) for slot in SLOTS),
    tuple((1, slot) for slot in SLOTS),
    tuple((2, slot) for slot in SLOTS),
    tuple((4, slot) for slot in SLOTS),
    ((6, 0), (6, 1)),
    ((6, 2), (6, 3)),
    tuple((flip_bits, slot) for flip_bits in (3, 5) for slot in SLOTS),
    ((7, 0), (7, 1)),
    ((7, 2), (7, 3)),
)
EXTRA = 16


STEP = 768


def weight_copies(info, refs, target, sem, start, width):
    if len(refs) == 1:
        return [pltpu.make_async_copy(refs[0], target, sem)]
    depth = refs[0].shape[1] - EXTRA
    copies = []
    for ref, parts in zip(refs, PIECES):
        for at, (flip_bits, slot) in enumerate(parts):
            row = pl.multiple_of((info[0] ^ flip_bits) * depth, depth)
            col = pl.multiple_of(info[2 + slot] * width, 128)
            copies.append(
                pltpu.make_async_copy(
                    ref.at[at, pl.ds(0, depth), pl.ds(start, width)],
                    target.at[pl.ds(row, depth), pl.ds(col, width)],
                    sem,
                )
            )
    return copies


def extras_kernel(info, *rest):
    refs, (out, sem) = rest[:-2], rest[-2:]
    depth = refs[0].shape[1] - EXTRA
    copies = []
    for ref, parts in zip(refs, PIECES):
        for at, (flip_bits, slot) in enumerate(parts):
            to = (info[0] ^ flip_bits) * QUARTERS + info[2 + slot]
            copies.append(pltpu.make_async_copy(ref.at[at, pl.ds(depth, EXTRA)], out.at[to], sem))
    run_all(copies)
    wait_all(copies)


def extras(info, refs):
    return pl.pallas_call(
        extras_kernel,
        out_shape=jax.ShapeDtypeStruct((8 * QUARTERS, EXTRA, refs[0].shape[2]), LOW),
        in_specs=[SMEM] + [ANY] * len(refs),
        out_specs=pl.BlockSpec(memory_space=pltpu.VMEM),
        scratch_shapes=[pltpu.SemaphoreType.DMA],
        compiler_params=params(),
        cost_estimate=LITTLE,
        name="extra_rows",
    )(info, *refs)


def run_all(copies):
    for copy in copies:
        copy.start()


def wait_all(copies):
    for copy in copies:
        copy.wait()


def key_value_kernel(info, tokens, gain, cosine, sine, *rest):
    count = len(rest) - 4
    refs, (normed, out, weight, sem) = rest[:count], rest[count:]
    copies = weight_copies(info, refs, weight, sem, D // QUARTERS, 128)
    run_all(copies)
    values = tokens[...].astype(WIDE)
    factor = lax.rsqrt(jnp.mean(values * values, axis=-1, keepdims=True) + EPSILON)
    low = (values * factor * gain[...]).astype(LOW)
    normed[...] = low
    wait_all(copies)
    both = nn(low, weight[...])
    half = HEAD_DIM // 2
    first = lax.broadcasted_iota(jnp.int32, (TOK_DEV, HEAD_DIM), 1) < half
    for g in range(KV_HEADS):
        one = both[:, 256 * g : 256 * g + 128]
        two = both[:, 256 * g + 128 : 256 * g + 256]
        key = jnp.where(first, one, pltpu.roll(two, half, 1))
        value = jnp.where(first, pltpu.roll(one, half, 1), two)
        out[:, 128 * g : 128 * g + 128] = turn(key, cosine[...], sine[...]).astype(LOW)
        out[:, KEY_WIDTH + 128 * g : KEY_WIDTH + 128 * g + 128] = value.astype(LOW)


def key_value(info, tokens, gain, cosine, sine, refs):
    return pl.pallas_call(
        key_value_kernel,
        out_shape=(
            jax.ShapeDtypeStruct((TOK_DEV, D), LOW),
            jax.ShapeDtypeStruct((TOK_DEV, 2 * KEY_WIDTH), LOW),
        ),
        in_specs=[SMEM] + [pl.BlockSpec(memory_space=pltpu.VMEM)] * 4 + [ANY] * len(refs),
        out_specs=(pl.BlockSpec(memory_space=pltpu.VMEM),) * 2,
        scratch_shapes=[pltpu.VMEM((D, 2 * KEY_WIDTH), LOW), pltpu.SemaphoreType.DMA],
        compiler_params=params(),
        cost_estimate=LITTLE,
        name="norm_key_value",
    )(info, tokens, gain, cosine, sine, *refs)


def query_kernel(info, normed, cosine, sine, *rest):
    count = len(rest) - 3
    refs, (out, weight, sem) = rest[:count], rest[count:]

    @pl.when(pl.program_id(0) == 0)
    def _():
        copies = weight_copies(info, refs, weight, sem, 0, D // QUARTERS)
        run_all(copies)
        wait_all(copies)

    at = pl.multiple_of(pl.program_id(0) * STEP, STEP)
    lin = nn(normed[...], weight[:, pl.ds(at, STEP)])
    for h in range(STEP // HEAD_DIM):
        out[:, 128 * h : 128 * h + 128] = turn(
            lin[:, 128 * h : 128 * h + 128], cosine[...], sine[...]
        ).astype(LOW)


def query(info, normed, cosine, sine, refs):
    return pl.pallas_call(
        query_kernel,
        grid=(D // STEP,),
        out_shape=jax.ShapeDtypeStruct((TOK_DEV, D), LOW),
        in_specs=[SMEM, whole((TOK_DEV, D)), whole((TOK_DEV, 128)), whole((TOK_DEV, 128))]
        + [ANY] * len(refs),
        out_specs=pl.BlockSpec((TOK_DEV, STEP), lambda i: (0, i)),
        scratch_shapes=[pltpu.VMEM((D, D), LOW), pltpu.SemaphoreType.DMA],
        compiler_params=params(),
        cost_estimate=LITTLE,
        name="query_projection",
    )(info, normed, cosine, sine, *refs)


KEYS = TRUNK + 2 * BRANCH
CHUNKS = TOK_DEV // BRANCH


def chunk_keys(info, source, own, column, chunk):
    at = pl.multiple_of(info[6 + chunk], BRANCH)
    rows = pl.multiple_of(chunk * BRANCH, BRANCH)
    columns = slice(column, column + HEAD_DIM)
    return jnp.concatenate(
        [
            source[0:TRUNK, columns],
            source[pl.ds(at, BRANCH), columns],
            own[pl.ds(rows, BRANCH), columns],
        ],
        axis=0,
    )


def chunk_allowed(info, chunk, query_axis, shape):
    query_row = lax.broadcasted_iota(jnp.int32, shape, query_axis) & (BRANCH - 1)
    key = lax.broadcasted_iota(jnp.int32, shape, 1 - query_axis)
    leaves = info[1] == 0
    trunk = jnp.logical_and(jnp.logical_not(leaves), chunk < TRUNK // BRANCH)
    limit = jnp.where(trunk, chunk * BRANCH + query_row, TRUNK - 1)
    branch_limit = jnp.where(leaves, TRUNK + BRANCH - 1, 0)
    own_limit = jnp.where(trunk, 0, query_row + TRUNK + BRANCH)
    top = jnp.where(key < TRUNK, limit, jnp.where(key < TRUNK + BRANCH, branch_limit, own_limit))
    return key <= top


def group_rows(ref, g):
    first = g * GROUP
    return jnp.concatenate(
        [ref[:, 128 * h : 128 * h + 128] for h in range(first, first + GROUP)], axis=0
    )


def keep_source(info, partner, own, source):
    @pl.when(pl.program_id(0) == 0)
    def _():
        @pl.when(info[1] == 0)
        def _():
            source[...] = partner[...]

        @pl.when(info[1] != 0)
        def _():
            source[...] = own[...]


def attention_kernel(info, queries, own, partner, out, source):
    keep_source(info, partner, own, source)
    chunk = pl.program_id(0)
    rows = GROUP * BRANCH
    allowed = chunk_allowed(info, chunk, 0, (rows, KEYS))
    for g in range(KV_HEADS):
        keys = chunk_keys(info, source, own, 128 * g, chunk)
        values = chunk_keys(info, source, own, KEY_WIDTH + 128 * g, chunk)
        scores = nt(group_rows(queries, g), keys) * HEAD_DIM**-0.5
        scores = jnp.where(allowed, scores, MASKED)
        weights = jnp.exp(scores - jnp.max(scores, axis=1, keepdims=True))
        total = jnp.sum(weights, axis=1, keepdims=True)
        mixed = nn((weights * (1.0 / total)).astype(LOW), values).astype(LOW)
        for h in range(GROUP):
            at = (g * GROUP + h) * 128
            out[:, at : at + 128] = mixed[h * BRANCH : (h + 1) * BRANCH]


def attention(info, queries, own, partner):
    return pl.pallas_call(
        attention_kernel,
        grid=(CHUNKS,),
        out_shape=jax.ShapeDtypeStruct((TOK_DEV, D), LOW),
        in_specs=[
            SMEM,
            pl.BlockSpec((BRANCH, D), lambda i: (i, 0)),
            whole((TOK_DEV, 2 * KEY_WIDTH)),
            whole((TOK_DEV, 2 * KEY_WIDTH)),
        ],
        out_specs=pl.BlockSpec((BRANCH, D), lambda i: (i, 0)),
        scratch_shapes=[pltpu.VMEM((TOK_DEV, 2 * KEY_WIDTH), LOW)],
        compiler_params=params(),
        cost_estimate=LITTLE,
        name="tree_attention",
    )(info, queries, own, partner)


def attention_back_kernel(
    info, queries, own, partner, grads, cosine, sine, grad_query, own_grad, source_grad, source
):
    keep_source(info, partner, own, source)
    chunk = pl.program_id(0)

    @pl.when(chunk == 0)
    def _():
        source_grad[...] = jnp.zeros_like(source_grad)

    rows = GROUP * BRANCH
    scale = HEAD_DIM**-0.5
    allowed = chunk_allowed(info, chunk, 1, (KEYS, rows))
    at = pl.multiple_of(info[6 + chunk], BRANCH)
    for g in range(KV_HEADS):
        keys = chunk_keys(info, source, own, 128 * g, chunk)
        values = chunk_keys(info, source, own, KEY_WIDTH + 128 * g, chunk)
        query_rows = group_rows(queries, g)
        grad_rows = group_rows(grads, g)
        scores = jnp.where(allowed, nt(keys, query_rows) * scale, MASKED)
        weights = jnp.exp(scores - jnp.max(scores, axis=0, keepdims=True))
        probs = weights * (1.0 / jnp.sum(weights, axis=0, keepdims=True))
        grad_probs = nt(values, grad_rows)
        mean = jnp.sum(probs * grad_probs, axis=0, keepdims=True)
        grad_scores = (probs * (grad_probs - mean)).astype(LOW)
        grad_values = nn(probs.astype(LOW), grad_rows)
        grad_keys = nn(grad_scores, query_rows) * scale
        grad_queries = tn(grad_scores, keys) * scale
        for h in range(GROUP):
            to = (g * GROUP + h) * 128
            grad_query[:, to : to + 128] = turn_back(
                grad_queries[h * BRANCH : (h + 1) * BRANCH], cosine[...], sine[...]
            ).astype(LOW)
        for column, grad in ((128 * g, grad_keys), (KEY_WIDTH + 128 * g, grad_values)):
            columns = slice(column, column + 128)
            source_grad[0:TRUNK, columns] += grad[0:TRUNK]
            source_grad[pl.ds(at, BRANCH), columns] += grad[TRUNK : TRUNK + BRANCH]
            own_grad[:, columns] = grad[TRUNK + BRANCH :]


def attention_back(info, queries, own, partner, grads, cosine, sine):
    chunked = pl.BlockSpec((BRANCH, D), lambda i: (i, 0))
    pair = (TOK_DEV, 2 * KEY_WIDTH)
    return pl.pallas_call(
        attention_back_kernel,
        grid=(CHUNKS,),
        out_shape=(
            jax.ShapeDtypeStruct((TOK_DEV, D), LOW),
            jax.ShapeDtypeStruct(pair, WIDE),
            jax.ShapeDtypeStruct(pair, WIDE),
        ),
        in_specs=[
            SMEM,
            chunked,
            whole(pair),
            whole(pair),
            chunked,
            pl.BlockSpec((BRANCH, 128), lambda i: (i, 0)),
            pl.BlockSpec((BRANCH, 128), lambda i: (i, 0)),
        ],
        out_specs=(
            chunked,
            pl.BlockSpec((BRANCH, 2 * KEY_WIDTH), lambda i: (i, 0)),
            whole(pair),
        ),
        scratch_shapes=[pltpu.VMEM(pair, LOW)],
        compiler_params=params(),
        cost_estimate=LITTLE,
        name="tree_attention_back",
    )(info, queries, own, partner, grads, cosine, sine)


def out_kernel(info, heads, tokens, gain, *rest):
    count = len(rest) - 4
    refs, (residual, normed, weight, sem) = rest[:count], rest[count:]

    @pl.when(pl.program_id(0) == 0)
    def _():
        copies = weight_copies(info, refs, weight, sem, D // QUARTERS + 128, D // QUARTERS)
        run_all(copies)
        wait_all(copies)

    at = pl.ds(pl.multiple_of(pl.program_id(0) * STEP, STEP), STEP)
    residual[:, at] = tokens[:, at].astype(WIDE) + nn(heads[...], weight[:, at])

    @pl.when(pl.program_id(0) == pl.num_programs(0) - 1)
    def _():
        values = residual[...]
        factor = lax.rsqrt(jnp.mean(values * values, axis=-1, keepdims=True) + EPSILON)
        normed[...] = (values * factor * gain[...]).astype(LOW)


def out_projection(info, heads, tokens, gain, refs):
    full = (TOK_DEV, D)
    return pl.pallas_call(
        out_kernel,
        grid=(D // STEP,),
        out_shape=(jax.ShapeDtypeStruct(full, WIDE), jax.ShapeDtypeStruct(full, LOW)),
        in_specs=[SMEM, whole(full), whole(full), whole((1, D))] + [ANY] * len(refs),
        out_specs=(whole(full), whole(full)),
        scratch_shapes=[pltpu.VMEM((D, D), LOW), pltpu.SemaphoreType.DMA],
        compiler_params=params(),
        cost_estimate=LITTLE,
        name="out_projection",
    )(info, heads, tokens, gain, *refs)


def hits_of(routes, ids):
    hit = ids == routes[0, 0:1]
    for k in range(1, TOP):
        hit = jnp.logical_or(hit, ids == routes[0, k : k + 1])
    return hit


def tables_kernel(capacity, local, total, info, routes, chosen_out, place_out, earlier):
    @pl.when(pl.program_id(0) == 0)
    def _():
        one = lax.broadcasted_iota(jnp.int32, (TOK_DEV, TOK_DEV), 0)
        two = lax.broadcasted_iota(jnp.int32, (TOK_DEV, TOK_DEV), 1)
        earlier[...] = jnp.where(one < two, 1.0, 0.0).astype(LOW)

    ids = lax.broadcasted_iota(jnp.int32, (total, TOK_DEV), 0)
    hit = hits_of(routes, ids)
    rank = nn(jnp.where(hit, 1.0, 0.0).astype(LOW), earlier[...])
    place = jnp.where(hit, rank, -1.0)
    spots = lax.broadcasted_iota(jnp.int32, (capacity, TOK_DEV), 0).astype(WIDE)
    place_out[0] = jnp.full(place_out.shape[1:], -1.0, WIDE)
    for e in range(local):
        mine = ids == info[0] * local + e
        place_row = jnp.sum(jnp.where(mine, place, 0.0), axis=0, keepdims=True)
        place_out[0, e : e + 1] = place_row
        chosen_out[0, e * capacity : (e + 1) * capacity] = jnp.where(
            spots == place_row, 1.0, 0.0
        ).astype(LOW)


def tables(info, routes, capacity, local, total):
    count = routes.shape[0]
    return pl.pallas_call(
        functools.partial(tables_kernel, capacity, local, total),
        grid=(count,),
        in_specs=[SMEM, pl.BlockSpec((1, TOP, TOK_DEV), lambda i: (i, 0, 0))],
        out_specs=[
            pl.BlockSpec((1, local * capacity, TOK_DEV), lambda i: (i, 0, 0)),
            pl.BlockSpec((1, 8, TOK_DEV), lambda i: (i, 0, 0)),
        ],
        scratch_shapes=[pltpu.VMEM((TOK_DEV, TOK_DEV), LOW)],
        out_shape=[
            jax.ShapeDtypeStruct((count, local * capacity, TOK_DEV), LOW),
            jax.ShapeDtypeStruct((count, 8, TOK_DEV), WIDE),
        ],
        compiler_params=params(),
        cost_estimate=LITTLE,
        name="route_tables",
    )(info, routes)


def pick_kernel(local, count, chosen, *rest):
    blocks, outs = rest[:count], rest[count : count + local]
    picks, block_in, out_block, sem_in, sem_out = rest[count + local :]
    capacity = outs[0].shape[1]
    copies = [
        (
            pltpu.make_async_copy(chosen.at[q], picks.at[q], sem_in.at[q, 0]),
            pltpu.make_async_copy(blocks[q], block_in.at[q], sem_in.at[q, 1]),
        )
        for q in range(count)
    ]
    for pair in copies:
        run_all(pair)
    sent = []
    for q in range(count):
        wait_all(copies[q])
        out_block[q] = nn(picks[q], block_in[q]).astype(LOW)
        for e in range(local):
            copy = pltpu.make_async_copy(
                out_block.at[q, pl.ds(e * capacity, capacity)], outs[e].at[q], sem_out.at[q, e]
            )
            copy.start()
            sent.append(copy)
    wait_all(sent)


def pick_rows(chosen, blocks, local):
    count, height, _ = chosen.shape
    return pl.pallas_call(
        functools.partial(pick_kernel, local, count),
        in_specs=[ANY] * (1 + count),
        out_specs=[ANY] * local,
        out_shape=[jax.ShapeDtypeStruct((count, height // local, D), LOW)] * local,
        scratch_shapes=[
            pltpu.VMEM((count, height, TOK_DEV), LOW),
            pltpu.VMEM((count, TOK_DEV, D), LOW),
            pltpu.VMEM((count, height, D), LOW),
            pltpu.SemaphoreType.DMA((count, 2)),
            pltpu.SemaphoreType.DMA((count, local)),
        ],
        compiler_params=params(),
        cost_estimate=LITTLE,
        name="pick_rows",
    )(chosen, *blocks)


def dispatch_kernel(local, info, rows, chosen, routes, router, *rest):
    outs, logits = rest[2 * local : 4 * local], rest[-1]
    total = router.shape[1]
    step = pl.program_id(0)
    block = rows[...]
    rows_of = nn(chosen[0], block).astype(LOW)
    capacity = outs[0].shape[1]
    for e in range(local):
        outs[e][0] = rows_of[e * capacity : (e + 1) * capacity]
    part = nn(block, router[...])

    @pl.when(step == 0)
    def _():
        logits[...] = part

    @pl.when(step > 0)
    def _():
        logits[...] += part

    @pl.when(step == pl.num_programs(0) - 1)
    def _():
        values = logits[...].T
        ids = lax.broadcasted_iota(jnp.int32, (total, TOK_DEV), 0)
        weights = jnp.exp(values - jnp.max(values, axis=0, keepdims=True))
        hit = hits_of(routes, ids)
        share = weights / jnp.sum(jnp.where(hit, weights, 0.0), axis=0, keepdims=True)
        for e in range(local):
            mine = ids == info[0] * local + e
            share_row = jnp.sum(jnp.where(mine, share, 0.0), axis=0, keepdims=True)
            picked = chosen[0, e * capacity : (e + 1) * capacity].astype(WIDE)
            outs[local + e][0] = jnp.sum(picked * share_row, axis=1, keepdims=True)


def dispatch(at, info, rows, chosen, routes, router, local, earlier):
    count, height, _ = chosen.shape
    capacity = height // local
    total = router.shape[1]
    wide = D
    out_shape = [jax.ShapeDtypeStruct((count, capacity, D), LOW)] * local + [
        jax.ShapeDtypeStruct((count, capacity, 1), WIDE)
    ] * local
    if earlier is None:
        earlier = [jnp.zeros((8, 128), shape.dtype) for shape in out_shape]
        aliases = {}
    else:
        aliases = {5 + i: i for i in range(len(out_shape))}
    return pl.pallas_call(
        functools.partial(dispatch_kernel, local),
        grid=(D // wide,),
        in_specs=[
            SMEM,
            pl.BlockSpec((TOK_DEV, wide), lambda i: (0, i)),
            pl.BlockSpec((1, height, TOK_DEV), lambda i: (at, 0, 0)),
            pl.BlockSpec((1, TOP, TOK_DEV), lambda i: (at, 0, 0)),
            pl.BlockSpec((wide, total), lambda i: (i, 0)),
        ]
        + [ANY] * len(out_shape),
        out_specs=[pl.BlockSpec((1, capacity, wide), lambda i: (at, 0, i))] * local
        + [pl.BlockSpec((1, capacity, 1), lambda i: (at, 0, 0))] * local,
        scratch_shapes=[pltpu.VMEM((TOK_DEV, total), WIDE)],
        out_shape=out_shape,
        input_output_aliases=aliases,
        compiler_params=params(),
        cost_estimate=LITTLE,
        name="dispatch",
    )(info, rows, chosen, routes, router, *earlier)


def spread_kernel(local, place, *rest):
    dots, out = rest[:local], rest[local]
    spots = lax.broadcasted_iota(jnp.int32, (dots[0].shape[1], TOK_DEV), 0).astype(WIDE)
    for e in range(local):
        chosen = spots == place[0, e : e + 1]
        out[0, e : e + 1] = jnp.sum(jnp.where(chosen, dots[e][0], 0.0), axis=0, keepdims=True)


def spread(place, dots):
    count, capacity, _ = dots[0].shape
    local = len(dots)
    return pl.pallas_call(
        functools.partial(spread_kernel, local),
        grid=(count,),
        out_shape=jax.ShapeDtypeStruct((count, local, TOK_DEV), WIDE),
        in_specs=[pl.BlockSpec((1, 8, TOK_DEV), lambda i: (i, 0, 0))]
        + [pl.BlockSpec((1, capacity, 1), lambda i: (i, 0, 0))] * local,
        out_specs=pl.BlockSpec((1, local, TOK_DEV), lambda i: (i, 0, 0)),
        compiler_params=params(),
        cost_estimate=LITTLE,
        name="spread",
    )(place, *dots)


def expert_kernel(slots, info, rows, grads, shares, *rest):
    refs, (out_rows, back_rows, grad_rows, acts, dots, weight, sem) = rest[:-7], rest[-7:]
    part = weight.shape[1] // slots

    @pl.when(pl.program_id(0) == 0)
    def _():
        def copies(ref, slot):
            return [
                pltpu.make_async_copy(
                    ref.at[pl.ds(which * part, part)],
                    weight.at[which, pl.ds(pl.multiple_of(slot * part, part), part)],
                    sem,
                )
                for which in range(3)
            ]

        if len(refs) == 1:
            for slot in range(slots):
                run_all(copies(refs[0].at[slot], slot))
            for slot in range(slots):
                wait_all(copies(refs[0].at[slot], slot))
        else:
            block, second, above, below, far = refs
            low_end = info[2] == 0
            end = jnp.logical_or(low_end, info[2] == 3)
            run_all(copies(block, info[2]))
            run_all(copies(second, info[3]))

            @pl.when(low_end)
            def _():
                run_all(copies(above, info[4]))

            @pl.when(jnp.logical_not(low_end))
            def _():
                run_all(copies(below, info[4]))

            @pl.when(end)
            def _():
                run_all(copies(far, info[5]))

            @pl.when(jnp.logical_not(end))
            def _():
                run_all(copies(above, info[5]))

            for slot in range(slots):
                wait_all(copies(block, slot))

    row_block = rows[...]
    share = shares[...]
    grad_float = grads[...].astype(WIDE)
    grad_low = (share * grad_float).astype(LOW)
    grad_rows[...] = grad_low
    gate_act = nt(row_block, weight[0])
    upward = nt(row_block, weight[1])
    sigmoid = 1.0 / (1.0 + jnp.exp(-gate_act))
    silu = gate_act * sigmoid
    hidden = (silu * upward).astype(LOW)
    expert_out = nn(hidden, weight[2]).astype(LOW).astype(WIDE)
    out_rows[...] = (share * expert_out).astype(LOW)
    dots[...] = jnp.sum(grad_float * expert_out, axis=1, keepdims=True)
    grad_hidden = nt(grad_low, weight[2])
    grad_gate = (grad_hidden * upward * sigmoid * (1.0 + gate_act * (1.0 - sigmoid))).astype(LOW)
    grad_up = (grad_hidden * silu).astype(LOW)
    back_rows[...] = (nn(grad_gate, weight[0]) + nn(grad_up, weight[1])).astype(LOW)
    for which, act in enumerate((grad_gate, grad_up, hidden)):
        turned = act.T
        for slot in range(slots):
            acts[slot, which * part : (which + 1) * part] = turned[
                slot * part : (slot + 1) * part
            ]


EXPERT_ROWS = 256


def expert(info, rows, grads, shares, refs, slots):
    height = rows.shape[0]
    part = refs[0].shape[-2] // 3
    wide_block = pl.BlockSpec((EXPERT_ROWS, D), lambda i: (i, 0))
    thin_block = pl.BlockSpec((EXPERT_ROWS, 1), lambda i: (i, 0))
    return pl.pallas_call(
        functools.partial(expert_kernel, slots),
        grid=(height // EXPERT_ROWS,),
        out_shape=[jax.ShapeDtypeStruct((height, D), LOW)] * 3
        + [
            jax.ShapeDtypeStruct((slots, 3 * part, height), LOW),
            jax.ShapeDtypeStruct((height, 1), WIDE),
        ],
        in_specs=[SMEM, wide_block, wide_block, thin_block] + [ANY] * len(refs),
        out_specs=[wide_block] * 3
        + [pl.BlockSpec((slots, 3 * part, EXPERT_ROWS), lambda i: (0, 0, i)), thin_block],
        scratch_shapes=[pltpu.VMEM((3, slots * part, D), LOW), pltpu.SemaphoreType.DMA],
        compiler_params=params(),
        cost_estimate=LITTLE,
        name="expert",
    )(info, rows, grads, shares, *refs)


def expert_grads_kernel(acts, rows, grads, out):
    slots, height, _ = acts.shape
    part = height // 3
    for slot in range(slots):
        out[slot, : 2 * part] = nn(acts[slot, : 2 * part], rows[...]).astype(LOW)
        out[slot, 2 * part :] = nn(acts[slot, 2 * part :], grads[...]).astype(LOW)


def expert_grads(acts, rows, grads):
    slots, part, height = acts.shape
    strip = pl.BlockSpec((height, 256), lambda i: (0, i))
    return pl.pallas_call(
        expert_grads_kernel,
        grid=(D // 256,),
        out_shape=jax.ShapeDtypeStruct((slots, part, D), LOW),
        in_specs=[whole(acts.shape), strip, strip],
        out_specs=pl.BlockSpec((slots, part, 256), lambda i: (0, 0, i)),
        compiler_params=params(),
        cost_estimate=LITTLE,
        name="expert_gradients",
    )(acts, rows, grads)


SHARE_ROWS = 32


def combine_kernel(local, first, step, info, chosen, *rest):
    rows, dots, out = rest[:local], rest[local:-6], rest[-6]
    picks, rows_in, out_block, sem_in, sem_out = rest[-5:]
    number = out.shape[0]
    capacity = rows[0].shape[1]
    copies = []
    for n in range(number):
        q = first + step * n
        copies.append(
            [pltpu.make_async_copy(chosen.at[q], picks.at[n], sem_in.at[n, local])]
            + [
                pltpu.make_async_copy(
                    rows[e].at[q],
                    rows_in.at[n, pl.ds(e * capacity, capacity)],
                    sem_in.at[n, e],
                )
                for e in range(local)
            ]
        )
    for group in copies:
        run_all(group)
    sent = []
    for n in range(number):
        wait_all(copies[n])
        out_block[n, :TOK_DEV] = tn(picks[n], rows_in[n]).astype(LOW)
        if dots:
            row = lax.broadcasted_iota(jnp.int32, (SHARE_ROWS, D), 0)
            values = jnp.zeros((SHARE_ROWS, D), WIDE)
            for e in range(local):
                picked = picks[n, e * capacity : (e + 1) * capacity].astype(WIDE)
                share = picked * dots[e][first + step * n]
                high, low = split(jnp.sum(share, axis=0, keepdims=True))
                pieces = [high.astype(WIDE), low.astype(WIDE)]
                pieces.append(jnp.zeros((1, D - 2 * TOK_DEV), WIDE))
                line = jnp.concatenate(pieces, axis=1)
                values = jnp.where(row == info[0] * local + e, line, values)
            out_block[n, TOK_DEV:] = values.astype(LOW)
        copy = pltpu.make_async_copy(out_block.at[n], out.at[n], sem_out.at[n])
        copy.start()
        sent.append(copy)
    wait_all(sent)


def combine(info, chosen, rows, first, step, dots=()):
    count, capacity, _ = rows[0].shape
    local = len(rows)
    number = (count - first + step - 1) // step
    height = TOK_DEV + (SHARE_ROWS if dots else 0)
    return pl.pallas_call(
        functools.partial(combine_kernel, local, first, step),
        out_shape=jax.ShapeDtypeStruct((number, height, D), LOW),
        in_specs=[SMEM, ANY]
        + [ANY] * local
        + [pl.BlockSpec(memory_space=pltpu.VMEM)] * len(dots),
        out_specs=ANY,
        scratch_shapes=[
            pltpu.VMEM((number, local * capacity, TOK_DEV), LOW),
            pltpu.VMEM((number, local * capacity, D), LOW),
            pltpu.VMEM((number, height, D), LOW),
            pltpu.SemaphoreType.DMA((number, local + 1)),
            pltpu.SemaphoreType.DMA((number,)),
        ],
        compiler_params=params(),
        cost_estimate=LITTLE,
        name="combine",
    )(info, chosen, *rows, *dots)


def chip_adds_kernel(keep, got, send_x, send_y, near_x, near_y, one, two, sem_in, sem_out):
    half = send_x.shape[1]
    copies = [
        (
            pltpu.make_async_copy(keep.at[i], one.at[i], sem_in.at[i, 0]),
            pltpu.make_async_copy(got.at[i], two.at[i], sem_in.at[i, 1]),
        )
        for i in range(4)
    ]
    for pair in copies:
        run_all(pair)
    sent = []
    for i in range(4):
        wait_all(copies[i])
        one[i] = (one[i].astype(WIDE) + two[i].astype(WIDE)).astype(LOW)
        upper = (near_x, send_x)[i % 2].at[i // 2]
        lower = (near_y, send_y)[i // 2].at[i % 2]
        for part, to in enumerate((upper, lower)):
            copy = pltpu.make_async_copy(
                one.at[i, pl.ds(part * half, half)], to, sem_out.at[i, part]
            )
            copy.start()
            sent.append(copy)
    wait_all(sent)


def chip_adds(keep, got):
    _, height, width = keep.shape
    shape = jax.ShapeDtypeStruct((2, height // 2, width), LOW)
    return pl.pallas_call(
        chip_adds_kernel,
        out_shape=(shape,) * 4,
        in_specs=[ANY, ANY],
        out_specs=(ANY,) * 4,
        scratch_shapes=[
            pltpu.VMEM(keep.shape, LOW),
            pltpu.VMEM(keep.shape, LOW),
            pltpu.SemaphoreType.DMA((4, 2)),
            pltpu.SemaphoreType.DMA((4, 2)),
        ],
        compiler_params=params(),
        cost_estimate=LITTLE,
        name="chip_sums",
    )(keep, got)


def corner_adds_kernel(near_x, got_x, near_y, got_y, send_y, send_x):
    send_y[...] = (near_x[0].astype(WIDE) + got_x[0].astype(WIDE)).astype(LOW)
    send_x[...] = (near_y[0].astype(WIDE) + got_y[0].astype(WIDE)).astype(LOW)


def corner_adds(near_x, got_x, near_y, got_y):
    _, half, width = near_x.shape
    rows = half
    block = pl.BlockSpec((1, rows, width), lambda i: (1, i, 0))
    out = pl.BlockSpec((rows, width), lambda i: (i, 0))
    return pl.pallas_call(
        corner_adds_kernel,
        grid=(half // rows,),
        out_shape=(jax.ShapeDtypeStruct((half, width), LOW),) * 2,
        in_specs=[block] * 4,
        out_specs=(out, out),
        compiler_params=params(),
        cost_estimate=LITTLE,
        name="corner_sums",
    )(near_x, got_x, near_y, got_y)


def split(values):
    high = values.astype(LOW)
    return high, (values - high.astype(WIDE)).astype(LOW)


def norm_back(values, gain, grad):
    factor = lax.rsqrt(jnp.mean(values * values, axis=-1, keepdims=True) + EPSILON)
    scaled = gain * grad
    mean = jnp.mean(values * scaled, axis=-1, keepdims=True)
    grad_values = factor * scaled - values * (factor * factor * factor * mean)
    grad_gain = jnp.sum(grad * values * factor, axis=0, keepdims=True)
    return grad_values, grad_gain


def router_back(logits, routes, grad_shares):
    ids = lax.broadcasted_iota(jnp.int32, logits.shape, 0)
    hit = ids == routes[0:1]
    for k in range(1, TOP):
        hit = jnp.logical_or(hit, ids == routes[k : k + 1])
    weights = jnp.exp(logits - jnp.max(logits, axis=0, keepdims=True))
    probs = weights / jnp.sum(weights, axis=0, keepdims=True)
    chosen = jnp.sum(jnp.where(hit, probs, 0.0), axis=0, keepdims=True)
    grads = jnp.where(hit, grad_shares, 0.0)
    mean = jnp.sum(probs * grads, axis=0, keepdims=True) / chosen
    grad_probs = jnp.where(hit, (grads - mean) / chosen, 0.0)
    return probs * (grad_probs - jnp.sum(probs * grad_probs, axis=0, keepdims=True))


def branch_back_kernel(
    parts, info, residual, normed, cotangent, routes, router, gain, *rest
):
    sums, rest = rest[:parts], rest[parts:]
    experts = router.shape[0]
    count = len(rest) - 7
    refs = rest[:count]
    grad_residual, grad_branch, grad_heads, grad_gain, grad_router, weight, sem = rest[count:]

    @pl.when(pl.program_id(0) == 0)
    def _():
        copies = weight_copies(info, refs, weight, sem, D // QUARTERS + 128, D // QUARTERS)
        run_all(copies)
        logits = nt(router[...], normed[...])
        if parts == 2:
            back_sum, grad_shares = sums[0][...], sums[1][...]
        else:
            values = [
                (ref[0] if len(ref.shape) == 3 else ref[...]).astype(WIDE) for ref in sums
            ]
            upper = values[0] + values[1] + values[2]
            lower = values[3] + values[4] + values[5]
            last = lower.shape[0] - SHARE_ROWS
            shares = lower[last : last + experts]
            grad_shares = shares[:, :TOK_DEV] + shares[:, TOK_DEV : 2 * TOK_DEV]
            back_sum = jnp.concatenate([upper, lower[:last]], axis=0)
        high, low = split(router_back(logits, routes[...], grad_shares))
        grad_router[...] = nn(high, normed[...]) + nn(low, normed[...])
        grad_normed = tn(high, router[...]) + tn(low, router[...])
        grad_normed += back_sum
        grad_values, gain_grad = norm_back(residual[...], gain[...], grad_normed)
        grad_gain[...] = gain_grad
        total = cotangent[...].astype(WIDE) + grad_values
        grad_residual[...] = total
        grad_branch[...] = total.astype(LOW)
        wait_all(copies)

    at = pl.ds(pl.multiple_of(pl.program_id(0) * STEP, STEP), STEP)
    grad_heads[...] = nt(grad_branch[...], weight[at, :]).astype(LOW)


def branch_back(info, residual, normed, sums, cotangent, routes, router, gain, refs):
    full = (TOK_DEV, D)
    total = router.shape[0]
    return pl.pallas_call(
        functools.partial(branch_back_kernel, len(sums)),
        grid=(D // STEP,),
        out_shape=(
            jax.ShapeDtypeStruct(full, WIDE),
            jax.ShapeDtypeStruct(full, LOW),
            jax.ShapeDtypeStruct(full, LOW),
            jax.ShapeDtypeStruct((1, D), WIDE),
            jax.ShapeDtypeStruct((total, D), WIDE),
        ),
        in_specs=[SMEM]
        + [whole(full)] * 3
        + [whole((TOP, TOK_DEV)), whole((total, D)), whole((1, D))]
        + [whole(part.shape if part.ndim == 2 else (1,) + part.shape[1:]) for part in sums]
        + [ANY] * len(refs),
        out_specs=(
            whole(full),
            whole(full),
            pl.BlockSpec((TOK_DEV, STEP), lambda i: (0, i)),
            whole((1, D)),
            whole((total, D)),
        ),
        scratch_shapes=[pltpu.VMEM((D, D), LOW), pltpu.SemaphoreType.DMA],
        compiler_params=params(),
        cost_estimate=LITTLE,
        name="experts_norm_back",
    )(info, residual, normed, cotangent, routes, router, gain, *sums, *refs)


def join_grads_kernel(info, own_grad, source_grad, arrived, cosine, sine, out):
    half = HEAD_DIM // 2
    first = lax.broadcasted_iota(jnp.int32, (TOK_DEV, HEAD_DIM), 1) < half
    leaves = info[1] == 0

    def total(column):
        columns = slice(column, column + 128)
        extra = source_grad[:, columns] + arrived[:, columns].astype(WIDE)
        return own_grad[:, columns] + jnp.where(leaves, 0.0, extra)

    for g in range(KV_HEADS):
        key = turn_back(total(128 * g), cosine[...], sine[...])
        value = total(KEY_WIDTH + 128 * g)
        out[:, 256 * g : 256 * g + 128] = jnp.where(
            first, key, pltpu.roll(value, half, 1)
        ).astype(LOW)
        out[:, 256 * g + 128 : 256 * g + 256] = jnp.where(
            first, pltpu.roll(key, half, 1), value
        ).astype(LOW)


def join_grads(info, own_grad, source_grad, arrived, cosine, sine):
    vmem = pl.BlockSpec(memory_space=pltpu.VMEM)
    return pl.pallas_call(
        join_grads_kernel,
        out_shape=jax.ShapeDtypeStruct((TOK_DEV, 2 * KEY_WIDTH), LOW),
        in_specs=[SMEM] + [vmem] * 5,
        out_specs=vmem,
        compiler_params=params(),
        cost_estimate=LITTLE,
        name="join_key_value_gradients",
    )(info, own_grad, source_grad, arrived, cosine, sine)


def normed_grad_kernel(info, grad_query, *rest):
    refs, (out, weight, sem) = rest[:-3], rest[-3:]

    @pl.when(pl.program_id(0) == 0)
    def _():
        copies = weight_copies(info, refs, weight, sem, 0, D // QUARTERS)
        run_all(copies)
        wait_all(copies)

    at = pl.ds(pl.multiple_of(pl.program_id(0) * STEP, STEP), STEP)
    out[...] = nt(grad_query[...], weight[at, :])


def normed_grad(info, grad_query, refs):
    return pl.pallas_call(
        normed_grad_kernel,
        grid=(D // STEP,),
        out_shape=jax.ShapeDtypeStruct((TOK_DEV, D), WIDE),
        in_specs=[SMEM, whole((TOK_DEV, D))] + [ANY] * len(refs),
        out_specs=pl.BlockSpec((TOK_DEV, STEP), lambda i: (0, i)),
        scratch_shapes=[pltpu.VMEM((D, D), LOW), pltpu.SemaphoreType.DMA],
        compiler_params=params(),
        cost_estimate=LITTLE,
        name="normed_gradient",
    )(info, grad_query, *refs)


def token_back_kernel(info, query_part, grad_pair, tokens, grad_residual, gain, *rest):
    refs, (out, grad_gain, weight, sem) = rest[:-4], rest[-4:]
    copies = weight_copies(info, refs, weight, sem, D // QUARTERS, 128)
    run_all(copies)
    wait_all(copies)
    grad_normed = query_part[...] + nt(grad_pair[...], weight[...])
    grad_values, gain_grad = norm_back(tokens[...].astype(WIDE), gain[...], grad_normed)
    grad_gain[...] = gain_grad
    out[...] = (grad_residual[...] + grad_values).astype(LOW)


def token_back(info, query_part, grad_pair, tokens, grad_residual, gain, refs):
    full = (TOK_DEV, D)
    vmem = pl.BlockSpec(memory_space=pltpu.VMEM)
    return pl.pallas_call(
        token_back_kernel,
        out_shape=(jax.ShapeDtypeStruct(full, LOW), jax.ShapeDtypeStruct((1, D), WIDE)),
        in_specs=[SMEM] + [vmem] * 5 + [ANY] * len(refs),
        out_specs=(vmem, vmem),
        scratch_shapes=[
            pltpu.VMEM((D, 2 * KEY_WIDTH), LOW),
            pltpu.SemaphoreType.DMA,
        ],
        compiler_params=params(),
        cost_estimate=LITTLE,
        name="token_gradient",
    )(info, query_part, grad_pair, tokens, grad_residual, gain, *refs)


def weight_grads_kernel(parts, info, *rest):
    ins, (keep, send) = rest[:-2], rest[-2:]
    depth = D // 8
    core = info[0] & 1
    chip = pl.program_id(0) ^ (info[0] >> 1)
    for strip_at, grads_at, start, width in parts:
        low = tn(ins[strip_at][...], ins[grads_at][...]).astype(LOW)
        columns = slice(start, start + width)
        for slot in range(QUARTERS):
            for j in range(QUARTERS):

                @pl.when(info[2 + slot] == j)
                def _():
                    piece = low[:, j * width : (j + 1) * width]
                    upper, lower = piece[:depth], piece[depth:]
                    keep[0, slot, :depth, columns] = jnp.where(core == 0, upper, lower)
                    send[0, slot, :depth, columns] = jnp.where(core == 0, lower, upper)

    if keep.shape[2] > depth:
        extra = ins[-1]
        for slot in range(QUARTERS):
            to = info[2 + slot]
            keep[0, slot, depth:] = extra[(chip * 2 + core) * QUARTERS + to]
            send[0, slot, depth:] = extra[(chip * 2 + 1 - core) * QUARTERS + to]


def weight_grads(info, strips, grads, parts, extra=None):
    depth = D // 8
    strip = pl.BlockSpec((TOK_DEV, 2 * depth), lambda i, info: (0, i ^ (info[0] >> 1)))
    more = [] if extra is None else [extra]
    width = sum(part[3] for part in parts)
    shape = (4, QUARTERS, depth + EXTRA * len(more), width)
    out = pl.BlockSpec((1,) + shape[1:], lambda i, info: (i, 0, 0, 0))
    return pl.pallas_call(
        functools.partial(weight_grads_kernel, parts),
        grid_spec=pltpu.PrefetchScalarGridSpec(
            num_scalar_prefetch=1,
            grid=(4,),
            in_specs=[strip] * len(strips)
            + [
                pl.BlockSpec(a.shape, lambda i, info, n=a.ndim: (0,) * n)
                for a in (*grads, *more)
            ],
            out_specs=(out, out),
        ),
        out_shape=(jax.ShapeDtypeStruct(shape, LOW),) * 2,
        compiler_params=params(),
        cost_estimate=LITTLE,
        name="weight_gradients",
    )(info, *strips, *grads, *more)


def last_sums_kernel(part, info, own, *rest):
    arrived, (query_out, key_out, value_out, out_out, extra_out) = rest[:-5], rest[-5:]
    total = own[...].astype(WIDE)
    for ref in arrived[:-1]:
        total += ref[...].astype(WIDE)
    end = jnp.logical_or(info[2] == 0, info[2] == 3)
    total += jnp.where(end, arrived[-1][...].astype(WIDE), 0.0)
    depth = query_out.shape[0]
    quarter = query_out.shape[1]
    query_out[...] = total[:depth, :quarter]
    pair = total[:depth, 2 * quarter :].T
    key_out[...] = pair[:part]
    value_out[...] = pair[part:]
    out_out[...] = total[:depth, quarter : 2 * quarter]
    extra_out[...] = total[depth:]


def last_sums(info, own, arrived, depth, part):
    height, width = own.shape
    quarter = D // QUARTERS
    vmem = pl.BlockSpec(memory_space=pltpu.VMEM)
    return pl.pallas_call(
        functools.partial(last_sums_kernel, part),
        out_shape=(
            jax.ShapeDtypeStruct((depth, quarter), WIDE),
            jax.ShapeDtypeStruct((part, depth), WIDE),
            jax.ShapeDtypeStruct((part, depth), WIDE),
            jax.ShapeDtypeStruct((depth, quarter), WIDE),
            jax.ShapeDtypeStruct((height - depth, width), WIDE),
        ),
        in_specs=[SMEM] + [vmem] * (1 + len(arrived)),
        out_specs=(vmem,) * 5,
        compiler_params=params(),
        cost_estimate=LITTLE,
        name="last_sums",
    )(info, own, *arrived)


def expert_sums_kernel(count, *rest):
    blocks, outs = rest[:count], rest[count:]
    part = outs[0].shape[1]
    for e in range(count):
        for which, out in enumerate(outs):
            out[e] = blocks[e][which * part : (which + 1) * part].astype(WIDE)


def expert_sums(blocks):
    count, part = len(blocks), blocks[0].shape[0] // 3
    vmem = pl.BlockSpec(memory_space=pltpu.VMEM)
    return pl.pallas_call(
        functools.partial(expert_sums_kernel, count),
        out_shape=(jax.ShapeDtypeStruct((count, part, D), WIDE),) * 3,
        in_specs=[vmem] * count,
        out_specs=(vmem,) * 3,
        compiler_params=params(),
        cost_estimate=LITTLE,
        name="expert_sums",
    )(*blocks)


def position_of(token_index):
    branch_place = TRUNK + (token_index - TRUNK) % BRANCH
    leaf_place = TRUNK + BRANCH + (token_index - TOK_DEV) % BRANCH
    return jnp.where(
        token_index < TRUNK, token_index, jnp.where(token_index < TOK_DEV, branch_place, leaf_place)
    )


def rotary_tables(positions):
    half_dim = HEAD_DIM // 2
    frequency = ROPE_BASE ** (-jnp.arange(half_dim, dtype=jnp.float32) / half_dim)
    angles = positions.astype(jnp.float32)[:, None] * frequency[None, :]
    cosine, sine = (jnp.cos(angles), jnp.sin(angles))
    return (
        jnp.concatenate([cosine, cosine], axis=1),
        jnp.concatenate([-sine, sine], axis=1),
    )


def after(values, *earlier):
    return lax.optimization_barrier((values, earlier))[0]


def fast_mesh():
    return lax.axis_size("rows") == 8 and lax.axis_size("cols") == 4


SLOT_SHARD = ((0, 2, 1, 3), (1, 3, 0, 2), (2, 0, 1, 3), (3, 1, 2, 0))
UP = [(0, 1), (1, 2), (2, 3)]
DOWN = [(1, 0), (2, 1), (3, 2)]
FAR = [(0, 3), (3, 0)]


def send_near(block):
    return lax.ppermute(block, "cols", DOWN), lax.ppermute(block, "cols", UP)


def send_far(block):
    return lax.ppermute(block, "cols", FAR)


def send_over(block):
    return lax.ppermute(block, "cols", [(0, 2), (1, 3), (2, 0), (3, 1)])


def send_second(block, near):
    place = lax.axis_index("cols")
    above, below = near
    payload = jnp.where(place == 1, above, jnp.where(place == 2, below, block))
    return lax.ppermute(payload, "cols", [(3, 1), (1, 0), (0, 2), (2, 3)])


def slot_list(block, near, second, far):
    place = lax.axis_index("cols")
    above, below = near
    end = (place == 0) | (place == 3)
    return [
        block,
        second,
        jnp.where(place == 0, above, below),
        jnp.where(end, far, above),
    ]


def send_slots(slots):
    place = lax.axis_index("cols")
    _, second, third, fourth = slots
    relay = lax.ppermute(second, "cols", [(1, 3), (0, 1), (2, 0), (3, 2)])
    relayed = relay.astype(WIDE)
    upward_load = (
        jnp.where(place == 0, third, fourth).astype(WIDE) + jnp.where(place == 1, relayed, 0.0)
    ).astype(LOW)
    downward_load = (third.astype(WIDE) + jnp.where(place == 2, relayed, 0.0)).astype(LOW)
    arrived = (
        lax.ppermute(upward_load, "cols", UP),
        lax.ppermute(downward_load, "cols", DOWN),
        send_far(after(fourth, upward_load, downward_load)),
        relay,
    )
    return arrived, upward_load


def flip(block, bit):
    count = lax.axis_size("rows")
    return lax.ppermute(block, "rows", [(i, i ^ bit) for i in range(count)])


def add_low(one, two):
    return (one.astype(WIDE) + two.astype(WIDE)).astype(LOW)


def chips_second(near_x, near_y, got_x, got_y):
    for_y, for_x = corner_adds(near_x, got_x, near_y, got_y)
    return (near_x, got_x, flip(for_y, 4), near_y, got_y, flip(for_x, 2))


def turn_corner(beside, across):
    half = beside.shape[0] // 2
    return jnp.concatenate([flip(beside[:half], 4), flip(across[half:], 2)], axis=0)


def send_chips(sums):
    return flip(sums[0], 2), flip(sums[1], 4)


def sum_parts(parts):
    wide = [(a[0] if a.ndim == 3 else a).astype(WIDE) for a in parts]
    if len(wide) == 1:
        return wide[0]
    return jnp.concatenate([wide[0] + wide[1] + wide[2], wide[3] + wide[4] + wide[5]], axis=0)


def on_device(
    tokens,
    query_weight,
    key_weight,
    value_weight,
    out_weight,
    router_weight,
    attention_gain,
    experts_gain,
    gate_weight,
    upward_weight,
    down_weight,
    routes,
    leaf_parent,
    cotangent,
):
    row_count = lax.axis_size("rows")
    col_count = lax.axis_size("cols")
    row_place = lax.axis_index("rows")
    col_place = lax.axis_index("cols")
    fast = fast_mesh()
    parity = lax.rem(col_place, 2)
    tree_id = lax.div(row_place * col_count + col_place, 2)
    parent_row = lax.dynamic_slice_in_dim(leaf_parent, tree_id, 1, 0)[0]
    depth, query_part = query_weight.shape
    key_part = key_weight.shape[1]
    router_part = router_weight.shape[1]
    gain_part = attention_gain.shape[0]
    expert_total = router_part * col_count
    local_experts = gate_weight.shape[0]
    capacity = TOK_DEV * TOP // expert_total * 5 // 4

    shards = (
        jnp.asarray(SLOT_SHARD, jnp.int32)[col_place]
        if fast
        else jnp.arange(4, dtype=jnp.int32)
    )
    branch_rows = jnp.where(parity == 0, TRUNK + BRANCH * parent_row, TRUNK)
    info = jnp.concatenate(
        [jnp.stack([row_place, parity]), shards, branch_rows, jnp.zeros((2,), jnp.int32)]
    ).astype(jnp.int32)

    packed = jnp.concatenate([query_weight, key_weight, value_weight, out_weight], axis=1)
    local_index = (1 - parity) * TOK_DEV + jnp.arange(TOK_DEV, dtype=jnp.int32)
    cosine, sine = rotary_tables(position_of(local_index))
    shard_blocks = [
        jnp.concatenate(
            [gate_weight[expert].T, upward_weight[expert].T, down_weight[expert]], axis=0
        )
        for expert in range(local_experts)
    ]
    expert_refs = []
    if fast:
        wide = packed.shape[1]
        gains = jnp.concatenate([attention_gain, experts_gain])[None, :]
        packed = jnp.concatenate(
            [
                packed,
                jnp.pad(router_weight.T, ((0, 0), (0, wide - depth))),
                jnp.pad(gains, ((0, 0), (0, wide - 2 * gain_part))),
                jnp.pad(routes.T.astype(LOW), ((0, 0), (0, wide - TOK_DEV))),
                jnp.zeros((EXTRA - router_part - 1 - TOP, wide), LOW),
            ],
            axis=0,
        )
        packed_near = send_near(packed)
        packed_far = send_far(packed)
        packed_second = send_over(packed)
        first_block = after(shard_blocks[0], *packed_near)
        first_near = send_near(first_block)
        first_far = send_far(first_block)
        own = jnp.stack(slot_list(packed, packed_near, packed_second, packed_far))
        own = after(own, info, cosine, sine)
        beside, across = flip(own, 2), flip(own, 4)
        own_in = flip(own, 1)
        beside, across = after((beside, across), own_in, *first_near)
        corner = [flip(beside[:2], 4), flip(across[2:], 2)]
        pair_in = flip(jnp.concatenate([beside, across], axis=0), 1)
        corner_in = [flip(piece, 1) for piece in corner]
        grad_in = after(cotangent, *corner)
        grad_flips = [flip(grad_in, 2), flip(grad_in, 4)]
        pieces = [own, own_in, beside, across, *corner, pair_in, *corner_in]
        at = depth + router_part + 1
        near_slots = [own, own_in, beside, pair_in, across, pair_in[4:], corner[0], corner_in[0]]
        routes_all = jnp.stack([part[0, at : at + TOP, :TOK_DEV] for part in near_slots])
        routes_all = routes_all.astype(jnp.int32)
        chosen, place_rows = tables(info, routes_all, capacity, local_experts, expert_total)
        query_refs = pair_refs = out_refs = pieces
        extra_rows = extras(info, pieces)
        router_all = extra_rows[:, :router_part, :depth]
        attention_scale = extra_rows[:, router_part, :gain_part]
        experts_scale = extra_rows[:, router_part, gain_part : 2 * gain_part]
    else:
        packed_all = lax.all_gather(lax.all_gather(packed, "cols", axis=0), "rows", axis=0)

        def unpack(start, width):
            part = packed_all[..., start : start + width]
            return jnp.swapaxes(part, 1, 2).reshape(row_count * depth, col_count * width)

        key_at = query_part
        query_refs = [unpack(0, query_part)]
        pair_refs = [
            jnp.concatenate(
                [
                    unpack(key_at, key_part).reshape(D, QUARTERS, -1),
                    unpack(key_at + key_part, key_part).reshape(D, QUARTERS, -1),
                ],
                axis=2,
            ).reshape(D, -1)
        ]
        out_refs = [unpack(key_at + 2 * key_part, query_part)]
        routes_all = lax.all_gather(routes.T, "rows", axis=0)
        chosen, place_rows = tables(info, routes_all, capacity, local_experts, expert_total)
        axes = ("rows", "cols")
        router_all = jnp.swapaxes(lax.all_gather(router_weight, axes, axis=0), 1, 2)
        attention_scale = lax.all_gather(attention_gain, axes, axis=0)
        experts_scale = lax.all_gather(experts_gain, axes, axis=0)

    attention_scale = attention_scale.reshape(1, D).astype(WIDE)
    experts_scale = experts_scale.reshape(1, D).astype(WIDE)
    router_rows = jnp.transpose(
        router_all.reshape(row_count, col_count, router_part, depth), (1, 2, 0, 3)
    ).reshape(expert_total, D)
    router_cols = router_rows.T
    tokens_in = after(tokens, first_far, chosen) if fast else tokens
    normed, own_pair = key_value(info, tokens_in, attention_scale, cosine, sine, pair_refs)
    pairs = [(i + 1, i) for i in range(0, col_count, 2)]
    partner = lax.ppermute(own_pair, "cols", pairs)
    if fast:
        own_grad_in = flip(grad_in, 1)
        normed_in = after(normed, own_grad_in)
    else:
        normed_in = normed
    queries = query(info, normed_in, cosine, sine, query_refs)
    if fast:
        first_second = send_second(after(first_block, partner, queries), first_near)
        expert_refs.append([first_block, first_second, *first_near, first_far])
    if fast:
        grad_flips = after(grad_flips, queries)
        grad_corner = turn_corner(*grad_flips)
    heads = attention(info, queries, own_pair, partner)
    if fast:
        grad_near = [*grad_flips, grad_corner]
        grad_blocks = [cotangent, own_grad_in]
        grad_blocks += [block for one in grad_near for block in (one, flip(one, 1))]
        heads = after(heads, grad_corner, grad_blocks[3], grad_blocks[5])
    else:
        grad_all = lax.all_gather(cotangent, "rows", axis=0)
        grad_blocks = [grad_all[q] for q in range(row_count)]
    residual, normed_two = out_projection(info, heads, tokens, experts_scale, out_refs)

    if fast:
        beside, across = flip(normed_two, 2), flip(normed_two, 4)
        beside_in = flip(normed_two, 1)
        later_block = after(shard_blocks[1], first_second, normed_two)
        expert_refs.append([lax.all_gather(later_block, "cols", axis=0)])
    else:
        rows_all = lax.all_gather(normed_two, "rows", axis=0)
        expert_refs = [[lax.all_gather(block, "cols", axis=0)] for block in shard_blocks]
    grad_rows = pick_rows(chosen, grad_blocks, local_experts)

    def place_block(q, block, picked):
        return dispatch(
            q, info, block, chosen, routes_all, router_cols, local_experts, picked
        )

    if fast:
        half = TOK_DEV // 2
        picked = place_block(0, normed_two, None)
        picked = place_block(1, beside_in, after(picked, *grad_rows))
        beside, across = after((beside, across), picked)
        corner = [flip(beside[:half], 4), flip(across[half:], 2)]
        picked = place_block(2, beside, picked)
        picked = place_block(4, across, picked)
        beside_in = flip(beside, 1)
        across_in = flip(across, 1)
        picked = place_block(3, beside_in, picked)
        picked = place_block(5, across_in, picked)
        corner = jnp.concatenate(after(corner, picked), axis=0)
        corner_in = flip(corner, 1)
        picked = place_block(6, corner, picked)
        picked = place_block(7, corner_in, picked)
    else:
        picked = None
        for q in range(row_count):
            picked = place_block(q, rows_all[q], picked)
    height = row_count * capacity
    token_rows = [a.reshape(height, D) for a in picked[:local_experts]]
    grad_rows = [a.reshape(height, D) for a in grad_rows]
    share_rows = [a.reshape(height, 1) for a in picked[local_experts:]]

    out_rows, back_rows, gate_dots, reduced = ([], [], [], [])
    for e in range(local_experts):
        rows_in = after(token_rows[e], *reduced_in) if e else token_rows[e]
        out_row, back_row, grad_row, acts, dots = expert(
            info, rows_in, grad_rows[e], share_rows[e], expert_refs[e], col_count
        )
        out_rows.append(out_row.reshape(row_count, capacity, D))
        back_rows.append(back_row.reshape(row_count, capacity, D))
        gate_dots.append(dots.reshape(row_count, capacity, 1))
        if fast and e == 1:
            got = flip(combine(info, chosen, back_rows, 1, 2, gate_dots), 1)
            back_keep = combine(info, chosen, back_rows, 0, 2, gate_dots)
            for_x, for_y, near_x, near_y = chip_adds(back_keep, got)
            acts = after(acts, for_x)
            back_flips = send_chips((for_x, for_y))
        slots = expert_grads(acts, token_rows[e], grad_row)
        reduced_in = (slots,)
        if e and fast:
            out_got = flip(combine(info, chosen, out_rows, 1, 2), 1)
            out_keep = combine(info, chosen, out_rows, 0, 2)
            back_flips = after(back_flips, slots, out_keep)
            back_parts = chips_second(near_x, near_y, *back_flips)
        else:
            reduced.append(lax.psum_scatter(slots, "cols", scatter_dimension=0, tiled=False))

    if fast:
        out_first = chip_adds(out_keep, out_got)
        back_parts = after(back_parts, out_first[0])
    else:
        spread_dots = spread(place_rows, gate_dots)
        grad_shares = lax.all_to_all(spread_dots, "rows", split_axis=0, concat_axis=0, tiled=True)

        def summed(rows):
            part = combine(info, chosen, rows, 0, 1)
            return lax.psum_scatter(part, "rows", scatter_dimension=0).astype(WIDE)

        back_parts = (summed(back_rows), grad_shares.reshape(expert_total, TOK_DEV))
        mixture = (summed(out_rows),)

    grad_residual, grad_branch, grad_heads, experts_gain_grad, router_grad = branch_back(
        info,
        residual,
        normed_two,
        back_parts,
        cotangent,
        routes.T,
        router_rows,
        experts_scale,
        out_refs,
    )
    if fast:
        out_flips = send_chips(after(out_first[:2], back_parts[2], back_parts[5]))
        slots = after(slots, reduced[0], back_parts[2])
        reduced.append(lax.psum_scatter(slots, "cols", scatter_dimension=0, tiled=False))
        main_width = 2 * query_part
        router_parts = jnp.transpose(
            router_grad.astype(LOW).reshape(col_count, router_part, row_count, depth),
            (2, 0, 1, 3),
        ).reshape(row_count * col_count, router_part, depth)
        gain_rows = experts_gain_grad.astype(LOW).reshape(row_count * col_count, 1, gain_part)
        extra = jnp.concatenate(
            [
                jnp.pad(router_parts, ((0, 0), (0, 0), (0, main_width - depth))),
                jnp.pad(gain_rows, ((0, 0), (0, 0), (0, main_width - gain_part))),
                jnp.zeros((row_count * col_count, EXTRA - router_part - 1, main_width), LOW),
            ],
            axis=1,
        )
    grad_query, own_grad, source_grad = attention_back(
        info, queries, own_pair, partner, grad_heads, cosine, sine
    )
    arrived = lax.ppermute(source_grad.astype(LOW), "cols", [(j, i) for i, j in pairs])
    if fast:
        parts = ((0, 2, 0, query_part), (1, 3, query_part, query_part))
        grad_branch = after(grad_branch, *out_flips)
        keep, send = weight_grads(
            info, [normed, heads], [grad_query, grad_branch], parts, extra
        )
        flat = (4, col_count * (depth + EXTRA), main_width)
        sent = flip(send, 1)
        main_first = chip_adds(keep.reshape(flat), sent.reshape(flat))
        main_chips = send_chips(main_first[:2])
        query_back = normed_grad(info, after(grad_query, main_first[0]), query_refs)
        main_chips = after(main_chips, query_back)
        main_x, main_y = main_first[2:]
        for_y, for_x = corner_adds(main_x, main_chips[0], main_y, main_chips[1])
        main_parts = (main_x, main_chips[0], flip(for_y, 4), main_y, main_chips[1])
        main_parts += (flip(for_x, 2),)
        arrived = after(arrived, for_y)
    else:
        query_back = normed_grad(info, grad_query, query_refs)
    grad_pair = join_grads(info, own_grad, source_grad, arrived, cosine, sine)
    if fast:
        keep, send = weight_grads(info, [normed], [grad_pair], ((0, 1, 0, 2 * key_part),))
        flat = (4, col_count * depth, 2 * key_part)
        pair_first = chip_adds(keep.reshape(flat), flip(send, 1).reshape(flat))
        pair_chips = send_chips(pair_first[:2])
        grad_pair = after(grad_pair, pair_first[0])
    tokens_grad, attention_gain_grad = token_back(
        info, query_back, grad_pair, tokens, grad_residual, attention_scale, pair_refs
    )

    if fast:
        pair_parts = chips_second(*pair_first[2:], *after(pair_chips, tokens_grad))
    if fast:
        main_parts = after(main_parts, tokens_grad)
        slots = sum_parts(main_parts).reshape(col_count, depth + EXTRA, main_width)
        pairs_sum = sum_parts(pair_parts).reshape(col_count, depth, 2 * key_part)
        width = query_part + 2 * key_part
        weights_own = jnp.stack([own[i, :depth, :width].astype(WIDE) for i in range(4)])
        gain_sums = jnp.sum(
            weights_own[..., :query_part] * slots[:, :depth, :query_part], axis=(0, 2)
        ) + jnp.sum(weights_own[..., query_part:] * pairs_sum, axis=(0, 2))
        own_gains = lax.dynamic_slice_in_dim(attention_scale[0], row_place * depth, depth, 0)
        gain_sums = (gain_sums / own_gains).reshape(col_count, 1, gain_part)
        gain_sums = jnp.pad(
            jnp.take(gain_sums, shards, axis=0),
            (
                (0, 0),
                (depth + router_part + 1, EXTRA - router_part - 2),
                (0, main_width - gain_part),
            ),
        )
        pairs_sum = jnp.pad(pairs_sum, ((0, 0), (0, EXTRA), (0, 0)))
        slots = jnp.concatenate([slots + gain_sums, pairs_sum], axis=2).astype(LOW)
        slots = after(slots, reduced[1])

        arrived, sent_load = send_slots(slots)
        near_x, near_y = out_first[2:]
        mixture = chips_second(near_x, near_y, *after(out_flips, sent_load))
        layer_output = (residual + sum_parts(mixture)).astype(LOW)
        gate_grad, upward_grad, down_grad = expert_sums(after(reduced, mixture[2], mixture[5]))
        earlier = (gate_grad, upward_grad, down_grad, layer_output)
        query_sum, key_sum, value_sum, out_sum, extra_sum = last_sums(
            info, slots[0], after(arrived, *earlier), depth, key_part
        )
        key_sum, value_sum = key_sum.T, value_sum.T
        router_sum = extra_sum[:router_part, :depth].T
        experts_gain_sum = extra_sum[router_part, :gain_part]
        attention_gain_sum = extra_sum[router_part + 1, :gain_part]
    else:
        layer_output = (residual + sum_parts(mixture)).astype(LOW)
        gate_grad, upward_grad, down_grad = expert_sums(reduced)
        full_grads = [
            tn(normed, grad_query),
            *jnp.moveaxis(tn(normed, grad_pair).reshape(D, QUARTERS, 2, -1), 2, 0),
            tn(heads, grad_branch),
        ]
        packed_grad = jnp.concatenate(
            [
                grad.astype(LOW).reshape(row_count, depth, col_count, -1)
                for grad in full_grads
            ],
            axis=3,
        )
        row_sums = lax.psum_scatter(packed_grad, "rows", scatter_dimension=0)
        sums = lax.psum_scatter(row_sums, "cols", scatter_dimension=1).astype(WIDE)
        key_at = query_part
        value_at = key_at + key_part
        out_at = value_at + key_part
        query_sum, out_sum = sums[:, :key_at], sums[:, out_at:]
        key_sum, value_sum = sums[:, key_at:value_at], sums[:, value_at:out_at]
        small_grads = jnp.concatenate(
            [
                attention_gain_grad.reshape(-1, gain_part),
                experts_gain_grad.reshape(-1, gain_part),
                jnp.transpose(
                    router_grad.reshape(col_count, router_part, row_count, depth), (2, 0, 3, 1)
                ).reshape(row_count * col_count, depth * router_part),
            ],
            axis=1,
        )
        small_grads = small_grads.reshape(row_count, -1)
        small_grads = lax.all_to_all(small_grads, "rows", split_axis=0, concat_axis=0, tiled=True)
        small_grads = jnp.sum(small_grads, axis=0).reshape(col_count, -1)
        small_grads = lax.all_to_all(small_grads, "cols", split_axis=0, concat_axis=0, tiled=True)
        small_sums = jnp.sum(small_grads, axis=0)
        attention_gain_sum = small_sums[:gain_part]
        experts_gain_sum = small_sums[gain_part : 2 * gain_part]
        router_sum = small_sums[2 * gain_part :].reshape(depth, router_part)

    return (
        layer_output,
        tokens_grad,
        query_sum,
        key_sum,
        value_sum,
        out_sum,
        router_sum,
        attention_gain_sum,
        experts_gain_sum,
        jnp.swapaxes(gate_grad, 1, 2),
        jnp.swapaxes(upward_grad, 1, 2),
        down_grad,
    )


def solution(mesh):
    in_specs = (
        P(("rows", "cols"), None),
        P("rows", "cols"),
        P("rows", "cols"),
        P("rows", "cols"),
        P("rows", "cols"),
        P("rows", "cols"),
        P(("rows", "cols")),
        P(("rows", "cols")),
        P("rows", None, "cols"),
        P("rows", None, "cols"),
        P("rows", "cols", None),
        P(("rows", "cols"), None),
        P(),
        P(("rows", "cols"), None),
    )
    out_specs = (
        P(("rows", "cols"), None),
        P(("rows", "cols"), None),
        P("rows", "cols"),
        P("rows", "cols"),
        P("rows", "cols"),
        P("rows", "cols"),
        P("rows", "cols"),
        P(("rows", "cols")),
        P(("rows", "cols")),
        P("rows", None, "cols"),
        P("rows", None, "cols"),
        P("rows", "cols", None),
    )
    return jax.shard_map(
        on_device, mesh=mesh, in_specs=in_specs, out_specs=out_specs, check_vma=False
    )
```
